32 devices in a mesh: section: 2 (over y), batch: 16 (over z, x, core).
Axes of the slice: x: 2, y: 2, z: 4, core: 2. Of those that a mesh axis runs over, the one named last changes fastest.
Arguments:
- captions: bfloat16 [64, 172, 768], P('batch'), may hold values from -6 to 6
- regions: bfloat16 [16, 36, 768], P('batch'), may hold values from -6 to 6
- image_ids: int32 [64], P('batch'), may hold values from 0 to 15, as said below
- caption_lengths: int32 [64], P('batch'), may hold values from 44 to 172
- cotangent: bfloat16 [64, 208, 768], P('batch'), may hold values from -6 to 6
- query_weight: bfloat16 [2, 768, 768], P('section'), may hold values from -0.21875 to 0.21875
- query_bias: bfloat16 [2, 768], P('section'), may hold values from -2 to 2
- key_weight: bfloat16 [2, 768, 768], P('section'), may hold values from -0.21875 to 0.21875
- value_weight: bfloat16 [2, 768, 768], P('section'), may hold values from -0.21875 to 0.21875
- value_bias: bfloat16 [2, 768], P('section'), may hold values from -2 to 2
- out_weight: bfloat16 [2, 768, 768], P('section'), may hold values from -1.75 to 1.75
- out_bias: bfloat16 [2, 768], P('section'), may hold values from -2 to 2
- norm1_gain: bfloat16 [2, 768], P('section'), may hold values from 0.5 to 1.5
- norm1_bias: bfloat16 [2, 768], P('section'), may hold values from -2 to 2
- up_weight: bfloat16 [2, 768, 3072], P('section'), may hold values from -0.21875 to 0.21875
- up_bias: bfloat16 [2, 3072], P('section'), may hold values from -2 to 2
- down_weight: bfloat16 [2, 3072, 768], P('section'), may hold values from -0.109375 to 0.109375
- down_bias: bfloat16 [2, 768], P('section'), may hold values from -2 to 2
- norm2_gain: bfloat16 [2, 768], P('section'), may hold values from 0.5 to 1.5
- norm2_bias: bfloat16 [2, 768], P('section'), may hold values from -2 to 2
Outputs:
- hidden_states: bfloat16 [2, 64, 208, 768], P('section', 'batch')
- section_grads: bfloat16 [2, 64, 208, 768], P('section', 'batch')
- grad_query_weight: float32 [2, 768, 768], P('section')
- grad_query_bias: float32 [2, 768], P('section')
- grad_key_weight: float32 [2, 768, 768], P('section')
- grad_value_weight: float32 [2, 768, 768], P('section')
- grad_value_bias: float32 [2, 768], P('section')
- grad_out_weight: float32 [2, 768, 768], P('section')
- grad_out_bias: float32 [2, 768], P('section')
- grad_norm1_gain: float32 [2, 768], P('section')
- grad_norm1_bias: float32 [2, 768], P('section')
- grad_up_weight: float32 [2, 768, 3072], P('section')
- grad_up_bias: float32 [2, 3072], P('section')
- grad_down_weight: float32 [2, 3072, 768], P('section')
- grad_down_bias: float32 [2, 768], P('section')
- grad_norm2_gain: float32 [2, 768], P('section')
- grad_norm2_bias: float32 [2, 768], P('section')
The draws below stay inside these ranges and needn't reach their ends.
Inputs may be any that keep to these rules, and one draw needn't show every extreme that they name: `image_ids`: image m is held at batch index m // 1; the image of item i is held at batch index b = i // 4 or at b - 1 or b + 1 (cyclically), and on every index some item names an image of b - 1 and some item one of b + 1. `caption_lengths`: caption rows at or past this count are padding, masked as keys.
All inputs are finite; a program needn't handle non-finite values.
Results may differ from the reference program's by a relative error of at most 0.029.
Values may be sent and summed in bfloat16 or wider, within the bound.
A program may use at most 320 MiB of HBM per device.

```python
import math
import jax
import jax.numpy as jnp
from jax import lax

D = 768
HEADS = 12
FF = 3072
CAP = 172
REG = 36
ITEMS_DEV = 4
IMG_DEV = 1
HEAD = 64
ROWS = 208
ITEMS = 64
IMAGES = 16
N_SECTION = 2


def draw_image_ids(key, part):
    key = jax.random.fold_in(key, 7)
    owners = IMAGES // IMG_DEV
    step_key, order_key, pick_key = jax.random.split(key, 3)
    shifts = jax.random.randint(step_key, (owners, ITEMS_DEV), -1, 2)
    orders = jax.vmap(lambda single: jax.random.permutation(single, ITEMS_DEV))(jax.random.split(order_key, owners))
    slots = jnp.arange(ITEMS_DEV, dtype=jnp.int32)[None, :]
    shifts = jnp.where(slots == orders[:, 0:1], -1, jnp.where(slots == orders[:, 1:2], 1, shifts))
    homes = jnp.arange(owners, dtype=jnp.int32)[:, None]
    holder = jnp.mod(homes + shifts, owners)
    picks = jax.random.randint(pick_key, (owners, ITEMS_DEV), 0, IMG_DEV)
    return (holder * IMG_DEV + picks).reshape(ITEMS).astype(jnp.int32)


def with_ends(drawn, key, least, top_value):
    longest = drawn.shape.index(max(drawn.shape))
    spots = []
    for shift in (0, 1):
        where = [jax.random.randint(jax.random.fold_in(key, axis), (), 0, length) for axis, length in enumerate(drawn.shape)]
        where[longest] = (where[longest] + shift) % drawn.shape[longest]
        spots.append(tuple(where))
    return drawn.at[spots[0]].set(least).at[spots[1]].set(top_value)


def block_levels(stream_key, dims, cuts, least, largest):
    def one(position, shards_of):
        steps = jax.random.uniform(jax.random.fold_in(jax.random.fold_in(stream_key, 6), position), (shards_of,), jnp.float32, least / len(cuts), largest / len(cuts))
        return jnp.repeat(jnp.exp(steps), dims[position] // shards_of).reshape((-1,) + (1,) * (len(dims) - position - 1))

    level = one(*cuts[0])
    for cut in cuts[1:]:
        level = level * one(*cut)
    return level


def gaussian(key, dims, spread, most, cuts=(), kind=jnp.bfloat16):
    level = block_levels(key, dims, cuts, -0.22, 0.18) if cuts else 1.0
    drawn = jax.random.normal(key, dims, jnp.float32) * spread * level
    return jnp.minimum(jnp.maximum(drawn, -most), most).astype(kind)


def setup_inputs(seed: int = 0) -> dict:
    streams_of = jax.random.split(jax.random.key(seed), 21)
    captions = gaussian(streams_of[0], (ITEMS, CAP, D), 1.0, 6.0, ((0, 16),))
    regions = gaussian(streams_of[1], (IMAGES, REG, D), 1.0, 6.0, ((0, 16),))
    image_ids = draw_image_ids(jax.random.fold_in(streams_of[20], 71), 0)
    caption_lengths = with_ends(jax.random.randint(streams_of[3], (ITEMS,), CAP // 4 + 1, CAP + 1), jax.random.fold_in(streams_of[3], 1), CAP // 4 + 1, CAP).astype(jnp.int32)
    cotangent = gaussian(streams_of[4], (ITEMS, ROWS, D), 1.0, 6.0, ((0, 16),))
    query_weight = gaussian(streams_of[5], (N_SECTION, D, D), D ** -0.5, 0.21875, ((0, 2),))
    query_bias = gaussian(streams_of[6], (N_SECTION, D), 0.3, 2.0, ((0, 2),))
    key_weight = gaussian(streams_of[7], (N_SECTION, D, D), D ** -0.5, 0.21875, ((0, 2),))
    value_weight = gaussian(streams_of[8], (N_SECTION, D, D), D ** -0.5, 0.21875, ((0, 2),))
    value_bias = gaussian(streams_of[9], (N_SECTION, D), 0.3, 2.0, ((0, 2),))
    out_weight = gaussian(streams_of[10], (N_SECTION, D, D), (D // 64) ** -0.5, 1.75, ((0, 2),))
    out_bias = gaussian(streams_of[11], (N_SECTION, D), 0.3, 2.0, ((0, 2),))
    norm1_gain = jnp.clip(1.0 + 0.1 * jax.random.normal(streams_of[12], (N_SECTION, D), jnp.float32), 0.5, 1.5).astype(jnp.bfloat16)
    norm1_bias = gaussian(streams_of[13], (N_SECTION, D), 0.3, 2.0, ((0, 2),))
    up_weight = gaussian(streams_of[14], (N_SECTION, D, FF), D ** -0.5, 0.21875, ((0, 2),))
    up_bias = gaussian(streams_of[15], (N_SECTION, FF), 0.3, 2.0, ((0, 2),))
    down_weight = gaussian(streams_of[16], (N_SECTION, FF, D), FF ** -0.5, 0.109375, ((0, 2),))
    down_bias = gaussian(streams_of[17], (N_SECTION, D), 0.3, 2.0, ((0, 2),))
    norm2_gain = jnp.clip(1.0 + 0.1 * jax.random.normal(streams_of[18], (N_SECTION, D), jnp.float32), 0.5, 1.5).astype(jnp.bfloat16)
    norm2_bias = gaussian(streams_of[19], (N_SECTION, D), 0.3, 2.0, ((0, 2),))
    return dict(captions=captions, regions=regions, image_ids=image_ids, caption_lengths=caption_lengths, cotangent=cotangent, query_weight=query_weight, query_bias=query_bias, key_weight=key_weight, value_weight=value_weight, value_bias=value_bias, out_weight=out_weight, out_bias=out_bias, norm1_gain=norm1_gain, norm1_bias=norm1_bias, up_weight=up_weight, up_bias=up_bias, down_weight=down_weight, down_bias=down_bias, norm2_gain=norm2_gain, norm2_bias=norm2_bias)


@jax.custom_vjp
def low(v):
    return lax.optimization_barrier(v.astype(jnp.bfloat16)).astype(jnp.float32)

@jax.custom_vjp
def low_back(v):
    return v

def low_keep(v):
    return (low(v), None)

def low_pass(kept, grad):
    return (grad,)

def back_keep(v):
    return (v, None)

def back_low(kept, grad):
    return (low(grad),)
low.defvjp(low_keep, low_pass)
low_back.defvjp(back_keep, back_low)
EPSILON = 1e-12
HIGHEST = lax.Precision.HIGHEST

def normalize(values, gain, shift):
    average = lax.optimization_barrier(jnp.mean(values, axis=-1, keepdims=True))
    centered = values - average
    variance = lax.optimization_barrier(jnp.mean(centered * centered, axis=-1, keepdims=True))
    return centered * lax.rsqrt(variance + EPSILON) * gain + shift

def layer(hidden, key_bias, params):
    w_query, b_query, w_key, w_value, b_value, w_out, b_out, gain_one, shift_one, w_up, b_up, w_down, b_down, gain_two, shift_two = params
    hidden = low_back(hidden)
    count, rows, width = hidden.shape
    scale = 1.0 / math.sqrt(HEAD)

    def project(source, weight):
        return jnp.einsum('brd,de->bre', source, weight, precision=HIGHEST)
    query = low_back(low(project(hidden, w_query) + b_query)).reshape(count, rows, HEADS, HEAD)
    keys = low_back(low(project(hidden, w_key))).reshape(count, rows, HEADS, HEAD)
    values = low_back(low(project(hidden, w_value) + b_value)).reshape(count, rows, HEADS, HEAD)
    scores = jnp.einsum('bqhe,bkhe->bhqk', query, keys, precision=HIGHEST) * scale
    scores = low_back(scores + key_bias[:, None, None, :])
    probs = low(jax.nn.softmax(scores, axis=-1))
    context = jnp.einsum('bhqk,bkhe->bqhe', probs, values, precision=HIGHEST).reshape(count, rows, width)
    context = low_back(low(context))
    attended = low_back(project(context, w_out) + b_out)
    first = normalize(hidden + attended, gain_one, shift_one)
    inner = low_back(project(low(first), w_up) + b_up)
    activated = low(jax.nn.gelu(inner, approximate=False))
    output = low_back(project(activated, w_down) + b_down)
    return low(normalize(first + output, gain_two, shift_two))

def run_layer(hidden, key_bias, params):
    shaped = hidden.reshape(-1, ITEMS_DEV, ROWS, D)
    biases = key_bias.reshape(-1, ITEMS_DEV, ROWS)
    step = jax.checkpoint(lambda pair: layer(pair[0], pair[1], params))
    return lax.map(step, (shaped, biases)).reshape(hidden.shape)

def reference(captions, regions, image_ids, caption_lengths, cotangent, query_weight, query_bias, key_weight, value_weight, value_bias, out_weight, out_bias, norm1_gain, norm1_bias, up_weight, up_bias, down_weight, down_bias, norm2_gain, norm2_bias):
    stacked = (query_weight, query_bias, key_weight, value_weight, value_bias, out_weight, out_bias, norm1_gain, norm1_bias, up_weight, up_bias, down_weight, down_bias, norm2_gain, norm2_bias)
    params_one = tuple((member[0].astype(jnp.float32) for member in stacked))
    params_two = tuple((member[1].astype(jnp.float32) for member in stacked))
    positions = jnp.arange(ROWS, dtype=jnp.int32)
    live = (positions[None, :] >= CAP) | (positions[None, :] < caption_lengths[:, None])
    key_bias = jnp.where(live, 0.0, -1000000000.0).astype(jnp.float32)
    rows_in = jnp.concatenate([captions.astype(jnp.float32), regions.astype(jnp.float32)[image_ids]], axis=1)
    hidden_one, back_one = jax.vjp(lambda source, params: run_layer(source, key_bias, params), rows_in, params_one)
    hidden_two, back_two = jax.vjp(lambda source, params: run_layer(source, key_bias, params), hidden_one, params_two)
    grad_hidden, grads_two = back_two(cotangent.astype(jnp.float32))
    grad_rows, grads_one = back_one(grad_hidden)
    hidden_states = jnp.stack([hidden_one, hidden_two]).astype(jnp.bfloat16)
    section_grads = jnp.stack([grad_rows, grad_hidden]).astype(jnp.bfloat16)
    grads = [jnp.stack([first_grad, second_grad]) for first_grad, second_grad in zip(grads_one, grads_two)]
    return (hidden_states, section_grads, grads[0], grads[1], grads[2], grads[3], grads[4], grads[5], grads[6], grads[7], grads[8], grads[9], grads[10], grads[11], grads[12], grads[13], grads[14])
```

```python
import functools
import math

import jax
import jax.numpy as jnp
from jax import lax
from jax.experimental import pallas as pl
from jax.experimental.pallas import tpu as pltpu
from jax.sharding import PartitionSpec as P

HEADS = 12
MICRO = 4


EPSILON = 1e-12
MESH = pl.DeviceIdType.MESH
VMEM_LIMIT = 60 * 1024 * 1024


GROUP = 16
CHUNK_GROUPS = 16
SPLIT_BITS = 4
LAG = 2


def local_grad_block(block, third, a_ref, b_ref, width):
    a_col = jnp.minimum(block, 4) + jnp.minimum(block // 8, 1) + jnp.minimum(block // 9, 1)
    b_col = jnp.maximum(block - 3, 0)
    rows = CHUNK_GROUPS * GROUP
    left = a_ref[:, pl.ds(pl.multiple_of(a_col * width + third * rows, rows), rows)]
    right = b_ref[:, pl.ds(pl.multiple_of(b_col * width, width), width)]
    return lax.dot_general(left, right, (((0,), (0,)), ((), ())), preferred_element_type=jnp.float32)


def reduce_kernel(
    bits,
    chunks,
    a_hbm,
    b_hbm,
    small_ref,
    out_hbm,
    small_out,
    a_ref,
    b_ref,
    acc,
    recv,
    recv_extra,
    small_acc,
    small_recv,
    load_sem,
    send_sem,
    recv_sem,
    keep_sem,
    small_send_sem,
    small_recv_sem,
):
    width = acc.shape[2]
    extra = bits - SPLIT_BITS
    stages = 2 * SPLIT_BITS + extra
    me = lax.axis_index("batch")
    section = lax.axis_index("section")

    load_a = pltpu.make_async_copy(a_hbm, a_ref, load_sem.at[0])
    load_b = pltpu.make_async_copy(b_hbm, b_ref, load_sem.at[1])
    load_a.start()
    load_b.start()

    def mate(stride):
        bit = (me // stride) % 2
        return bit, (section, me + stride * (1 - 2 * bit))

    barrier = pltpu.get_barrier_semaphore()
    for k in range(bits):
        pl.semaphore_signal(barrier, inc=1, device_id=mate(2**k)[1], device_id_type=MESH)
    pl.semaphore_wait(barrier, bits)

    def strides(c):
        kind = (c % 4) // 3
        return (1, 2 + 2 * kind, 4 - 2 * kind, 8)

    def offsets(c):
        found = [0]
        half = CHUNK_GROUPS
        for stride in strides(c):
            half = half // 2
            found.append(found[-1] + mate(stride)[0] * half)
        return found

    def scatter_copy(c, k):
        bit, peer = mate(strides(c)[k])
        half = CHUNK_GROUPS >> (k + 1)
        base = CHUNK_GROUPS - 2 * half
        start = c * CHUNK_GROUPS + offsets(c)[k] + (1 - bit) * half
        return pltpu.make_async_remote_copy(
            src_ref=acc.at[pl.ds(start, half)],
            dst_ref=recv.at[c, pl.ds(base, half)],
            send_sem=send_sem.at[c, k],
            recv_sem=recv_sem.at[c, k],
            device_id=peer,
            device_id_type=MESH,
        )

    def extra_copy(c, e):
        start = c * CHUNK_GROUPS + offsets(c)[SPLIT_BITS]
        return pltpu.make_async_remote_copy(
            src_ref=acc.at[pl.ds(start, 1)],
            dst_ref=recv_extra.at[c, pl.ds(e, 1)],
            send_sem=send_sem.at[c, SPLIT_BITS + e],
            recv_sem=recv_sem.at[c, SPLIT_BITS + e],
            device_id=mate(2 ** (SPLIT_BITS + e))[1],
            device_id_type=MESH,
        )

    def keep_copy(c):
        start = c * CHUNK_GROUPS + offsets(c)[SPLIT_BITS]
        return pltpu.make_async_copy(acc.at[pl.ds(start, 1)], out_hbm.at[pl.ds(start, 1)], keep_sem.at[c])

    def gather_copy(c, k):
        peer = mate(strides(c)[k])[1]
        held = CHUNK_GROUPS >> (k + 1)
        start = c * CHUNK_GROUPS + offsets(c)[k + 1]
        source = acc if k == SPLIT_BITS - 1 else out_hbm
        index = SPLIT_BITS + extra + (SPLIT_BITS - 1 - k)
        return pltpu.make_async_remote_copy(
            src_ref=source.at[pl.ds(start, held)],
            dst_ref=out_hbm.at[pl.ds(start, held)],
            send_sem=send_sem.at[c, index],
            recv_sem=recv_sem.at[c, index],
            device_id=peer,
            device_id_type=MESH,
        )

    def add_groups(start, count, c, base, source):
        def one(g, carry):
            total = acc[start + g].astype(jnp.float32) + source[c, base + g].astype(jnp.float32)
            acc[start + g] = total.astype(jnp.bfloat16)
            return carry

        lax.fori_loop(0, count, one, 0)

    def stage_copy(c, s):
        if s < SPLIT_BITS:
            return scatter_copy(c, s)
        if s < SPLIT_BITS + extra:
            return extra_copy(c, s - SPLIT_BITS)
        return gather_copy(c, 2 * SPLIT_BITS + extra - 1 - s)

    def finish_stage(c, s):
        stage_copy(c, s).wait()
        if s < SPLIT_BITS:
            half = CHUNK_GROUPS >> (s + 1)
            add_groups(c * CHUNK_GROUPS + offsets(c)[s + 1], half, c, CHUNK_GROUPS - 2 * half, recv)
        elif s < SPLIT_BITS + extra:
            add_groups(c * CHUNK_GROUPS + offsets(c)[SPLIT_BITS], 1, c, s - SPLIT_BITS, recv_extra)
        elif s == SPLIT_BITS + extra:
            keep_copy(c).wait()

    def small_copy(k):
        return pltpu.make_async_remote_copy(
            src_ref=small_acc.at[k],
            dst_ref=small_recv.at[k],
            send_sem=small_send_sem.at[k],
            recv_sem=small_recv_sem.at[k],
            device_id=mate(2**k)[1],
            device_id_type=MESH,
        )

    load_a.wait()
    load_b.wait()
    small_acc[0] = small_ref[...]

    def step(t, carry):
        for s in range(stages, 0, -1):
            c = t - LAG * s

            @pl.when((c >= 0) & (c < chunks))
            def _():
                finish_stage(c, s - 1)
                if s == SPLIT_BITS + extra:
                    keep_copy(c).start()
                if s < stages:
                    stage_copy(c, s).start()

        @pl.when(t < chunks)
        def _():
            grad = local_grad_block(t // 3, t % 3, a_ref, b_ref, width)
            acc[pl.ds(t * CHUNK_GROUPS, CHUNK_GROUPS)] = grad.astype(jnp.bfloat16).reshape(
                CHUNK_GROUPS, GROUP, width
            )
            stage_copy(t, 0).start()

        for k in range(bits + 1):

            @pl.when(t == LAG * k)
            def _():
                if k > 0:
                    small_copy(k - 1).wait()
                    small_acc[k] = small_acc[k - 1] + small_recv[k - 1]
                if k < bits:
                    small_copy(k).start()

        return carry

    lax.fori_loop(0, chunks + LAG * stages, step, 0)
    small_out[...] = small_acc[bits]


def reduced(a_side, b_side, small, count):
    width = small.shape[1]
    rows = a_side.shape[0]
    bits = count.bit_length() - 1
    extra = bits - SPLIT_BITS
    stages = 2 * SPLIT_BITS + extra
    blocks = 12
    chunks = blocks * width // (CHUNK_GROUPS * GROUP)
    groups = chunks * CHUNK_GROUPS
    return pl.pallas_call(
        functools.partial(reduce_kernel, bits, chunks),
        out_shape=(
            jax.ShapeDtypeStruct((groups, GROUP, width), jnp.bfloat16),
            jax.ShapeDtypeStruct(small.shape, jnp.float32),
        ),
        in_specs=[
            pl.BlockSpec(memory_space=pl.ANY),
            pl.BlockSpec(memory_space=pl.ANY),
            pl.BlockSpec(memory_space=pltpu.VMEM),
        ],
        out_specs=(pl.BlockSpec(memory_space=pl.ANY), pl.BlockSpec(memory_space=pltpu.VMEM)),
        scratch_shapes=[
            pltpu.VMEM(a_side.shape, jnp.bfloat16),
            pltpu.VMEM(b_side.shape, jnp.bfloat16),
            pltpu.VMEM((groups, GROUP, width), jnp.bfloat16),
            pltpu.VMEM((chunks, CHUNK_GROUPS - 1, GROUP, width), jnp.bfloat16),
            pltpu.VMEM((chunks if extra else 1, max(extra, 1), GROUP, width), jnp.bfloat16),
            pltpu.VMEM((bits + 1,) + small.shape, jnp.float32),
            pltpu.VMEM((bits,) + small.shape, jnp.float32),
            pltpu.SemaphoreType.DMA((2,)),
            pltpu.SemaphoreType.DMA((chunks, stages)),
            pltpu.SemaphoreType.DMA((chunks, stages)),
            pltpu.SemaphoreType.DMA((chunks,)),
            pltpu.SemaphoreType.DMA((bits,)),
            pltpu.SemaphoreType.DMA((bits,)),
        ],
        compiler_params=pltpu.CompilerParams(
            collective_id=1, has_side_effects=True, vmem_limit_bytes=VMEM_LIMIT
        ),
        cost_estimate=pl.CostEstimate(
            flops=2 * rows * blocks * width * width, bytes_accessed=80_000_000, transcendentals=0
        ),
    )(a_side, b_side, small)


def spread_kernel(sum_hbm, small_ref, *refs):
    width = small_ref.shape[1]
    outs = refs[:15]
    taken, given, in_sem, out_sem = refs[15:]
    (o_wq, o_bq, o_wk, o_wv, o_bv, o_wo, o_bo, o_g1, o_s1, o_up, o_bu, o_dn, o_bd, o_g2, o_s2) = outs
    wide = o_bu.shape[1] // width
    targets = [o_dn.at[0, pl.ds(j * width, width), :] for j in range(wide)]
    targets += [o_up.at[0, :, pl.ds(j * width, width)] for j in range(wide)]
    targets += [o_wo.at[0], o_wq.at[0], o_wk.at[0], o_wv.at[0]]
    depth = taken.shape[0]

    def load(i):
        return pltpu.make_async_copy(
            sum_hbm.at[pl.ds(i * width, width)], taken.at[i % depth], in_sem.at[i % depth]
        )

    def store(i):
        return pltpu.make_async_copy(given.at[i % depth], targets[i], out_sem.at[i % depth])

    for i in range(depth):
        load(i).start()
    singles = [o_bq, o_bv, o_bo, o_g1, o_s1, o_bd, o_g2, o_s2]
    for i, ref in enumerate(singles):
        ref[...] = small_ref[pl.ds(i, 1), :]
    for j in range(wide):
        o_bu[:, pl.ds(j * width, width)] = small_ref[pl.ds(len(singles) + j, 1), :]
    for i in range(len(targets)):
        load(i).wait()
        if i >= depth:
            store(i - depth).wait()

        def convert(r, carry):
            rows = pl.ds(pl.multiple_of(r * 64, 64), 64)
            given[i % depth, rows, :] = taken[i % depth, rows, :].astype(jnp.float32)
            return carry

        lax.fori_loop(0, width // 64, convert, 0)
        store(i).start()
        if i + depth < len(targets):
            load(i + depth).start()
    for i in range(len(targets) - depth, len(targets)):
        store(i).wait()


def spread(sums, small, params):
    width = small.shape[1]
    depth = 3
    matrices = [len(member.shape) == 3 for member in params]
    return pl.pallas_call(
        spread_kernel,
        out_shape=tuple(jax.ShapeDtypeStruct(member.shape, jnp.float32) for member in params),
        in_specs=[pl.BlockSpec(memory_space=pl.ANY), pl.BlockSpec(memory_space=pltpu.VMEM)],
        out_specs=tuple(
            pl.BlockSpec(memory_space=pl.ANY if matrix else pltpu.VMEM) for matrix in matrices
        ),
        scratch_shapes=[
            pltpu.VMEM((depth, width, width), jnp.bfloat16),
            pltpu.VMEM((depth, width, width), jnp.float32),
            pltpu.SemaphoreType.DMA((depth,)),
            pltpu.SemaphoreType.DMA((depth,)),
        ],
        compiler_params=pltpu.CompilerParams(vmem_limit_bytes=VMEM_LIMIT),
        cost_estimate=pl.CostEstimate(
            flops=12 * width * width, bytes_accessed=72 * width * width, transcendentals=0
        ),
    )(sums, small)


def padded(cells, sides, width):
    for axis, dim in sides:
        count = lax.axis_size(axis)
        head = lax.slice_in_dim(cells, 0, width, axis=dim)
        tail = lax.slice_in_dim(cells, cells.shape[dim] - width, cells.shape[dim], axis=dim)
        cells = jnp.concatenate(
            [
                lax.ppermute(tail, axis, [(i, (i + 1) % count) for i in range(count)]),
                cells,
                lax.ppermute(head, axis, [((i + 1) % count, i) for i in range(count)]),
            ],
            axis=dim,
        )
    return cells


def shifted(value, axis, by):
    peers = lax.axis_size(axis)
    pairs = [(i, i + by) for i in range(peers) if 0 <= i + by < peers]
    return lax.ppermute(value, axis, pairs)


def normalize(values, gain, shift):
    average = jnp.mean(values, axis=-1, keepdims=True)
    centered = values - average
    inverse = lax.rsqrt(jnp.mean(centered * centered, axis=-1, keepdims=True) + EPSILON)
    normed = centered * inverse
    return (normed * gain + shift, normed, inverse)


def norm_back(grad_normed, normed, inverse):
    first_mean = jnp.mean(grad_normed, axis=-1, keepdims=True)
    second_mean = jnp.mean(grad_normed * normed, axis=-1, keepdims=True)
    return inverse * (grad_normed - first_mean - normed * second_mean)


def matmul(left, right):
    return jnp.dot(left, right, preferred_element_type=jnp.float32)


def forward(hidden, key_bias, params):
    (
        w_query,
        b_query,
        w_key,
        w_value,
        b_value,
        w_out,
        b_out,
        gain_one,
        shift_one,
        w_up,
        b_up,
        w_down,
        b_down,
        gain_two,
        shift_two,
    ) = params
    count, rows, width = hidden.shape
    head_size = width // HEADS
    scale = 1.0 / math.sqrt(head_size)
    flat_rows = hidden.reshape(count * rows, width)
    query = (matmul(flat_rows, w_query) + b_query).astype(jnp.bfloat16)
    keys = matmul(flat_rows, w_key).astype(jnp.bfloat16)
    values = (matmul(flat_rows, w_value) + b_value).astype(jnp.bfloat16)
    query_heads = query.reshape(count, rows, HEADS, head_size)
    key_heads = keys.reshape(count, rows, HEADS, head_size)
    value_heads = values.reshape(count, rows, HEADS, head_size)
    scores = jnp.einsum(
        "bqhe,bkhe->bhqk", query_heads, key_heads, preferred_element_type=jnp.float32
    )
    scores = scores * scale + key_bias[:, None, None, :]
    row_max = jnp.max(scores, axis=-1, keepdims=True)
    expo = jnp.exp(scores - row_max)
    totals = jnp.sum(expo, axis=-1, keepdims=True)
    probs = (expo / totals).astype(jnp.bfloat16)
    log_total = row_max + jnp.log(totals)
    context = jnp.einsum("bhqk,bkhe->bqhe", probs, value_heads, preferred_element_type=jnp.float32)
    context = context.reshape(count * rows, width).astype(jnp.bfloat16)
    attended = matmul(context, w_out) + b_out
    first, normed_one, inverse_one = normalize(
        flat_rows.astype(jnp.float32) + attended, gain_one, shift_one
    )
    lowered = first.astype(jnp.bfloat16)
    inner = matmul(lowered, w_up) + b_up
    activated = jax.nn.gelu(inner, approximate=False).astype(jnp.bfloat16)
    output = matmul(activated, w_down) + b_down
    second, normed_two, inverse_two = normalize(first + output, gain_two, shift_two)
    result = second.astype(jnp.bfloat16).reshape(count, rows, width)
    state = (
        hidden,
        query,
        keys,
        values,
        log_total,
        context,
        normed_one,
        inverse_one,
        lowered,
        inner,
        activated,
        normed_two,
        inverse_two,
        key_bias,
    )
    return (result, state)


def backward(upstream, state, params):
    (
        w_query,
        b_query,
        w_key,
        w_value,
        b_value,
        w_out,
        b_out,
        gain_one,
        shift_one,
        w_up,
        b_up,
        w_down,
        b_down,
        gain_two,
        shift_two,
    ) = params
    (
        hidden,
        query,
        keys,
        values,
        log_total,
        context,
        normed_one,
        inverse_one,
        lowered,
        inner,
        activated,
        normed_two,
        inverse_two,
        key_bias,
    ) = state
    count, rows, width = hidden.shape
    head_size = width // HEADS
    scale = 1.0 / math.sqrt(head_size)
    flat_rows = hidden.reshape(count * rows, width)
    gradient = upstream.reshape(count * rows, width).astype(jnp.float32)
    d_gain_two = jnp.sum(gradient * normed_two, axis=0)
    d_shift_two = jnp.sum(gradient, axis=0)
    d_res_two = norm_back(gradient * gain_two, normed_two, inverse_two)
    d_output = d_res_two.astype(jnp.bfloat16)
    d_b_down = jnp.sum(d_output.astype(jnp.float32), axis=0)
    d_activated = jnp.einsum("nd,fd->nf", d_output, w_down, preferred_element_type=jnp.float32)
    cdf_part = 0.5 * (1.0 + lax.erf(inner / math.sqrt(2.0)))
    pdf_part = jnp.exp(-0.5 * inner * inner) / math.sqrt(2.0 * math.pi)
    d_inner = (d_activated * (cdf_part + inner * pdf_part)).astype(jnp.bfloat16)
    d_b_up = jnp.sum(d_inner.astype(jnp.float32), axis=0)
    d_first = d_res_two + jnp.einsum("nf,df->nd", d_inner, w_up, preferred_element_type=jnp.float32)
    d_gain_one = jnp.sum(d_first * normed_one, axis=0)
    d_shift_one = jnp.sum(d_first, axis=0)
    d_res_one = norm_back(d_first * gain_one, normed_one, inverse_one)
    d_attended = d_res_one.astype(jnp.bfloat16)
    d_b_out = jnp.sum(d_attended.astype(jnp.float32), axis=0)
    d_context = jnp.einsum("ne,de->nd", d_attended, w_out, preferred_element_type=jnp.float32)
    d_context = d_context.astype(jnp.bfloat16).reshape(count, rows, HEADS, head_size)
    query_heads = query.reshape(count, rows, HEADS, head_size)
    key_heads = keys.reshape(count, rows, HEADS, head_size)
    value_heads = values.reshape(count, rows, HEADS, head_size)
    scores = jnp.einsum(
        "bqhe,bkhe->bhqk", query_heads, key_heads, preferred_element_type=jnp.float32
    )
    scores = scores * scale + key_bias[:, None, None, :]
    probs = jnp.exp(scores - log_total)
    d_values = jnp.einsum(
        "bhqk,bqhe->bkhe", probs.astype(jnp.bfloat16), d_context, preferred_element_type=jnp.float32
    ).astype(jnp.bfloat16)
    d_probs = jnp.einsum(
        "bqhe,bkhe->bhqk", d_context, value_heads, preferred_element_type=jnp.float32
    )
    d_scores = probs * (d_probs - jnp.sum(d_probs * probs, axis=-1, keepdims=True))
    d_scores = d_scores.astype(jnp.bfloat16)
    d_query = (
        (
            jnp.einsum("bhqk,bkhe->bqhe", d_scores, key_heads, preferred_element_type=jnp.float32)
            * scale
        )
        .astype(jnp.bfloat16)
        .reshape(count * rows, width)
    )
    d_keys = (
        (
            jnp.einsum("bhqk,bqhe->bkhe", d_scores, query_heads, preferred_element_type=jnp.float32)
            * scale
        )
        .astype(jnp.bfloat16)
        .reshape(count * rows, width)
    )
    d_values = d_values.reshape(count * rows, width)
    d_b_query = jnp.sum(d_query.astype(jnp.float32), axis=0)
    d_b_value = jnp.sum(d_values.astype(jnp.float32), axis=0)
    d_hidden = (
        d_res_one
        + jnp.einsum("ne,de->nd", d_query, w_query, preferred_element_type=jnp.float32)
        + jnp.einsum("ne,de->nd", d_keys, w_key, preferred_element_type=jnp.float32)
        + jnp.einsum("ne,de->nd", d_values, w_value, preferred_element_type=jnp.float32)
    )
    d_hidden = d_hidden.astype(jnp.bfloat16).reshape(count, rows, width)
    small = jnp.concatenate(
        [
            jnp.stack(
                [
                    d_b_query,
                    d_b_value,
                    d_b_out,
                    d_gain_one,
                    d_shift_one,
                    d_b_down,
                    d_gain_two,
                    d_shift_two,
                ]
            ),
            d_b_up.reshape(-1, width),
        ]
    )
    small = jnp.pad(small, ((0, GROUP - small.shape[0]), (0, 0)))
    a_side = jnp.concatenate([activated, lowered, context, flat_rows], axis=1)
    b_side = jnp.concatenate([d_output, d_inner, d_attended, d_query, d_keys, d_values], axis=1)
    return (d_hidden, a_side, b_side, small)


def body(
    captions,
    regions,
    image_ids,
    caption_lengths,
    cotangent,
    query_weight,
    query_bias,
    key_weight,
    value_weight,
    value_bias,
    out_weight,
    out_bias,
    norm1_gain,
    norm1_bias,
    up_weight,
    up_bias,
    down_weight,
    down_bias,
    norm2_gain,
    norm2_bias,
):
    stacked = (
        query_weight,
        query_bias,
        key_weight,
        value_weight,
        value_bias,
        out_weight,
        out_bias,
        norm1_gain,
        norm1_bias,
        up_weight,
        up_bias,
        down_weight,
        down_bias,
        norm2_gain,
        norm2_bias,
    )
    params = tuple((member[0] for member in stacked))
    section_index = lax.axis_index("section")
    first_section = section_index == 0
    held_images = regions.shape[0]
    table = padded(regions, (("batch", 0),), held_images)
    batch_index = lax.axis_index("batch")
    image_total = held_images * lax.axis_size("batch")
    local_ids = jnp.mod(image_ids - (batch_index - 1) * held_images, image_total)
    count_items, cap_rows, width = captions.shape
    rows_in = jnp.concatenate([captions, table[local_ids]], axis=1)
    total_rows = rows_in.shape[1]
    positions = jnp.arange(total_rows, dtype=jnp.int32)
    live = (positions[None, :] >= cap_rows) | (positions[None, :] < caption_lengths[:, None])
    key_bias = jnp.where(live, 0.0, -1000000000.0).astype(jnp.float32)
    per_micro = count_items // MICRO

    def take(source, index_now):
        return lax.dynamic_slice_in_dim(source, index_now * per_micro, per_micro, 0)

    def place(target, value, index_now, valid):
        chosen = jnp.where(valid, value, take(target, index_now))
        return lax.dynamic_update_slice_in_dim(target, chosen, index_now * per_micro, 0)

    received = jnp.zeros((per_micro, total_rows, width), jnp.bfloat16)
    saved_inputs = jnp.zeros_like(rows_in)
    layer_outputs = jnp.zeros_like(rows_in)
    for tick_index in range(MICRO + 1):
        micro_now = tick_index - section_index
        valid = (micro_now >= 0) & (micro_now < MICRO)
        safe_index = jnp.clip(micro_now, 0, MICRO - 1)
        current = jnp.where(first_section, take(rows_in, safe_index), received)
        result, state = forward(current, take(key_bias, safe_index), params)
        saved_inputs = place(saved_inputs, current, safe_index, valid)
        layer_outputs = place(layer_outputs, result, safe_index, valid)
        if tick_index < MICRO:
            received = shifted(result, "section", 1)
    arriving = jnp.zeros((per_micro, total_rows, width), jnp.bfloat16)
    grad_inputs = jnp.zeros_like(rows_in)
    a_all = jnp.zeros((count_items * total_rows, 7 * width), jnp.bfloat16)
    b_all = jnp.zeros((count_items * total_rows, 9 * width), jnp.bfloat16)
    small_all = jnp.zeros((GROUP, width), jnp.float32)

    def place_rows(target, value, index_now, valid):
        start = index_now * value.shape[0]
        old = lax.dynamic_slice_in_dim(target, start, value.shape[0], 0)
        return lax.dynamic_update_slice_in_dim(target, jnp.where(valid, value, old), start, 0)

    for tick_index in range(MICRO + 1):
        micro_now = tick_index - (1 - section_index)
        valid = (micro_now >= 0) & (micro_now < MICRO)
        safe_index = jnp.clip(micro_now, 0, MICRO - 1)
        upstream = jnp.where(first_section, arriving, take(cotangent, safe_index))
        unused, state = forward(take(saved_inputs, safe_index), take(key_bias, safe_index), params)
        grad_in, a_side, b_side, small = backward(upstream, state, params)
        grad_inputs = place(grad_inputs, grad_in, safe_index, valid)
        if tick_index < MICRO:
            arriving = shifted(grad_in, "section", -1)
        a_all = place_rows(a_all, a_side, safe_index, valid)
        b_all = place_rows(b_all, b_side, safe_index, valid)
        small_all = small_all + jnp.where(valid, small, 0.0)
    sums, small_sums = reduced(a_all, b_all, small_all, lax.axis_size("batch"))
    grads = spread(sums.reshape(-1, width), small_sums, stacked)
    return (layer_outputs[None], grad_inputs[None]) + tuple(grads)


def solution(mesh):
    placed = (
        P("batch", None, None),
        P("batch", None, None),
        P("batch"),
        P("batch"),
        P("batch", None, None),
        P("section", None, None),
        P("section", None),
        P("section", None, None),
        P("section", None, None),
        P("section", None),
        P("section", None, None),
        P("section", None),
        P("section", None),
        P("section", None),
        P("section", None, None),
        P("section", None),
        P("section", None, None),
        P("section", None),
        P("section", None),
        P("section", None),
    )
    return jax.shard_map(
        body,
        mesh=mesh,
        in_specs=placed,
        out_specs=(
            P("section", "batch", None, None),
            P("section", "batch", None, None),
            P("section", None, None),
            P("section", None),
            P("section", None, None),
            P("section", None, None),
            P("section", None),
            P("section", None, None),
            P("section", None),
            P("section", None),
            P("section", None),
            P("section", None, None),
            P("section", None),
            P("section", None, None),
            P("section", None),
            P("section", None),
            P("section", None),
        ),
        check_vma=False,
    )
```

```python
import functools
import math

import jax
import jax.numpy as jnp
from jax import lax
from jax.experimental import pallas as pl
from jax.experimental.pallas import tpu as pltpu
from jax.sharding import PartitionSpec as P

HEADS = 12
EPSILON = 1e-12
MESH = pl.DeviceIdType.MESH
VMEM_LIMIT = 60 * 1024 * 1024
GROUP = 16
CHUNK_GROUPS = 16
SPLIT_BITS = 4
LAG = 2


def local_grad_block(block, third, a_ref, b_ref, width):
    a_col = jnp.minimum(block, 4) + jnp.minimum(block // 8, 1) + jnp.minimum(block // 9, 1)
    b_col = jnp.maximum(block - 3, 0)
    rows = CHUNK_GROUPS * GROUP
    left = a_ref[:, pl.ds(pl.multiple_of(a_col * width + third * rows, rows), rows)]
    right = b_ref[:, pl.ds(pl.multiple_of(b_col * width, width), width)]
    return lax.dot_general(left, right, (((0,), (0,)), ((), ())), preferred_element_type=jnp.float32)


def reduce_kernel(
    bits,
    chunks,
    a_hbm,
    b_hbm,
    small_ref,
    out_hbm,
    small_out,
    a_ref,
    b_ref,
    acc,
    recv,
    recv_extra,
    small_acc,
    small_recv,
    load_sem,
    send_sem,
    recv_sem,
    keep_sem,
    small_send_sem,
    small_recv_sem,
):
    width = acc.shape[2]
    extra = bits - SPLIT_BITS
    stages = 2 * SPLIT_BITS + extra
    me = lax.axis_index("batch")
    section = lax.axis_index("section")

    load_a = pltpu.make_async_copy(a_hbm, a_ref, load_sem.at[0])
    load_b = pltpu.make_async_copy(b_hbm, b_ref, load_sem.at[1])
    load_a.start()
    load_b.start()

    def mate(stride):
        bit = (me // stride) % 2
        return bit, (section, me + stride * (1 - 2 * bit))

    barrier = pltpu.get_barrier_semaphore()
    for k in range(bits):
        pl.semaphore_signal(barrier, inc=1, device_id=mate(2**k)[1], device_id_type=MESH)
    pl.semaphore_wait(barrier, bits)

    def strides(c):
        kind = (c % 4) // 3
        return (1, 2 + 2 * kind, 4 - 2 * kind, 8)

    def offsets(c):
        found = [0]
        half = CHUNK_GROUPS
        for stride in strides(c):
            half = half // 2
            found.append(found[-1] + mate(stride)[0] * half)
        return found

    def scatter_copy(c, k):
        bit, peer = mate(strides(c)[k])
        half = CHUNK_GROUPS >> (k + 1)
        base = CHUNK_GROUPS - 2 * half
        start = c * CHUNK_GROUPS + offsets(c)[k] + (1 - bit) * half
        return pltpu.make_async_remote_copy(
            src_ref=acc.at[pl.ds(start, half)],
            dst_ref=recv.at[c, pl.ds(base, half)],
            send_sem=send_sem.at[c, k],
            recv_sem=recv_sem.at[c, k],
            device_id=peer,
            device_id_type=MESH,
        )

    def extra_copy(c, e):
        start = c * CHUNK_GROUPS + offsets(c)[SPLIT_BITS]
        return pltpu.make_async_remote_copy(
            src_ref=acc.at[pl.ds(start, 1)],
            dst_ref=recv_extra.at[c, pl.ds(e, 1)],
            send_sem=send_sem.at[c, SPLIT_BITS + e],
            recv_sem=recv_sem.at[c, SPLIT_BITS + e],
            device_id=mate(2 ** (SPLIT_BITS + e))[1],
            device_id_type=MESH,
        )

    def keep_copy(c):
        start = c * CHUNK_GROUPS + offsets(c)[SPLIT_BITS]
        return pltpu.make_async_copy(acc.at[pl.ds(start, 1)], out_hbm.at[pl.ds(start, 1)], keep_sem.at[c])

    def gather_copy(c, k):
        peer = mate(strides(c)[k])[1]
        held = CHUNK_GROUPS >> (k + 1)
        start = c * CHUNK_GROUPS + offsets(c)[k + 1]
        source = acc if k == SPLIT_BITS - 1 else out_hbm
        index = SPLIT_BITS + extra + (SPLIT_BITS - 1 - k)
        return pltpu.make_async_remote_copy(
            src_ref=source.at[pl.ds(start, held)],
            dst_ref=out_hbm.at[pl.ds(start, held)],
            send_sem=send_sem.at[c, index],
            recv_sem=recv_sem.at[c, index],
            device_id=peer,
            device_id_type=MESH,
        )

    def add_groups(start, count, c, base, source):
        def one(g, carry):
            total = acc[start + g].astype(jnp.float32) + source[c, base + g].astype(jnp.float32)
            acc[start + g] = total.astype(jnp.bfloat16)
            return carry

        lax.fori_loop(0, count, one, 0)

    def stage_copy(c, s):
        if s < SPLIT_BITS:
            return scatter_copy(c, s)
        if s < SPLIT_BITS + extra:
            return extra_copy(c, s - SPLIT_BITS)
        return gather_copy(c, 2 * SPLIT_BITS + extra - 1 - s)

    def finish_stage(c, s):
        stage_copy(c, s).wait()
        if s < SPLIT_BITS:
            half = CHUNK_GROUPS >> (s + 1)
            add_groups(c * CHUNK_GROUPS + offsets(c)[s + 1], half, c, CHUNK_GROUPS - 2 * half, recv)
        elif s < SPLIT_BITS + extra:
            add_groups(c * CHUNK_GROUPS + offsets(c)[SPLIT_BITS], 1, c, s - SPLIT_BITS, recv_extra)
        elif s == SPLIT_BITS + extra:
            keep_copy(c).wait()

    def small_copy(k):
        return pltpu.make_async_remote_copy(
            src_ref=small_acc.at[k],
            dst_ref=small_recv.at[k],
            send_sem=small_send_sem.at[k],
            recv_sem=small_recv_sem.at[k],
            device_id=mate(2**k)[1],
            device_id_type=MESH,
        )

    load_a.wait()
    load_b.wait()
    small_acc[0] = small_ref[...]

    def step(t, carry):
        for s in range(stages, 0, -1):
            c = t - LAG * s

            @pl.when((c >= 0) & (c < chunks))
            def _():
                finish_stage(c, s - 1)
                if s == SPLIT_BITS + extra:
                    keep_copy(c).start()
                if s < stages:
                    stage_copy(c, s).start()

        @pl.when(t < chunks)
        def _():
            grad = local_grad_block(t // 3, t % 3, a_ref, b_ref, width)
            acc[pl.ds(t * CHUNK_GROUPS, CHUNK_GROUPS)] = grad.astype(jnp.bfloat16).reshape(
                CHUNK_GROUPS, GROUP, width
            )
            stage_copy(t, 0).start()

        for k in range(bits + 1):

            @pl.when(t == LAG * k)
            def _():
                if k > 0:
                    small_copy(k - 1).wait()
                    small_acc[k] = small_acc[k - 1] + small_recv[k - 1]
                if k < bits:
                    small_copy(k).start()

        return carry

    lax.fori_loop(0, chunks + LAG * stages, step, 0)
    small_out[...] = small_acc[bits]


def reduced(a_side, b_side, small, count):
    width = small.shape[1]
    rows = a_side.shape[0]
    bits = count.bit_length() - 1
    extra = bits - SPLIT_BITS
    stages = 2 * SPLIT_BITS + extra
    blocks = 12
    chunks = blocks * width // (CHUNK_GROUPS * GROUP)
    groups = chunks * CHUNK_GROUPS
    return pl.pallas_call(
        functools.partial(reduce_kernel, bits, chunks),
        out_shape=(
            jax.ShapeDtypeStruct((groups, GROUP, width), jnp.bfloat16),
            jax.ShapeDtypeStruct(small.shape, jnp.float32),
        ),
        in_specs=[
            pl.BlockSpec(memory_space=pl.ANY),
            pl.BlockSpec(memory_space=pl.ANY),
            pl.BlockSpec(memory_space=pltpu.VMEM),
        ],
        out_specs=(pl.BlockSpec(memory_space=pl.ANY), pl.BlockSpec(memory_space=pltpu.VMEM)),
        scratch_shapes=[
            pltpu.VMEM(a_side.shape, jnp.bfloat16),
            pltpu.VMEM(b_side.shape, jnp.bfloat16),
            pltpu.VMEM((groups, GROUP, width), jnp.bfloat16),
            pltpu.VMEM((chunks, CHUNK_GROUPS - 1, GROUP, width), jnp.bfloat16),
            pltpu.VMEM((chunks if extra else 1, max(extra, 1), GROUP, width), jnp.bfloat16),
            pltpu.VMEM((bits + 1,) + small.shape, jnp.float32),
            pltpu.VMEM((bits,) + small.shape, jnp.float32),
            pltpu.SemaphoreType.DMA((2,)),
            pltpu.SemaphoreType.DMA((chunks, stages)),
            pltpu.SemaphoreType.DMA((chunks, stages)),
            pltpu.SemaphoreType.DMA((chunks,)),
            pltpu.SemaphoreType.DMA((bits,)),
            pltpu.SemaphoreType.DMA((bits,)),
        ],
        compiler_params=pltpu.CompilerParams(
            collective_id=1, has_side_effects=True, vmem_limit_bytes=VMEM_LIMIT
        ),
        cost_estimate=pl.CostEstimate(
            flops=2 * rows * blocks * width * width, bytes_accessed=80_000_000, transcendentals=0
        ),
    )(a_side, b_side, small)


def spread_kernel(sum_hbm, small_ref, *refs):
    width = small_ref.shape[1]
    outs = refs[:15]
    taken, given, in_sem, out_sem = refs[15:]
    (o_wq, o_bq, o_wk, o_wv, o_bv, o_wo, o_bo, o_g1, o_s1, o_up, o_bu, o_dn, o_bd, o_g2, o_s2) = outs
    wide = o_bu.shape[1] // width
    targets = [o_dn.at[0, pl.ds(j * width, width), :] for j in range(wide)]
    targets += [o_up.at[0, :, pl.ds(j * width, width)] for j in range(wide)]
    targets += [o_wo.at[0], o_wq.at[0], o_wk.at[0], o_wv.at[0]]
    depth = taken.shape[0]

    def load(i):
        return pltpu.make_async_copy(
            sum_hbm.at[pl.ds(i * width, width)], taken.at[i % depth], in_sem.at[i % depth]
        )

    def store(i):
        return pltpu.make_async_copy(given.at[i % depth], targets[i], out_sem.at[i % depth])

    for i in range(depth):
        load(i).start()
    singles = [o_bq, o_bv, o_bo, o_g1, o_s1, o_bd, o_g2, o_s2]
    for i, ref in enumerate(singles):
        ref[...] = small_ref[pl.ds(i, 1), :]
    for j in range(wide):
        o_bu[:, pl.ds(j * width, width)] = small_ref[pl.ds(len(singles) + j, 1), :]
    for i in range(len(targets)):
        load(i).wait()
        if i >= depth:
            store(i - depth).wait()

        def convert(r, carry):
            rows = pl.ds(pl.multiple_of(r * 64, 64), 64)
            given[i % depth, rows, :] = taken[i % depth, rows, :].astype(jnp.float32)
            return carry

        lax.fori_loop(0, width // 64, convert, 0)
        store(i).start()
        if i + depth < len(targets):
            load(i + depth).start()
    for i in range(len(targets) - depth, len(targets)):
        store(i).wait()


def spread(sums, small, params):
    width = small.shape[1]
    depth = 3
    matrices = [len(member.shape) == 3 for member in params]
    return pl.pallas_call(
        spread_kernel,
        out_shape=tuple(jax.ShapeDtypeStruct(member.shape, jnp.float32) for member in params),
        in_specs=[pl.BlockSpec(memory_space=pl.ANY), pl.BlockSpec(memory_space=pltpu.VMEM)],
        out_specs=tuple(
            pl.BlockSpec(memory_space=pl.ANY if matrix else pltpu.VMEM) for matrix in matrices
        ),
        scratch_shapes=[
            pltpu.VMEM((depth, width, width), jnp.bfloat16),
            pltpu.VMEM((depth, width, width), jnp.float32),
            pltpu.SemaphoreType.DMA((depth,)),
            pltpu.SemaphoreType.DMA((depth,)),
        ],
        compiler_params=pltpu.CompilerParams(vmem_limit_bytes=VMEM_LIMIT),
        cost_estimate=pl.CostEstimate(
            flops=12 * width * width, bytes_accessed=72 * width * width, transcendentals=0
        ),
    )(sums, small)


ERF_P = 0.3275911 / math.sqrt(2.0)
ERF_A = (0.254829592, -0.284496736, 1.421413741, -1.453152027, 1.061405429)
SINGLES = ("bq", "bv", "bo", "g1", "s1", "bd", "g2", "s2")


def product(left, right):
    return lax.dot_general(left, right, (((1,), (0,)), ((), ())), preferred_element_type=jnp.float32)


def product_t(left, right):
    return lax.dot_general(left, right, (((1,), (1,)), ((), ())), preferred_element_type=jnp.float32)


def gelu_pair(z):
    bell = jnp.exp(-0.5 * z * z)
    t = pl.reciprocal(1.0 + ERF_P * jnp.abs(z))
    poly = ERF_A[4]
    for a in ERF_A[3::-1]:
        poly = poly * t + a
    half_tail = 0.5 * poly * t * bell
    cdf = jnp.where(z >= 0.0, 1.0 - half_tail, half_tail)
    return z * cdf, cdf + z * bell * (1.0 / math.sqrt(2.0 * math.pi))


def normed(values):
    average = jnp.mean(values, axis=-1, keepdims=True)
    centered = values - average
    inverse = lax.rsqrt(jnp.mean(centered * centered, axis=-1, keepdims=True) + EPSILON)
    return centered * inverse, inverse


def normed_back(grad, normal, inverse):
    first_mean = jnp.mean(grad, axis=-1, keepdims=True)
    second_mean = jnp.mean(grad * normal, axis=-1, keepdims=True)
    return inverse * (grad - first_mean - normal * second_mean)


def layer_kernel(
    ids_ref,
    lengths_ref,
    captions_ref,
    regions_ref,
    cotangent_hbm,
    wq_hbm,
    bq_ref,
    wk_hbm,
    wv_hbm,
    bv_ref,
    wo_hbm,
    bo_ref,
    g1_ref,
    s1_ref,
    wu_hbm,
    bu_ref,
    wd_hbm,
    bd_ref,
    g2_ref,
    s2_ref,
    states_hbm,
    grads_hbm,
    a_hbm,
    b_hbm,
    small_ref,
    wq,
    wk,
    wv,
    wo,
    wu,
    wd,
    table,
    hidden,
    upstream,
    query,
    keys,
    values,
    probs,
    context,
    normal1,
    normal2,
    lowered,
    active,
    slope,
    result,
    grad_in,
    staged,
    inverse1,
    inverse2,
    wide1,
    wide2,
    d_context,
    weight_sem,
    table_send,
    table_recv,
    fwd_send,
    fwd_recv,
    back_send,
    back_recv,
    out_sem,
):
    items, rows, width = hidden.shape
    held = regions_ref.shape[0]
    cap_rows = captions_ref.shape[1]
    wide = wu.shape[1] // width
    pairs = HEADS // 2
    pair_width = width // pairs
    head = width // HEADS
    section = lax.axis_index("section")
    batch = lax.axis_index("batch")
    count = lax.axis_size("batch")
    right = (section, lax.rem(batch + 1, count))
    left = (section, lax.rem(batch + count - 1, count))
    other = (1 - section, batch)

    weight_copies = [
        pltpu.make_async_copy(source.at[0], target, weight_sem.at[n])
        for n, (source, target) in enumerate(
            ((wq_hbm, wq), (wk_hbm, wk), (wv_hbm, wv), (wo_hbm, wo), (wu_hbm, wu), (wd_hbm, wd))
        )
    ]
    for copy in weight_copies:
        copy.start()
    cotangent_copy = pltpu.make_async_copy(cotangent_hbm, upstream, weight_sem.at[6])

    barrier = pltpu.get_barrier_semaphore()
    for peer in (right, left, other):
        pl.semaphore_signal(barrier, inc=1, device_id=peer, device_id_type=MESH)
    pl.semaphore_wait(barrier, 3)

    def table_copy(n, peer):
        return pltpu.make_async_remote_copy(
            src_ref=regions_ref,
            dst_ref=table.at[pl.ds(2 * n * held, held)],
            send_sem=table_send.at[n],
            recv_sem=table_recv.at[n],
            device_id=peer,
            device_id_type=MESH,
        )

    @pl.when(section == 0)
    def _():
        table_copy(0, right).start()
        table_copy(1, left).start()
        table[pl.ds(held, held)] = regions_ref[...]
        table_copy(0, right).wait()
        table_copy(1, left).wait()

    @pl.when(section == 1)
    def _():
        cotangent_copy.start()

    def forward_copy(i):
        return pltpu.make_async_remote_copy(
            src_ref=result.at[i],
            dst_ref=hidden.at[i],
            send_sem=fwd_send.at[i],
            recv_sem=fwd_recv.at[i],
            device_id=other,
            device_id_type=MESH,
        )

    def back_copy(i):
        return pltpu.make_async_remote_copy(
            src_ref=grad_in.at[i],
            dst_ref=upstream.at[i],
            send_sem=back_send.at[i],
            recv_sem=back_recv.at[i],
            device_id=other,
            device_id_type=MESH,
        )

    def saves(i):
        at = pl.ds(pl.multiple_of(i * rows, rows), rows)
        first = wide * width
        sources = (
            (active.at[i], a_hbm.at[at, pl.ds(0, first)]),
            (lowered.at[i], a_hbm.at[at, pl.ds(first, width)]),
            (context.at[i], a_hbm.at[at, pl.ds(first + width, width)]),
            (hidden.at[i], a_hbm.at[at, pl.ds(first + 2 * width, width)]),
            (result.at[i], states_hbm.at[0, i]),
        )
        return [pltpu.make_async_copy(s, d, out_sem.at[i, n]) for n, (s, d) in enumerate(sources)]

    def staged_save(i):
        at = pl.ds(pl.multiple_of(i * rows, rows), rows)
        return pltpu.make_async_copy(staged.at[lax.rem(i, 2)], b_hbm.at[at], out_sem.at[i, 5])

    def grad_save(i):
        return pltpu.make_async_copy(grad_in.at[i], grads_hbm.at[0, i], out_sem.at[i, 6])

    def vector(ref, j=0):
        return ref[:, j * width : (j + 1) * width].astype(jnp.float32)

    lane = lax.broadcasted_iota(jnp.int32, (rows, pair_width), 1)

    def only(block, h):
        return jnp.where((lane // head) == h, block, jnp.zeros_like(block))

    def assemble(i):
        total = count * held
        spot = jnp.minimum(lax.rem(ids_ref[i] - (batch - 1) * held + total, total), 3 * held - 1)
        whole = jnp.concatenate(
            [captions_ref[i].astype(jnp.float32), table[spot].astype(jnp.float32)], axis=0
        )
        hidden[i] = whole.astype(jnp.bfloat16)

    def forward(i):
        @pl.when(i == 0)
        def _():
            for copy in weight_copies[:3]:
                copy.wait()

        source = hidden[i]
        scaled = (product(source, wq[...]) + vector(bq_ref)).astype(jnp.bfloat16)
        query[i] = (scaled.astype(jnp.float32) * (1.0 / math.sqrt(head))).astype(jnp.bfloat16)
        keys[i] = product(source, wk[...]).astype(jnp.bfloat16)
        values[i] = (product(source, wv[...]) + vector(bv_ref)).astype(jnp.bfloat16)
        position = lax.broadcasted_iota(jnp.int32, (rows, 1), 0)
        live = (position >= cap_rows) | (position < lengths_ref[i])
        key_bias = jnp.where(live, 0.0, -1000000000.0)

        for p in range(pairs):
            lanes = slice(p * pair_width, (p + 1) * pair_width)
            q_pair = query[i, :, lanes]
            k_pair = keys[i, :, lanes]
            v_turned = values[i, :, lanes].astype(jnp.float32).T.astype(jnp.bfloat16)
            parts = []
            for h in range(2):
                scores = product_t(only(k_pair, h), q_pair) + key_bias
                expo = jnp.exp(scores - jnp.max(scores, axis=0, keepdims=True))
                share = pl.reciprocal(jnp.sum(expo, axis=0, keepdims=True))
                prob = (expo * share).astype(jnp.bfloat16)
                probs[i, 2 * p + h] = prob
                parts.append(product(v_turned[h * head : (h + 1) * head], prob))
            context[i, :, lanes] = jnp.concatenate(parts, axis=0).T.astype(jnp.bfloat16)

        @pl.when(i == 0)
        def _():
            for copy in weight_copies[3:]:
                copy.wait()

        attended = product(context[i], wo[...]) + vector(bo_ref)
        n1, inv1 = normed(source.astype(jnp.float32) + attended)
        normal1[i] = n1.astype(jnp.bfloat16)
        inverse1[i] = inv1
        first = n1 * vector(g1_ref) + vector(s1_ref)
        lowered[i] = first.astype(jnp.bfloat16)
        wide1[...] = first + vector(bd_ref)
        low = lowered[i]
        for j in range(wide):
            lanes = slice(j * width, (j + 1) * width)
            z = product(low, wu[:, lanes]) + vector(bu_ref, j)
            gelu, slant = gelu_pair(z)
            active[i, :, lanes] = gelu.astype(jnp.bfloat16)
            slope[i, :, lanes] = slant.astype(jnp.bfloat16)
            wide1[...] += product(active[i, :, lanes], wd[lanes, :])
        n2, inv2 = normed(wide1[...])
        normal2[i] = n2.astype(jnp.bfloat16)
        inverse2[i] = inv2
        result[i] = (n2 * vector(g2_ref) + vector(s2_ref)).astype(jnp.bfloat16)

    def add_small(row, value):
        small_ref[row : row + 1, :] += jnp.sum(value, axis=0, keepdims=True)

    def single(name, value):
        add_small(SINGLES.index(name), value)

    def backward(i):
        slot = lax.rem(i, 2)

        def stage(column, value):
            staged[slot, :, column * width : (column + 1) * width] = value

        gradient = upstream[i].astype(jnp.float32)
        n2 = normal2[i].astype(jnp.float32)
        single("g2", gradient * n2)
        single("s2", gradient)
        d_res2 = normed_back(gradient * vector(g2_ref), n2, inverse2[i])
        d_out = d_res2.astype(jnp.bfloat16)
        single("bd", d_out.astype(jnp.float32))
        stage(0, d_out)
        wide1[...] = d_res2
        for j in range(wide):
            lanes = slice(j * width, (j + 1) * width)
            d_active = product_t(d_out, wd[lanes, :])
            d_inner = (d_active * slope[i, :, lanes].astype(jnp.float32)).astype(jnp.bfloat16)
            add_small(len(SINGLES) + j, d_inner.astype(jnp.float32))
            stage(1 + j, d_inner)
            wide1[...] += product_t(d_inner, wu[:, lanes])
        d_first = wide1[...]
        n1 = normal1[i].astype(jnp.float32)
        single("g1", d_first * n1)
        single("s1", d_first)
        d_res1 = normed_back(d_first * vector(g1_ref), n1, inverse1[i])
        wide2[...] = d_res1
        d_att = d_res1.astype(jnp.bfloat16)
        single("bo", d_att.astype(jnp.float32))
        stage(1 + wide, d_att)
        d_context[...] = product_t(d_att, wo[...]).astype(jnp.bfloat16)

        for p in range(pairs):
            lanes = slice(p * pair_width, (p + 1) * pair_width)
            q_pair = query[i, :, lanes]
            k_pair = keys[i, :, lanes]
            v_pair = values[i, :, lanes]
            c_pair = d_context[:, lanes]
            k_turned = k_pair.astype(jnp.float32).T.astype(jnp.bfloat16)
            parts = []
            d_value = jnp.zeros((rows, pair_width), jnp.float32)
            d_key = jnp.zeros((rows, pair_width), jnp.float32)
            for h in range(2):
                prob = probs[i, 2 * p + h]
                d_value += product(prob, only(c_pair, h))
                d_prob = product_t(only(v_pair, h), c_pair)
                wide_prob = prob.astype(jnp.float32)
                drift = jnp.sum(d_prob * wide_prob, axis=0, keepdims=True)
                d_score = (wide_prob * (d_prob - drift)).astype(jnp.bfloat16)
                d_key += product(d_score, only(q_pair, h))
                parts.append(product(k_turned[h * head : (h + 1) * head], d_score))
            d_query = jnp.concatenate(parts, axis=0).T * (1.0 / math.sqrt(head))
            at = p * pair_width
            base = (2 + wide) * width
            for n, block in enumerate((d_query, d_key, d_value)):
                staged[slot, :, base + n * width + at : base + n * width + at + pair_width] = block.astype(
                    jnp.bfloat16
                )
        base = (2 + wide) * width
        d_query = staged[slot, :, base : base + width]
        d_key = staged[slot, :, base + width : base + 2 * width]
        d_value = staged[slot, :, base + 2 * width : base + 3 * width]
        single("bq", d_query.astype(jnp.float32))
        single("bv", d_value.astype(jnp.float32))
        total = wide2[...] + product_t(d_query, wq[...])
        total += product_t(d_key, wk[...])
        total += product_t(d_value, wv[...])
        grad_in[i] = total.astype(jnp.bfloat16)

    small_ref[...] = jnp.zeros_like(small_ref)

    def forward_step(i, carry):
        @pl.when(section == 0)
        def _():
            assemble(i)

        @pl.when(section == 1)
        def _():
            forward_copy(i).wait_recv()

        forward(i)

        @pl.when(section == 0)
        def _():
            forward_copy(i).start()

        for copy in saves(i):
            copy.start()
        return carry

    lax.fori_loop(0, items, forward_step, 0)

    @pl.when(section == 1)
    def _():
        cotangent_copy.wait()

    def backward_step(i, carry):
        @pl.when(section == 0)
        def _():
            back_copy(i).wait_recv()

        @pl.when(i >= 2)
        def _():
            staged_save(i - 2).wait()

        backward(i)

        @pl.when(section == 1)
        def _():
            back_copy(i).start()

        staged_save(i).start()
        grad_save(i).start()
        return carry

    lax.fori_loop(0, items, backward_step, 0)

    def finish(i, carry):
        for copy in saves(i):
            copy.wait()
        grad_save(i).wait()

        @pl.when(i >= items - 2)
        def _():
            staged_save(i).wait()

        @pl.when(section == 0)
        def _():
            forward_copy(i).wait_send()

        @pl.when(section == 1)
        def _():
            back_copy(i).wait_send()

        return carry

    lax.fori_loop(0, items, finish, 0)


def layered(image_ids, caption_lengths, captions, regions, cotangent, stacked):
    items, cap_rows, width = captions.shape
    held, region_rows, _ = regions.shape
    rows = cap_rows + region_rows
    inner = stacked[9].shape[2]
    low = jnp.bfloat16
    wide = inner // width

    def cells(*shape):
        return pltpu.VMEM(shape, low)

    anywhere = pl.BlockSpec(memory_space=pl.ANY)
    local = pl.BlockSpec(memory_space=pltpu.VMEM)
    scalars = pl.BlockSpec(memory_space=pltpu.SMEM)
    return pl.pallas_call(
        layer_kernel,
        out_shape=(
            jax.ShapeDtypeStruct((1, items, rows, width), low),
            jax.ShapeDtypeStruct((1, items, rows, width), low),
            jax.ShapeDtypeStruct((items * rows, (3 + wide) * width), low),
            jax.ShapeDtypeStruct((items * rows, (5 + wide) * width), low),
            jax.ShapeDtypeStruct((GROUP, width), jnp.float32),
        ),
        in_specs=[scalars, scalars, local, local, anywhere]
        + [anywhere if len(member.shape) == 3 else local for member in stacked],
        out_specs=(anywhere, anywhere, anywhere, anywhere, local),
        scratch_shapes=[
            cells(width, width),
            cells(width, width),
            cells(width, width),
            cells(width, width),
            cells(width, inner),
            cells(inner, width),
            cells(3 * held, region_rows, width),
            cells(items, rows, width),
            cells(items, rows, width),
            cells(items, rows, width),
            cells(items, rows, width),
            cells(items, rows, width),
            cells(items, HEADS, rows, rows),
            cells(items, rows, width),
            cells(items, rows, width),
            cells(items, rows, width),
            cells(items, rows, width),
            cells(items, rows, inner),
            cells(items, rows, inner),
            cells(items, rows, width),
            cells(items, rows, width),
            cells(2, rows, (5 + wide) * width),
            pltpu.VMEM((items, rows, 1), jnp.float32),
            pltpu.VMEM((items, rows, 1), jnp.float32),
            pltpu.VMEM((rows, width), jnp.float32),
            pltpu.VMEM((rows, width), jnp.float32),
            cells(rows, width),
            pltpu.SemaphoreType.DMA((7,)),
            pltpu.SemaphoreType.DMA((2,)),
            pltpu.SemaphoreType.DMA((2,)),
            pltpu.SemaphoreType.DMA((items,)),
            pltpu.SemaphoreType.DMA((items,)),
            pltpu.SemaphoreType.DMA((items,)),
            pltpu.SemaphoreType.DMA((items,)),
            pltpu.SemaphoreType.DMA((items, 7)),
        ],
        compiler_params=pltpu.CompilerParams(
            collective_id=0, has_side_effects=True, vmem_limit_bytes=VMEM_LIMIT
        ),
        cost_estimate=pl.CostEstimate(
            flops=4 * items * rows * (4 + 2 * wide) * width * width,
            bytes_accessed=60_000_000,
            transcendentals=0,
        ),
    )(image_ids, caption_lengths, captions, regions, cotangent, *stacked)


def body(
    captions,
    regions,
    image_ids,
    caption_lengths,
    cotangent,
    query_weight,
    query_bias,
    key_weight,
    value_weight,
    value_bias,
    out_weight,
    out_bias,
    norm1_gain,
    norm1_bias,
    up_weight,
    up_bias,
    down_weight,
    down_bias,
    norm2_gain,
    norm2_bias,
):
    stacked = (
        query_weight,
        query_bias,
        key_weight,
        value_weight,
        value_bias,
        out_weight,
        out_bias,
        norm1_gain,
        norm1_bias,
        up_weight,
        up_bias,
        down_weight,
        down_bias,
        norm2_gain,
        norm2_bias,
    )
    width = captions.shape[2]
    states, input_grads, a_side, b_side, small = layered(
        image_ids, caption_lengths, captions, regions, cotangent, stacked
    )
    sums, small_sums = reduced(a_side, b_side, small, lax.axis_size("batch"))
    grads = spread(sums.reshape(-1, width), small_sums, stacked)
    return (states, input_grads) + tuple(grads)


def solution(mesh):
    placed = (
        P("batch", None, None),
        P("batch", None, None),
        P("batch"),
        P("batch"),
        P("batch", None, None),
        P("section", None, None),
        P("section", None),
        P("section", None, None),
        P("section", None, None),
        P("section", None),
        P("section", None, None),
        P("section", None),
        P("section", None),
        P("section", None),
        P("section", None, None),
        P("section", None),
        P("section", None, None),
        P("section", None),
        P("section", None),
        P("section", None),
    )
    return jax.shard_map(
        body,
        mesh=mesh,
        in_specs=placed,
        out_specs=(
            P("section", "batch", None, None),
            P("section", "batch", None, None),
            P("section", None, None),
            P("section", None),
            P("section", None, None),
            P("section", None, None),
            P("section", None),
            P("section", None, None),
            P("section", None),
            P("section", None),
            P("section", None),
            P("section", None, None),
            P("section", None),
            P("section", None, None),
            P("section", None),
            P("section", None),
            P("section", None),
        ),
        check_vma=False,
    )
```

```python
import functools
import math

import jax
import jax.numpy as jnp
from jax import lax
from jax.experimental import pallas as pl
from jax.experimental.pallas import tpu as pltpu
from jax.sharding import PartitionSpec as P

HEADS = 12
EPSILON = 1e-12
MESH = pl.DeviceIdType.MESH
VMEM_LIMIT = 60 * 1024 * 1024
GROUP = 16
CHUNK_GROUPS = 16
SLOTS = 16
SLOT_GROUPS = 24
LAG = 2
LINE = 4
SPLIT_BITS = 4


def reduce_kernel(
    bits,
    chunks,
    a_hbm,
    b_hbm,
    small_ref,
    out_hbm,
    small_out,
    a_ref,
    b_ref,
    acc,
    recv,
    small_acc,
    small_recv,
    load_sem,
    send_sem,
    recv_sem,
    keep_sem,
    small_send_sem,
    small_recv_sem,
):
    width = acc.shape[2]
    extra = bits - SPLIT_BITS
    first_gather = SPLIT_BITS + 1 + extra
    stages = 2 * (SPLIT_BITS + 1) + extra
    me = lax.axis_index("batch")
    section = lax.axis_index("section")
    core, side, place = me % 2, (me // 2) % 2, (me // 4) % LINE
    blocks_a = a_hbm.shape[1] // width
    blocks_b = b_hbm.shape[1] // width
    per_block = width // (CHUNK_GROUPS * GROUP)

    def load(source, target, block, base):
        lanes = pl.ds(block * width, width)
        return pltpu.make_async_copy(source.at[:, lanes], target.at[:, lanes], load_sem.at[base + block])

    def load_a(block):
        return load(a_hbm, a_ref, block, 0)

    def load_b(block):
        return load(b_hbm, b_ref, block, blocks_a)

    wide = blocks_a - 3
    first_use = {0: [(load_a, 0), (load_b, 0)]}
    for j in range(1, wide):
        first_use[j] = [(load_a, j)]
    first_use[wide] = [(load_a, wide), (load_b, 1)]
    for j in range(1, wide):
        first_use[wide + j] = [(load_b, 1 + j)]
    first_use[2 * wide] = [(load_a, wide + 1), (load_b, wide + 1)]
    first_use[2 * wide + 1] = [(load_a, wide + 2), (load_b, wide + 2)]
    first_use[2 * wide + 2] = [(load_b, wide + 3)]
    first_use[2 * wide + 3] = [(load_b, wide + 4)]
    for j in range(2 * wide + 4):
        for kind, block in first_use[j]:
            kind(block).start()

    def bit_mate(k):
        bit = (me // 2**k) % 2
        return (section, me + 2**k * (1 - 2 * bit))

    core_mate, side_mate = bit_mate(0), bit_mate(1)
    mates = ((section, me - LINE), (section, me + LINE))
    ring = [(section, me + LINE * ((place + d) % LINE - place)) for d in (LINE - 1, 1)]

    barrier = pltpu.get_barrier_semaphore()
    for peer in [core_mate, side_mate] + ring + [bit_mate(k) for k in range(2, bits)]:
        pl.semaphore_signal(barrier, inc=1, device_id=peer, device_id_type=MESH)
    pl.semaphore_wait(barrier, bits + 2)

    def kind_of(c):
        return (c % 5) % 2

    def low_core(c):
        return c * CHUNK_GROUPS + core * 8

    def low_side(c):
        return low_core(c) + side * 4

    def block_start(c, kind, b):
        return low_side(c) + b if kind == 0 else low_core(c) + 2 * b

    def final(c, kind):
        return low_side(c) + place if kind == 0 else low_core(c) + 2 * place + side

    def remote(c, source, start, size, target, spot, index, peer):
        return pltpu.make_async_remote_copy(
            src_ref=source.at[pl.ds(start, size)],
            dst_ref=target.at[c % SLOTS, pl.ds(spot, size)] if target is recv else target.at[pl.ds(start, size)],
            send_sem=send_sem.at[c % SLOTS, index],
            recv_sem=recv_sem.at[c % SLOTS, index],
            device_id=peer,
            device_id_type=MESH,
        )

    def core_copy(c):
        return remote(c, acc, c * CHUNK_GROUPS + (1 - core) * 8, 8, recv, 0, 0, core_mate)

    def side_copy(c, kind):
        if kind == 0:
            return remote(c, acc, low_core(c) + (1 - side) * 4, 4, recv, 8, 1, side_mate)
        return remote(c, acc, low_core(c) + 2 * place + (1 - side), 1, recv, 8, 1, side_mate)

    def line_copy(c, kind, r, d):
        size = 1 + kind
        b = jnp.minimum(3 - r + place, 3) if d == 1 else jnp.maximum(r - 3 + place, 0)
        spot = 12 + 2 * (2 * r + d)
        return remote(c, acc, block_start(c, kind, b), size, recv, spot, 2 + 2 * r + d, mates[d])

    def spread_copy(c, kind, r, d):
        size = 1 + kind
        b = jnp.maximum(place - r, 0) if d == 1 else jnp.minimum(place + r, 3)
        source = acc if kind == 0 and r == 0 else out_hbm
        return remote(c, source, block_start(c, kind, b), size, out_hbm, 0, 8 + 2 * r + d, mates[d])

    def side_back_copy(c, kind):
        if kind == 0:
            return remote(c, out_hbm, low_side(c), 4, out_hbm, 0, 14, side_mate)
        return remote(c, acc, final(c, kind), 1, out_hbm, 0, 14, side_mate)

    def core_back_copy(c):
        return remote(c, out_hbm, low_core(c), 8, out_hbm, 0, 15, core_mate)

    def extra_copy(c, kind, e):
        return remote(c, acc, final(c, kind), 1, recv, 24 + e, 16 + e, bit_mate(SPLIT_BITS + e))

    def keep_copy(c, kind):
        at = pl.ds(final(c, kind), 1)
        return pltpu.make_async_copy(acc.at[at], out_hbm.at[at], keep_sem.at[c % SLOTS])

    def add_groups(start, count, c, spot):
        def one(g, carry):
            total = acc[start + g].astype(jnp.float32) + recv[c % SLOTS, spot + g].astype(jnp.float32)
            acc[start + g] = total.astype(jnp.bfloat16)
            return carry

        lax.fori_loop(0, count, one, 0)

    def name_of(kind, s):
        if s == 0:
            return ("core",)
        if s == stages - 1:
            return ("core_back",)
        if s < SPLIT_BITS + 1:
            order = [("side",), ("line", 0), ("line", 1), ("line", 2)]
            order = order if kind == 0 else order[1:] + order[:1]
            return order[s - 1]
        if s < first_gather:
            return ("extra", s - SPLIT_BITS - 1)
        order = [("spread", 0), ("spread", 1), ("spread", 2), ("side_back",)]
        order = order if kind == 0 else order[3:] + order[:3]
        return order[s - first_gather]

    def start_stage(c, kind, s):
        name = name_of(kind, s)
        if s == first_gather:
            keep_copy(c, kind).start()
        if name[0] == "core":
            core_copy(c).start()
        elif name[0] == "side":
            side_copy(c, kind).start()
        elif name[0] == "line":
            r = name[1]
            pl.when(place <= r)(lambda: line_copy(c, kind, r, 1).start())
            pl.when(place >= 3 - r)(lambda: line_copy(c, kind, r, 0).start())
        elif name[0] == "extra":
            extra_copy(c, kind, name[1]).start()
        elif name[0] == "spread":
            r = name[1]
            pl.when((place >= r) & (place <= 2))(lambda: spread_copy(c, kind, r, 1).start())
            pl.when((place >= 1) & (place <= 3 - r))(lambda: spread_copy(c, kind, r, 0).start())
        elif name[0] == "side_back":
            side_back_copy(c, kind).start()
        else:
            core_back_copy(c).start()

    def finish_stage(c, kind, s):
        name = name_of(kind, s)
        if name[0] == "core":
            core_copy(c).wait()
            add_groups(low_core(c), 8, c, 0)
        elif name[0] == "side":
            side_copy(c, kind).wait()
            if kind == 0:
                add_groups(low_side(c), 4, c, 8)
            else:
                add_groups(final(c, kind), 1, c, 8)
        elif name[0] == "line":
            r = name[1]

            @pl.when(place <= r)
            def _():
                line_copy(c, kind, r, 1).wait_send()

            @pl.when(place >= 3 - r)
            def _():
                line_copy(c, kind, r, 0).wait_send()

            @pl.when((place >= 1) & (place <= r + 1))
            def _():
                line_copy(c, kind, r, 1).wait_recv()
                add_groups(block_start(c, kind, 2 - r + place), 1 + kind, c, 12 + 2 * (2 * r + 1))

            @pl.when((place <= 2) & (place >= 2 - r))
            def _():
                line_copy(c, kind, r, 0).wait_recv()
                add_groups(block_start(c, kind, r - 2 + place), 1 + kind, c, 12 + 2 * (2 * r))

        elif name[0] == "extra":
            extra_copy(c, kind, name[1]).wait()
            add_groups(final(c, kind), 1, c, 24 + name[1])
        elif name[0] == "spread":
            r = name[1]
            pl.when((place >= r) & (place <= 2))(lambda: spread_copy(c, kind, r, 1).wait_send())
            pl.when((place >= 1) & (place <= 3 - r))(lambda: spread_copy(c, kind, r, 0).wait_send())
            pl.when(place >= r + 1)(lambda: spread_copy(c, kind, r, 1).wait_recv())
            pl.when(place <= 2 - r)(lambda: spread_copy(c, kind, r, 0).wait_recv())
        elif name[0] == "side_back":
            side_back_copy(c, kind).wait()
        else:
            core_back_copy(c).wait()
        if s == first_gather:
            keep_copy(c, kind).wait()

    def small_copy(k):
        return pltpu.make_async_remote_copy(
            src_ref=small_acc.at[k],
            dst_ref=small_recv.at[k],
            send_sem=small_send_sem.at[k],
            recv_sem=small_recv_sem.at[k],
            device_id=bit_mate(k),
            device_id_type=MESH,
        )

    small_acc[0] = small_ref[...]

    def step(t, carry):
        for s in range(stages, 0, -1):
            c = t - LAG * s
            for kind in range(2):

                @pl.when((c >= 0) & (c < chunks) & (kind_of(c) == kind))
                def _():
                    finish_stage(c, kind, s - 1)
                    if s < stages:
                        start_stage(c, kind, s)

        for j in range(2 * wide + 4):

            @pl.when(t == per_block * j)
            def _():
                for kind, block in first_use[j]:
                    kind(block).wait()

        @pl.when(t < chunks)
        def _():
            block, part = t // per_block, t % per_block
            a_col = jnp.minimum(block, wide) + jnp.minimum(block // (2 * wide), 1) + jnp.minimum(block // (2 * wide + 1), 1)
            b_col = jnp.maximum(block - wide + 1, 0)
            lines = CHUNK_GROUPS * GROUP
            left = a_ref[:, pl.ds(pl.multiple_of(a_col * width + part * lines, lines), lines)]
            right = b_ref[:, pl.ds(pl.multiple_of(b_col * width, width), width)]
            grad = lax.dot_general(left, right, (((0,), (0,)), ((), ())), preferred_element_type=jnp.float32)
            acc[pl.ds(t * CHUNK_GROUPS, CHUNK_GROUPS)] = grad.astype(jnp.bfloat16).reshape(
                CHUNK_GROUPS, GROUP, width
            )
            core_copy(t).start()

        for k in range(bits + 1):

            @pl.when(t == LAG * k)
            def _():
                if k > 0:
                    small_copy(k - 1).wait()
                    small_acc[k] = small_acc[k - 1] + small_recv[k - 1]
                if k < bits:
                    small_copy(k).start()

        return carry

    lax.fori_loop(0, chunks + LAG * stages, step, 0)
    small_out[...] = small_acc[bits]


def reduced(a_side, b_side, small, count):
    rows = a_side.shape[0]
    width = small.shape[1]
    bits = count.bit_length() - 1
    extra = bits - SPLIT_BITS
    blocks = 2 * (a_side.shape[1] // width - 3) + 4
    chunks = blocks * width // (CHUNK_GROUPS * GROUP)
    groups = chunks * CHUNK_GROUPS
    loads = (a_side.shape[1] + b_side.shape[1]) // width
    return pl.pallas_call(
        functools.partial(reduce_kernel, bits, chunks),
        out_shape=(
            jax.ShapeDtypeStruct((groups, GROUP, width), jnp.bfloat16),
            jax.ShapeDtypeStruct(small.shape, jnp.float32),
        ),
        in_specs=[
            pl.BlockSpec(memory_space=pl.ANY),
            pl.BlockSpec(memory_space=pl.ANY),
            pl.BlockSpec(memory_space=pltpu.VMEM),
        ],
        out_specs=(pl.BlockSpec(memory_space=pl.ANY), pl.BlockSpec(memory_space=pltpu.VMEM)),
        scratch_shapes=[
            pltpu.VMEM(a_side.shape, jnp.bfloat16),
            pltpu.VMEM(b_side.shape, jnp.bfloat16),
            pltpu.VMEM((groups, GROUP, width), jnp.bfloat16),
            pltpu.VMEM((SLOTS, SLOT_GROUPS + extra, GROUP, width), jnp.bfloat16),
            pltpu.VMEM((bits + 1,) + small.shape, jnp.float32),
            pltpu.VMEM((bits,) + small.shape, jnp.float32),
            pltpu.SemaphoreType.DMA((loads,)),
            pltpu.SemaphoreType.DMA((SLOTS, 16 + extra)),
            pltpu.SemaphoreType.DMA((SLOTS, 16 + extra)),
            pltpu.SemaphoreType.DMA((SLOTS,)),
            pltpu.SemaphoreType.DMA((bits,)),
            pltpu.SemaphoreType.DMA((bits,)),
        ],
        compiler_params=pltpu.CompilerParams(
            collective_id=1, has_side_effects=True, vmem_limit_bytes=VMEM_LIMIT
        ),
        cost_estimate=pl.CostEstimate(
            flops=2 * rows * blocks * width * width, bytes_accessed=80_000_000, transcendentals=0
        ),
    )(a_side, b_side, small)


def spread_kernel(sum_hbm, small_ref, *refs):
    width = small_ref.shape[1]
    outs = refs[:15]
    taken, given, in_sem, out_sem = refs[15:]
    (o_wq, o_bq, o_wk, o_wv, o_bv, o_wo, o_bo, o_g1, o_s1, o_up, o_bu, o_dn, o_bd, o_g2, o_s2) = outs
    wide = o_bu.shape[1] // width
    targets = [o_dn.at[0, pl.ds(j * width, width), :] for j in range(wide)]
    targets += [o_up.at[0, :, pl.ds(j * width, width)] for j in range(wide)]
    targets += [o_wo.at[0], o_wq.at[0], o_wk.at[0], o_wv.at[0]]
    depth = taken.shape[0]

    def load(i):
        return pltpu.make_async_copy(
            sum_hbm.at[pl.ds(i * width, width)], taken.at[i % depth], in_sem.at[i % depth]
        )

    def store(i):
        return pltpu.make_async_copy(given.at[i % depth], targets[i], out_sem.at[i % depth])

    for i in range(depth):
        load(i).start()
    singles = [o_bq, o_bv, o_bo, o_g1, o_s1, o_bd, o_g2, o_s2]
    for i, ref in enumerate(singles):
        ref[...] = small_ref[pl.ds(i, 1), :]
    for j in range(wide):
        o_bu[:, pl.ds(j * width, width)] = small_ref[pl.ds(len(singles) + j, 1), :]
    for i in range(len(targets)):
        load(i).wait()
        if i >= depth:
            store(i - depth).wait()

        def convert(r, carry):
            rows = pl.ds(pl.multiple_of(r * 64, 64), 64)
            given[i % depth, rows, :] = taken[i % depth, rows, :].astype(jnp.float32)
            return carry

        lax.fori_loop(0, width // 64, convert, 0)
        store(i).start()
        if i + depth < len(targets):
            load(i + depth).start()
    for i in range(len(targets) - depth, len(targets)):
        store(i).wait()


def spread(sums, small, params):
    width = small.shape[1]
    depth = 3
    matrices = [len(member.shape) == 3 for member in params]
    return pl.pallas_call(
        spread_kernel,
        out_shape=tuple(jax.ShapeDtypeStruct(member.shape, jnp.float32) for member in params),
        in_specs=[pl.BlockSpec(memory_space=pl.ANY), pl.BlockSpec(memory_space=pltpu.VMEM)],
        out_specs=tuple(
            pl.BlockSpec(memory_space=pl.ANY if matrix else pltpu.VMEM) for matrix in matrices
        ),
        scratch_shapes=[
            pltpu.VMEM((depth, width, width), jnp.bfloat16),
            pltpu.VMEM((depth, width, width), jnp.float32),
            pltpu.SemaphoreType.DMA((depth,)),
            pltpu.SemaphoreType.DMA((depth,)),
        ],
        compiler_params=pltpu.CompilerParams(vmem_limit_bytes=VMEM_LIMIT),
        cost_estimate=pl.CostEstimate(
            flops=12 * width * width, bytes_accessed=72 * width * width, transcendentals=0
        ),
    )(sums, small)


ERF_P = 0.3275911 / math.sqrt(2.0)
ERF_A = (0.254829592, -0.284496736, 1.421413741, -1.453152027, 1.061405429)
SINGLES = ("bq", "bv", "bo", "g1", "s1", "bd", "g2", "s2")


def product(left, right):
    return lax.dot_general(left, right, (((1,), (0,)), ((), ())), preferred_element_type=jnp.float32)


def product_t(left, right):
    return lax.dot_general(left, right, (((1,), (1,)), ((), ())), preferred_element_type=jnp.float32)


def gelu_pair(z):
    bell = jnp.exp(-0.5 * z * z)
    t = pl.reciprocal(1.0 + ERF_P * jnp.abs(z))
    poly = ERF_A[4]
    for a in ERF_A[3::-1]:
        poly = poly * t + a
    half_tail = 0.5 * poly * t * bell
    cdf = jnp.where(z >= 0.0, 1.0 - half_tail, half_tail)
    return z * cdf, cdf + z * bell * (1.0 / math.sqrt(2.0 * math.pi))


def normed(values):
    average = jnp.mean(values, axis=-1, keepdims=True)
    centered = values - average
    inverse = lax.rsqrt(jnp.mean(centered * centered, axis=-1, keepdims=True) + EPSILON)
    return centered * inverse, inverse


def normed_back(grad, normal, inverse):
    first_mean = jnp.mean(grad, axis=-1, keepdims=True)
    second_mean = jnp.mean(grad * normal, axis=-1, keepdims=True)
    return inverse * (grad - first_mean - normal * second_mean)


def layer_kernel(
    ids_ref,
    lengths_ref,
    captions_ref,
    regions_ref,
    cotangent_hbm,
    wq_hbm,
    bq_ref,
    wk_hbm,
    wv_hbm,
    bv_ref,
    wo_hbm,
    bo_ref,
    g1_ref,
    s1_ref,
    wu_hbm,
    bu_ref,
    wd_hbm,
    bd_ref,
    g2_ref,
    s2_ref,
    states_hbm,
    grads_hbm,
    a_hbm,
    b_hbm,
    small_ref,
    wqkv,
    wo,
    wu,
    wd,
    table,
    hidden,
    upstream,
    query,
    keys,
    values,
    probs,
    context,
    normal1,
    normal2,
    lowered,
    active,
    slope,
    result,
    grad_in,
    staged,
    inverse1,
    inverse2,
    wide1,
    wide2,
    d_context,
    weight_sem,
    table_send,
    table_recv,
    fwd_send,
    fwd_recv,
    back_send,
    back_recv,
    out_sem,
):
    items, rows, width = hidden.shape
    held = regions_ref.shape[0]
    cap_rows = captions_ref.shape[1]
    wide = wu.shape[1] // width
    pairs = HEADS // 2
    pair_width = width // pairs
    head = width // HEADS
    section = lax.axis_index("section")
    batch = lax.axis_index("batch")
    count = lax.axis_size("batch")
    right = (section, lax.rem(batch + 1, count))
    left = (section, lax.rem(batch + count - 1, count))
    other = (1 - section, batch)

    weight_copies = [
        pltpu.make_async_copy(source.at[0], target, weight_sem.at[n])
        for n, (source, target) in enumerate(
            (
                (wq_hbm, wqkv.at[:, pl.ds(0, width)]),
                (wk_hbm, wqkv.at[:, pl.ds(width, width)]),
                (wv_hbm, wqkv.at[:, pl.ds(2 * width, width)]),
                (wo_hbm, wo),
                (wu_hbm, wu),
                (wd_hbm, wd),
            )
        )
    ]
    for copy in weight_copies:
        copy.start()
    cotangent_copy = pltpu.make_async_copy(cotangent_hbm, upstream, weight_sem.at[6])

    barrier = pltpu.get_barrier_semaphore()
    for peer in (right, left, other):
        pl.semaphore_signal(barrier, inc=1, device_id=peer, device_id_type=MESH)
    pl.semaphore_wait(barrier, 3)

    def table_copy(n, peer):
        return pltpu.make_async_remote_copy(
            src_ref=regions_ref,
            dst_ref=table.at[pl.ds(2 * n * held, held)],
            send_sem=table_send.at[n],
            recv_sem=table_recv.at[n],
            device_id=peer,
            device_id_type=MESH,
        )

    @pl.when(section == 0)
    def _():
        table_copy(0, right).start()
        table_copy(1, left).start()
        table[pl.ds(held, held)] = regions_ref[...]
        table_copy(0, right).wait()
        table_copy(1, left).wait()

    @pl.when(section == 1)
    def _():
        cotangent_copy.start()

    def forward_copy(i):
        return pltpu.make_async_remote_copy(
            src_ref=result.at[i],
            dst_ref=hidden.at[i],
            send_sem=fwd_send.at[i],
            recv_sem=fwd_recv.at[i],
            device_id=other,
            device_id_type=MESH,
        )

    def back_copy(i):
        return pltpu.make_async_remote_copy(
            src_ref=grad_in.at[i],
            dst_ref=upstream.at[i],
            send_sem=back_send.at[i],
            recv_sem=back_recv.at[i],
            device_id=other,
            device_id_type=MESH,
        )

    def saves(i):
        at = pl.ds(pl.multiple_of(i * rows, rows), rows)
        first = wide * width
        sources = (
            (active.at[i], a_hbm.at[at, pl.ds(0, first)]),
            (lowered.at[i], a_hbm.at[at, pl.ds(first, width)]),
            (context.at[i], a_hbm.at[at, pl.ds(first + width, width)]),
            (hidden.at[i], a_hbm.at[at, pl.ds(first + 2 * width, width)]),
            (result.at[i], states_hbm.at[0, i]),
        )
        return [pltpu.make_async_copy(s, d, out_sem.at[i, n]) for n, (s, d) in enumerate(sources)]

    def staged_save(i):
        at = pl.ds(pl.multiple_of(i * rows, rows), rows)
        return pltpu.make_async_copy(staged.at[lax.rem(i, 2)], b_hbm.at[at], out_sem.at[i, 5])

    def grad_save(i):
        return pltpu.make_async_copy(grad_in.at[i], grads_hbm.at[0, i], out_sem.at[i, 6])

    def vector(ref, j=0):
        return ref[:, j * width : (j + 1) * width].astype(jnp.float32)

    lane = lax.broadcasted_iota(jnp.int32, (rows, pair_width), 1)

    def only(block, h):
        return jnp.where((lane // head) == h, block, jnp.zeros_like(block))

    def assemble(i):
        total = count * held
        spot = jnp.minimum(lax.rem(ids_ref[i] - (batch - 1) * held + total, total), 3 * held - 1)
        whole = jnp.concatenate(
            [captions_ref[i].astype(jnp.float32), table[spot].astype(jnp.float32)], axis=0
        )
        hidden[i] = whole.astype(jnp.bfloat16)

    def forward(i):
        @pl.when(i == 0)
        def _():
            for copy in weight_copies[:3]:
                copy.wait()

        source = hidden[i]
        mixed = product(source, wqkv[...])
        query[i] = ((mixed[:, :width] + vector(bq_ref)) * (1.0 / math.sqrt(head))).astype(jnp.bfloat16)
        keys[i] = mixed[:, width : 2 * width].astype(jnp.bfloat16)
        values[i] = (mixed[:, 2 * width :] + vector(bv_ref)).astype(jnp.bfloat16)
        position = lax.broadcasted_iota(jnp.int32, (rows, 1), 0)
        live = (position >= cap_rows) | (position < lengths_ref[i])
        key_bias = jnp.where(live, 0.0, -1000000000.0)

        for p in range(pairs):
            lanes = slice(p * pair_width, (p + 1) * pair_width)
            q_pair = query[i, :, lanes]
            k_pair = keys[i, :, lanes]
            v_turned = values[i, :, lanes].astype(jnp.float32).T.astype(jnp.bfloat16)
            parts = []
            both = product_t(jnp.concatenate([only(k_pair, 0), only(k_pair, 1)], axis=0), q_pair)
            for h in range(2):
                scores = both[h * rows : (h + 1) * rows] + key_bias
                expo = jnp.exp(scores - jnp.max(scores, axis=0, keepdims=True))
                share = pl.reciprocal(jnp.sum(expo, axis=0, keepdims=True))
                prob = (expo * share).astype(jnp.bfloat16)
                probs[i, 2 * p + h] = prob
                parts.append(product(v_turned[h * head : (h + 1) * head], prob))
            context[i, :, lanes] = jnp.concatenate(parts, axis=0).T.astype(jnp.bfloat16)

        @pl.when(i == 0)
        def _():
            for copy in weight_copies[3:]:
                copy.wait()

        attended = product(context[i], wo[...]) + vector(bo_ref)
        n1, inv1 = normed(source.astype(jnp.float32) + attended)
        normal1[i] = n1.astype(jnp.bfloat16)
        inverse1[i] = inv1
        first = n1 * vector(g1_ref) + vector(s1_ref)
        lowered[i] = first.astype(jnp.bfloat16)
        wide1[...] = first + vector(bd_ref)
        low = lowered[i]
        tile = 2 * width // 3
        tiles = wide * width // tile

        def raised(n):
            return product(low, wu[:, n * tile : (n + 1) * tile])

        z_next = raised(0)
        half = tiles // 2
        for n in range(tiles):
            lanes = slice(n * tile, (n + 1) * tile)
            z = z_next + bu_ref[:, lanes].astype(jnp.float32)
            if n + 1 < tiles:
                z_next = raised(n + 1)
            if n == half:
                wide1[...] += product(active[i, :, : half * tile], wd[: half * tile, :])
            gelu, slant = gelu_pair(z)
            active[i, :, lanes] = gelu.astype(jnp.bfloat16)
            slope[i, :, lanes] = slant.astype(jnp.bfloat16)
        wide1[...] += product(active[i, :, half * tile :], wd[half * tile :, :])
        n2, inv2 = normed(wide1[...])
        normal2[i] = n2.astype(jnp.bfloat16)
        inverse2[i] = inv2
        result[i] = (n2 * vector(g2_ref) + vector(s2_ref)).astype(jnp.bfloat16)

    def add_small(row, value):
        small_ref[row : row + 1, :] += jnp.sum(value, axis=0, keepdims=True)

    def single(name, value):
        add_small(SINGLES.index(name), value)

    def backward(i):
        slot = lax.rem(i, 2)

        def stage(column, value):
            staged[slot, :, column * width : (column + 1) * width] = value

        gradient = upstream[i].astype(jnp.float32)
        n2 = normal2[i].astype(jnp.float32)
        single("g2", gradient * n2)
        single("s2", gradient)
        d_res2 = normed_back(gradient * vector(g2_ref), n2, inverse2[i])
        d_out = d_res2.astype(jnp.bfloat16)
        single("bd", d_out.astype(jnp.float32))
        stage(0, d_out)
        wide1[...] = d_res2
        for j in range(wide):
            lanes = slice(j * width, (j + 1) * width)
            d_active = product_t(d_out, wd[lanes, :])
            d_inner = (d_active * slope[i, :, lanes].astype(jnp.float32)).astype(jnp.bfloat16)
            add_small(len(SINGLES) + j, d_inner.astype(jnp.float32))
            stage(1 + j, d_inner)
        d_first = wide1[...] + product_t(staged[slot, :, width : (1 + wide) * width], wu[...])
        n1 = normal1[i].astype(jnp.float32)
        single("g1", d_first * n1)
        single("s1", d_first)
        d_res1 = normed_back(d_first * vector(g1_ref), n1, inverse1[i])
        wide2[...] = d_res1
        d_att = d_res1.astype(jnp.bfloat16)
        single("bo", d_att.astype(jnp.float32))
        stage(1 + wide, d_att)
        d_context[...] = product_t(d_att, wo[...]).astype(jnp.bfloat16)

        for p in range(pairs):
            lanes = slice(p * pair_width, (p + 1) * pair_width)
            q_pair = query[i, :, lanes]
            k_pair = keys[i, :, lanes]
            v_pair = values[i, :, lanes]
            c_pair = d_context[:, lanes]
            k_turned = k_pair.astype(jnp.float32).T.astype(jnp.bfloat16)
            parts = []
            d_value = jnp.zeros((rows, pair_width), jnp.float32)
            d_key = jnp.zeros((rows, pair_width), jnp.float32)
            both = product_t(jnp.concatenate([only(v_pair, 0), only(v_pair, 1)], axis=0), c_pair)
            for h in range(2):
                prob = probs[i, 2 * p + h]
                d_value += product(prob, only(c_pair, h))
                d_prob = both[h * rows : (h + 1) * rows]
                wide_prob = prob.astype(jnp.float32)
                drift = jnp.sum(d_prob * wide_prob, axis=0, keepdims=True)
                d_score = (wide_prob * (d_prob - drift)).astype(jnp.bfloat16)
                d_key += product(d_score, only(q_pair, h))
                parts.append(product(k_turned[h * head : (h + 1) * head], d_score))
            d_query = jnp.concatenate(parts, axis=0).T * (1.0 / math.sqrt(head))
            at = p * pair_width
            base = (2 + wide) * width
            for n, block in enumerate((d_query, d_key, d_value)):
                staged[slot, :, base + n * width + at : base + n * width + at + pair_width] = block.astype(
                    jnp.bfloat16
                )
        base = (2 + wide) * width
        single("bq", staged[slot, :, base : base + width].astype(jnp.float32))
        single("bv", staged[slot, :, base + 2 * width : base + 3 * width].astype(jnp.float32))
        total = wide2[...] + product_t(staged[slot, :, base : base + 3 * width], wqkv[...])
        grad_in[i] = total.astype(jnp.bfloat16)

    small_ref[...] = jnp.zeros_like(small_ref)

    def forward_step(i, carry):
        @pl.when(section == 0)
        def _():
            assemble(i)

        @pl.when(section == 1)
        def _():
            forward_copy(i).wait_recv()

        forward(i)

        @pl.when(section == 0)
        def _():
            forward_copy(i).start()

        for copy in saves(i):
            copy.start()
        return carry

    lax.fori_loop(0, items, forward_step, 0)

    @pl.when(section == 1)
    def _():
        cotangent_copy.wait()

    def backward_step(i, carry):
        @pl.when(section == 0)
        def _():
            back_copy(i).wait_recv()

        @pl.when(i >= 2)
        def _():
            staged_save(i - 2).wait()

        backward(i)

        @pl.when(section == 1)
        def _():
            back_copy(i).start()

        staged_save(i).start()
        grad_save(i).start()
        return carry

    lax.fori_loop(0, items, backward_step, 0)

    def finish(i, carry):
        for copy in saves(i):
            copy.wait()
        grad_save(i).wait()

        @pl.when(i >= items - 2)
        def _():
            staged_save(i).wait()

        @pl.when(section == 0)
        def _():
            forward_copy(i).wait_send()

        @pl.when(section == 1)
        def _():
            back_copy(i).wait_send()

        return carry

    lax.fori_loop(0, items, finish, 0)


def layered(image_ids, caption_lengths, captions, regions, cotangent, stacked):
    items, cap_rows, width = captions.shape
    held, region_rows, _ = regions.shape
    rows = cap_rows + region_rows
    inner = stacked[9].shape[2]
    low = jnp.bfloat16
    wide = inner // width

    def cells(*shape):
        return pltpu.VMEM(shape, low)

    anywhere = pl.BlockSpec(memory_space=pl.ANY)
    local = pl.BlockSpec(memory_space=pltpu.VMEM)
    scalars = pl.BlockSpec(memory_space=pltpu.SMEM)
    return pl.pallas_call(
        layer_kernel,
        out_shape=(
            jax.ShapeDtypeStruct((1, items, rows, width), low),
            jax.ShapeDtypeStruct((1, items, rows, width), low),
            jax.ShapeDtypeStruct((items * rows, (3 + wide) * width), low),
            jax.ShapeDtypeStruct((items * rows, (5 + wide) * width), low),
            jax.ShapeDtypeStruct((GROUP, width), jnp.float32),
        ),
        in_specs=[scalars, scalars, local, local, anywhere]
        + [anywhere if len(member.shape) == 3 else local for member in stacked],
        out_specs=(anywhere, anywhere, anywhere, anywhere, local),
        scratch_shapes=[
            cells(width, 3 * width),
            cells(width, width),
            cells(width, inner),
            cells(inner, width),
            cells(3 * held, region_rows, width),
            cells(items, rows, width),
            cells(items, rows, width),
            cells(items, rows, width),
            cells(items, rows, width),
            cells(items, rows, width),
            cells(items, HEADS, rows, rows),
            cells(items, rows, width),
            cells(items, rows, width),
            cells(items, rows, width),
            cells(items, rows, width),
            cells(items, rows, inner),
            cells(items, rows, inner),
            cells(items, rows, width),
            cells(items, rows, width),
            cells(2, rows, (5 + wide) * width),
            pltpu.VMEM((items, rows, 1), jnp.float32),
            pltpu.VMEM((items, rows, 1), jnp.float32),
            pltpu.VMEM((rows, width), jnp.float32),
            pltpu.VMEM((rows, width), jnp.float32),
            cells(rows, width),
            pltpu.SemaphoreType.DMA((7,)),
            pltpu.SemaphoreType.DMA((2,)),
            pltpu.SemaphoreType.DMA((2,)),
            pltpu.SemaphoreType.DMA((items,)),
            pltpu.SemaphoreType.DMA((items,)),
            pltpu.SemaphoreType.DMA((items,)),
            pltpu.SemaphoreType.DMA((items,)),
            pltpu.SemaphoreType.DMA((items, 7)),
        ],
        compiler_params=pltpu.CompilerParams(
            collective_id=0, has_side_effects=True, vmem_limit_bytes=VMEM_LIMIT
        ),
        cost_estimate=pl.CostEstimate(
            flops=4 * items * rows * (4 + 2 * wide) * width * width,
            bytes_accessed=60_000_000,
            transcendentals=0,
        ),
    )(image_ids, caption_lengths, captions, regions, cotangent, *stacked)


def body(
    captions,
    regions,
    image_ids,
    caption_lengths,
    cotangent,
    query_weight,
    query_bias,
    key_weight,
    value_weight,
    value_bias,
    out_weight,
    out_bias,
    norm1_gain,
    norm1_bias,
    up_weight,
    up_bias,
    down_weight,
    down_bias,
    norm2_gain,
    norm2_bias,
):
    stacked = (
        query_weight,
        query_bias,
        key_weight,
        value_weight,
        value_bias,
        out_weight,
        out_bias,
        norm1_gain,
        norm1_bias,
        up_weight,
        up_bias,
        down_weight,
        down_bias,
        norm2_gain,
        norm2_bias,
    )
    width = captions.shape[2]
    states, input_grads, a_side, b_side, small = layered(
        image_ids, caption_lengths, captions, regions, cotangent, stacked
    )
    sums, small_sums = reduced(a_side, b_side, small, lax.axis_size("batch"))
    grads = spread(sums.reshape(-1, width), small_sums, stacked)
    return (states, input_grads) + tuple(grads)


def solution(mesh):
    placed = (
        P("batch", None, None),
        P("batch", None, None),
        P("batch"),
        P("batch"),
        P("batch", None, None),
        P("section", None, None),
        P("section", None),
        P("section", None, None),
        P("section", None, None),
        P("section", None),
        P("section", None, None),
        P("section", None),
        P("section", None),
        P("section", None),
        P("section", None, None),
        P("section", None),
        P("section", None, None),
        P("section", None),
        P("section", None),
        P("section", None),
    )
    return jax.shard_map(
        body,
        mesh=mesh,
        in_specs=placed,
        out_specs=(
            P("section", "batch", None, None),
            P("section", "batch", None, None),
            P("section", None, None),
            P("section", None),
            P("section", None, None),
            P("section", None, None),
            P("section", None),
            P("section", None, None),
            P("section", None),
            P("section", None),
            P("section", None),
            P("section", None, None),
            P("section", None),
            P("section", None, None),
            P("section", None),
            P("section", None),
            P("section", None),
        ),
        check_vma=False,
    )
```

```python
import functools
import math

import jax
import jax.numpy as jnp
from jax import lax
from jax.experimental import pallas as pl
from jax.experimental.pallas import tpu as pltpu
from jax.sharding import PartitionSpec as P

HEADS = 12
EPSILON = 1e-12
MESH = pl.DeviceIdType.MESH
VMEM_LIMIT = 60 * 1024 * 1024
GROUP = 16
CHUNK_GROUPS = 16
SLOTS = 16
SLOT_GROUPS = 24
LAG = 2
LINE = 4
SPLIT_BITS = 4


def reduce_kernel(
    bits,
    chunks,
    a_hbm,
    b_hbm,
    small_ref,
    out_hbm,
    small_out,
    a_ref,
    b_ref,
    acc,
    recv,
    small_acc,
    small_recv,
    load_sem,
    send_sem,
    recv_sem,
    keep_sem,
    small_send_sem,
    small_recv_sem,
):
    width = acc.shape[2]
    extra = bits - SPLIT_BITS
    first_gather = SPLIT_BITS + 1 + extra
    stages = 2 * (SPLIT_BITS + 1) + extra
    me = lax.axis_index("batch")
    section = lax.axis_index("section")
    core, side, place = me % 2, (me // 2) % 2, (me // 4) % LINE
    blocks_a = a_hbm.shape[1] // width
    blocks_b = b_hbm.shape[1] // width
    per_block = width // (CHUNK_GROUPS * GROUP)

    def load(source, target, block, base):
        lanes = pl.ds(block * width, width)
        return pltpu.make_async_copy(source.at[:, lanes], target.at[:, lanes], load_sem.at[base + block])

    def load_a(block):
        return load(a_hbm, a_ref, block, 0)

    def load_b(block):
        return load(b_hbm, b_ref, block, blocks_a)

    wide = blocks_a - 3
    first_use = {0: [(load_a, 0), (load_b, 0)]}
    for j in range(1, wide):
        first_use[j] = [(load_a, j)]
    first_use[wide] = [(load_a, wide), (load_b, 1)]
    for j in range(1, wide):
        first_use[wide + j] = [(load_b, 1 + j)]
    first_use[2 * wide] = [(load_a, wide + 1), (load_b, wide + 1)]
    first_use[2 * wide + 1] = [(load_a, wide + 2), (load_b, wide + 2)]
    first_use[2 * wide + 2] = [(load_b, wide + 3)]
    first_use[2 * wide + 3] = [(load_b, wide + 4)]
    for j in range(2 * wide + 4):
        for kind, block in first_use[j]:
            kind(block).start()

    def bit_mate(k):
        bit = (me // 2**k) % 2
        return (section, me + 2**k * (1 - 2 * bit))

    core_mate, side_mate = bit_mate(0), bit_mate(1)
    mates = ((section, me - LINE), (section, me + LINE))
    ring = [(section, me + LINE * ((place + d) % LINE - place)) for d in (LINE - 1, 1)]

    barrier = pltpu.get_barrier_semaphore()
    for peer in [core_mate, side_mate] + ring + [bit_mate(k) for k in range(2, bits)]:
        pl.semaphore_signal(barrier, inc=1, device_id=peer, device_id_type=MESH)
    pl.semaphore_wait(barrier, bits + 2)

    def kind_of(c):
        return (c % 5) % 2

    def low_core(c):
        return c * CHUNK_GROUPS + core * 8

    def low_side(c):
        return low_core(c) + side * 4

    def block_start(c, kind, b):
        return low_side(c) + b if kind == 0 else low_core(c) + 2 * b

    def final(c, kind):
        return low_side(c) + place if kind == 0 else low_core(c) + 2 * place + side

    def remote(c, source, start, size, target, spot, index, peer):
        return pltpu.make_async_remote_copy(
            src_ref=source.at[pl.ds(start, size)],
            dst_ref=target.at[c % SLOTS, pl.ds(spot, size)] if target is recv else target.at[pl.ds(start, size)],
            send_sem=send_sem.at[c % SLOTS, index],
            recv_sem=recv_sem.at[c % SLOTS, index],
            device_id=peer,
            device_id_type=MESH,
        )

    def core_copy(c):
        return remote(c, acc, c * CHUNK_GROUPS + (1 - core) * 8, 8, recv, 0, 0, core_mate)

    def side_copy(c, kind):
        if kind == 0:
            return remote(c, acc, low_core(c) + (1 - side) * 4, 4, recv, 8, 1, side_mate)
        return remote(c, acc, low_core(c) + 2 * place + (1 - side), 1, recv, 8, 1, side_mate)

    def line_copy(c, kind, r, d):
        size = 1 + kind
        b = jnp.minimum(3 - r + place, 3) if d == 1 else jnp.maximum(r - 3 + place, 0)
        spot = 12 + 2 * (2 * r + d)
        return remote(c, acc, block_start(c, kind, b), size, recv, spot, 2 + 2 * r + d, mates[d])

    def spread_copy(c, kind, r, d):
        size = 1 + kind
        b = jnp.maximum(place - r, 0) if d == 1 else jnp.minimum(place + r, 3)
        source = acc if kind == 0 and r == 0 else out_hbm
        return remote(c, source, block_start(c, kind, b), size, out_hbm, 0, 8 + 2 * r + d, mates[d])

    def side_back_copy(c, kind):
        if kind == 0:
            return remote(c, out_hbm, low_side(c), 4, out_hbm, 0, 14, side_mate)
        return remote(c, acc, final(c, kind), 1, out_hbm, 0, 14, side_mate)

    def core_back_copy(c):
        return remote(c, out_hbm, low_core(c), 8, out_hbm, 0, 15, core_mate)

    def extra_copy(c, kind, e):
        return remote(c, acc, final(c, kind), 1, recv, 24 + e, 16 + e, bit_mate(SPLIT_BITS + e))

    def keep_copy(c, kind):
        at = pl.ds(final(c, kind), 1)
        return pltpu.make_async_copy(acc.at[at], out_hbm.at[at], keep_sem.at[c % SLOTS])

    def add_groups(start, count, c, spot):
        def one(g, carry):
            total = acc[start + g].astype(jnp.float32) + recv[c % SLOTS, spot + g].astype(jnp.float32)
            acc[start + g] = total.astype(jnp.bfloat16)
            return carry

        lax.fori_loop(0, count, one, 0)

    def name_of(kind, s):
        if s == 0:
            return ("core",)
        if s == stages - 1:
            return ("core_back",)
        if s < SPLIT_BITS + 1:
            order = [("side",), ("line", 0), ("line", 1), ("line", 2)]
            order = order if kind == 0 else order[1:] + order[:1]
            return order[s - 1]
        if s < first_gather:
            return ("extra", s - SPLIT_BITS - 1)
        order = [("spread", 0), ("spread", 1), ("spread", 2), ("side_back",)]
        order = order if kind == 0 else order[3:] + order[:3]
        return order[s - first_gather]

    def start_stage(c, kind, s):
        name = name_of(kind, s)
        if s == first_gather:
            keep_copy(c, kind).start()
        if name[0] == "core":
            core_copy(c).start()
        elif name[0] == "side":
            side_copy(c, kind).start()
        elif name[0] == "line":
            r = name[1]
            pl.when(place <= r)(lambda: line_copy(c, kind, r, 1).start())
            pl.when(place >= 3 - r)(lambda: line_copy(c, kind, r, 0).start())
        elif name[0] == "extra":
            extra_copy(c, kind, name[1]).start()
        elif name[0] == "spread":
            r = name[1]
            pl.when((place >= r) & (place <= 2))(lambda: spread_copy(c, kind, r, 1).start())
            pl.when((place >= 1) & (place <= 3 - r))(lambda: spread_copy(c, kind, r, 0).start())
        elif name[0] == "side_back":
            side_back_copy(c, kind).start()
        else:
            core_back_copy(c).start()

    def finish_stage(c, kind, s):
        name = name_of(kind, s)
        if name[0] == "core":
            core_copy(c).wait()
            add_groups(low_core(c), 8, c, 0)
        elif name[0] == "side":
            side_copy(c, kind).wait()
            if kind == 0:
                add_groups(low_side(c), 4, c, 8)
            else:
                add_groups(final(c, kind), 1, c, 8)
        elif name[0] == "line":
            r = name[1]

            @pl.when(place <= r)
            def _():
                line_copy(c, kind, r, 1).wait_send()

            @pl.when(place >= 3 - r)
            def _():
                line_copy(c, kind, r, 0).wait_send()

            @pl.when((place >= 1) & (place <= r + 1))
            def _():
                line_copy(c, kind, r, 1).wait_recv()
                add_groups(block_start(c, kind, 2 - r + place), 1 + kind, c, 12 + 2 * (2 * r + 1))

            @pl.when((place <= 2) & (place >= 2 - r))
            def _():
                line_copy(c, kind, r, 0).wait_recv()
                add_groups(block_start(c, kind, r - 2 + place), 1 + kind, c, 12 + 2 * (2 * r))

        elif name[0] == "extra":
            extra_copy(c, kind, name[1]).wait()
            add_groups(final(c, kind), 1, c, 24 + name[1])
        elif name[0] == "spread":
            r = name[1]
            pl.when((place >= r) & (place <= 2))(lambda: spread_copy(c, kind, r, 1).wait_send())
            pl.when((place >= 1) & (place <= 3 - r))(lambda: spread_copy(c, kind, r, 0).wait_send())
            pl.when(place >= r + 1)(lambda: spread_copy(c, kind, r, 1).wait_recv())
            pl.when(place <= 2 - r)(lambda: spread_copy(c, kind, r, 0).wait_recv())
        elif name[0] == "side_back":
            side_back_copy(c, kind).wait()
        else:
            core_back_copy(c).wait()
        if s == first_gather:
            keep_copy(c, kind).wait()

    def small_copy(k):
        return pltpu.make_async_remote_copy(
            src_ref=small_acc.at[k],
            dst_ref=small_recv.at[k],
            send_sem=small_send_sem.at[k],
            recv_sem=small_recv_sem.at[k],
            device_id=bit_mate(k),
            device_id_type=MESH,
        )

    small_acc[0] = small_ref[...]

    def step(t, carry):
        for s in range(stages, 0, -1):
            c = t - LAG * s
            for kind in range(2):

                @pl.when((c >= 0) & (c < chunks) & (kind_of(c) == kind))
                def _():
                    finish_stage(c, kind, s - 1)
                    if s < stages:
                        start_stage(c, kind, s)

        for j in range(2 * wide + 4):

            @pl.when(t == per_block * j)
            def _():
                for kind, block in first_use[j]:
                    kind(block).wait()

        @pl.when(t < chunks)
        def _():
            block, part = t // per_block, t % per_block
            a_col = jnp.minimum(block, wide) + jnp.minimum(block // (2 * wide), 1) + jnp.minimum(block // (2 * wide + 1), 1)
            b_col = jnp.maximum(block - wide + 1, 0)
            lines = CHUNK_GROUPS * GROUP
            left = a_ref[:, pl.ds(pl.multiple_of(a_col * width + part * lines, lines), lines)]
            right = b_ref[:, pl.ds(pl.multiple_of(b_col * width, width), width)]
            grad = lax.dot_general(left, right, (((0,), (0,)), ((), ())), preferred_element_type=jnp.float32)
            acc[pl.ds(t * CHUNK_GROUPS, CHUNK_GROUPS)] = grad.astype(jnp.bfloat16).reshape(
                CHUNK_GROUPS, GROUP, width
            )
            core_copy(t).start()

        for k in range(bits + 1):

            @pl.when(t == LAG * k)
            def _():
                if k > 0:
                    small_copy(k - 1).wait()
                    small_acc[k] = small_acc[k - 1] + small_recv[k - 1]
                if k < bits:
                    small_copy(k).start()

        return carry

    lax.fori_loop(0, chunks + LAG * stages, step, 0)
    small_out[...] = small_acc[bits]


def reduced(a_side, b_side, small, count):
    rows = a_side.shape[0]
    width = small.shape[1]
    bits = count.bit_length() - 1
    extra = bits - SPLIT_BITS
    blocks = 2 * (a_side.shape[1] // width - 3) + 4
    chunks = blocks * width // (CHUNK_GROUPS * GROUP)
    groups = chunks * CHUNK_GROUPS
    loads = (a_side.shape[1] + b_side.shape[1]) // width
    return pl.pallas_call(
        functools.partial(reduce_kernel, bits, chunks),
        out_shape=(
            jax.ShapeDtypeStruct((groups, GROUP, width), jnp.bfloat16),
            jax.ShapeDtypeStruct(small.shape, jnp.float32),
        ),
        in_specs=[
            pl.BlockSpec(memory_space=pl.ANY),
            pl.BlockSpec(memory_space=pl.ANY),
            pl.BlockSpec(memory_space=pltpu.VMEM),
        ],
        out_specs=(pl.BlockSpec(memory_space=pl.ANY), pl.BlockSpec(memory_space=pltpu.VMEM)),
        scratch_shapes=[
            pltpu.VMEM(a_side.shape, jnp.bfloat16),
            pltpu.VMEM(b_side.shape, jnp.bfloat16),
            pltpu.VMEM((groups, GROUP, width), jnp.bfloat16),
            pltpu.VMEM((SLOTS, SLOT_GROUPS + extra, GROUP, width), jnp.bfloat16),
            pltpu.VMEM((bits + 1,) + small.shape, jnp.float32),
            pltpu.VMEM((bits,) + small.shape, jnp.float32),
            pltpu.SemaphoreType.DMA((loads,)),
            pltpu.SemaphoreType.DMA((SLOTS, 16 + extra)),
            pltpu.SemaphoreType.DMA((SLOTS, 16 + extra)),
            pltpu.SemaphoreType.DMA((SLOTS,)),
            pltpu.SemaphoreType.DMA((bits,)),
            pltpu.SemaphoreType.DMA((bits,)),
        ],
        compiler_params=pltpu.CompilerParams(
            collective_id=1, has_side_effects=True, vmem_limit_bytes=VMEM_LIMIT
        ),
        cost_estimate=pl.CostEstimate(
            flops=2 * rows * blocks * width * width, bytes_accessed=80_000_000, transcendentals=0
        ),
    )(a_side, b_side, small)


def spread_kernel(sum_hbm, small_ref, *refs):
    width = small_ref.shape[1]
    outs = refs[:15]
    taken, given, in_sem, out_sem = refs[15:]
    (o_wq, o_bq, o_wk, o_wv, o_bv, o_wo, o_bo, o_g1, o_s1, o_up, o_bu, o_dn, o_bd, o_g2, o_s2) = outs
    wide = o_bu.shape[1] // width
    targets = [o_dn.at[0, pl.ds(j * width, width), :] for j in range(wide)]
    targets += [o_up.at[0, :, pl.ds(j * width, width)] for j in range(wide)]
    targets += [o_wo.at[0], o_wq.at[0], o_wk.at[0], o_wv.at[0]]
    depth = taken.shape[0]

    def load(i):
        return pltpu.make_async_copy(
            sum_hbm.at[pl.ds(i * width, width)], taken.at[i % depth], in_sem.at[i % depth]
        )

    def store(i):
        return pltpu.make_async_copy(given.at[i % depth], targets[i], out_sem.at[i % depth])

    for i in range(depth):
        load(i).start()
    singles = [o_bq, o_bv, o_bo, o_g1, o_s1, o_bd, o_g2, o_s2]
    for i, ref in enumerate(singles):
        ref[...] = small_ref[pl.ds(i, 1), :]
    for j in range(wide):
        o_bu[:, pl.ds(j * width, width)] = small_ref[pl.ds(len(singles) + j, 1), :]
    for i in range(len(targets)):
        load(i).wait()
        if i >= depth:
            store(i - depth).wait()

        def convert(r, carry):
            rows = pl.ds(pl.multiple_of(r * 64, 64), 64)
            given[i % depth, rows, :] = taken[i % depth, rows, :].astype(jnp.float32)
            return carry

        lax.fori_loop(0, width // 64, convert, 0)
        store(i).start()
        if i + depth < len(targets):
            load(i + depth).start()
    for i in range(len(targets) - depth, len(targets)):
        store(i).wait()


def spread(sums, small, params):
    width = small.shape[1]
    depth = 3
    matrices = [len(member.shape) == 3 for member in params]
    return pl.pallas_call(
        spread_kernel,
        out_shape=tuple(jax.ShapeDtypeStruct(member.shape, jnp.float32) for member in params),
        in_specs=[pl.BlockSpec(memory_space=pl.ANY), pl.BlockSpec(memory_space=pltpu.VMEM)],
        out_specs=tuple(
            pl.BlockSpec(memory_space=pl.ANY if matrix else pltpu.VMEM) for matrix in matrices
        ),
        scratch_shapes=[
            pltpu.VMEM((depth, width, width), jnp.bfloat16),
            pltpu.VMEM((depth, width, width), jnp.float32),
            pltpu.SemaphoreType.DMA((depth,)),
            pltpu.SemaphoreType.DMA((depth,)),
        ],
        compiler_params=pltpu.CompilerParams(vmem_limit_bytes=VMEM_LIMIT),
        cost_estimate=pl.CostEstimate(
            flops=12 * width * width, bytes_accessed=72 * width * width, transcendentals=0
        ),
    )(sums, small)


SINGLES = ("bq", "bv", "bo", "g1", "s1", "bd", "g2", "s2")


def product(left, right):
    return lax.dot_general(left, right, (((1,), (0,)), ((), ())), preferred_element_type=jnp.float32)


def product_t(left, right):
    return lax.dot_general(left, right, (((1,), (1,)), ((), ())), preferred_element_type=jnp.float32)


def gelu_pair(z):
    cdf = 0.5 + 0.5 * lax.erf(z * (1.0 / math.sqrt(2.0)))
    bell = jnp.exp(-0.5 * z * z)
    return z * cdf, cdf + z * bell * (1.0 / math.sqrt(2.0 * math.pi))


def normed(values):
    average = jnp.mean(values, axis=-1, keepdims=True)
    centered = values - average
    inverse = lax.rsqrt(jnp.mean(centered * centered, axis=-1, keepdims=True) + EPSILON)
    return centered * inverse, inverse


def normed_back(grad, normal, inverse):
    first_mean = jnp.mean(grad, axis=-1, keepdims=True)
    second_mean = jnp.mean(grad * normal, axis=-1, keepdims=True)
    return inverse * (grad - first_mean - normal * second_mean)


def layer_kernel(
    ids_ref,
    lengths_ref,
    captions_ref,
    regions_ref,
    cotangent_hbm,
    wq_hbm,
    bq_ref,
    wk_hbm,
    wv_hbm,
    bv_ref,
    wo_hbm,
    bo_ref,
    g1_ref,
    s1_ref,
    wu_hbm,
    bu_ref,
    wd_hbm,
    bd_ref,
    g2_ref,
    s2_ref,
    states_hbm,
    grads_hbm,
    a_hbm,
    b_hbm,
    small_ref,
    wqkv,
    wo,
    wu,
    wd,
    table,
    hidden,
    upstream,
    query,
    keys,
    values,
    probs,
    context,
    normal1,
    normal2,
    lowered,
    active,
    slope,
    result,
    grad_in,
    staged,
    inverse1,
    inverse2,
    wide1,
    wide2,
    d_context,
    weight_sem,
    table_send,
    table_recv,
    fwd_send,
    fwd_recv,
    back_send,
    back_recv,
    out_sem,
):
    items, rows, width = hidden.shape
    held = regions_ref.shape[0]
    cap_rows = captions_ref.shape[1]
    wide = wu.shape[1] // width
    pairs = HEADS // 2
    pair_width = width // pairs
    head = width // HEADS
    section = lax.axis_index("section")
    batch = lax.axis_index("batch")
    count = lax.axis_size("batch")
    right = (section, lax.rem(batch + 1, count))
    left = (section, lax.rem(batch + count - 1, count))
    other = (1 - section, batch)

    weight_copies = [
        pltpu.make_async_copy(source.at[0], target, weight_sem.at[n])
        for n, (source, target) in enumerate(
            (
                (wq_hbm, wqkv.at[:, pl.ds(0, width)]),
                (wk_hbm, wqkv.at[:, pl.ds(width, width)]),
                (wv_hbm, wqkv.at[:, pl.ds(2 * width, width)]),
                (wo_hbm, wo),
                (wu_hbm, wu),
                (wd_hbm, wd),
            )
        )
    ]
    for copy in weight_copies:
        copy.start()
    cotangent_copy = pltpu.make_async_copy(cotangent_hbm, upstream, weight_sem.at[6])

    barrier = pltpu.get_barrier_semaphore()
    for peer in (right, left, other):
        pl.semaphore_signal(barrier, inc=1, device_id=peer, device_id_type=MESH)
    pl.semaphore_wait(barrier, 3)

    def table_copy(n, peer):
        return pltpu.make_async_remote_copy(
            src_ref=regions_ref,
            dst_ref=table.at[pl.ds(2 * n * held, held)],
            send_sem=table_send.at[n],
            recv_sem=table_recv.at[n],
            device_id=peer,
            device_id_type=MESH,
        )

    @pl.when(section == 0)
    def _():
        table_copy(0, right).start()
        table_copy(1, left).start()
        table[pl.ds(held, held)] = regions_ref[...]
        table_copy(0, right).wait()
        table_copy(1, left).wait()

    @pl.when(section == 1)
    def _():
        cotangent_copy.start()

    def forward_copy(i):
        return pltpu.make_async_remote_copy(
            src_ref=result.at[i],
            dst_ref=hidden.at[i],
            send_sem=fwd_send.at[i],
            recv_sem=fwd_recv.at[i],
            device_id=other,
            device_id_type=MESH,
        )

    def back_copy(i):
        return pltpu.make_async_remote_copy(
            src_ref=grad_in.at[i],
            dst_ref=upstream.at[i],
            send_sem=back_send.at[i],
            recv_sem=back_recv.at[i],
            device_id=other,
            device_id_type=MESH,
        )

    def saves(i):
        at = pl.ds(pl.multiple_of(i * rows, rows), rows)
        first = wide * width
        sources = (
            (active.at[i], a_hbm.at[at, pl.ds(0, first)]),
            (lowered.at[i], a_hbm.at[at, pl.ds(first, width)]),
            (context.at[i], a_hbm.at[at, pl.ds(first + width, width)]),
            (hidden.at[i], a_hbm.at[at, pl.ds(first + 2 * width, width)]),
            (result.at[i], states_hbm.at[0, i]),
        )
        return [pltpu.make_async_copy(s, d, out_sem.at[i, n]) for n, (s, d) in enumerate(sources)]

    def staged_save(i):
        at = pl.ds(pl.multiple_of(i * rows, rows), rows)
        return pltpu.make_async_copy(staged.at[lax.rem(i, 2)], b_hbm.at[at], out_sem.at[i, 5])

    def grad_save(i):
        return pltpu.make_async_copy(grad_in.at[i], grads_hbm.at[0, i], out_sem.at[i, 6])

    def vector(ref, j=0):
        return ref[:, j * width : (j + 1) * width].astype(jnp.float32)

    lane = lax.broadcasted_iota(jnp.int32, (rows, pair_width), 1)

    def only(block, h):
        return jnp.where((lane // head) == h, block, jnp.zeros_like(block))

    def assemble(i):
        total = count * held
        spot = jnp.minimum(lax.rem(ids_ref[i] - (batch - 1) * held + total, total), 3 * held - 1)
        whole = jnp.concatenate(
            [captions_ref[i].astype(jnp.float32), table[spot].astype(jnp.float32)], axis=0
        )
        hidden[i] = whole.astype(jnp.bfloat16)

    def forward(i):
        @pl.when(i == 0)
        def _():
            for copy in weight_copies[:3]:
                copy.wait()

        source = hidden[i]
        mixed = product(source, wqkv[...])
        query[i] = ((mixed[:, :width] + vector(bq_ref)) * (1.0 / math.sqrt(head))).astype(jnp.bfloat16)
        keys[i] = mixed[:, width : 2 * width].astype(jnp.bfloat16)
        values[i] = (mixed[:, 2 * width :] + vector(bv_ref)).astype(jnp.bfloat16)
        position = lax.broadcasted_iota(jnp.int32, (rows, 1), 0)
        live = (position >= cap_rows) | (position < lengths_ref[i])
        key_bias = jnp.where(live, 0.0, -1000000000.0)

        def lanes_of(p):
            return slice(p * pair_width, (p + 1) * pair_width)

        def scored(p):
            k_pair = keys[i, :, lanes_of(p)]
            stacked = jnp.concatenate([only(k_pair, 0), only(k_pair, 1)], axis=0)
            v_turned = values[i, :, lanes_of(p)].astype(jnp.float32).T.astype(jnp.bfloat16)
            return product_t(stacked, query[i, :, lanes_of(p)]), v_turned

        def weighed(p, both):
            for h in range(2):
                scores = both[h * rows : (h + 1) * rows] + key_bias
                expo = jnp.exp(scores - jnp.max(scores, axis=0, keepdims=True))
                share = pl.reciprocal(jnp.sum(expo, axis=0, keepdims=True))
                probs[i, 2 * p + h] = (expo * share).astype(jnp.bfloat16)

        def mixed_values(p, v_turned):
            return [product(v_turned[h * head : (h + 1) * head], probs[i, 2 * p + h]) for h in range(2)]

        def place_context(p, parts):
            context[i, :, lanes_of(p)] = jnp.concatenate(parts, axis=0).T.astype(jnp.bfloat16)

        ahead = scored(0)
        parts = None
        for p in range(pairs):
            both, v_turned = ahead
            if p + 1 < pairs:
                ahead = scored(p + 1)
            if parts is not None:
                place_context(p - 1, parts)
            weighed(p, both)
            parts = mixed_values(p, v_turned)
        place_context(pairs - 1, parts)

        @pl.when(i == 0)
        def _():
            for copy in weight_copies[3:]:
                copy.wait()

        attended = product(context[i], wo[...]) + vector(bo_ref)
        n1, inv1 = normed(source.astype(jnp.float32) + attended)
        normal1[i] = n1.astype(jnp.bfloat16)
        inverse1[i] = inv1
        first = n1 * vector(g1_ref) + vector(s1_ref)
        lowered[i] = first.astype(jnp.bfloat16)
        wide1[...] = first + vector(bd_ref)
        low = lowered[i]
        tile = 2 * width // 3
        tiles = wide * width // tile

        def raised(n):
            return product(low, wu[:, n * tile : (n + 1) * tile])

        z_next = raised(0)
        half = tiles // 2
        for n in range(tiles):
            lanes = slice(n * tile, (n + 1) * tile)
            z = z_next + bu_ref[:, lanes].astype(jnp.float32)
            if n + 1 < tiles:
                z_next = raised(n + 1)
            if n == half:
                wide1[...] += product(active[i, :, : half * tile], wd[: half * tile, :])
            gelu, slant = gelu_pair(z)
            active[i, :, lanes] = gelu.astype(jnp.bfloat16)
            slope[i, :, lanes] = slant.astype(jnp.bfloat16)
        wide1[...] += product(active[i, :, half * tile :], wd[half * tile :, :])
        n2, inv2 = normed(wide1[...])
        normal2[i] = n2.astype(jnp.bfloat16)
        inverse2[i] = inv2
        result[i] = (n2 * vector(g2_ref) + vector(s2_ref)).astype(jnp.bfloat16)

    def add_small(row, value):
        small_ref[row : row + 1, :] += jnp.sum(value, axis=0, keepdims=True)

    def single(name, value):
        add_small(SINGLES.index(name), value)

    def backward(i):
        slot = lax.rem(i, 2)

        def stage(column, value):
            staged[slot, :, column * width : (column + 1) * width] = value

        gradient = upstream[i].astype(jnp.float32)
        n2 = normal2[i].astype(jnp.float32)
        single("g2", gradient * n2)
        single("s2", gradient)
        d_res2 = normed_back(gradient * vector(g2_ref), n2, inverse2[i])
        d_out = d_res2.astype(jnp.bfloat16)
        single("bd", d_out.astype(jnp.float32))
        stage(0, d_out)
        wide1[...] = d_res2
        for j in range(wide):
            lanes = slice(j * width, (j + 1) * width)
            d_active = product_t(d_out, wd[lanes, :])
            d_inner = (d_active * slope[i, :, lanes].astype(jnp.float32)).astype(jnp.bfloat16)
            add_small(len(SINGLES) + j, d_inner.astype(jnp.float32))
            stage(1 + j, d_inner)
        d_first = wide1[...] + product_t(staged[slot, :, width : (1 + wide) * width], wu[...])
        n1 = normal1[i].astype(jnp.float32)
        single("g1", d_first * n1)
        single("s1", d_first)
        d_res1 = normed_back(d_first * vector(g1_ref), n1, inverse1[i])
        wide2[...] = d_res1
        d_att = d_res1.astype(jnp.bfloat16)
        single("bo", d_att.astype(jnp.float32))
        stage(1 + wide, d_att)
        d_context[...] = product_t(d_att, wo[...]).astype(jnp.bfloat16)

        base = (2 + wide) * width

        def lanes_of(p):
            return slice(p * pair_width, (p + 1) * pair_width)

        def place_grad(n, p, block):
            at = base + n * width + p * pair_width
            staged[slot, :, at : at + pair_width] = block.astype(jnp.bfloat16)

        def opened(p):
            v_pair = values[i, :, lanes_of(p)]
            c_pair = d_context[:, lanes_of(p)]
            stacked = jnp.concatenate([only(v_pair, 0), only(v_pair, 1)], axis=0)
            k_turned = keys[i, :, lanes_of(p)].astype(jnp.float32).T.astype(jnp.bfloat16)
            d_value = product(probs[i, 2 * p], only(c_pair, 0))
            d_value += product(probs[i, 2 * p + 1], only(c_pair, 1))
            return product_t(stacked, c_pair), k_turned, d_value

        def score_grads(p, both):
            found = []
            for h in range(2):
                prob = probs[i, 2 * p + h].astype(jnp.float32)
                d_prob = both[h * rows : (h + 1) * rows]
                drift = jnp.sum(d_prob * prob, axis=0, keepdims=True)
                found.append((prob * (d_prob - drift)).astype(jnp.bfloat16))
            return found

        def closed(p, found, k_turned):
            q_pair = query[i, :, lanes_of(p)]
            d_key = product(found[0], only(q_pair, 0)) + product(found[1], only(q_pair, 1))
            return d_key, [product(k_turned[h * head : (h + 1) * head], found[h]) for h in range(2)]

        def place_grads(p, d_value, d_key, parts):
            place_grad(0, p, jnp.concatenate(parts, axis=0).T * (1.0 / math.sqrt(head)))
            place_grad(1, p, d_key)
            place_grad(2, p, d_value)

        ahead = opened(0)
        waiting = None
        for p in range(pairs):
            both, k_turned, d_value = ahead
            if p + 1 < pairs:
                ahead = opened(p + 1)
            if waiting is not None:
                place_grads(*waiting)
            found = score_grads(p, both)
            d_key, parts = closed(p, found, k_turned)
            waiting = (p, d_value, d_key, parts)
        place_grads(*waiting)
        single("bq", staged[slot, :, base : base + width].astype(jnp.float32))
        single("bv", staged[slot, :, base + 2 * width : base + 3 * width].astype(jnp.float32))
        total = wide2[...] + product_t(staged[slot, :, base : base + 3 * width], wqkv[...])
        grad_in[i] = total.astype(jnp.bfloat16)

    small_ref[...] = jnp.zeros_like(small_ref)

    def forward_step(i, carry):
        @pl.when(section == 0)
        def _():
            assemble(i)

        @pl.when(section == 1)
        def _():
            forward_copy(i).wait_recv()

        forward(i)

        @pl.when(section == 0)
        def _():
            forward_copy(i).start()

        for copy in saves(i):
            copy.start()
        return carry

    lax.fori_loop(0, items, forward_step, 0)

    @pl.when(section == 1)
    def _():
        cotangent_copy.wait()

    def backward_step(i, carry):
        @pl.when(section == 0)
        def _():
            back_copy(i).wait_recv()

        @pl.when(i >= 2)
        def _():
            staged_save(i - 2).wait()

        backward(i)

        @pl.when(section == 1)
        def _():
            back_copy(i).start()

        staged_save(i).start()
        grad_save(i).start()
        return carry

    lax.fori_loop(0, items, backward_step, 0)

    def finish(i, carry):
        for copy in saves(i):
            copy.wait()
        grad_save(i).wait()

        @pl.when(i >= items - 2)
        def _():
            staged_save(i).wait()

        @pl.when(section == 0)
        def _():
            forward_copy(i).wait_send()

        @pl.when(section == 1)
        def _():
            back_copy(i).wait_send()

        return carry

    lax.fori_loop(0, items, finish, 0)


def layered(image_ids, caption_lengths, captions, regions, cotangent, stacked):
    items, cap_rows, width = captions.shape
    held, region_rows, _ = regions.shape
    rows = cap_rows + region_rows
    inner = stacked[9].shape[2]
    low = jnp.bfloat16
    wide = inner // width

    def cells(*shape):
        return pltpu.VMEM(shape, low)

    anywhere = pl.BlockSpec(memory_space=pl.ANY)
    local = pl.BlockSpec(memory_space=pltpu.VMEM)
    scalars = pl.BlockSpec(memory_space=pltpu.SMEM)
    return pl.pallas_call(
        layer_kernel,
        out_shape=(
            jax.ShapeDtypeStruct((1, items, rows, width), low),
            jax.ShapeDtypeStruct((1, items, rows, width), low),
            jax.ShapeDtypeStruct((items * rows, (3 + wide) * width), low),
            jax.ShapeDtypeStruct((items * rows, (5 + wide) * width), low),
            jax.ShapeDtypeStruct((GROUP, width), jnp.float32),
        ),
        in_specs=[scalars, scalars, local, local, anywhere]
        + [anywhere if len(member.shape) == 3 else local for member in stacked],
        out_specs=(anywhere, anywhere, anywhere, anywhere, local),
        scratch_shapes=[
            cells(width, 3 * width),
            cells(width, width),
            cells(width, inner),
            cells(inner, width),
            cells(3 * held, region_rows, width),
            cells(items, rows, width),
            cells(items, rows, width),
            cells(items, rows, width),
            cells(items, rows, width),
            cells(items, rows, width),
            cells(items, HEADS, rows, rows),
            cells(items, rows, width),
            cells(items, rows, width),
            cells(items, rows, width),
            cells(items, rows, width),
            cells(items, rows, inner),
            cells(items, rows, inner),
            cells(items, rows, width),
            cells(items, rows, width),
            cells(2, rows, (5 + wide) * width),
            pltpu.VMEM((items, rows, 1), jnp.float32),
            pltpu.VMEM((items, rows, 1), jnp.float32),
            pltpu.VMEM((rows, width), jnp.float32),
            pltpu.VMEM((rows, width), jnp.float32),
            cells(rows, width),
            pltpu.SemaphoreType.DMA((7,)),
            pltpu.SemaphoreType.DMA((2,)),
            pltpu.SemaphoreType.DMA((2,)),
            pltpu.SemaphoreType.DMA((items,)),
            pltpu.SemaphoreType.DMA((items,)),
            pltpu.SemaphoreType.DMA((items,)),
            pltpu.SemaphoreType.DMA((items,)),
            pltpu.SemaphoreType.DMA((items, 7)),
        ],
        compiler_params=pltpu.CompilerParams(
            collective_id=0, has_side_effects=True, vmem_limit_bytes=VMEM_LIMIT
        ),
        cost_estimate=pl.CostEstimate(
            flops=4 * items * rows * (4 + 2 * wide) * width * width,
            bytes_accessed=60_000_000,
            transcendentals=0,
        ),
    )(image_ids, caption_lengths, captions, regions, cotangent, *stacked)


def body(
    captions,
    regions,
    image_ids,
    caption_lengths,
    cotangent,
    query_weight,
    query_bias,
    key_weight,
    value_weight,
    value_bias,
    out_weight,
    out_bias,
    norm1_gain,
    norm1_bias,
    up_weight,
    up_bias,
    down_weight,
    down_bias,
    norm2_gain,
    norm2_bias,
):
    stacked = (
        query_weight,
        query_bias,
        key_weight,
        value_weight,
        value_bias,
        out_weight,
        out_bias,
        norm1_gain,
        norm1_bias,
        up_weight,
        up_bias,
        down_weight,
        down_bias,
        norm2_gain,
        norm2_bias,
    )
    width = captions.shape[2]
    states, input_grads, a_side, b_side, small = layered(
        image_ids, caption_lengths, captions, regions, cotangent, stacked
    )
    sums, small_sums = reduced(a_side, b_side, small, lax.axis_size("batch"))
    grads = spread(sums.reshape(-1, width), small_sums, stacked)
    return (states, input_grads) + tuple(grads)


def solution(mesh):
    placed = (
        P("batch", None, None),
        P("batch", None, None),
        P("batch"),
        P("batch"),
        P("batch", None, None),
        P("section", None, None),
        P("section", None),
        P("section", None, None),
        P("section", None, None),
        P("section", None),
        P("section", None, None),
        P("section", None),
        P("section", None),
        P("section", None),
        P("section", None, None),
        P("section", None),
        P("section", None, None),
        P("section", None),
        P("section", None),
        P("section", None),
    )
    return jax.shard_map(
        body,
        mesh=mesh,
        in_specs=placed,
        out_specs=(
            P("section", "batch", None, None),
            P("section", "batch", None, None),
            P("section", None, None),
            P("section", None),
            P("section", None, None),
            P("section", None, None),
            P("section", None),
            P("section", None, None),
            P("section", None),
            P("section", None),
            P("section", None),
            P("section", None, None),
            P("section", None),
            P("section", None, None),
            P("section", None),
            P("section", None),
            P("section", None),
        ),
        check_vma=False,
    )
```

```python
import functools
import math

import jax
import jax.numpy as jnp
from jax import lax
from jax.experimental import pallas as pl
from jax.experimental.pallas import tpu as pltpu
from jax.sharding import PartitionSpec as P

HEADS = 12
EPSILON = 1e-12
MESH = pl.DeviceIdType.MESH
VMEM_LIMIT = 60 * 1024 * 1024
GROUP = 16
CHUNK_GROUPS = 16
SLOTS = 16
SLOT_GROUPS = 24
LAG = 2
LINE = 4
SPLIT_BITS = 4


def reduce_kernel(
    bits,
    chunks,
    a_hbm,
    b_hbm,
    small_ref,
    out_hbm,
    small_out,
    a_ref,
    b_ref,
    acc,
    recv,
    small_acc,
    small_recv,
    load_sem,
    send_sem,
    recv_sem,
    keep_sem,
    small_send_sem,
    small_recv_sem,
):
    width = acc.shape[2]
    extra = bits - SPLIT_BITS
    first_gather = SPLIT_BITS + 1 + extra
    stages = 2 * (SPLIT_BITS + 1) + extra
    me = lax.axis_index("batch")
    section = lax.axis_index("section")
    core, side, place = me % 2, (me // 2) % 2, (me // 4) % LINE
    blocks_a = a_hbm.shape[1] // width
    blocks_b = b_hbm.shape[1] // width
    per_block = width // (CHUNK_GROUPS * GROUP)

    def load(source, target, block, base):
        lanes = pl.ds(block * width, width)
        return pltpu.make_async_copy(source.at[:, lanes], target.at[:, lanes], load_sem.at[base + block])

    def load_a(block):
        return load(a_hbm, a_ref, block, 0)

    def load_b(block):
        return load(b_hbm, b_ref, block, blocks_a)

    wide = blocks_a - 3
    first_use = {0: [(load_a, 0), (load_b, 0)]}
    for j in range(1, wide):
        first_use[j] = [(load_a, j)]
    first_use[wide] = [(load_a, wide), (load_b, 1)]
    for j in range(1, wide):
        first_use[wide + j] = [(load_b, 1 + j)]
    first_use[2 * wide] = [(load_a, wide + 1), (load_b, wide + 1)]
    first_use[2 * wide + 1] = [(load_a, wide + 2), (load_b, wide + 2)]
    first_use[2 * wide + 2] = [(load_b, wide + 3)]
    first_use[2 * wide + 3] = [(load_b, wide + 4)]
    for j in range(2 * wide + 4):
        for kind, block in first_use[j]:
            kind(block).start()

    def bit_mate(k):
        bit = (me // 2**k) % 2
        return (section, me + 2**k * (1 - 2 * bit))

    core_mate, side_mate = bit_mate(0), bit_mate(1)
    mates = ((section, me - LINE), (section, me + LINE))
    ring = [(section, me + LINE * ((place + d) % LINE - place)) for d in (LINE - 1, 1)]

    barrier = pltpu.get_barrier_semaphore()
    for peer in [core_mate, side_mate] + ring + [bit_mate(k) for k in range(2, bits)]:
        pl.semaphore_signal(barrier, inc=1, device_id=peer, device_id_type=MESH)
    pl.semaphore_wait(barrier, bits + 2)

    def kind_of(c):
        return (c % 5) % 2

    def low_core(c):
        return c * CHUNK_GROUPS + core * 8

    def low_side(c):
        return low_core(c) + side * 4

    def block_start(c, kind, b):
        return low_side(c) + b if kind == 0 else low_core(c) + 2 * b

    def final(c, kind):
        return low_side(c) + place if kind == 0 else low_core(c) + 2 * place + side

    def remote(c, source, start, size, target, spot, index, peer):
        return pltpu.make_async_remote_copy(
            src_ref=source.at[pl.ds(start, size)],
            dst_ref=target.at[c % SLOTS, pl.ds(spot, size)] if target is recv else target.at[pl.ds(start, size)],
            send_sem=send_sem.at[c % SLOTS, index],
            recv_sem=recv_sem.at[c % SLOTS, index],
            device_id=peer,
            device_id_type=MESH,
        )

    def core_copy(c):
        return remote(c, acc, c * CHUNK_GROUPS + (1 - core) * 8, 8, recv, 0, 0, core_mate)

    def side_copy(c, kind):
        if kind == 0:
            return remote(c, acc, low_core(c) + (1 - side) * 4, 4, recv, 8, 1, side_mate)
        return remote(c, acc, low_core(c) + 2 * place + (1 - side), 1, recv, 8, 1, side_mate)

    def line_copy(c, kind, r, d):
        size = 1 + kind
        b = jnp.minimum(3 - r + place, 3) if d == 1 else jnp.maximum(r - 3 + place, 0)
        spot = 12 + 2 * (2 * r + d)
        return remote(c, acc, block_start(c, kind, b), size, recv, spot, 2 + 2 * r + d, mates[d])

    def spread_copy(c, kind, r, d):
        size = 1 + kind
        b = jnp.maximum(place - r, 0) if d == 1 else jnp.minimum(place + r, 3)
        source = acc if kind == 0 and r == 0 else out_hbm
        return remote(c, source, block_start(c, kind, b), size, out_hbm, 0, 8 + 2 * r + d, mates[d])

    def side_back_copy(c, kind):
        if kind == 0:
            return remote(c, out_hbm, low_side(c), 4, out_hbm, 0, 14, side_mate)
        return remote(c, acc, final(c, kind), 1, out_hbm, 0, 14, side_mate)

    def core_back_copy(c):
        return remote(c, out_hbm, low_core(c), 8, out_hbm, 0, 15, core_mate)

    def extra_copy(c, kind, e):
        return remote(c, acc, final(c, kind), 1, recv, 24 + e, 16 + e, bit_mate(SPLIT_BITS + e))

    def keep_copy(c, kind):
        at = pl.ds(final(c, kind), 1)
        return pltpu.make_async_copy(acc.at[at], out_hbm.at[at], keep_sem.at[c % SLOTS])

    def add_groups(start, count, c, spot):
        def one(g, carry):
            total = acc[start + g].astype(jnp.float32) + recv[c % SLOTS, spot + g].astype(jnp.float32)
            acc[start + g] = total.astype(jnp.bfloat16)
            return carry

        lax.fori_loop(0, count, one, 0)

    def name_of(kind, s):
        if s == 0:
            return ("core",)
        if s == stages - 1:
            return ("core_back",)
        if s < SPLIT_BITS + 1:
            order = [("side",), ("line", 0), ("line", 1), ("line", 2)]
            order = order if kind == 0 else order[1:] + order[:1]
            return order[s - 1]
        if s < first_gather:
            return ("extra", s - SPLIT_BITS - 1)
        order = [("spread", 0), ("spread", 1), ("spread", 2), ("side_back",)]
        order = order if kind == 0 else order[3:] + order[:3]
        return order[s - first_gather]

    def start_stage(c, kind, s):
        name = name_of(kind, s)
        if s == first_gather:
            keep_copy(c, kind).start()
        if name[0] == "core":
            core_copy(c).start()
        elif name[0] == "side":
            side_copy(c, kind).start()
        elif name[0] == "line":
            r = name[1]
            pl.when(place <= r)(lambda: line_copy(c, kind, r, 1).start())
            pl.when(place >= 3 - r)(lambda: line_copy(c, kind, r, 0).start())
        elif name[0] == "extra":
            extra_copy(c, kind, name[1]).start()
        elif name[0] == "spread":
            r = name[1]
            pl.when((place >= r) & (place <= 2))(lambda: spread_copy(c, kind, r, 1).start())
            pl.when((place >= 1) & (place <= 3 - r))(lambda: spread_copy(c, kind, r, 0).start())
        elif name[0] == "side_back":
            side_back_copy(c, kind).start()
        else:
            core_back_copy(c).start()

    def finish_stage(c, kind, s):
        name = name_of(kind, s)
        if name[0] == "core":
            core_copy(c).wait()
            add_groups(low_core(c), 8, c, 0)
        elif name[0] == "side":
            side_copy(c, kind).wait()
            if kind == 0:
                add_groups(low_side(c), 4, c, 8)
            else:
                add_groups(final(c, kind), 1, c, 8)
        elif name[0] == "line":
            r = name[1]

            @pl.when(place <= r)
            def _():
                line_copy(c, kind, r, 1).wait_send()

            @pl.when(place >= 3 - r)
            def _():
                line_copy(c, kind, r, 0).wait_send()

            @pl.when((place >= 1) & (place <= r + 1))
            def _():
                line_copy(c, kind, r, 1).wait_recv()
                add_groups(block_start(c, kind, 2 - r + place), 1 + kind, c, 12 + 2 * (2 * r + 1))

            @pl.when((place <= 2) & (place >= 2 - r))
            def _():
                line_copy(c, kind, r, 0).wait_recv()
                add_groups(block_start(c, kind, r - 2 + place), 1 + kind, c, 12 + 2 * (2 * r))

        elif name[0] == "extra":
            extra_copy(c, kind, name[1]).wait()
            add_groups(final(c, kind), 1, c, 24 + name[1])
        elif name[0] == "spread":
            r = name[1]
            pl.when((place >= r) & (place <= 2))(lambda: spread_copy(c, kind, r, 1).wait_send())
            pl.when((place >= 1) & (place <= 3 - r))(lambda: spread_copy(c, kind, r, 0).wait_send())
            pl.when(place >= r + 1)(lambda: spread_copy(c, kind, r, 1).wait_recv())
            pl.when(place <= 2 - r)(lambda: spread_copy(c, kind, r, 0).wait_recv())
        elif name[0] == "side_back":
            side_back_copy(c, kind).wait()
        else:
            core_back_copy(c).wait()
        if s == first_gather:
            keep_copy(c, kind).wait()

    def small_copy(k):
        return pltpu.make_async_remote_copy(
            src_ref=small_acc.at[k],
            dst_ref=small_recv.at[k],
            send_sem=small_send_sem.at[k],
            recv_sem=small_recv_sem.at[k],
            device_id=bit_mate(k),
            device_id_type=MESH,
        )

    small_acc[0] = small_ref[...]

    def step(t, carry):
        for s in range(stages, 0, -1):
            c = t - LAG * s
            for kind in range(2):

                @pl.when((c >= 0) & (c < chunks) & (kind_of(c) == kind))
                def _():
                    finish_stage(c, kind, s - 1)
                    if s < stages:
                        start_stage(c, kind, s)

        for j in range(2 * wide + 4):

            @pl.when(t == per_block * j)
            def _():
                for kind, block in first_use[j]:
                    kind(block).wait()

        @pl.when(t < chunks)
        def _():
            block, part = t // per_block, t % per_block
            a_col = jnp.minimum(block, wide) + jnp.minimum(block // (2 * wide), 1) + jnp.minimum(block // (2 * wide + 1), 1)
            b_col = jnp.maximum(block - wide + 1, 0)
            lines = CHUNK_GROUPS * GROUP
            left = a_ref[:, pl.ds(pl.multiple_of(a_col * width + part * lines, lines), lines)]
            right = b_ref[:, pl.ds(pl.multiple_of(b_col * width, width), width)]
            grad = lax.dot_general(left, right, (((0,), (0,)), ((), ())), preferred_element_type=jnp.float32)
            acc[pl.ds(t * CHUNK_GROUPS, CHUNK_GROUPS)] = grad.astype(jnp.bfloat16).reshape(
                CHUNK_GROUPS, GROUP, width
            )
            core_copy(t).start()

        for k in range(bits + 1):

            @pl.when(t == LAG * k)
            def _():
                if k > 0:
                    small_copy(k - 1).wait()
                    small_acc[k] = small_acc[k - 1] + small_recv[k - 1]
                if k < bits:
                    small_copy(k).start()

        return carry

    lax.fori_loop(0, chunks + LAG * stages, step, 0)
    small_out[...] = small_acc[bits]


def reduced(a_side, b_side, small, count):
    rows = a_side.shape[0]
    width = small.shape[1]
    bits = count.bit_length() - 1
    extra = bits - SPLIT_BITS
    blocks = 2 * (a_side.shape[1] // width - 3) + 4
    chunks = blocks * width // (CHUNK_GROUPS * GROUP)
    groups = chunks * CHUNK_GROUPS
    loads = (a_side.shape[1] + b_side.shape[1]) // width
    return pl.pallas_call(
        functools.partial(reduce_kernel, bits, chunks),
        out_shape=(
            jax.ShapeDtypeStruct((groups, GROUP, width), jnp.bfloat16),
            jax.ShapeDtypeStruct(small.shape, jnp.float32),
        ),
        in_specs=[
            pl.BlockSpec(memory_space=pl.ANY),
            pl.BlockSpec(memory_space=pl.ANY),
            pl.BlockSpec(memory_space=pltpu.VMEM),
        ],
        out_specs=(pl.BlockSpec(memory_space=pl.ANY), pl.BlockSpec(memory_space=pltpu.VMEM)),
        scratch_shapes=[
            pltpu.VMEM(a_side.shape, jnp.bfloat16),
            pltpu.VMEM(b_side.shape, jnp.bfloat16),
            pltpu.VMEM((groups, GROUP, width), jnp.bfloat16),
            pltpu.VMEM((SLOTS, SLOT_GROUPS + extra, GROUP, width), jnp.bfloat16),
            pltpu.VMEM((bits + 1,) + small.shape, jnp.float32),
            pltpu.VMEM((bits,) + small.shape, jnp.float32),
            pltpu.SemaphoreType.DMA((loads,)),
            pltpu.SemaphoreType.DMA((SLOTS, 16 + extra)),
            pltpu.SemaphoreType.DMA((SLOTS, 16 + extra)),
            pltpu.SemaphoreType.DMA((SLOTS,)),
            pltpu.SemaphoreType.DMA((bits,)),
            pltpu.SemaphoreType.DMA((bits,)),
        ],
        compiler_params=pltpu.CompilerParams(
            collective_id=1, has_side_effects=True, vmem_limit_bytes=VMEM_LIMIT
        ),
        cost_estimate=pl.CostEstimate(
            flops=2 * rows * blocks * width * width, bytes_accessed=80_000_000, transcendentals=0
        ),
    )(a_side, b_side, small)


PIECE = 384
DEPTH = 4


def spread_kernel(sum_hbm, small_ref, states_hbm, grads_hbm, *refs):
    width = small_ref.shape[1]
    states_out, grads_out = refs[:2]
    (o_wq, o_bq, o_wk, o_wv, o_bv, o_wo, o_bo, o_g1, o_s1, o_up, o_bu, o_dn, o_bd, o_g2, o_s2) = refs[2:17]
    taken, given, in_sem, out_sem, pass_sem = refs[17:]
    passes = [
        pltpu.make_async_copy(states_hbm, states_out, pass_sem.at[0]),
        pltpu.make_async_copy(grads_hbm, grads_out, pass_sem.at[1]),
    ]
    for copy in passes:
        copy.start()
    wide = o_bu.shape[1] // width
    targets = []
    for j in range(wide):
        targets += [o_dn.at[0, pl.ds(j * width + r, PIECE), :] for r in range(0, width, PIECE)]
    for j in range(wide):
        targets += [o_up.at[0, pl.ds(r, PIECE), pl.ds(j * width, width)] for r in range(0, width, PIECE)]
    for ref in (o_wo, o_wq, o_wk, o_wv):
        targets += [ref.at[0, pl.ds(r, PIECE), :] for r in range(0, width, PIECE)]

    def load(i):
        return pltpu.make_async_copy(
            sum_hbm.at[pl.ds(i * PIECE, PIECE)], taken.at[i % DEPTH], in_sem.at[i % DEPTH]
        )

    def store(i):
        return pltpu.make_async_copy(given.at[i % DEPTH], targets[i], out_sem.at[i % DEPTH])

    for i in range(DEPTH):
        load(i).start()
    singles = [o_bq, o_bv, o_bo, o_g1, o_s1, o_bd, o_g2, o_s2]
    for i, ref in enumerate(singles):
        ref[...] = small_ref[pl.ds(i, 1), :]
    for j in range(wide):
        o_bu[:, pl.ds(j * width, width)] = small_ref[pl.ds(len(singles) + j, 1), :]
    for i in range(len(targets)):
        load(i).wait()
        if i >= DEPTH:
            store(i - DEPTH).wait()

        def convert(r, carry):
            rows = pl.ds(pl.multiple_of(r * 64, 64), 64)
            given[i % DEPTH, rows, :] = taken[i % DEPTH, rows, :].astype(jnp.float32)
            return carry

        lax.fori_loop(0, PIECE // 64, convert, 0)
        store(i).start()
        if i + DEPTH < len(targets):
            load(i + DEPTH).start()
    for i in range(len(targets) - DEPTH, len(targets)):
        store(i).wait()
    for copy in passes:
        copy.wait()


def spread(sums, small, states, input_grads, params):
    width = small.shape[1]
    anywhere = pl.BlockSpec(memory_space=pl.ANY)
    local = pl.BlockSpec(memory_space=pltpu.VMEM)
    return pl.pallas_call(
        spread_kernel,
        out_shape=(
            jax.ShapeDtypeStruct(states.shape, states.dtype),
            jax.ShapeDtypeStruct(input_grads.shape, input_grads.dtype),
        )
        + tuple(jax.ShapeDtypeStruct(member.shape, jnp.float32) for member in params),
        in_specs=[anywhere, local, anywhere, anywhere],
        out_specs=(anywhere, anywhere)
        + tuple(anywhere if len(member.shape) == 3 else local for member in params),
        scratch_shapes=[
            pltpu.VMEM((DEPTH, PIECE, width), jnp.bfloat16),
            pltpu.VMEM((DEPTH, PIECE, width), jnp.float32),
            pltpu.SemaphoreType.DMA((DEPTH,)),
            pltpu.SemaphoreType.DMA((DEPTH,)),
            pltpu.SemaphoreType.DMA((2,)),
        ],
        compiler_params=pltpu.CompilerParams(vmem_limit_bytes=VMEM_LIMIT),
        cost_estimate=pl.CostEstimate(
            flops=12 * width * width, bytes_accessed=80 * width * width, transcendentals=0
        ),
    )(sums, small, states, input_grads)


SINGLES = ("bq", "bv", "bo", "g1", "s1", "bd", "g2", "s2")


def product(left, right):
    return lax.dot_general(left, right, (((1,), (0,)), ((), ())), preferred_element_type=jnp.float32)


def product_t(left, right):
    return lax.dot_general(left, right, (((1,), (1,)), ((), ())), preferred_element_type=jnp.float32)


def gelu_pair(z):
    cdf = 0.5 + 0.5 * lax.erf(z * (1.0 / math.sqrt(2.0)))
    bell = jnp.exp(-0.5 * z * z)
    return z * cdf, cdf + z * bell * (1.0 / math.sqrt(2.0 * math.pi))


def normed(values):
    average = jnp.mean(values, axis=-1, keepdims=True)
    centered = values - average
    inverse = lax.rsqrt(jnp.mean(centered * centered, axis=-1, keepdims=True) + EPSILON)
    return centered * inverse, inverse


def normed_back(grad, normal, inverse):
    first_mean = jnp.mean(grad, axis=-1, keepdims=True)
    second_mean = jnp.mean(grad * normal, axis=-1, keepdims=True)
    return inverse * (grad - first_mean - normal * second_mean)


def layer_kernel(
    ids_ref,
    lengths_ref,
    captions_ref,
    regions_ref,
    cotangent_hbm,
    wq_hbm,
    bq_ref,
    wk_hbm,
    wv_hbm,
    bv_ref,
    wo_hbm,
    bo_ref,
    g1_ref,
    s1_ref,
    wu_hbm,
    bu_ref,
    wd_hbm,
    bd_ref,
    g2_ref,
    s2_ref,
    states_hbm,
    grads_hbm,
    a_hbm,
    b_hbm,
    small_ref,
    wqkv,
    wo,
    wu,
    wd,
    table,
    hidden,
    upstream,
    query,
    keys,
    values,
    probs,
    context,
    normal1,
    normal2,
    lowered,
    active,
    slope,
    result,
    grad_in,
    staged,
    inverse1,
    inverse2,
    wide1,
    wide2,
    d_context,
    d_scores,
    weight_sem,
    table_send,
    table_recv,
    fwd_send,
    fwd_recv,
    back_send,
    back_recv,
    out_sem,
):
    items, rows, width = hidden.shape
    held = regions_ref.shape[0]
    cap_rows = captions_ref.shape[1]
    wide = wu.shape[1] // width
    pairs = HEADS // 2
    pair_width = width // pairs
    head = width // HEADS
    section = lax.axis_index("section")
    batch = lax.axis_index("batch")
    count = lax.axis_size("batch")
    right = (section, lax.rem(batch + 1, count))
    left = (section, lax.rem(batch + count - 1, count))
    other = (1 - section, batch)

    weight_copies = [
        pltpu.make_async_copy(source.at[0], target, weight_sem.at[n])
        for n, (source, target) in enumerate(
            (
                (wq_hbm, wqkv.at[:, pl.ds(0, width)]),
                (wk_hbm, wqkv.at[:, pl.ds(width, width)]),
                (wv_hbm, wqkv.at[:, pl.ds(2 * width, width)]),
                (wo_hbm, wo),
                (wu_hbm, wu),
                (wd_hbm, wd),
            )
        )
    ]
    for copy in weight_copies:
        copy.start()
    cotangent_copy = pltpu.make_async_copy(cotangent_hbm, upstream, weight_sem.at[6])

    barrier = pltpu.get_barrier_semaphore()
    for peer in (right, left, other):
        pl.semaphore_signal(barrier, inc=1, device_id=peer, device_id_type=MESH)
    pl.semaphore_wait(barrier, 3)

    def table_copy(n, peer):
        return pltpu.make_async_remote_copy(
            src_ref=regions_ref,
            dst_ref=table.at[pl.ds(2 * n * held, held)],
            send_sem=table_send.at[n],
            recv_sem=table_recv.at[n],
            device_id=peer,
            device_id_type=MESH,
        )

    @pl.when(section == 0)
    def _():
        table_copy(0, right).start()
        table_copy(1, left).start()
        table[pl.ds(held, held)] = regions_ref[...]
        table_copy(0, right).wait()
        table_copy(1, left).wait()

    @pl.when(section == 1)
    def _():
        cotangent_copy.start()

    def forward_copy(i):
        return pltpu.make_async_remote_copy(
            src_ref=result.at[i],
            dst_ref=hidden.at[i],
            send_sem=fwd_send.at[i],
            recv_sem=fwd_recv.at[i],
            device_id=other,
            device_id_type=MESH,
        )

    def back_copy(i):
        return pltpu.make_async_remote_copy(
            src_ref=grad_in.at[i],
            dst_ref=upstream.at[i],
            send_sem=back_send.at[i],
            recv_sem=back_recv.at[i],
            device_id=other,
            device_id_type=MESH,
        )

    def saves(i):
        at = pl.ds(pl.multiple_of(i * rows, rows), rows)
        first = wide * width
        sources = (
            (active.at[i], a_hbm.at[at, pl.ds(0, first)]),
            (lowered.at[i], a_hbm.at[at, pl.ds(first, width)]),
            (context.at[i], a_hbm.at[at, pl.ds(first + width, width)]),
            (hidden.at[i], a_hbm.at[at, pl.ds(first + 2 * width, width)]),
            (result.at[i], states_hbm.at[0, i]),
        )
        return [pltpu.make_async_copy(s, d, out_sem.at[i, n]) for n, (s, d) in enumerate(sources)]

    def staged_save(i):
        at = pl.ds(pl.multiple_of(i * rows, rows), rows)
        return pltpu.make_async_copy(staged.at[lax.rem(i, 2)], b_hbm.at[at], out_sem.at[i, 5])

    def grad_save(i):
        return pltpu.make_async_copy(grad_in.at[i], grads_hbm.at[0, i], out_sem.at[i, 6])

    def vector(ref, j=0):
        return ref[:, j * width : (j + 1) * width].astype(jnp.float32)

    lane = lax.broadcasted_iota(jnp.int32, (rows, pair_width), 1)

    blocks = [slice(r, r + GROUP) for r in range(0, rows, GROUP)]
    spans = [slice(c, min(c + 128, rows)) for c in range(0, rows, 128)]

    def only(block, h):
        return jnp.where((lane // head) == h, block, jnp.zeros_like(block))

    def assemble(i):
        total = count * held
        spot = jnp.minimum(lax.rem(ids_ref[i] - (batch - 1) * held + total, total), 3 * held - 1)
        whole = jnp.concatenate(
            [captions_ref[i].astype(jnp.float32), table[spot].astype(jnp.float32)], axis=0
        )
        hidden[i] = whole.astype(jnp.bfloat16)

    def forward(i):
        @pl.when(i == 0)
        def _():
            for copy in weight_copies[:3]:
                copy.wait()

        source = hidden[i]
        mixed = product(source, wqkv[...])
        for at in blocks:
            scaled = (mixed[at, :width] + vector(bq_ref)) * (1.0 / math.sqrt(head))
            query[i, at, :] = scaled.astype(jnp.bfloat16)
            keys[i, at, :] = mixed[at, width : 2 * width].astype(jnp.bfloat16)
            values[i, at, :] = (mixed[at, 2 * width :] + vector(bv_ref)).astype(jnp.bfloat16)
        position = lax.broadcasted_iota(jnp.int32, (rows, 1), 0)
        live = (position >= cap_rows) | (position < lengths_ref[i])
        key_bias = jnp.where(live, 0.0, -1000000000.0)

        def lanes_of(p):
            return slice(p * pair_width, (p + 1) * pair_width)

        def scored(p):
            k_pair = keys[i, :, lanes_of(p)]
            stacked = jnp.concatenate([only(k_pair, 0), only(k_pair, 1)], axis=0)
            v_turned = values[i, :, lanes_of(p)].astype(jnp.float32).T.astype(jnp.bfloat16)
            return product_t(stacked, query[i, :, lanes_of(p)]), v_turned

        def weighed(p, both):
            for h in range(2):
                for span in spans:
                    scores = both[h * rows : (h + 1) * rows, span] + key_bias
                    expo = jnp.exp(scores - jnp.max(scores, axis=0, keepdims=True))
                    share = pl.reciprocal(jnp.sum(expo, axis=0, keepdims=True))
                    probs[i, 2 * p + h, :, span] = (expo * share).astype(jnp.bfloat16)

        def mixed_values(p, v_turned):
            return [product(v_turned[h * head : (h + 1) * head], probs[i, 2 * p + h]) for h in range(2)]

        def place_context(p, parts):
            context[i, :, lanes_of(p)] = jnp.concatenate(parts, axis=0).T.astype(jnp.bfloat16)

        ahead = scored(0)
        parts = None
        for p in range(pairs):
            both, v_turned = ahead
            if p + 1 < pairs:
                ahead = scored(p + 1)
            if parts is not None:
                place_context(p - 1, parts)
            weighed(p, both)
            parts = mixed_values(p, v_turned)
        place_context(pairs - 1, parts)

        @pl.when(i == 0)
        def _():
            for copy in weight_copies[3:]:
                copy.wait()

        attended = product(context[i], wo[...])
        for at in blocks:
            n1, inv1 = normed(hidden[i, at, :].astype(jnp.float32) + attended[at] + vector(bo_ref))
            normal1[i, at, :] = n1.astype(jnp.bfloat16)
            inverse1[i, at, :] = inv1
            first = n1 * vector(g1_ref) + vector(s1_ref)
            lowered[i, at, :] = first.astype(jnp.bfloat16)
            wide1[at, :] = first + vector(bd_ref)
        low = lowered[i]
        tile = 2 * width // 3
        tiles = wide * width // tile

        def raised(n):
            return product(low, wu[:, n * tile : (n + 1) * tile])

        z_next = raised(0)
        half = tiles // 2
        for n in range(tiles):
            lanes = slice(n * tile, (n + 1) * tile)
            z_tile = z_next
            if n + 1 < tiles:
                z_next = raised(n + 1)
            if n == half:
                wide1[...] += product(active[i, :, : half * tile], wd[: half * tile, :])
            for at in blocks:
                gelu, slant = gelu_pair(z_tile[at] + bu_ref[:, lanes].astype(jnp.float32))
                active[i, at, lanes] = gelu.astype(jnp.bfloat16)
                slope[i, at, lanes] = slant.astype(jnp.bfloat16)
        lowest = product(active[i, :, half * tile :], wd[half * tile :, :])
        for at in blocks:
            n2, inv2 = normed(wide1[at, :] + lowest[at])
            normal2[i, at, :] = n2.astype(jnp.bfloat16)
            inverse2[i, at, :] = inv2
            result[i, at, :] = (n2 * vector(g2_ref) + vector(s2_ref)).astype(jnp.bfloat16)

    def folded(value):
        return value[: GROUP // 2] + value[GROUP // 2 :]

    def keep_small(row, value):
        small_ref[row : row + 1, :] += jnp.sum(value, axis=0, keepdims=True)

    def single(name, value):
        keep_small(SINGLES.index(name), value)

    def backward(i):
        slot = lax.rem(i, 2)
        base = (2 + wide) * width

        def stage(at, column, value):
            staged[slot, at, column * width : (column + 1) * width] = value

        def norm_step(at, gradient, normal, inverse, gain, sums):
            n = normal[i, at, :].astype(jnp.float32)
            d_res = normed_back(gradient * vector(gain), n, inverse[i, at, :])
            d_low = d_res.astype(jnp.bfloat16)
            terms = [folded(gradient * n), folded(gradient), folded(d_low.astype(jnp.float32))]
            return d_res, d_low, terms if sums is None else [a + b for a, b in zip(sums, terms)]

        sums = None
        for at in blocks:
            gradient = upstream[i, at, :].astype(jnp.float32)
            d_res, d_low, sums = norm_step(at, gradient, normal2, inverse2, g2_ref, sums)
            wide1[at, :] = d_res
            stage(at, 0, d_low)
        for name, value in zip(("g2", "s2", "bd"), sums):
            single(name, value)
        d_out = staged[slot, :, :width]
        for j in range(wide):
            lanes = slice(j * width, (j + 1) * width)
            d_active = product_t(d_out, wd[lanes, :])
            total = None
            for at in blocks:
                d_inner = (d_active[at] * slope[i, at, lanes].astype(jnp.float32)).astype(jnp.bfloat16)
                stage(at, 1 + j, d_inner)
                term = folded(d_inner.astype(jnp.float32))
                total = term if total is None else total + term
            keep_small(len(SINGLES) + j, total)
        d_deep = product_t(staged[slot, :, width : (1 + wide) * width], wu[...])
        sums = None
        for at in blocks:
            d_res, d_low, sums = norm_step(at, wide1[at, :] + d_deep[at], normal1, inverse1, g1_ref, sums)
            wide2[at, :] = d_res
            stage(at, 1 + wide, d_low)
        for name, value in zip(("g1", "s1", "bo"), sums):
            single(name, value)
        d_att = staged[slot, :, (1 + wide) * width : (2 + wide) * width]
        d_context[...] = product_t(d_att, wo[...]).astype(jnp.bfloat16)

        def lanes_of(p):
            return slice(p * pair_width, (p + 1) * pair_width)

        def place_grad(n, p, block):
            at = base + n * width + p * pair_width
            staged[slot, :, at : at + pair_width] = block.astype(jnp.bfloat16)

        def opened(p):
            v_pair = values[i, :, lanes_of(p)]
            c_pair = d_context[:, lanes_of(p)]
            stacked = jnp.concatenate([only(v_pair, 0), only(v_pair, 1)], axis=0)
            k_turned = keys[i, :, lanes_of(p)].astype(jnp.float32).T.astype(jnp.bfloat16)
            d_value = product(probs[i, 2 * p], only(c_pair, 0))
            d_value += product(probs[i, 2 * p + 1], only(c_pair, 1))
            return product_t(stacked, c_pair), k_turned, d_value

        def score_grads(p, both):
            for h in range(2):
                for span in spans:
                    prob = probs[i, 2 * p + h, :, span].astype(jnp.float32)
                    d_prob = both[h * rows : (h + 1) * rows, span]
                    drift = jnp.sum(d_prob * prob, axis=0, keepdims=True)
                    d_scores[p % 2, h, :, span] = (prob * (d_prob - drift)).astype(jnp.bfloat16)
            return [d_scores[p % 2, h] for h in range(2)]

        def closed(p, found, k_turned):
            q_pair = query[i, :, lanes_of(p)]
            d_key = product(found[0], only(q_pair, 0)) + product(found[1], only(q_pair, 1))
            return d_key, [product(k_turned[h * head : (h + 1) * head], found[h]) for h in range(2)]

        def place_grads(p, d_value, d_key, parts):
            place_grad(0, p, jnp.concatenate(parts, axis=0).T * (1.0 / math.sqrt(head)))
            place_grad(1, p, d_key)
            place_grad(2, p, d_value)

        ahead = opened(0)
        waiting = None
        for p in range(pairs):
            both, k_turned, d_value = ahead
            if p + 1 < pairs:
                ahead = opened(p + 1)
            if waiting is not None:
                place_grads(*waiting)
            found = score_grads(p, both)
            d_key, parts = closed(p, found, k_turned)
            waiting = (p, d_value, d_key, parts)
        place_grads(*waiting)
        d_source = product_t(staged[slot, :, base : base + 3 * width], wqkv[...])
        sums = None
        for at in blocks:
            grad_in[i, at, :] = (wide2[at, :] + d_source[at]).astype(jnp.bfloat16)
            terms = [
                folded(staged[slot, at, base : base + width].astype(jnp.float32)),
                folded(staged[slot, at, base + 2 * width : base + 3 * width].astype(jnp.float32)),
            ]
            sums = terms if sums is None else [a + b for a, b in zip(sums, terms)]
        single("bq", sums[0])
        single("bv", sums[1])

    small_ref[...] = jnp.zeros_like(small_ref)

    def forward_step(i, carry):
        @pl.when(section == 0)
        def _():
            assemble(i)

        @pl.when(section == 1)
        def _():
            forward_copy(i).wait_recv()

        forward(i)

        @pl.when(section == 0)
        def _():
            forward_copy(i).start()

        for copy in saves(i):
            copy.start()
        return carry

    lax.fori_loop(0, items, forward_step, 0)

    @pl.when(section == 1)
    def _():
        cotangent_copy.wait()

    def backward_step(i, carry):
        @pl.when(section == 0)
        def _():
            back_copy(i).wait_recv()

        @pl.when(i >= 2)
        def _():
            staged_save(i - 2).wait()

        backward(i)

        @pl.when(section == 1)
        def _():
            back_copy(i).start()

        staged_save(i).start()
        grad_save(i).start()
        return carry

    lax.fori_loop(0, items, backward_step, 0)

    def finish(i, carry):
        for copy in saves(i):
            copy.wait()
        grad_save(i).wait()

        @pl.when(i >= items - 2)
        def _():
            staged_save(i).wait()

        @pl.when(section == 0)
        def _():
            forward_copy(i).wait_send()

        @pl.when(section == 1)
        def _():
            back_copy(i).wait_send()

        return carry

    lax.fori_loop(0, items, finish, 0)


def layered(image_ids, caption_lengths, captions, regions, cotangent, stacked):
    items, cap_rows, width = captions.shape
    held, region_rows, _ = regions.shape
    rows = cap_rows + region_rows
    inner = stacked[9].shape[2]
    low = jnp.bfloat16
    wide = inner // width

    def cells(*shape):
        return pltpu.VMEM(shape, low)

    anywhere = pl.BlockSpec(memory_space=pl.ANY)
    local = pl.BlockSpec(memory_space=pltpu.VMEM)
    scalars = pl.BlockSpec(memory_space=pltpu.SMEM)
    return pl.pallas_call(
        layer_kernel,
        out_shape=(
            jax.ShapeDtypeStruct((1, items, rows, width), low),
            jax.ShapeDtypeStruct((1, items, rows, width), low),
            jax.ShapeDtypeStruct((items * rows, (3 + wide) * width), low),
            jax.ShapeDtypeStruct((items * rows, (5 + wide) * width), low),
            jax.ShapeDtypeStruct((GROUP, width), jnp.float32),
        ),
        in_specs=[scalars, scalars, local, local, anywhere]
        + [anywhere if len(member.shape) == 3 else local for member in stacked],
        out_specs=(anywhere, anywhere, anywhere, anywhere, local),
        scratch_shapes=[
            cells(width, 3 * width),
            cells(width, width),
            cells(width, inner),
            cells(inner, width),
            cells(3 * held, region_rows, width),
            cells(items, rows, width),
            cells(items, rows, width),
            cells(items, rows, width),
            cells(items, rows, width),
            cells(items, rows, width),
            cells(items, HEADS, rows, rows),
            cells(items, rows, width),
            cells(items, rows, width),
            cells(items, rows, width),
            cells(items, rows, width),
            cells(items, rows, inner),
            cells(items, rows, inner),
            cells(items, rows, width),
            cells(items, rows, width),
            cells(2, rows, (5 + wide) * width),
            pltpu.VMEM((items, rows, 1), jnp.float32),
            pltpu.VMEM((items, rows, 1), jnp.float32),
            pltpu.VMEM((rows, width), jnp.float32),
            pltpu.VMEM((rows, width), jnp.float32),
            cells(rows, width),
            cells(2, 2, rows, rows),
            pltpu.SemaphoreType.DMA((7,)),
            pltpu.SemaphoreType.DMA((2,)),
            pltpu.SemaphoreType.DMA((2,)),
            pltpu.SemaphoreType.DMA((items,)),
            pltpu.SemaphoreType.DMA((items,)),
            pltpu.SemaphoreType.DMA((items,)),
            pltpu.SemaphoreType.DMA((items,)),
            pltpu.SemaphoreType.DMA((items, 7)),
        ],
        compiler_params=pltpu.CompilerParams(
            collective_id=0, has_side_effects=True, vmem_limit_bytes=VMEM_LIMIT
        ),
        cost_estimate=pl.CostEstimate(
            flops=4 * items * rows * (4 + 2 * wide) * width * width,
            bytes_accessed=60_000_000,
            transcendentals=0,
        ),
    )(image_ids, caption_lengths, captions, regions, cotangent, *stacked)


def body(
    captions,
    regions,
    image_ids,
    caption_lengths,
    cotangent,
    query_weight,
    query_bias,
    key_weight,
    value_weight,
    value_bias,
    out_weight,
    out_bias,
    norm1_gain,
    norm1_bias,
    up_weight,
    up_bias,
    down_weight,
    down_bias,
    norm2_gain,
    norm2_bias,
):
    stacked = (
        query_weight,
        query_bias,
        key_weight,
        value_weight,
        value_bias,
        out_weight,
        out_bias,
        norm1_gain,
        norm1_bias,
        up_weight,
        up_bias,
        down_weight,
        down_bias,
        norm2_gain,
        norm2_bias,
    )
    width = captions.shape[2]
    states, input_grads, a_side, b_side, small = layered(
        image_ids, caption_lengths, captions, regions, cotangent, stacked
    )
    sums, small_sums = reduced(a_side, b_side, small, lax.axis_size("batch"))
    return tuple(spread(sums.reshape(-1, width), small_sums, states, input_grads, stacked))


def solution(mesh):
    placed = (
        P("batch", None, None),
        P("batch", None, None),
        P("batch"),
        P("batch"),
        P("batch", None, None),
        P("section", None, None),
        P("section", None),
        P("section", None, None),
        P("section", None, None),
        P("section", None),
        P("section", None, None),
        P("section", None),
        P("section", None),
        P("section", None),
        P("section", None, None),
        P("section", None),
        P("section", None, None),
        P("section", None),
        P("section", None),
        P("section", None),
    )
    return jax.shard_map(
        body,
        mesh=mesh,
        in_specs=placed,
        out_specs=(
            P("section", "batch", None, None),
            P("section", "batch", None, None),
            P("section", None, None),
            P("section", None),
            P("section", None, None),
            P("section", None, None),
            P("section", None),
            P("section", None, None),
            P("section", None),
            P("section", None),
            P("section", None),
            P("section", None, None),
            P("section", None),
            P("section", None, None),
            P("section", None),
            P("section", None),
            P("section", None),
        ),
        check_vma=False,
    )
```

```python
import functools
import math

import jax
import jax.numpy as jnp
from jax import lax
from jax.experimental import pallas as pl
from jax.experimental.pallas import tpu as pltpu
from jax.sharding import PartitionSpec as P

HEADS = 12
EPSILON = 1e-12
MESH = pl.DeviceIdType.MESH
VMEM_LIMIT = 60 * 1024 * 1024
GROUP = 16
CHUNK_GROUPS = 16
SLOTS = 16
SLOT_GROUPS = 24
LAG = 2
LINE = 4
SPLIT_BITS = 4


def reduce_kernel(
    bits,
    chunks,
    a_hbm,
    b_hbm,
    small_ref,
    out_hbm,
    small_out,
    a_ref,
    b_ref,
    acc,
    whole,
    recv,
    small_acc,
    small_recv,
    load_sem,
    send_sem,
    recv_sem,
    save_sem,
    small_send_sem,
    small_recv_sem,
):
    width = acc.shape[2]
    extra = bits - SPLIT_BITS
    first_gather = SPLIT_BITS + 1 + extra
    stages = 2 * (SPLIT_BITS + 1) + extra + 1
    me = lax.axis_index("batch")
    section = lax.axis_index("section")
    core, side, place = me % 2, (me // 2) % 2, (me // 4) % LINE
    blocks_a = a_hbm.shape[1] // width
    blocks_b = b_hbm.shape[1] // width
    per_block = width // (CHUNK_GROUPS * GROUP)

    def load(source, target, block, base):
        lanes = pl.ds(block * width, width)
        return pltpu.make_async_copy(source.at[:, lanes], target.at[:, lanes], load_sem.at[base + block])

    def load_a(block):
        return load(a_hbm, a_ref, block, 0)

    def load_b(block):
        return load(b_hbm, b_ref, block, blocks_a)

    wide = blocks_a - 3
    first_use = {0: [(load_a, 0), (load_b, 0)]}
    for j in range(1, wide):
        first_use[j] = [(load_a, j)]
    first_use[wide] = [(load_a, wide), (load_b, 1)]
    for j in range(1, wide):
        first_use[wide + j] = [(load_b, 1 + j)]
    first_use[2 * wide] = [(load_a, wide + 1), (load_b, wide + 1)]
    first_use[2 * wide + 1] = [(load_a, wide + 2), (load_b, wide + 2)]
    first_use[2 * wide + 2] = [(load_b, wide + 3)]
    first_use[2 * wide + 3] = [(load_b, wide + 4)]
    for j in range(2 * wide + 4):
        for kind, block in first_use[j]:
            kind(block).start()

    def bit_mate(k):
        bit = (me // 2**k) % 2
        return (section, me + 2**k * (1 - 2 * bit))

    core_mate, side_mate = bit_mate(0), bit_mate(1)
    mates = ((section, me - LINE), (section, me + LINE))
    ring = [(section, me + LINE * ((place + d) % LINE - place)) for d in (LINE - 1, 1)]

    barrier = pltpu.get_barrier_semaphore()
    for peer in [core_mate, side_mate] + ring + [bit_mate(k) for k in range(2, bits)]:
        pl.semaphore_signal(barrier, inc=1, device_id=peer, device_id_type=MESH)
    pl.semaphore_wait(barrier, bits + 2)

    def kind_of(c):
        return (c % 5) % 2

    def low_core(c):
        return c * CHUNK_GROUPS + core * 8

    def low_side(c):
        return low_core(c) + side * 4

    def block_start(c, kind, b):
        return low_side(c) + b if kind == 0 else low_core(c) + 2 * b

    def final(c, kind):
        return low_side(c) + place if kind == 0 else low_core(c) + 2 * place + side

    def remote(c, source, start, size, target, spot, index, peer):
        return pltpu.make_async_remote_copy(
            src_ref=source.at[pl.ds(start, size)],
            dst_ref=target.at[c % SLOTS, pl.ds(spot, size)] if target is recv else target.at[pl.ds(start, size)],
            send_sem=send_sem.at[c % SLOTS, index],
            recv_sem=recv_sem.at[c % SLOTS, index],
            device_id=peer,
            device_id_type=MESH,
        )

    def core_copy(c):
        return remote(c, acc, c * CHUNK_GROUPS + (1 - core) * 8, 8, recv, 0, 0, core_mate)

    def side_copy(c, kind):
        if kind == 0:
            return remote(c, acc, low_core(c) + (1 - side) * 4, 4, recv, 8, 1, side_mate)
        return remote(c, acc, low_core(c) + 2 * place + (1 - side), 1, recv, 8, 1, side_mate)

    def line_copy(c, kind, r, d):
        size = 1 + kind
        b = jnp.minimum(3 - r + place, 3) if d == 1 else jnp.maximum(r - 3 + place, 0)
        spot = 12 + 2 * (2 * r + d)
        return remote(c, acc, block_start(c, kind, b), size, recv, spot, 2 + 2 * r + d, mates[d])

    def spread_copy(c, kind, r, d):
        size = 1 + kind
        b = jnp.maximum(place - r, 0) if d == 1 else jnp.minimum(place + r, 3)
        return remote(c, whole, block_start(c, kind, b), size, whole, 0, 8 + 2 * r + d, mates[d])

    def side_back_copy(c, kind):
        if kind == 0:
            return remote(c, whole, low_side(c), 4, whole, 0, 14, side_mate)
        return remote(c, whole, final(c, kind), 1, whole, 0, 14, side_mate)

    def core_back_copy(c):
        return remote(c, whole, low_core(c), 8, whole, 0, 15, core_mate)

    def extra_copy(c, kind, e):
        return remote(c, acc, final(c, kind), 1, recv, 24 + e, 16 + e, bit_mate(SPLIT_BITS + e))

    def save_copy(c):
        at = pl.ds(c * CHUNK_GROUPS, CHUNK_GROUPS)
        return pltpu.make_async_copy(whole.at[at], out_hbm.at[at], save_sem.at[c % SLOTS])

    def add_groups(start, count, c, spot):
        def one(g, carry):
            total = acc[start + g].astype(jnp.float32) + recv[c % SLOTS, spot + g].astype(jnp.float32)
            acc[start + g] = total.astype(jnp.bfloat16)
            return carry

        lax.fori_loop(0, count, one, 0)

    def name_of(kind, s):
        if s == 0:
            return ("core",)
        if s == stages - 1:
            return ("save",)
        if s == stages - 2:
            return ("core_back",)
        if s < SPLIT_BITS + 1:
            order = [("side",), ("line", 0), ("line", 1), ("line", 2)]
            order = order if kind == 0 else order[1:] + order[:1]
            return order[s - 1]
        if s < first_gather:
            return ("extra", s - SPLIT_BITS - 1)
        order = [("spread", 0), ("spread", 1), ("spread", 2), ("side_back",)]
        order = order if kind == 0 else order[3:] + order[:3]
        return order[s - first_gather]

    def start_stage(c, kind, s):
        name = name_of(kind, s)
        if s == first_gather:
            whole[final(c, kind)] = acc[final(c, kind)]
        if name[0] == "core":
            core_copy(c).start()
        elif name[0] == "side":
            side_copy(c, kind).start()
        elif name[0] == "line":
            r = name[1]
            pl.when(place <= r)(lambda: line_copy(c, kind, r, 1).start())
            pl.when(place >= 3 - r)(lambda: line_copy(c, kind, r, 0).start())
        elif name[0] == "extra":
            extra_copy(c, kind, name[1]).start()
        elif name[0] == "spread":
            r = name[1]
            pl.when((place >= r) & (place <= 2))(lambda: spread_copy(c, kind, r, 1).start())
            pl.when((place >= 1) & (place <= 3 - r))(lambda: spread_copy(c, kind, r, 0).start())
        elif name[0] == "side_back":
            side_back_copy(c, kind).start()
        elif name[0] == "core_back":
            core_back_copy(c).start()
        else:
            save_copy(c).start()

    def finish_stage(c, kind, s):
        name = name_of(kind, s)
        if name[0] == "core":
            core_copy(c).wait()
            add_groups(low_core(c), 8, c, 0)
        elif name[0] == "side":
            side_copy(c, kind).wait()
            if kind == 0:
                add_groups(low_side(c), 4, c, 8)
            else:
                add_groups(final(c, kind), 1, c, 8)
        elif name[0] == "line":
            r = name[1]

            @pl.when(place <= r)
            def _():
                line_copy(c, kind, r, 1).wait_send()

            @pl.when(place >= 3 - r)
            def _():
                line_copy(c, kind, r, 0).wait_send()

            @pl.when((place >= 1) & (place <= r + 1))
            def _():
                line_copy(c, kind, r, 1).wait_recv()
                add_groups(block_start(c, kind, 2 - r + place), 1 + kind, c, 12 + 2 * (2 * r + 1))

            @pl.when((place <= 2) & (place >= 2 - r))
            def _():
                line_copy(c, kind, r, 0).wait_recv()
                add_groups(block_start(c, kind, r - 2 + place), 1 + kind, c, 12 + 2 * (2 * r))

        elif name[0] == "extra":
            extra_copy(c, kind, name[1]).wait()
            add_groups(final(c, kind), 1, c, 24 + name[1])
        elif name[0] == "spread":
            r = name[1]
            pl.when((place >= r) & (place <= 2))(lambda: spread_copy(c, kind, r, 1).wait_send())
            pl.when((place >= 1) & (place <= 3 - r))(lambda: spread_copy(c, kind, r, 0).wait_send())
            pl.when(place >= r + 1)(lambda: spread_copy(c, kind, r, 1).wait_recv())
            pl.when(place <= 2 - r)(lambda: spread_copy(c, kind, r, 0).wait_recv())
        elif name[0] == "side_back":
            side_back_copy(c, kind).wait()
        elif name[0] == "core_back":
            core_back_copy(c).wait()
        else:
            save_copy(c).wait()

    def small_copy(k):
        return pltpu.make_async_remote_copy(
            src_ref=small_acc.at[k],
            dst_ref=small_recv.at[k],
            send_sem=small_send_sem.at[k],
            recv_sem=small_recv_sem.at[k],
            device_id=bit_mate(k),
            device_id_type=MESH,
        )

    small_acc[0] = small_ref[...]

    def step(t, carry):
        for s in range(stages, 0, -1):
            c = t - LAG * s
            for kind in range(2):

                @pl.when((c >= 0) & (c < chunks) & (kind_of(c) == kind))
                def _():
                    finish_stage(c, kind, s - 1)
                    if s < stages:
                        start_stage(c, kind, s)

        for j in range(2 * wide + 4):

            @pl.when(t == per_block * j)
            def _():
                for kind, block in first_use[j]:
                    kind(block).wait()

        @pl.when(t < chunks)
        def _():
            block, part = t // per_block, t % per_block
            a_col = jnp.minimum(block, wide) + jnp.minimum(block // (2 * wide), 1) + jnp.minimum(block // (2 * wide + 1), 1)
            b_col = jnp.maximum(block - wide + 1, 0)
            lines = CHUNK_GROUPS * GROUP
            left = a_ref[:, pl.ds(pl.multiple_of(a_col * width + part * lines, lines), lines)]
            right = b_ref[:, pl.ds(pl.multiple_of(b_col * width, width), width)]
            grad = lax.dot_general(left, right, (((0,), (0,)), ((), ())), preferred_element_type=jnp.float32)
            acc[pl.ds(t * CHUNK_GROUPS, CHUNK_GROUPS)] = grad.astype(jnp.bfloat16).reshape(
                CHUNK_GROUPS, GROUP, width
            )
            core_copy(t).start()

        for k in range(bits + 1):

            @pl.when(t == LAG * k)
            def _():
                if k > 0:
                    small_copy(k - 1).wait()
                    small_acc[k] = small_acc[k - 1] + small_recv[k - 1]
                if k < bits:
                    small_copy(k).start()

        return carry

    lax.fori_loop(0, chunks + LAG * stages, step, 0)
    small_out[...] = small_acc[bits]


def reduced(a_side, b_side, small, count):
    rows = a_side.shape[0]
    width = small.shape[1]
    bits = count.bit_length() - 1
    extra = bits - SPLIT_BITS
    blocks = 2 * (a_side.shape[1] // width - 3) + 4
    chunks = blocks * width // (CHUNK_GROUPS * GROUP)
    groups = chunks * CHUNK_GROUPS
    loads = (a_side.shape[1] + b_side.shape[1]) // width
    return pl.pallas_call(
        functools.partial(reduce_kernel, bits, chunks),
        out_shape=(
            jax.ShapeDtypeStruct((groups, GROUP, width), jnp.bfloat16),
            jax.ShapeDtypeStruct(small.shape, jnp.float32),
        ),
        in_specs=[
            pl.BlockSpec(memory_space=pl.ANY),
            pl.BlockSpec(memory_space=pl.ANY),
            pl.BlockSpec(memory_space=pltpu.VMEM),
        ],
        out_specs=(pl.BlockSpec(memory_space=pl.ANY), pl.BlockSpec(memory_space=pltpu.VMEM)),
        scratch_shapes=[
            pltpu.VMEM(a_side.shape, jnp.bfloat16),
            pltpu.VMEM(b_side.shape, jnp.bfloat16),
            pltpu.VMEM((groups, GROUP, width), jnp.bfloat16),
            pltpu.VMEM((groups, GROUP, width), jnp.bfloat16),
            pltpu.VMEM((SLOTS, SLOT_GROUPS + extra, GROUP, width), jnp.bfloat16),
            pltpu.VMEM((bits + 1,) + small.shape, jnp.float32),
            pltpu.VMEM((bits,) + small.shape, jnp.float32),
            pltpu.SemaphoreType.DMA((loads,)),
            pltpu.SemaphoreType.DMA((SLOTS, 16 + extra)),
            pltpu.SemaphoreType.DMA((SLOTS, 16 + extra)),
            pltpu.SemaphoreType.DMA((SLOTS,)),
            pltpu.SemaphoreType.DMA((bits,)),
            pltpu.SemaphoreType.DMA((bits,)),
        ],
        compiler_params=pltpu.CompilerParams(
            collective_id=1, has_side_effects=True, vmem_limit_bytes=VMEM_LIMIT
        ),
        cost_estimate=pl.CostEstimate(
            flops=2 * rows * blocks * width * width, bytes_accessed=80_000_000, transcendentals=0
        ),
    )(a_side, b_side, small)


PIECE = 384
DEPTH = 4


def spread_kernel(sum_hbm, small_ref, *refs):
    width = small_ref.shape[1]
    (o_wq, o_bq, o_wk, o_wv, o_bv, o_wo, o_bo, o_g1, o_s1, o_up, o_bu, o_dn, o_bd, o_g2, o_s2) = refs[:15]
    taken, given, in_sem, out_sem = refs[15:]
    wide = o_bu.shape[1] // width
    targets = []
    for j in range(wide):
        targets += [o_dn.at[0, pl.ds(j * width + r, PIECE), :] for r in range(0, width, PIECE)]
    for j in range(wide):
        targets += [o_up.at[0, pl.ds(r, PIECE), pl.ds(j * width, width)] for r in range(0, width, PIECE)]
    for ref in (o_wo, o_wq, o_wk, o_wv):
        targets += [ref.at[0, pl.ds(r, PIECE), :] for r in range(0, width, PIECE)]

    def load(i):
        return pltpu.make_async_copy(
            sum_hbm.at[pl.ds(i * PIECE, PIECE)], taken.at[i % DEPTH], in_sem.at[i % DEPTH]
        )

    def store(i):
        return pltpu.make_async_copy(given.at[i % DEPTH], targets[i], out_sem.at[i % DEPTH])

    for i in range(DEPTH):
        load(i).start()
    singles = [o_bq, o_bv, o_bo, o_g1, o_s1, o_bd, o_g2, o_s2]
    for i, ref in enumerate(singles):
        ref[...] = small_ref[pl.ds(i, 1), :]
    for j in range(wide):
        o_bu[:, pl.ds(j * width, width)] = small_ref[pl.ds(len(singles) + j, 1), :]
    for i in range(len(targets)):
        load(i).wait()
        if i >= DEPTH:
            store(i - DEPTH).wait()

        def convert(r, carry):
            rows = pl.ds(pl.multiple_of(r * 64, 64), 64)
            given[i % DEPTH, rows, :] = taken[i % DEPTH, rows, :].astype(jnp.float32)
            return carry

        lax.fori_loop(0, PIECE // 64, convert, 0)
        store(i).start()
        if i + DEPTH < len(targets):
            load(i + DEPTH).start()
    for i in range(len(targets) - DEPTH, len(targets)):
        store(i).wait()


def spread(sums, small, params):
    width = small.shape[1]
    anywhere = pl.BlockSpec(memory_space=pl.ANY)
    local = pl.BlockSpec(memory_space=pltpu.VMEM)
    return pl.pallas_call(
        spread_kernel,
        out_shape=tuple(jax.ShapeDtypeStruct(member.shape, jnp.float32) for member in params),
        in_specs=[anywhere, local],
        out_specs=tuple(anywhere if len(member.shape) == 3 else local for member in params),
        scratch_shapes=[
            pltpu.VMEM((DEPTH, PIECE, width), jnp.bfloat16),
            pltpu.VMEM((DEPTH, PIECE, width), jnp.float32),
            pltpu.SemaphoreType.DMA((DEPTH,)),
            pltpu.SemaphoreType.DMA((DEPTH,)),
        ],
        compiler_params=pltpu.CompilerParams(vmem_limit_bytes=VMEM_LIMIT),
        cost_estimate=pl.CostEstimate(
            flops=12 * width * width, bytes_accessed=80 * width * width, transcendentals=0
        ),
    )(sums, small)


SINGLES = ("bq", "bv", "bo", "g1", "s1", "bd", "g2", "s2")


def product(left, right):
    return lax.dot_general(left, right, (((1,), (0,)), ((), ())), preferred_element_type=jnp.float32)


def product_t(left, right):
    return lax.dot_general(left, right, (((1,), (1,)), ((), ())), preferred_element_type=jnp.float32)


def gelu_pair(z):
    cdf = 0.5 + 0.5 * lax.erf(z * (1.0 / math.sqrt(2.0)))
    bell = jnp.exp(-0.5 * z * z)
    return z * cdf, cdf + z * bell * (1.0 / math.sqrt(2.0 * math.pi))


def normed(values):
    average = jnp.mean(values, axis=-1, keepdims=True)
    centered = values - average
    inverse = lax.rsqrt(jnp.mean(centered * centered, axis=-1, keepdims=True) + EPSILON)
    return centered * inverse, inverse


def normed_back(grad, normal, inverse):
    first_mean = jnp.mean(grad, axis=-1, keepdims=True)
    second_mean = jnp.mean(grad * normal, axis=-1, keepdims=True)
    return inverse * (grad - first_mean - normal * second_mean)


def layer_kernel(
    ids_ref,
    lengths_ref,
    captions_ref,
    regions_ref,
    cotangent_hbm,
    wq_hbm,
    bq_ref,
    wk_hbm,
    wv_hbm,
    bv_ref,
    wo_hbm,
    bo_ref,
    g1_ref,
    s1_ref,
    wu_hbm,
    bu_ref,
    wd_hbm,
    bd_ref,
    g2_ref,
    s2_ref,
    states_hbm,
    grads_hbm,
    a_hbm,
    b_hbm,
    small_ref,
    wqkv,
    wo,
    wu,
    wd,
    table,
    hidden,
    upstream,
    query,
    keys,
    values,
    probs,
    context,
    normal1,
    normal2,
    lowered,
    active,
    slope,
    result,
    grad_in,
    staged,
    inverse1,
    inverse2,
    wide1,
    wide2,
    d_context,
    d_scores,
    weight_sem,
    table_send,
    table_recv,
    fwd_send,
    fwd_recv,
    back_send,
    back_recv,
    out_sem,
):
    items, rows, width = hidden.shape
    held = regions_ref.shape[0]
    cap_rows = captions_ref.shape[1]
    wide = wu.shape[1] // width
    pairs = HEADS // 2
    pair_width = width // pairs
    head = width // HEADS
    section = lax.axis_index("section")
    batch = lax.axis_index("batch")
    count = lax.axis_size("batch")
    right = (section, lax.rem(batch + 1, count))
    left = (section, lax.rem(batch + count - 1, count))
    other = (1 - section, batch)

    weight_copies = [
        pltpu.make_async_copy(source.at[0], target, weight_sem.at[n])
        for n, (source, target) in enumerate(
            (
                (wq_hbm, wqkv.at[:, pl.ds(0, width)]),
                (wk_hbm, wqkv.at[:, pl.ds(width, width)]),
                (wv_hbm, wqkv.at[:, pl.ds(2 * width, width)]),
                (wo_hbm, wo),
                (wu_hbm, wu),
                (wd_hbm, wd),
            )
        )
    ]
    for copy in weight_copies:
        copy.start()
    cotangent_copy = pltpu.make_async_copy(cotangent_hbm, upstream, weight_sem.at[6])

    barrier = pltpu.get_barrier_semaphore()
    for peer in (right, left, other):
        pl.semaphore_signal(barrier, inc=1, device_id=peer, device_id_type=MESH)
    pl.semaphore_wait(barrier, 3)

    def table_copy(n, peer):
        return pltpu.make_async_remote_copy(
            src_ref=regions_ref,
            dst_ref=table.at[pl.ds(2 * n * held, held)],
            send_sem=table_send.at[n],
            recv_sem=table_recv.at[n],
            device_id=peer,
            device_id_type=MESH,
        )

    @pl.when(section == 0)
    def _():
        table_copy(0, right).start()
        table_copy(1, left).start()
        table[pl.ds(held, held)] = regions_ref[...]
        table_copy(0, right).wait()
        table_copy(1, left).wait()

    @pl.when(section == 1)
    def _():
        cotangent_copy.start()

    def forward_copy(i):
        return pltpu.make_async_remote_copy(
            src_ref=result.at[i],
            dst_ref=hidden.at[i],
            send_sem=fwd_send.at[i],
            recv_sem=fwd_recv.at[i],
            device_id=other,
            device_id_type=MESH,
        )

    def back_copy(i):
        return pltpu.make_async_remote_copy(
            src_ref=grad_in.at[i],
            dst_ref=upstream.at[i],
            send_sem=back_send.at[i],
            recv_sem=back_recv.at[i],
            device_id=other,
            device_id_type=MESH,
        )

    def saves(i):
        at = pl.ds(pl.multiple_of(i * rows, rows), rows)
        first = wide * width
        sources = (
            (active.at[i], a_hbm.at[at, pl.ds(0, first)]),
            (lowered.at[i], a_hbm.at[at, pl.ds(first, width)]),
            (context.at[i], a_hbm.at[at, pl.ds(first + width, width)]),
            (hidden.at[i], a_hbm.at[at, pl.ds(first + 2 * width, width)]),
            (result.at[i], states_hbm.at[0, i]),
        )
        return [pltpu.make_async_copy(s, d, out_sem.at[i, n]) for n, (s, d) in enumerate(sources)]

    def staged_save(i):
        at = pl.ds(pl.multiple_of(i * rows, rows), rows)
        return pltpu.make_async_copy(staged.at[lax.rem(i, 2)], b_hbm.at[at], out_sem.at[i, 5])

    def grad_save(i):
        return pltpu.make_async_copy(grad_in.at[i], grads_hbm.at[0, i], out_sem.at[i, 6])

    def vector(ref, j=0):
        return ref[:, j * width : (j + 1) * width].astype(jnp.float32)

    lane = lax.broadcasted_iota(jnp.int32, (rows, pair_width), 1)

    blocks = [slice(r, r + GROUP) for r in range(0, rows, GROUP)]
    spans = [slice(c, min(c + 128, rows)) for c in range(0, rows, 128)]

    def only(block, h):
        return jnp.where((lane // head) == h, block, jnp.zeros_like(block))

    def assemble(i):
        total = count * held
        spot = jnp.minimum(lax.rem(ids_ref[i] - (batch - 1) * held + total, total), 3 * held - 1)
        whole = jnp.concatenate(
            [captions_ref[i].astype(jnp.float32), table[spot].astype(jnp.float32)], axis=0
        )
        hidden[i] = whole.astype(jnp.bfloat16)

    def forward(i):
        @pl.when(i == 0)
        def _():
            for copy in weight_copies[:3]:
                copy.wait()

        source = hidden[i]
        mixed = product(source, wqkv[...])
        for at in blocks:
            scaled = (mixed[at, :width] + vector(bq_ref)) * (1.0 / math.sqrt(head))
            query[i, at, :] = scaled.astype(jnp.bfloat16)
            keys[i, at, :] = mixed[at, width : 2 * width].astype(jnp.bfloat16)
            values[i, at, :] = (mixed[at, 2 * width :] + vector(bv_ref)).astype(jnp.bfloat16)
        position = lax.broadcasted_iota(jnp.int32, (rows, 1), 0)
        live = (position >= cap_rows) | (position < lengths_ref[i])
        key_bias = jnp.where(live, 0.0, -1000000000.0)

        def lanes_of(p):
            return slice(p * pair_width, (p + 1) * pair_width)

        def scored(p):
            k_pair = keys[i, :, lanes_of(p)]
            stacked = jnp.concatenate([only(k_pair, 0), only(k_pair, 1)], axis=0)
            v_turned = values[i, :, lanes_of(p)].astype(jnp.float32).T.astype(jnp.bfloat16)
            return product_t(stacked, query[i, :, lanes_of(p)]), v_turned

        def weighed(p, both):
            for h in range(2):
                for span in spans:
                    scores = both[h * rows : (h + 1) * rows, span] + key_bias
                    expo = jnp.exp(scores - jnp.max(scores, axis=0, keepdims=True))
                    share = pl.reciprocal(jnp.sum(expo, axis=0, keepdims=True))
                    probs[i, 2 * p + h, :, span] = (expo * share).astype(jnp.bfloat16)

        def mixed_values(p, v_turned):
            return [product(v_turned[h * head : (h + 1) * head], probs[i, 2 * p + h]) for h in range(2)]

        def place_context(p, parts):
            context[i, :, lanes_of(p)] = jnp.concatenate(parts, axis=0).T.astype(jnp.bfloat16)

        ahead = scored(0)
        parts = None
        for p in range(pairs):
            both, v_turned = ahead
            if p + 1 < pairs:
                ahead = scored(p + 1)
            if parts is not None:
                place_context(p - 1, parts)
            weighed(p, both)
            parts = mixed_values(p, v_turned)
        place_context(pairs - 1, parts)

        @pl.when(i == 0)
        def _():
            for copy in weight_copies[3:]:
                copy.wait()

        attended = product(context[i], wo[...])
        for at in blocks:
            n1, inv1 = normed(hidden[i, at, :].astype(jnp.float32) + attended[at] + vector(bo_ref))
            normal1[i, at, :] = n1.astype(jnp.bfloat16)
            inverse1[i, at, :] = inv1
            first = n1 * vector(g1_ref) + vector(s1_ref)
            lowered[i, at, :] = first.astype(jnp.bfloat16)
            wide1[at, :] = first + vector(bd_ref)
        low = lowered[i]
        tile = 2 * width // 3
        tiles = wide * width // tile

        def raised(n):
            return product(low, wu[:, n * tile : (n + 1) * tile])

        z_next = raised(0)
        half = tiles // 2
        for n in range(tiles):
            lanes = slice(n * tile, (n + 1) * tile)
            z_tile = z_next
            if n + 1 < tiles:
                z_next = raised(n + 1)
            if n == half:
                wide1[...] += product(active[i, :, : half * tile], wd[: half * tile, :])
            for at in blocks:
                gelu, slant = gelu_pair(z_tile[at] + bu_ref[:, lanes].astype(jnp.float32))
                active[i, at, lanes] = gelu.astype(jnp.bfloat16)
                slope[i, at, lanes] = slant.astype(jnp.bfloat16)
        lowest = product(active[i, :, half * tile :], wd[half * tile :, :])
        for at in blocks:
            n2, inv2 = normed(wide1[at, :] + lowest[at])
            normal2[i, at, :] = n2.astype(jnp.bfloat16)
            inverse2[i, at, :] = inv2
            result[i, at, :] = (n2 * vector(g2_ref) + vector(s2_ref)).astype(jnp.bfloat16)

    def folded(value):
        return value[: GROUP // 2] + value[GROUP // 2 :]

    def keep_small(row, value):
        small_ref[row : row + 1, :] += jnp.sum(value, axis=0, keepdims=True)

    def single(name, value):
        keep_small(SINGLES.index(name), value)

    def backward(i):
        slot = lax.rem(i, 2)
        base = (2 + wide) * width

        def stage(at, column, value):
            staged[slot, at, column * width : (column + 1) * width] = value

        def norm_step(at, gradient, normal, inverse, gain, sums):
            n = normal[i, at, :].astype(jnp.float32)
            d_res = normed_back(gradient * vector(gain), n, inverse[i, at, :])
            d_low = d_res.astype(jnp.bfloat16)
            terms = [folded(gradient * n), folded(gradient), folded(d_low.astype(jnp.float32))]
            return d_res, d_low, terms if sums is None else [a + b for a, b in zip(sums, terms)]

        sums = None
        for at in blocks:
            gradient = upstream[i, at, :].astype(jnp.float32)
            d_res, d_low, sums = norm_step(at, gradient, normal2, inverse2, g2_ref, sums)
            wide1[at, :] = d_res
            stage(at, 0, d_low)
        for name, value in zip(("g2", "s2", "bd"), sums):
            single(name, value)
        d_out = staged[slot, :, :width]
        for j in range(wide):
            lanes = slice(j * width, (j + 1) * width)
            d_active = product_t(d_out, wd[lanes, :])
            total = None
            for at in blocks:
                d_inner = (d_active[at] * slope[i, at, lanes].astype(jnp.float32)).astype(jnp.bfloat16)
                stage(at, 1 + j, d_inner)
                term = folded(d_inner.astype(jnp.float32))
                total = term if total is None else total + term
            keep_small(len(SINGLES) + j, total)
        d_deep = product_t(staged[slot, :, width : (1 + wide) * width], wu[...])
        sums = None
        for at in blocks:
            d_res, d_low, sums = norm_step(at, wide1[at, :] + d_deep[at], normal1, inverse1, g1_ref, sums)
            wide2[at, :] = d_res
            stage(at, 1 + wide, d_low)
        for name, value in zip(("g1", "s1", "bo"), sums):
            single(name, value)
        d_att = staged[slot, :, (1 + wide) * width : (2 + wide) * width]
        d_context[...] = product_t(d_att, wo[...]).astype(jnp.bfloat16)

        def lanes_of(p):
            return slice(p * pair_width, (p + 1) * pair_width)

        def place_grad(n, p, block):
            at = base + n * width + p * pair_width
            staged[slot, :, at : at + pair_width] = block.astype(jnp.bfloat16)

        def opened(p):
            v_pair = values[i, :, lanes_of(p)]
            c_pair = d_context[:, lanes_of(p)]
            stacked = jnp.concatenate([only(v_pair, 0), only(v_pair, 1)], axis=0)
            k_turned = keys[i, :, lanes_of(p)].astype(jnp.float32).T.astype(jnp.bfloat16)
            d_value = product(probs[i, 2 * p], only(c_pair, 0))
            d_value += product(probs[i, 2 * p + 1], only(c_pair, 1))
            return product_t(stacked, c_pair), k_turned, d_value

        def score_grads(p, both):
            for h in range(2):
                for span in spans:
                    prob = probs[i, 2 * p + h, :, span].astype(jnp.float32)
                    d_prob = both[h * rows : (h + 1) * rows, span]
                    drift = jnp.sum(d_prob * prob, axis=0, keepdims=True)
                    d_scores[p % 2, h, :, span] = (prob * (d_prob - drift)).astype(jnp.bfloat16)
            return [d_scores[p % 2, h] for h in range(2)]

        def closed(p, found, k_turned):
            q_pair = query[i, :, lanes_of(p)]
            d_key = product(found[0], only(q_pair, 0)) + product(found[1], only(q_pair, 1))
            return d_key, [product(k_turned[h * head : (h + 1) * head], found[h]) for h in range(2)]

        def place_grads(p, d_value, d_key, parts):
            place_grad(0, p, jnp.concatenate(parts, axis=0).T * (1.0 / math.sqrt(head)))
            place_grad(1, p, d_key)
            place_grad(2, p, d_value)

        ahead = opened(0)
        waiting = None
        for p in range(pairs):
            both, k_turned, d_value = ahead
            if p + 1 < pairs:
                ahead = opened(p + 1)
            if waiting is not None:
                place_grads(*waiting)
            found = score_grads(p, both)
            d_key, parts = closed(p, found, k_turned)
            waiting = (p, d_value, d_key, parts)
        place_grads(*waiting)
        d_source = product_t(staged[slot, :, base : base + 3 * width], wqkv[...])
        sums = None
        for at in blocks:
            grad_in[i, at, :] = (wide2[at, :] + d_source[at]).astype(jnp.bfloat16)
            terms = [
                folded(staged[slot, at, base : base + width].astype(jnp.float32)),
                folded(staged[slot, at, base + 2 * width : base + 3 * width].astype(jnp.float32)),
            ]
            sums = terms if sums is None else [a + b for a, b in zip(sums, terms)]
        single("bq", sums[0])
        single("bv", sums[1])

    small_ref[...] = jnp.zeros_like(small_ref)

    def forward_step(i, carry):
        @pl.when(section == 0)
        def _():
            assemble(i)

        @pl.when(section == 1)
        def _():
            forward_copy(i).wait_recv()

        forward(i)

        @pl.when(section == 0)
        def _():
            forward_copy(i).start()

        for copy in saves(i):
            copy.start()
        return carry

    lax.fori_loop(0, items, forward_step, 0)

    @pl.when(section == 1)
    def _():
        cotangent_copy.wait()

    def backward_step(i, carry):
        @pl.when(section == 0)
        def _():
            back_copy(i).wait_recv()

        @pl.when(i >= 2)
        def _():
            staged_save(i - 2).wait()

        backward(i)

        @pl.when(section == 1)
        def _():
            back_copy(i).start()

        staged_save(i).start()
        grad_save(i).start()
        return carry

    lax.fori_loop(0, items, backward_step, 0)

    def finish(i, carry):
        for copy in saves(i):
            copy.wait()
        grad_save(i).wait()

        @pl.when(i >= items - 2)
        def _():
            staged_save(i).wait()

        @pl.when(section == 0)
        def _():
            forward_copy(i).wait_send()

        @pl.when(section == 1)
        def _():
            back_copy(i).wait_send()

        return carry

    lax.fori_loop(0, items, finish, 0)


def layered(image_ids, caption_lengths, captions, regions, cotangent, stacked):
    items, cap_rows, width = captions.shape
    held, region_rows, _ = regions.shape
    rows = cap_rows + region_rows
    inner = stacked[9].shape[2]
    low = jnp.bfloat16
    wide = inner // width

    def cells(*shape):
        return pltpu.VMEM(shape, low)

    anywhere = pl.BlockSpec(memory_space=pl.ANY)
    local = pl.BlockSpec(memory_space=pltpu.VMEM)
    scalars = pl.BlockSpec(memory_space=pltpu.SMEM)
    return pl.pallas_call(
        layer_kernel,
        out_shape=(
            jax.ShapeDtypeStruct((1, items, rows, width), low),
            jax.ShapeDtypeStruct((1, items, rows, width), low),
            jax.ShapeDtypeStruct((items * rows, (3 + wide) * width), low),
            jax.ShapeDtypeStruct((items * rows, (5 + wide) * width), low),
            jax.ShapeDtypeStruct((GROUP, width), jnp.float32),
        ),
        in_specs=[scalars, scalars, local, local, anywhere]
        + [anywhere if len(member.shape) == 3 else local for member in stacked],
        out_specs=(anywhere, anywhere, anywhere, anywhere, local),
        scratch_shapes=[
            cells(width, 3 * width),
            cells(width, width),
            cells(width, inner),
            cells(inner, width),
            cells(3 * held, region_rows, width),
            cells(items, rows, width),
            cells(items, rows, width),
            cells(items, rows, width),
            cells(items, rows, width),
            cells(items, rows, width),
            cells(items, HEADS, rows, rows),
            cells(items, rows, width),
            cells(items, rows, width),
            cells(items, rows, width),
            cells(items, rows, width),
            cells(items, rows, inner),
            cells(items, rows, inner),
            cells(items, rows, width),
            cells(items, rows, width),
            cells(2, rows, (5 + wide) * width),
            pltpu.VMEM((items, rows, 1), jnp.float32),
            pltpu.VMEM((items, rows, 1), jnp.float32),
            pltpu.VMEM((rows, width), jnp.float32),
            pltpu.VMEM((rows, width), jnp.float32),
            cells(rows, width),
            cells(2, 2, rows, rows),
            pltpu.SemaphoreType.DMA((7,)),
            pltpu.SemaphoreType.DMA((2,)),
            pltpu.SemaphoreType.DMA((2,)),
            pltpu.SemaphoreType.DMA((items,)),
            pltpu.SemaphoreType.DMA((items,)),
            pltpu.SemaphoreType.DMA((items,)),
            pltpu.SemaphoreType.DMA((items,)),
            pltpu.SemaphoreType.DMA((items, 7)),
        ],
        compiler_params=pltpu.CompilerParams(
            collective_id=0, has_side_effects=True, vmem_limit_bytes=VMEM_LIMIT
        ),
        cost_estimate=pl.CostEstimate(
            flops=4 * items * rows * (4 + 2 * wide) * width * width,
            bytes_accessed=60_000_000,
            transcendentals=0,
        ),
    )(image_ids, caption_lengths, captions, regions, cotangent, *stacked)


def body(
    captions,
    regions,
    image_ids,
    caption_lengths,
    cotangent,
    query_weight,
    query_bias,
    key_weight,
    value_weight,
    value_bias,
    out_weight,
    out_bias,
    norm1_gain,
    norm1_bias,
    up_weight,
    up_bias,
    down_weight,
    down_bias,
    norm2_gain,
    norm2_bias,
):
    stacked = (
        query_weight,
        query_bias,
        key_weight,
        value_weight,
        value_bias,
        out_weight,
        out_bias,
        norm1_gain,
        norm1_bias,
        up_weight,
        up_bias,
        down_weight,
        down_bias,
        norm2_gain,
        norm2_bias,
    )
    width = captions.shape[2]
    states, input_grads, a_side, b_side, small = layered(
        image_ids, caption_lengths, captions, regions, cotangent, stacked
    )
    sums, small_sums = reduced(a_side, b_side, small, lax.axis_size("batch"))
    grads = spread(sums.reshape(-1, width), small_sums, stacked)
    return (states, input_grads) + tuple(grads)


def solution(mesh):
    placed = (
        P("batch", None, None),
        P("batch", None, None),
        P("batch"),
        P("batch"),
        P("batch", None, None),
        P("section", None, None),
        P("section", None),
        P("section", None, None),
        P("section", None, None),
        P("section", None),
        P("section", None, None),
        P("section", None),
        P("section", None),
        P("section", None),
        P("section", None, None),
        P("section", None),
        P("section", None, None),
        P("section", None),
        P("section", None),
        P("section", None),
    )
    return jax.shard_map(
        body,
        mesh=mesh,
        in_specs=placed,
        out_specs=(
            P("section", "batch", None, None),
            P("section", "batch", None, None),
            P("section", None, None),
            P("section", None),
            P("section", None, None),
            P("section", None, None),
            P("section", None),
            P("section", None, None),
            P("section", None),
            P("section", None),
            P("section", None),
            P("section", None, None),
            P("section", None),
            P("section", None, None),
            P("section", None),
            P("section", None),
            P("section", None),
        ),
        check_vma=False,
    )
```

```python
import functools
import math

import jax
import jax.numpy as jnp
from jax import lax
from jax.experimental import pallas as pl
from jax.experimental.pallas import tpu as pltpu
from jax.sharding import PartitionSpec as P

HEADS = 12
EPSILON = 1e-12
MESH = pl.DeviceIdType.MESH
VMEM_LIMIT = 62 * 1024 * 1024
GROUP = 16
CHUNK_GROUPS = 16
SLOTS = 16
SLOT_GROUPS = 24
LAGS = ((0, 1, 3, 4, 5, 6, 7, 8, 9, 11, 12, 13), (0, 1, 2, 3, 4, 5, 6, 7, 8, 9, 10, 11))
LINE = 4
SPLIT_BITS = 4


def reduce_kernel(
    bits,
    chunks,
    a_hbm,
    b_hbm,
    small_ref,
    out_hbm,
    small_out,
    a_ref,
    b_ref,
    acc,
    whole,
    recv,
    small_acc,
    small_recv,
    load_sem,
    send_sem,
    recv_sem,
    save_sem,
    small_send_sem,
    small_recv_sem,
):
    width = acc.shape[2]
    extra = bits - SPLIT_BITS
    first_gather = SPLIT_BITS + 1 + extra
    stages = 2 * (SPLIT_BITS + 1) + extra + 1
    me = lax.axis_index("batch")
    section = lax.axis_index("section")
    core, side, place = me % 2, (me // 2) % 2, (me // 4) % LINE
    lags = []
    for table in LAGS:
        cut = SPLIT_BITS + 1
        lags.append(
            [table[s] for s in range(cut + 1)]
            + [table[cut] + e + 1 for e in range(extra)]
            + [table[s] + extra for s in range(cut + 1, len(table))]
        )
    blocks_a = a_hbm.shape[1] // width
    blocks_b = b_hbm.shape[1] // width
    per_block = width // (CHUNK_GROUPS * GROUP)

    def load(source, target, block, base):
        lanes = pl.ds(block * width, width)
        return pltpu.make_async_copy(source.at[:, lanes], target.at[:, lanes], load_sem.at[base + block])

    def load_a(block):
        return load(a_hbm, a_ref, block, 0)

    def load_b(block):
        return load(b_hbm, b_ref, block, blocks_a)

    wide = blocks_a - 3
    first_use = {0: [(load_a, 0), (load_b, 0)]}
    for j in range(1, wide):
        first_use[j] = [(load_a, j)]
    first_use[wide] = [(load_a, wide), (load_b, 1)]
    for j in range(1, wide):
        first_use[wide + j] = [(load_b, 1 + j)]
    first_use[2 * wide] = [(load_a, wide + 1), (load_b, wide + 1)]
    first_use[2 * wide + 1] = [(load_a, wide + 2), (load_b, wide + 2)]
    first_use[2 * wide + 2] = [(load_b, wide + 3)]
    first_use[2 * wide + 3] = [(load_b, wide + 4)]
    for j in range(2 * wide + 4):
        for kind, block in first_use[j]:
            kind(block).start()

    def bit_mate(k):
        bit = (me // 2**k) % 2
        return (section, me + 2**k * (1 - 2 * bit))

    core_mate, side_mate = bit_mate(0), bit_mate(1)
    mates = ((section, me - LINE), (section, me + LINE))
    ring = [(section, me + LINE * ((place + d) % LINE - place)) for d in (LINE - 1, 1)]

    barrier = pltpu.get_barrier_semaphore()
    for peer in [core_mate, side_mate] + ring + [bit_mate(k) for k in range(2, bits)]:
        pl.semaphore_signal(barrier, inc=1, device_id=peer, device_id_type=MESH)
    pl.semaphore_wait(barrier, bits + 2)

    def kind_of(c):
        return (c % 5) % 2

    def low_core(c):
        return c * CHUNK_GROUPS + core * 8

    def low_side(c):
        return low_core(c) + side * 4

    def block_start(c, kind, b):
        return low_side(c) + b if kind == 0 else low_core(c) + 2 * b

    def final(c, kind):
        return low_side(c) + place if kind == 0 else low_core(c) + 2 * place + side

    def remote(c, source, start, size, target, spot, index, peer):
        return pltpu.make_async_remote_copy(
            src_ref=source.at[pl.ds(start, size)],
            dst_ref=target.at[c % SLOTS, pl.ds(spot, size)] if target is recv else target.at[pl.ds(start, size)],
            send_sem=send_sem.at[c % SLOTS, index],
            recv_sem=recv_sem.at[c % SLOTS, index],
            device_id=peer,
            device_id_type=MESH,
        )

    def core_copy(c):
        return remote(c, acc, c * CHUNK_GROUPS + (1 - core) * 8, 8, recv, 0, 0, core_mate)

    def side_copy(c, kind):
        if kind == 0:
            return remote(c, acc, low_core(c) + (1 - side) * 4, 4, recv, 8, 1, side_mate)
        return remote(c, acc, low_core(c) + 2 * place + (1 - side), 1, recv, 8, 1, side_mate)

    def line_copy(c, kind, r, d):
        size = 1 + kind
        b = jnp.minimum(3 - r + place, 3) if d == 1 else jnp.maximum(r - 3 + place, 0)
        spot = 12 + 2 * (2 * r + d)
        return remote(c, acc, block_start(c, kind, b), size, recv, spot, 2 + 2 * r + d, mates[d])

    def spread_copy(c, kind, r, d):
        size = 1 + kind
        b = jnp.maximum(place - r, 0) if d == 1 else jnp.minimum(place + r, 3)
        return remote(c, whole, block_start(c, kind, b), size, whole, 0, 8 + 2 * r + d, mates[d])

    def side_back_copy(c, kind):
        if kind == 0:
            return remote(c, whole, low_side(c), 4, whole, 0, 14, side_mate)
        return remote(c, whole, final(c, kind), 1, whole, 0, 14, side_mate)

    def core_back_copy(c):
        return remote(c, whole, low_core(c), 8, whole, 0, 15, core_mate)

    def extra_copy(c, kind, e):
        return remote(c, acc, final(c, kind), 1, recv, 24 + e, 16 + e, bit_mate(SPLIT_BITS + e))

    def save_copy(c):
        at = pl.ds(c * CHUNK_GROUPS, CHUNK_GROUPS)
        return pltpu.make_async_copy(whole.at[at], out_hbm.at[at], save_sem.at[c % SLOTS])

    def add_groups(start, count, c, spot):
        def one(g, carry):
            total = acc[start + g].astype(jnp.float32) + recv[c % SLOTS, spot + g].astype(jnp.float32)
            acc[start + g] = total.astype(jnp.bfloat16)
            return carry

        lax.fori_loop(0, count, one, 0)

    def name_of(kind, s):
        if s == 0:
            return ("core",)
        if s == stages - 1:
            return ("save",)
        if s == stages - 2:
            return ("core_back",)
        if s < SPLIT_BITS + 1:
            order = [("side",), ("line", 0), ("line", 1), ("line", 2)]
            order = order if kind == 0 else order[1:] + order[:1]
            return order[s - 1]
        if s < first_gather:
            return ("extra", s - SPLIT_BITS - 1)
        order = [("spread", 0), ("spread", 1), ("spread", 2), ("side_back",)]
        order = order if kind == 0 else order[3:] + order[:3]
        return order[s - first_gather]

    def start_stage(c, kind, s):
        name = name_of(kind, s)
        if s == first_gather:
            whole[final(c, kind)] = acc[final(c, kind)]
        if name[0] == "core":
            core_copy(c).start()
        elif name[0] == "side":
            side_copy(c, kind).start()
        elif name[0] == "line":
            r = name[1]
            pl.when(place <= r)(lambda: line_copy(c, kind, r, 1).start())
            pl.when(place >= 3 - r)(lambda: line_copy(c, kind, r, 0).start())
        elif name[0] == "extra":
            extra_copy(c, kind, name[1]).start()
        elif name[0] == "spread":
            r = name[1]
            pl.when((place >= r) & (place <= 2))(lambda: spread_copy(c, kind, r, 1).start())
            pl.when((place >= 1) & (place <= 3 - r))(lambda: spread_copy(c, kind, r, 0).start())
        elif name[0] == "side_back":
            side_back_copy(c, kind).start()
        elif name[0] == "core_back":
            core_back_copy(c).start()
        else:
            save_copy(c).start()

    def finish_stage(c, kind, s):
        name = name_of(kind, s)
        if name[0] == "core":
            core_copy(c).wait()
            add_groups(low_core(c), 8, c, 0)
        elif name[0] == "side":
            side_copy(c, kind).wait()
            if kind == 0:
                add_groups(low_side(c), 4, c, 8)
            else:
                add_groups(final(c, kind), 1, c, 8)
        elif name[0] == "line":
            r = name[1]

            @pl.when(place <= r)
            def _():
                line_copy(c, kind, r, 1).wait_send()

            @pl.when(place >= 3 - r)
            def _():
                line_copy(c, kind, r, 0).wait_send()

            @pl.when((place >= 1) & (place <= r + 1))
            def _():
                line_copy(c, kind, r, 1).wait_recv()
                add_groups(block_start(c, kind, 2 - r + place), 1 + kind, c, 12 + 2 * (2 * r + 1))

            @pl.when((place <= 2) & (place >= 2 - r))
            def _():
                line_copy(c, kind, r, 0).wait_recv()
                add_groups(block_start(c, kind, r - 2 + place), 1 + kind, c, 12 + 2 * (2 * r))

        elif name[0] == "extra":
            extra_copy(c, kind, name[1]).wait()
            add_groups(final(c, kind), 1, c, 24 + name[1])
        elif name[0] == "spread":
            r = name[1]
            pl.when((place >= r) & (place <= 2))(lambda: spread_copy(c, kind, r, 1).wait_send())
            pl.when((place >= 1) & (place <= 3 - r))(lambda: spread_copy(c, kind, r, 0).wait_send())
            pl.when(place >= r + 1)(lambda: spread_copy(c, kind, r, 1).wait_recv())
            pl.when(place <= 2 - r)(lambda: spread_copy(c, kind, r, 0).wait_recv())
        elif name[0] == "side_back":
            side_back_copy(c, kind).wait()
        elif name[0] == "core_back":
            core_back_copy(c).wait()
        else:
            save_copy(c).wait()

    def small_copy(k):
        return pltpu.make_async_remote_copy(
            src_ref=small_acc.at[k],
            dst_ref=small_recv.at[k],
            send_sem=small_send_sem.at[k],
            recv_sem=small_recv_sem.at[k],
            device_id=bit_mate(k),
            device_id_type=MESH,
        )

    small_acc[0] = small_ref[...]

    def step(t, carry):
        for s in range(stages, 0, -1):
            for kind in range(2):
                c = t - lags[kind][s]

                @pl.when((c >= 0) & (c < chunks) & (kind_of(c) == kind))
                def _():
                    finish_stage(c, kind, s - 1)
                    if s < stages:
                        start_stage(c, kind, s)

        for j in range(2 * wide + 4):

            @pl.when(t == per_block * j)
            def _():
                for kind, block in first_use[j]:
                    kind(block).wait()

        @pl.when(t < chunks)
        def _():
            block, part = t // per_block, t % per_block
            a_col = jnp.minimum(block, wide) + jnp.minimum(block // (2 * wide), 1) + jnp.minimum(block // (2 * wide + 1), 1)
            b_col = jnp.maximum(block - wide + 1, 0)
            lines = CHUNK_GROUPS * GROUP
            left = a_ref[:, pl.ds(pl.multiple_of(a_col * width + part * lines, lines), lines)]
            right = b_ref[:, pl.ds(pl.multiple_of(b_col * width, width), width)]
            grad = lax.dot_general(left, right, (((0,), (0,)), ((), ())), preferred_element_type=jnp.float32)
            acc[pl.ds(t * CHUNK_GROUPS, CHUNK_GROUPS)] = grad.astype(jnp.bfloat16).reshape(
                CHUNK_GROUPS, GROUP, width
            )
            core_copy(t).start()

        for k in range(bits + 1):

            @pl.when(t == 2 * k)
            def _():
                if k > 0:
                    small_copy(k - 1).wait()
                    small_acc[k] = small_acc[k - 1] + small_recv[k - 1]
                if k < bits:
                    small_copy(k).start()

        return carry

    lax.fori_loop(0, chunks + max(table[stages] for table in lags), step, 0)
    small_out[...] = small_acc[bits]


def reduced(a_side, b_side, small, count):
    rows = a_side.shape[0]
    width = small.shape[1]
    bits = count.bit_length() - 1
    extra = bits - SPLIT_BITS
    blocks = 2 * (a_side.shape[1] // width - 3) + 4
    chunks = blocks * width // (CHUNK_GROUPS * GROUP)
    groups = chunks * CHUNK_GROUPS
    loads = (a_side.shape[1] + b_side.shape[1]) // width
    return pl.pallas_call(
        functools.partial(reduce_kernel, bits, chunks),
        out_shape=(
            jax.ShapeDtypeStruct((groups, GROUP, width), jnp.bfloat16),
            jax.ShapeDtypeStruct(small.shape, jnp.float32),
        ),
        in_specs=[
            pl.BlockSpec(memory_space=pl.ANY),
            pl.BlockSpec(memory_space=pl.ANY),
            pl.BlockSpec(memory_space=pltpu.VMEM),
        ],
        out_specs=(pl.BlockSpec(memory_space=pl.ANY), pl.BlockSpec(memory_space=pltpu.VMEM)),
        scratch_shapes=[
            pltpu.VMEM(a_side.shape, jnp.bfloat16),
            pltpu.VMEM(b_side.shape, jnp.bfloat16),
            pltpu.VMEM((groups, GROUP, width), jnp.bfloat16),
            pltpu.VMEM((groups, GROUP, width), jnp.bfloat16),
            pltpu.VMEM((SLOTS, SLOT_GROUPS + extra, GROUP, width), jnp.bfloat16),
            pltpu.VMEM((bits + 1,) + small.shape, jnp.float32),
            pltpu.VMEM((bits,) + small.shape, jnp.float32),
            pltpu.SemaphoreType.DMA((loads,)),
            pltpu.SemaphoreType.DMA((SLOTS, 16 + extra)),
            pltpu.SemaphoreType.DMA((SLOTS, 16 + extra)),
            pltpu.SemaphoreType.DMA((SLOTS,)),
            pltpu.SemaphoreType.DMA((bits,)),
            pltpu.SemaphoreType.DMA((bits,)),
        ],
        compiler_params=pltpu.CompilerParams(
            collective_id=1, has_side_effects=True, vmem_limit_bytes=VMEM_LIMIT
        ),
        cost_estimate=pl.CostEstimate(
            flops=2 * rows * blocks * width * width, bytes_accessed=80_000_000, transcendentals=0
        ),
    )(a_side, b_side, small)


PIECE = 384
DEPTH = 4


def spread_kernel(sum_hbm, small_ref, *refs):
    width = small_ref.shape[1]
    (o_wq, o_bq, o_wk, o_wv, o_bv, o_wo, o_bo, o_g1, o_s1, o_up, o_bu, o_dn, o_bd, o_g2, o_s2) = refs[:15]
    taken, given, in_sem, out_sem = refs[15:]
    wide = o_bu.shape[1] // width
    targets = []
    for j in range(wide):
        targets += [o_dn.at[0, pl.ds(j * width + r, PIECE), :] for r in range(0, width, PIECE)]
    for j in range(wide):
        targets += [o_up.at[0, pl.ds(r, PIECE), pl.ds(j * width, width)] for r in range(0, width, PIECE)]
    for ref in (o_wo, o_wq, o_wk, o_wv):
        targets += [ref.at[0, pl.ds(r, PIECE), :] for r in range(0, width, PIECE)]

    def load(i):
        return pltpu.make_async_copy(
            sum_hbm.at[pl.ds(i * PIECE, PIECE)], taken.at[i % DEPTH], in_sem.at[i % DEPTH]
        )

    def store(i):
        return pltpu.make_async_copy(given.at[i % DEPTH], targets[i], out_sem.at[i % DEPTH])

    for i in range(DEPTH):
        load(i).start()
    singles = [o_bq, o_bv, o_bo, o_g1, o_s1, o_bd, o_g2, o_s2]
    for i, ref in enumerate(singles):
        ref[...] = small_ref[pl.ds(i, 1), :]
    for j in range(wide):
        o_bu[:, pl.ds(j * width, width)] = small_ref[pl.ds(len(singles) + j, 1), :]
    for i in range(len(targets)):
        load(i).wait()
        if i >= DEPTH:
            store(i - DEPTH).wait()

        def convert(r, carry):
            rows = pl.ds(pl.multiple_of(r * 64, 64), 64)
            given[i % DEPTH, rows, :] = taken[i % DEPTH, rows, :].astype(jnp.float32)
            return carry

        lax.fori_loop(0, PIECE // 64, convert, 0)
        store(i).start()
        if i + DEPTH < len(targets):
            load(i + DEPTH).start()
    for i in range(len(targets) - DEPTH, len(targets)):
        store(i).wait()


def spread(sums, small, params):
    width = small.shape[1]
    anywhere = pl.BlockSpec(memory_space=pl.ANY)
    local = pl.BlockSpec(memory_space=pltpu.VMEM)
    return pl.pallas_call(
        spread_kernel,
        out_shape=tuple(jax.ShapeDtypeStruct(member.shape, jnp.float32) for member in params),
        in_specs=[anywhere, local],
        out_specs=tuple(anywhere if len(member.shape) == 3 else local for member in params),
        scratch_shapes=[
            pltpu.VMEM((DEPTH, PIECE, width), jnp.bfloat16),
            pltpu.VMEM((DEPTH, PIECE, width), jnp.float32),
            pltpu.SemaphoreType.DMA((DEPTH,)),
            pltpu.SemaphoreType.DMA((DEPTH,)),
        ],
        compiler_params=pltpu.CompilerParams(vmem_limit_bytes=VMEM_LIMIT),
        cost_estimate=pl.CostEstimate(
            flops=12 * width * width, bytes_accessed=80 * width * width, transcendentals=0
        ),
    )(sums, small)


SINGLES = ("bq", "bv", "bo", "g1", "s1", "bd", "g2", "s2")


def product(left, right):
    return lax.dot_general(left, right, (((1,), (0,)), ((), ())), preferred_element_type=jnp.float32)


def product_t(left, right):
    return lax.dot_general(left, right, (((1,), (1,)), ((), ())), preferred_element_type=jnp.float32)


def gelu_pair(z):
    cdf = 0.5 + 0.5 * lax.erf(z * (1.0 / math.sqrt(2.0)))
    bell = jnp.exp(-0.5 * z * z)
    return z * cdf, cdf + z * bell * (1.0 / math.sqrt(2.0 * math.pi))


def normed(values):
    average = jnp.mean(values, axis=-1, keepdims=True)
    centered = values - average
    inverse = lax.rsqrt(jnp.mean(centered * centered, axis=-1, keepdims=True) + EPSILON)
    return centered * inverse, inverse


def normed_back(grad, normal, inverse):
    first_mean = jnp.mean(grad, axis=-1, keepdims=True)
    second_mean = jnp.mean(grad * normal, axis=-1, keepdims=True)
    return inverse * (grad - first_mean - normal * second_mean)


def layer_kernel(
    ids_ref,
    lengths_ref,
    captions_ref,
    regions_ref,
    cotangent_hbm,
    wq_hbm,
    bq_ref,
    wk_hbm,
    wv_hbm,
    bv_ref,
    wo_hbm,
    bo_ref,
    g1_ref,
    s1_ref,
    wu_hbm,
    bu_ref,
    wd_hbm,
    bd_ref,
    g2_ref,
    s2_ref,
    states_hbm,
    grads_hbm,
    a_hbm,
    b_hbm,
    small_ref,
    wqkv,
    wo,
    wu,
    wd,
    wqkv_t,
    wo_t,
    wu_t,
    wd_t,
    table,
    hidden,
    upstream,
    query,
    keys,
    values,
    probs,
    context,
    normal1,
    normal2,
    lowered,
    active,
    slope,
    result,
    staged,
    inverse1,
    inverse2,
    wide1,
    wide2,
    d_context,
    d_scores,
    weight_sem,
    table_send,
    table_recv,
    fwd_send,
    fwd_recv,
    back_send,
    back_recv,
    out_sem,
):
    items, rows, width = hidden.shape
    held = regions_ref.shape[0]
    cap_rows = captions_ref.shape[1]
    wide = wu.shape[1] // width
    pairs = HEADS // 2
    pair_width = width // pairs
    head = width // HEADS
    section = lax.axis_index("section")
    batch = lax.axis_index("batch")
    count = lax.axis_size("batch")
    right = (section, lax.rem(batch + 1, count))
    left = (section, lax.rem(batch + count - 1, count))
    other = (1 - section, batch)

    weight_copies = [
        pltpu.make_async_copy(source.at[0], target, weight_sem.at[n])
        for n, (source, target) in enumerate(
            (
                (wq_hbm, wqkv.at[:, pl.ds(0, width)]),
                (wk_hbm, wqkv.at[:, pl.ds(width, width)]),
                (wv_hbm, wqkv.at[:, pl.ds(2 * width, width)]),
                (wo_hbm, wo),
                (wu_hbm, wu),
                (wd_hbm, wd),
            )
        )
    ]
    for copy in weight_copies:
        copy.start()
    cotangent_copy = pltpu.make_async_copy(cotangent_hbm, upstream, weight_sem.at[6])

    barrier = pltpu.get_barrier_semaphore()
    for peer in (right, left, other):
        pl.semaphore_signal(barrier, inc=1, device_id=peer, device_id_type=MESH)
    pl.semaphore_wait(barrier, 3)

    def table_copy(n, peer):
        return pltpu.make_async_remote_copy(
            src_ref=regions_ref,
            dst_ref=table.at[pl.ds(2 * n * held, held)],
            send_sem=table_send.at[n],
            recv_sem=table_recv.at[n],
            device_id=peer,
            device_id_type=MESH,
        )

    @pl.when(section == 0)
    def _():
        table_copy(0, right).start()
        table_copy(1, left).start()
        table[pl.ds(held, held)] = regions_ref[...]
        table_copy(0, right).wait()
        table_copy(1, left).wait()

    @pl.when(section == 1)
    def _():
        cotangent_copy.start()

    def forward_copy(i):
        return pltpu.make_async_remote_copy(
            src_ref=result.at[i],
            dst_ref=hidden.at[i],
            send_sem=fwd_send.at[i],
            recv_sem=fwd_recv.at[i],
            device_id=other,
            device_id_type=MESH,
        )

    def back_copy(i):
        return pltpu.make_async_remote_copy(
            src_ref=result.at[i],
            dst_ref=upstream.at[i],
            send_sem=back_send.at[i],
            recv_sem=back_recv.at[i],
            device_id=other,
            device_id_type=MESH,
        )

    def save(i, n):
        at = pl.ds(pl.multiple_of(i * rows, rows), rows)
        first = wide * width
        turn = lax.rem(i, 2)
        if n == 0:
            source, target = active.at[turn], a_hbm.at[at, pl.ds(0, first)]
        elif n == 1:
            source, target = lowered.at[turn], a_hbm.at[at, pl.ds(first, width)]
        elif n == 2:
            source, target = context.at[turn], a_hbm.at[at, pl.ds(first + width, width)]
        elif n == 3:
            source, target = hidden.at[i], a_hbm.at[at, pl.ds(first + 2 * width, width)]
        else:
            source, target = result.at[i], states_hbm.at[0, i]
        return pltpu.make_async_copy(source, target, out_sem.at[i, n])

    def staged_save(i):
        at = pl.ds(pl.multiple_of(i * rows, rows), rows)
        return pltpu.make_async_copy(staged.at[lax.rem(i, 2)], b_hbm.at[at], out_sem.at[i, 5])

    def grad_save(i):
        return pltpu.make_async_copy(result.at[i], grads_hbm.at[0, i], out_sem.at[i, 6])

    def vector(ref, j=0):
        return ref[:, j * width : (j + 1) * width].astype(jnp.float32)

    lane = lax.broadcasted_iota(jnp.int32, (rows, pair_width), 1)

    blocks = [slice(r, r + GROUP) for r in range(0, rows, GROUP)]
    spans = [slice(c, min(c + 128, rows)) for c in range(0, rows, 128)]

    def only(block, h):
        return jnp.where((lane // head) == h, block, jnp.zeros_like(block))

    def assemble(i):
        total = count * held
        spot = jnp.minimum(lax.rem(ids_ref[i] - (batch - 1) * held + total, total), 3 * held - 1)
        whole = jnp.concatenate(
            [captions_ref[i].astype(jnp.float32), table[spot].astype(jnp.float32)], axis=0
        )
        hidden[i] = whole.astype(jnp.bfloat16)

    def forward(i):
        @pl.when((i == 0) & (section == 0))
        def _():
            for copy in weight_copies[:3]:
                copy.wait()

        turn = lax.rem(i, 2)
        source = hidden[i]
        mixed = product(source, wqkv[:, :width])
        for at in blocks:
            scaled = (mixed[at] + vector(bq_ref)) * (1.0 / math.sqrt(head))
            query[i, at, :] = scaled.astype(jnp.bfloat16)
        keys[i] = product(source, wqkv[:, width : 2 * width]).astype(jnp.bfloat16)
        mixed = product(source, wqkv[:, 2 * width :])
        for at in blocks:
            values[i, at, :] = (mixed[at] + vector(bv_ref)).astype(jnp.bfloat16)
        position = lax.broadcasted_iota(jnp.int32, (rows, 1), 0)
        live = (position >= cap_rows) | (position < lengths_ref[i])
        key_bias = jnp.where(live, 0.0, -1000000000.0)

        def lanes_of(p):
            return slice(p * pair_width, (p + 1) * pair_width)

        def scored(p):
            k_pair = keys[i, :, lanes_of(p)]
            stacked = jnp.concatenate([only(k_pair, 0), only(k_pair, 1)], axis=0)
            v_turned = values[i, :, lanes_of(p)].astype(jnp.float32).T.astype(jnp.bfloat16)
            return product_t(stacked, query[i, :, lanes_of(p)]), v_turned

        def weighed(p, both):
            for h in range(2):
                for span in spans:
                    scores = both[h * rows : (h + 1) * rows, span] + key_bias
                    expo = jnp.exp(scores - jnp.max(scores, axis=0, keepdims=True))
                    share = pl.reciprocal(jnp.sum(expo, axis=0, keepdims=True))
                    probs[i, 2 * p + h, :, span] = (expo * share).astype(jnp.bfloat16)

        def mixed_values(p, v_turned):
            return [product(v_turned[h * head : (h + 1) * head], probs[i, 2 * p + h]) for h in range(2)]

        def place_context(p, parts):
            context[turn, :, lanes_of(p)] = jnp.concatenate(parts, axis=0).T.astype(jnp.bfloat16)

        ahead = scored(0)
        parts = None
        for p in range(pairs):
            both, v_turned = ahead
            if p + 1 < pairs:
                ahead = scored(p + 1)
            if parts is not None:
                place_context(p - 1, parts)
            weighed(p, both)
            parts = mixed_values(p, v_turned)
        place_context(pairs - 1, parts)

        @pl.when((i == 0) & (section == 0))
        def _():
            for copy in weight_copies[3:]:
                copy.wait()

        attended = product(context[turn], wo[...])
        for at in blocks:
            n1, inv1 = normed(hidden[i, at, :].astype(jnp.float32) + attended[at] + vector(bo_ref))
            normal1[i, at, :] = n1.astype(jnp.bfloat16)
            inverse1[i, at, :] = inv1
            first = n1 * vector(g1_ref) + vector(s1_ref)
            lowered[turn, at, :] = first.astype(jnp.bfloat16)
            wide1[at, :] = first + vector(bd_ref)
        low = lowered[turn]
        tile = 2 * width // 3
        tiles = wide * width // tile

        def raised(n):
            return product(low, wu[:, n * tile : (n + 1) * tile])

        z_next = raised(0)
        half = tiles // 2
        for n in range(tiles):
            lanes = slice(n * tile, (n + 1) * tile)
            z_tile = z_next
            if n + 1 < tiles:
                z_next = raised(n + 1)
            if n == half:
                wide1[...] += product(active[turn, :, : half * tile], wd[: half * tile, :])
            for at in blocks:
                gelu, slant = gelu_pair(z_tile[at] + bu_ref[:, lanes].astype(jnp.float32))
                active[turn, at, lanes] = gelu.astype(jnp.bfloat16)
                slope[i, at, lanes] = slant.astype(jnp.bfloat16)
        lowest = product(active[turn, :, half * tile :], wd[half * tile :, :])
        for at in blocks:
            n2, inv2 = normed(wide1[at, :] + lowest[at])
            normal2[i, at, :] = n2.astype(jnp.bfloat16)
            inverse2[i, at, :] = inv2
            result[i, at, :] = (n2 * vector(g2_ref) + vector(s2_ref)).astype(jnp.bfloat16)

    def folded(value):
        return value[: GROUP // 2] + value[GROUP // 2 :]

    def keep_small(row, value):
        small_ref[row : row + 1, :] += jnp.sum(value, axis=0, keepdims=True)

    def single(name, value):
        keep_small(SINGLES.index(name), value)

    def backward(i):
        slot = lax.rem(i, 2)
        base = (2 + wide) * width

        def stage(at, column, value):
            staged[slot, at, column * width : (column + 1) * width] = value

        def norm_step(at, gradient, normal, inverse, gain, sums):
            n = normal[i, at, :].astype(jnp.float32)
            d_res = normed_back(gradient * vector(gain), n, inverse[i, at, :])
            d_low = d_res.astype(jnp.bfloat16)
            terms = [folded(gradient * n), folded(gradient), folded(d_low.astype(jnp.float32))]
            return d_res, d_low, terms if sums is None else [a + b for a, b in zip(sums, terms)]

        sums = None
        for at in blocks:
            gradient = upstream[i, at, :].astype(jnp.float32)
            d_res, d_low, sums = norm_step(at, gradient, normal2, inverse2, g2_ref, sums)
            wide1[at, :] = d_res
            stage(at, 0, d_low)
        for name, value in zip(("g2", "s2", "bd"), sums):
            single(name, value)
        d_out = staged[slot, :, :width]
        for j in range(wide):
            lanes = slice(j * width, (j + 1) * width)
            d_active = product(d_out, wd_t[:, lanes])
            total = None
            for at in blocks:
                d_inner = (d_active[at] * slope[i, at, lanes].astype(jnp.float32)).astype(jnp.bfloat16)
                stage(at, 1 + j, d_inner)
                term = folded(d_inner.astype(jnp.float32))
                total = term if total is None else total + term
            keep_small(len(SINGLES) + j, total)
        d_deep = product(staged[slot, :, width : (1 + wide) * width], wu_t[...])
        sums = None
        for at in blocks:
            d_res, d_low, sums = norm_step(at, wide1[at, :] + d_deep[at], normal1, inverse1, g1_ref, sums)
            wide2[at, :] = d_res
            stage(at, 1 + wide, d_low)
        for name, value in zip(("g1", "s1", "bo"), sums):
            single(name, value)
        d_att = staged[slot, :, (1 + wide) * width : (2 + wide) * width]
        d_context[...] = product(d_att, wo_t[...]).astype(jnp.bfloat16)

        def lanes_of(p):
            return slice(p * pair_width, (p + 1) * pair_width)

        def place_grad(n, p, block):
            at = base + n * width + p * pair_width
            staged[slot, :, at : at + pair_width] = block.astype(jnp.bfloat16)

        def opened(p):
            v_pair = values[i, :, lanes_of(p)]
            c_pair = d_context[:, lanes_of(p)]
            stacked = jnp.concatenate([only(v_pair, 0), only(v_pair, 1)], axis=0)
            k_turned = keys[i, :, lanes_of(p)].astype(jnp.float32).T.astype(jnp.bfloat16)
            d_value = product(probs[i, 2 * p], only(c_pair, 0))
            d_value += product(probs[i, 2 * p + 1], only(c_pair, 1))
            return product_t(stacked, c_pair), k_turned, d_value

        def score_grads(p, both):
            for h in range(2):
                for span in spans:
                    prob = probs[i, 2 * p + h, :, span].astype(jnp.float32)
                    d_prob = both[h * rows : (h + 1) * rows, span]
                    drift = jnp.sum(d_prob * prob, axis=0, keepdims=True)
                    d_scores[p % 2, h, :, span] = (prob * (d_prob - drift)).astype(jnp.bfloat16)
            return [d_scores[p % 2, h] for h in range(2)]

        def closed(p, found, k_turned):
            q_pair = query[i, :, lanes_of(p)]
            d_key = product(found[0], only(q_pair, 0)) + product(found[1], only(q_pair, 1))
            return d_key, [product(k_turned[h * head : (h + 1) * head], found[h]) for h in range(2)]

        def place_grads(p, d_value, d_key, parts):
            place_grad(0, p, jnp.concatenate(parts, axis=0).T * (1.0 / math.sqrt(head)))
            place_grad(1, p, d_key)
            place_grad(2, p, d_value)

        ahead = opened(0)
        waiting = None
        for p in range(pairs):
            both, k_turned, d_value = ahead
            if p + 1 < pairs:
                ahead = opened(p + 1)
            if waiting is not None:
                place_grads(*waiting)
            found = score_grads(p, both)
            d_key, parts = closed(p, found, k_turned)
            waiting = (p, d_value, d_key, parts)
        place_grads(*waiting)
        d_source = product(staged[slot, :, base : base + 3 * width], wqkv_t[...])
        sums = None
        for at in blocks:
            result[i, at, :] = (wide2[at, :] + d_source[at]).astype(jnp.bfloat16)
            terms = [
                folded(staged[slot, at, base : base + width].astype(jnp.float32)),
                folded(staged[slot, at, base + 2 * width : base + 3 * width].astype(jnp.float32)),
            ]
            sums = terms if sums is None else [a + b for a, b in zip(sums, terms)]
        single("bq", sums[0])
        single("bv", sums[1])

    small_ref[...] = jnp.zeros_like(small_ref)
    side = 256
    unit = lax.broadcasted_iota(jnp.int32, (side, side), 0) == lax.broadcasted_iota(jnp.int32, (side, side), 1)
    unit = jnp.where(unit, 1.0, 0.0).astype(jnp.bfloat16)

    def turn_weights():
        for natural, turned in ((wqkv, wqkv_t), (wo, wo_t), (wu, wu_t), (wd, wd_t)):
            for block in range(0, natural.shape[0], width):

                def one(n, carry):
                    at = pl.ds(pl.multiple_of(n * side, side), side)
                    tall = product_t(unit, natural[block : block + width, at])
                    turned[at, block : block + width] = tall.astype(jnp.bfloat16)
                    return carry

                lax.fori_loop(0, natural.shape[1] // side, one, 0)

    @pl.when(section == 1)
    def _():
        for copy in weight_copies:
            copy.wait()
        turn_weights()

    def forward_step(i, carry):
        @pl.when(section == 0)
        def _():
            assemble(i)

        @pl.when(section == 1)
        def _():
            forward_copy(i).wait_recv()

        @pl.when(i >= 2)
        def _():
            for n in range(3):
                save(i - 2, n).wait()

        forward(i)

        @pl.when(section == 0)
        def _():
            forward_copy(i).start()

        for n in range(5):
            save(i, n).start()
        return carry

    lax.fori_loop(0, items, forward_step, 0)

    @pl.when(section == 0)
    def _():
        turn_weights()

    @pl.when(section == 1)
    def _():
        cotangent_copy.wait()

    def backward_step(i, carry):
        @pl.when(section == 0)
        def _():
            back_copy(i).wait_recv()

        @pl.when(i >= 2)
        def _():
            staged_save(i - 2).wait()

        save(i, 4).wait()

        @pl.when(section == 0)
        def _():
            forward_copy(i).wait_send()

        backward(i)

        @pl.when(section == 1)
        def _():
            back_copy(i).start()

        staged_save(i).start()
        grad_save(i).start()
        return carry

    lax.fori_loop(0, items, backward_step, 0)

    def finish(i, carry):
        save(i, 3).wait()
        grad_save(i).wait()

        @pl.when(i >= items - 2)
        def _():
            staged_save(i).wait()
            for n in range(3):
                save(i, n).wait()

        @pl.when(section == 1)
        def _():
            back_copy(i).wait_send()

        return carry

    lax.fori_loop(0, items, finish, 0)


def layered(image_ids, caption_lengths, captions, regions, cotangent, stacked):
    items, cap_rows, width = captions.shape
    held, region_rows, _ = regions.shape
    rows = cap_rows + region_rows
    inner = stacked[9].shape[2]
    low = jnp.bfloat16
    wide = inner // width

    def cells(*shape):
        return pltpu.VMEM(shape, low)

    anywhere = pl.BlockSpec(memory_space=pl.ANY)
    local = pl.BlockSpec(memory_space=pltpu.VMEM)
    scalars = pl.BlockSpec(memory_space=pltpu.SMEM)
    return pl.pallas_call(
        layer_kernel,
        out_shape=(
            jax.ShapeDtypeStruct((1, items, rows, width), low),
            jax.ShapeDtypeStruct((1, items, rows, width), low),
            jax.ShapeDtypeStruct((items * rows, (3 + wide) * width), low),
            jax.ShapeDtypeStruct((items * rows, (5 + wide) * width), low),
            jax.ShapeDtypeStruct((GROUP, width), jnp.float32),
        ),
        in_specs=[scalars, scalars, local, local, anywhere]
        + [anywhere if len(member.shape) == 3 else local for member in stacked],
        out_specs=(anywhere, anywhere, anywhere, anywhere, local),
        scratch_shapes=[
            cells(width, 3 * width),
            cells(width, width),
            cells(width, inner),
            cells(inner, width),
            cells(3 * width, width),
            cells(width, width),
            cells(inner, width),
            cells(width, inner),
            cells(3 * held, region_rows, width),
            cells(items, rows, width),
            cells(items, rows, width),
            cells(items, rows, width),
            cells(items, rows, width),
            cells(items, rows, width),
            cells(items, HEADS, rows, rows),
            cells(2, rows, width),
            cells(items, rows, width),
            cells(items, rows, width),
            cells(2, rows, width),
            cells(2, rows, inner),
            cells(items, rows, inner),
            cells(items, rows, width),
            cells(2, rows, (5 + wide) * width),
            pltpu.VMEM((items, rows, 1), jnp.float32),
            pltpu.VMEM((items, rows, 1), jnp.float32),
            pltpu.VMEM((rows, width), jnp.float32),
            pltpu.VMEM((rows, width), jnp.float32),
            cells(rows, width),
            cells(2, 2, rows, rows),
            pltpu.SemaphoreType.DMA((7,)),
            pltpu.SemaphoreType.DMA((2,)),
            pltpu.SemaphoreType.DMA((2,)),
            pltpu.SemaphoreType.DMA((items,)),
            pltpu.SemaphoreType.DMA((items,)),
            pltpu.SemaphoreType.DMA((items,)),
            pltpu.SemaphoreType.DMA((items,)),
            pltpu.SemaphoreType.DMA((items, 7)),
        ],
        compiler_params=pltpu.CompilerParams(
            collective_id=0, has_side_effects=True, vmem_limit_bytes=VMEM_LIMIT
        ),
        cost_estimate=pl.CostEstimate(
            flops=4 * items * rows * (4 + 2 * wide) * width * width,
            bytes_accessed=60_000_000,
            transcendentals=0,
        ),
    )(image_ids, caption_lengths, captions, regions, cotangent, *stacked)


def body(
    captions,
    regions,
    image_ids,
    caption_lengths,
    cotangent,
    query_weight,
    query_bias,
    key_weight,
    value_weight,
    value_bias,
    out_weight,
    out_bias,
    norm1_gain,
    norm1_bias,
    up_weight,
    up_bias,
    down_weight,
    down_bias,
    norm2_gain,
    norm2_bias,
):
    stacked = (
        query_weight,
        query_bias,
        key_weight,
        value_weight,
        value_bias,
        out_weight,
        out_bias,
        norm1_gain,
        norm1_bias,
        up_weight,
        up_bias,
        down_weight,
        down_bias,
        norm2_gain,
        norm2_bias,
    )
    width = captions.shape[2]
    states, input_grads, a_side, b_side, small = layered(
        image_ids, caption_lengths, captions, regions, cotangent, stacked
    )
    sums, small_sums = reduced(a_side, b_side, small, lax.axis_size("batch"))
    grads = spread(sums.reshape(-1, width), small_sums, stacked)
    return (states, input_grads) + tuple(grads)


def solution(mesh):
    placed = (
        P("batch", None, None),
        P("batch", None, None),
        P("batch"),
        P("batch"),
        P("batch", None, None),
        P("section", None, None),
        P("section", None),
        P("section", None, None),
        P("section", None, None),
        P("section", None),
        P("section", None, None),
        P("section", None),
        P("section", None),
        P("section", None),
        P("section", None, None),
        P("section", None),
        P("section", None, None),
        P("section", None),
        P("section", None),
        P("section", None),
    )
    return jax.shard_map(
        body,
        mesh=mesh,
        in_specs=placed,
        out_specs=(
            P("section", "batch", None, None),
            P("section", "batch", None, None),
            P("section", None, None),
            P("section", None),
            P("section", None, None),
            P("section", None, None),
            P("section", None),
            P("section", None, None),
            P("section", None),
            P("section", None),
            P("section", None),
            P("section", None, None),
            P("section", None),
            P("section", None, None),
            P("section", None),
            P("section", None),
            P("section", None),
        ),
        check_vma=False,
    )
```

```python
import functools
import math

import jax
import jax.numpy as jnp
from jax import lax
from jax.experimental import pallas as pl
from jax.experimental.pallas import tpu as pltpu
from jax.sharding import PartitionSpec as P

HEADS = 12
EPSILON = 1e-12
MESH = pl.DeviceIdType.MESH
VMEM_LIMIT = 62 * 1024 * 1024
GROUP = 16
CHUNK_GROUPS = 16
SLOTS = 15
SLOT_GROUPS = 24
LAG = 2
CYCLE = 5
LINE = 4
SPLIT_BITS = 4


def reduce_kernel(
    bits,
    chunks,
    a_hbm,
    b_hbm,
    small_ref,
    out_hbm,
    small_out,
    a_ref,
    b_ref,
    acc,
    whole,
    recv,
    small_acc,
    small_recv,
    load_sem,
    send_sem,
    recv_sem,
    save_sem,
    small_send_sem,
    small_recv_sem,
):
    width = acc.shape[2]
    extra = bits - SPLIT_BITS
    first_gather = SPLIT_BITS + 1 + extra
    stages = 2 * (SPLIT_BITS + 1) + extra + 1
    me = lax.axis_index("batch")
    section = lax.axis_index("section")
    core, side, place = me % 2, (me // 2) % 2, (me // 4) % LINE
    blocks_a = a_hbm.shape[1] // width
    blocks_b = b_hbm.shape[1] // width
    per_block = width // (CHUNK_GROUPS * GROUP)

    def load(source, target, block, base):
        lanes = pl.ds(block * width, width)
        return pltpu.make_async_copy(source.at[:, lanes], target.at[:, lanes], load_sem.at[base + block])

    def load_a(block):
        return load(a_hbm, a_ref, block, 0)

    def load_b(block):
        return load(b_hbm, b_ref, block, blocks_a)

    wide = blocks_a - 3
    first_use = {0: [(load_a, 0), (load_b, 0)]}
    for j in range(1, wide):
        first_use[j] = [(load_a, j)]
    first_use[wide] = [(load_a, wide), (load_b, 1)]
    for j in range(1, wide):
        first_use[wide + j] = [(load_b, 1 + j)]
    first_use[2 * wide] = [(load_a, wide + 1), (load_b, wide + 1)]
    first_use[2 * wide + 1] = [(load_a, wide + 2), (load_b, wide + 2)]
    first_use[2 * wide + 2] = [(load_b, wide + 3)]
    first_use[2 * wide + 3] = [(load_b, wide + 4)]
    for j in range(2 * wide + 4):
        for kind, block in first_use[j]:
            kind(block).start()

    def bit_mate(k):
        bit = (me // 2**k) % 2
        return (section, me + 2**k * (1 - 2 * bit))

    core_mate, side_mate = bit_mate(0), bit_mate(1)
    mates = ((section, me - LINE), (section, me + LINE))
    ring = [(section, me + LINE * ((place + d) % LINE - place)) for d in (LINE - 1, 1)]

    barrier = pltpu.get_barrier_semaphore()
    for peer in [core_mate, side_mate] + ring + [bit_mate(k) for k in range(2, bits)]:
        pl.semaphore_signal(barrier, inc=1, device_id=peer, device_id_type=MESH)
    pl.semaphore_wait(barrier, bits + 2)

    def low_core(c):
        return c * CHUNK_GROUPS + core * 8

    def low_side(c):
        return low_core(c) + side * 4

    def block_start(c, kind, b):
        return low_side(c) + b if kind == 0 else low_core(c) + 2 * b

    def final(c, kind):
        return low_side(c) + place if kind == 0 else low_core(c) + 2 * place + side

    def remote(c, source, start, size, target, spot, index, peer):
        return pltpu.make_async_remote_copy(
            src_ref=source.at[pl.ds(start, size)],
            dst_ref=target.at[lax.rem(c, SLOTS), pl.ds(spot, size)] if target is recv else target.at[pl.ds(start, size)],
            send_sem=send_sem.at[lax.rem(c, SLOTS), index],
            recv_sem=recv_sem.at[lax.rem(c, SLOTS), index],
            device_id=peer,
            device_id_type=MESH,
        )

    def core_copy(c):
        return remote(c, acc, c * CHUNK_GROUPS + (1 - core) * 8, 8, recv, 0, 0, core_mate)

    def side_copy(c, kind):
        if kind == 0:
            return remote(c, acc, low_core(c) + (1 - side) * 4, 4, recv, 8, 1, side_mate)
        return remote(c, acc, low_core(c) + 2 * place + (1 - side), 1, recv, 8, 1, side_mate)

    def line_copy(c, kind, r, d):
        size = 1 + kind
        b = jnp.minimum(3 - r + place, 3) if d == 1 else jnp.maximum(r - 3 + place, 0)
        spot = 12 + 2 * (2 * r + d)
        return remote(c, acc, block_start(c, kind, b), size, recv, spot, 2 + 2 * r + d, mates[d])

    def spread_copy(c, kind, r, d):
        size = 1 + kind
        b = jnp.maximum(place - r, 0) if d == 1 else jnp.minimum(place + r, 3)
        return remote(c, whole, block_start(c, kind, b), size, whole, 0, 8 + 2 * r + d, mates[d])

    def side_back_copy(c, kind):
        if kind == 0:
            return remote(c, whole, low_side(c), 4, whole, 0, 14, side_mate)
        return remote(c, whole, final(c, kind), 1, whole, 0, 14, side_mate)

    def core_back_copy(c):
        return remote(c, whole, low_core(c), 8, whole, 0, 15, core_mate)

    def extra_copy(c, kind, e):
        return remote(c, acc, final(c, kind), 1, recv, 24 + e, 16 + e, bit_mate(SPLIT_BITS + e))

    def save_copy(c):
        at = pl.ds(c * CHUNK_GROUPS, CHUNK_GROUPS)
        return pltpu.make_async_copy(whole.at[at], out_hbm.at[at], save_sem.at[lax.rem(c, SLOTS)])

    def add_groups(start, count, c, spot):
        slot = lax.rem(c, SLOTS)
        for g in range(count):
            total = acc[start + g].astype(jnp.float32) + recv[slot, spot + g].astype(jnp.float32)
            acc[start + g] = total.astype(jnp.bfloat16)

    def name_of(kind, s):
        if s == 0:
            return ("core",)
        if s == stages - 1:
            return ("save",)
        if s == stages - 2:
            return ("core_back",)
        if s < SPLIT_BITS + 1:
            order = [("side",), ("line", 0), ("line", 1), ("line", 2)]
            order = order if kind == 0 else order[1:] + order[:1]
            return order[s - 1]
        if s < first_gather:
            return ("extra", s - SPLIT_BITS - 1)
        order = [("spread", 0), ("spread", 1), ("spread", 2), ("side_back",)]
        order = order if kind == 0 else order[3:] + order[:3]
        return order[s - first_gather]

    def start_stage(c, kind, s):
        name = name_of(kind, s)
        if s == first_gather:
            whole[final(c, kind)] = acc[final(c, kind)]
        if name[0] == "core":
            core_copy(c).start()
        elif name[0] == "side":
            side_copy(c, kind).start()
        elif name[0] == "line":
            r = name[1]
            pl.when(place <= r)(lambda: line_copy(c, kind, r, 1).start())
            pl.when(place >= 3 - r)(lambda: line_copy(c, kind, r, 0).start())
        elif name[0] == "extra":
            extra_copy(c, kind, name[1]).start()
        elif name[0] == "spread":
            r = name[1]
            pl.when((place >= r) & (place <= 2))(lambda: spread_copy(c, kind, r, 1).start())
            pl.when((place >= 1) & (place <= 3 - r))(lambda: spread_copy(c, kind, r, 0).start())
        elif name[0] == "side_back":
            side_back_copy(c, kind).start()
        elif name[0] == "core_back":
            core_back_copy(c).start()
        else:
            save_copy(c).start()

    def finish_stage(c, kind, s):
        name = name_of(kind, s)
        if name[0] == "core":
            core_copy(c).wait()
            add_groups(low_core(c), 8, c, 0)
        elif name[0] == "side":
            side_copy(c, kind).wait()
            if kind == 0:
                add_groups(low_side(c), 4, c, 8)
            else:
                add_groups(final(c, kind), 1, c, 8)
        elif name[0] == "line":
            r = name[1]

            @pl.when(place <= r)
            def _():
                line_copy(c, kind, r, 1).wait_send()

            @pl.when(place >= 3 - r)
            def _():
                line_copy(c, kind, r, 0).wait_send()

            @pl.when((place >= 1) & (place <= r + 1))
            def _():
                line_copy(c, kind, r, 1).wait_recv()
                add_groups(block_start(c, kind, 2 - r + place), 1 + kind, c, 12 + 2 * (2 * r + 1))

            @pl.when((place <= 2) & (place >= 2 - r))
            def _():
                line_copy(c, kind, r, 0).wait_recv()
                add_groups(block_start(c, kind, r - 2 + place), 1 + kind, c, 12 + 2 * (2 * r))

        elif name[0] == "extra":
            extra_copy(c, kind, name[1]).wait()
            add_groups(final(c, kind), 1, c, 24 + name[1])
        elif name[0] == "spread":
            r = name[1]
            pl.when((place >= r) & (place <= 2))(lambda: spread_copy(c, kind, r, 1).wait_send())
            pl.when((place >= 1) & (place <= 3 - r))(lambda: spread_copy(c, kind, r, 0).wait_send())
            pl.when(place >= r + 1)(lambda: spread_copy(c, kind, r, 1).wait_recv())
            pl.when(place <= 2 - r)(lambda: spread_copy(c, kind, r, 0).wait_recv())
        elif name[0] == "side_back":
            side_back_copy(c, kind).wait()
        elif name[0] == "core_back":
            core_back_copy(c).wait()
        else:
            save_copy(c).wait()

    def small_copy(k):
        return pltpu.make_async_remote_copy(
            src_ref=small_acc.at[k],
            dst_ref=small_recv.at[k],
            send_sem=small_send_sem.at[k],
            recv_sem=small_recv_sem.at[k],
            device_id=bit_mate(k),
            device_id_type=MESH,
        )

    small_acc[0] = small_ref[...]

    def step(t, phase):
        for s in range(stages, 0, -1):
            c = t - LAG * s
            kind = (phase - LAG * s) % CYCLE % 2

            @pl.when((c >= 0) & (c < chunks))
            def _():
                finish_stage(c, kind, s - 1)
                if s < stages:
                    start_stage(c, kind, s)

        for j in range(2 * wide + 4):

            @pl.when(t == per_block * j)
            def _():
                for kind, block in first_use[j]:
                    kind(block).wait()

        @pl.when(t < chunks)
        def _():
            block, part = t // per_block, t % per_block
            a_col = jnp.minimum(block, wide) + jnp.minimum(block // (2 * wide), 1) + jnp.minimum(block // (2 * wide + 1), 1)
            b_col = jnp.maximum(block - wide + 1, 0)
            lines = CHUNK_GROUPS * GROUP
            left = a_ref[:, pl.ds(pl.multiple_of(a_col * width + part * lines, lines), lines)]
            right = b_ref[:, pl.ds(pl.multiple_of(b_col * width, width), width)]
            grad = lax.dot_general(left, right, (((0,), (0,)), ((), ())), preferred_element_type=jnp.float32)
            acc[pl.ds(t * CHUNK_GROUPS, CHUNK_GROUPS)] = grad.astype(jnp.bfloat16).reshape(
                CHUNK_GROUPS, GROUP, width
            )
            core_copy(t).start()

        for k in range(bits + 1):

            @pl.when(t == LAG * k)
            def _():
                if k > 0:
                    small_copy(k - 1).wait()
                    small_acc[k] = small_acc[k - 1] + small_recv[k - 1]
                if k < bits:
                    small_copy(k).start()

    def cycle(n, carry):
        for phase in range(CYCLE):
            step(n * CYCLE + phase, phase)
        return carry

    lax.fori_loop(0, pl.cdiv(chunks + LAG * stages, CYCLE), cycle, 0)
    small_out[...] = small_acc[bits]


def reduced(a_side, b_side, small, count):
    rows = a_side.shape[0]
    width = small.shape[1]
    bits = count.bit_length() - 1
    extra = bits - SPLIT_BITS
    blocks = 2 * (a_side.shape[1] // width - 3) + 4
    chunks = blocks * width // (CHUNK_GROUPS * GROUP)
    groups = chunks * CHUNK_GROUPS
    loads = (a_side.shape[1] + b_side.shape[1]) // width
    return pl.pallas_call(
        functools.partial(reduce_kernel, bits, chunks),
        out_shape=(
            jax.ShapeDtypeStruct((groups, GROUP, width), jnp.bfloat16),
            jax.ShapeDtypeStruct(small.shape, jnp.float32),
        ),
        in_specs=[
            pl.BlockSpec(memory_space=pl.ANY),
            pl.BlockSpec(memory_space=pl.ANY),
            pl.BlockSpec(memory_space=pltpu.VMEM),
        ],
        out_specs=(pl.BlockSpec(memory_space=pl.ANY), pl.BlockSpec(memory_space=pltpu.VMEM)),
        scratch_shapes=[
            pltpu.VMEM(a_side.shape, jnp.bfloat16),
            pltpu.VMEM(b_side.shape, jnp.bfloat16),
            pltpu.VMEM((groups, GROUP, width), jnp.bfloat16),
            pltpu.VMEM((groups, GROUP, width), jnp.bfloat16),
            pltpu.VMEM((SLOTS, SLOT_GROUPS + extra, GROUP, width), jnp.bfloat16),
            pltpu.VMEM((bits + 1,) + small.shape, jnp.float32),
            pltpu.VMEM((bits,) + small.shape, jnp.float32),
            pltpu.SemaphoreType.DMA((loads,)),
            pltpu.SemaphoreType.DMA((SLOTS, 16 + extra)),
            pltpu.SemaphoreType.DMA((SLOTS, 16 + extra)),
            pltpu.SemaphoreType.DMA((SLOTS,)),
            pltpu.SemaphoreType.DMA((bits,)),
            pltpu.SemaphoreType.DMA((bits,)),
        ],
        compiler_params=pltpu.CompilerParams(
            collective_id=1, has_side_effects=True, vmem_limit_bytes=VMEM_LIMIT
        ),
        cost_estimate=pl.CostEstimate(
            flops=2 * rows * blocks * width * width, bytes_accessed=80_000_000, transcendentals=0
        ),
    )(a_side, b_side, small)


PIECE = 384
DEPTH = 4


def spread_kernel(sum_hbm, small_ref, *refs):
    width = small_ref.shape[1]
    (o_wq, o_bq, o_wk, o_wv, o_bv, o_wo, o_bo, o_g1, o_s1, o_up, o_bu, o_dn, o_bd, o_g2, o_s2) = refs[:15]
    taken, given, in_sem, out_sem = refs[15:]
    wide = o_bu.shape[1] // width
    targets = []
    for j in range(wide):
        targets += [o_dn.at[0, pl.ds(j * width + r, PIECE), :] for r in range(0, width, PIECE)]
    for j in range(wide):
        targets += [o_up.at[0, pl.ds(r, PIECE), pl.ds(j * width, width)] for r in range(0, width, PIECE)]
    for ref in (o_wo, o_wq, o_wk, o_wv):
        targets += [ref.at[0, pl.ds(r, PIECE), :] for r in range(0, width, PIECE)]

    def load(i):
        return pltpu.make_async_copy(
            sum_hbm.at[pl.ds(i * PIECE, PIECE)], taken.at[i % DEPTH], in_sem.at[i % DEPTH]
        )

    def store(i):
        return pltpu.make_async_copy(given.at[i % DEPTH], targets[i], out_sem.at[i % DEPTH])

    for i in range(DEPTH):
        load(i).start()
    singles = [o_bq, o_bv, o_bo, o_g1, o_s1, o_bd, o_g2, o_s2]
    for i, ref in enumerate(singles):
        ref[...] = small_ref[pl.ds(i, 1), :]
    for j in range(wide):
        o_bu[:, pl.ds(j * width, width)] = small_ref[pl.ds(len(singles) + j, 1), :]
    for i in range(len(targets)):
        load(i).wait()
        if i >= DEPTH:
            store(i - DEPTH).wait()

        def convert(r, carry):
            rows = pl.ds(pl.multiple_of(r * 64, 64), 64)
            given[i % DEPTH, rows, :] = taken[i % DEPTH, rows, :].astype(jnp.float32)
            return carry

        lax.fori_loop(0, PIECE // 64, convert, 0)
        store(i).start()
        if i + DEPTH < len(targets):
            load(i + DEPTH).start()
    for i in range(len(targets) - DEPTH, len(targets)):
        store(i).wait()


def spread(sums, small, params):
    width = small.shape[1]
    anywhere = pl.BlockSpec(memory_space=pl.ANY)
    local = pl.BlockSpec(memory_space=pltpu.VMEM)
    return pl.pallas_call(
        spread_kernel,
        out_shape=tuple(jax.ShapeDtypeStruct(member.shape, jnp.float32) for member in params),
        in_specs=[anywhere, local],
        out_specs=tuple(anywhere if len(member.shape) == 3 else local for member in params),
        scratch_shapes=[
            pltpu.VMEM((DEPTH, PIECE, width), jnp.bfloat16),
            pltpu.VMEM((DEPTH, PIECE, width), jnp.float32),
            pltpu.SemaphoreType.DMA((DEPTH,)),
            pltpu.SemaphoreType.DMA((DEPTH,)),
        ],
        compiler_params=pltpu.CompilerParams(vmem_limit_bytes=VMEM_LIMIT),
        cost_estimate=pl.CostEstimate(
            flops=12 * width * width, bytes_accessed=80 * width * width, transcendentals=0
        ),
    )(sums, small)


ERF_P = 0.3275911 / math.sqrt(2.0)
ERF_HALVES = tuple(0.5 * a for a in (0.254829592, -0.284496736, 1.421413741, -1.453152027, 1.061405429))
HALF_LOG = -0.5 / math.log(2.0)
BELL_SCALE = 1.0 / math.sqrt(2.0 * math.pi)
SINGLES = ("bq", "bv", "bo", "g1", "s1", "bd", "g2", "s2")


def product(left, right):
    return lax.dot_general(left, right, (((1,), (0,)), ((), ())), preferred_element_type=jnp.float32)


def product_t(left, right):
    return lax.dot_general(left, right, (((1,), (1,)), ((), ())), preferred_element_type=jnp.float32)


def gelu_pair(z):
    bell = jnp.exp2(z * z * HALF_LOG)
    t = pltpu.reciprocal(ERF_P * jnp.abs(z) + 1.0, approx=True)
    poly = ERF_HALVES[4]
    for a in ERF_HALVES[3::-1]:
        poly = poly * t + a
    tail = poly * t * bell
    cdf = jnp.where(z >= 0.0, 1.0 - tail, tail)
    return z * cdf, z * BELL_SCALE * bell + cdf


def normed(values):
    average = jnp.mean(values, axis=-1, keepdims=True)
    centered = values - average
    inverse = lax.rsqrt(jnp.mean(centered * centered, axis=-1, keepdims=True) + EPSILON)
    return centered * inverse, inverse


def normed_back(grad, normal, inverse):
    first_mean = jnp.mean(grad, axis=-1, keepdims=True)
    second_mean = jnp.mean(grad * normal, axis=-1, keepdims=True)
    return inverse * (grad - first_mean - normal * second_mean)


def layer_kernel(
    ids_ref,
    lengths_ref,
    captions_ref,
    regions_ref,
    cotangent_hbm,
    wq_hbm,
    bq_ref,
    wk_hbm,
    wv_hbm,
    bv_ref,
    wo_hbm,
    bo_ref,
    g1_ref,
    s1_ref,
    wu_hbm,
    bu_ref,
    wd_hbm,
    bd_ref,
    g2_ref,
    s2_ref,
    states_hbm,
    grads_hbm,
    a_hbm,
    b_hbm,
    small_ref,
    wqkv,
    wo,
    wu,
    wd,
    wqkv_t,
    wo_t,
    wu_t,
    wd_t,
    table,
    hidden,
    upstream,
    query,
    keys,
    values,
    probs,
    context,
    normal1,
    normal2,
    lowered,
    active,
    slope,
    result,
    staged,
    inverse1,
    inverse2,
    wide1,
    wide2,
    d_context,
    d_scores,
    weight_sem,
    table_send,
    table_recv,
    fwd_send,
    fwd_recv,
    back_send,
    back_recv,
    out_sem,
):
    items, rows, width = hidden.shape
    held = regions_ref.shape[0]
    cap_rows = captions_ref.shape[1]
    wide = wu.shape[1] // width
    pairs = HEADS // 2
    pair_width = width // pairs
    head = width // HEADS
    section = lax.axis_index("section")
    batch = lax.axis_index("batch")
    count = lax.axis_size("batch")
    right = (section, lax.rem(batch + 1, count))
    left = (section, lax.rem(batch + count - 1, count))
    other = (1 - section, batch)

    weight_copies = [
        pltpu.make_async_copy(source.at[0], target, weight_sem.at[n])
        for n, (source, target) in enumerate(
            (
                (wq_hbm, wqkv.at[:, pl.ds(0, width)]),
                (wk_hbm, wqkv.at[:, pl.ds(width, width)]),
                (wv_hbm, wqkv.at[:, pl.ds(2 * width, width)]),
                (wo_hbm, wo),
                (wu_hbm, wu),
                (wd_hbm, wd),
            )
        )
    ]
    for copy in weight_copies[:3]:
        copy.start()
    cotangent_copy = pltpu.make_async_copy(cotangent_hbm, upstream, weight_sem.at[6])

    barrier = pltpu.get_barrier_semaphore()
    for peer in (right, left, other):
        pl.semaphore_signal(barrier, inc=1, device_id=peer, device_id_type=MESH)
    pl.semaphore_wait(barrier, 3)

    def table_copy(n, peer):
        return pltpu.make_async_remote_copy(
            src_ref=regions_ref,
            dst_ref=table.at[pl.ds(2 * n * held, held)],
            send_sem=table_send.at[n],
            recv_sem=table_recv.at[n],
            device_id=peer,
            device_id_type=MESH,
        )

    @pl.when(section == 0)
    def _():
        table_copy(0, right).start()
        table_copy(1, left).start()
        table[pl.ds(held, held)] = regions_ref[...]
        table_copy(0, right).wait()
        table_copy(1, left).wait()

    for copy in weight_copies[3:]:
        copy.start()

    @pl.when(section == 1)
    def _():
        cotangent_copy.start()

    def forward_copy(i):
        return pltpu.make_async_remote_copy(
            src_ref=result.at[i],
            dst_ref=hidden.at[i],
            send_sem=fwd_send.at[i],
            recv_sem=fwd_recv.at[i],
            device_id=other,
            device_id_type=MESH,
        )

    def back_copy(i):
        return pltpu.make_async_remote_copy(
            src_ref=result.at[i],
            dst_ref=upstream.at[i],
            send_sem=back_send.at[i],
            recv_sem=back_recv.at[i],
            device_id=other,
            device_id_type=MESH,
        )

    def save(i, n):
        at = pl.ds(pl.multiple_of(i * rows, rows), rows)
        first = wide * width
        turn = lax.rem(i, 2)
        if n == 0:
            source, target = active.at[turn], a_hbm.at[at, pl.ds(0, first)]
        elif n == 1:
            source, target = lowered.at[turn], a_hbm.at[at, pl.ds(first, width)]
        elif n == 2:
            source, target = context.at[turn], a_hbm.at[at, pl.ds(first + width, width)]
        elif n == 3:
            source, target = hidden.at[i], a_hbm.at[at, pl.ds(first + 2 * width, width)]
        else:
            source, target = result.at[i], states_hbm.at[0, i]
        return pltpu.make_async_copy(source, target, out_sem.at[i, n])

    def staged_save(i):
        at = pl.ds(pl.multiple_of(i * rows, rows), rows)
        return pltpu.make_async_copy(staged.at[lax.rem(i, 2)], b_hbm.at[at], out_sem.at[i, 5])

    def grad_save(i):
        return pltpu.make_async_copy(result.at[i], grads_hbm.at[0, i], out_sem.at[i, 6])

    def vector(ref, j=0):
        return ref[:, j * width : (j + 1) * width].astype(jnp.float32)

    lane = lax.broadcasted_iota(jnp.int32, (rows, pair_width), 1)

    blocks = [slice(r, r + GROUP) for r in range(0, rows, GROUP)]
    spans = [slice(c, min(c + 128, rows)) for c in range(0, rows, 128)]

    def only(block, h):
        return jnp.where((lane // head) == h, block, jnp.zeros_like(block))

    def assemble(i):
        total = count * held
        spot = jnp.minimum(lax.rem(ids_ref[i] - (batch - 1) * held + total, total), 3 * held - 1)
        whole = jnp.concatenate(
            [captions_ref[i].astype(jnp.float32), table[spot].astype(jnp.float32)], axis=0
        )
        hidden[i] = whole.astype(jnp.bfloat16)

    def forward(i):
        @pl.when((i == 0) & (section == 0))
        def _():
            for copy in weight_copies[:3]:
                copy.wait()

        turn = lax.rem(i, 2)
        source = hidden[i]
        mixed = product(source, wqkv[:, :width])
        for at in blocks:
            scaled = (mixed[at] + vector(bq_ref)) * (1.0 / math.sqrt(head))
            query[i, at, :] = scaled.astype(jnp.bfloat16)
        keys[i] = product(source, wqkv[:, width : 2 * width]).astype(jnp.bfloat16)
        mixed = product(source, wqkv[:, 2 * width :])
        for at in blocks:
            values[i, at, :] = (mixed[at] + vector(bv_ref)).astype(jnp.bfloat16)
        position = lax.broadcasted_iota(jnp.int32, (rows, 1), 0)
        live = (position >= cap_rows) | (position < lengths_ref[i])
        key_bias = jnp.where(live, 0.0, -1000000000.0)

        def lanes_of(p):
            return slice(p * pair_width, (p + 1) * pair_width)

        def scored(p):
            k_pair = keys[i, :, lanes_of(p)]
            stacked = jnp.concatenate([only(k_pair, 0), only(k_pair, 1)], axis=0)
            v_turned = values[i, :, lanes_of(p)].astype(jnp.float32).T.astype(jnp.bfloat16)
            return product_t(stacked, query[i, :, lanes_of(p)]), v_turned

        def weighed(p, both):
            for h in range(2):
                for span in spans:
                    scores = both[h * rows : (h + 1) * rows, span] + key_bias
                    expo = jnp.exp(scores - jnp.max(scores, axis=0, keepdims=True))
                    share = pltpu.reciprocal(jnp.sum(expo, axis=0, keepdims=True), approx=True)
                    probs[i, 2 * p + h, :, span] = (expo * share).astype(jnp.bfloat16)

        def mixed_values(p, v_turned):
            return [product(v_turned[h * head : (h + 1) * head], probs[i, 2 * p + h]) for h in range(2)]

        def place_context(p, parts):
            context[turn, :, lanes_of(p)] = jnp.concatenate(parts, axis=0).T.astype(jnp.bfloat16)

        ahead = scored(0)
        parts = None
        for p in range(pairs):
            both, v_turned = ahead
            if p + 1 < pairs:
                ahead = scored(p + 1)
            if parts is not None:
                place_context(p - 1, parts)
            weighed(p, both)
            parts = mixed_values(p, v_turned)
        place_context(pairs - 1, parts)

        @pl.when((i == 0) & (section == 0))
        def _():
            for copy in weight_copies[3:]:
                copy.wait()

        attended = product(context[turn], wo[...])
        for at in blocks:
            n1, inv1 = normed(hidden[i, at, :].astype(jnp.float32) + attended[at] + vector(bo_ref))
            normal1[i, at, :] = n1.astype(jnp.bfloat16)
            inverse1[i, at, :] = inv1
            first = n1 * vector(g1_ref) + vector(s1_ref)
            lowered[turn, at, :] = first.astype(jnp.bfloat16)
            wide1[at, :] = first + vector(bd_ref)
        low = lowered[turn]
        tile = 2 * width // 3
        tiles = wide * width // tile

        def raised(n):
            return product(low, wu[:, n * tile : (n + 1) * tile])

        z_next = raised(0)
        half = tiles // 2
        for n in range(tiles):
            lanes = slice(n * tile, (n + 1) * tile)
            z_tile = z_next
            if n + 1 < tiles:
                z_next = raised(n + 1)
            if n == half:
                wide1[...] += product(active[turn, :, : half * tile], wd[: half * tile, :])
            for at in blocks:
                gelu, slant = gelu_pair(z_tile[at] + bu_ref[:, lanes].astype(jnp.float32))
                active[turn, at, lanes] = gelu.astype(jnp.bfloat16)
                slope[i, at, lanes] = slant.astype(jnp.bfloat16)
        lowest = product(active[turn, :, half * tile :], wd[half * tile :, :])
        for at in blocks:
            n2, inv2 = normed(wide1[at, :] + lowest[at])
            normal2[i, at, :] = n2.astype(jnp.bfloat16)
            inverse2[i, at, :] = inv2
            result[i, at, :] = (n2 * vector(g2_ref) + vector(s2_ref)).astype(jnp.bfloat16)

    def folded(value):
        return value[: GROUP // 2] + value[GROUP // 2 :]

    def keep_small(row, value):
        small_ref[row : row + 1, :] += jnp.sum(value, axis=0, keepdims=True)

    def single(name, value):
        keep_small(SINGLES.index(name), value)

    def backward(i):
        slot = lax.rem(i, 2)
        base = (2 + wide) * width

        def stage(at, column, value):
            staged[slot, at, column * width : (column + 1) * width] = value

        def norm_step(at, gradient, normal, inverse, gain, sums):
            n = normal[i, at, :].astype(jnp.float32)
            d_res = normed_back(gradient * vector(gain), n, inverse[i, at, :])
            d_low = d_res.astype(jnp.bfloat16)
            terms = [folded(gradient * n), folded(gradient), folded(d_low.astype(jnp.float32))]
            return d_res, d_low, terms if sums is None else [a + b for a, b in zip(sums, terms)]

        sums = None
        for at in blocks:
            gradient = upstream[i, at, :].astype(jnp.float32)
            d_res, d_low, sums = norm_step(at, gradient, normal2, inverse2, g2_ref, sums)
            wide1[at, :] = d_res
            stage(at, 0, d_low)
        for name, value in zip(("g2", "s2", "bd"), sums):
            single(name, value)
        d_out = staged[slot, :, :width]
        for j in range(wide):
            lanes = slice(j * width, (j + 1) * width)
            d_active = product(d_out, wd_t[:, lanes])
            total = None
            for at in blocks:
                d_inner = (d_active[at] * slope[i, at, lanes].astype(jnp.float32)).astype(jnp.bfloat16)
                stage(at, 1 + j, d_inner)
                term = folded(d_inner.astype(jnp.float32))
                total = term if total is None else total + term
            keep_small(len(SINGLES) + j, total)
        d_deep = product(staged[slot, :, width : (1 + wide) * width], wu_t[...])
        sums = None
        for at in blocks:
            d_res, d_low, sums = norm_step(at, wide1[at, :] + d_deep[at], normal1, inverse1, g1_ref, sums)
            wide2[at, :] = d_res
            stage(at, 1 + wide, d_low)
        for name, value in zip(("g1", "s1", "bo"), sums):
            single(name, value)
        d_att = staged[slot, :, (1 + wide) * width : (2 + wide) * width]
        d_context[...] = product(d_att, wo_t[...]).astype(jnp.bfloat16)

        def lanes_of(p):
            return slice(p * pair_width, (p + 1) * pair_width)

        def place_grad(n, p, block):
            at = base + n * width + p * pair_width
            staged[slot, :, at : at + pair_width] = block.astype(jnp.bfloat16)

        def opened(p):
            v_pair = values[i, :, lanes_of(p)]
            c_pair = d_context[:, lanes_of(p)]
            stacked = jnp.concatenate([only(v_pair, 0), only(v_pair, 1)], axis=0)
            k_turned = keys[i, :, lanes_of(p)].astype(jnp.float32).T.astype(jnp.bfloat16)
            d_value = product(probs[i, 2 * p], only(c_pair, 0))
            d_value += product(probs[i, 2 * p + 1], only(c_pair, 1))
            return product_t(stacked, c_pair), k_turned, d_value

        def score_grads(p, both):
            for h in range(2):
                for span in spans:
                    prob = probs[i, 2 * p + h, :, span].astype(jnp.float32)
                    d_prob = both[h * rows : (h + 1) * rows, span]
                    drift = jnp.sum(d_prob * prob, axis=0, keepdims=True)
                    d_scores[p % 2, h, :, span] = (prob * (d_prob - drift)).astype(jnp.bfloat16)
            return [d_scores[p % 2, h] for h in range(2)]

        def closed(p, found, k_turned):
            q_pair = query[i, :, lanes_of(p)]
            d_key = product(found[0], only(q_pair, 0)) + product(found[1], only(q_pair, 1))
            return d_key, [product(k_turned[h * head : (h + 1) * head], found[h]) for h in range(2)]

        def place_grads(p, d_value, d_key, parts):
            place_grad(0, p, jnp.concatenate(parts, axis=0).T * (1.0 / math.sqrt(head)))
            place_grad(1, p, d_key)
            place_grad(2, p, d_value)

        ahead = opened(0)
        waiting = None
        for p in range(pairs):
            both, k_turned, d_value = ahead
            if p + 1 < pairs:
                ahead = opened(p + 1)
            if waiting is not None:
                place_grads(*waiting)
            found = score_grads(p, both)
            d_key, parts = closed(p, found, k_turned)
            waiting = (p, d_value, d_key, parts)
        place_grads(*waiting)
        d_source = product(staged[slot, :, base : base + 3 * width], wqkv_t[...])
        sums = None
        for at in blocks:
            result[i, at, :] = (wide2[at, :] + d_source[at]).astype(jnp.bfloat16)
            terms = [
                folded(staged[slot, at, base : base + width].astype(jnp.float32)),
                folded(staged[slot, at, base + 2 * width : base + 3 * width].astype(jnp.float32)),
            ]
            sums = terms if sums is None else [a + b for a, b in zip(sums, terms)]
        single("bq", sums[0])
        single("bv", sums[1])

    small_ref[...] = jnp.zeros_like(small_ref)
    side = 256
    unit = lax.broadcasted_iota(jnp.int32, (side, side), 0) == lax.broadcasted_iota(jnp.int32, (side, side), 1)
    unit = jnp.where(unit, 1.0, 0.0).astype(jnp.bfloat16)

    def turn_weights():
        for natural, turned in ((wqkv, wqkv_t), (wo, wo_t), (wu, wu_t), (wd, wd_t)):
            for block in range(0, natural.shape[0], width):

                def one(n, carry):
                    at = pl.ds(pl.multiple_of(n * side, side), side)
                    tall = product_t(unit, natural[block : block + width, at])
                    turned[at, block : block + width] = tall.astype(jnp.bfloat16)
                    return carry

                lax.fori_loop(0, natural.shape[1] // side, one, 0)

    @pl.when(section == 1)
    def _():
        for copy in weight_copies:
            copy.wait()
        turn_weights()

    def forward_step(i, carry):
        @pl.when(section == 0)
        def _():
            assemble(i)

        @pl.when(section == 1)
        def _():
            forward_copy(i).wait_recv()

        @pl.when(i >= 2)
        def _():
            for n in range(3):
                save(i - 2, n).wait()

        forward(i)

        @pl.when(section == 0)
        def _():
            forward_copy(i).start()

        for n in range(5):
            save(i, n).start()
        return carry

    lax.fori_loop(0, items, forward_step, 0)

    @pl.when(section == 0)
    def _():
        turn_weights()

    @pl.when(section == 1)
    def _():
        cotangent_copy.wait()

    def backward_step(i, carry):
        @pl.when(section == 0)
        def _():
            back_copy(i).wait_recv()

        @pl.when(i >= 2)
        def _():
            staged_save(i - 2).wait()

        save(i, 4).wait()

        @pl.when(section == 0)
        def _():
            forward_copy(i).wait_send()

        backward(i)

        @pl.when(section == 1)
        def _():
            back_copy(i).start()

        staged_save(i).start()
        grad_save(i).start()
        return carry

    lax.fori_loop(0, items, backward_step, 0)

    def finish(i, carry):
        save(i, 3).wait()
        grad_save(i).wait()

        @pl.when(i >= items - 2)
        def _():
            staged_save(i).wait()
            for n in range(3):
                save(i, n).wait()

        @pl.when(section == 1)
        def _():
            back_copy(i).wait_send()

        return carry

    lax.fori_loop(0, items, finish, 0)


def layered(image_ids, caption_lengths, captions, regions, cotangent, stacked):
    items, cap_rows, width = captions.shape
    held, region_rows, _ = regions.shape
    rows = cap_rows + region_rows
    inner = stacked[9].shape[2]
    low = jnp.bfloat16
    wide = inner // width

    def cells(*shape):
        return pltpu.VMEM(shape, low)

    anywhere = pl.BlockSpec(memory_space=pl.ANY)
    local = pl.BlockSpec(memory_space=pltpu.VMEM)
    scalars = pl.BlockSpec(memory_space=pltpu.SMEM)
    return pl.pallas_call(
        layer_kernel,
        out_shape=(
            jax.ShapeDtypeStruct((1, items, rows, width), low),
            jax.ShapeDtypeStruct((1, items, rows, width), low),
            jax.ShapeDtypeStruct((items * rows, (3 + wide) * width), low),
            jax.ShapeDtypeStruct((items * rows, (5 + wide) * width), low),
            jax.ShapeDtypeStruct((GROUP, width), jnp.float32),
        ),
        in_specs=[scalars, scalars, local, local, anywhere]
        + [anywhere if len(member.shape) == 3 else local for member in stacked],
        out_specs=(anywhere, anywhere, anywhere, anywhere, local),
        scratch_shapes=[
            cells(width, 3 * width),
            cells(width, width),
            cells(width, inner),
            cells(inner, width),
            cells(3 * width, width),
            cells(width, width),
            cells(inner, width),
            cells(width, inner),
            cells(3 * held, region_rows, width),
            cells(items, rows, width),
            cells(items, rows, width),
            cells(items, rows, width),
            cells(items, rows, width),
            cells(items, rows, width),
            cells(items, HEADS, rows, rows),
            cells(2, rows, width),
            cells(items, rows, width),
            cells(items, rows, width),
            cells(2, rows, width),
            cells(2, rows, inner),
            cells(items, rows, inner),
            cells(items, rows, width),
            cells(2, rows, (5 + wide) * width),
            pltpu.VMEM((items, rows, 1), jnp.float32),
            pltpu.VMEM((items, rows, 1), jnp.float32),
            pltpu.VMEM((rows, width), jnp.float32),
            pltpu.VMEM((rows, width), jnp.float32),
            cells(rows, width),
            cells(2, 2, rows, rows),
            pltpu.SemaphoreType.DMA((7,)),
            pltpu.SemaphoreType.DMA((2,)),
            pltpu.SemaphoreType.DMA((2,)),
            pltpu.SemaphoreType.DMA((items,)),
            pltpu.SemaphoreType.DMA((items,)),
            pltpu.SemaphoreType.DMA((items,)),
            pltpu.SemaphoreType.DMA((items,)),
            pltpu.SemaphoreType.DMA((items, 7)),
        ],
        compiler_params=pltpu.CompilerParams(
            collective_id=0, has_side_effects=True, vmem_limit_bytes=VMEM_LIMIT
        ),
        cost_estimate=pl.CostEstimate(
            flops=4 * items * rows * (4 + 2 * wide) * width * width,
            bytes_accessed=60_000_000,
            transcendentals=0,
        ),
    )(image_ids, caption_lengths, captions, regions, cotangent, *stacked)


def body(
    captions,
    regions,
    image_ids,
    caption_lengths,
    cotangent,
    query_weight,
    query_bias,
    key_weight,
    value_weight,
    value_bias,
    out_weight,
    out_bias,
    norm1_gain,
    norm1_bias,
    up_weight,
    up_bias,
    down_weight,
    down_bias,
    norm2_gain,
    norm2_bias,
):
    stacked = (
        query_weight,
        query_bias,
        key_weight,
        value_weight,
        value_bias,
        out_weight,
        out_bias,
        norm1_gain,
        norm1_bias,
        up_weight,
        up_bias,
        down_weight,
        down_bias,
        norm2_gain,
        norm2_bias,
    )
    width = captions.shape[2]
    states, input_grads, a_side, b_side, small = layered(
        image_ids, caption_lengths, captions, regions, cotangent, stacked
    )
    sums, small_sums = reduced(a_side, b_side, small, lax.axis_size("batch"))
    grads = spread(sums.reshape(-1, width), small_sums, stacked)
    return (states, input_grads) + tuple(grads)


def solution(mesh):
    placed = (
        P("batch", None, None),
        P("batch", None, None),
        P("batch"),
        P("batch"),
        P("batch", None, None),
        P("section", None, None),
        P("section", None),
        P("section", None, None),
        P("section", None, None),
        P("section", None),
        P("section", None, None),
        P("section", None),
        P("section", None),
        P("section", None),
        P("section", None, None),
        P("section", None),
        P("section", None, None),
        P("section", None),
        P("section", None),
        P("section", None),
    )
    return jax.shard_map(
        body,
        mesh=mesh,
        in_specs=placed,
        out_specs=(
            P("section", "batch", None, None),
            P("section", "batch", None, None),
            P("section", None, None),
            P("section", None),
            P("section", None, None),
            P("section", None, None),
            P("section", None),
            P("section", None, None),
            P("section", None),
            P("section", None),
            P("section", None),
            P("section", None, None),
            P("section", None),
            P("section", None, None),
            P("section", None),
            P("section", None),
            P("section", None),
        ),
        check_vma=False,
    )
```

```python
import functools
import math

import jax
import jax.numpy as jnp
from jax import lax
from jax.experimental import pallas as pl
from jax.experimental.pallas import tpu as pltpu
from jax.sharding import PartitionSpec as P

HEADS = 12
EPSILON = 1e-12
MESH = pl.DeviceIdType.MESH
VMEM_LIMIT = 63 * 1024 * 1024
GROUP = 16
CHUNK_GROUPS = 16
SLOTS = 15
SLOT_GROUPS = 24
LAG = 2
CYCLE = 5
HALVES = 2
LINE = 4
SPLIT_BITS = 4


def reduce_kernel(
    bits,
    chunks,
    a_hbm,
    b_hbm,
    small_ref,
    out_hbm,
    small_out,
    a_ref,
    b_ref,
    acc,
    whole,
    recv,
    small_acc,
    small_recv,
    load_sem,
    send_sem,
    recv_sem,
    save_sem,
    small_send_sem,
    small_recv_sem,
):
    width = acc.shape[2]
    slim = width // HALVES
    extra = bits - SPLIT_BITS
    first_gather = SPLIT_BITS + 1 + extra
    stages = 2 * (SPLIT_BITS + 1) + extra + 1
    me = lax.axis_index("batch")
    section = lax.axis_index("section")
    core, side, place = me % 2, (me // 2) % 2, (me // 4) % LINE
    blocks_a = a_hbm.shape[1] // width
    blocks_b = b_hbm.shape[1] // width
    per_block = width // (CHUNK_GROUPS * GROUP)

    def load(source, target, block, base):
        lanes = pl.ds(block * width, width)
        return pltpu.make_async_copy(source.at[:, lanes], target.at[:, lanes], load_sem.at[base + block])

    def load_a(block):
        return load(a_hbm, a_ref, block, 0)

    def load_b(block):
        return load(b_hbm, b_ref, block, blocks_a)

    wide = blocks_a - 3
    first_use = {0: [(load_a, 0), (load_b, 0)]}
    for j in range(1, wide):
        first_use[j] = [(load_a, j)]
    first_use[wide] = [(load_a, wide), (load_b, 1)]
    for j in range(1, wide):
        first_use[wide + j] = [(load_b, 1 + j)]
    first_use[2 * wide] = [(load_a, wide + 1), (load_b, wide + 1)]
    first_use[2 * wide + 1] = [(load_a, wide + 2), (load_b, wide + 2)]
    first_use[2 * wide + 2] = [(load_b, wide + 3)]
    first_use[2 * wide + 3] = [(load_b, wide + 4)]
    for j in range(2 * wide + 4):
        for kind, block in first_use[j]:
            kind(block).start()

    def bit_mate(k):
        bit = (me // 2**k) % 2
        return (section, me + 2**k * (1 - 2 * bit))

    core_mate, side_mate = bit_mate(0), bit_mate(1)
    mates = ((section, me - LINE), (section, me + LINE))
    ring = [(section, me + LINE * ((place + d) % LINE - place)) for d in (LINE - 1, 1)]

    barrier = pltpu.get_barrier_semaphore()
    for peer in [core_mate, side_mate] + ring + [bit_mate(k) for k in range(2, bits)]:
        pl.semaphore_signal(barrier, inc=1, device_id=peer, device_id_type=MESH)
    pl.semaphore_wait(barrier, bits + 2)

    def top(c):
        return c // HALVES * CHUNK_GROUPS

    def lanes_of(c):
        return pl.ds(pl.multiple_of(lax.rem(c, HALVES) * slim, slim), slim)

    def low_core(c):
        return top(c) + core * 8

    def low_side(c):
        return low_core(c) + side * 4

    def block_start(c, kind, b):
        return low_side(c) + b if kind == 0 else low_core(c) + 2 * b

    def final(c, kind):
        return low_side(c) + place if kind == 0 else low_core(c) + 2 * place + side

    def remote(c, source, start, size, target, spot, index, peer):
        return pltpu.make_async_remote_copy(
            src_ref=source.at[pl.ds(start, size), :, lanes_of(c)],
            dst_ref=recv.at[lax.rem(c, SLOTS), pl.ds(spot, size)]
            if target is recv
            else target.at[pl.ds(start, size), :, lanes_of(c)],
            send_sem=send_sem.at[lax.rem(c, SLOTS), index],
            recv_sem=recv_sem.at[lax.rem(c, SLOTS), index],
            device_id=peer,
            device_id_type=MESH,
        )

    def core_copy(c):
        return remote(c, acc, top(c) + (1 - core) * 8, 8, recv, 0, 0, core_mate)

    def side_copy(c, kind):
        if kind == 0:
            return remote(c, acc, low_core(c) + (1 - side) * 4, 4, recv, 8, 1, side_mate)
        return remote(c, acc, low_core(c) + 2 * place + (1 - side), 1, recv, 8, 1, side_mate)

    def line_copy(c, kind, r, d):
        size = 1 + kind
        b = jnp.minimum(3 - r + place, 3) if d == 1 else jnp.maximum(r - 3 + place, 0)
        spot = 12 + 2 * (2 * r + d)
        return remote(c, acc, block_start(c, kind, b), size, recv, spot, 2 + 2 * r + d, mates[d])

    def spread_copy(c, kind, r, d):
        size = 1 + kind
        b = jnp.maximum(place - r, 0) if d == 1 else jnp.minimum(place + r, 3)
        return remote(c, whole, block_start(c, kind, b), size, whole, 0, 8 + 2 * r + d, mates[d])

    def side_back_copy(c, kind):
        if kind == 0:
            return remote(c, whole, low_side(c), 4, whole, 0, 14, side_mate)
        return remote(c, whole, final(c, kind), 1, whole, 0, 14, side_mate)

    def core_back_copy(c):
        return remote(c, whole, low_core(c), 8, whole, 0, 15, core_mate)

    def extra_copy(c, kind, e):
        return remote(c, acc, final(c, kind), 1, recv, 24 + e, 16 + e, bit_mate(SPLIT_BITS + e))

    def save_copy(c):
        at = pl.ds(top(c), CHUNK_GROUPS)
        lanes = lanes_of(c)
        return pltpu.make_async_copy(
            whole.at[at, :, lanes], out_hbm.at[at, :, lanes], save_sem.at[lax.rem(c, SLOTS)]
        )

    def add_groups(start, count, c, spot):
        slot = lax.rem(c, SLOTS)
        for g in range(count):
            old = acc[start + g, :, lanes_of(c)].astype(jnp.float32)
            total = old + recv[slot, spot + g].astype(jnp.float32)
            acc[start + g, :, lanes_of(c)] = total.astype(jnp.bfloat16)

    def name_of(kind, s):
        if s == 0:
            return ("core",)
        if s == stages - 1:
            return ("save",)
        if s == stages - 2:
            return ("core_back",)
        if s < SPLIT_BITS + 1:
            order = [("side",), ("line", 0), ("line", 1), ("line", 2)]
            order = order if kind == 0 else order[1:] + order[:1]
            return order[s - 1]
        if s < first_gather:
            return ("extra", s - SPLIT_BITS - 1)
        order = [("spread", 0), ("spread", 1), ("spread", 2), ("side_back",)]
        order = order if kind == 0 else order[3:] + order[:3]
        return order[s - first_gather]

    def start_stage(c, kind, s):
        name = name_of(kind, s)
        if s == first_gather:
            whole[final(c, kind), :, lanes_of(c)] = acc[final(c, kind), :, lanes_of(c)]
        if name[0] == "core":
            core_copy(c).start()
        elif name[0] == "side":
            side_copy(c, kind).start()
        elif name[0] == "line":
            r = name[1]
            pl.when(place <= r)(lambda: line_copy(c, kind, r, 1).start())
            pl.when(place >= 3 - r)(lambda: line_copy(c, kind, r, 0).start())
        elif name[0] == "extra":
            extra_copy(c, kind, name[1]).start()
        elif name[0] == "spread":
            r = name[1]
            pl.when((place >= r) & (place <= 2))(lambda: spread_copy(c, kind, r, 1).start())
            pl.when((place >= 1) & (place <= 3 - r))(lambda: spread_copy(c, kind, r, 0).start())
        elif name[0] == "side_back":
            side_back_copy(c, kind).start()
        elif name[0] == "core_back":
            core_back_copy(c).start()
        else:
            save_copy(c).start()

    def finish_stage(c, kind, s):
        name = name_of(kind, s)
        if name[0] == "core":
            core_copy(c).wait()
            add_groups(low_core(c), 8, c, 0)
        elif name[0] == "side":
            side_copy(c, kind).wait()
            if kind == 0:
                add_groups(low_side(c), 4, c, 8)
            else:
                add_groups(final(c, kind), 1, c, 8)
        elif name[0] == "line":
            r = name[1]

            @pl.when(place <= r)
            def _():
                line_copy(c, kind, r, 1).wait_send()

            @pl.when(place >= 3 - r)
            def _():
                line_copy(c, kind, r, 0).wait_send()

            @pl.when((place >= 1) & (place <= r + 1))
            def _():
                line_copy(c, kind, r, 1).wait_recv()
                add_groups(block_start(c, kind, 2 - r + place), 1 + kind, c, 12 + 2 * (2 * r + 1))

            @pl.when((place <= 2) & (place >= 2 - r))
            def _():
                line_copy(c, kind, r, 0).wait_recv()
                add_groups(block_start(c, kind, r - 2 + place), 1 + kind, c, 12 + 2 * (2 * r))

        elif name[0] == "extra":
            extra_copy(c, kind, name[1]).wait()
            add_groups(final(c, kind), 1, c, 24 + name[1])
        elif name[0] == "spread":
            r = name[1]
            pl.when((place >= r) & (place <= 2))(lambda: spread_copy(c, kind, r, 1).wait_send())
            pl.when((place >= 1) & (place <= 3 - r))(lambda: spread_copy(c, kind, r, 0).wait_send())
            pl.when(place >= r + 1)(lambda: spread_copy(c, kind, r, 1).wait_recv())
            pl.when(place <= 2 - r)(lambda: spread_copy(c, kind, r, 0).wait_recv())
        elif name[0] == "side_back":
            side_back_copy(c, kind).wait()
        elif name[0] == "core_back":
            core_back_copy(c).wait()
        else:
            save_copy(c).wait()

    def small_copy(k):
        return pltpu.make_async_remote_copy(
            src_ref=small_acc.at[k],
            dst_ref=small_recv.at[k],
            send_sem=small_send_sem.at[k],
            recv_sem=small_recv_sem.at[k],
            device_id=bit_mate(k),
            device_id_type=MESH,
        )

    small_acc[0] = small_ref[...]

    def step(t, phase):
        for s in range(stages, 0, -1):
            c = t - LAG * s
            kind = (phase - LAG * s) % CYCLE % 2

            @pl.when((c >= 0) & (c < chunks))
            def _():
                finish_stage(c, kind, s - 1)
                if s < stages:
                    start_stage(c, kind, s)

        for j in range(2 * wide + 4):

            @pl.when(t == HALVES * per_block * j)
            def _():
                for kind, block in first_use[j]:
                    kind(block).wait()

        @pl.when((t < chunks) & (lax.rem(t, HALVES) == 0))
        def _():
            part = t // HALVES
            block, part = part // per_block, lax.rem(part, per_block)
            a_col = jnp.minimum(block, wide) + jnp.minimum(block // (2 * wide), 1) + jnp.minimum(block // (2 * wide + 1), 1)
            b_col = jnp.maximum(block - wide + 1, 0)
            lines = CHUNK_GROUPS * GROUP
            left = a_ref[:, pl.ds(pl.multiple_of(a_col * width + part * lines, lines), lines)]
            right = b_ref[:, pl.ds(pl.multiple_of(b_col * width, width), width)]
            grad = lax.dot_general(left, right, (((0,), (0,)), ((), ())), preferred_element_type=jnp.float32)
            acc[pl.ds(top(t), CHUNK_GROUPS)] = grad.astype(jnp.bfloat16).reshape(CHUNK_GROUPS, GROUP, width)

        @pl.when(t < chunks)
        def _():
            core_copy(t).start()

        for k in range(bits + 1):

            @pl.when(t == LAG * k)
            def _():
                if k > 0:
                    small_copy(k - 1).wait()
                    small_acc[k] = small_acc[k - 1] + small_recv[k - 1]
                if k < bits:
                    small_copy(k).start()

    def cycle(n, carry):
        for phase in range(CYCLE):
            step(n * CYCLE + phase, phase)
        return carry

    lax.fori_loop(0, pl.cdiv(chunks + LAG * stages, CYCLE), cycle, 0)
    small_out[...] = small_acc[bits]


def reduced(a_side, b_side, small, count):
    rows = a_side.shape[0]
    width = small.shape[1]
    bits = count.bit_length() - 1
    extra = bits - SPLIT_BITS
    blocks = 2 * (a_side.shape[1] // width - 3) + 4
    groups = blocks * width // GROUP
    chunks = groups // CHUNK_GROUPS * HALVES
    loads = (a_side.shape[1] + b_side.shape[1]) // width
    return pl.pallas_call(
        functools.partial(reduce_kernel, bits, chunks),
        out_shape=(
            jax.ShapeDtypeStruct((groups, GROUP, width), jnp.bfloat16),
            jax.ShapeDtypeStruct(small.shape, jnp.float32),
        ),
        in_specs=[
            pl.BlockSpec(memory_space=pl.ANY),
            pl.BlockSpec(memory_space=pl.ANY),
            pl.BlockSpec(memory_space=pltpu.VMEM),
        ],
        out_specs=(pl.BlockSpec(memory_space=pl.ANY), pl.BlockSpec(memory_space=pltpu.VMEM)),
        scratch_shapes=[
            pltpu.VMEM(a_side.shape, jnp.bfloat16),
            pltpu.VMEM(b_side.shape, jnp.bfloat16),
            pltpu.VMEM((groups, GROUP, width), jnp.bfloat16),
            pltpu.VMEM((groups, GROUP, width), jnp.bfloat16),
            pltpu.VMEM((SLOTS, SLOT_GROUPS + extra, GROUP, width // HALVES), jnp.bfloat16),
            pltpu.VMEM((bits + 1,) + small.shape, jnp.float32),
            pltpu.VMEM((bits,) + small.shape, jnp.float32),
            pltpu.SemaphoreType.DMA((loads,)),
            pltpu.SemaphoreType.DMA((SLOTS, 16 + extra)),
            pltpu.SemaphoreType.DMA((SLOTS, 16 + extra)),
            pltpu.SemaphoreType.DMA((SLOTS,)),
            pltpu.SemaphoreType.DMA((bits,)),
            pltpu.SemaphoreType.DMA((bits,)),
        ],
        compiler_params=pltpu.CompilerParams(
            collective_id=1, has_side_effects=True, vmem_limit_bytes=VMEM_LIMIT
        ),
        cost_estimate=pl.CostEstimate(
            flops=2 * rows * blocks * width * width, bytes_accessed=80_000_000, transcendentals=0
        ),
    )(a_side, b_side, small)


PIECE = 384
DEPTH = 4


def spread_kernel(sum_hbm, small_ref, *refs):
    width = small_ref.shape[1]
    (o_wq, o_bq, o_wk, o_wv, o_bv, o_wo, o_bo, o_g1, o_s1, o_up, o_bu, o_dn, o_bd, o_g2, o_s2) = refs[:15]
    taken, given, in_sem, out_sem = refs[15:]
    wide = o_bu.shape[1] // width
    targets = []
    for j in range(wide):
        targets += [o_dn.at[0, pl.ds(j * width + r, PIECE), :] for r in range(0, width, PIECE)]
    for j in range(wide):
        targets += [o_up.at[0, pl.ds(r, PIECE), pl.ds(j * width, width)] for r in range(0, width, PIECE)]
    for ref in (o_wo, o_wq, o_wk, o_wv):
        targets += [ref.at[0, pl.ds(r, PIECE), :] for r in range(0, width, PIECE)]

    def load(i):
        return pltpu.make_async_copy(
            sum_hbm.at[pl.ds(i * PIECE, PIECE)], taken.at[i % DEPTH], in_sem.at[i % DEPTH]
        )

    def store(i):
        return pltpu.make_async_copy(given.at[i % DEPTH], targets[i], out_sem.at[i % DEPTH])

    for i in range(DEPTH):
        load(i).start()
    singles = [o_bq, o_bv, o_bo, o_g1, o_s1, o_bd, o_g2, o_s2]
    for i, ref in enumerate(singles):
        ref[...] = small_ref[pl.ds(i, 1), :]
    for j in range(wide):
        o_bu[:, pl.ds(j * width, width)] = small_ref[pl.ds(len(singles) + j, 1), :]
    for i in range(len(targets)):
        load(i).wait()
        if i >= DEPTH:
            store(i - DEPTH).wait()

        def convert(r, carry):
            rows = pl.ds(pl.multiple_of(r * 64, 64), 64)
            given[i % DEPTH, rows, :] = taken[i % DEPTH, rows, :].astype(jnp.float32)
            return carry

        lax.fori_loop(0, PIECE // 64, convert, 0)
        store(i).start()
        if i + DEPTH < len(targets):
            load(i + DEPTH).start()
    for i in range(len(targets) - DEPTH, len(targets)):
        store(i).wait()


def spread(sums, small, params):
    width = small.shape[1]
    anywhere = pl.BlockSpec(memory_space=pl.ANY)
    local = pl.BlockSpec(memory_space=pltpu.VMEM)
    return pl.pallas_call(
        spread_kernel,
        out_shape=tuple(jax.ShapeDtypeStruct(member.shape, jnp.float32) for member in params),
        in_specs=[anywhere, local],
        out_specs=tuple(anywhere if len(member.shape) == 3 else local for member in params),
        scratch_shapes=[
            pltpu.VMEM((DEPTH, PIECE, width), jnp.bfloat16),
            pltpu.VMEM((DEPTH, PIECE, width), jnp.float32),
            pltpu.SemaphoreType.DMA((DEPTH,)),
            pltpu.SemaphoreType.DMA((DEPTH,)),
        ],
        compiler_params=pltpu.CompilerParams(vmem_limit_bytes=VMEM_LIMIT),
        cost_estimate=pl.CostEstimate(
            flops=12 * width * width, bytes_accessed=80 * width * width, transcendentals=0
        ),
    )(sums, small)


TILE = 256
HALF_LOG = -0.5 / math.log(2.0)
BELL_SCALE = 1.0 / math.sqrt(2.0 * math.pi)
SINGLES = ("bq", "bv", "bo", "g1", "s1", "bd", "g2", "s2")


def product(left, right):
    return lax.dot_general(left, right, (((1,), (0,)), ((), ())), preferred_element_type=jnp.float32)


def product_t(left, right):
    return lax.dot_general(left, right, (((1,), (1,)), ((), ())), preferred_element_type=jnp.float32)


def gelu_pair(z):
    cdf = 0.5 * lax.erf(z * (1.0 / math.sqrt(2.0))) + 0.5
    bell = jnp.exp2(z * z * HALF_LOG)
    return z * cdf, z * BELL_SCALE * bell + cdf


def normed(values):
    average = jnp.mean(values, axis=-1, keepdims=True)
    centered = values - average
    inverse = lax.rsqrt(jnp.mean(centered * centered, axis=-1, keepdims=True) + EPSILON)
    return centered * inverse, inverse


def normed_back(grad, normal, inverse):
    first_mean = jnp.mean(grad, axis=-1, keepdims=True)
    second_mean = jnp.mean(grad * normal, axis=-1, keepdims=True)
    return inverse * (grad - first_mean - normal * second_mean)


def layer_kernel(
    ids_ref,
    lengths_ref,
    captions_hbm,
    regions_ref,
    cotangent_hbm,
    wq_hbm,
    bq_ref,
    wk_hbm,
    wv_hbm,
    bv_ref,
    wo_hbm,
    bo_ref,
    g1_ref,
    s1_ref,
    wu_hbm,
    bu_ref,
    wd_hbm,
    bd_ref,
    g2_ref,
    s2_ref,
    states_hbm,
    grads_hbm,
    a_hbm,
    b_hbm,
    small_ref,
    wqkv,
    wo,
    wu,
    wd,
    wqkv_t,
    wo_t,
    wu_t,
    wd_t,
    table,
    hidden,
    upstream,
    query,
    keys,
    values,
    probs,
    context,
    normal1,
    normal2,
    lowered,
    active,
    slope,
    result,
    staged,
    inverse1,
    inverse2,
    wide1,
    wide2,
    raised,
    caption_cells,
    weight_sem,
    table_send,
    table_recv,
    fwd_send,
    fwd_recv,
    back_send,
    back_recv,
    out_sem,
):
    items, rows, width = hidden.shape
    held = regions_ref.shape[0]
    cap_rows = captions_hbm.shape[1]
    wide = wu.shape[1] // width
    pairs = HEADS // 2
    pair_width = width // pairs
    head = width // HEADS
    section = lax.axis_index("section")
    batch = lax.axis_index("batch")
    count = lax.axis_size("batch")
    right = (section, lax.rem(batch + 1, count))
    left = (section, lax.rem(batch + count - 1, count))
    other = (1 - section, batch)

    weight_copies = [
        pltpu.make_async_copy(source.at[0], target, weight_sem.at[n])
        for n, (source, target) in enumerate(
            (
                (wq_hbm, wqkv.at[:, pl.ds(0, width)]),
                (wk_hbm, wqkv.at[:, pl.ds(width, width)]),
                (wv_hbm, wqkv.at[:, pl.ds(2 * width, width)]),
                (wo_hbm, wo),
                (wu_hbm, wu),
                (wd_hbm, wd),
            )
        )
    ]
    for copy in weight_copies[:3]:
        copy.start()
    cotangent_copy = pltpu.make_async_copy(cotangent_hbm, upstream, weight_sem.at[6])

    barrier = pltpu.get_barrier_semaphore()
    for peer in (right, left, other):
        pl.semaphore_signal(barrier, inc=1, device_id=peer, device_id_type=MESH)
    pl.semaphore_wait(barrier, 3)

    def table_copy(n, peer):
        return pltpu.make_async_remote_copy(
            src_ref=regions_ref,
            dst_ref=table.at[pl.ds(2 * n * held, held)],
            send_sem=table_send.at[n],
            recv_sem=table_recv.at[n],
            device_id=peer,
            device_id_type=MESH,
        )

    @pl.when(section == 0)
    def _():
        pltpu.make_async_copy(captions_hbm.at[0], caption_cells, weight_sem.at[7]).start()
        table_copy(0, right).start()
        table_copy(1, left).start()
        table[pl.ds(held, held)] = regions_ref[...]
        table_copy(0, right).wait()
        table_copy(1, left).wait()

    for copy in weight_copies[3:]:
        copy.start()

    @pl.when(section == 1)
    def _():
        cotangent_copy.start()

    def forward_copy(i):
        return pltpu.make_async_remote_copy(
            src_ref=result.at[i],
            dst_ref=hidden.at[i],
            send_sem=fwd_send.at[i],
            recv_sem=fwd_recv.at[i],
            device_id=other,
            device_id_type=MESH,
        )

    def back_copy(i):
        return pltpu.make_async_remote_copy(
            src_ref=result.at[i],
            dst_ref=upstream.at[i],
            send_sem=back_send.at[i],
            recv_sem=back_recv.at[i],
            device_id=other,
            device_id_type=MESH,
        )

    def save(i, n):
        at = pl.ds(pl.multiple_of(i * rows, rows), rows)
        first = wide * width
        turn = lax.rem(i, 2)
        if n == 0:
            source, target = active.at[turn], a_hbm.at[at, pl.ds(0, first)]
        elif n == 1:
            source, target = lowered.at[turn], a_hbm.at[at, pl.ds(first, width)]
        elif n == 2:
            source, target = context.at[turn], a_hbm.at[at, pl.ds(first + width, width)]
        elif n == 3:
            source, target = hidden.at[i], a_hbm.at[at, pl.ds(first + 2 * width, width)]
        else:
            source, target = result.at[i], states_hbm.at[0, i]
        return pltpu.make_async_copy(source, target, out_sem.at[i, n])

    def staged_save(i):
        at = pl.ds(pl.multiple_of(i * rows, rows), rows)
        return pltpu.make_async_copy(staged.at[lax.rem(i, 2)], b_hbm.at[at], out_sem.at[i, 5])

    def grad_save(i):
        return pltpu.make_async_copy(result.at[i], grads_hbm.at[0, i], out_sem.at[i, 6])

    def vector(ref, j=0):
        return ref[:, j * width : (j + 1) * width].astype(jnp.float32)

    lane = lax.broadcasted_iota(jnp.int32, (rows, pair_width), 1)

    blocks = [slice(r, r + GROUP) for r in range(0, rows, GROUP)]
    spans = [slice(c, min(c + 128, rows)) for c in range(0, rows, 128)]

    def only(block, h):
        return jnp.where((lane // head) == h, block, jnp.zeros_like(block))

    def caption_copy(i):
        return pltpu.make_async_copy(captions_hbm.at[i], caption_cells, weight_sem.at[7])

    def assemble(i):
        total = count * held
        spot = jnp.minimum(lax.rem(ids_ref[i] - (batch - 1) * held + total, total), 3 * held - 1)
        caption_copy(i).wait()
        whole = jnp.concatenate(
            [caption_cells[...].astype(jnp.float32), table[spot].astype(jnp.float32)], axis=0
        )
        hidden[i] = whole.astype(jnp.bfloat16)

        @pl.when(i + 1 < items)
        def _():
            caption_copy(i + 1).start()

    def forward(i):
        @pl.when((i == 0) & (section == 0))
        def _():
            for copy in weight_copies[:3]:
                copy.wait()

        turn = lax.rem(i, 2)
        source = hidden[i]
        mixed = product(source, wqkv[:, :width])
        for at in blocks:
            scaled = (mixed[at] + vector(bq_ref)) * (1.0 / math.sqrt(head))
            query[i, at, :] = scaled.astype(jnp.bfloat16)
        keys[i] = product(source, wqkv[:, width : 2 * width]).astype(jnp.bfloat16)
        mixed = product(source, wqkv[:, 2 * width :])
        for at in blocks:
            values[i, at, :] = (mixed[at] + vector(bv_ref)).astype(jnp.bfloat16)
        position = lax.broadcasted_iota(jnp.int32, (rows, 1), 0)
        live = (position >= cap_rows) | (position < lengths_ref[i])
        key_bias = jnp.where(live, 0.0, -1000000000.0)

        def lanes_of(p):
            return slice(p * pair_width, (p + 1) * pair_width)

        def scored(p):
            k_pair = keys[i, :, lanes_of(p)]
            stacked = jnp.concatenate([only(k_pair, 0), only(k_pair, 1)], axis=0)
            v_turned = values[i, :, lanes_of(p)].astype(jnp.float32).T.astype(jnp.bfloat16)
            return product_t(stacked, query[i, :, lanes_of(p)]), v_turned

        def weighed(p, both):
            for h in range(2):
                for span in spans:
                    scores = both[h * rows : (h + 1) * rows, span] + key_bias
                    expo = jnp.exp(scores - jnp.max(scores, axis=0, keepdims=True))
                    share = pltpu.reciprocal(jnp.sum(expo, axis=0, keepdims=True), approx=True)
                    probs[i, 2 * p + h, :, span] = (expo * share).astype(jnp.bfloat16)

        def mixed_values(p, v_turned):
            return [product(v_turned[h * head : (h + 1) * head], probs[i, 2 * p + h]) for h in range(2)]

        def place_context(p, parts):
            context[turn, :, lanes_of(p)] = jnp.concatenate(parts, axis=0).T.astype(jnp.bfloat16)

        ahead = scored(0)
        parts = None
        for p in range(pairs):
            both, v_turned = ahead
            if p + 1 < pairs:
                ahead = scored(p + 1)
            if parts is not None:
                place_context(p - 1, parts)
            weighed(p, both)
            parts = mixed_values(p, v_turned)
        place_context(pairs - 1, parts)

        @pl.when((i == 0) & (section == 0))
        def _():
            for copy in weight_copies[3:]:
                copy.wait()

        attended = product(context[turn], wo[...])
        for at in blocks:
            n1, inv1 = normed(hidden[i, at, :].astype(jnp.float32) + attended[at] + vector(bo_ref))
            normal1[i, at, :] = n1.astype(jnp.bfloat16)
            inverse1[i, at, :] = inv1
            first = n1 * vector(g1_ref) + vector(s1_ref)
            lowered[turn, at, :] = first.astype(jnp.bfloat16)
            wide1[at, :] = first + vector(bd_ref)
        tile = TILE
        tiles = wide * width // tile

        def span_of(n):
            return pl.ds(pl.multiple_of(n * tile, tile), tile)

        def raise_tile(n, parity):
            raised[parity] = product(lowered[turn], wu[:, span_of(n)])

        def bend_tile(n, parity):
            lanes = span_of(n)
            bias = bu_ref[:, lanes].astype(jnp.float32)
            for at in blocks:
                gelu, slant = gelu_pair(raised[parity, at, :] + bias)
                active[turn, at, lanes] = gelu.astype(jnp.bfloat16)
                slope[i, at, lanes] = slant.astype(jnp.bfloat16)

        def lower_tile(n):
            return product(active[turn, :, span_of(n)], wd[span_of(n), :])

        def pipe(n, parity):
            raise_tile(n + 1, 1 - parity)
            bend_tile(n, parity)
            wide1[...] += lower_tile(n - 1)

        raise_tile(0, 0)
        raise_tile(1, 1)
        bend_tile(0, 0)

        def two(m, carry):
            pipe(2 * m + 1, 1)
            pipe(2 * m + 2, 0)
            return carry

        lax.fori_loop(0, tiles // 2 - 1, two, 0)
        bend_tile(tiles - 1, 1)
        wide1[...] += lower_tile(tiles - 2)
        lowest = lower_tile(tiles - 1)
        for at in blocks:
            n2, inv2 = normed(wide1[at, :] + lowest[at])
            normal2[i, at, :] = n2.astype(jnp.bfloat16)
            inverse2[i, at, :] = inv2
            result[i, at, :] = (n2 * vector(g2_ref) + vector(s2_ref)).astype(jnp.bfloat16)

    def folded(value):
        return value[: GROUP // 2] + value[GROUP // 2 :]

    def keep_small(row, value):
        small_ref[row : row + 1, :] += jnp.sum(value, axis=0, keepdims=True)

    def single(name, value):
        keep_small(SINGLES.index(name), value)

    def backward(i):
        slot = lax.rem(i, 2)
        base = (2 + wide) * width

        def stage(at, column, value):
            staged[slot, at, column * width : (column + 1) * width] = value

        def norm_step(at, gradient, normal, inverse, gain, sums):
            n = normal[i, at, :].astype(jnp.float32)
            d_res = normed_back(gradient * vector(gain), n, inverse[i, at, :])
            d_low = d_res.astype(jnp.bfloat16)
            terms = [folded(gradient * n), folded(gradient), folded(d_low.astype(jnp.float32))]
            return d_res, d_low, terms if sums is None else [a + b for a, b in zip(sums, terms)]

        sums = None
        for at in blocks:
            gradient = upstream[i, at, :].astype(jnp.float32)
            d_res, d_low, sums = norm_step(at, gradient, normal2, inverse2, g2_ref, sums)
            wide1[at, :] = d_res
            stage(at, 0, d_low)
        for name, value in zip(("g2", "s2", "bd"), sums):
            single(name, value)
        d_out = staged[slot, :, :width]
        for j in range(wide):
            lanes = slice(j * width, (j + 1) * width)
            d_active = product(d_out, wd_t[:, lanes])
            total = None
            for at in blocks:
                d_inner = (d_active[at] * slope[i, at, lanes].astype(jnp.float32)).astype(jnp.bfloat16)
                stage(at, 1 + j, d_inner)
                term = folded(d_inner.astype(jnp.float32))
                total = term if total is None else total + term
            keep_small(len(SINGLES) + j, total)
        d_deep = product(staged[slot, :, width : (1 + wide) * width], wu_t[...])
        sums = None
        for at in blocks:
            d_res, d_low, sums = norm_step(at, wide1[at, :] + d_deep[at], normal1, inverse1, g1_ref, sums)
            wide2[at, :] = d_res
            stage(at, 1 + wide, d_low)
        for name, value in zip(("g1", "s1", "bo"), sums):
            single(name, value)
        d_att = staged[slot, :, (1 + wide) * width : (2 + wide) * width]
        @pl.when(i == 0)
        def _():
            save(items - 2, 0).wait()
            save(items - 1, 0).wait()

        active[0, :, :width] = product(d_att, wo_t[...]).astype(jnp.bfloat16)

        def lanes_of(p):
            return slice(p * pair_width, (p + 1) * pair_width)

        def place_grad(n, p, block):
            at = base + n * width + p * pair_width
            staged[slot, :, at : at + pair_width] = block.astype(jnp.bfloat16)

        def opened(p):
            v_pair = values[i, :, lanes_of(p)]
            c_pair = active[0, :, lanes_of(p)]
            stacked = jnp.concatenate([only(v_pair, 0), only(v_pair, 1)], axis=0)
            k_turned = keys[i, :, lanes_of(p)].astype(jnp.float32).T.astype(jnp.bfloat16)
            d_value = product(probs[i, 2 * p], only(c_pair, 0))
            d_value += product(probs[i, 2 * p + 1], only(c_pair, 1))
            return product_t(stacked, c_pair), k_turned, d_value

        def score_base(p, h):
            return (2 * (p % 2) + h) * 2 * 128

        def score_grads(p, both):
            for h in range(2):
                for span in spans:
                    prob = probs[i, 2 * p + h, :, span].astype(jnp.float32)
                    d_prob = both[h * rows : (h + 1) * rows, span]
                    drift = jnp.sum(d_prob * prob, axis=0, keepdims=True)
                    at = score_base(p, h)
                    active[1, :, at + span.start : at + span.stop] = (prob * (d_prob - drift)).astype(jnp.bfloat16)
            return [active[1, :, score_base(p, h) : score_base(p, h) + rows] for h in range(2)]

        def closed(p, found, k_turned):
            q_pair = query[i, :, lanes_of(p)]
            d_key = product(found[0], only(q_pair, 0)) + product(found[1], only(q_pair, 1))
            return d_key, [product(k_turned[h * head : (h + 1) * head], found[h]) for h in range(2)]

        def place_grads(p, d_value, d_key, parts):
            place_grad(0, p, jnp.concatenate(parts, axis=0).T * (1.0 / math.sqrt(head)))
            place_grad(1, p, d_key)
            place_grad(2, p, d_value)

        ahead = opened(0)
        waiting = None
        for p in range(pairs):
            both, k_turned, d_value = ahead
            if p + 1 < pairs:
                ahead = opened(p + 1)
            if waiting is not None:
                place_grads(*waiting)
            found = score_grads(p, both)
            d_key, parts = closed(p, found, k_turned)
            waiting = (p, d_value, d_key, parts)
        place_grads(*waiting)
        d_source = product(staged[slot, :, base : base + 3 * width], wqkv_t[...])
        sums = None
        for at in blocks:
            result[i, at, :] = (wide2[at, :] + d_source[at]).astype(jnp.bfloat16)
            terms = [
                folded(staged[slot, at, base : base + width].astype(jnp.float32)),
                folded(staged[slot, at, base + 2 * width : base + 3 * width].astype(jnp.float32)),
            ]
            sums = terms if sums is None else [a + b for a, b in zip(sums, terms)]
        single("bq", sums[0])
        single("bv", sums[1])

    small_ref[...] = jnp.zeros_like(small_ref)
    side = 256
    unit = lax.broadcasted_iota(jnp.int32, (side, side), 0) == lax.broadcasted_iota(jnp.int32, (side, side), 1)
    unit = jnp.where(unit, 1.0, 0.0).astype(jnp.bfloat16)

    def turn_weights():
        for natural, turned in ((wqkv, wqkv_t), (wo, wo_t), (wu, wu_t), (wd, wd_t)):
            for block in range(0, natural.shape[0], width):

                def one(n, carry):
                    at = pl.ds(pl.multiple_of(n * side, side), side)
                    tall = product_t(unit, natural[block : block + width, at])
                    turned[at, block : block + width] = tall.astype(jnp.bfloat16)
                    return carry

                lax.fori_loop(0, natural.shape[1] // side, one, 0)

    @pl.when(section == 1)
    def _():
        for copy in weight_copies:
            copy.wait()
        turn_weights()

    def forward_step(i, carry):
        @pl.when(section == 0)
        def _():
            assemble(i)

        @pl.when(section == 1)
        def _():
            forward_copy(i).wait_recv()

        @pl.when(i >= 2)
        def _():
            for n in range(3):
                save(i - 2, n).wait()

        forward(i)

        @pl.when(section == 0)
        def _():
            forward_copy(i).start()

        for n in range(5):
            save(i, n).start()
        return carry

    lax.fori_loop(0, items, forward_step, 0)

    @pl.when(section == 0)
    def _():
        turn_weights()

    @pl.when(section == 1)
    def _():
        cotangent_copy.wait()

    def backward_step(i, carry):
        @pl.when(section == 0)
        def _():
            back_copy(i).wait_recv()

        @pl.when(i >= 2)
        def _():
            staged_save(i - 2).wait()

        save(i, 4).wait()

        @pl.when(section == 0)
        def _():
            forward_copy(i).wait_send()

        backward(i)

        @pl.when(section == 1)
        def _():
            back_copy(i).start()

        staged_save(i).start()
        grad_save(i).start()
        return carry

    lax.fori_loop(0, items, backward_step, 0)

    def finish(i, carry):
        save(i, 3).wait()
        grad_save(i).wait()

        @pl.when(i >= items - 2)
        def _():
            staged_save(i).wait()
            for n in range(1, 3):
                save(i, n).wait()

        @pl.when(section == 1)
        def _():
            back_copy(i).wait_send()

        return carry

    lax.fori_loop(0, items, finish, 0)


def layered(image_ids, caption_lengths, captions, regions, cotangent, stacked):
    items, cap_rows, width = captions.shape
    held, region_rows, _ = regions.shape
    rows = cap_rows + region_rows
    inner = stacked[9].shape[2]
    low = jnp.bfloat16
    wide = inner // width

    def cells(*shape):
        return pltpu.VMEM(shape, low)

    anywhere = pl.BlockSpec(memory_space=pl.ANY)
    local = pl.BlockSpec(memory_space=pltpu.VMEM)
    scalars = pl.BlockSpec(memory_space=pltpu.SMEM)
    return pl.pallas_call(
        layer_kernel,
        out_shape=(
            jax.ShapeDtypeStruct((1, items, rows, width), low),
            jax.ShapeDtypeStruct((1, items, rows, width), low),
            jax.ShapeDtypeStruct((items * rows, (3 + wide) * width), low),
            jax.ShapeDtypeStruct((items * rows, (5 + wide) * width), low),
            jax.ShapeDtypeStruct((GROUP, width), jnp.float32),
        ),
        in_specs=[scalars, scalars, anywhere, local, anywhere]
        + [anywhere if len(member.shape) == 3 else local for member in stacked],
        out_specs=(anywhere, anywhere, anywhere, anywhere, local),
        scratch_shapes=[
            cells(width, 3 * width),
            cells(width, width),
            cells(width, inner),
            cells(inner, width),
            cells(3 * width, width),
            cells(width, width),
            cells(inner, width),
            cells(width, inner),
            cells(3 * held, region_rows, width),
            cells(items, rows, width),
            cells(items, rows, width),
            cells(items, rows, width),
            cells(items, rows, width),
            cells(items, rows, width),
            cells(items, HEADS, rows, rows),
            cells(2, rows, width),
            cells(items, rows, width),
            cells(items, rows, width),
            cells(2, rows, width),
            cells(2, rows, inner),
            cells(items, rows, inner),
            cells(items, rows, width),
            cells(2, rows, (5 + wide) * width),
            pltpu.VMEM((items, rows, 1), jnp.float32),
            pltpu.VMEM((items, rows, 1), jnp.float32),
            pltpu.VMEM((rows, width), jnp.float32),
            pltpu.VMEM((rows, width), jnp.float32),
            pltpu.VMEM((2, rows, TILE), jnp.float32),
            cells(cap_rows, width),
            pltpu.SemaphoreType.DMA((8,)),
            pltpu.SemaphoreType.DMA((2,)),
            pltpu.SemaphoreType.DMA((2,)),
            pltpu.SemaphoreType.DMA((items,)),
            pltpu.SemaphoreType.DMA((items,)),
            pltpu.SemaphoreType.DMA((items,)),
            pltpu.SemaphoreType.DMA((items,)),
            pltpu.SemaphoreType.DMA((items, 7)),
        ],
        compiler_params=pltpu.CompilerParams(
            collective_id=0, has_side_effects=True, vmem_limit_bytes=VMEM_LIMIT
        ),
        cost_estimate=pl.CostEstimate(
            flops=4 * items * rows * (4 + 2 * wide) * width * width,
            bytes_accessed=60_000_000,
            transcendentals=0,
        ),
    )(image_ids, caption_lengths, captions, regions, cotangent, *stacked)


def body(
    captions,
    regions,
    image_ids,
    caption_lengths,
    cotangent,
    query_weight,
    query_bias,
    key_weight,
    value_weight,
    value_bias,
    out_weight,
    out_bias,
    norm1_gain,
    norm1_bias,
    up_weight,
    up_bias,
    down_weight,
    down_bias,
    norm2_gain,
    norm2_bias,
):
    stacked = (
        query_weight,
        query_bias,
        key_weight,
        value_weight,
        value_bias,
        out_weight,
        out_bias,
        norm1_gain,
        norm1_bias,
        up_weight,
        up_bias,
        down_weight,
        down_bias,
        norm2_gain,
        norm2_bias,
    )
    width = captions.shape[2]
    states, input_grads, a_side, b_side, small = layered(
        image_ids, caption_lengths, captions, regions, cotangent, stacked
    )
    sums, small_sums = reduced(a_side, b_side, small, lax.axis_size("batch"))
    grads = spread(sums.reshape(-1, width), small_sums, stacked)
    return (states, input_grads) + tuple(grads)


def solution(mesh):
    placed = (
        P("batch", None, None),
        P("batch", None, None),
        P("batch"),
        P("batch"),
        P("batch", None, None),
        P("section", None, None),
        P("section", None),
        P("section", None, None),
        P("section", None, None),
        P("section", None),
        P("section", None, None),
        P("section", None),
        P("section", None),
        P("section", None),
        P("section", None, None),
        P("section", None),
        P("section", None, None),
        P("section", None),
        P("section", None),
        P("section", None),
    )
    return jax.shard_map(
        body,
        mesh=mesh,
        in_specs=placed,
        out_specs=(
            P("section", "batch", None, None),
            P("section", "batch", None, None),
            P("section", None, None),
            P("section", None),
            P("section", None, None),
            P("section", None, None),
            P("section", None),
            P("section", None, None),
            P("section", None),
            P("section", None),
            P("section", None),
            P("section", None, None),
            P("section", None),
            P("section", None, None),
            P("section", None),
            P("section", None),
            P("section", None),
        ),
        check_vma=False,
    )
```

```python
import functools
import math

import jax
import jax.numpy as jnp
from jax import lax
from jax.experimental import pallas as pl
from jax.experimental.pallas import tpu as pltpu
from jax.sharding import PartitionSpec as P

HEADS = 12
EPSILON = 1e-12
MESH = pl.DeviceIdType.MESH
VMEM_LIMIT = 63 * 1024 * 1024
GROUP = 16
CHUNK_GROUPS = 16
SLOTS = 18
SLOT_GROUPS = 24
LAG = 3
CYCLE = 3
LINE = 4
SPLIT_BITS = 4


def reduce_kernel(
    bits,
    chunks,
    a_hbm,
    b_hbm,
    small_ref,
    out_hbm,
    small_out,
    a_ref,
    b_ref,
    acc,
    whole,
    recv,
    small_acc,
    small_recv,
    load_sem,
    send_sem,
    recv_sem,
    save_sem,
    small_send_sem,
    small_recv_sem,
):
    width = acc.shape[2]
    extra = bits - SPLIT_BITS
    first_gather = SPLIT_BITS + 1 + extra
    stages = 2 * (SPLIT_BITS + 1) + extra + 1
    me = lax.axis_index("batch")
    section = lax.axis_index("section")
    core, side, place = me % 2, (me // 2) % 2, (me // 4) % LINE
    blocks_a = a_hbm.shape[1] // width
    blocks_b = b_hbm.shape[1] // width
    per_block = width // (CHUNK_GROUPS * GROUP)

    def load(source, target, block, base):
        lanes = pl.ds(block * width, width)
        return pltpu.make_async_copy(source.at[:, lanes], target.at[:, lanes], load_sem.at[base + block])

    def load_a(block):
        return load(a_hbm, a_ref, block, 0)

    def load_b(block):
        return load(b_hbm, b_ref, block, blocks_a)

    wide = blocks_a - 3
    first_use = {0: [(load_a, 0), (load_b, 0)]}
    for j in range(1, wide):
        first_use[j] = [(load_a, j)]
    first_use[wide] = [(load_a, wide), (load_b, 1)]
    for j in range(1, wide):
        first_use[wide + j] = [(load_b, 1 + j)]
    first_use[2 * wide] = [(load_a, wide + 1), (load_b, wide + 1)]
    first_use[2 * wide + 1] = [(load_a, wide + 2), (load_b, wide + 2)]
    first_use[2 * wide + 2] = [(load_b, wide + 3)]
    first_use[2 * wide + 3] = [(load_b, wide + 4)]
    for j in range(2 * wide + 4):
        for kind, block in first_use[j]:
            kind(block).start()

    def bit_mate(k):
        bit = (me // 2**k) % 2
        return (section, me + 2**k * (1 - 2 * bit))

    core_mate, side_mate = bit_mate(0), bit_mate(1)
    mates = ((section, me - LINE), (section, me + LINE))
    ring = [(section, me + LINE * ((place + d) % LINE - place)) for d in (LINE - 1, 1)]

    barrier = pltpu.get_barrier_semaphore()
    for peer in [core_mate, side_mate] + ring + [bit_mate(k) for k in range(2, bits)]:
        pl.semaphore_signal(barrier, inc=1, device_id=peer, device_id_type=MESH)
    pl.semaphore_wait(barrier, bits + 2)

    def low_core(c):
        return c * CHUNK_GROUPS + core * 8

    def low_side(c):
        return low_core(c) + side * 4

    def block_start(c, kind, b):
        return low_side(c) + b if kind == 0 else low_core(c) + 2 * b

    def final(c, kind):
        return low_side(c) + place if kind == 0 else low_core(c) + 2 * place + side

    def remote(c, source, start, size, target, spot, index, peer):
        return pltpu.make_async_remote_copy(
            src_ref=source.at[pl.ds(start, size)],
            dst_ref=target.at[lax.rem(c, SLOTS), pl.ds(spot, size)] if target is recv else target.at[pl.ds(start, size)],
            send_sem=send_sem.at[lax.rem(c, SLOTS), index],
            recv_sem=recv_sem.at[lax.rem(c, SLOTS), index],
            device_id=peer,
            device_id_type=MESH,
        )

    def core_copy(c):
        return remote(c, acc, c * CHUNK_GROUPS + (1 - core) * 8, 8, recv, 0, 0, core_mate)

    def side_copy(c, kind):
        if kind == 0:
            return remote(c, acc, low_core(c) + (1 - side) * 4, 4, recv, 8, 1, side_mate)
        return remote(c, acc, low_core(c) + 2 * place + (1 - side), 1, recv, 8, 1, side_mate)

    def line_copy(c, kind, r, d):
        size = 1 + kind
        b = jnp.minimum(3 - r + place, 3) if d == 1 else jnp.maximum(r - 3 + place, 0)
        spot = 12 + 2 * (2 * r + d)
        return remote(c, acc, block_start(c, kind, b), size, recv, spot, 2 + 2 * r + d, mates[d])

    def spread_copy(c, kind, r, d):
        size = 1 + kind
        b = jnp.maximum(place - r, 0) if d == 1 else jnp.minimum(place + r, 3)
        return remote(c, whole, block_start(c, kind, b), size, whole, 0, 8 + 2 * r + d, mates[d])

    def side_back_copy(c, kind):
        if kind == 0:
            return remote(c, whole, low_side(c), 4, whole, 0, 14, side_mate)
        return remote(c, whole, final(c, kind), 1, whole, 0, 14, side_mate)

    def core_back_copy(c):
        return remote(c, whole, low_core(c), 8, whole, 0, 15, core_mate)

    def extra_copy(c, kind, e):
        return remote(c, acc, final(c, kind), 1, recv, 24 + e, 16 + e, bit_mate(SPLIT_BITS + e))

    def save_copy(c):
        at = pl.ds(c * CHUNK_GROUPS, CHUNK_GROUPS)
        return pltpu.make_async_copy(whole.at[at], out_hbm.at[at], save_sem.at[lax.rem(c, SLOTS)])

    def add_groups(start, count, c, spot):
        slot = lax.rem(c, SLOTS)
        for g in range(count):
            total = acc[start + g].astype(jnp.float32) + recv[slot, spot + g].astype(jnp.float32)
            acc[start + g] = total.astype(jnp.bfloat16)

    def name_of(kind, s):
        if s == 0:
            return ("core",)
        if s == stages - 1:
            return ("save",)
        if s == stages - 2:
            return ("core_back",)
        if s < SPLIT_BITS + 1:
            order = [("side",), ("line", 0), ("line", 1), ("line", 2)]
            order = order if kind == 0 else order[1:] + order[:1]
            return order[s - 1]
        if s < first_gather:
            return ("extra", s - SPLIT_BITS - 1)
        order = [("spread", 0), ("spread", 1), ("spread", 2), ("side_back",)]
        order = order if kind == 0 else order[3:] + order[:3]
        return order[s - first_gather]

    def start_stage(c, kind, s):
        name = name_of(kind, s)
        if s == first_gather:
            whole[final(c, kind)] = acc[final(c, kind)]
        if name[0] == "core":
            core_copy(c).start()
        elif name[0] == "side":
            side_copy(c, kind).start()
        elif name[0] == "line":
            r = name[1]
            pl.when(place <= r)(lambda: line_copy(c, kind, r, 1).start())
            pl.when(place >= 3 - r)(lambda: line_copy(c, kind, r, 0).start())
        elif name[0] == "extra":
            extra_copy(c, kind, name[1]).start()
        elif name[0] == "spread":
            r = name[1]
            pl.when((place >= r) & (place <= 2))(lambda: spread_copy(c, kind, r, 1).start())
            pl.when((place >= 1) & (place <= 3 - r))(lambda: spread_copy(c, kind, r, 0).start())
        elif name[0] == "side_back":
            side_back_copy(c, kind).start()
        elif name[0] == "core_back":
            core_back_copy(c).start()
        else:
            save_copy(c).start()

    def finish_stage(c, kind, s):
        name = name_of(kind, s)
        if name[0] == "core":
            core_copy(c).wait()
            add_groups(low_core(c), 8, c, 0)
        elif name[0] == "side":
            side_copy(c, kind).wait()
            if kind == 0:
                add_groups(low_side(c), 4, c, 8)
            else:
                add_groups(final(c, kind), 1, c, 8)
        elif name[0] == "line":
            r = name[1]

            @pl.when(place <= r)
            def _():
                line_copy(c, kind, r, 1).wait_send()

            @pl.when(place >= 3 - r)
            def _():
                line_copy(c, kind, r, 0).wait_send()

            @pl.when((place >= 1) & (place <= r + 1))
            def _():
                line_copy(c, kind, r, 1).wait_recv()
                add_groups(block_start(c, kind, 2 - r + place), 1 + kind, c, 12 + 2 * (2 * r + 1))

            @pl.when((place <= 2) & (place >= 2 - r))
            def _():
                line_copy(c, kind, r, 0).wait_recv()
                add_groups(block_start(c, kind, r - 2 + place), 1 + kind, c, 12 + 2 * (2 * r))

        elif name[0] == "extra":
            extra_copy(c, kind, name[1]).wait()
            add_groups(final(c, kind), 1, c, 24 + name[1])
        elif name[0] == "spread":
            r = name[1]
            pl.when((place >= r) & (place <= 2))(lambda: spread_copy(c, kind, r, 1).wait_send())
            pl.when((place >= 1) & (place <= 3 - r))(lambda: spread_copy(c, kind, r, 0).wait_send())
            pl.when(place >= r + 1)(lambda: spread_copy(c, kind, r, 1).wait_recv())
            pl.when(place <= 2 - r)(lambda: spread_copy(c, kind, r, 0).wait_recv())
        elif name[0] == "side_back":
            side_back_copy(c, kind).wait()
        elif name[0] == "core_back":
            core_back_copy(c).wait()
        else:
            save_copy(c).wait()

    def small_copy(k):
        return pltpu.make_async_remote_copy(
            src_ref=small_acc.at[k],
            dst_ref=small_recv.at[k],
            send_sem=small_send_sem.at[k],
            recv_sem=small_recv_sem.at[k],
            device_id=bit_mate(k),
            device_id_type=MESH,
        )

    small_acc[0] = small_ref[...]

    def step(t, phase):
        for s in range(stages, 0, -1):
            c = t - LAG * s
            kind = (phase - LAG * s) % CYCLE // 2

            @pl.when((c >= 0) & (c < chunks))
            def _():
                finish_stage(c, kind, s - 1)
                if s < stages:
                    start_stage(c, kind, s)

        for j in range(2 * wide + 4):

            @pl.when(t == per_block * j)
            def _():
                for kind, block in first_use[j]:
                    kind(block).wait()

        @pl.when(t < chunks)
        def _():
            block, part = t // per_block, t % per_block
            a_col = jnp.minimum(block, wide) + jnp.minimum(block // (2 * wide), 1) + jnp.minimum(block // (2 * wide + 1), 1)
            b_col = jnp.maximum(block - wide + 1, 0)
            lines = CHUNK_GROUPS * GROUP
            left = a_ref[:, pl.ds(pl.multiple_of(a_col * width + part * lines, lines), lines)]
            right = b_ref[:, pl.ds(pl.multiple_of(b_col * width, width), width)]
            grad = lax.dot_general(left, right, (((0,), (0,)), ((), ())), preferred_element_type=jnp.float32)
            acc[pl.ds(t * CHUNK_GROUPS, CHUNK_GROUPS)] = grad.astype(jnp.bfloat16).reshape(
                CHUNK_GROUPS, GROUP, width
            )
            core_copy(t).start()

        for k in range(bits + 1):

            @pl.when(t == LAG * k)
            def _():
                if k > 0:
                    small_copy(k - 1).wait()
                    small_acc[k] = small_acc[k - 1] + small_recv[k - 1]
                if k < bits:
                    small_copy(k).start()

    def cycle(n, carry):
        for phase in range(CYCLE):
            step(n * CYCLE + phase, phase)
        return carry

    lax.fori_loop(0, pl.cdiv(chunks + LAG * stages, CYCLE), cycle, 0)
    small_out[...] = small_acc[bits]


def reduced(a_side, b_side, small, count):
    rows = a_side.shape[0]
    width = small.shape[1]
    bits = count.bit_length() - 1
    extra = bits - SPLIT_BITS
    blocks = 2 * (a_side.shape[1] // width - 3) + 4
    chunks = blocks * width // (CHUNK_GROUPS * GROUP)
    groups = chunks * CHUNK_GROUPS
    loads = (a_side.shape[1] + b_side.shape[1]) // width
    return pl.pallas_call(
        functools.partial(reduce_kernel, bits, chunks),
        out_shape=(
            jax.ShapeDtypeStruct((groups, GROUP, width), jnp.bfloat16),
            jax.ShapeDtypeStruct(small.shape, jnp.float32),
        ),
        in_specs=[
            pl.BlockSpec(memory_space=pl.ANY),
            pl.BlockSpec(memory_space=pl.ANY),
            pl.BlockSpec(memory_space=pltpu.VMEM),
        ],
        out_specs=(pl.BlockSpec(memory_space=pl.ANY), pl.BlockSpec(memory_space=pltpu.VMEM)),
        scratch_shapes=[
            pltpu.VMEM(a_side.shape, jnp.bfloat16),
            pltpu.VMEM(b_side.shape, jnp.bfloat16),
            pltpu.VMEM((groups, GROUP, width), jnp.bfloat16),
            pltpu.VMEM((groups, GROUP, width), jnp.bfloat16),
            pltpu.VMEM((SLOTS, SLOT_GROUPS + extra, GROUP, width), jnp.bfloat16),
            pltpu.VMEM((bits + 1,) + small.shape, jnp.float32),
            pltpu.VMEM((bits,) + small.shape, jnp.float32),
            pltpu.SemaphoreType.DMA((loads,)),
            pltpu.SemaphoreType.DMA((SLOTS, 16 + extra)),
            pltpu.SemaphoreType.DMA((SLOTS, 16 + extra)),
            pltpu.SemaphoreType.DMA((SLOTS,)),
            pltpu.SemaphoreType.DMA((bits,)),
            pltpu.SemaphoreType.DMA((bits,)),
        ],
        compiler_params=pltpu.CompilerParams(
            collective_id=1, has_side_effects=True, vmem_limit_bytes=VMEM_LIMIT
        ),
        cost_estimate=pl.CostEstimate(
            flops=2 * rows * blocks * width * width, bytes_accessed=80_000_000, transcendentals=0
        ),
    )(a_side, b_side, small)


PIECE = 384
DEPTH = 4


def spread_kernel(sum_hbm, small_ref, states_hbm, grads_hbm, *refs):
    width = small_ref.shape[1]
    (o_wq, o_bq, o_wk, o_wv, o_bv, o_wo, o_bo, o_g1, o_s1, o_up, o_bu, o_dn, o_bd, o_g2, o_s2) = refs[2:17]
    states_out, grads_out = refs[:2]
    taken, given, held, in_sem, out_sem, held_sem = refs[17:]
    wide = o_bu.shape[1] // width
    targets = []
    for j in range(wide):
        targets += [o_dn.at[0, pl.ds(j * width + r, PIECE), :] for r in range(0, width, PIECE)]
    for j in range(wide):
        targets += [o_up.at[0, pl.ds(r, PIECE), pl.ds(j * width, width)] for r in range(0, width, PIECE)]
    for ref in (o_wo, o_wq, o_wk, o_wv):
        targets += [ref.at[0, pl.ds(r, PIECE), :] for r in range(0, width, PIECE)]

    items = states_hbm.shape[1]
    passes = [(states_hbm.at[0, i], states_out.at[0, i]) for i in range(items)]
    passes += [(grads_hbm.at[0, i], grads_out.at[0, i]) for i in range(items)]

    def pass_in(i):
        return pltpu.make_async_copy(passes[i][0], held.at[i], held_sem.at[i])

    def pass_out(i):
        return pltpu.make_async_copy(held.at[i], passes[i][1], held_sem.at[i])

    def load(i):
        return pltpu.make_async_copy(
            sum_hbm.at[pl.ds(i * PIECE, PIECE)], taken.at[i % DEPTH], in_sem.at[i % DEPTH]
        )

    def store(i):
        return pltpu.make_async_copy(given.at[i % DEPTH], targets[i], out_sem.at[i % DEPTH])

    for i in range(DEPTH):
        load(i).start()
    for i in range(len(passes)):
        pass_in(i).start()
    singles = [o_bq, o_bv, o_bo, o_g1, o_s1, o_bd, o_g2, o_s2]
    for i, ref in enumerate(singles):
        ref[...] = small_ref[pl.ds(i, 1), :]
    for j in range(wide):
        o_bu[:, pl.ds(j * width, width)] = small_ref[pl.ds(len(singles) + j, 1), :]
    for i in range(len(targets)):
        load(i).wait()
        if i >= DEPTH:
            store(i - DEPTH).wait()

        def convert(r, carry):
            rows = pl.ds(pl.multiple_of(r * 64, 64), 64)
            given[i % DEPTH, rows, :] = taken[i % DEPTH, rows, :].astype(jnp.float32)
            return carry

        lax.fori_loop(0, PIECE // 64, convert, 0)
        store(i).start()
        if i + DEPTH < len(targets):
            load(i + DEPTH).start()
        if i < len(passes):
            pass_in(i).wait()
            pass_out(i).start()
    for i in range(len(targets) - DEPTH, len(targets)):
        store(i).wait()
    for i in range(len(passes)):
        pass_out(i).wait()


def spread(sums, small, states, input_grads, params):
    width = small.shape[1]
    anywhere = pl.BlockSpec(memory_space=pl.ANY)
    local = pl.BlockSpec(memory_space=pltpu.VMEM)
    return pl.pallas_call(
        spread_kernel,
        out_shape=(
            jax.ShapeDtypeStruct(states.shape, states.dtype),
            jax.ShapeDtypeStruct(input_grads.shape, input_grads.dtype),
        )
        + tuple(jax.ShapeDtypeStruct(member.shape, jnp.float32) for member in params),
        in_specs=[anywhere, local, anywhere, anywhere],
        out_specs=(anywhere, anywhere)
        + tuple(anywhere if len(member.shape) == 3 else local for member in params),
        scratch_shapes=[
            pltpu.VMEM((DEPTH, PIECE, width), jnp.bfloat16),
            pltpu.VMEM((DEPTH, PIECE, width), jnp.float32),
            pltpu.VMEM((2 * states.shape[1],) + states.shape[2:], states.dtype),
            pltpu.SemaphoreType.DMA((DEPTH,)),
            pltpu.SemaphoreType.DMA((DEPTH,)),
            pltpu.SemaphoreType.DMA((2 * states.shape[1],)),
        ],
        compiler_params=pltpu.CompilerParams(vmem_limit_bytes=VMEM_LIMIT),
        cost_estimate=pl.CostEstimate(
            flops=12 * width * width, bytes_accessed=80 * width * width, transcendentals=0
        ),
    )(sums, small, states, input_grads)


HALF_LOG = -0.5 / math.log(2.0)
BELL_SCALE = 1.0 / math.sqrt(2.0 * math.pi)
SINGLES = ("bq", "bv", "bo", "g1", "s1", "bd", "g2", "s2")


def product(left, right):
    return lax.dot_general(left, right, (((1,), (0,)), ((), ())), preferred_element_type=jnp.float32)


def product_t(left, right):
    return lax.dot_general(left, right, (((1,), (1,)), ((), ())), preferred_element_type=jnp.float32)


def gelu_pair(z):
    cdf = 0.5 * lax.erf(z * (1.0 / math.sqrt(2.0))) + 0.5
    bell = jnp.exp2(z * z * HALF_LOG)
    return z * cdf, z * BELL_SCALE * bell + cdf


def normed(values):
    average = jnp.mean(values, axis=-1, keepdims=True)
    centered = values - average
    inverse = lax.rsqrt(jnp.mean(centered * centered, axis=-1, keepdims=True) + EPSILON)
    return centered * inverse, inverse


def normed_back(grad, normal, inverse):
    first_mean = jnp.mean(grad, axis=-1, keepdims=True)
    second_mean = jnp.mean(grad * normal, axis=-1, keepdims=True)
    return inverse * (grad - first_mean - normal * second_mean)


def layer_kernel(
    ids_ref,
    lengths_ref,
    captions_hbm,
    regions_ref,
    cotangent_hbm,
    wq_hbm,
    bq_ref,
    wk_hbm,
    wv_hbm,
    bv_ref,
    wo_hbm,
    bo_ref,
    g1_ref,
    s1_ref,
    wu_hbm,
    bu_ref,
    wd_hbm,
    bd_ref,
    g2_ref,
    s2_ref,
    states_hbm,
    grads_hbm,
    a_hbm,
    b_hbm,
    small_ref,
    wqkv,
    wo,
    wu,
    wd,
    wqkv_t,
    wo_t,
    wu_t,
    wd_t,
    table,
    hidden,
    upstream,
    query,
    keys,
    values,
    probs,
    context,
    normal1,
    normal2,
    lowered,
    active,
    slope,
    result,
    staged,
    inverse1,
    inverse2,
    wide1,
    wide2,
    caption_cells,
    weight_sem,
    table_send,
    table_recv,
    fwd_send,
    fwd_recv,
    back_send,
    back_recv,
    out_sem,
):
    items, rows, width = hidden.shape
    held = regions_ref.shape[0]
    cap_rows = captions_hbm.shape[1]
    wide = wu.shape[1] // width
    pairs = HEADS // 2
    pair_width = width // pairs
    head = width // HEADS
    section = lax.axis_index("section")
    batch = lax.axis_index("batch")
    count = lax.axis_size("batch")
    right = (section, lax.rem(batch + 1, count))
    left = (section, lax.rem(batch + count - 1, count))
    other = (1 - section, batch)

    weight_copies = [
        pltpu.make_async_copy(source.at[0], target, weight_sem.at[n])
        for n, (source, target) in enumerate(
            (
                (wq_hbm, wqkv.at[:, pl.ds(0, width)]),
                (wk_hbm, wqkv.at[:, pl.ds(width, width)]),
                (wv_hbm, wqkv.at[:, pl.ds(2 * width, width)]),
                (wo_hbm, wo),
                (wu_hbm, wu),
                (wd_hbm, wd),
            )
        )
    ]
    for copy in weight_copies[:3]:
        copy.start()
    cotangent_copy = pltpu.make_async_copy(cotangent_hbm, upstream, weight_sem.at[6])

    barrier = pltpu.get_barrier_semaphore()
    for peer in (right, left, other):
        pl.semaphore_signal(barrier, inc=1, device_id=peer, device_id_type=MESH)
    pl.semaphore_wait(barrier, 3)

    def table_copy(n, peer):
        return pltpu.make_async_remote_copy(
            src_ref=regions_ref,
            dst_ref=table.at[pl.ds(2 * n * held, held)],
            send_sem=table_send.at[n],
            recv_sem=table_recv.at[n],
            device_id=peer,
            device_id_type=MESH,
        )

    @pl.when(section == 0)
    def _():
        pltpu.make_async_copy(captions_hbm.at[0], caption_cells, weight_sem.at[7]).start()
        table_copy(0, right).start()
        table_copy(1, left).start()
        table[pl.ds(held, held)] = regions_ref[...]
        table_copy(0, right).wait()
        table_copy(1, left).wait()

    for copy in weight_copies[3:]:
        copy.start()

    @pl.when(section == 1)
    def _():
        cotangent_copy.start()

    def forward_copy(i):
        return pltpu.make_async_remote_copy(
            src_ref=result.at[i],
            dst_ref=hidden.at[i],
            send_sem=fwd_send.at[i],
            recv_sem=fwd_recv.at[i],
            device_id=other,
            device_id_type=MESH,
        )

    def back_copy(i):
        return pltpu.make_async_remote_copy(
            src_ref=result.at[i],
            dst_ref=upstream.at[i],
            send_sem=back_send.at[i],
            recv_sem=back_recv.at[i],
            device_id=other,
            device_id_type=MESH,
        )

    def save(i, n):
        at = pl.ds(pl.multiple_of(i * rows, rows), rows)
        first = wide * width
        turn = lax.rem(i, 2)
        if n == 0:
            source, target = active.at[turn], a_hbm.at[at, pl.ds(0, first)]
        elif n == 1:
            source, target = lowered.at[turn], a_hbm.at[at, pl.ds(first, width)]
        elif n == 2:
            source, target = context.at[turn], a_hbm.at[at, pl.ds(first + width, width)]
        elif n == 3:
            source, target = hidden.at[i], a_hbm.at[at, pl.ds(first + 2 * width, width)]
        else:
            source, target = result.at[i], states_hbm.at[0, i]
        return pltpu.make_async_copy(source, target, out_sem.at[i, n])

    def staged_save(i):
        at = pl.ds(pl.multiple_of(i * rows, rows), rows)
        return pltpu.make_async_copy(staged.at[lax.rem(i, 2)], b_hbm.at[at], out_sem.at[i, 5])

    def grad_save(i):
        return pltpu.make_async_copy(result.at[i], grads_hbm.at[0, i], out_sem.at[i, 6])

    def vector(ref, j=0):
        return ref[:, j * width : (j + 1) * width].astype(jnp.float32)

    lane = lax.broadcasted_iota(jnp.int32, (rows, pair_width), 1)

    blocks = [slice(r, r + GROUP) for r in range(0, rows, GROUP)]
    spans = [slice(c, min(c + 128, rows)) for c in range(0, rows, 128)]

    def only(block, h):
        return jnp.where((lane // head) == h, block, jnp.zeros_like(block))

    def caption_copy(i):
        return pltpu.make_async_copy(captions_hbm.at[i], caption_cells, weight_sem.at[7])

    def assemble(i):
        total = count * held
        spot = jnp.minimum(lax.rem(ids_ref[i] - (batch - 1) * held + total, total), 3 * held - 1)
        caption_copy(i).wait()
        whole = jnp.concatenate(
            [caption_cells[...].astype(jnp.float32), table[spot].astype(jnp.float32)], axis=0
        )
        hidden[i] = whole.astype(jnp.bfloat16)

        @pl.when(i + 1 < items)
        def _():
            caption_copy(i + 1).start()

    def forward(i):
        @pl.when((i == 0) & (section == 0))
        def _():
            for copy in weight_copies[:3]:
                copy.wait()

        turn = lax.rem(i, 2)
        source = hidden[i]
        mixed = product(source, wqkv[...])
        for at in blocks:
            scaled = (mixed[at, :width] + vector(bq_ref)) * (1.0 / math.sqrt(head))
            query[i, at, :] = scaled.astype(jnp.bfloat16)
            keys[i, at, :] = mixed[at, width : 2 * width].astype(jnp.bfloat16)
            values[i, at, :] = (mixed[at, 2 * width :] + vector(bv_ref)).astype(jnp.bfloat16)
        position = lax.broadcasted_iota(jnp.int32, (rows, 1), 0)
        live = (position >= cap_rows) | (position < lengths_ref[i])
        key_bias = jnp.where(live, 0.0, -1000000000.0)

        def lanes_of(p):
            return slice(p * pair_width, (p + 1) * pair_width)

        def scored(p):
            k_pair = keys[i, :, lanes_of(p)]
            stacked = jnp.concatenate([only(k_pair, 0), only(k_pair, 1)], axis=0)
            v_turned = values[i, :, lanes_of(p)].astype(jnp.float32).T.astype(jnp.bfloat16)
            return product_t(stacked, query[i, :, lanes_of(p)]), v_turned

        def weighed(p, both):
            for h in range(2):
                for span in spans:
                    scores = both[h * rows : (h + 1) * rows, span] + key_bias
                    expo = jnp.exp(scores - jnp.max(scores, axis=0, keepdims=True))
                    share = pltpu.reciprocal(jnp.sum(expo, axis=0, keepdims=True), approx=True)
                    probs[i, 2 * p + h, :, span] = (expo * share).astype(jnp.bfloat16)

        def mixed_values(p, v_turned):
            return [product(v_turned[h * head : (h + 1) * head], probs[i, 2 * p + h]) for h in range(2)]

        def place_context(p, parts):
            context[turn, :, lanes_of(p)] = jnp.concatenate(parts, axis=0).T.astype(jnp.bfloat16)

        ahead = scored(0)
        parts = None
        for p in range(pairs):
            both, v_turned = ahead
            if p + 1 < pairs:
                ahead = scored(p + 1)
            if parts is not None:
                place_context(p - 1, parts)
            weighed(p, both)
            parts = mixed_values(p, v_turned)
        place_context(pairs - 1, parts)

        @pl.when((i == 0) & (section == 0))
        def _():
            for copy in weight_copies[3:]:
                copy.wait()

        attended = product(context[turn], wo[...])
        for at in blocks:
            n1, inv1 = normed(hidden[i, at, :].astype(jnp.float32) + attended[at] + vector(bo_ref))
            normal1[i, at, :] = n1.astype(jnp.bfloat16)
            inverse1[i, at, :] = inv1
            first = n1 * vector(g1_ref) + vector(s1_ref)
            lowered[turn, at, :] = first.astype(jnp.bfloat16)
            wide1[at, :] = first + vector(bd_ref)
        half = wide * width // 2

        def raised(n):
            return product(lowered[turn], wu[:, n * half : (n + 1) * half])

        def bend(n, z_tile):
            for part in range(0, half, width):
                lanes = slice(n * half + part, n * half + part + width)
                bias = bu_ref[:, lanes].astype(jnp.float32)
                for at in blocks:
                    gelu, slant = gelu_pair(z_tile[at, part : part + width] + bias)
                    active[turn, at, lanes] = gelu.astype(jnp.bfloat16)
                    slope[i, at, lanes] = slant.astype(jnp.bfloat16)

        z_first = raised(0)
        z_second = raised(1)
        bend(0, z_first)
        wide1[...] += product(active[turn, :, :half], wd[:half, :])
        bend(1, z_second)
        lowest = product(active[turn, :, half:], wd[half:, :])
        for at in blocks:
            n2, inv2 = normed(wide1[at, :] + lowest[at])
            normal2[i, at, :] = n2.astype(jnp.bfloat16)
            inverse2[i, at, :] = inv2
            result[i, at, :] = (n2 * vector(g2_ref) + vector(s2_ref)).astype(jnp.bfloat16)

    def folded(value):
        return value[: GROUP // 2] + value[GROUP // 2 :]

    def keep_small(row, value):
        small_ref[row : row + 1, :] += jnp.sum(value, axis=0, keepdims=True)

    def single(name, value):
        keep_small(SINGLES.index(name), value)

    def backward(i):
        slot = lax.rem(i, 2)
        base = (2 + wide) * width

        def stage(at, column, value):
            staged[slot, at, column * width : (column + 1) * width] = value

        def norm_step(at, gradient, normal, inverse, gain, sums):
            n = normal[i, at, :].astype(jnp.float32)
            d_res = normed_back(gradient * vector(gain), n, inverse[i, at, :])
            d_low = d_res.astype(jnp.bfloat16)
            terms = [folded(gradient * n), folded(gradient), folded(d_low.astype(jnp.float32))]
            return d_res, d_low, terms if sums is None else [a + b for a, b in zip(sums, terms)]

        sums = None
        for at in blocks:
            gradient = upstream[i, at, :].astype(jnp.float32)
            d_res, d_low, sums = norm_step(at, gradient, normal2, inverse2, g2_ref, sums)
            wide1[at, :] = d_res
            stage(at, 0, d_low)
        for name, value in zip(("g2", "s2", "bd"), sums):
            single(name, value)
        d_out = staged[slot, :, :width]
        half = wide * width // 2
        for n in range(2):
            d_active = product(d_out, wd_t[:, n * half : (n + 1) * half])
            for part in range(0, half, width):
                j = (n * half + part) // width
                lanes = slice(j * width, (j + 1) * width)
                total = None
                for at in blocks:
                    d_inner = d_active[at, part : part + width] * slope[i, at, lanes].astype(jnp.float32)
                    d_inner = d_inner.astype(jnp.bfloat16)
                    stage(at, 1 + j, d_inner)
                    term = folded(d_inner.astype(jnp.float32))
                    total = term if total is None else total + term
                keep_small(len(SINGLES) + j, total)
        d_deep = product(staged[slot, :, width : (1 + wide) * width], wu_t[...])
        sums = None
        for at in blocks:
            d_res, d_low, sums = norm_step(at, wide1[at, :] + d_deep[at], normal1, inverse1, g1_ref, sums)
            wide2[at, :] = d_res
            stage(at, 1 + wide, d_low)
        for name, value in zip(("g1", "s1", "bo"), sums):
            single(name, value)
        d_att = staged[slot, :, (1 + wide) * width : (2 + wide) * width]
        @pl.when(i == 0)
        def _():
            save(items - 2, 0).wait()
            save(items - 1, 0).wait()

        active[0, :, :width] = product(d_att, wo_t[...]).astype(jnp.bfloat16)

        def lanes_of(p):
            return slice(p * pair_width, (p + 1) * pair_width)

        def place_grad(n, p, block):
            at = base + n * width + p * pair_width
            staged[slot, :, at : at + pair_width] = block.astype(jnp.bfloat16)

        def opened(p):
            v_pair = values[i, :, lanes_of(p)]
            c_pair = active[0, :, lanes_of(p)]
            stacked = jnp.concatenate([only(v_pair, 0), only(v_pair, 1)], axis=0)
            k_turned = keys[i, :, lanes_of(p)].astype(jnp.float32).T.astype(jnp.bfloat16)
            d_value = product(probs[i, 2 * p], only(c_pair, 0))
            d_value += product(probs[i, 2 * p + 1], only(c_pair, 1))
            return product_t(stacked, c_pair), k_turned, d_value

        def score_base(p, h):
            return (2 * (p % 2) + h) * 2 * 128

        def score_grads(p, both):
            for h in range(2):
                for span in spans:
                    prob = probs[i, 2 * p + h, :, span].astype(jnp.float32)
                    d_prob = both[h * rows : (h + 1) * rows, span]
                    drift = jnp.sum(d_prob * prob, axis=0, keepdims=True)
                    at = score_base(p, h)
                    active[1, :, at + span.start : at + span.stop] = (prob * (d_prob - drift)).astype(jnp.bfloat16)
            return [active[1, :, score_base(p, h) : score_base(p, h) + rows] for h in range(2)]

        def closed(p, found, k_turned):
            q_pair = query[i, :, lanes_of(p)]
            d_key = product(found[0], only(q_pair, 0)) + product(found[1], only(q_pair, 1))
            return d_key, [product(k_turned[h * head : (h + 1) * head], found[h]) for h in range(2)]

        def place_grads(p, d_value, d_key, parts):
            place_grad(0, p, jnp.concatenate(parts, axis=0).T * (1.0 / math.sqrt(head)))
            place_grad(1, p, d_key)
            place_grad(2, p, d_value)

        ahead = opened(0)
        waiting = None
        for p in range(pairs):
            both, k_turned, d_value = ahead
            if p + 1 < pairs:
                ahead = opened(p + 1)
            if waiting is not None:
                place_grads(*waiting)
            found = score_grads(p, both)
            d_key, parts = closed(p, found, k_turned)
            waiting = (p, d_value, d_key, parts)
        place_grads(*waiting)
        d_source = product(staged[slot, :, base : base + 3 * width], wqkv_t[...])
        sums = None
        for at in blocks:
            result[i, at, :] = (wide2[at, :] + d_source[at]).astype(jnp.bfloat16)
            terms = [
                folded(staged[slot, at, base : base + width].astype(jnp.float32)),
                folded(staged[slot, at, base + 2 * width : base + 3 * width].astype(jnp.float32)),
            ]
            sums = terms if sums is None else [a + b for a, b in zip(sums, terms)]
        single("bq", sums[0])
        single("bv", sums[1])

    small_ref[...] = jnp.zeros_like(small_ref)
    side = 256
    unit = lax.broadcasted_iota(jnp.int32, (side, side), 0) == lax.broadcasted_iota(jnp.int32, (side, side), 1)
    unit = jnp.where(unit, 1.0, 0.0).astype(jnp.bfloat16)

    def turn_weights():
        for natural, turned in ((wqkv, wqkv_t), (wo, wo_t), (wu, wu_t), (wd, wd_t)):
            for block in range(0, natural.shape[0], width):

                def one(n, carry):
                    at = pl.ds(pl.multiple_of(n * side, side), side)
                    tall = product_t(unit, natural[block : block + width, at])
                    turned[at, block : block + width] = tall.astype(jnp.bfloat16)
                    return carry

                lax.fori_loop(0, natural.shape[1] // side, one, 0)

    @pl.when(section == 1)
    def _():
        for copy in weight_copies:
            copy.wait()
        turn_weights()

    def forward_step(i, carry):
        @pl.when(section == 0)
        def _():
            assemble(i)

        @pl.when(section == 1)
        def _():
            forward_copy(i).wait_recv()

        @pl.when(i >= 2)
        def _():
            for n in range(3):
                save(i - 2, n).wait()

        forward(i)

        @pl.when(section == 0)
        def _():
            forward_copy(i).start()

        for n in range(5):
            save(i, n).start()
        return carry

    lax.fori_loop(0, items, forward_step, 0)

    @pl.when(section == 0)
    def _():
        turn_weights()

    @pl.when(section == 1)
    def _():
        cotangent_copy.wait()

    def backward_step(i, carry):
        @pl.when(section == 0)
        def _():
            back_copy(i).wait_recv()

        @pl.when(i >= 2)
        def _():
            staged_save(i - 2).wait()

        save(i, 4).wait()

        @pl.when(section == 0)
        def _():
            forward_copy(i).wait_send()

        backward(i)

        @pl.when(section == 1)
        def _():
            back_copy(i).start()

        staged_save(i).start()
        grad_save(i).start()
        return carry

    lax.fori_loop(0, items, backward_step, 0)

    def finish(i, carry):
        save(i, 3).wait()
        grad_save(i).wait()

        @pl.when(i >= items - 2)
        def _():
            staged_save(i).wait()
            for n in range(1, 3):
                save(i, n).wait()

        @pl.when(section == 1)
        def _():
            back_copy(i).wait_send()

        return carry

    lax.fori_loop(0, items, finish, 0)


def layered(image_ids, caption_lengths, captions, regions, cotangent, stacked):
    items, cap_rows, width = captions.shape
    held, region_rows, _ = regions.shape
    rows = cap_rows + region_rows
    inner = stacked[9].shape[2]
    low = jnp.bfloat16
    wide = inner // width

    def cells(*shape):
        return pltpu.VMEM(shape, low)

    anywhere = pl.BlockSpec(memory_space=pl.ANY)
    local = pl.BlockSpec(memory_space=pltpu.VMEM)
    scalars = pl.BlockSpec(memory_space=pltpu.SMEM)
    return pl.pallas_call(
        layer_kernel,
        out_shape=(
            jax.ShapeDtypeStruct((1, items, rows, width), low),
            jax.ShapeDtypeStruct((1, items, rows, width), low),
            jax.ShapeDtypeStruct((items * rows, (3 + wide) * width), low),
            jax.ShapeDtypeStruct((items * rows, (5 + wide) * width), low),
            jax.ShapeDtypeStruct((GROUP, width), jnp.float32),
        ),
        in_specs=[scalars, scalars, anywhere, local, anywhere]
        + [anywhere if len(member.shape) == 3 else local for member in stacked],
        out_specs=(anywhere, anywhere, anywhere, anywhere, local),
        scratch_shapes=[
            cells(width, 3 * width),
            cells(width, width),
            cells(width, inner),
            cells(inner, width),
            cells(3 * width, width),
            cells(width, width),
            cells(inner, width),
            cells(width, inner),
            cells(3 * held, region_rows, width),
            cells(items, rows, width),
            cells(items, rows, width),
            cells(items, rows, width),
            cells(items, rows, width),
            cells(items, rows, width),
            cells(items, HEADS, rows, rows),
            cells(2, rows, width),
            cells(items, rows, width),
            cells(items, rows, width),
            cells(2, rows, width),
            cells(2, rows, inner),
            cells(items, rows, inner),
            cells(items, rows, width),
            cells(2, rows, (5 + wide) * width),
            pltpu.VMEM((items, rows, 1), jnp.float32),
            pltpu.VMEM((items, rows, 1), jnp.float32),
            pltpu.VMEM((rows, width), jnp.float32),
            pltpu.VMEM((rows, width), jnp.float32),
            cells(cap_rows, width),
            pltpu.SemaphoreType.DMA((8,)),
            pltpu.SemaphoreType.DMA((2,)),
            pltpu.SemaphoreType.DMA((2,)),
            pltpu.SemaphoreType.DMA((items,)),
            pltpu.SemaphoreType.DMA((items,)),
            pltpu.SemaphoreType.DMA((items,)),
            pltpu.SemaphoreType.DMA((items,)),
            pltpu.SemaphoreType.DMA((items, 7)),
        ],
        compiler_params=pltpu.CompilerParams(
            collective_id=0, has_side_effects=True, vmem_limit_bytes=VMEM_LIMIT
        ),
        cost_estimate=pl.CostEstimate(
            flops=4 * items * rows * (4 + 2 * wide) * width * width,
            bytes_accessed=60_000_000,
            transcendentals=0,
        ),
    )(image_ids, caption_lengths, captions, regions, cotangent, *stacked)


def body(
    captions,
    regions,
    image_ids,
    caption_lengths,
    cotangent,
    query_weight,
    query_bias,
    key_weight,
    value_weight,
    value_bias,
    out_weight,
    out_bias,
    norm1_gain,
    norm1_bias,
    up_weight,
    up_bias,
    down_weight,
    down_bias,
    norm2_gain,
    norm2_bias,
):
    stacked = (
        query_weight,
        query_bias,
        key_weight,
        value_weight,
        value_bias,
        out_weight,
        out_bias,
        norm1_gain,
        norm1_bias,
        up_weight,
        up_bias,
        down_weight,
        down_bias,
        norm2_gain,
        norm2_bias,
    )
    width = captions.shape[2]
    states, input_grads, a_side, b_side, small = layered(
        image_ids, caption_lengths, captions, regions, cotangent, stacked
    )
    sums, small_sums = reduced(a_side, b_side, small, lax.axis_size("batch"))
    return tuple(spread(sums.reshape(-1, width), small_sums, states, input_grads, stacked))


def solution(mesh):
    placed = (
        P("batch", None, None),
        P("batch", None, None),
        P("batch"),
        P("batch"),
        P("batch", None, None),
        P("section", None, None),
        P("section", None),
        P("section", None, None),
        P("section", None, None),
        P("section", None),
        P("section", None, None),
        P("section", None),
        P("section", None),
        P("section", None),
        P("section", None, None),
        P("section", None),
        P("section", None, None),
        P("section", None),
        P("section", None),
        P("section", None),
    )
    return jax.shard_map(
        body,
        mesh=mesh,
        in_specs=placed,
        out_specs=(
            P("section", "batch", None, None),
            P("section", "batch", None, None),
            P("section", None, None),
            P("section", None),
            P("section", None, None),
            P("section", None, None),
            P("section", None),
            P("section", None, None),
            P("section", None),
            P("section", None),
            P("section", None),
            P("section", None, None),
            P("section", None),
            P("section", None, None),
            P("section", None),
            P("section", None),
            P("section", None),
        ),
        check_vma=False,
    )
```

```python
import functools
import math

import jax
import jax.numpy as jnp
from jax import lax
from jax.experimental import pallas as pl
from jax.experimental.pallas import tpu as pltpu
from jax.sharding import PartitionSpec as P

HEADS = 12
EPSILON = 1e-12
MESH = pl.DeviceIdType.MESH
VMEM_LIMIT = 63 * 1024 * 1024
GROUP = 16
CHUNK_GROUPS = 16
SLOTS = 18
SLOT_GROUPS = 24
LAG = 3
CYCLE = 3
MOVED = 2
LINE = 4
SPLIT_BITS = 4


def reduce_kernel(
    bits,
    chunks,
    a_hbm,
    b_hbm,
    small_ref,
    out_hbm,
    small_out,
    a_ref,
    b_ref,
    acc,
    whole,
    recv,
    small_acc,
    small_recv,
    load_sem,
    send_sem,
    recv_sem,
    save_sem,
    small_send_sem,
    small_recv_sem,
    moved_send,
    moved_recv,
    returned_send,
    returned_recv,
):
    width = acc.shape[2]
    extra = bits - SPLIT_BITS
    first_gather = SPLIT_BITS + 1 + extra
    stages = 2 * (SPLIT_BITS + 1) + extra + 1
    me = lax.axis_index("batch")
    section = lax.axis_index("section")
    core, side, place = me % 2, (me // 2) % 2, (me // 4) % LINE
    blocks_a = a_hbm.shape[1] // width
    blocks_b = b_hbm.shape[1] // width
    per_block = width // (CHUNK_GROUPS * GROUP)

    def load(source, target, block, base):
        lanes = pl.ds(block * width, width)
        return pltpu.make_async_copy(source.at[:, lanes], target.at[:, lanes], load_sem.at[base + block])

    def load_a(block):
        return load(a_hbm, a_ref, block, 0)

    def load_b(block):
        return load(b_hbm, b_ref, block, blocks_a)

    wide = blocks_a - 3
    order = [(load_a, 0), (load_b, 0)] + [(load_a, j) for j in range(1, wide)]
    order += [(load_a, wide)] + [(load_b, 1 + j) for j in range(wide)]
    order += [(load_a, wide + 1), (load_b, wide + 1), (load_a, wide + 2)]
    order += [(load_b, wide + 2 + j) for j in range(3)]
    for kind, block in order:
        kind(block).start()

    def bit_mate(k):
        bit = (me // 2**k) % 2
        return (section, me + 2**k * (1 - 2 * bit))

    core_mate, side_mate = bit_mate(0), bit_mate(1)
    mates = ((section, me - LINE), (section, me + LINE))
    ring = [(section, me + LINE * ((place + d) % LINE - place)) for d in (LINE - 1, 1)]

    other = (1 - section, me)
    chunks_here = chunks - MOVED + 2 * MOVED * section
    own = chunks - MOVED * (1 - section)
    barrier = pltpu.get_barrier_semaphore()
    for peer in [core_mate, side_mate] + ring + [bit_mate(k) for k in range(2, bits)]:
        pl.semaphore_signal(barrier, inc=1, device_id=peer, device_id_type=MESH)

    @pl.when(section == 1)
    def _():
        pl.semaphore_signal(barrier, inc=1, device_id=other, device_id_type=MESH)


    def low_core(c):
        return c * CHUNK_GROUPS + core * 8

    def low_side(c):
        return low_core(c) + side * 4

    def block_start(c, kind, b):
        return low_side(c) + b if kind == 0 else low_core(c) + 2 * b

    def final(c, kind):
        return low_side(c) + place if kind == 0 else low_core(c) + 2 * place + side

    def remote(c, source, start, size, target, spot, index, peer):
        return pltpu.make_async_remote_copy(
            src_ref=source.at[pl.ds(start, size)],
            dst_ref=target.at[lax.rem(c, SLOTS), pl.ds(spot, size)] if target is recv else target.at[pl.ds(start, size)],
            send_sem=send_sem.at[lax.rem(c, SLOTS), index],
            recv_sem=recv_sem.at[lax.rem(c, SLOTS), index],
            device_id=peer,
            device_id_type=MESH,
        )

    def core_copy(c):
        return remote(c, acc, c * CHUNK_GROUPS + (1 - core) * 8, 8, recv, 0, 0, core_mate)

    def side_copy(c, kind):
        if kind == 0:
            return remote(c, acc, low_core(c) + (1 - side) * 4, 4, recv, 8, 1, side_mate)
        return remote(c, acc, low_core(c) + 2 * place + (1 - side), 1, recv, 8, 1, side_mate)

    def line_copy(c, kind, r, d):
        size = 1 + kind
        b = jnp.minimum(3 - r + place, 3) if d == 1 else jnp.maximum(r - 3 + place, 0)
        spot = 12 + 2 * (2 * r + d)
        return remote(c, acc, block_start(c, kind, b), size, recv, spot, 2 + 2 * r + d, mates[d])

    def spread_copy(c, kind, r, d):
        size = 1 + kind
        b = jnp.maximum(place - r, 0) if d == 1 else jnp.minimum(place + r, 3)
        return remote(c, whole, block_start(c, kind, b), size, whole, 0, 8 + 2 * r + d, mates[d])

    def side_back_copy(c, kind):
        if kind == 0:
            return remote(c, whole, low_side(c), 4, whole, 0, 14, side_mate)
        return remote(c, whole, final(c, kind), 1, whole, 0, 14, side_mate)

    def core_back_copy(c):
        return remote(c, whole, low_core(c), 8, whole, 0, 15, core_mate)

    def extra_copy(c, kind, e):
        return remote(c, acc, final(c, kind), 1, recv, 24 + e, 16 + e, bit_mate(SPLIT_BITS + e))

    def save_copy(c):
        at = pl.ds(c * CHUNK_GROUPS, CHUNK_GROUPS)
        return pltpu.make_async_copy(whole.at[at], out_hbm.at[at], save_sem.at[lax.rem(c, SLOTS)])

    def chunk_at(c):
        return pl.ds(c * CHUNK_GROUPS, CHUNK_GROUPS)

    def moved_copy(f):
        return pltpu.make_async_remote_copy(
            src_ref=acc.at[chunk_at(chunks - MOVED + f)],
            dst_ref=acc.at[chunk_at(chunks + f)],
            send_sem=moved_send.at[f],
            recv_sem=moved_recv.at[f],
            device_id=other,
            device_id_type=MESH,
        )

    def returned_copy(f):
        return pltpu.make_async_remote_copy(
            src_ref=whole.at[chunk_at(chunks + f)],
            dst_ref=whole.at[chunk_at(chunks - MOVED + f)],
            send_sem=returned_send.at[f],
            recv_sem=returned_recv.at[f],
            device_id=other,
            device_id_type=MESH,
        )

    def returned_save(f):
        at = chunk_at(chunks - MOVED + f)
        return pltpu.make_async_copy(whole.at[at], out_hbm.at[at], moved_send.at[f])

    def add_groups(start, count, c, spot):
        slot = lax.rem(c, SLOTS)
        for g in range(count):
            total = acc[start + g].astype(jnp.float32) + recv[slot, spot + g].astype(jnp.float32)
            acc[start + g] = total.astype(jnp.bfloat16)

    def name_of(kind, s):
        if s == 0:
            return ("core",)
        if s == stages - 1:
            return ("save",)
        if s == stages - 2:
            return ("core_back",)
        if s < SPLIT_BITS + 1:
            order = [("side",), ("line", 0), ("line", 1), ("line", 2)]
            order = order if kind == 0 else order[1:] + order[:1]
            return order[s - 1]
        if s < first_gather:
            return ("extra", s - SPLIT_BITS - 1)
        order = [("spread", 0), ("spread", 1), ("spread", 2), ("side_back",)]
        order = order if kind == 0 else order[3:] + order[:3]
        return order[s - first_gather]

    def start_stage(c, kind, s):
        name = name_of(kind, s)
        if s == first_gather:
            whole[final(c, kind)] = acc[final(c, kind)]
        if name[0] == "core":
            core_copy(c).start()
        elif name[0] == "side":
            side_copy(c, kind).start()
        elif name[0] == "line":
            r = name[1]
            pl.when(place <= r)(lambda: line_copy(c, kind, r, 1).start())
            pl.when(place >= 3 - r)(lambda: line_copy(c, kind, r, 0).start())
        elif name[0] == "extra":
            extra_copy(c, kind, name[1]).start()
        elif name[0] == "spread":
            r = name[1]
            pl.when((place >= r) & (place <= 2))(lambda: spread_copy(c, kind, r, 1).start())
            pl.when((place >= 1) & (place <= 3 - r))(lambda: spread_copy(c, kind, r, 0).start())
        elif name[0] == "side_back":
            side_back_copy(c, kind).start()
        elif name[0] == "core_back":
            core_back_copy(c).start()
        else:
            pl.when(c < chunks)(lambda: save_copy(c).start())
            for f in range(MOVED):
                pl.when(c == chunks + f)(lambda: returned_copy(f).start())

    def finish_stage(c, kind, s):
        name = name_of(kind, s)
        if name[0] == "core":
            core_copy(c).wait()
            add_groups(low_core(c), 8, c, 0)
        elif name[0] == "side":
            side_copy(c, kind).wait()
            if kind == 0:
                add_groups(low_side(c), 4, c, 8)
            else:
                add_groups(final(c, kind), 1, c, 8)
        elif name[0] == "line":
            r = name[1]

            @pl.when(place <= r)
            def _():
                line_copy(c, kind, r, 1).wait_send()

            @pl.when(place >= 3 - r)
            def _():
                line_copy(c, kind, r, 0).wait_send()

            @pl.when((place >= 1) & (place <= r + 1))
            def _():
                line_copy(c, kind, r, 1).wait_recv()
                add_groups(block_start(c, kind, 2 - r + place), 1 + kind, c, 12 + 2 * (2 * r + 1))

            @pl.when((place <= 2) & (place >= 2 - r))
            def _():
                line_copy(c, kind, r, 0).wait_recv()
                add_groups(block_start(c, kind, r - 2 + place), 1 + kind, c, 12 + 2 * (2 * r))

        elif name[0] == "extra":
            extra_copy(c, kind, name[1]).wait()
            add_groups(final(c, kind), 1, c, 24 + name[1])
        elif name[0] == "spread":
            r = name[1]
            pl.when((place >= r) & (place <= 2))(lambda: spread_copy(c, kind, r, 1).wait_send())
            pl.when((place >= 1) & (place <= 3 - r))(lambda: spread_copy(c, kind, r, 0).wait_send())
            pl.when(place >= r + 1)(lambda: spread_copy(c, kind, r, 1).wait_recv())
            pl.when(place <= 2 - r)(lambda: spread_copy(c, kind, r, 0).wait_recv())
        elif name[0] == "side_back":
            side_back_copy(c, kind).wait()
        elif name[0] == "core_back":
            core_back_copy(c).wait()
        else:
            pl.when(c < chunks)(lambda: save_copy(c).wait())
            for f in range(MOVED):
                pl.when(c == chunks + f)(lambda: returned_copy(f).wait_send())

    def small_copy(k):
        return pltpu.make_async_remote_copy(
            src_ref=small_acc.at[k],
            dst_ref=small_recv.at[k],
            send_sem=small_send_sem.at[k],
            recv_sem=small_recv_sem.at[k],
            device_id=bit_mate(k),
            device_id_type=MESH,
        )

    small_acc[0] = small_ref[...]

    def multiply(c):
        block, part = c // per_block, lax.rem(c, per_block)
        a_col = jnp.minimum(block, wide) + jnp.minimum(block // (2 * wide), 1) + jnp.minimum(block // (2 * wide + 1), 1)
        b_col = jnp.maximum(block - wide + 1, 0)
        lines = CHUNK_GROUPS * GROUP
        left = a_ref[:, pl.ds(pl.multiple_of(a_col * width + part * lines, lines), lines)]
        right = b_ref[:, pl.ds(pl.multiple_of(b_col * width, width), width)]
        grad = lax.dot_general(left, right, (((0,), (0,)), ((), ())), preferred_element_type=jnp.float32)
        acc[chunk_at(c)] = grad.astype(jnp.bfloat16).reshape(CHUNK_GROUPS, GROUP, width)

    for kind, block in order[:2]:
        kind(block).wait()
    multiply(0)
    pl.semaphore_wait(barrier, bits + 3 - section)

    def step(t, phase):
        for s in range(stages, 0, -1):
            c = t - LAG * s
            kind = (phase - LAG * s) % CYCLE // 2

            @pl.when((c >= 0) & (c < chunks_here))
            def _():
                finish_stage(c, kind, s - 1)
                if s < stages:
                    start_stage(c, kind, s)

        @pl.when(t == per_block - 1)
        def _():
            for kind, block in order[2:]:
                kind(block).wait()

        for f in range(MOVED):
            pl.when(t == chunks + f)(lambda: pl.when(section == 1)(lambda: moved_copy(f).wait_recv()))

        @pl.when(t < chunks_here)
        def _():
            core_copy(t).start()

        @pl.when(t + 1 < own)
        def _():
            multiply(t + 1)

        for k in range(bits + 1):

            @pl.when(t == LAG * k)
            def _():
                if k > 0:
                    small_copy(k - 1).wait()
                    small_acc[k] = small_acc[k - 1] + small_recv[k - 1]
                if k < bits:
                    small_copy(k).start()

    def cycle(n, carry):
        for phase in range(CYCLE):
            step(n * CYCLE + phase, phase)

        @pl.when((section == 0) & (n >= 1) & (n <= MOVED))
        def _():
            multiply(chunks - MOVED - 1 + n)
            for f in range(MOVED):
                pl.when(n == 1 + f)(lambda: moved_copy(f).start())

        return carry

    lax.fori_loop(0, pl.cdiv(chunks + MOVED + LAG * stages, CYCLE), cycle, 0)

    @pl.when(section == 0)
    def _():
        for f in range(MOVED):
            moved_copy(f).wait_send()
        for f in range(MOVED):
            returned_copy(f).wait_recv()
            returned_save(f).start()
        for f in range(MOVED):
            returned_save(f).wait()

    small_out[...] = small_acc[bits]


def reduced(a_side, b_side, small, count):
    rows = a_side.shape[0]
    width = small.shape[1]
    bits = count.bit_length() - 1
    extra = bits - SPLIT_BITS
    blocks = 2 * (a_side.shape[1] // width - 3) + 4
    chunks = blocks * width // (CHUNK_GROUPS * GROUP)
    groups = chunks * CHUNK_GROUPS
    loads = (a_side.shape[1] + b_side.shape[1]) // width
    return pl.pallas_call(
        functools.partial(reduce_kernel, bits, chunks),
        out_shape=(
            jax.ShapeDtypeStruct((groups, GROUP, width), jnp.bfloat16),
            jax.ShapeDtypeStruct(small.shape, jnp.float32),
        ),
        in_specs=[
            pl.BlockSpec(memory_space=pl.ANY),
            pl.BlockSpec(memory_space=pl.ANY),
            pl.BlockSpec(memory_space=pltpu.VMEM),
        ],
        out_specs=(pl.BlockSpec(memory_space=pl.ANY), pl.BlockSpec(memory_space=pltpu.VMEM)),
        scratch_shapes=[
            pltpu.VMEM(a_side.shape, jnp.bfloat16),
            pltpu.VMEM(b_side.shape, jnp.bfloat16),
            pltpu.VMEM((groups + MOVED * CHUNK_GROUPS, GROUP, width), jnp.bfloat16),
            pltpu.VMEM((groups + MOVED * CHUNK_GROUPS, GROUP, width), jnp.bfloat16),
            pltpu.VMEM((SLOTS, SLOT_GROUPS + extra, GROUP, width), jnp.bfloat16),
            pltpu.VMEM((bits + 1,) + small.shape, jnp.float32),
            pltpu.VMEM((bits,) + small.shape, jnp.float32),
            pltpu.SemaphoreType.DMA((loads,)),
            pltpu.SemaphoreType.DMA((SLOTS, 16 + extra)),
            pltpu.SemaphoreType.DMA((SLOTS, 16 + extra)),
            pltpu.SemaphoreType.DMA((SLOTS,)),
            pltpu.SemaphoreType.DMA((bits,)),
            pltpu.SemaphoreType.DMA((bits,)),
            pltpu.SemaphoreType.DMA((MOVED,)),
            pltpu.SemaphoreType.DMA((MOVED,)),
            pltpu.SemaphoreType.DMA((MOVED,)),
            pltpu.SemaphoreType.DMA((MOVED,)),
        ],
        compiler_params=pltpu.CompilerParams(
            collective_id=1, has_side_effects=True, vmem_limit_bytes=VMEM_LIMIT
        ),
        cost_estimate=pl.CostEstimate(
            flops=2 * rows * blocks * width * width, bytes_accessed=80_000_000, transcendentals=0
        ),
    )(a_side, b_side, small)


PIECE = 384
DEPTH = 4


def spread_kernel(sum_hbm, small_ref, states_hbm, grads_hbm, *refs):
    width = small_ref.shape[1]
    (o_wq, o_bq, o_wk, o_wv, o_bv, o_wo, o_bo, o_g1, o_s1, o_up, o_bu, o_dn, o_bd, o_g2, o_s2) = refs[2:17]
    states_out, grads_out = refs[:2]
    taken, given, held, in_sem, out_sem, held_sem = refs[17:]
    wide = o_bu.shape[1] // width
    targets = []
    for j in range(wide):
        targets += [o_dn.at[0, pl.ds(j * width + r, PIECE), :] for r in range(0, width, PIECE)]
    for j in range(wide):
        targets += [o_up.at[0, pl.ds(r, PIECE), pl.ds(j * width, width)] for r in range(0, width, PIECE)]
    for ref in (o_wo, o_wq, o_wk, o_wv):
        targets += [ref.at[0, pl.ds(r, PIECE), :] for r in range(0, width, PIECE)]

    items = states_hbm.shape[1]
    passes = [(states_hbm.at[0, i], states_out.at[0, i]) for i in range(items)]
    passes += [(grads_hbm.at[0, i], grads_out.at[0, i]) for i in range(items)]

    def pass_in(i):
        return pltpu.make_async_copy(passes[i][0], held.at[i], held_sem.at[i])

    def pass_out(i):
        return pltpu.make_async_copy(held.at[i], passes[i][1], held_sem.at[i])

    def load(i):
        return pltpu.make_async_copy(
            sum_hbm.at[pl.ds(i * PIECE, PIECE)], taken.at[i % DEPTH], in_sem.at[i % DEPTH]
        )

    def store(i):
        return pltpu.make_async_copy(given.at[i % DEPTH], targets[i], out_sem.at[i % DEPTH])

    for i in range(DEPTH):
        load(i).start()
    for i in range(len(passes)):
        pass_in(i).start()
    singles = [o_bq, o_bv, o_bo, o_g1, o_s1, o_bd, o_g2, o_s2]
    for i, ref in enumerate(singles):
        ref[...] = small_ref[pl.ds(i, 1), :]
    for j in range(wide):
        o_bu[:, pl.ds(j * width, width)] = small_ref[pl.ds(len(singles) + j, 1), :]
    for i in range(len(targets)):
        load(i).wait()
        if i >= DEPTH:
            store(i - DEPTH).wait()

        def convert(r, carry):
            rows = pl.ds(pl.multiple_of(r * 64, 64), 64)
            given[i % DEPTH, rows, :] = taken[i % DEPTH, rows, :].astype(jnp.float32)
            return carry

        lax.fori_loop(0, PIECE // 64, convert, 0)
        store(i).start()
        if i + DEPTH < len(targets):
            load(i + DEPTH).start()
        if i < len(passes):
            pass_in(i).wait()
            pass_out(i).start()
    for i in range(len(targets) - DEPTH, len(targets)):
        store(i).wait()
    for i in range(len(passes)):
        pass_out(i).wait()


def spread(sums, small, states, input_grads, params):
    width = small.shape[1]
    anywhere = pl.BlockSpec(memory_space=pl.ANY)
    local = pl.BlockSpec(memory_space=pltpu.VMEM)
    return pl.pallas_call(
        spread_kernel,
        out_shape=(
            jax.ShapeDtypeStruct(states.shape, states.dtype),
            jax.ShapeDtypeStruct(input_grads.shape, input_grads.dtype),
        )
        + tuple(jax.ShapeDtypeStruct(member.shape, jnp.float32) for member in params),
        in_specs=[anywhere, local, anywhere, anywhere],
        out_specs=(anywhere, anywhere)
        + tuple(anywhere if len(member.shape) == 3 else local for member in params),
        scratch_shapes=[
            pltpu.VMEM((DEPTH, PIECE, width), jnp.bfloat16),
            pltpu.VMEM((DEPTH, PIECE, width), jnp.float32),
            pltpu.VMEM((2 * states.shape[1],) + states.shape[2:], states.dtype),
            pltpu.SemaphoreType.DMA((DEPTH,)),
            pltpu.SemaphoreType.DMA((DEPTH,)),
            pltpu.SemaphoreType.DMA((2 * states.shape[1],)),
        ],
        compiler_params=pltpu.CompilerParams(vmem_limit_bytes=VMEM_LIMIT),
        cost_estimate=pl.CostEstimate(
            flops=12 * width * width, bytes_accessed=80 * width * width, transcendentals=0
        ),
    )(sums, small, states, input_grads)


HALF_LOG = -0.5 / math.log(2.0)
BELL_SCALE = 1.0 / math.sqrt(2.0 * math.pi)
SINGLES = ("bq", "bv", "bo", "g1", "s1", "bd", "g2", "s2")


def product(left, right):
    return lax.dot_general(left, right, (((1,), (0,)), ((), ())), preferred_element_type=jnp.float32)


def product_t(left, right):
    return lax.dot_general(left, right, (((1,), (1,)), ((), ())), preferred_element_type=jnp.float32)


def gelu_pair(z):
    cdf = 0.5 * lax.erf(z * (1.0 / math.sqrt(2.0))) + 0.5
    bell = jnp.exp2(z * z * HALF_LOG)
    return z * cdf, z * BELL_SCALE * bell + cdf


def normed(values):
    average = jnp.mean(values, axis=-1, keepdims=True)
    centered = values - average
    inverse = lax.rsqrt(jnp.mean(centered * centered, axis=-1, keepdims=True) + EPSILON)
    return centered * inverse, inverse


def normed_back(grad, normal, inverse):
    first_mean = jnp.mean(grad, axis=-1, keepdims=True)
    second_mean = jnp.mean(grad * normal, axis=-1, keepdims=True)
    return inverse * (grad - first_mean - normal * second_mean)


def layer_kernel(
    ids_ref,
    lengths_ref,
    captions_hbm,
    regions_ref,
    cotangent_hbm,
    wq_hbm,
    bq_ref,
    wk_hbm,
    wv_hbm,
    bv_ref,
    wo_hbm,
    bo_ref,
    g1_ref,
    s1_ref,
    wu_hbm,
    bu_ref,
    wd_hbm,
    bd_ref,
    g2_ref,
    s2_ref,
    states_hbm,
    grads_hbm,
    a_hbm,
    b_hbm,
    small_ref,
    wqkv,
    wo,
    wu,
    wd,
    wqkv_t,
    wo_t,
    wu_t,
    wd_t,
    table,
    hidden,
    upstream,
    query,
    keys,
    values,
    probs,
    context,
    normal1,
    normal2,
    lowered,
    active,
    slope,
    result,
    staged,
    inverse1,
    inverse2,
    wide1,
    wide2,
    caption_cells,
    weight_sem,
    table_send,
    table_recv,
    fwd_send,
    fwd_recv,
    back_send,
    back_recv,
    out_sem,
):
    items, rows, width = hidden.shape
    held = regions_ref.shape[0]
    cap_rows = captions_hbm.shape[1]
    wide = wu.shape[1] // width
    pairs = HEADS // 2
    pair_width = width // pairs
    head = width // HEADS
    section = lax.axis_index("section")
    batch = lax.axis_index("batch")
    count = lax.axis_size("batch")
    right = (section, lax.rem(batch + 1, count))
    left = (section, lax.rem(batch + count - 1, count))
    other = (1 - section, batch)

    weight_copies = [
        pltpu.make_async_copy(source.at[0], target, weight_sem.at[n])
        for n, (source, target) in enumerate(
            (
                (wq_hbm, wqkv.at[:, pl.ds(0, width)]),
                (wk_hbm, wqkv.at[:, pl.ds(width, width)]),
                (wv_hbm, wqkv.at[:, pl.ds(2 * width, width)]),
                (wo_hbm, wo),
                (wu_hbm, wu),
                (wd_hbm, wd),
            )
        )
    ]
    for copy in weight_copies[:3]:
        copy.start()
    cotangent_copy = pltpu.make_async_copy(cotangent_hbm, upstream, weight_sem.at[6])

    barrier = pltpu.get_barrier_semaphore()
    for peer in (right, left, other):
        pl.semaphore_signal(barrier, inc=1, device_id=peer, device_id_type=MESH)
    pl.semaphore_wait(barrier, 3)

    def table_copy(n, peer):
        return pltpu.make_async_remote_copy(
            src_ref=regions_ref,
            dst_ref=table.at[pl.ds(2 * n * held, held)],
            send_sem=table_send.at[n],
            recv_sem=table_recv.at[n],
            device_id=peer,
            device_id_type=MESH,
        )

    @pl.when(section == 0)
    def _():
        pltpu.make_async_copy(captions_hbm.at[0], caption_cells, weight_sem.at[7]).start()
        table_copy(0, right).start()
        table_copy(1, left).start()
        table[pl.ds(held, held)] = regions_ref[...]
        table_copy(0, right).wait()
        table_copy(1, left).wait()

    for copy in weight_copies[3:]:
        copy.start()

    @pl.when(section == 1)
    def _():
        cotangent_copy.start()

    def forward_copy(i):
        return pltpu.make_async_remote_copy(
            src_ref=result.at[i],
            dst_ref=hidden.at[i],
            send_sem=fwd_send.at[i],
            recv_sem=fwd_recv.at[i],
            device_id=other,
            device_id_type=MESH,
        )

    def back_copy(i):
        return pltpu.make_async_remote_copy(
            src_ref=result.at[i],
            dst_ref=upstream.at[i],
            send_sem=back_send.at[i],
            recv_sem=back_recv.at[i],
            device_id=other,
            device_id_type=MESH,
        )

    def save(i, n):
        at = pl.ds(pl.multiple_of(i * rows, rows), rows)
        first = wide * width
        turn = lax.rem(i, 2)
        if n == 0:
            source, target = active.at[turn], a_hbm.at[at, pl.ds(0, first)]
        elif n == 1:
            source, target = lowered.at[turn], a_hbm.at[at, pl.ds(first, width)]
        elif n == 2:
            source, target = context.at[turn], a_hbm.at[at, pl.ds(first + width, width)]
        elif n == 3:
            source, target = hidden.at[i], a_hbm.at[at, pl.ds(first + 2 * width, width)]
        else:
            source, target = result.at[i], states_hbm.at[0, i]
        return pltpu.make_async_copy(source, target, out_sem.at[i, n])

    def staged_save(i):
        at = pl.ds(pl.multiple_of(i * rows, rows), rows)
        return pltpu.make_async_copy(staged.at[lax.rem(i, 2)], b_hbm.at[at], out_sem.at[i, 5])

    def grad_save(i):
        return pltpu.make_async_copy(result.at[i], grads_hbm.at[0, i], out_sem.at[i, 6])

    def vector(ref, j=0):
        return ref[:, j * width : (j + 1) * width].astype(jnp.float32)

    lane = lax.broadcasted_iota(jnp.int32, (rows, pair_width), 1)

    blocks = [slice(r, r + GROUP) for r in range(0, rows, GROUP)]
    spans = [slice(c, min(c + 128, rows)) for c in range(0, rows, 128)]

    def only(block, h):
        return jnp.where((lane // head) == h, block, jnp.zeros_like(block))

    def caption_copy(i):
        return pltpu.make_async_copy(captions_hbm.at[i], caption_cells, weight_sem.at[7])

    def assemble(i):
        total = count * held
        spot = jnp.minimum(lax.rem(ids_ref[i] - (batch - 1) * held + total, total), 3 * held - 1)
        caption_copy(i).wait()
        whole = jnp.concatenate(
            [caption_cells[...].astype(jnp.float32), table[spot].astype(jnp.float32)], axis=0
        )
        hidden[i] = whole.astype(jnp.bfloat16)

        @pl.when(i + 1 < items)
        def _():
            caption_copy(i + 1).start()

    def forward(i):
        @pl.when((i == 0) & (section == 0))
        def _():
            for copy in weight_copies[:3]:
                copy.wait()

        turn = lax.rem(i, 2)
        source = hidden[i]
        mixed = product(source, wqkv[...])
        for at in blocks:
            scaled = (mixed[at, :width] + vector(bq_ref)) * (1.0 / math.sqrt(head))
            query[i, at, :] = scaled.astype(jnp.bfloat16)
            keys[i, at, :] = mixed[at, width : 2 * width].astype(jnp.bfloat16)
            values[i, at, :] = (mixed[at, 2 * width :] + vector(bv_ref)).astype(jnp.bfloat16)
        position = lax.broadcasted_iota(jnp.int32, (rows, 1), 0)
        live = (position >= cap_rows) | (position < lengths_ref[i])
        key_bias = jnp.where(live, 0.0, -1000000000.0)

        def lanes_of(p):
            return slice(p * pair_width, (p + 1) * pair_width)

        def scored(p):
            k_pair = keys[i, :, lanes_of(p)]
            stacked = jnp.concatenate([only(k_pair, 0), only(k_pair, 1)], axis=0)
            v_turned = values[i, :, lanes_of(p)].astype(jnp.float32).T.astype(jnp.bfloat16)
            return product_t(stacked, query[i, :, lanes_of(p)]), v_turned

        def weighed(p, both):
            for h in range(2):
                for span in spans:
                    scores = both[h * rows : (h + 1) * rows, span] + key_bias
                    expo = jnp.exp(scores - jnp.max(scores, axis=0, keepdims=True))
                    share = pltpu.reciprocal(jnp.sum(expo, axis=0, keepdims=True), approx=True)
                    probs[i, 2 * p + h, :, span] = (expo * share).astype(jnp.bfloat16)

        def mixed_values(p, v_turned):
            return [product(v_turned[h * head : (h + 1) * head], probs[i, 2 * p + h]) for h in range(2)]

        def place_context(p, parts):
            context[turn, :, lanes_of(p)] = jnp.concatenate(parts, axis=0).T.astype(jnp.bfloat16)

        ahead = scored(0)
        parts = None
        for p in range(pairs):
            both, v_turned = ahead
            if p + 1 < pairs:
                ahead = scored(p + 1)
            if parts is not None:
                place_context(p - 1, parts)
            weighed(p, both)
            parts = mixed_values(p, v_turned)
        place_context(pairs - 1, parts)

        @pl.when((i == 0) & (section == 0))
        def _():
            for copy in weight_copies[3:]:
                copy.wait()

        attended = product(context[turn], wo[...])
        for at in blocks:
            n1, inv1 = normed(hidden[i, at, :].astype(jnp.float32) + attended[at] + vector(bo_ref))
            normal1[i, at, :] = n1.astype(jnp.bfloat16)
            inverse1[i, at, :] = inv1
            first = n1 * vector(g1_ref) + vector(s1_ref)
            lowered[turn, at, :] = first.astype(jnp.bfloat16)
            wide1[at, :] = first + vector(bd_ref)
        half = wide * width // 2

        def raised(n):
            return product(lowered[turn], wu[:, n * half : (n + 1) * half])

        def bend(n, z_tile):
            for part in range(0, half, width):
                lanes = slice(n * half + part, n * half + part + width)
                bias = bu_ref[:, lanes].astype(jnp.float32)
                for at in blocks:
                    gelu, slant = gelu_pair(z_tile[at, part : part + width] + bias)
                    active[turn, at, lanes] = gelu.astype(jnp.bfloat16)
                    slope[i, at, lanes] = slant.astype(jnp.bfloat16)

        z_first = raised(0)
        z_second = raised(1)
        bend(0, z_first)
        wide1[...] += product(active[turn, :, :half], wd[:half, :])
        bend(1, z_second)
        lowest = product(active[turn, :, half:], wd[half:, :])
        for at in blocks:
            n2, inv2 = normed(wide1[at, :] + lowest[at])
            normal2[i, at, :] = n2.astype(jnp.bfloat16)
            inverse2[i, at, :] = inv2
            result[i, at, :] = (n2 * vector(g2_ref) + vector(s2_ref)).astype(jnp.bfloat16)

    def folded(value):
        return value[: GROUP // 2] + value[GROUP // 2 :]

    def keep_small(row, value):
        small_ref[row : row + 1, :] += jnp.sum(value, axis=0, keepdims=True)

    def single(name, value):
        keep_small(SINGLES.index(name), value)

    def backward(i):
        slot = lax.rem(i, 2)
        base = (2 + wide) * width

        def stage(at, column, value):
            staged[slot, at, column * width : (column + 1) * width] = value

        def norm_step(at, gradient, normal, inverse, gain, sums):
            n = normal[i, at, :].astype(jnp.float32)
            d_res = normed_back(gradient * vector(gain), n, inverse[i, at, :])
            d_low = d_res.astype(jnp.bfloat16)
            terms = [folded(gradient * n), folded(gradient), folded(d_low.astype(jnp.float32))]
            return d_res, d_low, terms if sums is None else [a + b for a, b in zip(sums, terms)]

        sums = None
        for at in blocks:
            gradient = upstream[i, at, :].astype(jnp.float32)
            d_res, d_low, sums = norm_step(at, gradient, normal2, inverse2, g2_ref, sums)
            wide1[at, :] = d_res
            stage(at, 0, d_low)
        for name, value in zip(("g2", "s2", "bd"), sums):
            single(name, value)
        d_out = staged[slot, :, :width]
        half = wide * width // 2
        for n in range(2):
            d_active = product(d_out, wd_t[:, n * half : (n + 1) * half])
            for part in range(0, half, width):
                j = (n * half + part) // width
                lanes = slice(j * width, (j + 1) * width)
                total = None
                for at in blocks:
                    d_inner = d_active[at, part : part + width] * slope[i, at, lanes].astype(jnp.float32)
                    d_inner = d_inner.astype(jnp.bfloat16)
                    stage(at, 1 + j, d_inner)
                    term = folded(d_inner.astype(jnp.float32))
                    total = term if total is None else total + term
                keep_small(len(SINGLES) + j, total)
        d_deep = product(staged[slot, :, width : (1 + wide) * width], wu_t[...])
        sums = None
        for at in blocks:
            d_res, d_low, sums = norm_step(at, wide1[at, :] + d_deep[at], normal1, inverse1, g1_ref, sums)
            wide2[at, :] = d_res
            stage(at, 1 + wide, d_low)
        for name, value in zip(("g1", "s1", "bo"), sums):
            single(name, value)
        d_att = staged[slot, :, (1 + wide) * width : (2 + wide) * width]
        @pl.when(i == 0)
        def _():
            save(items - 2, 0).wait()
            save(items - 1, 0).wait()

        active[0, :, :width] = product(d_att, wo_t[...]).astype(jnp.bfloat16)

        def lanes_of(p):
            return slice(p * pair_width, (p + 1) * pair_width)

        def place_grad(n, p, block):
            at = base + n * width + p * pair_width
            staged[slot, :, at : at + pair_width] = block.astype(jnp.bfloat16)

        def opened(p):
            v_pair = values[i, :, lanes_of(p)]
            c_pair = active[0, :, lanes_of(p)]
            stacked = jnp.concatenate([only(v_pair, 0), only(v_pair, 1)], axis=0)
            k_turned = keys[i, :, lanes_of(p)].astype(jnp.float32).T.astype(jnp.bfloat16)
            d_value = product(probs[i, 2 * p], only(c_pair, 0))
            d_value += product(probs[i, 2 * p + 1], only(c_pair, 1))
            return product_t(stacked, c_pair), k_turned, d_value

        def score_base(p, h):
            return (2 * (p % 2) + h) * 2 * 128

        def score_grads(p, both):
            for h in range(2):
                for span in spans:
                    prob = probs[i, 2 * p + h, :, span].astype(jnp.float32)
                    d_prob = both[h * rows : (h + 1) * rows, span]
                    drift = jnp.sum(d_prob * prob, axis=0, keepdims=True)
                    at = score_base(p, h)
                    active[1, :, at + span.start : at + span.stop] = (prob * (d_prob - drift)).astype(jnp.bfloat16)
            return [active[1, :, score_base(p, h) : score_base(p, h) + rows] for h in range(2)]

        def closed(p, found, k_turned):
            q_pair = query[i, :, lanes_of(p)]
            d_key = product(found[0], only(q_pair, 0)) + product(found[1], only(q_pair, 1))
            return d_key, [product(k_turned[h * head : (h + 1) * head], found[h]) for h in range(2)]

        def place_grads(p, d_value, d_key, parts):
            place_grad(0, p, jnp.concatenate(parts, axis=0).T * (1.0 / math.sqrt(head)))
            place_grad(1, p, d_key)
            place_grad(2, p, d_value)

        ahead = opened(0)
        waiting = None
        for p in range(pairs):
            both, k_turned, d_value = ahead
            if p + 1 < pairs:
                ahead = opened(p + 1)
            if waiting is not None:
                place_grads(*waiting)
            found = score_grads(p, both)
            d_key, parts = closed(p, found, k_turned)
            waiting = (p, d_value, d_key, parts)
        place_grads(*waiting)
        d_source = product(staged[slot, :, base : base + 3 * width], wqkv_t[...])
        sums = None
        for at in blocks:
            result[i, at, :] = (wide2[at, :] + d_source[at]).astype(jnp.bfloat16)
            terms = [
                folded(staged[slot, at, base : base + width].astype(jnp.float32)),
                folded(staged[slot, at, base + 2 * width : base + 3 * width].astype(jnp.float32)),
            ]
            sums = terms if sums is None else [a + b for a, b in zip(sums, terms)]
        single("bq", sums[0])
        single("bv", sums[1])

    small_ref[...] = jnp.zeros_like(small_ref)
    side = 256
    unit = lax.broadcasted_iota(jnp.int32, (side, side), 0) == lax.broadcasted_iota(jnp.int32, (side, side), 1)
    unit = jnp.where(unit, 1.0, 0.0).astype(jnp.bfloat16)

    def turn_weights():
        for natural, turned in ((wqkv, wqkv_t), (wo, wo_t), (wu, wu_t), (wd, wd_t)):
            for block in range(0, natural.shape[0], width):

                def one(n, carry):
                    at = pl.ds(pl.multiple_of(n * side, side), side)
                    tall = product_t(unit, natural[block : block + width, at])
                    turned[at, block : block + width] = tall.astype(jnp.bfloat16)
                    return carry

                lax.fori_loop(0, natural.shape[1] // side, one, 0)

    @pl.when(section == 1)
    def _():
        for copy in weight_copies:
            copy.wait()
        turn_weights()

    def forward_step(i, carry):
        @pl.when(section == 0)
        def _():
            assemble(i)

        @pl.when(section == 1)
        def _():
            forward_copy(i).wait_recv()

        @pl.when(i >= 2)
        def _():
            for n in range(3):
                save(i - 2, n).wait()

        forward(i)

        @pl.when(section == 0)
        def _():
            forward_copy(i).start()

        for n in range(5):
            save(i, n).start()
        return carry

    lax.fori_loop(0, items, forward_step, 0)

    @pl.when(section == 0)
    def _():
        turn_weights()

    @pl.when(section == 1)
    def _():
        cotangent_copy.wait()

    def backward_step(i, carry):
        @pl.when(section == 0)
        def _():
            back_copy(i).wait_recv()

        @pl.when(i >= 2)
        def _():
            staged_save(i - 2).wait()

        save(i, 4).wait()

        @pl.when(section == 0)
        def _():
            forward_copy(i).wait_send()

        backward(i)

        @pl.when(section == 1)
        def _():
            back_copy(i).start()

        staged_save(i).start()
        grad_save(i).start()
        return carry

    lax.fori_loop(0, items, backward_step, 0)

    def finish(i, carry):
        save(i, 3).wait()
        grad_save(i).wait()

        @pl.when(i >= items - 2)
        def _():
            staged_save(i).wait()
            for n in range(1, 3):
                save(i, n).wait()

        @pl.when(section == 1)
        def _():
            back_copy(i).wait_send()

        return carry

    lax.fori_loop(0, items, finish, 0)


def layered(image_ids, caption_lengths, captions, regions, cotangent, stacked):
    items, cap_rows, width = captions.shape
    held, region_rows, _ = regions.shape
    rows = cap_rows + region_rows
    inner = stacked[9].shape[2]
    low = jnp.bfloat16
    wide = inner // width

    def cells(*shape):
        return pltpu.VMEM(shape, low)

    anywhere = pl.BlockSpec(memory_space=pl.ANY)
    local = pl.BlockSpec(memory_space=pltpu.VMEM)
    scalars = pl.BlockSpec(memory_space=pltpu.SMEM)
    return pl.pallas_call(
        layer_kernel,
        out_shape=(
            jax.ShapeDtypeStruct((1, items, rows, width), low),
            jax.ShapeDtypeStruct((1, items, rows, width), low),
            jax.ShapeDtypeStruct((items * rows, (3 + wide) * width), low),
            jax.ShapeDtypeStruct((items * rows, (5 + wide) * width), low),
            jax.ShapeDtypeStruct((GROUP, width), jnp.float32),
        ),
        in_specs=[scalars, scalars, anywhere, local, anywhere]
        + [anywhere if len(member.shape) == 3 else local for member in stacked],
        out_specs=(anywhere, anywhere, anywhere, anywhere, local),
        scratch_shapes=[
            cells(width, 3 * width),
            cells(width, width),
            cells(width, inner),
            cells(inner, width),
            cells(3 * width, width),
            cells(width, width),
            cells(inner, width),
            cells(width, inner),
            cells(3 * held, region_rows, width),
            cells(items, rows, width),
            cells(items, rows, width),
            cells(items, rows, width),
            cells(items, rows, width),
            cells(items, rows, width),
            cells(items, HEADS, rows, rows),
            cells(2, rows, width),
            cells(items, rows, width),
            cells(items, rows, width),
            cells(2, rows, width),
            cells(2, rows, inner),
            cells(items, rows, inner),
            cells(items, rows, width),
            cells(2, rows, (5 + wide) * width),
            pltpu.VMEM((items, rows, 1), jnp.float32),
            pltpu.VMEM((items, rows, 1), jnp.float32),
            pltpu.VMEM((rows, width), jnp.float32),
            pltpu.VMEM((rows, width), jnp.float32),
            cells(cap_rows, width),
            pltpu.SemaphoreType.DMA((8,)),
            pltpu.SemaphoreType.DMA((2,)),
            pltpu.SemaphoreType.DMA((2,)),
            pltpu.SemaphoreType.DMA((items,)),
            pltpu.SemaphoreType.DMA((items,)),
            pltpu.SemaphoreType.DMA((items,)),
            pltpu.SemaphoreType.DMA((items,)),
            pltpu.SemaphoreType.DMA((items, 7)),
        ],
        compiler_params=pltpu.CompilerParams(
            collective_id=0, has_side_effects=True, vmem_limit_bytes=VMEM_LIMIT
        ),
        cost_estimate=pl.CostEstimate(
            flops=4 * items * rows * (4 + 2 * wide) * width * width,
            bytes_accessed=60_000_000,
            transcendentals=0,
        ),
    )(image_ids, caption_lengths, captions, regions, cotangent, *stacked)


def body(
    captions,
    regions,
    image_ids,
    caption_lengths,
    cotangent,
    query_weight,
    query_bias,
    key_weight,
    value_weight,
    value_bias,
    out_weight,
    out_bias,
    norm1_gain,
    norm1_bias,
    up_weight,
    up_bias,
    down_weight,
    down_bias,
    norm2_gain,
    norm2_bias,
):
    stacked = (
        query_weight,
        query_bias,
        key_weight,
        value_weight,
        value_bias,
        out_weight,
        out_bias,
        norm1_gain,
        norm1_bias,
        up_weight,
        up_bias,
        down_weight,
        down_bias,
        norm2_gain,
        norm2_bias,
    )
    width = captions.shape[2]
    states, input_grads, a_side, b_side, small = layered(
        image_ids, caption_lengths, captions, regions, cotangent, stacked
    )
    sums, small_sums = reduced(a_side, b_side, small, lax.axis_size("batch"))
    return tuple(spread(sums.reshape(-1, width), small_sums, states, input_grads, stacked))


def solution(mesh):
    placed = (
        P("batch", None, None),
        P("batch", None, None),
        P("batch"),
        P("batch"),
        P("batch", None, None),
        P("section", None, None),
        P("section", None),
        P("section", None, None),
        P("section", None, None),
        P("section", None),
        P("section", None, None),
        P("section", None),
        P("section", None),
        P("section", None),
        P("section", None, None),
        P("section", None),
        P("section", None, None),
        P("section", None),
        P("section", None),
        P("section", None),
    )
    return jax.shard_map(
        body,
        mesh=mesh,
        in_specs=placed,
        out_specs=(
            P("section", "batch", None, None),
            P("section", "batch", None, None),
            P("section", None, None),
            P("section", None),
            P("section", None, None),
            P("section", None, None),
            P("section", None),
            P("section", None, None),
            P("section", None),
            P("section", None),
            P("section", None),
            P("section", None, None),
            P("section", None),
            P("section", None, None),
            P("section", None),
            P("section", None),
            P("section", None),
        ),
        check_vma=False,
    )
```

```python
import functools
import math

import jax
import jax.numpy as jnp
from jax import lax
from jax.experimental import pallas as pl
from jax.experimental.pallas import tpu as pltpu
from jax.sharding import PartitionSpec as P

HEADS = 12
EPSILON = 1e-12
MESH = pl.DeviceIdType.MESH
VMEM_LIMIT = 63 * 1024 * 1024
GROUP = 16
CHUNK_GROUPS = 16
SLOTS = 18
SLOT_GROUPS = 24
LAG = 3
CYCLE = 3
MOVED = 2
MOVED_AT = 16
LINE = 4
SPLIT_BITS = 4


def reduce_kernel(
    bits,
    chunks,
    a_hbm,
    b_hbm,
    small_ref,
    out_hbm,
    small_out,
    a_ref,
    b_ref,
    acc,
    whole,
    recv,
    small_acc,
    small_recv,
    load_sem,
    send_sem,
    recv_sem,
    save_sem,
    small_send_sem,
    small_recv_sem,
    moved_send,
    moved_recv,
    returned_send,
    returned_recv,
):
    width = acc.shape[2]
    extra = bits - SPLIT_BITS
    first_gather = SPLIT_BITS + 1 + extra
    stages = 2 * (SPLIT_BITS + 1) + extra + 1
    me = lax.axis_index("batch")
    section = lax.axis_index("section")
    core, side, place = me % 2, (me // 2) % 2, (me // 4) % LINE
    blocks_a = a_hbm.shape[1] // width
    blocks_b = b_hbm.shape[1] // width
    per_block = width // (CHUNK_GROUPS * GROUP)

    def load(source, target, block, base):
        lanes = pl.ds(block * width, width)
        return pltpu.make_async_copy(source.at[:, lanes], target.at[:, lanes], load_sem.at[base + block])

    def load_a(block):
        return load(a_hbm, a_ref, block, 0)

    def load_b(block):
        return load(b_hbm, b_ref, block, blocks_a)

    wide = blocks_a - 3
    order = [(load_a, 0), (load_b, 0)] + [(load_a, j) for j in range(1, wide)]
    order += [(load_a, wide)] + [(load_b, 1 + j) for j in range(wide)]
    order += [(load_a, wide + 1), (load_b, wide + 1), (load_a, wide + 2)]
    order += [(load_b, wide + 2 + j) for j in range(3)]
    for kind, block in order:
        kind(block).start()

    def bit_mate(k):
        bit = (me // 2**k) % 2
        return (section, me + 2**k * (1 - 2 * bit))

    core_mate, side_mate = bit_mate(0), bit_mate(1)
    mates = ((section, me - LINE), (section, me + LINE))
    ring = [(section, me + LINE * ((place + d) % LINE - place)) for d in (LINE - 1, 1)]

    other = (1 - section, me)
    chunks_here = chunks - MOVED + 2 * MOVED * section
    barrier = pltpu.get_barrier_semaphore()
    for peer in [core_mate, side_mate] + ring + [bit_mate(k) for k in range(2, bits)]:
        pl.semaphore_signal(barrier, inc=1, device_id=peer, device_id_type=MESH)

    @pl.when(section == 1)
    def _():
        pl.semaphore_signal(barrier, inc=1, device_id=other, device_id_type=MESH)


    def chunk_of(c):
        taken = jnp.minimum(c // MOVED_AT, 1)
        past = jnp.minimum(c // (MOVED_AT + MOVED), 1)
        return c + section * ((chunks - MOVED_AT) * (taken - past) - MOVED * past)

    def top(c):
        return chunk_of(c) * CHUNK_GROUPS

    def low_core(c):
        return top(c) + core * 8

    def low_side(c):
        return low_core(c) + side * 4

    def block_start(c, kind, b):
        return low_side(c) + b if kind == 0 else low_core(c) + 2 * b

    def final(c, kind):
        return low_side(c) + place if kind == 0 else low_core(c) + 2 * place + side

    def remote(c, source, start, size, target, spot, index, peer):
        return pltpu.make_async_remote_copy(
            src_ref=source.at[pl.ds(start, size)],
            dst_ref=target.at[lax.rem(c, SLOTS), pl.ds(spot, size)] if target is recv else target.at[pl.ds(start, size)],
            send_sem=send_sem.at[lax.rem(c, SLOTS), index],
            recv_sem=recv_sem.at[lax.rem(c, SLOTS), index],
            device_id=peer,
            device_id_type=MESH,
        )

    def core_copy(c):
        return remote(c, acc, top(c) + (1 - core) * 8, 8, recv, 0, 0, core_mate)

    def side_copy(c, kind):
        if kind == 0:
            return remote(c, acc, low_core(c) + (1 - side) * 4, 4, recv, 8, 1, side_mate)
        return remote(c, acc, low_core(c) + 2 * place + (1 - side), 1, recv, 8, 1, side_mate)

    def line_copy(c, kind, r, d):
        size = 1 + kind
        b = jnp.minimum(3 - r + place, 3) if d == 1 else jnp.maximum(r - 3 + place, 0)
        spot = 12 + 2 * (2 * r + d)
        return remote(c, acc, block_start(c, kind, b), size, recv, spot, 2 + 2 * r + d, mates[d])

    def spread_copy(c, kind, r, d):
        size = 1 + kind
        b = jnp.maximum(place - r, 0) if d == 1 else jnp.minimum(place + r, 3)
        return remote(c, whole, block_start(c, kind, b), size, whole, 0, 8 + 2 * r + d, mates[d])

    def side_back_copy(c, kind):
        if kind == 0:
            return remote(c, whole, low_side(c), 4, whole, 0, 14, side_mate)
        return remote(c, whole, final(c, kind), 1, whole, 0, 14, side_mate)

    def core_back_copy(c):
        return remote(c, whole, low_core(c), 8, whole, 0, 15, core_mate)

    def extra_copy(c, kind, e):
        return remote(c, acc, final(c, kind), 1, recv, 24 + e, 16 + e, bit_mate(SPLIT_BITS + e))

    def save_copy(c):
        at = pl.ds(top(c), CHUNK_GROUPS)
        return pltpu.make_async_copy(whole.at[at], out_hbm.at[at], save_sem.at[lax.rem(c, SLOTS)])

    def chunk_at(c):
        return pl.ds(c * CHUNK_GROUPS, CHUNK_GROUPS)

    def moved_copy(f):
        return pltpu.make_async_remote_copy(
            src_ref=acc.at[chunk_at(chunks - MOVED + f)],
            dst_ref=acc.at[chunk_at(chunks + f)],
            send_sem=moved_send.at[f],
            recv_sem=moved_recv.at[f],
            device_id=other,
            device_id_type=MESH,
        )

    def returned_copy(f):
        return pltpu.make_async_remote_copy(
            src_ref=whole.at[chunk_at(chunks + f)],
            dst_ref=whole.at[chunk_at(chunks - MOVED + f)],
            send_sem=returned_send.at[f],
            recv_sem=returned_recv.at[f],
            device_id=other,
            device_id_type=MESH,
        )

    def returned_save(f):
        at = chunk_at(chunks - MOVED + f)
        return pltpu.make_async_copy(whole.at[at], out_hbm.at[at], moved_send.at[f])

    def add_groups(start, count, c, spot):
        slot = lax.rem(c, SLOTS)
        for g in range(count):
            total = acc[start + g].astype(jnp.float32) + recv[slot, spot + g].astype(jnp.float32)
            acc[start + g] = total.astype(jnp.bfloat16)

    def name_of(kind, s):
        if s == 0:
            return ("core",)
        if s == stages - 1:
            return ("save",)
        if s == stages - 2:
            return ("core_back",)
        if s < SPLIT_BITS + 1:
            order = [("side",), ("line", 0), ("line", 1), ("line", 2)]
            order = order if kind == 0 else order[1:] + order[:1]
            return order[s - 1]
        if s < first_gather:
            return ("extra", s - SPLIT_BITS - 1)
        order = [("spread", 0), ("spread", 1), ("spread", 2), ("side_back",)]
        order = order if kind == 0 else order[3:] + order[:3]
        return order[s - first_gather]

    def start_stage(c, kind, s):
        name = name_of(kind, s)
        if s == first_gather:
            whole[final(c, kind)] = acc[final(c, kind)]
        if name[0] == "core":
            core_copy(c).start()
        elif name[0] == "side":
            side_copy(c, kind).start()
        elif name[0] == "line":
            r = name[1]
            pl.when(place <= r)(lambda: line_copy(c, kind, r, 1).start())
            pl.when(place >= 3 - r)(lambda: line_copy(c, kind, r, 0).start())
        elif name[0] == "extra":
            extra_copy(c, kind, name[1]).start()
        elif name[0] == "spread":
            r = name[1]
            pl.when((place >= r) & (place <= 2))(lambda: spread_copy(c, kind, r, 1).start())
            pl.when((place >= 1) & (place <= 3 - r))(lambda: spread_copy(c, kind, r, 0).start())
        elif name[0] == "side_back":
            side_back_copy(c, kind).start()
        elif name[0] == "core_back":
            core_back_copy(c).start()
        else:
            pl.when(chunk_of(c) < chunks)(lambda: save_copy(c).start())
            for f in range(MOVED):
                pl.when(chunk_of(c) == chunks + f)(lambda: returned_copy(f).start())

    def finish_stage(c, kind, s):
        name = name_of(kind, s)
        if name[0] == "core":
            core_copy(c).wait()
            add_groups(low_core(c), 8, c, 0)
        elif name[0] == "side":
            side_copy(c, kind).wait()
            if kind == 0:
                add_groups(low_side(c), 4, c, 8)
            else:
                add_groups(final(c, kind), 1, c, 8)
        elif name[0] == "line":
            r = name[1]

            @pl.when(place <= r)
            def _():
                line_copy(c, kind, r, 1).wait_send()

            @pl.when(place >= 3 - r)
            def _():
                line_copy(c, kind, r, 0).wait_send()

            @pl.when((place >= 1) & (place <= r + 1))
            def _():
                line_copy(c, kind, r, 1).wait_recv()
                add_groups(block_start(c, kind, 2 - r + place), 1 + kind, c, 12 + 2 * (2 * r + 1))

            @pl.when((place <= 2) & (place >= 2 - r))
            def _():
                line_copy(c, kind, r, 0).wait_recv()
                add_groups(block_start(c, kind, r - 2 + place), 1 + kind, c, 12 + 2 * (2 * r))

        elif name[0] == "extra":
            extra_copy(c, kind, name[1]).wait()
            add_groups(final(c, kind), 1, c, 24 + name[1])
        elif name[0] == "spread":
            r = name[1]
            pl.when((place >= r) & (place <= 2))(lambda: spread_copy(c, kind, r, 1).wait_send())
            pl.when((place >= 1) & (place <= 3 - r))(lambda: spread_copy(c, kind, r, 0).wait_send())
            pl.when(place >= r + 1)(lambda: spread_copy(c, kind, r, 1).wait_recv())
            pl.when(place <= 2 - r)(lambda: spread_copy(c, kind, r, 0).wait_recv())
        elif name[0] == "side_back":
            side_back_copy(c, kind).wait()
        elif name[0] == "core_back":
            core_back_copy(c).wait()
        else:
            pl.when(chunk_of(c) < chunks)(lambda: save_copy(c).wait())
            for f in range(MOVED):
                pl.when(chunk_of(c) == chunks + f)(lambda: returned_copy(f).wait_send())

    def small_copy(k):
        return pltpu.make_async_remote_copy(
            src_ref=small_acc.at[k],
            dst_ref=small_recv.at[k],
            send_sem=small_send_sem.at[k],
            recv_sem=small_recv_sem.at[k],
            device_id=bit_mate(k),
            device_id_type=MESH,
        )

    small_acc[0] = small_ref[...]

    def multiply(c):
        block, part = c // per_block, lax.rem(c, per_block)
        a_col = jnp.minimum(block, wide) + jnp.minimum(block // (2 * wide), 1) + jnp.minimum(block // (2 * wide + 1), 1)
        b_col = jnp.maximum(block - wide + 1, 0)
        lines = CHUNK_GROUPS * GROUP
        left = a_ref[:, pl.ds(pl.multiple_of(a_col * width + part * lines, lines), lines)]
        right = b_ref[:, pl.ds(pl.multiple_of(b_col * width, width), width)]
        grad = lax.dot_general(left, right, (((0,), (0,)), ((), ())), preferred_element_type=jnp.float32)
        acc[chunk_at(c)] = grad.astype(jnp.bfloat16).reshape(CHUNK_GROUPS, GROUP, width)

    for kind, block in order[:2]:
        kind(block).wait()
    multiply(0)
    pl.semaphore_wait(barrier, bits + 3 - section)

    def step(t, phase):
        for s in range(stages, 0, -1):
            c = t - LAG * s
            kind = (phase - LAG * s) % CYCLE // 2

            @pl.when((c >= 0) & (c < chunks_here))
            def _():
                finish_stage(c, kind, s - 1)
                if s < stages:
                    start_stage(c, kind, s)

        @pl.when(t == per_block - 1)
        def _():
            for kind, block in order[2:]:
                kind(block).wait()

        for f in range(MOVED):
            pl.when((t == MOVED_AT + f) & (section == 1))(lambda: moved_copy(f).wait_recv())

        @pl.when(t < chunks_here)
        def _():
            core_copy(t).start()

        @pl.when((t + 1 < chunks_here) & (chunk_of(t + 1) < chunks))
        def _():
            multiply(chunk_of(t + 1))

        for k in range(bits + 1):

            @pl.when(t == LAG * k)
            def _():
                if k > 0:
                    small_copy(k - 1).wait()
                    small_acc[k] = small_acc[k - 1] + small_recv[k - 1]
                if k < bits:
                    small_copy(k).start()

    def cycle(n, carry):
        for phase in range(CYCLE):
            step(n * CYCLE + phase, phase)

        @pl.when((section == 0) & (n >= 1) & (n <= MOVED))
        def _():
            multiply(chunks - MOVED - 1 + n)
            for f in range(MOVED):
                pl.when(n == 1 + f)(lambda: moved_copy(f).start())

        return carry

    lax.fori_loop(0, pl.cdiv(chunks + MOVED + LAG * stages, CYCLE), cycle, 0)

    @pl.when(section == 0)
    def _():
        for f in range(MOVED):
            moved_copy(f).wait_send()
        for f in range(MOVED):
            returned_copy(f).wait_recv()
            returned_save(f).start()
        for f in range(MOVED):
            returned_save(f).wait()

    small_out[...] = small_acc[bits]


def reduced(a_side, b_side, small, count):
    rows = a_side.shape[0]
    width = small.shape[1]
    bits = count.bit_length() - 1
    extra = bits - SPLIT_BITS
    blocks = 2 * (a_side.shape[1] // width - 3) + 4
    chunks = blocks * width // (CHUNK_GROUPS * GROUP)
    groups = chunks * CHUNK_GROUPS
    loads = (a_side.shape[1] + b_side.shape[1]) // width
    return pl.pallas_call(
        functools.partial(reduce_kernel, bits, chunks),
        out_shape=(
            jax.ShapeDtypeStruct((groups, GROUP, width), jnp.bfloat16),
            jax.ShapeDtypeStruct(small.shape, jnp.float32),
        ),
        in_specs=[
            pl.BlockSpec(memory_space=pl.ANY),
            pl.BlockSpec(memory_space=pl.ANY),
            pl.BlockSpec(memory_space=pltpu.VMEM),
        ],
        out_specs=(pl.BlockSpec(memory_space=pl.ANY), pl.BlockSpec(memory_space=pltpu.VMEM)),
        scratch_shapes=[
            pltpu.VMEM(a_side.shape, jnp.bfloat16),
            pltpu.VMEM(b_side.shape, jnp.bfloat16),
            pltpu.VMEM((groups + MOVED * CHUNK_GROUPS, GROUP, width), jnp.bfloat16),
            pltpu.VMEM((groups + MOVED * CHUNK_GROUPS, GROUP, width), jnp.bfloat16),
            pltpu.VMEM((SLOTS, SLOT_GROUPS + extra, GROUP, width), jnp.bfloat16),
            pltpu.VMEM((bits + 1,) + small.shape, jnp.float32),
            pltpu.VMEM((bits,) + small.shape, jnp.float32),
            pltpu.SemaphoreType.DMA((loads,)),
            pltpu.SemaphoreType.DMA((SLOTS, 16 + extra)),
            pltpu.SemaphoreType.DMA((SLOTS, 16 + extra)),
            pltpu.SemaphoreType.DMA((SLOTS,)),
            pltpu.SemaphoreType.DMA((bits,)),
            pltpu.SemaphoreType.DMA((bits,)),
            pltpu.SemaphoreType.DMA((MOVED,)),
            pltpu.SemaphoreType.DMA((MOVED,)),
            pltpu.SemaphoreType.DMA((MOVED,)),
            pltpu.SemaphoreType.DMA((MOVED,)),
        ],
        compiler_params=pltpu.CompilerParams(
            collective_id=1, has_side_effects=True, vmem_limit_bytes=VMEM_LIMIT
        ),
        cost_estimate=pl.CostEstimate(
            flops=2 * rows * blocks * width * width, bytes_accessed=80_000_000, transcendentals=0
        ),
    )(a_side, b_side, small)


PIECE = 384
DEPTH = 4


def spread_kernel(sum_hbm, small_ref, states_hbm, grads_hbm, *refs):
    width = small_ref.shape[1]
    (o_wq, o_bq, o_wk, o_wv, o_bv, o_wo, o_bo, o_g1, o_s1, o_up, o_bu, o_dn, o_bd, o_g2, o_s2) = refs[2:17]
    states_out, grads_out = refs[:2]
    taken, given, held, in_sem, out_sem, held_sem = refs[17:]
    wide = o_bu.shape[1] // width
    targets = []
    for j in range(wide):
        targets += [o_dn.at[0, pl.ds(j * width + r, PIECE), :] for r in range(0, width, PIECE)]
    for j in range(wide):
        targets += [o_up.at[0, pl.ds(r, PIECE), pl.ds(j * width, width)] for r in range(0, width, PIECE)]
    for ref in (o_wo, o_wq, o_wk, o_wv):
        targets += [ref.at[0, pl.ds(r, PIECE), :] for r in range(0, width, PIECE)]

    items = states_hbm.shape[1]
    passes = [(states_hbm.at[0, i], states_out.at[0, i]) for i in range(items)]
    passes += [(grads_hbm.at[0, i], grads_out.at[0, i]) for i in range(items)]

    def pass_in(i):
        return pltpu.make_async_copy(passes[i][0], held.at[i], held_sem.at[i])

    def pass_out(i):
        return pltpu.make_async_copy(held.at[i], passes[i][1], held_sem.at[i])

    def load(i):
        return pltpu.make_async_copy(
            sum_hbm.at[pl.ds(i * PIECE, PIECE)], taken.at[i % DEPTH], in_sem.at[i % DEPTH]
        )

    def store(i):
        return pltpu.make_async_copy(given.at[i % DEPTH], targets[i], out_sem.at[i % DEPTH])

    for i in range(DEPTH):
        load(i).start()
    for i in range(len(passes)):
        pass_in(i).start()
    singles = [o_bq, o_bv, o_bo, o_g1, o_s1, o_bd, o_g2, o_s2]
    for i, ref in enumerate(singles):
        ref[...] = small_ref[pl.ds(i, 1), :]
    for j in range(wide):
        o_bu[:, pl.ds(j * width, width)] = small_ref[pl.ds(len(singles) + j, 1), :]
    for i in range(len(targets)):
        load(i).wait()
        if i >= DEPTH:
            store(i - DEPTH).wait()

        def convert(r, carry):
            rows = pl.ds(pl.multiple_of(r * 64, 64), 64)
            given[i % DEPTH, rows, :] = taken[i % DEPTH, rows, :].astype(jnp.float32)
            return carry

        lax.fori_loop(0, PIECE // 64, convert, 0)
        store(i).start()
        if i + DEPTH < len(targets):
            load(i + DEPTH).start()
        if i < len(passes):
            pass_in(i).wait()
            pass_out(i).start()
    for i in range(len(targets) - DEPTH, len(targets)):
        store(i).wait()
    for i in range(len(passes)):
        pass_out(i).wait()


def spread(sums, small, states, input_grads, params):
    width = small.shape[1]
    anywhere = pl.BlockSpec(memory_space=pl.ANY)
    local = pl.BlockSpec(memory_space=pltpu.VMEM)
    return pl.pallas_call(
        spread_kernel,
        out_shape=(
            jax.ShapeDtypeStruct(states.shape, states.dtype),
            jax.ShapeDtypeStruct(input_grads.shape, input_grads.dtype),
        )
        + tuple(jax.ShapeDtypeStruct(member.shape, jnp.float32) for member in params),
        in_specs=[anywhere, local, anywhere, anywhere],
        out_specs=(anywhere, anywhere)
        + tuple(anywhere if len(member.shape) == 3 else local for member in params),
        scratch_shapes=[
            pltpu.VMEM((DEPTH, PIECE, width), jnp.bfloat16),
            pltpu.VMEM((DEPTH, PIECE, width), jnp.float32),
            pltpu.VMEM((2 * states.shape[1],) + states.shape[2:], states.dtype),
            pltpu.SemaphoreType.DMA((DEPTH,)),
            pltpu.SemaphoreType.DMA((DEPTH,)),
            pltpu.SemaphoreType.DMA((2 * states.shape[1],)),
        ],
        compiler_params=pltpu.CompilerParams(vmem_limit_bytes=VMEM_LIMIT),
        cost_estimate=pl.CostEstimate(
            flops=12 * width * width, bytes_accessed=80 * width * width, transcendentals=0
        ),
    )(sums, small, states, input_grads)


HALF_LOG = -0.5 / math.log(2.0)
BELL_SCALE = 1.0 / math.sqrt(2.0 * math.pi)
SINGLES = ("bq", "bv", "bo", "g1", "s1", "bd", "g2", "s2")


def product(left, right):
    return lax.dot_general(left, right, (((1,), (0,)), ((), ())), preferred_element_type=jnp.float32)


def product_t(left, right):
    return lax.dot_general(left, right, (((1,), (1,)), ((), ())), preferred_element_type=jnp.float32)


def gelu_pair(z):
    cdf = 0.5 * lax.erf(z * (1.0 / math.sqrt(2.0))) + 0.5
    bell = jnp.exp2(z * z * HALF_LOG)
    return z * cdf, z * BELL_SCALE * bell + cdf


def normed(values):
    average = jnp.mean(values, axis=-1, keepdims=True)
    centered = values - average
    inverse = lax.rsqrt(jnp.mean(centered * centered, axis=-1, keepdims=True) + EPSILON)
    return centered * inverse, inverse


def normed_back(grad, normal, inverse):
    first_mean = jnp.mean(grad, axis=-1, keepdims=True)
    second_mean = jnp.mean(grad * normal, axis=-1, keepdims=True)
    return inverse * (grad - first_mean - normal * second_mean)


def layer_kernel(
    ids_ref,
    lengths_ref,
    captions_hbm,
    regions_ref,
    cotangent_hbm,
    wq_hbm,
    bq_ref,
    wk_hbm,
    wv_hbm,
    bv_ref,
    wo_hbm,
    bo_ref,
    g1_ref,
    s1_ref,
    wu_hbm,
    bu_ref,
    wd_hbm,
    bd_ref,
    g2_ref,
    s2_ref,
    states_hbm,
    grads_hbm,
    a_hbm,
    b_hbm,
    small_ref,
    wqkv,
    wo,
    wu,
    wd,
    wqkv_t,
    wo_t,
    wu_t,
    wd_t,
    table,
    hidden,
    upstream,
    query,
    keys,
    values,
    probs,
    context,
    normal1,
    normal2,
    lowered,
    active,
    slope,
    result,
    staged,
    inverse1,
    inverse2,
    wide1,
    wide2,
    caption_cells,
    weight_sem,
    table_send,
    table_recv,
    fwd_send,
    fwd_recv,
    back_send,
    back_recv,
    out_sem,
):
    items, rows, width = hidden.shape
    held = regions_ref.shape[0]
    cap_rows = captions_hbm.shape[1]
    wide = wu.shape[1] // width
    pairs = HEADS // 2
    pair_width = width // pairs
    head = width // HEADS
    section = lax.axis_index("section")
    batch = lax.axis_index("batch")
    count = lax.axis_size("batch")
    right = (section, lax.rem(batch + 1, count))
    left = (section, lax.rem(batch + count - 1, count))
    other = (1 - section, batch)

    weight_copies = [
        pltpu.make_async_copy(source.at[0], target, weight_sem.at[n])
        for n, (source, target) in enumerate(
            (
                (wq_hbm, wqkv.at[:, pl.ds(0, width)]),
                (wk_hbm, wqkv.at[:, pl.ds(width, width)]),
                (wv_hbm, wqkv.at[:, pl.ds(2 * width, width)]),
                (wo_hbm, wo),
                (wu_hbm, wu),
                (wd_hbm, wd),
            )
        )
    ]
    for copy in weight_copies[:3]:
        copy.start()
    cotangent_copy = pltpu.make_async_copy(cotangent_hbm, upstream, weight_sem.at[6])

    barrier = pltpu.get_barrier_semaphore()
    for peer in (right, left, other):
        pl.semaphore_signal(barrier, inc=1, device_id=peer, device_id_type=MESH)
    pl.semaphore_wait(barrier, 3)

    def table_copy(n, peer):
        return pltpu.make_async_remote_copy(
            src_ref=regions_ref,
            dst_ref=table.at[pl.ds(2 * n * held, held)],
            send_sem=table_send.at[n],
            recv_sem=table_recv.at[n],
            device_id=peer,
            device_id_type=MESH,
        )

    @pl.when(section == 0)
    def _():
        pltpu.make_async_copy(captions_hbm.at[0], caption_cells, weight_sem.at[7]).start()
        table_copy(0, right).start()
        table_copy(1, left).start()
        table[pl.ds(held, held)] = regions_ref[...]
        table_copy(0, right).wait()
        table_copy(1, left).wait()

    for copy in weight_copies[3:]:
        copy.start()

    @pl.when(section == 1)
    def _():
        cotangent_copy.start()

    def forward_copy(i):
        return pltpu.make_async_remote_copy(
            src_ref=result.at[i],
            dst_ref=hidden.at[i],
            send_sem=fwd_send.at[i],
            recv_sem=fwd_recv.at[i],
            device_id=other,
            device_id_type=MESH,
        )

    def back_copy(i):
        return pltpu.make_async_remote_copy(
            src_ref=result.at[i],
            dst_ref=upstream.at[i],
            send_sem=back_send.at[i],
            recv_sem=back_recv.at[i],
            device_id=other,
            device_id_type=MESH,
        )

    def save(i, n):
        at = pl.ds(pl.multiple_of(i * rows, rows), rows)
        first = wide * width
        turn = lax.rem(i, 2)
        if n == 0:
            source, target = active.at[turn], a_hbm.at[at, pl.ds(0, first)]
        elif n == 1:
            source, target = lowered.at[turn], a_hbm.at[at, pl.ds(first, width)]
        elif n == 2:
            source, target = context.at[turn], a_hbm.at[at, pl.ds(first + width, width)]
        elif n == 3:
            source, target = hidden.at[i], a_hbm.at[at, pl.ds(first + 2 * width, width)]
        else:
            source, target = result.at[i], states_hbm.at[0, i]
        return pltpu.make_async_copy(source, target, out_sem.at[i, n])

    def staged_save(i):
        at = pl.ds(pl.multiple_of(i * rows, rows), rows)
        return pltpu.make_async_copy(staged.at[lax.rem(i, 2)], b_hbm.at[at], out_sem.at[i, 5])

    def grad_save(i):
        return pltpu.make_async_copy(result.at[i], grads_hbm.at[0, i], out_sem.at[i, 6])

    def vector(ref, j=0):
        return ref[:, j * width : (j + 1) * width].astype(jnp.float32)

    lane = lax.broadcasted_iota(jnp.int32, (rows, pair_width), 1)

    blocks = [slice(r, r + GROUP) for r in range(0, rows, GROUP)]
    spans = [slice(c, min(c + 128, rows)) for c in range(0, rows, 128)]

    def only(block, h):
        return jnp.where((lane // head) == h, block, jnp.zeros_like(block))

    def caption_copy(i):
        return pltpu.make_async_copy(captions_hbm.at[i], caption_cells, weight_sem.at[7])

    def assemble(i):
        total = count * held
        spot = jnp.minimum(lax.rem(ids_ref[i] - (batch - 1) * held + total, total), 3 * held - 1)
        caption_copy(i).wait()
        whole = jnp.concatenate(
            [caption_cells[...].astype(jnp.float32), table[spot].astype(jnp.float32)], axis=0
        )
        hidden[i] = whole.astype(jnp.bfloat16)

        @pl.when(i + 1 < items)
        def _():
            caption_copy(i + 1).start()

    def forward(i):
        @pl.when((i == 0) & (section == 0))
        def _():
            for copy in weight_copies[:3]:
                copy.wait()

        turn = lax.rem(i, 2)
        source = hidden[i]
        mixed = product(source, wqkv[...])
        for at in blocks:
            scaled = (mixed[at, :width] + vector(bq_ref)) * (1.0 / math.sqrt(head))
            query[i, at, :] = scaled.astype(jnp.bfloat16)
            keys[i, at, :] = mixed[at, width : 2 * width].astype(jnp.bfloat16)
            values[i, at, :] = (mixed[at, 2 * width :] + vector(bv_ref)).astype(jnp.bfloat16)
        position = lax.broadcasted_iota(jnp.int32, (rows, 1), 0)
        live = (position >= cap_rows) | (position < lengths_ref[i])
        key_bias = jnp.where(live, 0.0, -1000000000.0)

        def lanes_of(p):
            return slice(p * pair_width, (p + 1) * pair_width)

        def scored(p):
            k_pair = keys[i, :, lanes_of(p)]
            stacked = jnp.concatenate([only(k_pair, 0), only(k_pair, 1)], axis=0)
            v_turned = values[i, :, lanes_of(p)].astype(jnp.float32).T.astype(jnp.bfloat16)
            return product_t(stacked, query[i, :, lanes_of(p)]), v_turned

        def weighed(p, both):
            for h in range(2):
                for span in spans:
                    scores = both[h * rows : (h + 1) * rows, span] + key_bias
                    expo = jnp.exp(scores - jnp.max(scores, axis=0, keepdims=True))
                    share = pltpu.reciprocal(jnp.sum(expo, axis=0, keepdims=True), approx=True)
                    probs[i, 2 * p + h, :, span] = (expo * share).astype(jnp.bfloat16)

        def mixed_values(p, v_turned):
            return [product(v_turned[h * head : (h + 1) * head], probs[i, 2 * p + h]) for h in range(2)]

        def place_context(p, parts):
            context[turn, :, lanes_of(p)] = jnp.concatenate(parts, axis=0).T.astype(jnp.bfloat16)

        ahead = scored(0)
        parts = None
        for p in range(pairs):
            both, v_turned = ahead
            if p + 1 < pairs:
                ahead = scored(p + 1)
            if parts is not None:
                place_context(p - 1, parts)
            weighed(p, both)
            parts = mixed_values(p, v_turned)
        place_context(pairs - 1, parts)

        @pl.when((i == 0) & (section == 0))
        def _():
            for copy in weight_copies[3:]:
                copy.wait()

        attended = product(context[turn], wo[...])
        for at in blocks:
            n1, inv1 = normed(hidden[i, at, :].astype(jnp.float32) + attended[at] + vector(bo_ref))
            normal1[i, at, :] = n1.astype(jnp.bfloat16)
            inverse1[i, at, :] = inv1
            first = n1 * vector(g1_ref) + vector(s1_ref)
            lowered[turn, at, :] = first.astype(jnp.bfloat16)
            wide1[at, :] = first + vector(bd_ref)
        half = wide * width // 2

        def raised(n):
            return product(lowered[turn], wu[:, n * half : (n + 1) * half])

        def bend(n, z_tile):
            for part in range(0, half, width):
                lanes = slice(n * half + part, n * half + part + width)
                bias = bu_ref[:, lanes].astype(jnp.float32)
                for at in blocks:
                    gelu, slant = gelu_pair(z_tile[at, part : part + width] + bias)
                    active[turn, at, lanes] = gelu.astype(jnp.bfloat16)
                    slope[i, at, lanes] = slant.astype(jnp.bfloat16)

        z_first = raised(0)
        z_second = raised(1)
        bend(0, z_first)
        wide1[...] += product(active[turn, :, :half], wd[:half, :])
        bend(1, z_second)
        lowest = product(active[turn, :, half:], wd[half:, :])
        for at in blocks:
            n2, inv2 = normed(wide1[at, :] + lowest[at])
            normal2[i, at, :] = n2.astype(jnp.bfloat16)
            inverse2[i, at, :] = inv2
            result[i, at, :] = (n2 * vector(g2_ref) + vector(s2_ref)).astype(jnp.bfloat16)

    def folded(value):
        return value[: GROUP // 2] + value[GROUP // 2 :]

    def keep_small(row, value):
        small_ref[row : row + 1, :] += jnp.sum(value, axis=0, keepdims=True)

    def single(name, value):
        keep_small(SINGLES.index(name), value)

    def backward(i):
        slot = lax.rem(i, 2)
        base = (2 + wide) * width

        def stage(at, column, value):
            staged[slot, at, column * width : (column + 1) * width] = value

        def norm_step(at, gradient, normal, inverse, gain, sums):
            n = normal[i, at, :].astype(jnp.float32)
            d_res = normed_back(gradient * vector(gain), n, inverse[i, at, :])
            d_low = d_res.astype(jnp.bfloat16)
            terms = [folded(gradient * n), folded(gradient), folded(d_low.astype(jnp.float32))]
            return d_res, d_low, terms if sums is None else [a + b for a, b in zip(sums, terms)]

        sums = None
        for at in blocks:
            gradient = upstream[i, at, :].astype(jnp.float32)
            d_res, d_low, sums = norm_step(at, gradient, normal2, inverse2, g2_ref, sums)
            wide1[at, :] = d_res
            stage(at, 0, d_low)
        for name, value in zip(("g2", "s2", "bd"), sums):
            single(name, value)
        d_out = staged[slot, :, :width]
        half = wide * width // 2
        for n in range(2):
            d_active = product(d_out, wd_t[:, n * half : (n + 1) * half])
            for part in range(0, half, width):
                j = (n * half + part) // width
                lanes = slice(j * width, (j + 1) * width)
                total = None
                for at in blocks:
                    d_inner = d_active[at, part : part + width] * slope[i, at, lanes].astype(jnp.float32)
                    d_inner = d_inner.astype(jnp.bfloat16)
                    stage(at, 1 + j, d_inner)
                    term = folded(d_inner.astype(jnp.float32))
                    total = term if total is None else total + term
                keep_small(len(SINGLES) + j, total)
        d_deep = product(staged[slot, :, width : (1 + wide) * width], wu_t[...])
        sums = None
        for at in blocks:
            d_res, d_low, sums = norm_step(at, wide1[at, :] + d_deep[at], normal1, inverse1, g1_ref, sums)
            wide2[at, :] = d_res
            stage(at, 1 + wide, d_low)
        for name, value in zip(("g1", "s1", "bo"), sums):
            single(name, value)
        d_att = staged[slot, :, (1 + wide) * width : (2 + wide) * width]
        @pl.when(i == 0)
        def _():
            save(items - 2, 0).wait()
            save(items - 1, 0).wait()

        active[0, :, :width] = product(d_att, wo_t[...]).astype(jnp.bfloat16)

        def lanes_of(p):
            return slice(p * pair_width, (p + 1) * pair_width)

        def place_grad(n, p, block):
            at = base + n * width + p * pair_width
            staged[slot, :, at : at + pair_width] = block.astype(jnp.bfloat16)

        def opened(p):
            v_pair = values[i, :, lanes_of(p)]
            c_pair = active[0, :, lanes_of(p)]
            stacked = jnp.concatenate([only(v_pair, 0), only(v_pair, 1)], axis=0)
            k_turned = keys[i, :, lanes_of(p)].astype(jnp.float32).T.astype(jnp.bfloat16)
            d_value = product(probs[i, 2 * p], only(c_pair, 0))
            d_value += product(probs[i, 2 * p + 1], only(c_pair, 1))
            return product_t(stacked, c_pair), k_turned, d_value

        def score_base(p, h):
            return (2 * (p % 2) + h) * 2 * 128

        def score_grads(p, both):
            for h in range(2):
                for span in spans:
                    prob = probs[i, 2 * p + h, :, span].astype(jnp.float32)
                    d_prob = both[h * rows : (h + 1) * rows, span]
                    drift = jnp.sum(d_prob * prob, axis=0, keepdims=True)
                    at = score_base(p, h)
                    active[1, :, at + span.start : at + span.stop] = (prob * (d_prob - drift)).astype(jnp.bfloat16)
            return [active[1, :, score_base(p, h) : score_base(p, h) + rows] for h in range(2)]

        def closed(p, found, k_turned):
            q_pair = query[i, :, lanes_of(p)]
            d_key = product(found[0], only(q_pair, 0)) + product(found[1], only(q_pair, 1))
            return d_key, [product(k_turned[h * head : (h + 1) * head], found[h]) for h in range(2)]

        def place_grads(p, d_value, d_key, parts):
            place_grad(0, p, jnp.concatenate(parts, axis=0).T * (1.0 / math.sqrt(head)))
            place_grad(1, p, d_key)
            place_grad(2, p, d_value)

        ahead = opened(0)
        waiting = None
        for p in range(pairs):
            both, k_turned, d_value = ahead
            if p + 1 < pairs:
                ahead = opened(p + 1)
            if waiting is not None:
                place_grads(*waiting)
            found = score_grads(p, both)
            d_key, parts = closed(p, found, k_turned)
            waiting = (p, d_value, d_key, parts)
        place_grads(*waiting)
        d_source = product(staged[slot, :, base : base + 3 * width], wqkv_t[...])
        sums = None
        for at in blocks:
            result[i, at, :] = (wide2[at, :] + d_source[at]).astype(jnp.bfloat16)
            terms = [
                folded(staged[slot, at, base : base + width].astype(jnp.float32)),
                folded(staged[slot, at, base + 2 * width : base + 3 * width].astype(jnp.float32)),
            ]
            sums = terms if sums is None else [a + b for a, b in zip(sums, terms)]
        single("bq", sums[0])
        single("bv", sums[1])

    small_ref[...] = jnp.zeros_like(small_ref)
    side = 256
    unit = lax.broadcasted_iota(jnp.int32, (side, side), 0) == lax.broadcasted_iota(jnp.int32, (side, side), 1)
    unit = jnp.where(unit, 1.0, 0.0).astype(jnp.bfloat16)

    def turn_weights():
        for natural, turned in ((wqkv, wqkv_t), (wo, wo_t), (wu, wu_t), (wd, wd_t)):
            for block in range(0, natural.shape[0], width):

                def one(n, carry):
                    at = pl.ds(pl.multiple_of(n * side, side), side)
                    tall = product_t(unit, natural[block : block + width, at])
                    turned[at, block : block + width] = tall.astype(jnp.bfloat16)
                    return carry

                lax.fori_loop(0, natural.shape[1] // side, one, 0)

    @pl.when(section == 1)
    def _():
        for copy in weight_copies:
            copy.wait()
        turn_weights()

    def forward_step(i, carry):
        @pl.when(section == 0)
        def _():
            assemble(i)

        @pl.when(section == 1)
        def _():
            forward_copy(i).wait_recv()

        @pl.when(i >= 2)
        def _():
            for n in range(3):
                save(i - 2, n).wait()

        forward(i)

        @pl.when(section == 0)
        def _():
            forward_copy(i).start()

        for n in range(5):
            save(i, n).start()
        return carry

    lax.fori_loop(0, items, forward_step, 0)

    @pl.when(section == 0)
    def _():
        turn_weights()

    @pl.when(section == 1)
    def _():
        cotangent_copy.wait()

    def backward_step(i, carry):
        @pl.when(section == 0)
        def _():
            back_copy(i).wait_recv()

        @pl.when(i >= 2)
        def _():
            staged_save(i - 2).wait()

        save(i, 4).wait()

        @pl.when(section == 0)
        def _():
            forward_copy(i).wait_send()

        backward(i)

        @pl.when(section == 1)
        def _():
            back_copy(i).start()

        staged_save(i).start()
        grad_save(i).start()
        return carry

    lax.fori_loop(0, items, backward_step, 0)

    def finish(i, carry):
        save(i, 3).wait()
        grad_save(i).wait()

        @pl.when(i >= items - 2)
        def _():
            staged_save(i).wait()
            for n in range(1, 3):
                save(i, n).wait()

        @pl.when(section == 1)
        def _():
            back_copy(i).wait_send()

        return carry

    lax.fori_loop(0, items, finish, 0)


def layered(image_ids, caption_lengths, captions, regions, cotangent, stacked):
    items, cap_rows, width = captions.shape
    held, region_rows, _ = regions.shape
    rows = cap_rows + region_rows
    inner = stacked[9].shape[2]
    low = jnp.bfloat16
    wide = inner // width

    def cells(*shape):
        return pltpu.VMEM(shape, low)

    anywhere = pl.BlockSpec(memory_space=pl.ANY)
    local = pl.BlockSpec(memory_space=pltpu.VMEM)
    scalars = pl.BlockSpec(memory_space=pltpu.SMEM)
    return pl.pallas_call(
        layer_kernel,
        out_shape=(
            jax.ShapeDtypeStruct((1, items, rows, width), low),
            jax.ShapeDtypeStruct((1, items, rows, width), low),
            jax.ShapeDtypeStruct((items * rows, (3 + wide) * width), low),
            jax.ShapeDtypeStruct((items * rows, (5 + wide) * width), low),
            jax.ShapeDtypeStruct((GROUP, width), jnp.float32),
        ),
        in_specs=[scalars, scalars, anywhere, local, anywhere]
        + [anywhere if len(member.shape) == 3 else local for member in stacked],
        out_specs=(anywhere, anywhere, anywhere, anywhere, local),
        scratch_shapes=[
            cells(width, 3 * width),
            cells(width, width),
            cells(width, inner),
            cells(inner, width),
            cells(3 * width, width),
            cells(width, width),
            cells(inner, width),
            cells(width, inner),
            cells(3 * held, region_rows, width),
            cells(items, rows, width),
            cells(items, rows, width),
            cells(items, rows, width),
            cells(items, rows, width),
            cells(items, rows, width),
            cells(items, HEADS, rows, rows),
            cells(2, rows, width),
            cells(items, rows, width),
            cells(items, rows, width),
            cells(2, rows, width),
            cells(2, rows, inner),
            cells(items, rows, inner),
            cells(items, rows, width),
            cells(2, rows, (5 + wide) * width),
            pltpu.VMEM((items, rows, 1), jnp.float32),
            pltpu.VMEM((items, rows, 1), jnp.float32),
            pltpu.VMEM((rows, width), jnp.float32),
            pltpu.VMEM((rows, width), jnp.float32),
            cells(cap_rows, width),
            pltpu.SemaphoreType.DMA((8,)),
            pltpu.SemaphoreType.DMA((2,)),
            pltpu.SemaphoreType.DMA((2,)),
            pltpu.SemaphoreType.DMA((items,)),
            pltpu.SemaphoreType.DMA((items,)),
            pltpu.SemaphoreType.DMA((items,)),
            pltpu.SemaphoreType.DMA((items,)),
            pltpu.SemaphoreType.DMA((items, 7)),
        ],
        compiler_params=pltpu.CompilerParams(
            collective_id=0, has_side_effects=True, vmem_limit_bytes=VMEM_LIMIT
        ),
        cost_estimate=pl.CostEstimate(
            flops=4 * items * rows * (4 + 2 * wide) * width * width,
            bytes_accessed=60_000_000,
            transcendentals=0,
        ),
    )(image_ids, caption_lengths, captions, regions, cotangent, *stacked)


def body(
    captions,
    regions,
    image_ids,
    caption_lengths,
    cotangent,
    query_weight,
    query_bias,
    key_weight,
    value_weight,
    value_bias,
    out_weight,
    out_bias,
    norm1_gain,
    norm1_bias,
    up_weight,
    up_bias,
    down_weight,
    down_bias,
    norm2_gain,
    norm2_bias,
):
    stacked = (
        query_weight,
        query_bias,
        key_weight,
        value_weight,
        value_bias,
        out_weight,
        out_bias,
        norm1_gain,
        norm1_bias,
        up_weight,
        up_bias,
        down_weight,
        down_bias,
        norm2_gain,
        norm2_bias,
    )
    width = captions.shape[2]
    states, input_grads, a_side, b_side, small = layered(
        image_ids, caption_lengths, captions, regions, cotangent, stacked
    )
    sums, small_sums = reduced(a_side, b_side, small, lax.axis_size("batch"))
    return tuple(spread(sums.reshape(-1, width), small_sums, states, input_grads, stacked))


def solution(mesh):
    placed = (
        P("batch", None, None),
        P("batch", None, None),
        P("batch"),
        P("batch"),
        P("batch", None, None),
        P("section", None, None),
        P("section", None),
        P("section", None, None),
        P("section", None, None),
        P("section", None),
        P("section", None, None),
        P("section", None),
        P("section", None),
        P("section", None),
        P("section", None, None),
        P("section", None),
        P("section", None, None),
        P("section", None),
        P("section", None),
        P("section", None),
    )
    return jax.shard_map(
        body,
        mesh=mesh,
        in_specs=placed,
        out_specs=(
            P("section", "batch", None, None),
            P("section", "batch", None, None),
            P("section", None, None),
            P("section", None),
            P("section", None, None),
            P("section", None, None),
            P("section", None),
            P("section", None, None),
            P("section", None),
            P("section", None),
            P("section", None),
            P("section", None, None),
            P("section", None),
            P("section", None, None),
            P("section", None),
            P("section", None),
            P("section", None),
        ),
        check_vma=False,
    )
```

```python
import functools
import math

import jax
import jax.numpy as jnp
from jax import lax
from jax.experimental import pallas as pl
from jax.experimental.pallas import tpu as pltpu
from jax.sharding import PartitionSpec as P

HEADS = 12
EPSILON = 1e-12
MESH = pl.DeviceIdType.MESH
VMEM_LIMIT = 63 * 1024 * 1024
GROUP = 16
CHUNK_GROUPS = 16
SLOTS = 18
SLOT_GROUPS = 24
LAG = 3
CYCLE = 3
LINE = 4
SPLIT_BITS = 4


def reduce_kernel(
    bits,
    chunks,
    a_hbm,
    b_hbm,
    small_ref,
    out_hbm,
    small_out,
    a_ref,
    b_ref,
    acc,
    whole,
    recv,
    small_acc,
    small_recv,
    load_sem,
    send_sem,
    recv_sem,
    save_sem,
    small_send_sem,
    small_recv_sem,
):
    width = acc.shape[2]
    extra = bits - SPLIT_BITS
    first_gather = SPLIT_BITS + 1 + extra
    stages = 2 * (SPLIT_BITS + 1) + extra + 1
    me = lax.axis_index("batch")
    section = lax.axis_index("section")
    core, side, place = me % 2, (me // 2) % 2, (me // 4) % LINE
    blocks_a = a_hbm.shape[1] // width
    blocks_b = b_hbm.shape[1] // width
    per_block = width // (CHUNK_GROUPS * GROUP)

    def load(source, target, block, base):
        lanes = pl.ds(block * width, width)
        return pltpu.make_async_copy(source.at[:, lanes], target.at[:, lanes], load_sem.at[base + block])

    def load_a(block):
        return load(a_hbm, a_ref, block, 0)

    def load_b(block):
        return load(b_hbm, b_ref, block, blocks_a)

    wide = blocks_a - 3
    order = [(load_a, 0), (load_b, 0)] + [(load_a, j) for j in range(1, wide)]
    order += [(load_a, wide)] + [(load_b, 1 + j) for j in range(wide)]
    order += [(load_a, wide + 1), (load_b, wide + 1), (load_a, wide + 2)]
    order += [(load_b, wide + 2 + j) for j in range(3)]
    for kind, block in order:
        kind(block).start()

    def bit_mate(k):
        bit = (me // 2**k) % 2
        return (section, me + 2**k * (1 - 2 * bit))

    core_mate, side_mate = bit_mate(0), bit_mate(1)
    mates = ((section, me - LINE), (section, me + LINE))
    ring = [(section, me + LINE * ((place + d) % LINE - place)) for d in (LINE - 1, 1)]

    barrier = pltpu.get_barrier_semaphore()
    for peer in [core_mate, side_mate] + ring + [bit_mate(k) for k in range(2, bits)]:
        pl.semaphore_signal(barrier, inc=1, device_id=peer, device_id_type=MESH)

    def low_core(c):
        return c * CHUNK_GROUPS + core * 8

    def low_side(c):
        return low_core(c) + side * 4

    def block_start(c, kind, b):
        return low_side(c) + b if kind == 0 else low_core(c) + 2 * b

    def final(c, kind):
        return low_side(c) + place if kind == 0 else low_core(c) + 2 * place + side

    def remote(c, source, start, size, target, spot, index, peer):
        return pltpu.make_async_remote_copy(
            src_ref=source.at[pl.ds(start, size)],
            dst_ref=target.at[lax.rem(c, SLOTS), pl.ds(spot, size)] if target is recv else target.at[pl.ds(start, size)],
            send_sem=send_sem.at[lax.rem(c, SLOTS), index],
            recv_sem=recv_sem.at[lax.rem(c, SLOTS), index],
            device_id=peer,
            device_id_type=MESH,
        )

    def core_copy(c):
        return remote(c, acc, c * CHUNK_GROUPS + (1 - core) * 8, 8, recv, 0, 0, core_mate)

    def side_copy(c, kind):
        if kind == 0:
            return remote(c, acc, low_core(c) + (1 - side) * 4, 4, recv, 8, 1, side_mate)
        return remote(c, acc, low_core(c) + 2 * place + (1 - side), 1, recv, 8, 1, side_mate)

    def line_copy(c, kind, r, d):
        size = 1 + kind
        b = jnp.minimum(3 - r + place, 3) if d == 1 else jnp.maximum(r - 3 + place, 0)
        spot = 12 + 2 * (2 * r + d)
        return remote(c, acc, block_start(c, kind, b), size, recv, spot, 2 + 2 * r + d, mates[d])

    def spread_copy(c, kind, r, d):
        size = 1 + kind
        b = jnp.maximum(place - r, 0) if d == 1 else jnp.minimum(place + r, 3)
        return remote(c, whole, block_start(c, kind, b), size, whole, 0, 8 + 2 * r + d, mates[d])

    def side_back_copy(c, kind):
        if kind == 0:
            return remote(c, whole, low_side(c), 4, whole, 0, 14, side_mate)
        return remote(c, whole, final(c, kind), 1, whole, 0, 14, side_mate)

    def core_back_copy(c):
        return remote(c, whole, low_core(c), 8, whole, 0, 15, core_mate)

    def extra_copy(c, kind, e):
        return remote(c, acc, final(c, kind), 1, recv, 24 + e, 16 + e, bit_mate(SPLIT_BITS + e))

    def save_copy(c):
        at = pl.ds(c * CHUNK_GROUPS, CHUNK_GROUPS)
        return pltpu.make_async_copy(whole.at[at], out_hbm.at[at], save_sem.at[lax.rem(c, SLOTS)])

    def add_groups(start, count, c, spot):
        slot = lax.rem(c, SLOTS)
        for g in range(count):
            total = acc[start + g].astype(jnp.float32) + recv[slot, spot + g].astype(jnp.float32)
            acc[start + g] = total.astype(jnp.bfloat16)

    def name_of(kind, s):
        if s == 0:
            return ("core",)
        if s == stages - 1:
            return ("save",)
        if s == stages - 2:
            return ("core_back",)
        if s < SPLIT_BITS + 1:
            order = [("side",), ("line", 0), ("line", 1), ("line", 2)]
            order = order if kind == 0 else order[1:] + order[:1]
            return order[s - 1]
        if s < first_gather:
            return ("extra", s - SPLIT_BITS - 1)
        order = [("spread", 0), ("spread", 1), ("spread", 2), ("side_back",)]
        order = order if kind == 0 else order[3:] + order[:3]
        return order[s - first_gather]

    def start_stage(c, kind, s):
        name = name_of(kind, s)
        if s == first_gather:
            whole[final(c, kind)] = acc[final(c, kind)]
        if name[0] == "core":
            core_copy(c).start()
        elif name[0] == "side":
            side_copy(c, kind).start()
        elif name[0] == "line":
            r = name[1]
            pl.when(place <= r)(lambda: line_copy(c, kind, r, 1).start())
            pl.when(place >= 3 - r)(lambda: line_copy(c, kind, r, 0).start())
        elif name[0] == "extra":
            extra_copy(c, kind, name[1]).start()
        elif name[0] == "spread":
            r = name[1]
            pl.when((place >= r) & (place <= 2))(lambda: spread_copy(c, kind, r, 1).start())
            pl.when((place >= 1) & (place <= 3 - r))(lambda: spread_copy(c, kind, r, 0).start())
        elif name[0] == "side_back":
            side_back_copy(c, kind).start()
        elif name[0] == "core_back":
            core_back_copy(c).start()
        else:
            save_copy(c).start()

    def finish_stage(c, kind, s):
        name = name_of(kind, s)
        if name[0] == "core":
            core_copy(c).wait()
            add_groups(low_core(c), 8, c, 0)
        elif name[0] == "side":
            side_copy(c, kind).wait()
            if kind == 0:
                add_groups(low_side(c), 4, c, 8)
            else:
                add_groups(final(c, kind), 1, c, 8)
        elif name[0] == "line":
            r = name[1]

            @pl.when(place <= r)
            def _():
                line_copy(c, kind, r, 1).wait_send()

            @pl.when(place >= 3 - r)
            def _():
                line_copy(c, kind, r, 0).wait_send()

            @pl.when((place >= 1) & (place <= r + 1))
            def _():
                line_copy(c, kind, r, 1).wait_recv()
                add_groups(block_start(c, kind, 2 - r + place), 1 + kind, c, 12 + 2 * (2 * r + 1))

            @pl.when((place <= 2) & (place >= 2 - r))
            def _():
                line_copy(c, kind, r, 0).wait_recv()
                add_groups(block_start(c, kind, r - 2 + place), 1 + kind, c, 12 + 2 * (2 * r))

        elif name[0] == "extra":
            extra_copy(c, kind, name[1]).wait()
            add_groups(final(c, kind), 1, c, 24 + name[1])
        elif name[0] == "spread":
            r = name[1]
            pl.when((place >= r) & (place <= 2))(lambda: spread_copy(c, kind, r, 1).wait_send())
            pl.when((place >= 1) & (place <= 3 - r))(lambda: spread_copy(c, kind, r, 0).wait_send())
            pl.when(place >= r + 1)(lambda: spread_copy(c, kind, r, 1).wait_recv())
            pl.when(place <= 2 - r)(lambda: spread_copy(c, kind, r, 0).wait_recv())
        elif name[0] == "side_back":
            side_back_copy(c, kind).wait()
        elif name[0] == "core_back":
            core_back_copy(c).wait()
        else:
            save_copy(c).wait()

    def small_copy(k):
        return pltpu.make_async_remote_copy(
            src_ref=small_acc.at[k],
            dst_ref=small_recv.at[k],
            send_sem=small_send_sem.at[k],
            recv_sem=small_recv_sem.at[k],
            device_id=bit_mate(k),
            device_id_type=MESH,
        )

    small_acc[0] = small_ref[...]

    def multiply(c):
        block, part = c // per_block, lax.rem(c, per_block)
        a_col = jnp.minimum(block, wide) + jnp.minimum(block // (2 * wide), 1) + jnp.minimum(block // (2 * wide + 1), 1)
        b_col = jnp.maximum(block - wide + 1, 0)
        lines = CHUNK_GROUPS * GROUP
        left = a_ref[:, pl.ds(pl.multiple_of(a_col * width + part * lines, lines), lines)]
        right = b_ref[:, pl.ds(pl.multiple_of(b_col * width, width), width)]
        grad = lax.dot_general(left, right, (((0,), (0,)), ((), ())), preferred_element_type=jnp.float32)
        acc[pl.ds(c * CHUNK_GROUPS, CHUNK_GROUPS)] = grad.astype(jnp.bfloat16).reshape(
            CHUNK_GROUPS, GROUP, width
        )

    for kind, block in order[:2]:
        kind(block).wait()
    multiply(0)
    pl.semaphore_wait(barrier, bits + 2)

    def step(t, phase):
        for s in range(stages, 0, -1):
            c = t - LAG * s
            kind = (phase - LAG * s) % CYCLE // 2

            @pl.when((c >= 0) & (c < chunks))
            def _():
                finish_stage(c, kind, s - 1)
                if s < stages:
                    start_stage(c, kind, s)

        @pl.when(t == per_block - 1)
        def _():
            for kind, block in order[2:]:
                kind(block).wait()

        @pl.when(t < chunks)
        def _():
            core_copy(t).start()

        @pl.when(t + 1 < chunks)
        def _():
            multiply(t + 1)

        for k in range(bits + 1):

            @pl.when(t == LAG * k)
            def _():
                if k > 0:
                    small_copy(k - 1).wait()
                    small_acc[k] = small_acc[k - 1] + small_recv[k - 1]
                if k < bits:
                    small_copy(k).start()

    def cycle(n, carry):
        for phase in range(CYCLE):
            step(n * CYCLE + phase, phase)
        return carry

    lax.fori_loop(0, pl.cdiv(chunks + LAG * stages, CYCLE), cycle, 0)
    small_out[...] = small_acc[bits]


def reduced(a_side, b_side, small, count):
    rows = a_side.shape[0]
    width = small.shape[1]
    bits = count.bit_length() - 1
    extra = bits - SPLIT_BITS
    blocks = 2 * (a_side.shape[1] // width - 3) + 4
    chunks = blocks * width // (CHUNK_GROUPS * GROUP)
    groups = chunks * CHUNK_GROUPS
    loads = (a_side.shape[1] + b_side.shape[1]) // width
    return pl.pallas_call(
        functools.partial(reduce_kernel, bits, chunks),
        out_shape=(
            jax.ShapeDtypeStruct((groups, GROUP, width), jnp.bfloat16),
            jax.ShapeDtypeStruct(small.shape, jnp.float32),
        ),
        in_specs=[
            pl.BlockSpec(memory_space=pl.ANY),
            pl.BlockSpec(memory_space=pl.ANY),
            pl.BlockSpec(memory_space=pltpu.VMEM),
        ],
        out_specs=(pl.BlockSpec(memory_space=pl.ANY), pl.BlockSpec(memory_space=pltpu.VMEM)),
        scratch_shapes=[
            pltpu.VMEM(a_side.shape, jnp.bfloat16),
            pltpu.VMEM(b_side.shape, jnp.bfloat16),
            pltpu.VMEM((groups, GROUP, width), jnp.bfloat16),
            pltpu.VMEM((groups, GROUP, width), jnp.bfloat16),
            pltpu.VMEM((SLOTS, SLOT_GROUPS + extra, GROUP, width), jnp.bfloat16),
            pltpu.VMEM((bits + 1,) + small.shape, jnp.float32),
            pltpu.VMEM((bits,) + small.shape, jnp.float32),
            pltpu.SemaphoreType.DMA((loads,)),
            pltpu.SemaphoreType.DMA((SLOTS, 16 + extra)),
            pltpu.SemaphoreType.DMA((SLOTS, 16 + extra)),
            pltpu.SemaphoreType.DMA((SLOTS,)),
            pltpu.SemaphoreType.DMA((bits,)),
            pltpu.SemaphoreType.DMA((bits,)),
        ],
        compiler_params=pltpu.CompilerParams(
            collective_id=1, has_side_effects=True, vmem_limit_bytes=VMEM_LIMIT
        ),
        cost_estimate=pl.CostEstimate(
            flops=2 * rows * blocks * width * width, bytes_accessed=80_000_000, transcendentals=0
        ),
    )(a_side, b_side, small)


PIECE = 384
DEPTH = 4


def spread_kernel(sum_hbm, small_ref, states_hbm, grads_hbm, *refs):
    width = small_ref.shape[1]
    (o_wq, o_bq, o_wk, o_wv, o_bv, o_wo, o_bo, o_g1, o_s1, o_up, o_bu, o_dn, o_bd, o_g2, o_s2) = refs[2:17]
    states_out, grads_out = refs[:2]
    taken, given, held, in_sem, out_sem, held_sem = refs[17:]
    wide = o_bu.shape[1] // width
    targets = []
    for j in range(wide):
        targets += [o_dn.at[0, pl.ds(j * width + r, PIECE), :] for r in range(0, width, PIECE)]
    for j in range(wide):
        targets += [o_up.at[0, pl.ds(r, PIECE), pl.ds(j * width, width)] for r in range(0, width, PIECE)]
    for ref in (o_wo, o_wq, o_wk, o_wv):
        targets += [ref.at[0, pl.ds(r, PIECE), :] for r in range(0, width, PIECE)]

    items = states_hbm.shape[1]
    passes = [(states_hbm.at[0, i], states_out.at[0, i]) for i in range(items)]
    passes += [(grads_hbm.at[0, i], grads_out.at[0, i]) for i in range(items)]

    def pass_in(i):
        return pltpu.make_async_copy(passes[i][0], held.at[i], held_sem.at[i])

    def pass_out(i):
        return pltpu.make_async_copy(held.at[i], passes[i][1], held_sem.at[i])

    def load(i):
        return pltpu.make_async_copy(
            sum_hbm.at[pl.ds(i * PIECE, PIECE)], taken.at[i % DEPTH], in_sem.at[i % DEPTH]
        )

    def store(i):
        return pltpu.make_async_copy(given.at[i % DEPTH], targets[i], out_sem.at[i % DEPTH])

    for i in range(DEPTH):
        load(i).start()
    for i in range(len(passes)):
        pass_in(i).start()
    singles = [o_bq, o_bv, o_bo, o_g1, o_s1, o_bd, o_g2, o_s2]
    for i, ref in enumerate(singles):
        ref[...] = small_ref[pl.ds(i, 1), :]
    for j in range(wide):
        o_bu[:, pl.ds(j * width, width)] = small_ref[pl.ds(len(singles) + j, 1), :]
    for i in range(len(targets)):
        load(i).wait()
        if i >= DEPTH:
            store(i - DEPTH).wait()

        def convert(r, carry):
            rows = pl.ds(pl.multiple_of(r * 64, 64), 64)
            given[i % DEPTH, rows, :] = taken[i % DEPTH, rows, :].astype(jnp.float32)
            return carry

        lax.fori_loop(0, PIECE // 64, convert, 0)
        store(i).start()
        if i + DEPTH < len(targets):
            load(i + DEPTH).start()
        if i < len(passes):
            pass_in(i).wait()
            pass_out(i).start()
    for i in range(len(targets) - DEPTH, len(targets)):
        store(i).wait()
    for i in range(len(passes)):
        pass_out(i).wait()


def spread(sums, small, states, input_grads, params):
    width = small.shape[1]
    anywhere = pl.BlockSpec(memory_space=pl.ANY)
    local = pl.BlockSpec(memory_space=pltpu.VMEM)
    return pl.pallas_call(
        spread_kernel,
        out_shape=(
            jax.ShapeDtypeStruct(states.shape, states.dtype),
            jax.ShapeDtypeStruct(input_grads.shape, input_grads.dtype),
        )
        + tuple(jax.ShapeDtypeStruct(member.shape, jnp.float32) for member in params),
        in_specs=[anywhere, local, anywhere, anywhere],
        out_specs=(anywhere, anywhere)
        + tuple(anywhere if len(member.shape) == 3 else local for member in params),
        scratch_shapes=[
            pltpu.VMEM((DEPTH, PIECE, width), jnp.bfloat16),
            pltpu.VMEM((DEPTH, PIECE, width), jnp.float32),
            pltpu.VMEM((2 * states.shape[1],) + states.shape[2:], states.dtype),
            pltpu.SemaphoreType.DMA((DEPTH,)),
            pltpu.SemaphoreType.DMA((DEPTH,)),
            pltpu.SemaphoreType.DMA((2 * states.shape[1],)),
        ],
        compiler_params=pltpu.CompilerParams(vmem_limit_bytes=VMEM_LIMIT),
        cost_estimate=pl.CostEstimate(
            flops=12 * width * width, bytes_accessed=80 * width * width, transcendentals=0
        ),
    )(sums, small, states, input_grads)


HALF_LOG = -0.5 / math.log(2.0)
BELL_SCALE = 1.0 / math.sqrt(2.0 * math.pi)
SINGLES = ("bq", "bv", "bo", "g1", "s1", "bd", "g2", "s2")


def product(left, right):
    return lax.dot_general(left, right, (((1,), (0,)), ((), ())), preferred_element_type=jnp.float32)


def product_t(left, right):
    return lax.dot_general(left, right, (((1,), (1,)), ((), ())), preferred_element_type=jnp.float32)


def gelu_pair(z):
    cdf = 0.5 * lax.erf(z * (1.0 / math.sqrt(2.0))) + 0.5
    bell = jnp.exp2(z * z * HALF_LOG)
    return z * cdf, z * BELL_SCALE * bell + cdf


def normed(values):
    average = jnp.mean(values, axis=-1, keepdims=True)
    centered = values - average
    inverse = lax.rsqrt(jnp.mean(centered * centered, axis=-1, keepdims=True) + EPSILON)
    return centered * inverse, inverse


def normed_back(grad, normal, inverse):
    first_mean = jnp.mean(grad, axis=-1, keepdims=True)
    second_mean = jnp.mean(grad * normal, axis=-1, keepdims=True)
    return inverse * (grad - first_mean - normal * second_mean)


def layer_kernel(
    ids_ref,
    lengths_ref,
    captions_hbm,
    regions_ref,
    cotangent_hbm,
    wq_hbm,
    bq_ref,
    wk_hbm,
    wv_hbm,
    bv_ref,
    wo_hbm,
    bo_ref,
    g1_ref,
    s1_ref,
    wu_hbm,
    bu_ref,
    wd_hbm,
    bd_ref,
    g2_ref,
    s2_ref,
    states_hbm,
    grads_hbm,
    a_hbm,
    b_hbm,
    small_ref,
    wqkv,
    wo,
    wu,
    wd,
    wqkv_t,
    wo_t,
    wu_t,
    wd_t,
    table,
    hidden,
    upstream,
    query,
    keys,
    values,
    probs,
    context,
    normal1,
    normal2,
    lowered,
    active,
    slope,
    result,
    staged,
    inverse1,
    inverse2,
    wide1,
    wide2,
    caption_cells,
    weight_sem,
    table_send,
    table_recv,
    fwd_send,
    fwd_recv,
    back_send,
    back_recv,
    out_sem,
):
    items, rows, width = hidden.shape
    held = regions_ref.shape[0]
    cap_rows = captions_hbm.shape[1]
    wide = wu.shape[1] // width
    pairs = HEADS // 2
    pair_width = width // pairs
    head = width // HEADS
    section = lax.axis_index("section")
    batch = lax.axis_index("batch")
    count = lax.axis_size("batch")
    right = (section, lax.rem(batch + 1, count))
    left = (section, lax.rem(batch + count - 1, count))
    other = (1 - section, batch)

    weight_copies = [
        pltpu.make_async_copy(source.at[0], target, weight_sem.at[n])
        for n, (source, target) in enumerate(
            (
                (wq_hbm, wqkv.at[:, pl.ds(0, width)]),
                (wk_hbm, wqkv.at[:, pl.ds(width, width)]),
                (wv_hbm, wqkv.at[:, pl.ds(2 * width, width)]),
                (wo_hbm, wo),
                (wu_hbm, wu),
                (wd_hbm, wd),
            )
        )
    ]
    for copy in weight_copies[:3]:
        copy.start()
    cotangent_copy = pltpu.make_async_copy(cotangent_hbm, upstream, weight_sem.at[6])

    barrier = pltpu.get_barrier_semaphore()
    for peer in (right, left, other):
        pl.semaphore_signal(barrier, inc=1, device_id=peer, device_id_type=MESH)
    pl.semaphore_wait(barrier, 3)

    def table_copy(n, peer):
        return pltpu.make_async_remote_copy(
            src_ref=regions_ref,
            dst_ref=table.at[pl.ds(2 * n * held, held)],
            send_sem=table_send.at[n],
            recv_sem=table_recv.at[n],
            device_id=peer,
            device_id_type=MESH,
        )

    @pl.when(section == 0)
    def _():
        pltpu.make_async_copy(captions_hbm.at[0], caption_cells, weight_sem.at[7]).start()
        table_copy(0, right).start()
        table_copy(1, left).start()
        table[pl.ds(held, held)] = regions_ref[...]
        table_copy(0, right).wait()
        table_copy(1, left).wait()

    for copy in weight_copies[3:]:
        copy.start()

    @pl.when(section == 1)
    def _():
        cotangent_copy.start()

    def forward_copy(i):
        return pltpu.make_async_remote_copy(
            src_ref=result.at[i],
            dst_ref=hidden.at[i],
            send_sem=fwd_send.at[i],
            recv_sem=fwd_recv.at[i],
            device_id=other,
            device_id_type=MESH,
        )

    def back_copy(i):
        return pltpu.make_async_remote_copy(
            src_ref=result.at[i],
            dst_ref=upstream.at[i],
            send_sem=back_send.at[i],
            recv_sem=back_recv.at[i],
            device_id=other,
            device_id_type=MESH,
        )

    def save(i, n):
        at = pl.ds(pl.multiple_of(i * rows, rows), rows)
        first = wide * width
        turn = lax.rem(i, 2)
        if n == 0:
            source, target = active.at[turn], a_hbm.at[at, pl.ds(0, first)]
        elif n == 1:
            source, target = lowered.at[turn], a_hbm.at[at, pl.ds(first, width)]
        elif n == 2:
            source, target = context.at[turn], a_hbm.at[at, pl.ds(first + width, width)]
        elif n == 3:
            source, target = hidden.at[i], a_hbm.at[at, pl.ds(first + 2 * width, width)]
        else:
            source, target = result.at[i], states_hbm.at[0, i]
        return pltpu.make_async_copy(source, target, out_sem.at[i, n])

    def staged_save(i):
        at = pl.ds(pl.multiple_of(i * rows, rows), rows)
        return pltpu.make_async_copy(staged.at[lax.rem(i, 2)], b_hbm.at[at], out_sem.at[i, 5])

    def grad_save(i):
        return pltpu.make_async_copy(result.at[i], grads_hbm.at[0, i], out_sem.at[i, 6])

    def vector(ref, j=0):
        return ref[:, j * width : (j + 1) * width].astype(jnp.float32)

    lane = lax.broadcasted_iota(jnp.int32, (rows, pair_width), 1)

    blocks = [slice(r, r + GROUP) for r in range(0, rows, GROUP)]
    spans = [slice(c, min(c + 128, rows)) for c in range(0, rows, 128)]

    def only(block, h):
        return jnp.where((lane // head) == h, block, jnp.zeros_like(block))

    def caption_copy(i):
        return pltpu.make_async_copy(captions_hbm.at[i], caption_cells, weight_sem.at[7])

    def assemble(i):
        total = count * held
        spot = jnp.minimum(lax.rem(ids_ref[i] - (batch - 1) * held + total, total), 3 * held - 1)
        caption_copy(i).wait()
        whole = jnp.concatenate(
            [caption_cells[...].astype(jnp.float32), table[spot].astype(jnp.float32)], axis=0
        )
        hidden[i] = whole.astype(jnp.bfloat16)

        @pl.when(i + 1 < items)
        def _():
            caption_copy(i + 1).start()

    def forward(i):
        @pl.when((i == 0) & (section == 0))
        def _():
            for copy in weight_copies[:3]:
                copy.wait()

        turn = lax.rem(i, 2)
        source = hidden[i]
        mixed = product(source, wqkv[...])
        for at in blocks:
            scaled = (mixed[at, :width] + vector(bq_ref)) * (1.0 / math.sqrt(head))
            query[i, at, :] = scaled.astype(jnp.bfloat16)
            keys[i, at, :] = mixed[at, width : 2 * width].astype(jnp.bfloat16)
            values[i, at, :] = (mixed[at, 2 * width :] + vector(bv_ref)).astype(jnp.bfloat16)
        position = lax.broadcasted_iota(jnp.int32, (rows, 1), 0)
        live = (position >= cap_rows) | (position < lengths_ref[i])
        key_bias = jnp.where(live, 0.0, -1000000000.0)

        def lanes_of(p):
            return slice(p * pair_width, (p + 1) * pair_width)

        def scored(p):
            k_pair = keys[i, :, lanes_of(p)]
            stacked = jnp.concatenate([only(k_pair, 0), only(k_pair, 1)], axis=0)
            v_turned = values[i, :, lanes_of(p)].astype(jnp.float32).T.astype(jnp.bfloat16)
            return product_t(stacked, query[i, :, lanes_of(p)]), v_turned

        def weighed(p, both):
            for h in range(2):
                for span in spans:
                    scores = both[h * rows : (h + 1) * rows, span] + key_bias
                    expo = jnp.exp(scores - jnp.max(scores, axis=0, keepdims=True))
                    share = pltpu.reciprocal(jnp.sum(expo, axis=0, keepdims=True), approx=True)
                    probs[i, 2 * p + h, :, span] = (expo * share).astype(jnp.bfloat16)

        def mixed_values(p, v_turned):
            return [product(v_turned[h * head : (h + 1) * head], probs[i, 2 * p + h]) for h in range(2)]

        def place_context(p, parts):
            context[turn, :, lanes_of(p)] = jnp.concatenate(parts, axis=0).T.astype(jnp.bfloat16)

        ahead = scored(0)
        parts = None
        for p in range(pairs):
            both, v_turned = ahead
            if p + 1 < pairs:
                ahead = scored(p + 1)
            if parts is not None:
                place_context(p - 1, parts)
            weighed(p, both)
            parts = mixed_values(p, v_turned)
        place_context(pairs - 1, parts)

        @pl.when((i == 0) & (section == 0))
        def _():
            for copy in weight_copies[3:]:
                copy.wait()

        attended = product(context[turn], wo[...])
        for at in blocks:
            n1, inv1 = normed(hidden[i, at, :].astype(jnp.float32) + attended[at] + vector(bo_ref))
            normal1[i, at, :] = n1.astype(jnp.bfloat16)
            inverse1[i, at, :] = inv1
            first = n1 * vector(g1_ref) + vector(s1_ref)
            lowered[turn, at, :] = first.astype(jnp.bfloat16)
            wide1[at, :] = first + vector(bd_ref)
        half = wide * width // 2

        def raised(n):
            return product(lowered[turn], wu[:, n * half : (n + 1) * half])

        def bend(n, z_tile):
            for part in range(0, half, width):
                lanes = slice(n * half + part, n * half + part + width)
                bias = bu_ref[:, lanes].astype(jnp.float32)
                for at in blocks:
                    gelu, slant = gelu_pair(z_tile[at, part : part + width] + bias)
                    active[turn, at, lanes] = gelu.astype(jnp.bfloat16)
                    slope[i, at, lanes] = slant.astype(jnp.bfloat16)

        z_first = raised(0)
        z_second = raised(1)
        bend(0, z_first)
        wide1[...] += product(active[turn, :, :half], wd[:half, :])
        bend(1, z_second)
        lowest = product(active[turn, :, half:], wd[half:, :])
        for at in blocks:
            n2, inv2 = normed(wide1[at, :] + lowest[at])
            normal2[i, at, :] = n2.astype(jnp.bfloat16)
            inverse2[i, at, :] = inv2
            result[i, at, :] = (n2 * vector(g2_ref) + vector(s2_ref)).astype(jnp.bfloat16)

    def folded(value):
        return value[: GROUP // 2] + value[GROUP // 2 :]

    def keep_small(row, value):
        small_ref[row : row + 1, :] += jnp.sum(value, axis=0, keepdims=True)

    def single(name, value):
        keep_small(SINGLES.index(name), value)

    def backward(i):
        slot = lax.rem(i, 2)
        base = (2 + wide) * width

        def stage(at, column, value):
            staged[slot, at, column * width : (column + 1) * width] = value

        def norm_step(at, gradient, normal, inverse, gain, sums):
            n = normal[i, at, :].astype(jnp.float32)
            d_res = normed_back(gradient * vector(gain), n, inverse[i, at, :])
            d_low = d_res.astype(jnp.bfloat16)
            terms = [folded(gradient * n), folded(gradient), folded(d_low.astype(jnp.float32))]
            return d_res, d_low, terms if sums is None else [a + b for a, b in zip(sums, terms)]

        sums = None
        for at in blocks:
            gradient = upstream[i, at, :].astype(jnp.float32)
            d_res, d_low, sums = norm_step(at, gradient, normal2, inverse2, g2_ref, sums)
            wide1[at, :] = d_res
            stage(at, 0, d_low)
        for name, value in zip(("g2", "s2", "bd"), sums):
            single(name, value)
        d_out = staged[slot, :, :width]
        half = wide * width // 2
        for n in range(2):
            d_active = product(d_out, wd_t[:, n * half : (n + 1) * half])
            for part in range(0, half, width):
                j = (n * half + part) // width
                lanes = slice(j * width, (j + 1) * width)
                total = None
                for at in blocks:
                    d_inner = d_active[at, part : part + width] * slope[i, at, lanes].astype(jnp.float32)
                    d_inner = d_inner.astype(jnp.bfloat16)
                    stage(at, 1 + j, d_inner)
                    term = folded(d_inner.astype(jnp.float32))
                    total = term if total is None else total + term
                keep_small(len(SINGLES) + j, total)
        d_deep = product(staged[slot, :, width : (1 + wide) * width], wu_t[...])
        sums = None
        for at in blocks:
            d_res, d_low, sums = norm_step(at, wide1[at, :] + d_deep[at], normal1, inverse1, g1_ref, sums)
            wide2[at, :] = d_res
            stage(at, 1 + wide, d_low)
        for name, value in zip(("g1", "s1", "bo"), sums):
            single(name, value)
        d_att = staged[slot, :, (1 + wide) * width : (2 + wide) * width]
        @pl.when((section == 0) & (i == 0))
        def _():
            save(items - 2, 0).wait()
            save(items - 1, 0).wait()

        pl.when(section == 1)(lambda: save(i, 0).wait())

        active[0, :, :width] = product(d_att, wo_t[...]).astype(jnp.bfloat16)

        def lanes_of(p):
            return slice(p * pair_width, (p + 1) * pair_width)

        def place_grad(n, p, block):
            at = base + n * width + p * pair_width
            staged[slot, :, at : at + pair_width] = block.astype(jnp.bfloat16)

        def opened(p):
            v_pair = values[i, :, lanes_of(p)]
            c_pair = active[0, :, lanes_of(p)]
            stacked = jnp.concatenate([only(v_pair, 0), only(v_pair, 1)], axis=0)
            k_turned = keys[i, :, lanes_of(p)].astype(jnp.float32).T.astype(jnp.bfloat16)
            d_value = product(probs[i, 2 * p], only(c_pair, 0))
            d_value += product(probs[i, 2 * p + 1], only(c_pair, 1))
            return product_t(stacked, c_pair), k_turned, d_value

        def score_base(p, h):
            return (2 * (p % 2) + h) * 2 * 128

        def score_grads(p, both):
            for h in range(2):
                for span in spans:
                    prob = probs[i, 2 * p + h, :, span].astype(jnp.float32)
                    d_prob = both[h * rows : (h + 1) * rows, span]
                    drift = jnp.sum(d_prob * prob, axis=0, keepdims=True)
                    at = score_base(p, h)
                    active[1, :, at + span.start : at + span.stop] = (prob * (d_prob - drift)).astype(jnp.bfloat16)
            return [active[1, :, score_base(p, h) : score_base(p, h) + rows] for h in range(2)]

        def closed(p, found, k_turned):
            q_pair = query[i, :, lanes_of(p)]
            d_key = product(found[0], only(q_pair, 0)) + product(found[1], only(q_pair, 1))
            return d_key, [product(k_turned[h * head : (h + 1) * head], found[h]) for h in range(2)]

        def place_grads(p, d_value, d_key, parts):
            place_grad(0, p, jnp.concatenate(parts, axis=0).T * (1.0 / math.sqrt(head)))
            place_grad(1, p, d_key)
            place_grad(2, p, d_value)

        ahead = opened(0)
        waiting = None
        for p in range(pairs):
            both, k_turned, d_value = ahead
            if p + 1 < pairs:
                ahead = opened(p + 1)
            if waiting is not None:
                place_grads(*waiting)
            found = score_grads(p, both)
            d_key, parts = closed(p, found, k_turned)
            waiting = (p, d_value, d_key, parts)
        place_grads(*waiting)
        d_source = product(staged[slot, :, base : base + 3 * width], wqkv_t[...])
        sums = None
        for at in blocks:
            result[i, at, :] = (wide2[at, :] + d_source[at]).astype(jnp.bfloat16)
            terms = [
                folded(staged[slot, at, base : base + width].astype(jnp.float32)),
                folded(staged[slot, at, base + 2 * width : base + 3 * width].astype(jnp.float32)),
            ]
            sums = terms if sums is None else [a + b for a, b in zip(sums, terms)]
        single("bq", sums[0])
        single("bv", sums[1])

    small_ref[...] = jnp.zeros_like(small_ref)
    side = 256
    unit = lax.broadcasted_iota(jnp.int32, (side, side), 0) == lax.broadcasted_iota(jnp.int32, (side, side), 1)
    unit = jnp.where(unit, 1.0, 0.0).astype(jnp.bfloat16)

    def turn_weights():
        for natural, turned in ((wqkv, wqkv_t), (wo, wo_t), (wu, wu_t), (wd, wd_t)):
            for block in range(0, natural.shape[0], width):

                def one(n, carry):
                    at = pl.ds(pl.multiple_of(n * side, side), side)
                    tall = product_t(unit, natural[block : block + width, at])
                    turned[at, block : block + width] = tall.astype(jnp.bfloat16)
                    return carry

                lax.fori_loop(0, natural.shape[1] // side, one, 0)

    @pl.when(section == 1)
    def _():
        for copy in weight_copies:
            copy.wait()
        cotangent_copy.wait()

    def forward_step(i):
        @pl.when(section == 0)
        def _():
            assemble(i)

        @pl.when(section == 1)
        def _():
            forward_copy(i).wait_recv()

        @pl.when(i >= 2)
        def _():
            for n in range(1, 3):
                save(i - 2, n).wait()
            pl.when(section == 0)(lambda: save(i - 2, 0).wait())

        forward(i)

        @pl.when(section == 0)
        def _():
            forward_copy(i).start()

        for n in range(5):
            save(i, n).start()

    def backward_step(i):
        @pl.when(section == 0)
        def _():
            back_copy(i).wait_recv()

        @pl.when(i >= 2)
        def _():
            staged_save(i - 2).wait()

        save(i, 4).wait()

        @pl.when(section == 0)
        def _():
            forward_copy(i).wait_send()

        backward(i)

        @pl.when(section == 1)
        def _():
            back_copy(i).start()

        staged_save(i).start()
        grad_save(i).start()

    def one_step(n, carry):
        @pl.when(n == items * (1 - section))
        def _():
            turn_weights()

        goes_back = (1 - section) * (n // items) + section * lax.rem(n, 2)
        i = (1 - section) * lax.rem(n, items) + section * (n // 2)
        pl.when(goes_back == 0)(lambda: forward_step(i))
        pl.when(goes_back == 1)(lambda: backward_step(i))
        return carry

    lax.fori_loop(0, 2 * items, one_step, 0)

    def finish(i, carry):
        save(i, 3).wait()
        grad_save(i).wait()

        @pl.when(i >= items - 2)
        def _():
            staged_save(i).wait()
            for n in range(1, 3):
                save(i, n).wait()

        @pl.when(section == 1)
        def _():
            back_copy(i).wait_send()

        return carry

    lax.fori_loop(0, items, finish, 0)


def layered(image_ids, caption_lengths, captions, regions, cotangent, stacked):
    items, cap_rows, width = captions.shape
    held, region_rows, _ = regions.shape
    rows = cap_rows + region_rows
    inner = stacked[9].shape[2]
    low = jnp.bfloat16
    wide = inner // width

    def cells(*shape):
        return pltpu.VMEM(shape, low)

    anywhere = pl.BlockSpec(memory_space=pl.ANY)
    local = pl.BlockSpec(memory_space=pltpu.VMEM)
    scalars = pl.BlockSpec(memory_space=pltpu.SMEM)
    return pl.pallas_call(
        layer_kernel,
        out_shape=(
            jax.ShapeDtypeStruct((1, items, rows, width), low),
            jax.ShapeDtypeStruct((1, items, rows, width), low),
            jax.ShapeDtypeStruct((items * rows, (3 + wide) * width), low),
            jax.ShapeDtypeStruct((items * rows, (5 + wide) * width), low),
            jax.ShapeDtypeStruct((GROUP, width), jnp.float32),
        ),
        in_specs=[scalars, scalars, anywhere, local, anywhere]
        + [anywhere if len(member.shape) == 3 else local for member in stacked],
        out_specs=(anywhere, anywhere, anywhere, anywhere, local),
        scratch_shapes=[
            cells(width, 3 * width),
            cells(width, width),
            cells(width, inner),
            cells(inner, width),
            cells(3 * width, width),
            cells(width, width),
            cells(inner, width),
            cells(width, inner),
            cells(3 * held, region_rows, width),
            cells(items, rows, width),
            cells(items, rows, width),
            cells(items, rows, width),
            cells(items, rows, width),
            cells(items, rows, width),
            cells(items, HEADS, rows, rows),
            cells(2, rows, width),
            cells(items, rows, width),
            cells(items, rows, width),
            cells(2, rows, width),
            cells(2, rows, inner),
            cells(items, rows, inner),
            cells(items, rows, width),
            cells(2, rows, (5 + wide) * width),
            pltpu.VMEM((items, rows, 1), jnp.float32),
            pltpu.VMEM((items, rows, 1), jnp.float32),
            pltpu.VMEM((rows, width), jnp.float32),
            pltpu.VMEM((rows, width), jnp.float32),
            cells(cap_rows, width),
            pltpu.SemaphoreType.DMA((8,)),
            pltpu.SemaphoreType.DMA((2,)),
            pltpu.SemaphoreType.DMA((2,)),
            pltpu.SemaphoreType.DMA((items,)),
            pltpu.SemaphoreType.DMA((items,)),
            pltpu.SemaphoreType.DMA((items,)),
            pltpu.SemaphoreType.DMA((items,)),
            pltpu.SemaphoreType.DMA((items, 7)),
        ],
        compiler_params=pltpu.CompilerParams(
            collective_id=0, has_side_effects=True, vmem_limit_bytes=VMEM_LIMIT
        ),
        cost_estimate=pl.CostEstimate(
            flops=4 * items * rows * (4 + 2 * wide) * width * width,
            bytes_accessed=60_000_000,
            transcendentals=0,
        ),
    )(image_ids, caption_lengths, captions, regions, cotangent, *stacked)


def body(
    captions,
    regions,
    image_ids,
    caption_lengths,
    cotangent,
    query_weight,
    query_bias,
    key_weight,
    value_weight,
    value_bias,
    out_weight,
    out_bias,
    norm1_gain,
    norm1_bias,
    up_weight,
    up_bias,
    down_weight,
    down_bias,
    norm2_gain,
    norm2_bias,
):
    stacked = (
        query_weight,
        query_bias,
        key_weight,
        value_weight,
        value_bias,
        out_weight,
        out_bias,
        norm1_gain,
        norm1_bias,
        up_weight,
        up_bias,
        down_weight,
        down_bias,
        norm2_gain,
        norm2_bias,
    )
    width = captions.shape[2]
    states, input_grads, a_side, b_side, small = layered(
        image_ids, caption_lengths, captions, regions, cotangent, stacked
    )
    sums, small_sums = reduced(a_side, b_side, small, lax.axis_size("batch"))
    return tuple(spread(sums.reshape(-1, width), small_sums, states, input_grads, stacked))


def solution(mesh):
    placed = (
        P("batch", None, None),
        P("batch", None, None),
        P("batch"),
        P("batch"),
        P("batch", None, None),
        P("section", None, None),
        P("section", None),
        P("section", None, None),
        P("section", None, None),
        P("section", None),
        P("section", None, None),
        P("section", None),
        P("section", None),
        P("section", None),
        P("section", None, None),
        P("section", None),
        P("section", None, None),
        P("section", None),
        P("section", None),
        P("section", None),
    )
    return jax.shard_map(
        body,
        mesh=mesh,
        in_specs=placed,
        out_specs=(
            P("section", "batch", None, None),
            P("section", "batch", None, None),
            P("section", None, None),
            P("section", None),
            P("section", None, None),
            P("section", None, None),
            P("section", None),
            P("section", None, None),
            P("section", None),
            P("section", None),
            P("section", None),
            P("section", None, None),
            P("section", None),
            P("section", None, None),
            P("section", None),
            P("section", None),
            P("section", None),
        ),
        check_vma=False,
    )
```

```python
import functools
import math

import jax
import jax.numpy as jnp
from jax import lax
from jax.experimental import pallas as pl
from jax.experimental.pallas import tpu as pltpu
from jax.sharding import PartitionSpec as P

HEADS = 12
EPSILON = 1e-12
MESH = pl.DeviceIdType.MESH
VMEM_LIMIT = 63 * 1024 * 1024
GROUP = 16
CHUNK_GROUPS = 16
SLOTS = 18
SLOT_GROUPS = 24
LAG = 3
CYCLE = 3
LINE = 4
SPLIT_BITS = 4


def reduce_kernel(
    bits,
    chunks,
    a_hbm,
    b_hbm,
    small_ref,
    out_hbm,
    small_out,
    a_ref,
    b_ref,
    acc,
    whole,
    recv,
    small_acc,
    small_recv,
    load_sem,
    send_sem,
    recv_sem,
    save_sem,
    small_send_sem,
    small_recv_sem,
):
    width = acc.shape[2]
    extra = bits - SPLIT_BITS
    first_gather = SPLIT_BITS + 1 + extra
    stages = 2 * (SPLIT_BITS + 1) + extra + 1
    me = lax.axis_index("batch")
    section = lax.axis_index("section")
    core, side, place = me % 2, (me // 2) % 2, (me // 4) % LINE
    blocks_a = a_hbm.shape[1] // width
    blocks_b = b_hbm.shape[1] // width
    per_block = width // (CHUNK_GROUPS * GROUP)

    def load(source, target, block, base):
        lanes = pl.ds(block * width, width)
        return pltpu.make_async_copy(source.at[:, lanes], target.at[:, lanes], load_sem.at[base + block])

    def load_a(block):
        return load(a_hbm, a_ref, block, 0)

    def load_b(block):
        return load(b_hbm, b_ref, block, blocks_a)

    wide = blocks_a - 3
    first_use = {0: [(load_a, 0), (load_b, 0)]}
    for j in range(1, wide):
        first_use[j] = [(load_a, j)]
    first_use[wide] = [(load_a, wide), (load_b, 1)]
    for j in range(1, wide):
        first_use[wide + j] = [(load_b, 1 + j)]
    first_use[2 * wide] = [(load_a, wide + 1), (load_b, wide + 1)]
    first_use[2 * wide + 1] = [(load_a, wide + 2), (load_b, wide + 2)]
    first_use[2 * wide + 2] = [(load_b, wide + 3)]
    first_use[2 * wide + 3] = [(load_b, wide + 4)]
    for j in range(2 * wide + 4):
        for kind, block in first_use[j]:
            kind(block).start()

    def bit_mate(k):
        bit = (me // 2**k) % 2
        return (section, me + 2**k * (1 - 2 * bit))

    core_mate, side_mate = bit_mate(0), bit_mate(1)
    mates = ((section, me - LINE), (section, me + LINE))
    ring = [(section, me + LINE * ((place + d) % LINE - place)) for d in (LINE - 1, 1)]

    barrier = pltpu.get_barrier_semaphore()
    for peer in [core_mate, side_mate] + ring + [bit_mate(k) for k in range(2, bits)]:
        pl.semaphore_signal(barrier, inc=1, device_id=peer, device_id_type=MESH)
    pl.semaphore_wait(barrier, bits + 2)

    def low_core(c):
        return c * CHUNK_GROUPS + core * 8

    def low_side(c):
        return low_core(c) + side * 4

    def block_start(c, kind, b):
        return low_side(c) + b if kind == 0 else low_core(c) + 2 * b

    def final(c, kind):
        return low_side(c) + place if kind == 0 else low_core(c) + 2 * place + side

    def remote(c, source, start, size, target, spot, index, peer):
        return pltpu.make_async_remote_copy(
            src_ref=source.at[pl.ds(start, size)],
            dst_ref=target.at[lax.rem(c, SLOTS), pl.ds(spot, size)] if target is recv else target.at[pl.ds(start, size)],
            send_sem=send_sem.at[lax.rem(c, SLOTS), index],
            recv_sem=recv_sem.at[lax.rem(c, SLOTS), index],
            device_id=peer,
            device_id_type=MESH,
        )

    def core_copy(c):
        return remote(c, acc, c * CHUNK_GROUPS + (1 - core) * 8, 8, recv, 0, 0, core_mate)

    def side_copy(c, kind):
        if kind == 0:
            return remote(c, acc, low_core(c) + (1 - side) * 4, 4, recv, 8, 1, side_mate)
        return remote(c, acc, low_core(c) + 2 * place + (1 - side), 1, recv, 8, 1, side_mate)

    def line_copy(c, kind, r, d):
        size = 1 + kind
        b = jnp.minimum(3 - r + place, 3) if d == 1 else jnp.maximum(r - 3 + place, 0)
        spot = 12 + 2 * (2 * r + d)
        return remote(c, acc, block_start(c, kind, b), size, recv, spot, 2 + 2 * r + d, mates[d])

    def spread_copy(c, kind, r, d):
        size = 1 + kind
        b = jnp.maximum(place - r, 0) if d == 1 else jnp.minimum(place + r, 3)
        return remote(c, whole, block_start(c, kind, b), size, whole, 0, 8 + 2 * r + d, mates[d])

    def side_back_copy(c, kind):
        if kind == 0:
            return remote(c, whole, low_side(c), 4, whole, 0, 14, side_mate)
        return remote(c, whole, final(c, kind), 1, whole, 0, 14, side_mate)

    def core_back_copy(c):
        return remote(c, whole, low_core(c), 8, whole, 0, 15, core_mate)

    def extra_copy(c, kind, e):
        return remote(c, acc, final(c, kind), 1, recv, 24 + e, 16 + e, bit_mate(SPLIT_BITS + e))

    def save_copy(c):
        at = pl.ds(c * CHUNK_GROUPS, CHUNK_GROUPS)
        return pltpu.make_async_copy(whole.at[at], out_hbm.at[at], save_sem.at[lax.rem(c, SLOTS)])

    def add_groups(start, count, c, spot):
        slot = lax.rem(c, SLOTS)
        for g in range(count):
            total = acc[start + g].astype(jnp.float32) + recv[slot, spot + g].astype(jnp.float32)
            acc[start + g] = total.astype(jnp.bfloat16)

    def name_of(kind, s):
        if s == 0:
            return ("core",)
        if s == stages - 1:
            return ("save",)
        if s == stages - 2:
            return ("core_back",)
        if s < SPLIT_BITS + 1:
            order = [("side",), ("line", 0), ("line", 1), ("line", 2)]
            order = order if kind == 0 else order[1:] + order[:1]
            return order[s - 1]
        if s < first_gather:
            return ("extra", s - SPLIT_BITS - 1)
        order = [("spread", 0), ("spread", 1), ("spread", 2), ("side_back",)]
        order = order if kind == 0 else order[3:] + order[:3]
        return order[s - first_gather]

    def start_stage(c, kind, s):
        name = name_of(kind, s)
        if s == first_gather:
            whole[final(c, kind)] = acc[final(c, kind)]
        if name[0] == "core":
            core_copy(c).start()
        elif name[0] == "side":
            side_copy(c, kind).start()
        elif name[0] == "line":
            r = name[1]
            pl.when(place <= r)(lambda: line_copy(c, kind, r, 1).start())
            pl.when(place >= 3 - r)(lambda: line_copy(c, kind, r, 0).start())
        elif name[0] == "extra":
            extra_copy(c, kind, name[1]).start()
        elif name[0] == "spread":
            r = name[1]
            pl.when((place >= r) & (place <= 2))(lambda: spread_copy(c, kind, r, 1).start())
            pl.when((place >= 1) & (place <= 3 - r))(lambda: spread_copy(c, kind, r, 0).start())
        elif name[0] == "side_back":
            side_back_copy(c, kind).start()
        elif name[0] == "core_back":
            core_back_copy(c).start()
        else:
            save_copy(c).start()

    def finish_stage(c, kind, s):
        name = name_of(kind, s)
        if name[0] == "core":
            core_copy(c).wait()
            add_groups(low_core(c), 8, c, 0)
        elif name[0] == "side":
            side_copy(c, kind).wait()
            if kind == 0:
                add_groups(low_side(c), 4, c, 8)
            else:
                add_groups(final(c, kind), 1, c, 8)
        elif name[0] == "line":
            r = name[1]

            @pl.when(place <= r)
            def _():
                line_copy(c, kind, r, 1).wait_send()

            @pl.when(place >= 3 - r)
            def _():
                line_copy(c, kind, r, 0).wait_send()

            @pl.when((place >= 1) & (place <= r + 1))
            def _():
                line_copy(c, kind, r, 1).wait_recv()
                add_groups(block_start(c, kind, 2 - r + place), 1 + kind, c, 12 + 2 * (2 * r + 1))

            @pl.when((place <= 2) & (place >= 2 - r))
            def _():
                line_copy(c, kind, r, 0).wait_recv()
                add_groups(block_start(c, kind, r - 2 + place), 1 + kind, c, 12 + 2 * (2 * r))

        elif name[0] == "extra":
            extra_copy(c, kind, name[1]).wait()
            add_groups(final(c, kind), 1, c, 24 + name[1])
        elif name[0] == "spread":
            r = name[1]
            pl.when((place >= r) & (place <= 2))(lambda: spread_copy(c, kind, r, 1).wait_send())
            pl.when((place >= 1) & (place <= 3 - r))(lambda: spread_copy(c, kind, r, 0).wait_send())
            pl.when(place >= r + 1)(lambda: spread_copy(c, kind, r, 1).wait_recv())
            pl.when(place <= 2 - r)(lambda: spread_copy(c, kind, r, 0).wait_recv())
        elif name[0] == "side_back":
            side_back_copy(c, kind).wait()
        elif name[0] == "core_back":
            core_back_copy(c).wait()
        else:
            save_copy(c).wait()

    def small_copy(k):
        return pltpu.make_async_remote_copy(
            src_ref=small_acc.at[k],
            dst_ref=small_recv.at[k],
            send_sem=small_send_sem.at[k],
            recv_sem=small_recv_sem.at[k],
            device_id=bit_mate(k),
            device_id_type=MESH,
        )

    small_acc[0] = small_ref[...]

    def step(t, phase):
        for s in range(stages, 0, -1):
            c = t - LAG * s
            kind = (phase - LAG * s) % CYCLE // 2

            @pl.when((c >= 0) & (c < chunks))
            def _():
                finish_stage(c, kind, s - 1)
                if s < stages:
                    start_stage(c, kind, s)

        for j in range(2 * wide + 4):

            @pl.when(t == per_block * j)
            def _():
                for kind, block in first_use[j]:
                    kind(block).wait()

        @pl.when(t < chunks)
        def _():
            block, part = t // per_block, t % per_block
            a_col = jnp.minimum(block, wide) + jnp.minimum(block // (2 * wide), 1) + jnp.minimum(block // (2 * wide + 1), 1)
            b_col = jnp.maximum(block - wide + 1, 0)
            lines = CHUNK_GROUPS * GROUP
            left = a_ref[:, pl.ds(pl.multiple_of(a_col * width + part * lines, lines), lines)]
            right = b_ref[:, pl.ds(pl.multiple_of(b_col * width, width), width)]
            grad = lax.dot_general(left, right, (((0,), (0,)), ((), ())), preferred_element_type=jnp.float32)
            acc[pl.ds(t * CHUNK_GROUPS, CHUNK_GROUPS)] = grad.astype(jnp.bfloat16).reshape(
                CHUNK_GROUPS, GROUP, width
            )
            core_copy(t).start()

        for k in range(bits + 1):

            @pl.when(t == LAG * k)
            def _():
                if k > 0:
                    small_copy(k - 1).wait()
                    small_acc[k] = small_acc[k - 1] + small_recv[k - 1]
                if k < bits:
                    small_copy(k).start()

    def cycle(n, carry):
        for phase in range(CYCLE):
            step(n * CYCLE + phase, phase)
        return carry

    lax.fori_loop(0, pl.cdiv(chunks + LAG * stages, CYCLE), cycle, 0)
    small_out[...] = small_acc[bits]


def reduced(a_side, b_side, small, count):
    rows = a_side.shape[0]
    width = small.shape[1]
    bits = count.bit_length() - 1
    extra = bits - SPLIT_BITS
    blocks = 2 * (a_side.shape[1] // width - 3) + 4
    chunks = blocks * width // (CHUNK_GROUPS * GROUP)
    groups = chunks * CHUNK_GROUPS
    loads = (a_side.shape[1] + b_side.shape[1]) // width
    return pl.pallas_call(
        functools.partial(reduce_kernel, bits, chunks),
        out_shape=(
            jax.ShapeDtypeStruct((groups, GROUP, width), jnp.bfloat16),
            jax.ShapeDtypeStruct(small.shape, jnp.float32),
        ),
        in_specs=[
            pl.BlockSpec(memory_space=pl.ANY),
            pl.BlockSpec(memory_space=pl.ANY),
            pl.BlockSpec(memory_space=pltpu.VMEM),
        ],
        out_specs=(pl.BlockSpec(memory_space=pl.ANY), pl.BlockSpec(memory_space=pltpu.VMEM)),
        scratch_shapes=[
            pltpu.VMEM(a_side.shape, jnp.bfloat16),
            pltpu.VMEM(b_side.shape, jnp.bfloat16),
            pltpu.VMEM((groups, GROUP, width), jnp.bfloat16),
            pltpu.VMEM((groups, GROUP, width), jnp.bfloat16),
            pltpu.VMEM((SLOTS, SLOT_GROUPS + extra, GROUP, width), jnp.bfloat16),
            pltpu.VMEM((bits + 1,) + small.shape, jnp.float32),
            pltpu.VMEM((bits,) + small.shape, jnp.float32),
            pltpu.SemaphoreType.DMA((loads,)),
            pltpu.SemaphoreType.DMA((SLOTS, 16 + extra)),
            pltpu.SemaphoreType.DMA((SLOTS, 16 + extra)),
            pltpu.SemaphoreType.DMA((SLOTS,)),
            pltpu.SemaphoreType.DMA((bits,)),
            pltpu.SemaphoreType.DMA((bits,)),
        ],
        compiler_params=pltpu.CompilerParams(
            collective_id=1, has_side_effects=True, vmem_limit_bytes=VMEM_LIMIT
        ),
        cost_estimate=pl.CostEstimate(
            flops=2 * rows * blocks * width * width, bytes_accessed=80_000_000, transcendentals=0
        ),
    )(a_side, b_side, small)


PIECE = 384
DEPTH = 4


def spread_kernel(sum_hbm, small_ref, states_hbm, grads_hbm, *refs):
    width = small_ref.shape[1]
    (o_wq, o_bq, o_wk, o_wv, o_bv, o_wo, o_bo, o_g1, o_s1, o_up, o_bu, o_dn, o_bd, o_g2, o_s2) = refs[2:17]
    states_out, grads_out = refs[:2]
    taken, given, held, in_sem, out_sem, held_sem = refs[17:]
    wide = o_bu.shape[1] // width
    targets = []
    for j in range(wide):
        targets += [o_dn.at[0, pl.ds(j * width + r, PIECE), :] for r in range(0, width, PIECE)]
    for j in range(wide):
        targets += [o_up.at[0, pl.ds(r, PIECE), pl.ds(j * width, width)] for r in range(0, width, PIECE)]
    for ref in (o_wo, o_wq, o_wk, o_wv):
        targets += [ref.at[0, pl.ds(r, PIECE), :] for r in range(0, width, PIECE)]

    items = states_hbm.shape[1]
    passes = [(states_hbm.at[0, i], states_out.at[0, i]) for i in range(items)]
    passes += [(grads_hbm.at[0, i], grads_out.at[0, i]) for i in range(items)]

    def pass_in(i):
        return pltpu.make_async_copy(passes[i][0], held.at[i], held_sem.at[i])

    def pass_out(i):
        return pltpu.make_async_copy(held.at[i], passes[i][1], held_sem.at[i])

    def load(i):
        return pltpu.make_async_copy(
            sum_hbm.at[pl.ds(i * PIECE, PIECE)], taken.at[i % DEPTH], in_sem.at[i % DEPTH]
        )

    def store(i):
        return pltpu.make_async_copy(given.at[i % DEPTH], targets[i], out_sem.at[i % DEPTH])

    for i in range(DEPTH):
        load(i).start()
    for i in range(len(passes)):
        pass_in(i).start()
    singles = [o_bq, o_bv, o_bo, o_g1, o_s1, o_bd, o_g2, o_s2]
    for i, ref in enumerate(singles):
        ref[...] = small_ref[pl.ds(i, 1), :]
    for j in range(wide):
        o_bu[:, pl.ds(j * width, width)] = small_ref[pl.ds(len(singles) + j, 1), :]
    for i in range(len(targets)):
        load(i).wait()
        if i >= DEPTH:
            store(i - DEPTH).wait()

        def convert(r, carry):
            rows = pl.ds(pl.multiple_of(r * 64, 64), 64)
            given[i % DEPTH, rows, :] = taken[i % DEPTH, rows, :].astype(jnp.float32)
            return carry

        lax.fori_loop(0, PIECE // 64, convert, 0)
        store(i).start()
        if i + DEPTH < len(targets):
            load(i + DEPTH).start()
        if i < len(passes):
            pass_in(i).wait()
            pass_out(i).start()
    for i in range(len(targets) - DEPTH, len(targets)):
        store(i).wait()
    for i in range(len(passes)):
        pass_out(i).wait()


def spread(sums, small, states, input_grads, params):
    width = small.shape[1]
    anywhere = pl.BlockSpec(memory_space=pl.ANY)
    local = pl.BlockSpec(memory_space=pltpu.VMEM)
    return pl.pallas_call(
        spread_kernel,
        out_shape=(
            jax.ShapeDtypeStruct(states.shape, states.dtype),
            jax.ShapeDtypeStruct(input_grads.shape, input_grads.dtype),
        )
        + tuple(jax.ShapeDtypeStruct(member.shape, jnp.float32) for member in params),
        in_specs=[anywhere, local, anywhere, anywhere],
        out_specs=(anywhere, anywhere)
        + tuple(anywhere if len(member.shape) == 3 else local for member in params),
        scratch_shapes=[
            pltpu.VMEM((DEPTH, PIECE, width), jnp.bfloat16),
            pltpu.VMEM((DEPTH, PIECE, width), jnp.float32),
            pltpu.VMEM((2 * states.shape[1],) + states.shape[2:], states.dtype),
            pltpu.SemaphoreType.DMA((DEPTH,)),
            pltpu.SemaphoreType.DMA((DEPTH,)),
            pltpu.SemaphoreType.DMA((2 * states.shape[1],)),
        ],
        compiler_params=pltpu.CompilerParams(vmem_limit_bytes=VMEM_LIMIT),
        cost_estimate=pl.CostEstimate(
            flops=12 * width * width, bytes_accessed=80 * width * width, transcendentals=0
        ),
    )(sums, small, states, input_grads)


HALF_LOG = -0.5 / math.log(2.0)
BELL_SCALE = 1.0 / math.sqrt(2.0 * math.pi)
SINGLES = ("bq", "bv", "bo", "g1", "s1", "bd", "g2", "s2")


def product(left, right):
    return lax.dot_general(left, right, (((1,), (0,)), ((), ())), preferred_element_type=jnp.float32)


def product_t(left, right):
    return lax.dot_general(left, right, (((1,), (1,)), ((), ())), preferred_element_type=jnp.float32)


def gelu_pair(z):
    cdf = 0.5 * lax.erf(z * (1.0 / math.sqrt(2.0))) + 0.5
    bell = jnp.exp2(z * z * HALF_LOG)
    return z * cdf, z * BELL_SCALE * bell + cdf


def normed(values):
    average = jnp.mean(values, axis=-1, keepdims=True)
    centered = values - average
    inverse = lax.rsqrt(jnp.mean(centered * centered, axis=-1, keepdims=True) + EPSILON)
    return centered * inverse, inverse


def normed_back(grad, normal, inverse):
    first_mean = jnp.mean(grad, axis=-1, keepdims=True)
    second_mean = jnp.mean(grad * normal, axis=-1, keepdims=True)
    return inverse * (grad - first_mean - normal * second_mean)


def layer_kernel(
    ids_ref,
    lengths_ref,
    captions_hbm,
    regions_ref,
    cotangent_hbm,
    wq_hbm,
    bq_ref,
    wk_hbm,
    wv_hbm,
    bv_ref,
    wo_hbm,
    bo_ref,
    g1_ref,
    s1_ref,
    wu_hbm,
    bu_ref,
    wd_hbm,
    bd_ref,
    g2_ref,
    s2_ref,
    states_hbm,
    grads_hbm,
    a_hbm,
    b_hbm,
    small_ref,
    wqkv,
    wo,
    wu,
    wd,
    wqkv_t,
    wo_t,
    wu_t,
    wd_t,
    table,
    hidden,
    upstream,
    query,
    keys,
    values,
    probs,
    context,
    normal1,
    normal2,
    lowered,
    active,
    slope,
    result,
    staged,
    inverses,
    wide1,
    caption_cells,
    weight_sem,
    table_send,
    table_recv,
    fwd_send,
    fwd_recv,
    back_send,
    back_recv,
    out_sem,
):
    items, rows, width = hidden.shape
    held = regions_ref.shape[0]
    cap_rows = captions_hbm.shape[0]
    wide = wu.shape[1] // width
    pairs = HEADS // 2
    pair_width = width // pairs
    head = width // HEADS
    section = lax.axis_index("section")
    batch = lax.axis_index("batch")
    count = lax.axis_size("batch")
    right = (section, lax.rem(batch + 1, count))
    left = (section, lax.rem(batch + count - 1, count))
    other = (1 - section, batch)
    core = lax.rem(batch, 2)

    weight_copies = [
        pltpu.make_async_copy(source.at[0], target, weight_sem.at[n])
        for n, (source, target) in enumerate(
            (
                (wq_hbm, wqkv.at[:, pl.ds(0, width)]),
                (wk_hbm, wqkv.at[:, pl.ds(width, width)]),
                (wv_hbm, wqkv.at[:, pl.ds(2 * width, width)]),
                (wo_hbm, wo),
                (wu_hbm, wu),
                (wd_hbm, wd),
            )
        )
    ]
    for copy in weight_copies[:3]:
        copy.start()
    cotangent_copy = pltpu.make_async_copy(cotangent_hbm, upstream, weight_sem.at[6])

    barrier = pltpu.get_barrier_semaphore()
    for peer in (right, left, other):
        pl.semaphore_signal(barrier, inc=1, device_id=peer, device_id_type=MESH)
    pl.semaphore_wait(barrier, 3)

    def table_copy(n, peer):
        return pltpu.make_async_remote_copy(
            src_ref=regions_ref,
            dst_ref=table.at[pl.ds(2 * n * held, held)],
            send_sem=table_send.at[n],
            recv_sem=table_recv.at[n],
            device_id=peer,
            device_id_type=MESH,
        )

    @pl.when(section == 0)
    def _():
        caption_copy = pltpu.make_async_copy(captions_hbm, caption_cells, weight_sem.at[7])
        caption_copy.start()
        table_copy(0, right).start()
        table_copy(1, left).start()
        table[pl.ds(held, held)] = regions_ref[...]
        table_copy(0, right).wait()
        table_copy(1, left).wait()
        caption_copy.wait()

    for copy in weight_copies[3:]:
        copy.start()

    @pl.when(section == 1)
    def _():
        cotangent_copy.start()

    def forward_copy(i):
        return pltpu.make_async_remote_copy(
            src_ref=result.at[i],
            dst_ref=hidden.at[i],
            send_sem=fwd_send.at[i],
            recv_sem=fwd_recv.at[i],
            device_id=other,
            device_id_type=MESH,
        )

    def back_copy(i):
        return pltpu.make_async_remote_copy(
            src_ref=result.at[i],
            dst_ref=upstream.at[i],
            send_sem=back_send.at[i],
            recv_sem=back_recv.at[i],
            device_id=other,
            device_id_type=MESH,
        )

    def save(i, n):
        at = pl.ds(pl.multiple_of(i * rows, rows), rows)
        first = wide * width
        turn = lax.rem(i, 2)
        if n == 0:
            source, target = active.at[turn], a_hbm.at[at, pl.ds(0, first)]
        elif n == 1:
            source, target = lowered.at[turn], a_hbm.at[at, pl.ds(first, width)]
        elif n == 2:
            source, target = context.at[turn], a_hbm.at[at, pl.ds(first + width, width)]
        elif n == 3:
            source, target = hidden.at[i], a_hbm.at[at, pl.ds(first + 2 * width, width)]
        else:
            source, target = result.at[i], states_hbm.at[0, i]
        return pltpu.make_async_copy(source, target, out_sem.at[i, n])

    def staged_save(i):
        at = pl.ds(pl.multiple_of(i * rows, rows), rows)
        return pltpu.make_async_copy(staged.at[lax.rem(i, 2)], b_hbm.at[at], out_sem.at[i, 5])

    def grad_save(i):
        return pltpu.make_async_copy(result.at[i], grads_hbm.at[0, i], out_sem.at[i, 6])

    def vector(ref, j=0):
        return ref[:, j * width : (j + 1) * width].astype(jnp.float32)

    lane = lax.broadcasted_iota(jnp.int32, (rows, pair_width), 1)

    blocks = [slice(r, r + GROUP) for r in range(0, rows, GROUP)]
    spans = [slice(c, min(c + 128, rows)) for c in range(0, rows, 128)]

    def only(block, h):
        return jnp.where((lane // head) == h, block, jnp.zeros_like(block))

    def assemble(i):
        total = count * held
        spot = jnp.minimum(lax.rem(ids_ref[i] - (batch - 1) * held + total, total), 3 * held - 1)
        for n in range(items):

            @pl.when(i == n)
            def _():
                whole = jnp.concatenate(
                    [caption_cells[:, n, :].astype(jnp.float32), table[spot].astype(jnp.float32)], axis=0
                )
                hidden[n] = whole.astype(jnp.bfloat16)

    def forward(i):
        @pl.when((i == 0) & (section == 0))
        def _():
            for copy in weight_copies[:3]:
                copy.wait()

        turn = lax.rem(i, 2)
        source = hidden[i]
        mixed = product(source, wqkv[...])
        for at in blocks:
            scaled = (mixed[at, :width] + vector(bq_ref)) * (1.0 / math.sqrt(head))
            query[i, at, :] = scaled.astype(jnp.bfloat16)
            keys[i, at, :] = mixed[at, width : 2 * width].astype(jnp.bfloat16)
            values[i, at, :] = (mixed[at, 2 * width :] + vector(bv_ref)).astype(jnp.bfloat16)
        position = lax.broadcasted_iota(jnp.int32, (rows, 1), 0)
        live = (position >= cap_rows) | (position < lengths_ref[i])
        key_bias = jnp.where(live, 0.0, -1000000000.0)

        def lanes_of(p):
            return slice(p * pair_width, (p + 1) * pair_width)

        def scored(p):
            k_pair = keys[i, :, lanes_of(p)]
            stacked = jnp.concatenate([only(k_pair, 0), only(k_pair, 1)], axis=0)
            v_turned = values[i, :, lanes_of(p)].astype(jnp.float32).T.astype(jnp.bfloat16)
            return product_t(stacked, query[i, :, lanes_of(p)]), v_turned

        def weighed(p, both):
            for h in range(2):
                for span in spans:
                    scores = both[h * rows : (h + 1) * rows, span] + key_bias
                    expo = jnp.exp(scores - jnp.max(scores, axis=0, keepdims=True))
                    share = pltpu.reciprocal(jnp.sum(expo, axis=0, keepdims=True), approx=True)
                    probs[i, 2 * p + h, :, span] = (expo * share).astype(jnp.bfloat16)

        def mixed_values(p, v_turned):
            return [product(v_turned[h * head : (h + 1) * head], probs[i, 2 * p + h]) for h in range(2)]

        def place_context(p, parts):
            context[turn, :, lanes_of(p)] = jnp.concatenate(parts, axis=0).T.astype(jnp.bfloat16)

        ahead = scored(0)
        parts = None
        for p in range(pairs):
            both, v_turned = ahead
            if p + 1 < pairs:
                ahead = scored(p + 1)
            if parts is not None:
                place_context(p - 1, parts)
            weighed(p, both)
            parts = mixed_values(p, v_turned)
        place_context(pairs - 1, parts)

        @pl.when((i == 0) & (section == 0))
        def _():
            for copy in weight_copies[3:]:
                copy.wait()

        @pl.when((section == 0) & (core == 1) & (i >= 1))
        def _():
            forward_copy(i - 1).start()

        attended = product(context[turn], wo[...])
        for at in blocks:
            n1, inv1 = normed(hidden[i, at, :].astype(jnp.float32) + attended[at] + vector(bo_ref))
            normal1[i, at, :] = n1.astype(jnp.bfloat16)
            inverses[i, at, 0:1] = inv1
            first = n1 * vector(g1_ref) + vector(s1_ref)
            lowered[turn, at, :] = first.astype(jnp.bfloat16)
            wide1[at, :] = first + vector(bd_ref)
        half = wide * width // 2

        def raised(n):
            return product(lowered[turn], wu[:, n * half : (n + 1) * half])

        def bend(n, z_tile):
            for part in range(0, half, width):
                lanes = slice(n * half + part, n * half + part + width)
                bias = bu_ref[:, lanes].astype(jnp.float32)
                for at in blocks:
                    gelu, slant = gelu_pair(z_tile[at, part : part + width] + bias)
                    active[turn, at, lanes] = gelu.astype(jnp.bfloat16)
                    slope[i, at, lanes] = slant.astype(jnp.bfloat16)

        z_first = raised(0)
        z_second = raised(1)
        bend(0, z_first)
        wide1[...] += product(active[turn, :, :half], wd[:half, :])
        bend(1, z_second)
        lowest = product(active[turn, :, half:], wd[half:, :])
        for at in blocks:
            n2, inv2 = normed(wide1[at, :] + lowest[at])
            normal2[i, at, :] = n2.astype(jnp.bfloat16)
            inverses[i, at, 1:2] = inv2
            result[i, at, :] = (n2 * vector(g2_ref) + vector(s2_ref)).astype(jnp.bfloat16)

    def folded(value):
        return value[: GROUP // 2] + value[GROUP // 2 :]

    def keep_small(row, value):
        small_ref[row : row + 1, :] += jnp.sum(value, axis=0, keepdims=True)

    def single(name, value):
        keep_small(SINGLES.index(name), value)

    def backward(i):
        slot = lax.rem(i, 2)
        base = (2 + wide) * width

        def stage(at, column, value):
            staged[slot, at, column * width : (column + 1) * width] = value

        def norm_step(at, gradient, normal, layer_norm, gain, sums):
            n = normal[i, at, :].astype(jnp.float32)
            d_res = normed_back(gradient * vector(gain), n, inverses[i, at, layer_norm : layer_norm + 1])
            d_low = d_res.astype(jnp.bfloat16)
            terms = [folded(gradient * n), folded(gradient), folded(d_low.astype(jnp.float32))]
            return d_res, d_low, terms if sums is None else [a + b for a, b in zip(sums, terms)]

        sums = None
        for at in blocks:
            gradient = upstream[i, at, :].astype(jnp.float32)
            d_res, d_low, sums = norm_step(at, gradient, normal2, 1, g2_ref, sums)
            wide1[at, :] = d_res
            stage(at, 0, d_low)
        for name, value in zip(("g2", "s2", "bd"), sums):
            single(name, value)
        d_out = staged[slot, :, :width]
        half = wide * width // 2
        for n in range(2):
            d_active = product(d_out, wd_t[:, n * half : (n + 1) * half])
            for part in range(0, half, width):
                j = (n * half + part) // width
                lanes = slice(j * width, (j + 1) * width)
                total = None
                for at in blocks:
                    d_inner = d_active[at, part : part + width] * slope[i, at, lanes].astype(jnp.float32)
                    d_inner = d_inner.astype(jnp.bfloat16)
                    stage(at, 1 + j, d_inner)
                    term = folded(d_inner.astype(jnp.float32))
                    total = term if total is None else total + term
                keep_small(len(SINGLES) + j, total)
        d_deep = product(staged[slot, :, width : (1 + wide) * width], wu_t[...])
        sums = None
        for at in blocks:
            d_res, d_low, sums = norm_step(at, wide1[at, :] + d_deep[at], normal1, 0, g1_ref, sums)
            wide1[at, :] = d_res
            stage(at, 1 + wide, d_low)
        for name, value in zip(("g1", "s1", "bo"), sums):
            single(name, value)
        d_att = staged[slot, :, (1 + wide) * width : (2 + wide) * width]
        @pl.when(i == 0)
        def _():
            save(items - 2, 0).wait()
            save(items - 1, 0).wait()

        active[0, :, :width] = product(d_att, wo_t[...]).astype(jnp.bfloat16)

        def lanes_of(p):
            return slice(p * pair_width, (p + 1) * pair_width)

        def place_grad(n, p, block):
            at = base + n * width + p * pair_width
            staged[slot, :, at : at + pair_width] = block.astype(jnp.bfloat16)

        def opened(p):
            v_pair = values[i, :, lanes_of(p)]
            c_pair = active[0, :, lanes_of(p)]
            stacked = jnp.concatenate([only(v_pair, 0), only(v_pair, 1)], axis=0)
            k_turned = keys[i, :, lanes_of(p)].astype(jnp.float32).T.astype(jnp.bfloat16)
            d_value = product(probs[i, 2 * p], only(c_pair, 0))
            d_value += product(probs[i, 2 * p + 1], only(c_pair, 1))
            return product_t(stacked, c_pair), k_turned, d_value

        def score_base(p, h):
            return (2 * (p % 2) + h) * 2 * 128

        def score_grads(p, both):
            for h in range(2):
                for span in spans:
                    prob = probs[i, 2 * p + h, :, span].astype(jnp.float32)
                    d_prob = both[h * rows : (h + 1) * rows, span]
                    drift = jnp.sum(d_prob * prob, axis=0, keepdims=True)
                    at = score_base(p, h)
                    active[1, :, at + span.start : at + span.stop] = (prob * (d_prob - drift)).astype(jnp.bfloat16)
            return [active[1, :, score_base(p, h) : score_base(p, h) + rows] for h in range(2)]

        def closed(p, found, k_turned):
            q_pair = query[i, :, lanes_of(p)]
            d_key = product(found[0], only(q_pair, 0)) + product(found[1], only(q_pair, 1))
            return d_key, [product(k_turned[h * head : (h + 1) * head], found[h]) for h in range(2)]

        def place_grads(p, d_value, d_key, parts):
            place_grad(0, p, jnp.concatenate(parts, axis=0).T * (1.0 / math.sqrt(head)))
            place_grad(1, p, d_key)
            place_grad(2, p, d_value)

        ahead = opened(0)
        waiting = None
        for p in range(pairs):
            both, k_turned, d_value = ahead
            if p + 1 < pairs:
                ahead = opened(p + 1)
            if waiting is not None:
                place_grads(*waiting)
            found = score_grads(p, both)
            d_key, parts = closed(p, found, k_turned)
            waiting = (p, d_value, d_key, parts)
        place_grads(*waiting)
        d_source = product(staged[slot, :, base : base + 3 * width], wqkv_t[...])
        sums = None
        for at in blocks:
            result[i, at, :] = (wide1[at, :] + d_source[at]).astype(jnp.bfloat16)
            terms = [
                folded(staged[slot, at, base : base + width].astype(jnp.float32)),
                folded(staged[slot, at, base + 2 * width : base + 3 * width].astype(jnp.float32)),
            ]
            sums = terms if sums is None else [a + b for a, b in zip(sums, terms)]
        single("bq", sums[0])
        single("bv", sums[1])

    small_ref[...] = jnp.zeros_like(small_ref)
    side = 256
    unit = lax.broadcasted_iota(jnp.int32, (side, side), 0) == lax.broadcasted_iota(jnp.int32, (side, side), 1)
    unit = jnp.where(unit, 1.0, 0.0).astype(jnp.bfloat16)

    def turn_weights():
        for natural, turned in ((wqkv, wqkv_t), (wo, wo_t), (wu, wu_t), (wd, wd_t)):
            for block in range(0, natural.shape[0], width):

                def one(n, carry):
                    at = pl.ds(pl.multiple_of(n * side, side), side)
                    tall = product_t(unit, natural[block : block + width, at])
                    turned[at, block : block + width] = tall.astype(jnp.bfloat16)
                    return carry

                lax.fori_loop(0, natural.shape[1] // side, one, 0)

    @pl.when(section == 1)
    def _():
        for copy in weight_copies:
            copy.wait()
        turn_weights()

    def forward_step(i, carry):
        @pl.when(section == 0)
        def _():
            assemble(i)

        @pl.when(section == 1)
        def _():
            forward_copy(i).wait_recv()

        @pl.when(i >= 2)
        def _():
            for n in range(3):
                save(i - 2, n).wait()

        forward(i)

        @pl.when((section == 0) & ((core == 0) | (i == items - 1)))
        def _():
            forward_copy(i).start()

        for n in range(5):
            save(i, n).start()
        return carry

    lax.fori_loop(0, items, forward_step, 0)

    @pl.when(section == 0)
    def _():
        turn_weights()

    @pl.when(section == 1)
    def _():
        cotangent_copy.wait()

    def backward_step(i, carry):
        @pl.when(section == 0)
        def _():
            back_copy(i).wait_recv()

        @pl.when(i >= 2)
        def _():
            staged_save(i - 2).wait()

        save(i, 4).wait()

        @pl.when(section == 0)
        def _():
            forward_copy(i).wait_send()

        backward(i)

        @pl.when(section == 1)
        def _():
            back_copy(i).start()

        staged_save(i).start()
        grad_save(i).start()
        return carry

    lax.fori_loop(0, items, backward_step, 0)

    def finish(i, carry):
        save(i, 3).wait()
        grad_save(i).wait()

        @pl.when(i >= items - 2)
        def _():
            staged_save(i).wait()
            for n in range(1, 3):
                save(i, n).wait()

        @pl.when(section == 1)
        def _():
            back_copy(i).wait_send()

        return carry

    lax.fori_loop(0, items, finish, 0)


def layered(image_ids, caption_lengths, captions, regions, cotangent, stacked):
    items, cap_rows, width = captions.shape
    held, region_rows, _ = regions.shape
    rows = cap_rows + region_rows
    inner = stacked[9].shape[2]
    low = jnp.bfloat16
    wide = inner // width

    def cells(*shape):
        return pltpu.VMEM(shape, low)

    anywhere = pl.BlockSpec(memory_space=pl.ANY)
    local = pl.BlockSpec(memory_space=pltpu.VMEM)
    scalars = pl.BlockSpec(memory_space=pltpu.SMEM)
    return pl.pallas_call(
        layer_kernel,
        out_shape=(
            jax.ShapeDtypeStruct((1, items, rows, width), low),
            jax.ShapeDtypeStruct((1, items, rows, width), low),
            jax.ShapeDtypeStruct((items * rows, (3 + wide) * width), low),
            jax.ShapeDtypeStruct((items * rows, (5 + wide) * width), low),
            jax.ShapeDtypeStruct((GROUP, width), jnp.float32),
        ),
        in_specs=[scalars, scalars, anywhere, local, anywhere]
        + [anywhere if len(member.shape) == 3 else local for member in stacked],
        out_specs=(anywhere, anywhere, anywhere, anywhere, local),
        scratch_shapes=[
            cells(width, 3 * width),
            cells(width, width),
            cells(width, inner),
            cells(inner, width),
            cells(3 * width, width),
            cells(width, width),
            cells(inner, width),
            cells(width, inner),
            cells(3 * held, region_rows, width),
            cells(items, rows, width),
            cells(items, rows, width),
            cells(items, rows, width),
            cells(items, rows, width),
            cells(items, rows, width),
            cells(items, HEADS, rows, rows),
            cells(2, rows, width),
            cells(items, rows, width),
            cells(items, rows, width),
            cells(2, rows, width),
            cells(2, rows, inner),
            cells(items, rows, inner),
            cells(items, rows, width),
            cells(2, rows, (5 + wide) * width),
            pltpu.VMEM((items, rows, 2), jnp.float32),
            pltpu.VMEM((rows, width), jnp.float32),
            cells(cap_rows, items, width),
            pltpu.SemaphoreType.DMA((8,)),
            pltpu.SemaphoreType.DMA((2,)),
            pltpu.SemaphoreType.DMA((2,)),
            pltpu.SemaphoreType.DMA((items,)),
            pltpu.SemaphoreType.DMA((items,)),
            pltpu.SemaphoreType.DMA((items,)),
            pltpu.SemaphoreType.DMA((items,)),
            pltpu.SemaphoreType.DMA((items, 7)),
        ],
        compiler_params=pltpu.CompilerParams(
            collective_id=0, has_side_effects=True, vmem_limit_bytes=VMEM_LIMIT
        ),
        cost_estimate=pl.CostEstimate(
            flops=4 * items * rows * (4 + 2 * wide) * width * width,
            bytes_accessed=60_000_000,
            transcendentals=0,
        ),
    )(image_ids, caption_lengths, captions.transpose(1, 0, 2), regions, cotangent, *stacked)


def body(
    captions,
    regions,
    image_ids,
    caption_lengths,
    cotangent,
    query_weight,
    query_bias,
    key_weight,
    value_weight,
    value_bias,
    out_weight,
    out_bias,
    norm1_gain,
    norm1_bias,
    up_weight,
    up_bias,
    down_weight,
    down_bias,
    norm2_gain,
    norm2_bias,
):
    stacked = (
        query_weight,
        query_bias,
        key_weight,
        value_weight,
        value_bias,
        out_weight,
        out_bias,
        norm1_gain,
        norm1_bias,
        up_weight,
        up_bias,
        down_weight,
        down_bias,
        norm2_gain,
        norm2_bias,
    )
    width = captions.shape[2]
    states, input_grads, a_side, b_side, small = layered(
        image_ids, caption_lengths, captions, regions, cotangent, stacked
    )
    sums, small_sums = reduced(a_side, b_side, small, lax.axis_size("batch"))
    return tuple(spread(sums.reshape(-1, width), small_sums, states, input_grads, stacked))


def solution(mesh):
    placed = (
        P("batch", None, None),
        P("batch", None, None),
        P("batch"),
        P("batch"),
        P("batch", None, None),
        P("section", None, None),
        P("section", None),
        P("section", None, None),
        P("section", None, None),
        P("section", None),
        P("section", None, None),
        P("section", None),
        P("section", None),
        P("section", None),
        P("section", None, None),
        P("section", None),
        P("section", None, None),
        P("section", None),
        P("section", None),
        P("section", None),
    )
    return jax.shard_map(
        body,
        mesh=mesh,
        in_specs=placed,
        out_specs=(
            P("section", "batch", None, None),
            P("section", "batch", None, None),
            P("section", None, None),
            P("section", None),
            P("section", None, None),
            P("section", None, None),
            P("section", None),
            P("section", None, None),
            P("section", None),
            P("section", None),
            P("section", None),
            P("section", None, None),
            P("section", None),
            P("section", None, None),
            P("section", None),
            P("section", None),
            P("section", None),
        ),
        check_vma=False,
    )
```

```python
import functools
import math

import jax
import jax.numpy as jnp
from jax import lax
from jax.experimental import pallas as pl
from jax.experimental.pallas import tpu as pltpu
from jax.sharding import PartitionSpec as P

HEADS = 12
EPSILON = 1e-12
MESH = pl.DeviceIdType.MESH
VMEM_LIMIT = 63 * 1024 * 1024
GROUP = 16
CHUNK_GROUPS = 16
SLOTS = 18
SLOT_GROUPS = 24
LAG = 3
CYCLE = 3
LINE = 4
SPLIT_BITS = 4


def reduce_kernel(
    bits,
    chunks,
    a_hbm,
    b_hbm,
    small_ref,
    out_hbm,
    small_out,
    a_ref,
    b_ref,
    acc,
    whole,
    recv,
    small_acc,
    small_recv,
    load_sem,
    send_sem,
    recv_sem,
    save_sem,
    small_send_sem,
    small_recv_sem,
):
    width = acc.shape[2]
    extra = bits - SPLIT_BITS
    first_gather = SPLIT_BITS + 1 + extra
    stages = 2 * (SPLIT_BITS + 1) + extra + 1
    me = lax.axis_index("batch")
    section = lax.axis_index("section")
    core, side, place = me % 2, (me // 2) % 2, (me // 4) % LINE
    blocks_a = a_hbm.shape[1] // width
    blocks_b = b_hbm.shape[1] // width
    per_block = width // (CHUNK_GROUPS * GROUP)

    def load(source, target, block, base):
        lanes = pl.ds(block * width, width)
        return pltpu.make_async_copy(source.at[:, lanes], target.at[:, lanes], load_sem.at[base + block])

    def load_a(block):
        return load(a_hbm, a_ref, block, 0)

    def load_b(block):
        return load(b_hbm, b_ref, block, blocks_a)

    wide = blocks_a - 3
    first_use = {0: [(load_a, 0), (load_b, 0)]}
    for j in range(1, wide):
        first_use[j] = [(load_a, j)]
    first_use[wide] = [(load_a, wide), (load_b, 1)]
    for j in range(1, wide):
        first_use[wide + j] = [(load_b, 1 + j)]
    first_use[2 * wide] = [(load_a, wide + 1), (load_b, wide + 1)]
    first_use[2 * wide + 1] = [(load_a, wide + 2), (load_b, wide + 2)]
    first_use[2 * wide + 2] = [(load_b, wide + 3)]
    first_use[2 * wide + 3] = [(load_b, wide + 4)]
    for j in range(2 * wide + 4):
        for kind, block in first_use[j]:
            kind(block).start()

    def bit_mate(k):
        bit = (me // 2**k) % 2
        return (section, me + 2**k * (1 - 2 * bit))

    core_mate, side_mate = bit_mate(0), bit_mate(1)
    mates = ((section, me - LINE), (section, me + LINE))
    ring = [(section, me + LINE * ((place + d) % LINE - place)) for d in (LINE - 1, 1)]

    barrier = pltpu.get_barrier_semaphore()
    for peer in [core_mate, side_mate] + ring + [bit_mate(k) for k in range(2, bits)]:
        pl.semaphore_signal(barrier, inc=1, device_id=peer, device_id_type=MESH)
    pl.semaphore_wait(barrier, bits + 2)

    def low_core(c):
        return c * CHUNK_GROUPS + core * 8

    def low_side(c):
        return low_core(c) + side * 4

    def block_start(c, kind, b):
        return low_side(c) + b if kind == 0 else low_core(c) + 2 * b

    def final(c, kind):
        return low_side(c) + place if kind == 0 else low_core(c) + 2 * place + side

    def remote(c, source, start, size, target, spot, index, peer):
        return pltpu.make_async_remote_copy(
            src_ref=source.at[pl.ds(start, size)],
            dst_ref=target.at[lax.rem(c, SLOTS), pl.ds(spot, size)] if target is recv else target.at[pl.ds(start, size)],
            send_sem=send_sem.at[lax.rem(c, SLOTS), index],
            recv_sem=recv_sem.at[lax.rem(c, SLOTS), index],
            device_id=peer,
            device_id_type=MESH,
        )

    def core_copy(c):
        return remote(c, acc, c * CHUNK_GROUPS + (1 - core) * 8, 8, recv, 0, 0, core_mate)

    def side_copy(c, kind):
        if kind == 0:
            return remote(c, acc, low_core(c) + (1 - side) * 4, 4, recv, 8, 1, side_mate)
        return remote(c, acc, low_core(c) + 2 * place + (1 - side), 1, recv, 8, 1, side_mate)

    def line_copy(c, kind, r, d):
        size = 1 + kind
        b = jnp.minimum(3 - r + place, 3) if d == 1 else jnp.maximum(r - 3 + place, 0)
        spot = 12 + 2 * (2 * r + d)
        return remote(c, acc, block_start(c, kind, b), size, recv, spot, 2 + 2 * r + d, mates[d])

    def spread_copy(c, kind, r, d):
        size = 1 + kind
        b = jnp.maximum(place - r, 0) if d == 1 else jnp.minimum(place + r, 3)
        return remote(c, whole, block_start(c, kind, b), size, whole, 0, 8 + 2 * r + d, mates[d])

    def side_back_copy(c, kind):
        if kind == 0:
            return remote(c, whole, low_side(c), 4, whole, 0, 14, side_mate)
        return remote(c, whole, final(c, kind), 1, whole, 0, 14, side_mate)

    def core_back_copy(c):
        return remote(c, whole, low_core(c), 8, whole, 0, 15, core_mate)

    def extra_copy(c, kind, e):
        return remote(c, acc, final(c, kind), 1, recv, 24 + e, 16 + e, bit_mate(SPLIT_BITS + e))

    def save_copy(c):
        at = pl.ds(c * CHUNK_GROUPS, CHUNK_GROUPS)
        return pltpu.make_async_copy(whole.at[at], out_hbm.at[at], save_sem.at[lax.rem(c, SLOTS)])

    def add_groups(start, count, c, spot):
        slot = lax.rem(c, SLOTS)
        for g in range(count):
            total = acc[start + g].astype(jnp.float32) + recv[slot, spot + g].astype(jnp.float32)
            acc[start + g] = total.astype(jnp.bfloat16)

    def name_of(kind, s):
        if s == 0:
            return ("core",)
        if s == stages - 1:
            return ("save",)
        if s == stages - 2:
            return ("core_back",)
        if s < SPLIT_BITS + 1:
            order = [("side",), ("line", 0), ("line", 1), ("line", 2)]
            order = order if kind == 0 else order[1:] + order[:1]
            return order[s - 1]
        if s < first_gather:
            return ("extra", s - SPLIT_BITS - 1)
        order = [("spread", 0), ("spread", 1), ("spread", 2), ("side_back",)]
        order = order if kind == 0 else order[3:] + order[:3]
        return order[s - first_gather]

    def start_stage(c, kind, s):
        name = name_of(kind, s)
        if s == first_gather:
            whole[final(c, kind)] = acc[final(c, kind)]
        if name[0] == "core":
            core_copy(c).start()
        elif name[0] == "side":
            side_copy(c, kind).start()
        elif name[0] == "line":
            r = name[1]
            pl.when(place <= r)(lambda: line_copy(c, kind, r, 1).start())
            pl.when(place >= 3 - r)(lambda: line_copy(c, kind, r, 0).start())
        elif name[0] == "extra":
            extra_copy(c, kind, name[1]).start()
        elif name[0] == "spread":
            r = name[1]
            pl.when((place >= r) & (place <= 2))(lambda: spread_copy(c, kind, r, 1).start())
            pl.when((place >= 1) & (place <= 3 - r))(lambda: spread_copy(c, kind, r, 0).start())
        elif name[0] == "side_back":
            side_back_copy(c, kind).start()
        elif name[0] == "core_back":
            core_back_copy(c).start()
        else:
            save_copy(c).start()

    def finish_stage(c, kind, s):
        name = name_of(kind, s)
        if name[0] == "core":
            core_copy(c).wait()
            add_groups(low_core(c), 8, c, 0)
        elif name[0] == "side":
            side_copy(c, kind).wait()
            if kind == 0:
                add_groups(low_side(c), 4, c, 8)
            else:
                add_groups(final(c, kind), 1, c, 8)
        elif name[0] == "line":
            r = name[1]

            @pl.when(place <= r)
            def _():
                line_copy(c, kind, r, 1).wait_send()

            @pl.when(place >= 3 - r)
            def _():
                line_copy(c, kind, r, 0).wait_send()

            @pl.when((place >= 1) & (place <= r + 1))
            def _():
                line_copy(c, kind, r, 1).wait_recv()
                add_groups(block_start(c, kind, 2 - r + place), 1 + kind, c, 12 + 2 * (2 * r + 1))

            @pl.when((place <= 2) & (place >= 2 - r))
            def _():
                line_copy(c, kind, r, 0).wait_recv()
                add_groups(block_start(c, kind, r - 2 + place), 1 + kind, c, 12 + 2 * (2 * r))

        elif name[0] == "extra":
            extra_copy(c, kind, name[1]).wait()
            add_groups(final(c, kind), 1, c, 24 + name[1])
        elif name[0] == "spread":
            r = name[1]
            pl.when((place >= r) & (place <= 2))(lambda: spread_copy(c, kind, r, 1).wait_send())
            pl.when((place >= 1) & (place <= 3 - r))(lambda: spread_copy(c, kind, r, 0).wait_send())
            pl.when(place >= r + 1)(lambda: spread_copy(c, kind, r, 1).wait_recv())
            pl.when(place <= 2 - r)(lambda: spread_copy(c, kind, r, 0).wait_recv())
        elif name[0] == "side_back":
            side_back_copy(c, kind).wait()
        elif name[0] == "core_back":
            core_back_copy(c).wait()
        else:
            save_copy(c).wait()

    def small_copy(k):
        return pltpu.make_async_remote_copy(
            src_ref=small_acc.at[k],
            dst_ref=small_recv.at[k],
            send_sem=small_send_sem.at[k],
            recv_sem=small_recv_sem.at[k],
            device_id=bit_mate(k),
            device_id_type=MESH,
        )

    small_acc[0] = small_ref[...]

    def step(t, phase):
        for s in range(stages, 0, -1):
            c = t - LAG * s
            kind = (phase - LAG * s) % CYCLE // 2

            @pl.when((c >= 0) & (c < chunks))
            def _():
                finish_stage(c, kind, s - 1)
                if s < stages:
                    start_stage(c, kind, s)

        for j in range(2 * wide + 4):

            @pl.when(t == per_block * j)
            def _():
                for kind, block in first_use[j]:
                    kind(block).wait()

        @pl.when(t < chunks)
        def _():
            block, part = t // per_block, t % per_block
            a_col = jnp.minimum(block, wide) + jnp.minimum(block // (2 * wide), 1) + jnp.minimum(block // (2 * wide + 1), 1)
            b_col = jnp.maximum(block - wide + 1, 0)
            lines = CHUNK_GROUPS * GROUP
            left = a_ref[:, pl.ds(pl.multiple_of(a_col * width + part * lines, lines), lines)]
            right = b_ref[:, pl.ds(pl.multiple_of(b_col * width, width), width)]
            grad = lax.dot_general(left, right, (((0,), (0,)), ((), ())), preferred_element_type=jnp.float32)
            acc[pl.ds(t * CHUNK_GROUPS, CHUNK_GROUPS)] = grad.astype(jnp.bfloat16).reshape(
                CHUNK_GROUPS, GROUP, width
            )
            core_copy(t).start()

        for k in range(bits + 1):

            @pl.when(t == LAG * k)
            def _():
                if k > 0:
                    small_copy(k - 1).wait()
                    small_acc[k] = small_acc[k - 1] + small_recv[k - 1]
                if k < bits:
                    small_copy(k).start()

    def cycle(n, carry):
        for phase in range(CYCLE):
            step(n * CYCLE + phase, phase)
        return carry

    lax.fori_loop(0, pl.cdiv(chunks + LAG * stages, CYCLE), cycle, 0)
    small_out[...] = small_acc[bits]


def reduced(a_side, b_side, small, count):
    rows = a_side.shape[0]
    width = small.shape[1]
    bits = count.bit_length() - 1
    extra = bits - SPLIT_BITS
    blocks = 2 * (a_side.shape[1] // width - 3) + 4
    chunks = blocks * width // (CHUNK_GROUPS * GROUP)
    groups = chunks * CHUNK_GROUPS
    loads = (a_side.shape[1] + b_side.shape[1]) // width
    return pl.pallas_call(
        functools.partial(reduce_kernel, bits, chunks),
        out_shape=(
            jax.ShapeDtypeStruct((groups, GROUP, width), jnp.bfloat16),
            jax.ShapeDtypeStruct(small.shape, jnp.float32),
        ),
        in_specs=[
            pl.BlockSpec(memory_space=pl.ANY),
            pl.BlockSpec(memory_space=pl.ANY),
            pl.BlockSpec(memory_space=pltpu.VMEM),
        ],
        out_specs=(pl.BlockSpec(memory_space=pl.ANY), pl.BlockSpec(memory_space=pltpu.VMEM)),
        scratch_shapes=[
            pltpu.VMEM(a_side.shape, jnp.bfloat16),
            pltpu.VMEM(b_side.shape, jnp.bfloat16),
            pltpu.VMEM((groups, GROUP, width), jnp.bfloat16),
            pltpu.VMEM((groups, GROUP, width), jnp.bfloat16),
            pltpu.VMEM((SLOTS, SLOT_GROUPS + extra, GROUP, width), jnp.bfloat16),
            pltpu.VMEM((bits + 1,) + small.shape, jnp.float32),
            pltpu.VMEM((bits,) + small.shape, jnp.float32),
            pltpu.SemaphoreType.DMA((loads,)),
            pltpu.SemaphoreType.DMA((SLOTS, 16 + extra)),
            pltpu.SemaphoreType.DMA((SLOTS, 16 + extra)),
            pltpu.SemaphoreType.DMA((SLOTS,)),
            pltpu.SemaphoreType.DMA((bits,)),
            pltpu.SemaphoreType.DMA((bits,)),
        ],
        compiler_params=pltpu.CompilerParams(
            collective_id=1, has_side_effects=True, vmem_limit_bytes=VMEM_LIMIT
        ),
        cost_estimate=pl.CostEstimate(
            flops=2 * rows * blocks * width * width, bytes_accessed=80_000_000, transcendentals=0
        ),
    )(a_side, b_side, small)


PIECE = 384
DEPTH = 4


def spread_kernel(sum_hbm, small_ref, states_hbm, grads_hbm, *refs):
    width = small_ref.shape[1]
    (o_wq, o_bq, o_wk, o_wv, o_bv, o_wo, o_bo, o_g1, o_s1, o_up, o_bu, o_dn, o_bd, o_g2, o_s2) = refs[2:17]
    states_out, grads_out = refs[:2]
    taken, given, held, in_sem, out_sem, held_sem = refs[17:]
    wide = o_bu.shape[1] // width
    targets = []
    for j in range(wide):
        targets += [o_dn.at[0, pl.ds(j * width + r, PIECE), :] for r in range(0, width, PIECE)]
    for j in range(wide):
        targets += [o_up.at[0, pl.ds(r, PIECE), pl.ds(j * width, width)] for r in range(0, width, PIECE)]
    for ref in (o_wo, o_wq, o_wk, o_wv):
        targets += [ref.at[0, pl.ds(r, PIECE), :] for r in range(0, width, PIECE)]

    items = states_hbm.shape[1]
    passes = [(states_hbm.at[0, i], states_out.at[0, i]) for i in range(items)]
    passes += [(grads_hbm.at[0, i], grads_out.at[0, i]) for i in range(items)]

    def pass_in(i):
        return pltpu.make_async_copy(passes[i][0], held.at[i], held_sem.at[i])

    def pass_out(i):
        return pltpu.make_async_copy(held.at[i], passes[i][1], held_sem.at[i])

    def load(i):
        return pltpu.make_async_copy(
            sum_hbm.at[pl.ds(i * PIECE, PIECE)], taken.at[i % DEPTH], in_sem.at[i % DEPTH]
        )

    def store(i):
        return pltpu.make_async_copy(given.at[i % DEPTH], targets[i], out_sem.at[i % DEPTH])

    for i in range(DEPTH):
        load(i).start()
    for i in range(len(passes)):
        pass_in(i).start()
    singles = [o_bq, o_bv, o_bo, o_g1, o_s1, o_bd, o_g2, o_s2]
    for i, ref in enumerate(singles):
        ref[...] = small_ref[pl.ds(i, 1), :]
    for j in range(wide):
        o_bu[:, pl.ds(j * width, width)] = small_ref[pl.ds(len(singles) + j, 1), :]
    for i in range(len(targets)):
        load(i).wait()
        if i >= DEPTH:
            store(i - DEPTH).wait()

        def convert(r, carry):
            rows = pl.ds(pl.multiple_of(r * 64, 64), 64)
            given[i % DEPTH, rows, :] = taken[i % DEPTH, rows, :].astype(jnp.float32)
            return carry

        lax.fori_loop(0, PIECE // 64, convert, 0)
        store(i).start()
        if i + DEPTH < len(targets):
            load(i + DEPTH).start()
        if i < len(passes):
            pass_in(i).wait()
            pass_out(i).start()
    for i in range(len(targets) - DEPTH, len(targets)):
        store(i).wait()
    for i in range(len(passes)):
        pass_out(i).wait()


def spread(sums, small, states, input_grads, params):
    width = small.shape[1]
    anywhere = pl.BlockSpec(memory_space=pl.ANY)
    local = pl.BlockSpec(memory_space=pltpu.VMEM)
    return pl.pallas_call(
        spread_kernel,
        out_shape=(
            jax.ShapeDtypeStruct(states.shape, states.dtype),
            jax.ShapeDtypeStruct(input_grads.shape, input_grads.dtype),
        )
        + tuple(jax.ShapeDtypeStruct(member.shape, jnp.float32) for member in params),
        in_specs=[anywhere, local, anywhere, anywhere],
        out_specs=(anywhere, anywhere)
        + tuple(anywhere if len(member.shape) == 3 else local for member in params),
        scratch_shapes=[
            pltpu.VMEM((DEPTH, PIECE, width), jnp.bfloat16),
            pltpu.VMEM((DEPTH, PIECE, width), jnp.float32),
            pltpu.VMEM((2 * states.shape[1],) + states.shape[2:], states.dtype),
            pltpu.SemaphoreType.DMA((DEPTH,)),
            pltpu.SemaphoreType.DMA((DEPTH,)),
            pltpu.SemaphoreType.DMA((2 * states.shape[1],)),
        ],
        compiler_params=pltpu.CompilerParams(vmem_limit_bytes=VMEM_LIMIT),
        cost_estimate=pl.CostEstimate(
            flops=12 * width * width, bytes_accessed=80 * width * width, transcendentals=0
        ),
    )(sums, small, states, input_grads)


HALF_LOG = -0.5 / math.log(2.0)
BELL_SCALE = 1.0 / math.sqrt(2.0 * math.pi)
SINGLES = ("bq", "bv", "bo", "g1", "s1", "bd", "g2", "s2")


def product(left, right):
    return lax.dot_general(left, right, (((1,), (0,)), ((), ())), preferred_element_type=jnp.float32)


def product_t(left, right):
    return lax.dot_general(left, right, (((1,), (1,)), ((), ())), preferred_element_type=jnp.float32)


def gelu_pair(z):
    cdf = 0.5 * lax.erf(z * (1.0 / math.sqrt(2.0))) + 0.5
    bell = jnp.exp2(z * z * HALF_LOG)
    return z * cdf, z * BELL_SCALE * bell + cdf


def normed(values):
    average = jnp.mean(values, axis=-1, keepdims=True)
    centered = values - average
    inverse = lax.rsqrt(jnp.mean(centered * centered, axis=-1, keepdims=True) + EPSILON)
    return centered * inverse, inverse


def normed_back(grad, normal, inverse):
    first_mean = jnp.mean(grad, axis=-1, keepdims=True)
    second_mean = jnp.mean(grad * normal, axis=-1, keepdims=True)
    return inverse * (grad - first_mean - normal * second_mean)


def layer_kernel(
    ids_ref,
    lengths_ref,
    captions_hbm,
    regions_ref,
    cotangent_hbm,
    wq_hbm,
    bq_ref,
    wk_hbm,
    wv_hbm,
    bv_ref,
    wo_hbm,
    bo_ref,
    g1_ref,
    s1_ref,
    wu_hbm,
    bu_ref,
    wd_hbm,
    bd_ref,
    g2_ref,
    s2_ref,
    states_hbm,
    grads_hbm,
    a_hbm,
    b_hbm,
    small_ref,
    wqkv,
    wo,
    wu,
    wd,
    wqkv_t,
    wo_t,
    wu_t,
    wd_t,
    table,
    hidden,
    upstream,
    query,
    keys,
    values,
    probs,
    context,
    normal1,
    normal2,
    lowered,
    active,
    slope,
    result,
    staged,
    inverses,
    wide1,
    caption_cells,
    weight_sem,
    table_send,
    table_recv,
    fwd_send,
    fwd_recv,
    back_send,
    back_recv,
    out_sem,
):
    items, rows, width = hidden.shape
    held = regions_ref.shape[0]
    cap_rows = captions_hbm.shape[0]
    wide = wu.shape[1] // width
    pairs = HEADS // 2
    pair_width = width // pairs
    head = width // HEADS
    section = lax.axis_index("section")
    batch = lax.axis_index("batch")
    count = lax.axis_size("batch")
    right = (section, lax.rem(batch + 1, count))
    left = (section, lax.rem(batch + count - 1, count))
    other = (1 - section, batch)
    core = lax.rem(batch, 2)

    weight_copies = [
        pltpu.make_async_copy(source.at[0], target, weight_sem.at[n])
        for n, (source, target) in enumerate(
            (
                (wq_hbm, wqkv.at[:, pl.ds(0, width)]),
                (wk_hbm, wqkv.at[:, pl.ds(width, width)]),
                (wv_hbm, wqkv.at[:, pl.ds(2 * width, width)]),
                (wo_hbm, wo),
                (wu_hbm, wu),
                (wd_hbm, wd),
            )
        )
    ]
    for copy in weight_copies[:3]:
        copy.start()
    cotangent_copy = pltpu.make_async_copy(cotangent_hbm, upstream, weight_sem.at[6])

    barrier = pltpu.get_barrier_semaphore()
    for peer in (right, left, other):
        pl.semaphore_signal(barrier, inc=1, device_id=peer, device_id_type=MESH)
    pl.semaphore_wait(barrier, 3)

    def table_copy(n, peer):
        return pltpu.make_async_remote_copy(
            src_ref=regions_ref,
            dst_ref=table.at[pl.ds(2 * n * held, held)],
            send_sem=table_send.at[n],
            recv_sem=table_recv.at[n],
            device_id=peer,
            device_id_type=MESH,
        )

    @pl.when(section == 0)
    def _():
        caption_copy = pltpu.make_async_copy(captions_hbm, caption_cells, weight_sem.at[7])
        caption_copy.start()
        table_copy(0, right).start()
        table_copy(1, left).start()
        table[pl.ds(held, held)] = regions_ref[...]
        table_copy(0, right).wait()
        table_copy(1, left).wait()
        caption_copy.wait()

    for copy in weight_copies[3:]:
        copy.start()

    @pl.when(section == 1)
    def _():
        cotangent_copy.start()

    def forward_copy(i):
        return pltpu.make_async_remote_copy(
            src_ref=result.at[i],
            dst_ref=hidden.at[i],
            send_sem=fwd_send.at[i],
            recv_sem=fwd_recv.at[i],
            device_id=other,
            device_id_type=MESH,
        )

    def back_copy(i):
        return pltpu.make_async_remote_copy(
            src_ref=result.at[i],
            dst_ref=upstream.at[i],
            send_sem=back_send.at[i],
            recv_sem=back_recv.at[i],
            device_id=other,
            device_id_type=MESH,
        )

    def save(i, n):
        at = pl.ds(pl.multiple_of(i * rows, rows), rows)
        first = wide * width
        turn = lax.rem(i, 2)
        if n == 0:
            source, target = active.at[turn], a_hbm.at[at, pl.ds(0, first)]
        elif n == 1:
            source, target = lowered.at[turn], a_hbm.at[at, pl.ds(first, width)]
        elif n == 2:
            source, target = context.at[turn], a_hbm.at[at, pl.ds(first + width, width)]
        elif n == 3:
            source, target = hidden.at[i], a_hbm.at[at, pl.ds(first + 2 * width, width)]
        else:
            source, target = result.at[i], states_hbm.at[0, i]
        return pltpu.make_async_copy(source, target, out_sem.at[i, n])

    def staged_save(i):
        at = pl.ds(pl.multiple_of(i * rows, rows), rows)
        return pltpu.make_async_copy(staged.at[lax.rem(i, 2)], b_hbm.at[at], out_sem.at[i, 5])

    def grad_save(i):
        return pltpu.make_async_copy(result.at[i], grads_hbm.at[0, i], out_sem.at[i, 6])

    def vector(ref, j=0):
        return ref[:, j * width : (j + 1) * width].astype(jnp.float32)

    lane = lax.broadcasted_iota(jnp.int32, (rows, pair_width), 1)

    blocks = [slice(r, r + GROUP) for r in range(0, rows, GROUP)]
    spans = [slice(c, min(c + 128, rows)) for c in range(0, rows, 128)]

    def only(block, h):
        return jnp.where((lane // head) == h, block, jnp.zeros_like(block))

    def assemble(i):
        total = count * held
        spot = jnp.minimum(lax.rem(ids_ref[i] - (batch - 1) * held + total, total), 3 * held - 1)
        for n in range(items):

            @pl.when(i == n)
            def _():
                whole = jnp.concatenate(
                    [caption_cells[:, n, :].astype(jnp.float32), table[spot].astype(jnp.float32)], axis=0
                )
                hidden[n] = whole.astype(jnp.bfloat16)

    def forward(i):
        @pl.when((i == 0) & (section == 0))
        def _():
            for copy in weight_copies[:3]:
                copy.wait()

        turn = lax.rem(i, 2)
        source = hidden[i]
        mixed = product(source, wqkv[...])
        for at in blocks:
            scaled = (mixed[at, :width] + vector(bq_ref)) * (1.0 / math.sqrt(head))
            query[i, at, :] = scaled.astype(jnp.bfloat16)
            keys[i, at, :] = mixed[at, width : 2 * width].astype(jnp.bfloat16)
            values[i, at, :] = (mixed[at, 2 * width :] + vector(bv_ref)).astype(jnp.bfloat16)
        position = lax.broadcasted_iota(jnp.int32, (rows, 1), 0)
        live = (position >= cap_rows) | (position < lengths_ref[i])
        key_bias = jnp.where(live, 0.0, -1000000000.0)

        def wait_rest():
            @pl.when((i == 0) & (section == 0))
            def _():
                for copy in weight_copies[3:]:
                    copy.wait()

        def lanes_of(p):
            return slice(p * pair_width, (p + 1) * pair_width)

        def scored(p):
            k_pair = keys[i, :, lanes_of(p)]
            stacked = jnp.concatenate([only(k_pair, 0), only(k_pair, 1)], axis=0)
            v_turned = values[i, :, lanes_of(p)].astype(jnp.float32).T.astype(jnp.bfloat16)
            return product_t(stacked, query[i, :, lanes_of(p)]), v_turned

        def weighed(p, both):
            for h in range(2):
                for span in spans:
                    scores = both[h * rows : (h + 1) * rows, span] + key_bias
                    expo = jnp.exp(scores - jnp.max(scores, axis=0, keepdims=True))
                    share = pltpu.reciprocal(jnp.sum(expo, axis=0, keepdims=True), approx=True)
                    probs[i, 2 * p + h, :, span] = (expo * share).astype(jnp.bfloat16)

        def mixed_values(p, v_turned):
            return [product(v_turned[h * head : (h + 1) * head], probs[i, 2 * p + h]) for h in range(2)]

        def place_context(p, parts):
            context[turn, :, lanes_of(p)] = jnp.concatenate(parts, axis=0).T.astype(jnp.bfloat16)

        def projected(group):
            lanes = slice(group * 2 * pair_width, (group + 1) * 2 * pair_width)
            return product(context[turn, :, lanes], wo[lanes, :])

        ahead = scored(0)
        parts = None
        attended = None
        for p in range(pairs):
            both, v_turned = ahead
            if p + 1 < pairs:
                ahead = scored(p + 1)
            if parts is not None:
                place_context(p - 1, parts)
            if p in (2, 4):
                if p == 2:
                    wait_rest()
                piece = projected(p // 2 - 1)
                attended = piece if attended is None else attended + piece
            weighed(p, both)
            parts = mixed_values(p, v_turned)
        place_context(pairs - 1, parts)
        attended += projected(pairs // 2 - 1)

        @pl.when((section == 0) & (core == 1) & (i >= 1))
        def _():
            forward_copy(i - 1).start()

        for at in blocks:
            n1, inv1 = normed(hidden[i, at, :].astype(jnp.float32) + attended[at] + vector(bo_ref))
            normal1[i, at, :] = n1.astype(jnp.bfloat16)
            inverses[i, at, 0:1] = inv1
            first = n1 * vector(g1_ref) + vector(s1_ref)
            lowered[turn, at, :] = first.astype(jnp.bfloat16)
            wide1[at, :] = first + vector(bd_ref)
        half = wide * width // 2

        def raised(n):
            return product(lowered[turn], wu[:, n * half : (n + 1) * half])

        def bend(n, z_tile):
            for part in range(0, half, width):
                lanes = slice(n * half + part, n * half + part + width)
                bias = bu_ref[:, lanes].astype(jnp.float32)
                for at in blocks:
                    gelu, slant = gelu_pair(z_tile[at, part : part + width] + bias)
                    active[turn, at, lanes] = gelu.astype(jnp.bfloat16)
                    slope[i, at, lanes] = slant.astype(jnp.bfloat16)

        z_first = raised(0)
        z_second = raised(1)
        bend(0, z_first)
        wide1[...] += product(active[turn, :, :half], wd[:half, :])
        bend(1, z_second)
        lowest = product(active[turn, :, half:], wd[half:, :])
        for at in blocks:
            n2, inv2 = normed(wide1[at, :] + lowest[at])
            normal2[i, at, :] = n2.astype(jnp.bfloat16)
            inverses[i, at, 1:2] = inv2
            result[i, at, :] = (n2 * vector(g2_ref) + vector(s2_ref)).astype(jnp.bfloat16)

    def folded(value):
        return value[: GROUP // 2] + value[GROUP // 2 :]

    def keep_small(row, value):
        small_ref[row : row + 1, :] += jnp.sum(value, axis=0, keepdims=True)

    def single(name, value):
        keep_small(SINGLES.index(name), value)

    def backward(i):
        slot = lax.rem(i, 2)
        base = (2 + wide) * width

        def stage(at, column, value):
            staged[slot, at, column * width : (column + 1) * width] = value

        def norm_step(at, gradient, normal, layer_norm, gain, sums):
            n = normal[i, at, :].astype(jnp.float32)
            d_res = normed_back(gradient * vector(gain), n, inverses[i, at, layer_norm : layer_norm + 1])
            d_low = d_res.astype(jnp.bfloat16)
            terms = [folded(gradient * n), folded(gradient), folded(d_low.astype(jnp.float32))]
            return d_res, d_low, terms if sums is None else [a + b for a, b in zip(sums, terms)]

        sums = None
        for at in blocks:
            gradient = upstream[i, at, :].astype(jnp.float32)
            d_res, d_low, sums = norm_step(at, gradient, normal2, 1, g2_ref, sums)
            wide1[at, :] = d_res
            stage(at, 0, d_low)
        for name, value in zip(("g2", "s2", "bd"), sums):
            single(name, value)
        d_out = staged[slot, :, :width]
        half = wide * width // 2

        def opened_half(n):
            return product(d_out, wd_t[:, n * half : (n + 1) * half])

        def bent_half(n, d_active):
            for part in range(0, half, width):
                j = (n * half + part) // width
                lanes = slice(j * width, (j + 1) * width)
                total = None
                for at in blocks:
                    d_inner = d_active[at, part : part + width] * slope[i, at, lanes].astype(jnp.float32)
                    d_inner = d_inner.astype(jnp.bfloat16)
                    stage(at, 1 + j, d_inner)
                    term = folded(d_inner.astype(jnp.float32))
                    total = term if total is None else total + term
                keep_small(len(SINGLES) + j, total)

        def closed_half(n):
            at = width + n * half
            return product(staged[slot, :, at : at + half], wu_t[n * half : (n + 1) * half, :])

        d_first = opened_half(0)
        d_second = opened_half(1)
        bent_half(0, d_first)
        d_deep = closed_half(0)
        bent_half(1, d_second)
        d_deeper = closed_half(1)
        sums = None
        for at in blocks:
            d_res, d_low, sums = norm_step(at, wide1[at, :] + d_deep[at] + d_deeper[at], normal1, 0, g1_ref, sums)
            wide1[at, :] = d_res
            stage(at, 1 + wide, d_low)
        for name, value in zip(("g1", "s1", "bo"), sums):
            single(name, value)
        d_att = staged[slot, :, (1 + wide) * width : (2 + wide) * width]
        @pl.when(i == 0)
        def _():
            save(items - 2, 0).wait()
            save(items - 1, 0).wait()

        active[0, :, :width] = product(d_att, wo_t[...]).astype(jnp.bfloat16)

        def lanes_of(p):
            return slice(p * pair_width, (p + 1) * pair_width)

        def place_grad(n, p, block):
            at = base + n * width + p * pair_width
            staged[slot, :, at : at + pair_width] = block.astype(jnp.bfloat16)

        def opened(p):
            v_pair = values[i, :, lanes_of(p)]
            c_pair = active[0, :, lanes_of(p)]
            stacked = jnp.concatenate([only(v_pair, 0), only(v_pair, 1)], axis=0)
            k_turned = keys[i, :, lanes_of(p)].astype(jnp.float32).T.astype(jnp.bfloat16)
            d_value = product(probs[i, 2 * p], only(c_pair, 0))
            d_value += product(probs[i, 2 * p + 1], only(c_pair, 1))
            return product_t(stacked, c_pair), k_turned, d_value

        def score_base(p, h):
            return (2 * (p % 2) + h) * 2 * 128

        def score_grads(p, both):
            for h in range(2):
                for span in spans:
                    prob = probs[i, 2 * p + h, :, span].astype(jnp.float32)
                    d_prob = both[h * rows : (h + 1) * rows, span]
                    drift = jnp.sum(d_prob * prob, axis=0, keepdims=True)
                    at = score_base(p, h)
                    active[1, :, at + span.start : at + span.stop] = (prob * (d_prob - drift)).astype(jnp.bfloat16)
            return [active[1, :, score_base(p, h) : score_base(p, h) + rows] for h in range(2)]

        def closed(p, found, k_turned):
            q_pair = query[i, :, lanes_of(p)]
            d_key = product(found[0], only(q_pair, 0)) + product(found[1], only(q_pair, 1))
            return d_key, [product(k_turned[h * head : (h + 1) * head], found[h]) for h in range(2)]

        def place_grads(p, d_value, d_key, parts):
            place_grad(0, p, jnp.concatenate(parts, axis=0).T * (1.0 / math.sqrt(head)))
            place_grad(1, p, d_key)
            place_grad(2, p, d_value)

        ahead = opened(0)
        waiting = None
        d_source = None

        def source_grad(group):
            found = None
            for n in range(3):
                at = n * width + group * 2 * pair_width
                piece = product(
                    staged[slot, :, base + at : base + at + 2 * pair_width], wqkv_t[at : at + 2 * pair_width, :]
                )
                found = piece if found is None else found + piece
            return found

        for p in range(pairs):
            both, k_turned, d_value = ahead
            if p + 1 < pairs:
                ahead = opened(p + 1)
            if waiting is not None:
                place_grads(*waiting)
            if p in (2, 4):
                piece = source_grad(p // 2 - 1)
                d_source = piece if d_source is None else d_source + piece
            found = score_grads(p, both)
            d_key, parts = closed(p, found, k_turned)
            waiting = (p, d_value, d_key, parts)
        place_grads(*waiting)
        d_source += source_grad(pairs // 2 - 1)
        sums = None
        for at in blocks:
            result[i, at, :] = (wide1[at, :] + d_source[at]).astype(jnp.bfloat16)
            terms = [
                folded(staged[slot, at, base : base + width].astype(jnp.float32)),
                folded(staged[slot, at, base + 2 * width : base + 3 * width].astype(jnp.float32)),
            ]
            sums = terms if sums is None else [a + b for a, b in zip(sums, terms)]
        single("bq", sums[0])
        single("bv", sums[1])

    small_ref[...] = jnp.zeros_like(small_ref)
    side = 256
    unit = lax.broadcasted_iota(jnp.int32, (side, side), 0) == lax.broadcasted_iota(jnp.int32, (side, side), 1)
    unit = jnp.where(unit, 1.0, 0.0).astype(jnp.bfloat16)

    def turn_weights():
        for natural, turned in ((wqkv, wqkv_t), (wo, wo_t), (wu, wu_t), (wd, wd_t)):
            for block in range(0, natural.shape[0], width):

                def one(n, carry):
                    at = pl.ds(pl.multiple_of(n * side, side), side)
                    tall = product_t(unit, natural[block : block + width, at])
                    turned[at, block : block + width] = tall.astype(jnp.bfloat16)
                    return carry

                lax.fori_loop(0, natural.shape[1] // side, one, 0)

    @pl.when(section == 1)
    def _():
        for copy in weight_copies:
            copy.wait()
        turn_weights()

    def forward_step(i, carry):
        @pl.when(section == 0)
        def _():
            assemble(i)

        @pl.when(section == 1)
        def _():
            forward_copy(i).wait_recv()

        @pl.when(i >= 2)
        def _():
            for n in range(3):
                save(i - 2, n).wait()

        forward(i)

        @pl.when((section == 0) & ((core == 0) | (i == items - 1)))
        def _():
            forward_copy(i).start()

        for n in range(5):
            save(i, n).start()
        return carry

    lax.fori_loop(0, items, forward_step, 0)

    @pl.when(section == 0)
    def _():
        turn_weights()

    @pl.when(section == 1)
    def _():
        cotangent_copy.wait()

    def backward_step(i, carry):
        @pl.when(section == 0)
        def _():
            back_copy(i).wait_recv()

        @pl.when(i >= 2)
        def _():
            staged_save(i - 2).wait()

        save(i, 4).wait()

        @pl.when(section == 0)
        def _():
            forward_copy(i).wait_send()

        backward(i)

        @pl.when(section == 1)
        def _():
            back_copy(i).start()

        staged_save(i).start()
        grad_save(i).start()
        return carry

    lax.fori_loop(0, items, backward_step, 0)

    def finish(i, carry):
        save(i, 3).wait()
        grad_save(i).wait()

        @pl.when(i >= items - 2)
        def _():
            staged_save(i).wait()
            for n in range(1, 3):
                save(i, n).wait()

        @pl.when(section == 1)
        def _():
            back_copy(i).wait_send()

        return carry

    lax.fori_loop(0, items, finish, 0)


def layered(image_ids, caption_lengths, captions, regions, cotangent, stacked):
    items, cap_rows, width = captions.shape
    held, region_rows, _ = regions.shape
    rows = cap_rows + region_rows
    inner = stacked[9].shape[2]
    low = jnp.bfloat16
    wide = inner // width

    def cells(*shape):
        return pltpu.VMEM(shape, low)

    anywhere = pl.BlockSpec(memory_space=pl.ANY)
    local = pl.BlockSpec(memory_space=pltpu.VMEM)
    scalars = pl.BlockSpec(memory_space=pltpu.SMEM)
    return pl.pallas_call(
        layer_kernel,
        out_shape=(
            jax.ShapeDtypeStruct((1, items, rows, width), low),
            jax.ShapeDtypeStruct((1, items, rows, width), low),
            jax.ShapeDtypeStruct((items * rows, (3 + wide) * width), low),
            jax.ShapeDtypeStruct((items * rows, (5 + wide) * width), low),
            jax.ShapeDtypeStruct((GROUP, width), jnp.float32),
        ),
        in_specs=[scalars, scalars, anywhere, local, anywhere]
        + [anywhere if len(member.shape) == 3 else local for member in stacked],
        out_specs=(anywhere, anywhere, anywhere, anywhere, local),
        scratch_shapes=[
            cells(width, 3 * width),
            cells(width, width),
            cells(width, inner),
            cells(inner, width),
            cells(3 * width, width),
            cells(width, width),
            cells(inner, width),
            cells(width, inner),
            cells(3 * held, region_rows, width),
            cells(items, rows, width),
            cells(items, rows, width),
            cells(items, rows, width),
            cells(items, rows, width),
            cells(items, rows, width),
            cells(items, HEADS, rows, rows),
            cells(2, rows, width),
            cells(items, rows, width),
            cells(items, rows, width),
            cells(2, rows, width),
            cells(2, rows, inner),
            cells(items, rows, inner),
            cells(items, rows, width),
            cells(2, rows, (5 + wide) * width),
            pltpu.VMEM((items, rows, 2), jnp.float32),
            pltpu.VMEM((rows, width), jnp.float32),
            cells(cap_rows, items, width),
            pltpu.SemaphoreType.DMA((8,)),
            pltpu.SemaphoreType.DMA((2,)),
            pltpu.SemaphoreType.DMA((2,)),
            pltpu.SemaphoreType.DMA((items,)),
            pltpu.SemaphoreType.DMA((items,)),
            pltpu.SemaphoreType.DMA((items,)),
            pltpu.SemaphoreType.DMA((items,)),
            pltpu.SemaphoreType.DMA((items, 7)),
        ],
        compiler_params=pltpu.CompilerParams(
            collective_id=0, has_side_effects=True, vmem_limit_bytes=VMEM_LIMIT
        ),
        cost_estimate=pl.CostEstimate(
            flops=4 * items * rows * (4 + 2 * wide) * width * width,
            bytes_accessed=60_000_000,
            transcendentals=0,
        ),
    )(image_ids, caption_lengths, captions.transpose(1, 0, 2), regions, cotangent, *stacked)


def body(
    captions,
    regions,
    image_ids,
    caption_lengths,
    cotangent,
    query_weight,
    query_bias,
    key_weight,
    value_weight,
    value_bias,
    out_weight,
    out_bias,
    norm1_gain,
    norm1_bias,
    up_weight,
    up_bias,
    down_weight,
    down_bias,
    norm2_gain,
    norm2_bias,
):
    stacked = (
        query_weight,
        query_bias,
        key_weight,
        value_weight,
        value_bias,
        out_weight,
        out_bias,
        norm1_gain,
        norm1_bias,
        up_weight,
        up_bias,
        down_weight,
        down_bias,
        norm2_gain,
        norm2_bias,
    )
    width = captions.shape[2]
    states, input_grads, a_side, b_side, small = layered(
        image_ids, caption_lengths, captions, regions, cotangent, stacked
    )
    sums, small_sums = reduced(a_side, b_side, small, lax.axis_size("batch"))
    return tuple(spread(sums.reshape(-1, width), small_sums, states, input_grads, stacked))


def solution(mesh):
    placed = (
        P("batch", None, None),
        P("batch", None, None),
        P("batch"),
        P("batch"),
        P("batch", None, None),
        P("section", None, None),
        P("section", None),
        P("section", None, None),
        P("section", None, None),
        P("section", None),
        P("section", None, None),
        P("section", None),
        P("section", None),
        P("section", None),
        P("section", None, None),
        P("section", None),
        P("section", None, None),
        P("section", None),
        P("section", None),
        P("section", None),
    )
    return jax.shard_map(
        body,
        mesh=mesh,
        in_specs=placed,
        out_specs=(
            P("section", "batch", None, None),
            P("section", "batch", None, None),
            P("section", None, None),
            P("section", None),
            P("section", None, None),
            P("section", None, None),
            P("section", None),
            P("section", None, None),
            P("section", None),
            P("section", None),
            P("section", None),
            P("section", None, None),
            P("section", None),
            P("section", None, None),
            P("section", None),
            P("section", None),
            P("section", None),
        ),
        check_vma=False,
    )
```

```python
import functools
import math

import jax
import jax.numpy as jnp
from jax import lax
from jax.experimental import pallas as pl
from jax.experimental.pallas import tpu as pltpu
from jax.sharding import PartitionSpec as P

HEADS = 12
EPSILON = 1e-12
MESH = pl.DeviceIdType.MESH
VMEM_LIMIT = 63 * 1024 * 1024
VMEM_BESIDE = 47 * 1024 * 1024
GROUP = 16
CHUNK_GROUPS = 16
SLOTS = 18
SLOT_GROUPS = 24
LAG = 3
CYCLE = 3
LINE = 4
SPLIT_BITS = 4


def reduce_kernel(
    bits,
    chunks,
    a_hbm,
    b_hbm,
    small_ref,
    whole,
    small_out,
    a_ref,
    b_ref,
    acc,
    recv,
    small_acc,
    small_recv,
    load_sem,
    send_sem,
    recv_sem,
    small_send_sem,
    small_recv_sem,
):
    width = acc.shape[2]
    extra = bits - SPLIT_BITS
    first_gather = SPLIT_BITS + 1 + extra
    stages = 2 * (SPLIT_BITS + 1) + extra
    me = lax.axis_index("batch")
    section = lax.axis_index("section")
    core, side, place = me % 2, (me // 2) % 2, (me // 4) % LINE
    blocks_a = a_hbm.shape[1] // width
    blocks_b = b_hbm.shape[1] // width
    per_block = width // (CHUNK_GROUPS * GROUP)

    def load(source, target, block, base):
        lanes = pl.ds(block * width, width)
        return pltpu.make_async_copy(source.at[:, lanes], target.at[:, lanes], load_sem.at[base + block])

    def load_a(block):
        return load(a_hbm, a_ref, block, 0)

    def load_b(block):
        return load(b_hbm, b_ref, block, blocks_a)

    wide = blocks_a - 3
    first_use = {0: [(load_a, 0), (load_b, 0)]}
    for j in range(1, wide):
        first_use[j] = [(load_a, j)]
    first_use[wide] = [(load_a, wide), (load_b, 1)]
    for j in range(1, wide):
        first_use[wide + j] = [(load_b, 1 + j)]
    first_use[2 * wide] = [(load_a, wide + 1), (load_b, wide + 1)]
    first_use[2 * wide + 1] = [(load_a, wide + 2), (load_b, wide + 2)]
    first_use[2 * wide + 2] = [(load_b, wide + 3)]
    first_use[2 * wide + 3] = [(load_b, wide + 4)]
    for j in range(2 * wide + 4):
        for kind, block in first_use[j]:
            kind(block).start()

    def bit_mate(k):
        bit = (me // 2**k) % 2
        return (section, me + 2**k * (1 - 2 * bit))

    core_mate, side_mate = bit_mate(0), bit_mate(1)
    mates = ((section, me - LINE), (section, me + LINE))
    ring = [(section, me + LINE * ((place + d) % LINE - place)) for d in (LINE - 1, 1)]

    barrier = pltpu.get_barrier_semaphore()
    for peer in [core_mate, side_mate] + ring + [bit_mate(k) for k in range(2, bits)]:
        pl.semaphore_signal(barrier, inc=1, device_id=peer, device_id_type=MESH)
    pl.semaphore_wait(barrier, bits + 2)

    def low_core(c):
        return c * CHUNK_GROUPS + core * 8

    def low_side(c):
        return low_core(c) + side * 4

    def block_start(c, kind, b):
        return low_side(c) + b if kind == 0 else low_core(c) + 2 * b

    def final(c, kind):
        return low_side(c) + place if kind == 0 else low_core(c) + 2 * place + side

    def remote(c, source, start, size, target, spot, index, peer):
        return pltpu.make_async_remote_copy(
            src_ref=source.at[pl.ds(start, size)],
            dst_ref=target.at[lax.rem(c, SLOTS), pl.ds(spot, size)] if target is recv else target.at[pl.ds(start, size)],
            send_sem=send_sem.at[lax.rem(c, SLOTS), index],
            recv_sem=recv_sem.at[lax.rem(c, SLOTS), index],
            device_id=peer,
            device_id_type=MESH,
        )

    def core_copy(c):
        return remote(c, acc, c * CHUNK_GROUPS + (1 - core) * 8, 8, recv, 0, 0, core_mate)

    def side_copy(c, kind):
        if kind == 0:
            return remote(c, acc, low_core(c) + (1 - side) * 4, 4, recv, 8, 1, side_mate)
        return remote(c, acc, low_core(c) + 2 * place + (1 - side), 1, recv, 8, 1, side_mate)

    def line_copy(c, kind, r, d):
        size = 1 + kind
        b = jnp.minimum(3 - r + place, 3) if d == 1 else jnp.maximum(r - 3 + place, 0)
        spot = 12 + 2 * (2 * r + d)
        return remote(c, acc, block_start(c, kind, b), size, recv, spot, 2 + 2 * r + d, mates[d])

    def spread_copy(c, kind, r, d):
        size = 1 + kind
        b = jnp.maximum(place - r, 0) if d == 1 else jnp.minimum(place + r, 3)
        return remote(c, whole, block_start(c, kind, b), size, whole, 0, 8 + 2 * r + d, mates[d])

    def side_back_copy(c, kind):
        if kind == 0:
            return remote(c, whole, low_side(c), 4, whole, 0, 14, side_mate)
        return remote(c, whole, final(c, kind), 1, whole, 0, 14, side_mate)

    def core_back_copy(c):
        return remote(c, whole, low_core(c), 8, whole, 0, 15, core_mate)

    def extra_copy(c, kind, e):
        return remote(c, acc, final(c, kind), 1, recv, 24 + e, 16 + e, bit_mate(SPLIT_BITS + e))

    def add_groups(start, count, c, spot):
        slot = lax.rem(c, SLOTS)
        for g in range(count):
            total = acc[start + g].astype(jnp.float32) + recv[slot, spot + g].astype(jnp.float32)
            acc[start + g] = total.astype(jnp.bfloat16)

    def name_of(kind, s):
        if s == 0:
            return ("core",)
        if s == stages - 1:
            return ("core_back",)
        if s < SPLIT_BITS + 1:
            order = [("side",), ("line", 0), ("line", 1), ("line", 2)]
            order = order if kind == 0 else order[1:] + order[:1]
            return order[s - 1]
        if s < first_gather:
            return ("extra", s - SPLIT_BITS - 1)
        order = [("spread", 0), ("spread", 1), ("spread", 2), ("side_back",)]
        order = order if kind == 0 else order[3:] + order[:3]
        return order[s - first_gather]

    def start_stage(c, kind, s):
        name = name_of(kind, s)
        if s == first_gather:
            whole[final(c, kind)] = acc[final(c, kind)]
        if name[0] == "core":
            core_copy(c).start()
        elif name[0] == "side":
            side_copy(c, kind).start()
        elif name[0] == "line":
            r = name[1]
            pl.when(place <= r)(lambda: line_copy(c, kind, r, 1).start())
            pl.when(place >= 3 - r)(lambda: line_copy(c, kind, r, 0).start())
        elif name[0] == "extra":
            extra_copy(c, kind, name[1]).start()
        elif name[0] == "spread":
            r = name[1]
            pl.when((place >= r) & (place <= 2))(lambda: spread_copy(c, kind, r, 1).start())
            pl.when((place >= 1) & (place <= 3 - r))(lambda: spread_copy(c, kind, r, 0).start())
        elif name[0] == "side_back":
            side_back_copy(c, kind).start()
        else:
            core_back_copy(c).start()

    def finish_stage(c, kind, s):
        name = name_of(kind, s)
        if name[0] == "core":
            core_copy(c).wait()
            add_groups(low_core(c), 8, c, 0)
        elif name[0] == "side":
            side_copy(c, kind).wait()
            if kind == 0:
                add_groups(low_side(c), 4, c, 8)
            else:
                add_groups(final(c, kind), 1, c, 8)
        elif name[0] == "line":
            r = name[1]

            @pl.when(place <= r)
            def _():
                line_copy(c, kind, r, 1).wait_send()

            @pl.when(place >= 3 - r)
            def _():
                line_copy(c, kind, r, 0).wait_send()

            @pl.when((place >= 1) & (place <= r + 1))
            def _():
                line_copy(c, kind, r, 1).wait_recv()
                add_groups(block_start(c, kind, 2 - r + place), 1 + kind, c, 12 + 2 * (2 * r + 1))

            @pl.when((place <= 2) & (place >= 2 - r))
            def _():
                line_copy(c, kind, r, 0).wait_recv()
                add_groups(block_start(c, kind, r - 2 + place), 1 + kind, c, 12 + 2 * (2 * r))

        elif name[0] == "extra":
            extra_copy(c, kind, name[1]).wait()
            add_groups(final(c, kind), 1, c, 24 + name[1])
        elif name[0] == "spread":
            r = name[1]
            pl.when((place >= r) & (place <= 2))(lambda: spread_copy(c, kind, r, 1).wait_send())
            pl.when((place >= 1) & (place <= 3 - r))(lambda: spread_copy(c, kind, r, 0).wait_send())
            pl.when(place >= r + 1)(lambda: spread_copy(c, kind, r, 1).wait_recv())
            pl.when(place <= 2 - r)(lambda: spread_copy(c, kind, r, 0).wait_recv())
        elif name[0] == "side_back":
            side_back_copy(c, kind).wait()
        else:
            core_back_copy(c).wait()

    def small_copy(k):
        return pltpu.make_async_remote_copy(
            src_ref=small_acc.at[k],
            dst_ref=small_recv.at[k],
            send_sem=small_send_sem.at[k],
            recv_sem=small_recv_sem.at[k],
            device_id=bit_mate(k),
            device_id_type=MESH,
        )

    small_acc[0] = small_ref[...]

    def step(t, phase):
        for s in range(stages, 0, -1):
            c = t - LAG * s
            kind = (phase - LAG * s) % CYCLE // 2

            @pl.when((c >= 0) & (c < chunks))
            def _():
                finish_stage(c, kind, s - 1)
                if s < stages:
                    start_stage(c, kind, s)

        for j in range(2 * wide + 4):

            @pl.when(t == per_block * j)
            def _():
                for kind, block in first_use[j]:
                    kind(block).wait()

        @pl.when(t < chunks)
        def _():
            block, part = t // per_block, t % per_block
            a_col = jnp.minimum(block, wide) + jnp.minimum(block // (2 * wide), 1) + jnp.minimum(block // (2 * wide + 1), 1)
            b_col = jnp.maximum(block - wide + 1, 0)
            lines = CHUNK_GROUPS * GROUP
            left = a_ref[:, pl.ds(pl.multiple_of(a_col * width + part * lines, lines), lines)]
            right = b_ref[:, pl.ds(pl.multiple_of(b_col * width, width), width)]
            grad = lax.dot_general(left, right, (((0,), (0,)), ((), ())), preferred_element_type=jnp.float32)
            acc[pl.ds(t * CHUNK_GROUPS, CHUNK_GROUPS)] = grad.astype(jnp.bfloat16).reshape(
                CHUNK_GROUPS, GROUP, width
            )
            core_copy(t).start()

        for k in range(bits + 1):

            @pl.when(t == LAG * k)
            def _():
                if k > 0:
                    small_copy(k - 1).wait()
                    small_acc[k] = small_acc[k - 1] + small_recv[k - 1]
                if k < bits:
                    small_copy(k).start()

    def cycle(n, carry):
        for phase in range(CYCLE):
            step(n * CYCLE + phase, phase)
        return carry

    lax.fori_loop(0, pl.cdiv(chunks + LAG * stages, CYCLE), cycle, 0)
    small_out[...] = small_acc[bits]


def reduced(a_side, b_side, small, count):
    rows = a_side.shape[0]
    width = small.shape[1]
    bits = count.bit_length() - 1
    extra = bits - SPLIT_BITS
    blocks = 2 * (a_side.shape[1] // width - 3) + 4
    chunks = blocks * width // (CHUNK_GROUPS * GROUP)
    groups = chunks * CHUNK_GROUPS
    loads = (a_side.shape[1] + b_side.shape[1]) // width
    return pl.pallas_call(
        functools.partial(reduce_kernel, bits, chunks),
        out_shape=(
            pltpu.VMEM((groups, GROUP, width), jnp.bfloat16),
            jax.ShapeDtypeStruct(small.shape, jnp.float32),
        ),
        in_specs=[
            pl.BlockSpec(memory_space=pl.ANY),
            pl.BlockSpec(memory_space=pl.ANY),
            pl.BlockSpec(memory_space=pltpu.VMEM),
        ],
        out_specs=(pl.BlockSpec(memory_space=pltpu.VMEM), pl.BlockSpec(memory_space=pltpu.VMEM)),
        scratch_shapes=[
            pltpu.VMEM(a_side.shape, jnp.bfloat16),
            pltpu.VMEM(b_side.shape, jnp.bfloat16),
            pltpu.VMEM((groups, GROUP, width), jnp.bfloat16),
            pltpu.VMEM((SLOTS, SLOT_GROUPS + extra, GROUP, width), jnp.bfloat16),
            pltpu.VMEM((bits + 1,) + small.shape, jnp.float32),
            pltpu.VMEM((bits,) + small.shape, jnp.float32),
            pltpu.SemaphoreType.DMA((loads,)),
            pltpu.SemaphoreType.DMA((SLOTS, 16 + extra)),
            pltpu.SemaphoreType.DMA((SLOTS, 16 + extra)),
            pltpu.SemaphoreType.DMA((bits,)),
            pltpu.SemaphoreType.DMA((bits,)),
        ],
        compiler_params=pltpu.CompilerParams(
            collective_id=1, has_side_effects=True, vmem_limit_bytes=VMEM_BESIDE
        ),
        cost_estimate=pl.CostEstimate(
            flops=2 * rows * blocks * width * width, bytes_accessed=80_000_000, transcendentals=0
        ),
    )(a_side, b_side, small)


PIECE = 384
DEPTH = 4


def spread_kernel(sum_ref, small_ref, states_hbm, grads_hbm, *refs):
    width = small_ref.shape[1]
    (o_wq, o_bq, o_wk, o_wv, o_bv, o_wo, o_bo, o_g1, o_s1, o_up, o_bu, o_dn, o_bd, o_g2, o_s2) = refs[2:17]
    states_out, grads_out = refs[:2]
    given, held, out_sem, held_sem = refs[17:]
    wide = o_bu.shape[1] // width
    targets = []
    for j in range(wide):
        targets += [o_dn.at[0, pl.ds(j * width + r, PIECE), :] for r in range(0, width, PIECE)]
    for j in range(wide):
        targets += [o_up.at[0, pl.ds(r, PIECE), pl.ds(j * width, width)] for r in range(0, width, PIECE)]
    for ref in (o_wo, o_wq, o_wk, o_wv):
        targets += [ref.at[0, pl.ds(r, PIECE), :] for r in range(0, width, PIECE)]

    items = states_hbm.shape[1]
    passes = [(states_hbm.at[0, i], states_out.at[0, i]) for i in range(items)]
    passes += [(grads_hbm.at[0, i], grads_out.at[0, i]) for i in range(items)]

    def pass_in(i):
        return pltpu.make_async_copy(passes[i][0], held.at[i], held_sem.at[i])

    def pass_out(i):
        return pltpu.make_async_copy(held.at[i], passes[i][1], held_sem.at[i])

    def store(i):
        return pltpu.make_async_copy(given.at[i % DEPTH], targets[i], out_sem.at[i % DEPTH])

    for i in range(len(passes)):
        pass_in(i).start()
    singles = [o_bq, o_bv, o_bo, o_g1, o_s1, o_bd, o_g2, o_s2]
    for i, ref in enumerate(singles):
        ref[...] = small_ref[pl.ds(i, 1), :]
    for j in range(wide):
        o_bu[:, pl.ds(j * width, width)] = small_ref[pl.ds(len(singles) + j, 1), :]
    for i in range(len(targets)):
        if i >= DEPTH:
            store(i - DEPTH).wait()

        def convert(r, carry):
            block = sum_ref[pl.ds(i * (PIECE // GROUP) + r * 4, 4)].astype(jnp.float32)
            rows = pl.ds(pl.multiple_of(r * 4 * GROUP, 4 * GROUP), 4 * GROUP)
            given[i % DEPTH, rows, :] = block.reshape(4 * GROUP, width)
            return carry

        lax.fori_loop(0, PIECE // (4 * GROUP), convert, 0)
        store(i).start()
        if i < len(passes):
            pass_in(i).wait()
            pass_out(i).start()
    for i in range(len(targets) - DEPTH, len(targets)):
        store(i).wait()
    for i in range(len(passes)):
        pass_out(i).wait()


def spread(sums, small, states, input_grads, params):
    width = small.shape[1]
    anywhere = pl.BlockSpec(memory_space=pl.ANY)
    local = pl.BlockSpec(memory_space=pltpu.VMEM)
    return pl.pallas_call(
        spread_kernel,
        out_shape=(
            jax.ShapeDtypeStruct(states.shape, states.dtype),
            jax.ShapeDtypeStruct(input_grads.shape, input_grads.dtype),
        )
        + tuple(jax.ShapeDtypeStruct(member.shape, jnp.float32) for member in params),
        in_specs=[local, local, anywhere, anywhere],
        out_specs=(anywhere, anywhere)
        + tuple(anywhere if len(member.shape) == 3 else local for member in params),
        scratch_shapes=[
            pltpu.VMEM((DEPTH, PIECE, width), jnp.float32),
            pltpu.VMEM((2 * states.shape[1],) + states.shape[2:], states.dtype),
            pltpu.SemaphoreType.DMA((DEPTH,)),
            pltpu.SemaphoreType.DMA((2 * states.shape[1],)),
        ],
        compiler_params=pltpu.CompilerParams(vmem_limit_bytes=VMEM_BESIDE),
        cost_estimate=pl.CostEstimate(
            flops=12 * width * width, bytes_accessed=80 * width * width, transcendentals=0
        ),
    )(pltpu.with_memory_space_constraint(sums, pltpu.VMEM), small, states, input_grads)


HALF_LOG = -0.5 / math.log(2.0)
BELL_SCALE = 1.0 / math.sqrt(2.0 * math.pi)
SINGLES = ("bq", "bv", "bo", "g1", "s1", "bd", "g2", "s2")


def product(left, right):
    return lax.dot_general(left, right, (((1,), (0,)), ((), ())), preferred_element_type=jnp.float32)


def product_t(left, right):
    return lax.dot_general(left, right, (((1,), (1,)), ((), ())), preferred_element_type=jnp.float32)


def gelu_pair(z):
    cdf = 0.5 * lax.erf(z * (1.0 / math.sqrt(2.0))) + 0.5
    bell = jnp.exp2(z * z * HALF_LOG)
    return z * cdf, z * BELL_SCALE * bell + cdf


def normed(values):
    average = jnp.mean(values, axis=-1, keepdims=True)
    centered = values - average
    inverse = lax.rsqrt(jnp.mean(centered * centered, axis=-1, keepdims=True) + EPSILON)
    return centered * inverse, inverse


def normed_back(grad, normal, inverse):
    first_mean = jnp.mean(grad, axis=-1, keepdims=True)
    second_mean = jnp.mean(grad * normal, axis=-1, keepdims=True)
    return inverse * (grad - first_mean - normal * second_mean)


def layer_kernel(
    ids_ref,
    lengths_ref,
    captions_hbm,
    regions_ref,
    cotangent_hbm,
    wq_hbm,
    bq_ref,
    wk_hbm,
    wv_hbm,
    bv_ref,
    wo_hbm,
    bo_ref,
    g1_ref,
    s1_ref,
    wu_hbm,
    bu_ref,
    wd_hbm,
    bd_ref,
    g2_ref,
    s2_ref,
    states_hbm,
    grads_hbm,
    a_hbm,
    b_hbm,
    small_ref,
    wqkv,
    wo,
    wu,
    wd,
    wqkv_t,
    wo_t,
    wu_t,
    wd_t,
    table,
    hidden,
    upstream,
    query,
    keys,
    values,
    probs,
    context,
    normal1,
    normal2,
    lowered,
    active,
    slope,
    result,
    staged,
    inverses,
    wide1,
    caption_cells,
    weight_sem,
    table_send,
    table_recv,
    fwd_send,
    fwd_recv,
    back_send,
    back_recv,
    out_sem,
):
    items, rows, width = hidden.shape
    held = regions_ref.shape[0]
    cap_rows = captions_hbm.shape[0]
    wide = wu.shape[1] // width
    pairs = HEADS // 2
    pair_width = width // pairs
    head = width // HEADS
    section = lax.axis_index("section")
    batch = lax.axis_index("batch")
    count = lax.axis_size("batch")
    right = (section, lax.rem(batch + 1, count))
    left = (section, lax.rem(batch + count - 1, count))
    other = (1 - section, batch)
    core = lax.rem(batch, 2)

    weight_copies = [
        pltpu.make_async_copy(source.at[0], target, weight_sem.at[n])
        for n, (source, target) in enumerate(
            (
                (wq_hbm, wqkv.at[:, pl.ds(0, width)]),
                (wk_hbm, wqkv.at[:, pl.ds(width, width)]),
                (wv_hbm, wqkv.at[:, pl.ds(2 * width, width)]),
                (wo_hbm, wo),
                (wu_hbm, wu),
                (wd_hbm, wd),
            )
        )
    ]
    for copy in weight_copies[:3]:
        copy.start()
    cotangent_copy = pltpu.make_async_copy(cotangent_hbm, upstream, weight_sem.at[6])

    barrier = pltpu.get_barrier_semaphore()
    for peer in (right, left, other):
        pl.semaphore_signal(barrier, inc=1, device_id=peer, device_id_type=MESH)
    pl.semaphore_wait(barrier, 3)

    def table_copy(n, peer):
        return pltpu.make_async_remote_copy(
            src_ref=regions_ref,
            dst_ref=table.at[pl.ds(2 * n * held, held)],
            send_sem=table_send.at[n],
            recv_sem=table_recv.at[n],
            device_id=peer,
            device_id_type=MESH,
        )

    @pl.when(section == 0)
    def _():
        caption_copy = pltpu.make_async_copy(captions_hbm, caption_cells, weight_sem.at[7])
        caption_copy.start()
        table_copy(0, right).start()
        table_copy(1, left).start()
        table[pl.ds(held, held)] = regions_ref[...]
        table_copy(0, right).wait()
        table_copy(1, left).wait()
        caption_copy.wait()

    for copy in weight_copies[3:]:
        copy.start()

    @pl.when(section == 1)
    def _():
        cotangent_copy.start()

    def forward_copy(i):
        return pltpu.make_async_remote_copy(
            src_ref=result.at[i],
            dst_ref=hidden.at[i],
            send_sem=fwd_send.at[i],
            recv_sem=fwd_recv.at[i],
            device_id=other,
            device_id_type=MESH,
        )

    def back_copy(i):
        return pltpu.make_async_remote_copy(
            src_ref=result.at[i],
            dst_ref=upstream.at[i],
            send_sem=back_send.at[i],
            recv_sem=back_recv.at[i],
            device_id=other,
            device_id_type=MESH,
        )

    def save(i, n):
        at = pl.ds(pl.multiple_of(i * rows, rows), rows)
        first = wide * width
        turn = lax.rem(i, 2)
        if n == 0:
            source, target = active.at[turn], a_hbm.at[at, pl.ds(0, first)]
        elif n == 1:
            source, target = lowered.at[turn], a_hbm.at[at, pl.ds(first, width)]
        elif n == 2:
            source, target = context.at[turn], a_hbm.at[at, pl.ds(first + width, width)]
        elif n == 3:
            source, target = hidden.at[i], a_hbm.at[at, pl.ds(first + 2 * width, width)]
        else:
            source, target = result.at[i], states_hbm.at[0, i]
        return pltpu.make_async_copy(source, target, out_sem.at[i, n])

    def staged_save(i):
        at = pl.ds(pl.multiple_of(i * rows, rows), rows)
        return pltpu.make_async_copy(staged.at[lax.rem(i, 2)], b_hbm.at[at], out_sem.at[i, 5])

    def grad_save(i):
        return pltpu.make_async_copy(result.at[i], grads_hbm.at[0, i], out_sem.at[i, 6])

    def vector(ref, j=0):
        return ref[:, j * width : (j + 1) * width].astype(jnp.float32)

    lane = lax.broadcasted_iota(jnp.int32, (rows, pair_width), 1)

    blocks = [slice(r, r + GROUP) for r in range(0, rows, GROUP)]
    spans = [slice(c, min(c + 128, rows)) for c in range(0, rows, 128)]

    def only(block, h):
        return jnp.where((lane // head) == h, block, jnp.zeros_like(block))

    def assemble(i):
        total = count * held
        spot = jnp.minimum(lax.rem(ids_ref[i] - (batch - 1) * held + total, total), 3 * held - 1)
        for n in range(items):

            @pl.when(i == n)
            def _():
                whole = jnp.concatenate(
                    [caption_cells[:, n, :].astype(jnp.float32), table[spot].astype(jnp.float32)], axis=0
                )
                hidden[n] = whole.astype(jnp.bfloat16)

    def forward(i):
        @pl.when((i == 0) & (section == 0))
        def _():
            for copy in weight_copies[:3]:
                copy.wait()

        turn = lax.rem(i, 2)
        source = hidden[i]
        mixed = product(source, wqkv[...])
        for at in blocks:
            scaled = (mixed[at, :width] + vector(bq_ref)) * (1.0 / math.sqrt(head))
            query[i, at, :] = scaled.astype(jnp.bfloat16)
            keys[i, at, :] = mixed[at, width : 2 * width].astype(jnp.bfloat16)
            values[i, at, :] = (mixed[at, 2 * width :] + vector(bv_ref)).astype(jnp.bfloat16)
        position = lax.broadcasted_iota(jnp.int32, (rows, 1), 0)
        live = (position >= cap_rows) | (position < lengths_ref[i])
        key_bias = jnp.where(live, 0.0, -1000000000.0)

        def wait_rest():
            @pl.when((i == 0) & (section == 0))
            def _():
                for copy in weight_copies[3:]:
                    copy.wait()

        def lanes_of(p):
            return slice(p * pair_width, (p + 1) * pair_width)

        def scored(p):
            k_pair = keys[i, :, lanes_of(p)]
            stacked = jnp.concatenate([only(k_pair, 0), only(k_pair, 1)], axis=0)
            v_turned = values[i, :, lanes_of(p)].astype(jnp.float32).T.astype(jnp.bfloat16)
            return product_t(stacked, query[i, :, lanes_of(p)]), v_turned

        def weighed(p, both):
            for h in range(2):
                for span in spans:
                    scores = both[h * rows : (h + 1) * rows, span] + key_bias
                    expo = jnp.exp(scores - jnp.max(scores, axis=0, keepdims=True))
                    share = pltpu.reciprocal(jnp.sum(expo, axis=0, keepdims=True), approx=True)
                    probs[i, 2 * p + h, :, span] = (expo * share).astype(jnp.bfloat16)

        def mixed_values(p, v_turned):
            return [product(v_turned[h * head : (h + 1) * head], probs[i, 2 * p + h]) for h in range(2)]

        def place_context(p, parts):
            context[turn, :, lanes_of(p)] = jnp.concatenate(parts, axis=0).T.astype(jnp.bfloat16)

        def projected(group):
            lanes = slice(group * 2 * pair_width, (group + 1) * 2 * pair_width)
            return product(context[turn, :, lanes], wo[lanes, :])

        ahead = scored(0)
        parts = None
        attended = None
        for p in range(pairs):
            both, v_turned = ahead
            if p + 1 < pairs:
                ahead = scored(p + 1)
            if parts is not None:
                place_context(p - 1, parts)
            if p in (2, 4):
                if p == 2:
                    wait_rest()
                piece = projected(p // 2 - 1)
                attended = piece if attended is None else attended + piece
            weighed(p, both)
            parts = mixed_values(p, v_turned)
        place_context(pairs - 1, parts)
        attended += projected(pairs // 2 - 1)

        @pl.when((section == 0) & (core == 1) & (i >= 1))
        def _():
            forward_copy(i - 1).start()

        for at in blocks:
            n1, inv1 = normed(hidden[i, at, :].astype(jnp.float32) + attended[at] + vector(bo_ref))
            normal1[i, at, :] = n1.astype(jnp.bfloat16)
            inverses[i, at, 0:1] = inv1
            first = n1 * vector(g1_ref) + vector(s1_ref)
            lowered[turn, at, :] = first.astype(jnp.bfloat16)
            wide1[at, :] = first + vector(bd_ref)
        half = wide * width // 2

        def raised(n):
            return product(lowered[turn], wu[:, n * half : (n + 1) * half])

        def bend(n, z_tile):
            for part in range(0, half, width):
                lanes = slice(n * half + part, n * half + part + width)
                bias = bu_ref[:, lanes].astype(jnp.float32)
                for at in blocks:
                    gelu, slant = gelu_pair(z_tile[at, part : part + width] + bias)
                    active[turn, at, lanes] = gelu.astype(jnp.bfloat16)
                    slope[i, at, lanes] = slant.astype(jnp.bfloat16)

        z_first = raised(0)
        z_second = raised(1)
        bend(0, z_first)
        wide1[...] += product(active[turn, :, :half], wd[:half, :])
        bend(1, z_second)
        lowest = product(active[turn, :, half:], wd[half:, :])
        for at in blocks:
            n2, inv2 = normed(wide1[at, :] + lowest[at])
            normal2[i, at, :] = n2.astype(jnp.bfloat16)
            inverses[i, at, 1:2] = inv2
            result[i, at, :] = (n2 * vector(g2_ref) + vector(s2_ref)).astype(jnp.bfloat16)

    def folded(value):
        return value[: GROUP // 2] + value[GROUP // 2 :]

    def keep_small(row, value):
        small_ref[row : row + 1, :] += jnp.sum(value, axis=0, keepdims=True)

    def single(name, value):
        keep_small(SINGLES.index(name), value)

    def backward(i):
        slot = lax.rem(i, 2)
        base = (2 + wide) * width

        def stage(at, column, value):
            staged[slot, at, column * width : (column + 1) * width] = value

        def norm_step(at, gradient, normal, layer_norm, gain, sums):
            n = normal[i, at, :].astype(jnp.float32)
            d_res = normed_back(gradient * vector(gain), n, inverses[i, at, layer_norm : layer_norm + 1])
            d_low = d_res.astype(jnp.bfloat16)
            terms = [folded(gradient * n), folded(gradient), folded(d_low.astype(jnp.float32))]
            return d_res, d_low, terms if sums is None else [a + b for a, b in zip(sums, terms)]

        sums = None
        for at in blocks:
            gradient = upstream[i, at, :].astype(jnp.float32)
            d_res, d_low, sums = norm_step(at, gradient, normal2, 1, g2_ref, sums)
            wide1[at, :] = d_res
            stage(at, 0, d_low)
        for name, value in zip(("g2", "s2", "bd"), sums):
            single(name, value)
        d_out = staged[slot, :, :width]
        half = wide * width // 2

        def opened_half(n):
            return product(d_out, wd_t[:, n * half : (n + 1) * half])

        def bent_half(n, d_active):
            for part in range(0, half, width):
                j = (n * half + part) // width
                lanes = slice(j * width, (j + 1) * width)
                total = None
                for at in blocks:
                    d_inner = d_active[at, part : part + width] * slope[i, at, lanes].astype(jnp.float32)
                    d_inner = d_inner.astype(jnp.bfloat16)
                    stage(at, 1 + j, d_inner)
                    term = folded(d_inner.astype(jnp.float32))
                    total = term if total is None else total + term
                keep_small(len(SINGLES) + j, total)

        def closed_half(n):
            at = width + n * half
            return product(staged[slot, :, at : at + half], wu_t[n * half : (n + 1) * half, :])

        d_first = opened_half(0)
        d_second = opened_half(1)
        bent_half(0, d_first)
        d_deep = closed_half(0)
        bent_half(1, d_second)
        d_deeper = closed_half(1)
        sums = None
        for at in blocks:
            d_res, d_low, sums = norm_step(at, wide1[at, :] + d_deep[at] + d_deeper[at], normal1, 0, g1_ref, sums)
            wide1[at, :] = d_res
            stage(at, 1 + wide, d_low)
        for name, value in zip(("g1", "s1", "bo"), sums):
            single(name, value)
        d_att = staged[slot, :, (1 + wide) * width : (2 + wide) * width]
        @pl.when(i == 0)
        def _():
            save(items - 2, 0).wait()
            save(items - 1, 0).wait()

        active[0, :, :width] = product(d_att, wo_t[...]).astype(jnp.bfloat16)

        def lanes_of(p):
            return slice(p * pair_width, (p + 1) * pair_width)

        def place_grad(n, p, block):
            at = base + n * width + p * pair_width
            staged[slot, :, at : at + pair_width] = block.astype(jnp.bfloat16)

        def opened(p):
            v_pair = values[i, :, lanes_of(p)]
            c_pair = active[0, :, lanes_of(p)]
            stacked = jnp.concatenate([only(v_pair, 0), only(v_pair, 1)], axis=0)
            k_turned = keys[i, :, lanes_of(p)].astype(jnp.float32).T.astype(jnp.bfloat16)
            d_value = product(probs[i, 2 * p], only(c_pair, 0))
            d_value += product(probs[i, 2 * p + 1], only(c_pair, 1))
            return product_t(stacked, c_pair), k_turned, d_value

        def score_base(p, h):
            return (2 * (p % 2) + h) * 2 * 128

        def score_grads(p, both):
            for h in range(2):
                for span in spans:
                    prob = probs[i, 2 * p + h, :, span].astype(jnp.float32)
                    d_prob = both[h * rows : (h + 1) * rows, span]
                    drift = jnp.sum(d_prob * prob, axis=0, keepdims=True)
                    at = score_base(p, h)
                    active[1, :, at + span.start : at + span.stop] = (prob * (d_prob - drift)).astype(jnp.bfloat16)
            return [active[1, :, score_base(p, h) : score_base(p, h) + rows] for h in range(2)]

        def closed(p, found, k_turned):
            q_pair = query[i, :, lanes_of(p)]
            d_key = product(found[0], only(q_pair, 0)) + product(found[1], only(q_pair, 1))
            return d_key, [product(k_turned[h * head : (h + 1) * head], found[h]) for h in range(2)]

        def place_grads(p, d_value, d_key, parts):
            place_grad(0, p, jnp.concatenate(parts, axis=0).T * (1.0 / math.sqrt(head)))
            place_grad(1, p, d_key)
            place_grad(2, p, d_value)

        ahead = opened(0)
        waiting = None
        d_source = None

        def source_grad(group):
            found = None
            for n in range(3):
                at = n * width + group * 2 * pair_width
                piece = product(
                    staged[slot, :, base + at : base + at + 2 * pair_width], wqkv_t[at : at + 2 * pair_width, :]
                )
                found = piece if found is None else found + piece
            return found

        for p in range(pairs):
            both, k_turned, d_value = ahead
            if p + 1 < pairs:
                ahead = opened(p + 1)
            if waiting is not None:
                place_grads(*waiting)
            if p in (2, 4):
                piece = source_grad(p // 2 - 1)
                d_source = piece if d_source is None else d_source + piece
            found = score_grads(p, both)
            d_key, parts = closed(p, found, k_turned)
            waiting = (p, d_value, d_key, parts)
        place_grads(*waiting)
        d_source += source_grad(pairs // 2 - 1)
        sums = None
        for at in blocks:
            result[i, at, :] = (wide1[at, :] + d_source[at]).astype(jnp.bfloat16)
            terms = [
                folded(staged[slot, at, base : base + width].astype(jnp.float32)),
                folded(staged[slot, at, base + 2 * width : base + 3 * width].astype(jnp.float32)),
            ]
            sums = terms if sums is None else [a + b for a, b in zip(sums, terms)]
        single("bq", sums[0])
        single("bv", sums[1])

    small_ref[...] = jnp.zeros_like(small_ref)
    side = 256
    unit = lax.broadcasted_iota(jnp.int32, (side, side), 0) == lax.broadcasted_iota(jnp.int32, (side, side), 1)
    unit = jnp.where(unit, 1.0, 0.0).astype(jnp.bfloat16)

    def turn_weights():
        for natural, turned in ((wqkv, wqkv_t), (wo, wo_t), (wu, wu_t), (wd, wd_t)):
            for block in range(0, natural.shape[0], width):

                def one(n, carry):
                    at = pl.ds(pl.multiple_of(n * side, side), side)
                    tall = product_t(unit, natural[block : block + width, at])
                    turned[at, block : block + width] = tall.astype(jnp.bfloat16)
                    return carry

                lax.fori_loop(0, natural.shape[1] // side, one, 0)

    @pl.when(section == 1)
    def _():
        for copy in weight_copies:
            copy.wait()
        turn_weights()

    def forward_step(i, carry):
        @pl.when(section == 0)
        def _():
            assemble(i)

        @pl.when(section == 1)
        def _():
            forward_copy(i).wait_recv()

        @pl.when(i >= 2)
        def _():
            for n in range(3):
                save(i - 2, n).wait()

        forward(i)

        @pl.when((section == 0) & ((core == 0) | (i == items - 1)))
        def _():
            forward_copy(i).start()

        for n in range(5):
            save(i, n).start()
        return carry

    lax.fori_loop(0, items, forward_step, 0)

    @pl.when(section == 0)
    def _():
        turn_weights()

    @pl.when(section == 1)
    def _():
        cotangent_copy.wait()

    def backward_step(i, carry):
        @pl.when(section == 0)
        def _():
            back_copy(i).wait_recv()

        @pl.when(i >= 2)
        def _():
            staged_save(i - 2).wait()

        save(i, 4).wait()

        @pl.when(section == 0)
        def _():
            forward_copy(i).wait_send()

        backward(i)

        @pl.when(section == 1)
        def _():
            back_copy(i).start()

        staged_save(i).start()
        grad_save(i).start()
        return carry

    lax.fori_loop(0, items, backward_step, 0)

    def finish(i, carry):
        save(i, 3).wait()
        grad_save(i).wait()

        @pl.when(i >= items - 2)
        def _():
            staged_save(i).wait()
            for n in range(1, 3):
                save(i, n).wait()

        @pl.when(section == 1)
        def _():
            back_copy(i).wait_send()

        return carry

    lax.fori_loop(0, items, finish, 0)


def layered(image_ids, caption_lengths, captions, regions, cotangent, stacked):
    items, cap_rows, width = captions.shape
    held, region_rows, _ = regions.shape
    rows = cap_rows + region_rows
    inner = stacked[9].shape[2]
    low = jnp.bfloat16
    wide = inner // width

    def cells(*shape):
        return pltpu.VMEM(shape, low)

    anywhere = pl.BlockSpec(memory_space=pl.ANY)
    local = pl.BlockSpec(memory_space=pltpu.VMEM)
    scalars = pl.BlockSpec(memory_space=pltpu.SMEM)
    return pl.pallas_call(
        layer_kernel,
        out_shape=(
            jax.ShapeDtypeStruct((1, items, rows, width), low),
            jax.ShapeDtypeStruct((1, items, rows, width), low),
            jax.ShapeDtypeStruct((items * rows, (3 + wide) * width), low),
            jax.ShapeDtypeStruct((items * rows, (5 + wide) * width), low),
            jax.ShapeDtypeStruct((GROUP, width), jnp.float32),
        ),
        in_specs=[scalars, scalars, anywhere, local, anywhere]
        + [anywhere if len(member.shape) == 3 else local for member in stacked],
        out_specs=(anywhere, anywhere, anywhere, anywhere, local),
        scratch_shapes=[
            cells(width, 3 * width),
            cells(width, width),
            cells(width, inner),
            cells(inner, width),
            cells(3 * width, width),
            cells(width, width),
            cells(inner, width),
            cells(width, inner),
            cells(3 * held, region_rows, width),
            cells(items, rows, width),
            cells(items, rows, width),
            cells(items, rows, width),
            cells(items, rows, width),
            cells(items, rows, width),
            cells(items, HEADS, rows, rows),
            cells(2, rows, width),
            cells(items, rows, width),
            cells(items, rows, width),
            cells(2, rows, width),
            cells(2, rows, inner),
            cells(items, rows, inner),
            cells(items, rows, width),
            cells(2, rows, (5 + wide) * width),
            pltpu.VMEM((items, rows, 2), jnp.float32),
            pltpu.VMEM((rows, width), jnp.float32),
            cells(cap_rows, items, width),
            pltpu.SemaphoreType.DMA((8,)),
            pltpu.SemaphoreType.DMA((2,)),
            pltpu.SemaphoreType.DMA((2,)),
            pltpu.SemaphoreType.DMA((items,)),
            pltpu.SemaphoreType.DMA((items,)),
            pltpu.SemaphoreType.DMA((items,)),
            pltpu.SemaphoreType.DMA((items,)),
            pltpu.SemaphoreType.DMA((items, 7)),
        ],
        compiler_params=pltpu.CompilerParams(
            collective_id=0, has_side_effects=True, vmem_limit_bytes=VMEM_LIMIT
        ),
        cost_estimate=pl.CostEstimate(
            flops=4 * items * rows * (4 + 2 * wide) * width * width,
            bytes_accessed=60_000_000,
            transcendentals=0,
        ),
    )(image_ids, caption_lengths, captions.transpose(1, 0, 2), regions, cotangent, *stacked)


def body(
    captions,
    regions,
    image_ids,
    caption_lengths,
    cotangent,
    query_weight,
    query_bias,
    key_weight,
    value_weight,
    value_bias,
    out_weight,
    out_bias,
    norm1_gain,
    norm1_bias,
    up_weight,
    up_bias,
    down_weight,
    down_bias,
    norm2_gain,
    norm2_bias,
):
    stacked = (
        query_weight,
        query_bias,
        key_weight,
        value_weight,
        value_bias,
        out_weight,
        out_bias,
        norm1_gain,
        norm1_bias,
        up_weight,
        up_bias,
        down_weight,
        down_bias,
        norm2_gain,
        norm2_bias,
    )
    states, input_grads, a_side, b_side, small = layered(
        image_ids, caption_lengths, captions, regions, cotangent, stacked
    )
    sums, small_sums = reduced(a_side, b_side, small, lax.axis_size("batch"))
    return tuple(spread(sums, small_sums, states, input_grads, stacked))


def solution(mesh):
    placed = (
        P("batch", None, None),
        P("batch", None, None),
        P("batch"),
        P("batch"),
        P("batch", None, None),
        P("section", None, None),
        P("section", None),
        P("section", None, None),
        P("section", None, None),
        P("section", None),
        P("section", None, None),
        P("section", None),
        P("section", None),
        P("section", None),
        P("section", None, None),
        P("section", None),
        P("section", None, None),
        P("section", None),
        P("section", None),
        P("section", None),
    )
    return jax.shard_map(
        body,
        mesh=mesh,
        in_specs=placed,
        out_specs=(
            P("section", "batch", None, None),
            P("section", "batch", None, None),
            P("section", None, None),
            P("section", None),
            P("section", None, None),
            P("section", None, None),
            P("section", None),
            P("section", None, None),
            P("section", None),
            P("section", None),
            P("section", None),
            P("section", None, None),
            P("section", None),
            P("section", None, None),
            P("section", None),
            P("section", None),
            P("section", None),
        ),
        check_vma=False,
    )
```

```python
import functools
import math

import jax
import jax.numpy as jnp
from jax import lax
from jax.experimental import pallas as pl
from jax.experimental.pallas import tpu as pltpu
from jax.sharding import PartitionSpec as P

HEADS = 12
EPSILON = 1e-12
MESH = pl.DeviceIdType.MESH
VMEM_LIMIT = 63 * 1024 * 1024
VMEM_BESIDE = 47 * 1024 * 1024
GROUP = 16
CHUNK_GROUPS = 16
SLOTS = 18
SLOT_GROUPS = 24
LAG = 3
CYCLE = 3
LINE = 4
SPLIT_BITS = 4


def reduce_kernel(
    bits,
    chunks,
    a_hbm,
    b_hbm,
    small_ref,
    whole,
    small_out,
    a_ref,
    b_ref,
    acc,
    recv,
    small_acc,
    small_recv,
    load_sem,
    send_sem,
    recv_sem,
    small_send_sem,
    small_recv_sem,
):
    width = acc.shape[2]
    extra = bits - SPLIT_BITS
    first_gather = SPLIT_BITS + 1 + extra
    stages = 2 * (SPLIT_BITS + 1) + extra
    me = lax.axis_index("batch")
    section = lax.axis_index("section")
    core, side, place = me % 2, (me // 2) % 2, (me // 4) % LINE
    blocks_a = a_hbm.shape[1] // width
    blocks_b = b_hbm.shape[1] // width
    per_block = width // (CHUNK_GROUPS * GROUP)

    def load(source, target, block, base):
        lanes = pl.ds(block * width, width)
        return pltpu.make_async_copy(source.at[:, lanes], target.at[:, lanes], load_sem.at[base + block])

    def load_a(block):
        return load(a_hbm, a_ref, block, 0)

    def load_b(block):
        return load(b_hbm, b_ref, block, blocks_a)

    wide = blocks_a - 3
    first_use = {0: [(load_a, 0), (load_b, 0)]}
    for j in range(1, wide):
        first_use[j] = [(load_a, j)]
    first_use[wide] = [(load_a, wide), (load_b, 1)]
    for j in range(1, wide):
        first_use[wide + j] = [(load_b, 1 + j)]
    first_use[2 * wide] = [(load_a, wide + 1), (load_b, wide + 1)]
    first_use[2 * wide + 1] = [(load_a, wide + 2), (load_b, wide + 2)]
    first_use[2 * wide + 2] = [(load_b, wide + 3)]
    first_use[2 * wide + 3] = [(load_b, wide + 4)]
    for j in range(2 * wide + 4):
        for kind, block in first_use[j]:
            kind(block).start()

    def bit_mate(k):
        bit = (me // 2**k) % 2
        return (section, me + 2**k * (1 - 2 * bit))

    core_mate, side_mate = bit_mate(0), bit_mate(1)
    mates = ((section, me - LINE), (section, me + LINE))
    ring = [(section, me + LINE * ((place + d) % LINE - place)) for d in (LINE - 1, 1)]

    barrier = pltpu.get_barrier_semaphore()
    for peer in [core_mate, side_mate] + ring + [bit_mate(k) for k in range(2, bits)]:
        pl.semaphore_signal(barrier, inc=1, device_id=peer, device_id_type=MESH)
    pl.semaphore_wait(barrier, bits + 2)

    def low_core(c):
        return c * CHUNK_GROUPS + core * 8

    def low_side(c):
        return low_core(c) + side * 4

    def block_start(c, kind, b):
        return low_side(c) + b if kind == 0 else low_core(c) + 2 * b

    def final(c, kind):
        return low_side(c) + place if kind == 0 else low_core(c) + 2 * place + side

    def remote(c, source, start, size, target, spot, index, peer):
        return pltpu.make_async_remote_copy(
            src_ref=source.at[pl.ds(start, size)],
            dst_ref=target.at[lax.rem(c, SLOTS), pl.ds(spot, size)] if target is recv else target.at[pl.ds(start, size)],
            send_sem=send_sem.at[lax.rem(c, SLOTS), index],
            recv_sem=recv_sem.at[lax.rem(c, SLOTS), index],
            device_id=peer,
            device_id_type=MESH,
        )

    def core_copy(c):
        return remote(c, acc, c * CHUNK_GROUPS + (1 - core) * 8, 8, recv, 0, 0, core_mate)

    def side_copy(c, kind):
        if kind == 0:
            return remote(c, acc, low_core(c) + (1 - side) * 4, 4, recv, 8, 1, side_mate)
        return remote(c, acc, low_core(c) + 2 * place + (1 - side), 1, recv, 8, 1, side_mate)

    def line_copy(c, kind, r, d):
        size = 1 + kind
        b = jnp.minimum(3 - r + place, 3) if d == 1 else jnp.maximum(r - 3 + place, 0)
        spot = 12 + 2 * (2 * r + d)
        return remote(c, acc, block_start(c, kind, b), size, recv, spot, 2 + 2 * r + d, mates[d])

    def spread_copy(c, kind, r, d):
        size = 1 + kind
        b = jnp.maximum(place - r, 0) if d == 1 else jnp.minimum(place + r, 3)
        return remote(c, whole, block_start(c, kind, b), size, whole, 0, 8 + 2 * r + d, mates[d])

    def side_back_copy(c, kind):
        if kind == 0:
            return remote(c, whole, low_side(c), 4, whole, 0, 14, side_mate)
        return remote(c, whole, final(c, kind), 1, whole, 0, 14, side_mate)

    def core_back_copy(c):
        return remote(c, whole, low_core(c), 8, whole, 0, 15, core_mate)

    def extra_copy(c, kind, e):
        return remote(c, acc, final(c, kind), 1, recv, 24 + e, 16 + e, bit_mate(SPLIT_BITS + e))

    def add_groups(start, count, c, spot):
        slot = lax.rem(c, SLOTS)
        for g in range(count):
            total = acc[start + g].astype(jnp.float32) + recv[slot, spot + g].astype(jnp.float32)
            acc[start + g] = total.astype(jnp.bfloat16)

    def name_of(kind, s):
        if s == 0:
            return ("core",)
        if s == stages - 1:
            return ("core_back",)
        if s < SPLIT_BITS + 1:
            order = [("side",), ("line", 0), ("line", 1), ("line", 2)]
            order = order if kind == 0 else order[1:] + order[:1]
            return order[s - 1]
        if s < first_gather:
            return ("extra", s - SPLIT_BITS - 1)
        order = [("spread", 0), ("spread", 1), ("spread", 2), ("side_back",)]
        order = order if kind == 0 else order[3:] + order[:3]
        return order[s - first_gather]

    def start_stage(c, kind, s):
        name = name_of(kind, s)
        if s == first_gather:
            whole[final(c, kind)] = acc[final(c, kind)]
        if name[0] == "core":
            core_copy(c).start()
        elif name[0] == "side":
            side_copy(c, kind).start()
        elif name[0] == "line":
            r = name[1]
            pl.when(place <= r)(lambda: line_copy(c, kind, r, 1).start())
            pl.when(place >= 3 - r)(lambda: line_copy(c, kind, r, 0).start())
        elif name[0] == "extra":
            extra_copy(c, kind, name[1]).start()
        elif name[0] == "spread":
            r = name[1]
            pl.when((place >= r) & (place <= 2))(lambda: spread_copy(c, kind, r, 1).start())
            pl.when((place >= 1) & (place <= 3 - r))(lambda: spread_copy(c, kind, r, 0).start())
        elif name[0] == "side_back":
            side_back_copy(c, kind).start()
        else:
            core_back_copy(c).start()

    def finish_stage(c, kind, s):
        name = name_of(kind, s)
        if name[0] == "core":
            core_copy(c).wait()
            add_groups(low_core(c), 8, c, 0)
        elif name[0] == "side":
            side_copy(c, kind).wait()
            if kind == 0:
                add_groups(low_side(c), 4, c, 8)
            else:
                add_groups(final(c, kind), 1, c, 8)
        elif name[0] == "line":
            r = name[1]

            @pl.when(place <= r)
            def _():
                line_copy(c, kind, r, 1).wait_send()

            @pl.when(place >= 3 - r)
            def _():
                line_copy(c, kind, r, 0).wait_send()

            @pl.when((place >= 1) & (place <= r + 1))
            def _():
                line_copy(c, kind, r, 1).wait_recv()
                add_groups(block_start(c, kind, 2 - r + place), 1 + kind, c, 12 + 2 * (2 * r + 1))

            @pl.when((place <= 2) & (place >= 2 - r))
            def _():
                line_copy(c, kind, r, 0).wait_recv()
                add_groups(block_start(c, kind, r - 2 + place), 1 + kind, c, 12 + 2 * (2 * r))

        elif name[0] == "extra":
            extra_copy(c, kind, name[1]).wait()
            add_groups(final(c, kind), 1, c, 24 + name[1])
        elif name[0] == "spread":
            r = name[1]
            pl.when((place >= r) & (place <= 2))(lambda: spread_copy(c, kind, r, 1).wait_send())
            pl.when((place >= 1) & (place <= 3 - r))(lambda: spread_copy(c, kind, r, 0).wait_send())
            pl.when(place >= r + 1)(lambda: spread_copy(c, kind, r, 1).wait_recv())
            pl.when(place <= 2 - r)(lambda: spread_copy(c, kind, r, 0).wait_recv())
        elif name[0] == "side_back":
            side_back_copy(c, kind).wait()
        else:
            core_back_copy(c).wait()

    def small_copy(k):
        return pltpu.make_async_remote_copy(
            src_ref=small_acc.at[k],
            dst_ref=small_recv.at[k],
            send_sem=small_send_sem.at[k],
            recv_sem=small_recv_sem.at[k],
            device_id=bit_mate(k),
            device_id_type=MESH,
        )

    small_acc[0] = small_ref[...]

    def step(t, phase):
        for s in range(stages, 0, -1):
            c = t - LAG * s
            kind = (phase - LAG * s) % CYCLE // 2

            @pl.when((c >= 0) & (c < chunks))
            def _():
                finish_stage(c, kind, s - 1)
                if s < stages:
                    start_stage(c, kind, s)

        for j in range(2 * wide + 4):

            @pl.when(t == per_block * j)
            def _():
                for kind, block in first_use[j]:
                    kind(block).wait()

        @pl.when(t < chunks)
        def _():
            block, part = t // per_block, t % per_block
            a_col = jnp.minimum(block, wide) + jnp.minimum(block // (2 * wide), 1) + jnp.minimum(block // (2 * wide + 1), 1)
            b_col = jnp.maximum(block - wide + 1, 0)
            lines = CHUNK_GROUPS * GROUP
            left = a_ref[:, pl.ds(pl.multiple_of(a_col * width + part * lines, lines), lines)]
            right = b_ref[:, pl.ds(pl.multiple_of(b_col * width, width), width)]
            grad = lax.dot_general(left, right, (((0,), (0,)), ((), ())), preferred_element_type=jnp.float32)
            acc[pl.ds(t * CHUNK_GROUPS, CHUNK_GROUPS)] = grad.astype(jnp.bfloat16).reshape(
                CHUNK_GROUPS, GROUP, width
            )
            core_copy(t).start()

        for k in range(bits + 1):

            @pl.when(t == LAG * k)
            def _():
                if k > 0:
                    small_copy(k - 1).wait()
                    small_acc[k] = small_acc[k - 1] + small_recv[k - 1]
                if k < bits:
                    small_copy(k).start()

    def cycle(n, carry):
        for phase in range(CYCLE):
            step(n * CYCLE + phase, phase)
        return carry

    lax.fori_loop(0, pl.cdiv(chunks + LAG * stages, CYCLE), cycle, 0)
    small_out[...] = small_acc[bits]


def reduced(a_side, b_side, small, count):
    rows = a_side.shape[0]
    width = small.shape[1]
    bits = count.bit_length() - 1
    extra = bits - SPLIT_BITS
    blocks = 2 * (a_side.shape[1] // width - 3) + 4
    chunks = blocks * width // (CHUNK_GROUPS * GROUP)
    groups = chunks * CHUNK_GROUPS
    loads = (a_side.shape[1] + b_side.shape[1]) // width
    return pl.pallas_call(
        functools.partial(reduce_kernel, bits, chunks),
        out_shape=(
            pltpu.VMEM((groups, GROUP, width), jnp.bfloat16),
            jax.ShapeDtypeStruct(small.shape, jnp.float32),
        ),
        in_specs=[
            pl.BlockSpec(memory_space=pl.ANY),
            pl.BlockSpec(memory_space=pl.ANY),
            pl.BlockSpec(memory_space=pltpu.VMEM),
        ],
        out_specs=(pl.BlockSpec(memory_space=pltpu.VMEM), pl.BlockSpec(memory_space=pltpu.VMEM)),
        scratch_shapes=[
            pltpu.VMEM(a_side.shape, jnp.bfloat16),
            pltpu.VMEM(b_side.shape, jnp.bfloat16),
            pltpu.VMEM((groups, GROUP, width), jnp.bfloat16),
            pltpu.VMEM((SLOTS, SLOT_GROUPS + extra, GROUP, width), jnp.bfloat16),
            pltpu.VMEM((bits + 1,) + small.shape, jnp.float32),
            pltpu.VMEM((bits,) + small.shape, jnp.float32),
            pltpu.SemaphoreType.DMA((loads,)),
            pltpu.SemaphoreType.DMA((SLOTS, 16 + extra)),
            pltpu.SemaphoreType.DMA((SLOTS, 16 + extra)),
            pltpu.SemaphoreType.DMA((bits,)),
            pltpu.SemaphoreType.DMA((bits,)),
        ],
        compiler_params=pltpu.CompilerParams(
            collective_id=1, has_side_effects=True, vmem_limit_bytes=VMEM_BESIDE
        ),
        cost_estimate=pl.CostEstimate(
            flops=2 * rows * blocks * width * width, bytes_accessed=80_000_000, transcendentals=0
        ),
    )(a_side, b_side, small)


PIECE = 192
DEPTH = 8


def spread_kernel(sum_ref, small_ref, states_hbm, grads_hbm, *refs):
    width = small_ref.shape[1]
    (o_wq, o_bq, o_wk, o_wv, o_bv, o_wo, o_bo, o_g1, o_s1, o_up, o_bu, o_dn, o_bd, o_g2, o_s2) = refs[2:17]
    states_out, grads_out = refs[:2]
    given, held, out_sem, held_sem = refs[17:]
    wide = o_bu.shape[1] // width
    targets = []
    for j in range(wide):
        targets += [o_dn.at[0, pl.ds(j * width + r, PIECE), :] for r in range(0, width, PIECE)]
    for j in range(wide):
        targets += [o_up.at[0, pl.ds(r, PIECE), pl.ds(j * width, width)] for r in range(0, width, PIECE)]
    for ref in (o_wo, o_wq, o_wk, o_wv):
        targets += [ref.at[0, pl.ds(r, PIECE), :] for r in range(0, width, PIECE)]

    items = states_hbm.shape[1]
    passes = [(states_hbm.at[0, i], states_out.at[0, i]) for i in range(items)]
    passes += [(grads_hbm.at[0, i], grads_out.at[0, i]) for i in range(items)]

    def pass_in(i):
        return pltpu.make_async_copy(passes[i][0], held.at[i], held_sem.at[i])

    def pass_out(i):
        return pltpu.make_async_copy(held.at[i], passes[i][1], held_sem.at[i])

    def store(i):
        return pltpu.make_async_copy(given.at[i % DEPTH], targets[i], out_sem.at[i % DEPTH])

    for i in range(len(passes)):
        pass_in(i).start()
    singles = [o_bq, o_bv, o_bo, o_g1, o_s1, o_bd, o_g2, o_s2]
    for i, ref in enumerate(singles):
        ref[...] = small_ref[pl.ds(i, 1), :]
    for j in range(wide):
        o_bu[:, pl.ds(j * width, width)] = small_ref[pl.ds(len(singles) + j, 1), :]
    for i in range(len(targets)):
        if i >= DEPTH:
            store(i - DEPTH).wait()

        def convert(r, carry):
            block = sum_ref[pl.ds(i * (PIECE // GROUP) + r * 4, 4)].astype(jnp.float32)
            rows = pl.ds(pl.multiple_of(r * 4 * GROUP, 4 * GROUP), 4 * GROUP)
            given[i % DEPTH, rows, :] = block.reshape(4 * GROUP, width)
            return carry

        lax.fori_loop(0, PIECE // (4 * GROUP), convert, 0)
        store(i).start()
        if i < len(passes):
            pass_in(i).wait()
            pass_out(i).start()
    for i in range(len(targets) - DEPTH, len(targets)):
        store(i).wait()
    for i in range(len(passes)):
        pass_out(i).wait()


def spread(sums, small, states, input_grads, params):
    width = small.shape[1]
    anywhere = pl.BlockSpec(memory_space=pl.ANY)
    local = pl.BlockSpec(memory_space=pltpu.VMEM)
    return pl.pallas_call(
        spread_kernel,
        out_shape=(
            jax.ShapeDtypeStruct(states.shape, states.dtype),
            jax.ShapeDtypeStruct(input_grads.shape, input_grads.dtype),
        )
        + tuple(jax.ShapeDtypeStruct(member.shape, jnp.float32) for member in params),
        in_specs=[local, local, anywhere, anywhere],
        out_specs=(anywhere, anywhere)
        + tuple(anywhere if len(member.shape) == 3 else local for member in params),
        scratch_shapes=[
            pltpu.VMEM((DEPTH, PIECE, width), jnp.float32),
            pltpu.VMEM((2 * states.shape[1],) + states.shape[2:], states.dtype),
            pltpu.SemaphoreType.DMA((DEPTH,)),
            pltpu.SemaphoreType.DMA((2 * states.shape[1],)),
        ],
        compiler_params=pltpu.CompilerParams(vmem_limit_bytes=VMEM_BESIDE),
        cost_estimate=pl.CostEstimate(
            flops=12 * width * width, bytes_accessed=80 * width * width, transcendentals=0
        ),
    )(pltpu.with_memory_space_constraint(sums, pltpu.VMEM), small, states, input_grads)


HALF_LOG = -0.5 / math.log(2.0)
BELL_SCALE = 1.0 / math.sqrt(2.0 * math.pi)
SINGLES = ("bq", "bv", "bo", "g1", "s1", "bd", "g2", "s2")


def product(left, right):
    return lax.dot_general(left, right, (((1,), (0,)), ((), ())), preferred_element_type=jnp.float32)


def product_t(left, right):
    return lax.dot_general(left, right, (((1,), (1,)), ((), ())), preferred_element_type=jnp.float32)


def gelu_pair(z):
    cdf = 0.5 * lax.erf(z * (1.0 / math.sqrt(2.0))) + 0.5
    bell = jnp.exp2(z * z * HALF_LOG)
    return z * cdf, z * BELL_SCALE * bell + cdf


def normed(values):
    average = jnp.mean(values, axis=-1, keepdims=True)
    centered = values - average
    inverse = lax.rsqrt(jnp.mean(centered * centered, axis=-1, keepdims=True) + EPSILON)
    return centered * inverse, inverse


def normed_back(grad, normal, inverse):
    first_mean = jnp.mean(grad, axis=-1, keepdims=True)
    second_mean = jnp.mean(grad * normal, axis=-1, keepdims=True)
    return inverse * (grad - first_mean - normal * second_mean)


def layer_kernel(
    ids_ref,
    lengths_ref,
    captions_hbm,
    regions_ref,
    cotangent_hbm,
    wq_hbm,
    bq_ref,
    wk_hbm,
    wv_hbm,
    bv_ref,
    wo_hbm,
    bo_ref,
    g1_ref,
    s1_ref,
    wu_hbm,
    bu_ref,
    wd_hbm,
    bd_ref,
    g2_ref,
    s2_ref,
    states_hbm,
    grads_hbm,
    a_hbm,
    b_hbm,
    small_ref,
    wqkv,
    wo,
    wu,
    wd,
    wqkv_t,
    wo_t,
    wu_t,
    wd_t,
    table,
    hidden,
    upstream,
    query,
    keys,
    values,
    probs,
    context,
    normal1,
    normal2,
    lowered,
    active,
    slope,
    result,
    staged,
    inverses,
    wide1,
    caption_cells,
    weight_sem,
    table_send,
    table_recv,
    fwd_send,
    fwd_recv,
    back_send,
    back_recv,
    out_sem,
):
    items, rows, width = hidden.shape
    held = regions_ref.shape[0]
    cap_rows = captions_hbm.shape[0]
    wide = wu.shape[1] // width
    pairs = HEADS // 2
    pair_width = width // pairs
    head = width // HEADS
    section = lax.axis_index("section")
    batch = lax.axis_index("batch")
    count = lax.axis_size("batch")
    right = (section, lax.rem(batch + 1, count))
    left = (section, lax.rem(batch + count - 1, count))
    other = (1 - section, batch)
    core = lax.rem(batch, 2)

    weight_copies = [
        pltpu.make_async_copy(source.at[0], target, weight_sem.at[n])
        for n, (source, target) in enumerate(
            (
                (wq_hbm, wqkv.at[:, pl.ds(0, width)]),
                (wk_hbm, wqkv.at[:, pl.ds(width, width)]),
                (wv_hbm, wqkv.at[:, pl.ds(2 * width, width)]),
                (wo_hbm, wo),
                (wu_hbm, wu),
                (wd_hbm, wd),
            )
        )
    ]
    for copy in weight_copies[:3]:
        copy.start()
    cotangent_copy = pltpu.make_async_copy(cotangent_hbm, upstream, weight_sem.at[6])

    barrier = pltpu.get_barrier_semaphore()
    for peer in (right, left, other):
        pl.semaphore_signal(barrier, inc=1, device_id=peer, device_id_type=MESH)
    pl.semaphore_wait(barrier, 3)

    def table_copy(n, peer):
        return pltpu.make_async_remote_copy(
            src_ref=regions_ref,
            dst_ref=table.at[pl.ds(2 * n * held, held)],
            send_sem=table_send.at[n],
            recv_sem=table_recv.at[n],
            device_id=peer,
            device_id_type=MESH,
        )

    @pl.when(section == 0)
    def _():
        caption_copy = pltpu.make_async_copy(captions_hbm, caption_cells, weight_sem.at[7])
        caption_copy.start()
        table_copy(0, right).start()
        table_copy(1, left).start()
        table[pl.ds(held, held)] = regions_ref[...]
        table_copy(0, right).wait()
        table_copy(1, left).wait()
        caption_copy.wait()

    for copy in weight_copies[3:]:
        copy.start()

    @pl.when(section == 1)
    def _():
        cotangent_copy.start()

    def forward_copy(i):
        return pltpu.make_async_remote_copy(
            src_ref=result.at[i],
            dst_ref=hidden.at[i],
            send_sem=fwd_send.at[i],
            recv_sem=fwd_recv.at[i],
            device_id=other,
            device_id_type=MESH,
        )

    def back_copy(i):
        return pltpu.make_async_remote_copy(
            src_ref=result.at[i],
            dst_ref=upstream.at[i],
            send_sem=back_send.at[i],
            recv_sem=back_recv.at[i],
            device_id=other,
            device_id_type=MESH,
        )

    def save(i, n):
        at = pl.ds(pl.multiple_of(i * rows, rows), rows)
        first = wide * width
        turn = lax.rem(i, 2)
        if n == 0:
            source, target = active.at[turn], a_hbm.at[at, pl.ds(0, first)]
        elif n == 1:
            source, target = lowered.at[turn], a_hbm.at[at, pl.ds(first, width)]
        elif n == 2:
            source, target = context.at[turn], a_hbm.at[at, pl.ds(first + width, width)]
        elif n == 3:
            source, target = hidden.at[i], a_hbm.at[at, pl.ds(first + 2 * width, width)]
        else:
            source, target = result.at[i], states_hbm.at[0, i]
        return pltpu.make_async_copy(source, target, out_sem.at[i, n])

    def staged_save(i):
        at = pl.ds(pl.multiple_of(i * rows, rows), rows)
        lanes = pl.ds((1 + wide) * width, 4 * width)
        return pltpu.make_async_copy(
            staged.at[lax.rem(i, 2), :, lanes], b_hbm.at[at, lanes], out_sem.at[i, 5]
        )

    def early_save(i):
        at = pl.ds(pl.multiple_of(i * rows, rows), rows)
        lanes = pl.ds(0, (1 + wide) * width)
        return pltpu.make_async_copy(
            staged.at[lax.rem(i, 2), :, lanes], b_hbm.at[at, lanes], out_sem.at[i, 7]
        )

    def grad_save(i):
        return pltpu.make_async_copy(result.at[i], grads_hbm.at[0, i], out_sem.at[i, 6])

    def vector(ref, j=0):
        return ref[:, j * width : (j + 1) * width].astype(jnp.float32)

    lane = lax.broadcasted_iota(jnp.int32, (rows, pair_width), 1)

    blocks = [slice(r, r + GROUP) for r in range(0, rows, GROUP)]
    spans = [slice(c, min(c + 128, rows)) for c in range(0, rows, 128)]

    def only(block, h):
        return jnp.where((lane // head) == h, block, jnp.zeros_like(block))

    def assemble(i):
        total = count * held
        spot = jnp.minimum(lax.rem(ids_ref[i] - (batch - 1) * held + total, total), 3 * held - 1)
        for n in range(items):

            @pl.when(i == n)
            def _():
                whole = jnp.concatenate(
                    [caption_cells[:, n, :].astype(jnp.float32), table[spot].astype(jnp.float32)], axis=0
                )
                hidden[n] = whole.astype(jnp.bfloat16)

    def forward(i):
        @pl.when((i == 0) & (section == 0))
        def _():
            for copy in weight_copies[:3]:
                copy.wait()

        turn = lax.rem(i, 2)
        source = hidden[i]
        mixed = product(source, wqkv[...])
        for at in blocks:
            scaled = (mixed[at, :width] + vector(bq_ref)) * (1.0 / math.sqrt(head))
            query[i, at, :] = scaled.astype(jnp.bfloat16)
            keys[i, at, :] = mixed[at, width : 2 * width].astype(jnp.bfloat16)
            values[i, at, :] = (mixed[at, 2 * width :] + vector(bv_ref)).astype(jnp.bfloat16)
        position = lax.broadcasted_iota(jnp.int32, (rows, 1), 0)
        live = (position >= cap_rows) | (position < lengths_ref[i])
        key_bias = jnp.where(live, 0.0, -1000000000.0)

        def wait_rest():
            @pl.when((i == 0) & (section == 0))
            def _():
                for copy in weight_copies[3:]:
                    copy.wait()

        def lanes_of(p):
            return slice(p * pair_width, (p + 1) * pair_width)

        def scored(p):
            k_pair = keys[i, :, lanes_of(p)]
            stacked = jnp.concatenate([only(k_pair, 0), only(k_pair, 1)], axis=0)
            v_turned = values[i, :, lanes_of(p)].astype(jnp.float32).T.astype(jnp.bfloat16)
            return product_t(stacked, query[i, :, lanes_of(p)]), v_turned

        def weighed(p, both):
            for h in range(2):
                for span in spans:
                    scores = both[h * rows : (h + 1) * rows, span] + key_bias
                    expo = jnp.exp(scores - jnp.max(scores, axis=0, keepdims=True))
                    share = pltpu.reciprocal(jnp.sum(expo, axis=0, keepdims=True), approx=True)
                    probs[i, 2 * p + h, :, span] = (expo * share).astype(jnp.bfloat16)

        def mixed_values(p, v_turned):
            return [product(v_turned[h * head : (h + 1) * head], probs[i, 2 * p + h]) for h in range(2)]

        def place_context(p, parts):
            context[turn, :, lanes_of(p)] = jnp.concatenate(parts, axis=0).T.astype(jnp.bfloat16)

        def projected(group):
            lanes = slice(group * 2 * pair_width, (group + 1) * 2 * pair_width)
            return product(context[turn, :, lanes], wo[lanes, :])

        ahead = scored(0)
        parts = None
        attended = None
        for p in range(pairs):
            both, v_turned = ahead
            if p + 1 < pairs:
                ahead = scored(p + 1)
            if parts is not None:
                place_context(p - 1, parts)
            if p in (2, 4):
                if p == 2:
                    wait_rest()
                piece = projected(p // 2 - 1)
                attended = piece if attended is None else attended + piece
            weighed(p, both)
            parts = mixed_values(p, v_turned)
        place_context(pairs - 1, parts)
        attended += projected(pairs // 2 - 1)

        @pl.when((section == 0) & (core == 1) & (i >= 1))
        def _():
            forward_copy(i - 1).start()

        for at in blocks:
            n1, inv1 = normed(hidden[i, at, :].astype(jnp.float32) + attended[at] + vector(bo_ref))
            normal1[i, at, :] = n1.astype(jnp.bfloat16)
            inverses[i, at, 0:1] = inv1
            first = n1 * vector(g1_ref) + vector(s1_ref)
            lowered[turn, at, :] = first.astype(jnp.bfloat16)
            wide1[at, :] = first + vector(bd_ref)
        half = wide * width // 2

        def raised(n):
            return product(lowered[turn], wu[:, n * half : (n + 1) * half])

        def bend(n, z_tile):
            for part in range(0, half, width):
                lanes = slice(n * half + part, n * half + part + width)
                bias = bu_ref[:, lanes].astype(jnp.float32)
                for at in blocks:
                    gelu, slant = gelu_pair(z_tile[at, part : part + width] + bias)
                    active[turn, at, lanes] = gelu.astype(jnp.bfloat16)
                    slope[i, at, lanes] = slant.astype(jnp.bfloat16)

        z_first = raised(0)
        z_second = raised(1)
        bend(0, z_first)
        wide1[...] += product(active[turn, :, :half], wd[:half, :])
        bend(1, z_second)
        lowest = product(active[turn, :, half:], wd[half:, :])
        for at in blocks:
            n2, inv2 = normed(wide1[at, :] + lowest[at])
            normal2[i, at, :] = n2.astype(jnp.bfloat16)
            inverses[i, at, 1:2] = inv2
            result[i, at, :] = (n2 * vector(g2_ref) + vector(s2_ref)).astype(jnp.bfloat16)

    def folded(value):
        return value[: GROUP // 2] + value[GROUP // 2 :]

    def keep_small(row, value):
        small_ref[row : row + 1, :] += jnp.sum(value, axis=0, keepdims=True)

    def single(name, value):
        keep_small(SINGLES.index(name), value)

    def backward(i):
        slot = lax.rem(i, 2)
        base = (2 + wide) * width

        def stage(at, column, value):
            staged[slot, at, column * width : (column + 1) * width] = value

        def norm_step(at, gradient, normal, layer_norm, gain, sums):
            n = normal[i, at, :].astype(jnp.float32)
            d_res = normed_back(gradient * vector(gain), n, inverses[i, at, layer_norm : layer_norm + 1])
            d_low = d_res.astype(jnp.bfloat16)
            terms = [folded(gradient * n), folded(gradient), folded(d_low.astype(jnp.float32))]
            return d_res, d_low, terms if sums is None else [a + b for a, b in zip(sums, terms)]

        sums = None
        for at in blocks:
            gradient = upstream[i, at, :].astype(jnp.float32)
            d_res, d_low, sums = norm_step(at, gradient, normal2, 1, g2_ref, sums)
            wide1[at, :] = d_res
            stage(at, 0, d_low)
        for name, value in zip(("g2", "s2", "bd"), sums):
            single(name, value)
        d_out = staged[slot, :, :width]
        half = wide * width // 2

        def opened_half(n):
            return product(d_out, wd_t[:, n * half : (n + 1) * half])

        def bent_half(n, d_active):
            for part in range(0, half, width):
                j = (n * half + part) // width
                lanes = slice(j * width, (j + 1) * width)
                total = None
                for at in blocks:
                    d_inner = d_active[at, part : part + width] * slope[i, at, lanes].astype(jnp.float32)
                    d_inner = d_inner.astype(jnp.bfloat16)
                    stage(at, 1 + j, d_inner)
                    term = folded(d_inner.astype(jnp.float32))
                    total = term if total is None else total + term
                keep_small(len(SINGLES) + j, total)

        def closed_half(n):
            at = width + n * half
            return product(staged[slot, :, at : at + half], wu_t[n * half : (n + 1) * half, :])

        d_first = opened_half(0)
        d_second = opened_half(1)
        bent_half(0, d_first)
        d_deep = closed_half(0)
        bent_half(1, d_second)
        d_deeper = closed_half(1)
        early_save(i).start()
        sums = None
        for at in blocks:
            d_res, d_low, sums = norm_step(at, wide1[at, :] + d_deep[at] + d_deeper[at], normal1, 0, g1_ref, sums)
            wide1[at, :] = d_res
            stage(at, 1 + wide, d_low)
        for name, value in zip(("g1", "s1", "bo"), sums):
            single(name, value)
        d_att = staged[slot, :, (1 + wide) * width : (2 + wide) * width]
        @pl.when(i == 0)
        def _():
            save(items - 2, 0).wait()
            save(items - 1, 0).wait()

        active[0, :, :width] = product(d_att, wo_t[...]).astype(jnp.bfloat16)

        def lanes_of(p):
            return slice(p * pair_width, (p + 1) * pair_width)

        def place_grad(n, p, block):
            at = base + n * width + p * pair_width
            staged[slot, :, at : at + pair_width] = block.astype(jnp.bfloat16)

        def opened(p):
            v_pair = values[i, :, lanes_of(p)]
            c_pair = active[0, :, lanes_of(p)]
            stacked = jnp.concatenate([only(v_pair, 0), only(v_pair, 1)], axis=0)
            k_turned = keys[i, :, lanes_of(p)].astype(jnp.float32).T.astype(jnp.bfloat16)
            d_value = product(probs[i, 2 * p], only(c_pair, 0))
            d_value += product(probs[i, 2 * p + 1], only(c_pair, 1))
            return product_t(stacked, c_pair), k_turned, d_value

        def score_base(p, h):
            return (2 * (p % 2) + h) * 2 * 128

        def score_grads(p, both):
            for h in range(2):
                for span in spans:
                    prob = probs[i, 2 * p + h, :, span].astype(jnp.float32)
                    d_prob = both[h * rows : (h + 1) * rows, span]
                    drift = jnp.sum(d_prob * prob, axis=0, keepdims=True)
                    at = score_base(p, h)
                    active[1, :, at + span.start : at + span.stop] = (prob * (d_prob - drift)).astype(jnp.bfloat16)
            return [active[1, :, score_base(p, h) : score_base(p, h) + rows] for h in range(2)]

        def closed(p, found, k_turned):
            q_pair = query[i, :, lanes_of(p)]
            d_key = product(found[0], only(q_pair, 0)) + product(found[1], only(q_pair, 1))
            return d_key, [product(k_turned[h * head : (h + 1) * head], found[h]) for h in range(2)]

        def place_grads(p, d_value, d_key, parts):
            place_grad(0, p, jnp.concatenate(parts, axis=0).T * (1.0 / math.sqrt(head)))
            place_grad(1, p, d_key)
            place_grad(2, p, d_value)

        ahead = opened(0)
        waiting = None
        d_source = None

        def source_grad(group):
            found = None
            for n in range(3):
                at = n * width + group * 2 * pair_width
                piece = product(
                    staged[slot, :, base + at : base + at + 2 * pair_width], wqkv_t[at : at + 2 * pair_width, :]
                )
                found = piece if found is None else found + piece
            return found

        for p in range(pairs):
            both, k_turned, d_value = ahead
            if p + 1 < pairs:
                ahead = opened(p + 1)
            if waiting is not None:
                place_grads(*waiting)
            if p in (2, 4):
                piece = source_grad(p // 2 - 1)
                d_source = piece if d_source is None else d_source + piece
            found = score_grads(p, both)
            d_key, parts = closed(p, found, k_turned)
            waiting = (p, d_value, d_key, parts)
        place_grads(*waiting)
        d_source += source_grad(pairs // 2 - 1)
        sums = None
        for at in blocks:
            result[i, at, :] = (wide1[at, :] + d_source[at]).astype(jnp.bfloat16)
            terms = [
                folded(staged[slot, at, base : base + width].astype(jnp.float32)),
                folded(staged[slot, at, base + 2 * width : base + 3 * width].astype(jnp.float32)),
            ]
            sums = terms if sums is None else [a + b for a, b in zip(sums, terms)]
        single("bq", sums[0])
        single("bv", sums[1])

    small_ref[...] = jnp.zeros_like(small_ref)
    side = 256
    unit = lax.broadcasted_iota(jnp.int32, (side, side), 0) == lax.broadcasted_iota(jnp.int32, (side, side), 1)
    unit = jnp.where(unit, 1.0, 0.0).astype(jnp.bfloat16)

    def turn_weights():
        for natural, turned in ((wqkv, wqkv_t), (wo, wo_t), (wu, wu_t), (wd, wd_t)):
            for block in range(0, natural.shape[0], width):

                def one(n, carry):
                    at = pl.ds(pl.multiple_of(n * side, side), side)
                    tall = product_t(unit, natural[block : block + width, at])
                    turned[at, block : block + width] = tall.astype(jnp.bfloat16)
                    return carry

                lax.fori_loop(0, natural.shape[1] // side, one, 0)

    @pl.when(section == 1)
    def _():
        for copy in weight_copies:
            copy.wait()
        turn_weights()

    def forward_step(i, carry):
        @pl.when(section == 0)
        def _():
            assemble(i)

        @pl.when(section == 1)
        def _():
            forward_copy(i).wait_recv()

        @pl.when(i >= 2)
        def _():
            for n in range(3):
                save(i - 2, n).wait()

        forward(i)

        @pl.when((section == 0) & ((core == 0) | (i == items - 1)))
        def _():
            forward_copy(i).start()

        for n in range(5):
            save(i, n).start()
        return carry

    lax.fori_loop(0, items, forward_step, 0)

    @pl.when(section == 0)
    def _():
        turn_weights()

    @pl.when(section == 1)
    def _():
        cotangent_copy.wait()

    def backward_step(i, carry):
        @pl.when(section == 0)
        def _():
            back_copy(i).wait_recv()

        @pl.when(i >= 2)
        def _():
            staged_save(i - 2).wait()
            early_save(i - 2).wait()

        save(i, 4).wait()

        @pl.when(section == 0)
        def _():
            forward_copy(i).wait_send()

        backward(i)

        @pl.when(section == 1)
        def _():
            back_copy(i).start()

        staged_save(i).start()
        grad_save(i).start()
        return carry

    lax.fori_loop(0, items, backward_step, 0)

    def finish(i, carry):
        save(i, 3).wait()
        grad_save(i).wait()

        @pl.when(i >= items - 2)
        def _():
            staged_save(i).wait()
            early_save(i).wait()
            for n in range(1, 3):
                save(i, n).wait()

        @pl.when(section == 1)
        def _():
            back_copy(i).wait_send()

        return carry

    lax.fori_loop(0, items, finish, 0)


def layered(image_ids, caption_lengths, captions, regions, cotangent, stacked):
    items, cap_rows, width = captions.shape
    held, region_rows, _ = regions.shape
    rows = cap_rows + region_rows
    inner = stacked[9].shape[2]
    low = jnp.bfloat16
    wide = inner // width

    def cells(*shape):
        return pltpu.VMEM(shape, low)

    anywhere = pl.BlockSpec(memory_space=pl.ANY)
    local = pl.BlockSpec(memory_space=pltpu.VMEM)
    scalars = pl.BlockSpec(memory_space=pltpu.SMEM)
    return pl.pallas_call(
        layer_kernel,
        out_shape=(
            jax.ShapeDtypeStruct((1, items, rows, width), low),
            jax.ShapeDtypeStruct((1, items, rows, width), low),
            jax.ShapeDtypeStruct((items * rows, (3 + wide) * width), low),
            jax.ShapeDtypeStruct((items * rows, (5 + wide) * width), low),
            jax.ShapeDtypeStruct((GROUP, width), jnp.float32),
        ),
        in_specs=[scalars, scalars, anywhere, local, anywhere]
        + [anywhere if len(member.shape) == 3 else local for member in stacked],
        out_specs=(anywhere, anywhere, anywhere, anywhere, local),
        scratch_shapes=[
            cells(width, 3 * width),
            cells(width, width),
            cells(width, inner),
            cells(inner, width),
            cells(3 * width, width),
            cells(width, width),
            cells(inner, width),
            cells(width, inner),
            cells(3 * held, region_rows, width),
            cells(items, rows, width),
            cells(items, rows, width),
            cells(items, rows, width),
            cells(items, rows, width),
            cells(items, rows, width),
            cells(items, HEADS, rows, rows),
            cells(2, rows, width),
            cells(items, rows, width),
            cells(items, rows, width),
            cells(2, rows, width),
            cells(2, rows, inner),
            cells(items, rows, inner),
            cells(items, rows, width),
            cells(2, rows, (5 + wide) * width),
            pltpu.VMEM((items, rows, 2), jnp.float32),
            pltpu.VMEM((rows, width), jnp.float32),
            cells(cap_rows, items, width),
            pltpu.SemaphoreType.DMA((8,)),
            pltpu.SemaphoreType.DMA((2,)),
            pltpu.SemaphoreType.DMA((2,)),
            pltpu.SemaphoreType.DMA((items,)),
            pltpu.SemaphoreType.DMA((items,)),
            pltpu.SemaphoreType.DMA((items,)),
            pltpu.SemaphoreType.DMA((items,)),
            pltpu.SemaphoreType.DMA((items, 8)),
        ],
        compiler_params=pltpu.CompilerParams(
            collective_id=0, has_side_effects=True, vmem_limit_bytes=VMEM_LIMIT
        ),
        cost_estimate=pl.CostEstimate(
            flops=4 * items * rows * (4 + 2 * wide) * width * width,
            bytes_accessed=60_000_000,
            transcendentals=0,
        ),
    )(image_ids, caption_lengths, captions.transpose(1, 0, 2), regions, cotangent, *stacked)


def body(
    captions,
    regions,
    image_ids,
    caption_lengths,
    cotangent,
    query_weight,
    query_bias,
    key_weight,
    value_weight,
    value_bias,
    out_weight,
    out_bias,
    norm1_gain,
    norm1_bias,
    up_weight,
    up_bias,
    down_weight,
    down_bias,
    norm2_gain,
    norm2_bias,
):
    stacked = (
        query_weight,
        query_bias,
        key_weight,
        value_weight,
        value_bias,
        out_weight,
        out_bias,
        norm1_gain,
        norm1_bias,
        up_weight,
        up_bias,
        down_weight,
        down_bias,
        norm2_gain,
        norm2_bias,
    )
    states, input_grads, a_side, b_side, small = layered(
        image_ids, caption_lengths, captions, regions, cotangent, stacked
    )
    sums, small_sums = reduced(a_side, b_side, small, lax.axis_size("batch"))
    return tuple(spread(sums, small_sums, states, input_grads, stacked))


def solution(mesh):
    placed = (
        P("batch", None, None),
        P("batch", None, None),
        P("batch"),
        P("batch"),
        P("batch", None, None),
        P("section", None, None),
        P("section", None),
        P("section", None, None),
        P("section", None, None),
        P("section", None),
        P("section", None, None),
        P("section", None),
        P("section", None),
        P("section", None),
        P("section", None, None),
        P("section", None),
        P("section", None, None),
        P("section", None),
        P("section", None),
        P("section", None),
    )
    return jax.shard_map(
        body,
        mesh=mesh,
        in_specs=placed,
        out_specs=(
            P("section", "batch", None, None),
            P("section", "batch", None, None),
            P("section", None, None),
            P("section", None),
            P("section", None, None),
            P("section", None, None),
            P("section", None),
            P("section", None, None),
            P("section", None),
            P("section", None),
            P("section", None),
            P("section", None, None),
            P("section", None),
            P("section", None, None),
            P("section", None),
            P("section", None),
            P("section", None),
        ),
        check_vma=False,
    )
```

```python
import functools
import math

import jax
import jax.numpy as jnp
from jax import lax
from jax.experimental import pallas as pl
from jax.experimental.pallas import tpu as pltpu
from jax.sharding import PartitionSpec as P

HEADS = 12
EPSILON = 1e-12
MESH = pl.DeviceIdType.MESH
VMEM_LIMIT = 63 * 1024 * 1024
VMEM_BESIDE = 47 * 1024 * 1024
GROUP = 16
CHUNK_GROUPS = 16
SLOTS = 18
SLOT_GROUPS = 24
LAG = 3
EARLY = 6
LINE = 4
SPLIT_BITS = 4


def reduce_kernel(
    bits,
    chunks,
    a_hbm,
    b_hbm,
    small_ref,
    whole,
    small_out,
    a_ref,
    b_ref,
    acc,
    recv,
    small_acc,
    small_recv,
    load_sem,
    send_sem,
    recv_sem,
    small_send_sem,
    small_recv_sem,
):
    width = acc.shape[2]
    extra = bits - SPLIT_BITS
    first_gather = SPLIT_BITS + 1 + extra
    stages = 2 * (SPLIT_BITS + 1) + extra
    me = lax.axis_index("batch")
    section = lax.axis_index("section")
    core, side, place = me % 2, (me // 2) % 2, (me // 4) % LINE
    blocks_a = a_hbm.shape[1] // width
    blocks_b = b_hbm.shape[1] // width
    per_block = width // (CHUNK_GROUPS * GROUP)

    def load(source, target, block, base):
        lanes = pl.ds(block * width, width)
        return pltpu.make_async_copy(source.at[:, lanes], target.at[:, lanes], load_sem.at[base + block])

    def load_a(block):
        return load(a_hbm, a_ref, block, 0)

    def load_b(block):
        return load(b_hbm, b_ref, block, blocks_a)

    wide = blocks_a - 3
    first_use = {0: [(load_a, 0), (load_b, 0)]}
    for j in range(1, wide):
        first_use[j] = [(load_a, j)]
    first_use[wide] = [(load_a, wide), (load_b, 1)]
    for j in range(1, wide):
        first_use[wide + j] = [(load_b, 1 + j)]
    first_use[2 * wide] = [(load_a, wide + 1), (load_b, wide + 1)]
    first_use[2 * wide + 1] = [(load_a, wide + 2), (load_b, wide + 2)]
    first_use[2 * wide + 2] = [(load_b, wide + 3)]
    first_use[2 * wide + 3] = [(load_b, wide + 4)]
    for j in range(2 * wide + 4):
        for kind, block in first_use[j]:
            kind(block).start()

    def bit_mate(k):
        bit = (me // 2**k) % 2
        return (section, me + 2**k * (1 - 2 * bit))

    core_mate, side_mate = bit_mate(0), bit_mate(1)
    mates = ((section, me - LINE), (section, me + LINE))
    ring = [(section, me + LINE * ((place + d) % LINE - place)) for d in (LINE - 1, 1)]

    barrier = pltpu.get_barrier_semaphore()
    for peer in [core_mate, side_mate] + ring + [bit_mate(k) for k in range(2, bits)]:
        pl.semaphore_signal(barrier, inc=1, device_id=peer, device_id_type=MESH)
    pl.semaphore_wait(barrier, bits + 2)

    def low_core(c):
        return c * CHUNK_GROUPS + core * 8

    def low_side(c):
        return low_core(c) + side * 4

    def block_start(c, kind, b):
        return low_side(c) + b if kind == 0 else low_core(c) + 2 * b

    def final(c, kind):
        return low_side(c) + place if kind == 0 else low_core(c) + 2 * place + side

    def remote(c, source, start, size, target, spot, index, peer):
        return pltpu.make_async_remote_copy(
            src_ref=source.at[pl.ds(start, size)],
            dst_ref=target.at[lax.rem(c, SLOTS), pl.ds(spot, size)] if target is recv else target.at[pl.ds(start, size)],
            send_sem=send_sem.at[lax.rem(c, SLOTS), index],
            recv_sem=recv_sem.at[lax.rem(c, SLOTS), index],
            device_id=peer,
            device_id_type=MESH,
        )

    def core_copy(c):
        return remote(c, acc, c * CHUNK_GROUPS + (1 - core) * 8, 8, recv, 0, 0, core_mate)

    def side_copy(c, kind):
        if kind == 0:
            return remote(c, acc, low_core(c) + (1 - side) * 4, 4, recv, 8, 1, side_mate)
        return remote(c, acc, low_core(c) + 2 * place + (1 - side), 1, recv, 8, 1, side_mate)

    def line_copy(c, kind, r, d):
        size = 1 + kind
        b = jnp.minimum(3 - r + place, 3) if d == 1 else jnp.maximum(r - 3 + place, 0)
        spot = 12 + 2 * (2 * r + d)
        return remote(c, acc, block_start(c, kind, b), size, recv, spot, 2 + 2 * r + d, mates[d])

    def spread_copy(c, kind, r, d):
        size = 1 + kind
        b = jnp.maximum(place - r, 0) if d == 1 else jnp.minimum(place + r, 3)
        return remote(c, whole, block_start(c, kind, b), size, whole, 0, 8 + 2 * r + d, mates[d])

    def side_back_copy(c, kind):
        if kind == 0:
            return remote(c, whole, low_side(c), 4, whole, 0, 14, side_mate)
        return remote(c, whole, final(c, kind), 1, whole, 0, 14, side_mate)

    def core_back_copy(c):
        return remote(c, whole, low_core(c), 8, whole, 0, 15, core_mate)

    def extra_copy(c, kind, e):
        return remote(c, acc, final(c, kind), 1, recv, 24 + e, 16 + e, bit_mate(SPLIT_BITS + e))

    def add_groups(start, count, c, spot):
        slot = lax.rem(c, SLOTS)
        for g in range(count):
            total = acc[start + g].astype(jnp.float32) + recv[slot, spot + g].astype(jnp.float32)
            acc[start + g] = total.astype(jnp.bfloat16)

    def name_of(kind, s):
        if s == 0:
            return ("core",)
        if s == stages - 1:
            return ("core_back",)
        if s < SPLIT_BITS + 1:
            order = [("side",), ("line", 0), ("line", 1), ("line", 2)]
            order = order if kind == 0 else order[1:] + order[:1]
            return order[s - 1]
        if s < first_gather:
            return ("extra", s - SPLIT_BITS - 1)
        order = [("spread", 0), ("spread", 1), ("spread", 2), ("side_back",)]
        order = order if kind == 0 else order[3:] + order[:3]
        return order[s - first_gather]

    def start_stage(c, kind, s):
        name = name_of(kind, s)
        if s == first_gather:
            whole[final(c, kind)] = acc[final(c, kind)]
        if name[0] == "core":
            core_copy(c).start()
        elif name[0] == "side":
            side_copy(c, kind).start()
        elif name[0] == "line":
            r = name[1]
            pl.when(place <= r)(lambda: line_copy(c, kind, r, 1).start())
            pl.when(place >= 3 - r)(lambda: line_copy(c, kind, r, 0).start())
        elif name[0] == "extra":
            extra_copy(c, kind, name[1]).start()
        elif name[0] == "spread":
            r = name[1]
            pl.when((place >= r) & (place <= 2))(lambda: spread_copy(c, kind, r, 1).start())
            pl.when((place >= 1) & (place <= 3 - r))(lambda: spread_copy(c, kind, r, 0).start())
        elif name[0] == "side_back":
            side_back_copy(c, kind).start()
        else:
            core_back_copy(c).start()

    def finish_stage(c, kind, s):
        name = name_of(kind, s)
        if name[0] == "core":
            core_copy(c).wait()
            add_groups(low_core(c), 8, c, 0)
        elif name[0] == "side":
            side_copy(c, kind).wait()
            if kind == 0:
                add_groups(low_side(c), 4, c, 8)
            else:
                add_groups(final(c, kind), 1, c, 8)
        elif name[0] == "line":
            r = name[1]

            @pl.when(place <= r)
            def _():
                line_copy(c, kind, r, 1).wait_send()

            @pl.when(place >= 3 - r)
            def _():
                line_copy(c, kind, r, 0).wait_send()

            @pl.when((place >= 1) & (place <= r + 1))
            def _():
                line_copy(c, kind, r, 1).wait_recv()
                add_groups(block_start(c, kind, 2 - r + place), 1 + kind, c, 12 + 2 * (2 * r + 1))

            @pl.when((place <= 2) & (place >= 2 - r))
            def _():
                line_copy(c, kind, r, 0).wait_recv()
                add_groups(block_start(c, kind, r - 2 + place), 1 + kind, c, 12 + 2 * (2 * r))

        elif name[0] == "extra":
            extra_copy(c, kind, name[1]).wait()
            add_groups(final(c, kind), 1, c, 24 + name[1])
        elif name[0] == "spread":
            r = name[1]
            pl.when((place >= r) & (place <= 2))(lambda: spread_copy(c, kind, r, 1).wait_send())
            pl.when((place >= 1) & (place <= 3 - r))(lambda: spread_copy(c, kind, r, 0).wait_send())
            pl.when(place >= r + 1)(lambda: spread_copy(c, kind, r, 1).wait_recv())
            pl.when(place <= 2 - r)(lambda: spread_copy(c, kind, r, 0).wait_recv())
        elif name[0] == "side_back":
            side_back_copy(c, kind).wait()
        else:
            core_back_copy(c).wait()

    def small_copy(k):
        return pltpu.make_async_remote_copy(
            src_ref=small_acc.at[k],
            dst_ref=small_recv.at[k],
            send_sem=small_send_sem.at[k],
            recv_sem=small_recv_sem.at[k],
            device_id=bit_mate(k),
            device_id_type=MESH,
        )

    small_acc[0] = small_ref[...]

    def kind_of(c):
        early = 1 - jnp.minimum(c // EARLY, 1)
        return early * (c % 2) + (1 - early) * ((c - EARLY + 4) % 4 // 3)

    def step(t, carry):
        for s in range(stages, 0, -1):
            c = t - LAG * s
            for kind in range(2):

                @pl.when((c >= 0) & (c < chunks) & (kind_of(c) == kind))
                def _():
                    finish_stage(c, kind, s - 1)
                    if s < stages:
                        start_stage(c, kind, s)

        for j in range(2 * wide + 4):

            @pl.when(t == per_block * j)
            def _():
                for kind, block in first_use[j]:
                    kind(block).wait()

        @pl.when(t < chunks)
        def _():
            block, part = t // per_block, t % per_block
            a_col = jnp.minimum(block, wide) + jnp.minimum(block // (2 * wide), 1) + jnp.minimum(block // (2 * wide + 1), 1)
            b_col = jnp.maximum(block - wide + 1, 0)
            lines = CHUNK_GROUPS * GROUP
            left = a_ref[:, pl.ds(pl.multiple_of(a_col * width + part * lines, lines), lines)]
            right = b_ref[:, pl.ds(pl.multiple_of(b_col * width, width), width)]
            grad = lax.dot_general(left, right, (((0,), (0,)), ((), ())), preferred_element_type=jnp.float32)
            acc[pl.ds(t * CHUNK_GROUPS, CHUNK_GROUPS)] = grad.astype(jnp.bfloat16).reshape(
                CHUNK_GROUPS, GROUP, width
            )
            core_copy(t).start()

        for k in range(bits + 1):

            @pl.when(t == LAG * k)
            def _():
                if k > 0:
                    small_copy(k - 1).wait()
                    small_acc[k] = small_acc[k - 1] + small_recv[k - 1]
                if k < bits:
                    small_copy(k).start()

        return carry

    lax.fori_loop(0, chunks + LAG * stages, step, 0)
    small_out[...] = small_acc[bits]


def reduced(a_side, b_side, small, count):
    rows = a_side.shape[0]
    width = small.shape[1]
    bits = count.bit_length() - 1
    extra = bits - SPLIT_BITS
    blocks = 2 * (a_side.shape[1] // width - 3) + 4
    chunks = blocks * width // (CHUNK_GROUPS * GROUP)
    groups = chunks * CHUNK_GROUPS
    loads = (a_side.shape[1] + b_side.shape[1]) // width
    return pl.pallas_call(
        functools.partial(reduce_kernel, bits, chunks),
        out_shape=(
            pltpu.VMEM((groups, GROUP, width), jnp.bfloat16),
            jax.ShapeDtypeStruct(small.shape, jnp.float32),
        ),
        in_specs=[
            pl.BlockSpec(memory_space=pl.ANY),
            pl.BlockSpec(memory_space=pl.ANY),
            pl.BlockSpec(memory_space=pltpu.VMEM),
        ],
        out_specs=(pl.BlockSpec(memory_space=pltpu.VMEM), pl.BlockSpec(memory_space=pltpu.VMEM)),
        scratch_shapes=[
            pltpu.VMEM(a_side.shape, jnp.bfloat16),
            pltpu.VMEM(b_side.shape, jnp.bfloat16),
            pltpu.VMEM((groups, GROUP, width), jnp.bfloat16),
            pltpu.VMEM((SLOTS, SLOT_GROUPS + extra, GROUP, width), jnp.bfloat16),
            pltpu.VMEM((bits + 1,) + small.shape, jnp.float32),
            pltpu.VMEM((bits,) + small.shape, jnp.float32),
            pltpu.SemaphoreType.DMA((loads,)),
            pltpu.SemaphoreType.DMA((SLOTS, 16 + extra)),
            pltpu.SemaphoreType.DMA((SLOTS, 16 + extra)),
            pltpu.SemaphoreType.DMA((bits,)),
            pltpu.SemaphoreType.DMA((bits,)),
        ],
        compiler_params=pltpu.CompilerParams(
            collective_id=1, has_side_effects=True, vmem_limit_bytes=VMEM_BESIDE
        ),
        cost_estimate=pl.CostEstimate(
            flops=2 * rows * blocks * width * width, bytes_accessed=80_000_000, transcendentals=0
        ),
    )(a_side, b_side, small)


PIECE = 768
DEPTH = 4


def spread_kernel(sum_ref, small_ref, states_hbm, grads_hbm, *refs):
    width = small_ref.shape[1]
    (o_wq, o_bq, o_wk, o_wv, o_bv, o_wo, o_bo, o_g1, o_s1, o_up, o_bu, o_dn, o_bd, o_g2, o_s2) = refs[2:17]
    states_out, grads_out = refs[:2]
    given, held, out_sem, held_sem = refs[17:]
    wide = o_bu.shape[1] // width
    targets = []
    for j in range(wide):
        targets += [o_dn.at[0, pl.ds(j * width + r, PIECE), :] for r in range(0, width, PIECE)]
    for j in range(wide):
        targets += [o_up.at[0, pl.ds(r, PIECE), pl.ds(j * width, width)] for r in range(0, width, PIECE)]
    for ref in (o_wo, o_wq, o_wk, o_wv):
        targets += [ref.at[0, pl.ds(r, PIECE), :] for r in range(0, width, PIECE)]

    items = states_hbm.shape[1]
    passes = [(states_hbm.at[0, i], states_out.at[0, i]) for i in range(items)]
    passes += [(grads_hbm.at[0, i], grads_out.at[0, i]) for i in range(items)]

    def pass_in(i):
        return pltpu.make_async_copy(passes[i][0], held.at[i], held_sem.at[i])

    def pass_out(i):
        return pltpu.make_async_copy(held.at[i], passes[i][1], held_sem.at[i])

    def store(i):
        return pltpu.make_async_copy(given.at[i % DEPTH], targets[i], out_sem.at[i % DEPTH])

    for i in range(len(passes)):
        pass_in(i).start()
    singles = [o_bq, o_bv, o_bo, o_g1, o_s1, o_bd, o_g2, o_s2]
    for i, ref in enumerate(singles):
        ref[...] = small_ref[pl.ds(i, 1), :]
    for j in range(wide):
        o_bu[:, pl.ds(j * width, width)] = small_ref[pl.ds(len(singles) + j, 1), :]
    for i in range(len(targets)):
        if i >= DEPTH:
            store(i - DEPTH).wait()

        def convert(r, carry):
            block = sum_ref[pl.ds(i * (PIECE // GROUP) + r * 4, 4)].astype(jnp.float32)
            rows = pl.ds(pl.multiple_of(r * 4 * GROUP, 4 * GROUP), 4 * GROUP)
            given[i % DEPTH, rows, :] = block.reshape(4 * GROUP, width)
            return carry

        lax.fori_loop(0, PIECE // (4 * GROUP), convert, 0)
        store(i).start()
        if i < len(passes):
            pass_in(i).wait()
            pass_out(i).start()
    for i in range(len(targets) - DEPTH, len(targets)):
        store(i).wait()
    for i in range(len(passes)):
        pass_out(i).wait()


def spread(sums, small, states, input_grads, params):
    width = small.shape[1]
    anywhere = pl.BlockSpec(memory_space=pl.ANY)
    local = pl.BlockSpec(memory_space=pltpu.VMEM)
    return pl.pallas_call(
        spread_kernel,
        out_shape=(
            jax.ShapeDtypeStruct(states.shape, states.dtype),
            jax.ShapeDtypeStruct(input_grads.shape, input_grads.dtype),
        )
        + tuple(jax.ShapeDtypeStruct(member.shape, jnp.float32) for member in params),
        in_specs=[local, local, anywhere, anywhere],
        out_specs=(anywhere, anywhere)
        + tuple(anywhere if len(member.shape) == 3 else local for member in params),
        scratch_shapes=[
            pltpu.VMEM((DEPTH, PIECE, width), jnp.float32),
            pltpu.VMEM((2 * states.shape[1],) + states.shape[2:], states.dtype),
            pltpu.SemaphoreType.DMA((DEPTH,)),
            pltpu.SemaphoreType.DMA((2 * states.shape[1],)),
        ],
        compiler_params=pltpu.CompilerParams(vmem_limit_bytes=VMEM_BESIDE),
        cost_estimate=pl.CostEstimate(
            flops=12 * width * width, bytes_accessed=80 * width * width, transcendentals=0
        ),
    )(pltpu.with_memory_space_constraint(sums, pltpu.VMEM), small, states, input_grads)


HALF_LOG = -0.5 / math.log(2.0)
BELL_SCALE = 1.0 / math.sqrt(2.0 * math.pi)
SINGLES = ("bq", "bv", "bo", "g1", "s1", "bd", "g2", "s2")


def product(left, right):
    return lax.dot_general(left, right, (((1,), (0,)), ((), ())), preferred_element_type=jnp.float32)


def product_t(left, right):
    return lax.dot_general(left, right, (((1,), (1,)), ((), ())), preferred_element_type=jnp.float32)


def gelu_pair(z):
    cdf = 0.5 * lax.erf(z * (1.0 / math.sqrt(2.0))) + 0.5
    bell = jnp.exp2(z * z * HALF_LOG)
    return z * cdf, z * BELL_SCALE * bell + cdf


def normed(values):
    average = jnp.mean(values, axis=-1, keepdims=True)
    centered = values - average
    inverse = lax.rsqrt(jnp.mean(centered * centered, axis=-1, keepdims=True) + EPSILON)
    return centered * inverse, inverse


def normed_back(grad, normal, inverse):
    first_mean = jnp.mean(grad, axis=-1, keepdims=True)
    second_mean = jnp.mean(grad * normal, axis=-1, keepdims=True)
    return inverse * (grad - first_mean - normal * second_mean)


def layer_kernel(
    ids_ref,
    lengths_ref,
    captions_hbm,
    regions_ref,
    cotangent_hbm,
    wq_hbm,
    bq_ref,
    wk_hbm,
    wv_hbm,
    bv_ref,
    wo_hbm,
    bo_ref,
    g1_ref,
    s1_ref,
    wu_hbm,
    bu_ref,
    wd_hbm,
    bd_ref,
    g2_ref,
    s2_ref,
    states_hbm,
    grads_hbm,
    a_hbm,
    b_hbm,
    small_ref,
    wqkv,
    wo,
    wu,
    wd,
    wqkv_t,
    wo_t,
    wu_t,
    wd_t,
    table,
    hidden,
    upstream,
    query,
    keys,
    values,
    probs,
    context,
    normal1,
    normal2,
    lowered,
    active,
    slope,
    result,
    staged,
    inverses,
    wide1,
    caption_cells,
    weight_sem,
    table_send,
    table_recv,
    fwd_send,
    fwd_recv,
    back_send,
    back_recv,
    out_sem,
):
    items, rows, width = hidden.shape
    held = regions_ref.shape[0]
    cap_rows = captions_hbm.shape[0]
    wide = wu.shape[1] // width
    pairs = HEADS // 2
    pair_width = width // pairs
    head = width // HEADS
    section = lax.axis_index("section")
    batch = lax.axis_index("batch")
    count = lax.axis_size("batch")
    right = (section, lax.rem(batch + 1, count))
    left = (section, lax.rem(batch + count - 1, count))
    other = (1 - section, batch)
    core = lax.rem(batch, 2)

    weight_copies = [
        pltpu.make_async_copy(source.at[0], target, weight_sem.at[n])
        for n, (source, target) in enumerate(
            (
                (wq_hbm, wqkv.at[:, pl.ds(0, width)]),
                (wk_hbm, wqkv.at[:, pl.ds(width, width)]),
                (wv_hbm, wqkv.at[:, pl.ds(2 * width, width)]),
                (wo_hbm, wo),
                (wu_hbm, wu),
                (wd_hbm, wd),
            )
        )
    ]
    for copy in weight_copies[:3]:
        copy.start()
    cotangent_copy = pltpu.make_async_copy(cotangent_hbm, upstream, weight_sem.at[6])

    barrier = pltpu.get_barrier_semaphore()
    for peer in (right, left, other):
        pl.semaphore_signal(barrier, inc=1, device_id=peer, device_id_type=MESH)
    pl.semaphore_wait(barrier, 3)

    def table_copy(n, peer):
        return pltpu.make_async_remote_copy(
            src_ref=regions_ref,
            dst_ref=table.at[pl.ds(2 * n * held, held)],
            send_sem=table_send.at[n],
            recv_sem=table_recv.at[n],
            device_id=peer,
            device_id_type=MESH,
        )

    @pl.when(section == 0)
    def _():
        caption_copy = pltpu.make_async_copy(captions_hbm, caption_cells, weight_sem.at[7])
        caption_copy.start()
        table_copy(0, right).start()
        table_copy(1, left).start()
        table[pl.ds(held, held)] = regions_ref[...]
        table_copy(0, right).wait()
        table_copy(1, left).wait()
        caption_copy.wait()

    for copy in weight_copies[3:]:
        copy.start()

    @pl.when(section == 1)
    def _():
        cotangent_copy.start()

    def forward_copy(i):
        return pltpu.make_async_remote_copy(
            src_ref=result.at[i],
            dst_ref=hidden.at[i],
            send_sem=fwd_send.at[i],
            recv_sem=fwd_recv.at[i],
            device_id=other,
            device_id_type=MESH,
        )

    def back_copy(i):
        return pltpu.make_async_remote_copy(
            src_ref=result.at[i],
            dst_ref=upstream.at[i],
            send_sem=back_send.at[i],
            recv_sem=back_recv.at[i],
            device_id=other,
            device_id_type=MESH,
        )

    def save(i, n):
        at = pl.ds(pl.multiple_of(i * rows, rows), rows)
        first = wide * width
        turn = lax.rem(i, 2)
        if n == 0:
            source, target = active.at[turn], a_hbm.at[at, pl.ds(0, first)]
        elif n == 1:
            source, target = lowered.at[turn], a_hbm.at[at, pl.ds(first, width)]
        elif n == 2:
            source, target = context.at[turn], a_hbm.at[at, pl.ds(first + width, width)]
        elif n == 3:
            source, target = hidden.at[i], a_hbm.at[at, pl.ds(first + 2 * width, width)]
        else:
            source, target = result.at[i], states_hbm.at[0, i]
        return pltpu.make_async_copy(source, target, out_sem.at[i, n])

    def staged_save(i):
        at = pl.ds(pl.multiple_of(i * rows, rows), rows)
        lanes = pl.ds((1 + wide) * width, 4 * width)
        return pltpu.make_async_copy(
            staged.at[lax.rem(i, 2), :, lanes], b_hbm.at[at, lanes], out_sem.at[i, 5]
        )

    def early_save(i):
        at = pl.ds(pl.multiple_of(i * rows, rows), rows)
        lanes = pl.ds(0, (1 + wide) * width)
        return pltpu.make_async_copy(
            staged.at[lax.rem(i, 2), :, lanes], b_hbm.at[at, lanes], out_sem.at[i, 7]
        )

    def grad_save(i):
        return pltpu.make_async_copy(result.at[i], grads_hbm.at[0, i], out_sem.at[i, 6])

    def vector(ref, j=0):
        return ref[:, j * width : (j + 1) * width].astype(jnp.float32)

    lane = lax.broadcasted_iota(jnp.int32, (rows, pair_width), 1)

    blocks = [slice(r, r + GROUP) for r in range(0, rows, GROUP)]
    spans = [slice(c, min(c + 128, rows)) for c in range(0, rows, 128)]

    def only(block, h):
        return jnp.where((lane // head) == h, block, jnp.zeros_like(block))

    def assemble(i):
        total = count * held
        spot = jnp.minimum(lax.rem(ids_ref[i] - (batch - 1) * held + total, total), 3 * held - 1)
        for n in range(items):

            @pl.when(i == n)
            def _():
                whole = jnp.concatenate(
                    [caption_cells[:, n, :].astype(jnp.float32), table[spot].astype(jnp.float32)], axis=0
                )
                hidden[n] = whole.astype(jnp.bfloat16)

    def forward(i):
        @pl.when((i == 0) & (section == 0))
        def _():
            for copy in weight_copies[:3]:
                copy.wait()

        turn = lax.rem(i, 2)
        source = hidden[i]
        mixed = product(source, wqkv[...])
        for at in blocks:
            scaled = (mixed[at, :width] + vector(bq_ref)) * (1.0 / math.sqrt(head))
            query[i, at, :] = scaled.astype(jnp.bfloat16)
            keys[i, at, :] = mixed[at, width : 2 * width].astype(jnp.bfloat16)
            values[i, at, :] = (mixed[at, 2 * width :] + vector(bv_ref)).astype(jnp.bfloat16)
        position = lax.broadcasted_iota(jnp.int32, (rows, 1), 0)
        live = (position >= cap_rows) | (position < lengths_ref[i])
        key_bias = jnp.where(live, 0.0, -1000000000.0)

        def wait_rest():
            @pl.when((i == 0) & (section == 0))
            def _():
                for copy in weight_copies[3:]:
                    copy.wait()

        def lanes_of(p):
            return slice(p * pair_width, (p + 1) * pair_width)

        def scored(p):
            k_pair = keys[i, :, lanes_of(p)]
            stacked = jnp.concatenate([only(k_pair, 0), only(k_pair, 1)], axis=0)
            v_turned = values[i, :, lanes_of(p)].astype(jnp.float32).T.astype(jnp.bfloat16)
            return product_t(stacked, query[i, :, lanes_of(p)]), v_turned

        def weighed(p, both):
            for h in range(2):
                for span in spans:
                    scores = both[h * rows : (h + 1) * rows, span] + key_bias
                    expo = jnp.exp(scores - jnp.max(scores, axis=0, keepdims=True))
                    share = pltpu.reciprocal(jnp.sum(expo, axis=0, keepdims=True), approx=True)
                    probs[i, 2 * p + h, :, span] = (expo * share).astype(jnp.bfloat16)

        def mixed_values(p, v_turned):
            return [product(v_turned[h * head : (h + 1) * head], probs[i, 2 * p + h]) for h in range(2)]

        def place_context(p, parts):
            context[turn, :, lanes_of(p)] = jnp.concatenate(parts, axis=0).T.astype(jnp.bfloat16)

        def projected(group):
            lanes = slice(group * 2 * pair_width, (group + 1) * 2 * pair_width)
            return product(context[turn, :, lanes], wo[lanes, :])

        ahead = scored(0)
        parts = None
        attended = None
        for p in range(pairs):
            both, v_turned = ahead
            if p + 1 < pairs:
                ahead = scored(p + 1)
            if parts is not None:
                place_context(p - 1, parts)
            if p in (2, 4):
                if p == 2:
                    wait_rest()
                piece = projected(p // 2 - 1)
                attended = piece if attended is None else attended + piece
            weighed(p, both)
            parts = mixed_values(p, v_turned)
        place_context(pairs - 1, parts)
        attended += projected(pairs // 2 - 1)

        @pl.when((section == 0) & (core == 1) & (i >= 1))
        def _():
            forward_copy(i - 1).start()

        for at in blocks:
            n1, inv1 = normed(hidden[i, at, :].astype(jnp.float32) + attended[at] + vector(bo_ref))
            normal1[i, at, :] = n1.astype(jnp.bfloat16)
            inverses[i, at, 0:1] = inv1
            first = n1 * vector(g1_ref) + vector(s1_ref)
            lowered[turn, at, :] = first.astype(jnp.bfloat16)
            wide1[at, :] = first + vector(bd_ref)
        half = wide * width // 2

        def raised(n):
            return product(lowered[turn], wu[:, n * half : (n + 1) * half])

        def bend(n, z_tile):
            for part in range(0, half, width):
                lanes = slice(n * half + part, n * half + part + width)
                bias = bu_ref[:, lanes].astype(jnp.float32)
                for at in blocks:
                    gelu, slant = gelu_pair(z_tile[at, part : part + width] + bias)
                    active[turn, at, lanes] = gelu.astype(jnp.bfloat16)
                    slope[i, at, lanes] = slant.astype(jnp.bfloat16)

        z_first = raised(0)
        z_second = raised(1)
        bend(0, z_first)
        wide1[...] += product(active[turn, :, :half], wd[:half, :])
        bend(1, z_second)
        lowest = product(active[turn, :, half:], wd[half:, :])
        for at in blocks:
            n2, inv2 = normed(wide1[at, :] + lowest[at])
            normal2[i, at, :] = n2.astype(jnp.bfloat16)
            inverses[i, at, 1:2] = inv2
            result[i, at, :] = (n2 * vector(g2_ref) + vector(s2_ref)).astype(jnp.bfloat16)

    def folded(value):
        return value[: GROUP // 2] + value[GROUP // 2 :]

    def keep_small(row, value):
        small_ref[row : row + 1, :] += jnp.sum(value, axis=0, keepdims=True)

    def single(name, value):
        keep_small(SINGLES.index(name), value)

    def backward(i):
        slot = lax.rem(i, 2)
        base = (2 + wide) * width

        def stage(at, column, value):
            staged[slot, at, column * width : (column + 1) * width] = value

        def norm_step(at, gradient, normal, layer_norm, gain, sums):
            n = normal[i, at, :].astype(jnp.float32)
            d_res = normed_back(gradient * vector(gain), n, inverses[i, at, layer_norm : layer_norm + 1])
            d_low = d_res.astype(jnp.bfloat16)
            terms = [folded(gradient * n), folded(gradient), folded(d_low.astype(jnp.float32))]
            return d_res, d_low, terms if sums is None else [a + b for a, b in zip(sums, terms)]

        sums = None
        for at in blocks:
            gradient = upstream[i, at, :].astype(jnp.float32)
            d_res, d_low, sums = norm_step(at, gradient, normal2, 1, g2_ref, sums)
            wide1[at, :] = d_res
            stage(at, 0, d_low)
        for name, value in zip(("g2", "s2", "bd"), sums):
            single(name, value)
        d_out = staged[slot, :, :width]
        half = wide * width // 2

        def opened_half(n):
            return product(d_out, wd_t[:, n * half : (n + 1) * half])

        def bent_half(n, d_active):
            for part in range(0, half, width):
                j = (n * half + part) // width
                lanes = slice(j * width, (j + 1) * width)
                total = None
                for at in blocks:
                    d_inner = d_active[at, part : part + width] * slope[i, at, lanes].astype(jnp.float32)
                    d_inner = d_inner.astype(jnp.bfloat16)
                    stage(at, 1 + j, d_inner)
                    term = folded(d_inner.astype(jnp.float32))
                    total = term if total is None else total + term
                keep_small(len(SINGLES) + j, total)

        def closed_half(n):
            at = width + n * half
            return product(staged[slot, :, at : at + half], wu_t[n * half : (n + 1) * half, :])

        d_first = opened_half(0)
        d_second = opened_half(1)
        bent_half(0, d_first)
        d_deep = closed_half(0)
        bent_half(1, d_second)
        d_deeper = closed_half(1)
        early_save(i).start()
        sums = None
        for at in blocks:
            d_res, d_low, sums = norm_step(at, wide1[at, :] + d_deep[at] + d_deeper[at], normal1, 0, g1_ref, sums)
            wide1[at, :] = d_res
            stage(at, 1 + wide, d_low)
        for name, value in zip(("g1", "s1", "bo"), sums):
            single(name, value)
        d_att = staged[slot, :, (1 + wide) * width : (2 + wide) * width]
        @pl.when(i == 0)
        def _():
            save(items - 2, 0).wait()
            save(items - 1, 0).wait()

        active[0, :, :width] = product(d_att, wo_t[...]).astype(jnp.bfloat16)

        def lanes_of(p):
            return slice(p * pair_width, (p + 1) * pair_width)

        def place_grad(n, p, block):
            at = base + n * width + p * pair_width
            staged[slot, :, at : at + pair_width] = block.astype(jnp.bfloat16)

        def opened(p):
            v_pair = values[i, :, lanes_of(p)]
            c_pair = active[0, :, lanes_of(p)]
            stacked = jnp.concatenate([only(v_pair, 0), only(v_pair, 1)], axis=0)
            k_turned = keys[i, :, lanes_of(p)].astype(jnp.float32).T.astype(jnp.bfloat16)
            d_value = product(probs[i, 2 * p], only(c_pair, 0))
            d_value += product(probs[i, 2 * p + 1], only(c_pair, 1))
            return product_t(stacked, c_pair), k_turned, d_value

        def score_base(p, h):
            return (2 * (p % 2) + h) * 2 * 128

        def score_grads(p, both):
            for h in range(2):
                for span in spans:
                    prob = probs[i, 2 * p + h, :, span].astype(jnp.float32)
                    d_prob = both[h * rows : (h + 1) * rows, span]
                    drift = jnp.sum(d_prob * prob, axis=0, keepdims=True)
                    at = score_base(p, h)
                    active[1, :, at + span.start : at + span.stop] = (prob * (d_prob - drift)).astype(jnp.bfloat16)
            return [active[1, :, score_base(p, h) : score_base(p, h) + rows] for h in range(2)]

        def closed(p, found, k_turned):
            q_pair = query[i, :, lanes_of(p)]
            d_key = product(found[0], only(q_pair, 0)) + product(found[1], only(q_pair, 1))
            return d_key, [product(k_turned[h * head : (h + 1) * head], found[h]) for h in range(2)]

        def place_grads(p, d_value, d_key, parts):
            place_grad(0, p, jnp.concatenate(parts, axis=0).T * (1.0 / math.sqrt(head)))
            place_grad(1, p, d_key)
            place_grad(2, p, d_value)

        ahead = opened(0)
        waiting = None
        d_source = None

        def source_grad(group):
            found = None
            for n in range(3):
                at = n * width + group * 2 * pair_width
                piece = product(
                    staged[slot, :, base + at : base + at + 2 * pair_width], wqkv_t[at : at + 2 * pair_width, :]
                )
                found = piece if found is None else found + piece
            return found

        for p in range(pairs):
            both, k_turned, d_value = ahead
            if p + 1 < pairs:
                ahead = opened(p + 1)
            if waiting is not None:
                place_grads(*waiting)
            if p in (2, 4):
                piece = source_grad(p // 2 - 1)
                d_source = piece if d_source is None else d_source + piece
            found = score_grads(p, both)
            d_key, parts = closed(p, found, k_turned)
            waiting = (p, d_value, d_key, parts)
        place_grads(*waiting)
        staged_save(i).start()
        d_source += source_grad(pairs // 2 - 1)
        sums = None
        for at in blocks:
            result[i, at, :] = (wide1[at, :] + d_source[at]).astype(jnp.bfloat16)
            terms = [
                folded(staged[slot, at, base : base + width].astype(jnp.float32)),
                folded(staged[slot, at, base + 2 * width : base + 3 * width].astype(jnp.float32)),
            ]
            sums = terms if sums is None else [a + b for a, b in zip(sums, terms)]
        single("bq", sums[0])
        single("bv", sums[1])

    small_ref[...] = jnp.zeros_like(small_ref)
    side = 256
    unit = lax.broadcasted_iota(jnp.int32, (side, side), 0) == lax.broadcasted_iota(jnp.int32, (side, side), 1)
    unit = jnp.where(unit, 1.0, 0.0).astype(jnp.bfloat16)

    def turn_weights():
        for natural, turned in ((wqkv, wqkv_t), (wo, wo_t), (wu, wu_t), (wd, wd_t)):
            for block in range(0, natural.shape[0], width):

                def one(n, carry):
                    at = pl.ds(pl.multiple_of(n * side, side), side)
                    tall = product_t(unit, natural[block : block + width, at])
                    turned[at, block : block + width] = tall.astype(jnp.bfloat16)
                    return carry

                lax.fori_loop(0, natural.shape[1] // side, one, 0)

    @pl.when(section == 1)
    def _():
        for copy in weight_copies:
            copy.wait()
        turn_weights()

    def forward_step(i, carry):
        @pl.when(section == 0)
        def _():
            assemble(i)

        @pl.when(section == 1)
        def _():
            forward_copy(i).wait_recv()

        @pl.when(i >= 2)
        def _():
            for n in range(3):
                save(i - 2, n).wait()

        forward(i)

        @pl.when((section == 0) & ((core == 0) | (i == items - 1)))
        def _():
            forward_copy(i).start()

        for n in range(5):
            save(i, n).start()
        return carry

    lax.fori_loop(0, items, forward_step, 0)

    @pl.when(section == 0)
    def _():
        turn_weights()

    @pl.when(section == 1)
    def _():
        cotangent_copy.wait()

    def backward_step(i, carry):
        @pl.when(section == 0)
        def _():
            back_copy(i).wait_recv()

        @pl.when(i >= 2)
        def _():
            staged_save(i - 2).wait()
            early_save(i - 2).wait()

        save(i, 4).wait()

        @pl.when(section == 0)
        def _():
            forward_copy(i).wait_send()

        backward(i)

        @pl.when(section == 1)
        def _():
            back_copy(i).start()

        grad_save(i).start()
        return carry

    lax.fori_loop(0, items, backward_step, 0)

    def finish(i, carry):
        save(i, 3).wait()
        grad_save(i).wait()

        @pl.when(i >= items - 2)
        def _():
            staged_save(i).wait()
            early_save(i).wait()
            for n in range(1, 3):
                save(i, n).wait()

        @pl.when(section == 1)
        def _():
            back_copy(i).wait_send()

        return carry

    lax.fori_loop(0, items, finish, 0)


def layered(image_ids, caption_lengths, captions, regions, cotangent, stacked):
    items, cap_rows, width = captions.shape
    held, region_rows, _ = regions.shape
    rows = cap_rows + region_rows
    inner = stacked[9].shape[2]
    low = jnp.bfloat16
    wide = inner // width

    def cells(*shape):
        return pltpu.VMEM(shape, low)

    anywhere = pl.BlockSpec(memory_space=pl.ANY)
    local = pl.BlockSpec(memory_space=pltpu.VMEM)
    scalars = pl.BlockSpec(memory_space=pltpu.SMEM)
    return pl.pallas_call(
        layer_kernel,
        out_shape=(
            jax.ShapeDtypeStruct((1, items, rows, width), low),
            jax.ShapeDtypeStruct((1, items, rows, width), low),
            jax.ShapeDtypeStruct((items * rows, (3 + wide) * width), low),
            jax.ShapeDtypeStruct((items * rows, (5 + wide) * width), low),
            jax.ShapeDtypeStruct((GROUP, width), jnp.float32),
        ),
        in_specs=[scalars, scalars, anywhere, local, anywhere]
        + [anywhere if len(member.shape) == 3 else local for member in stacked],
        out_specs=(anywhere, anywhere, anywhere, anywhere, local),
        scratch_shapes=[
            cells(width, 3 * width),
            cells(width, width),
            cells(width, inner),
            cells(inner, width),
            cells(3 * width, width),
            cells(width, width),
            cells(inner, width),
            cells(width, inner),
            cells(3 * held, region_rows, width),
            cells(items, rows, width),
            cells(items, rows, width),
            cells(items, rows, width),
            cells(items, rows, width),
            cells(items, rows, width),
            cells(items, HEADS, rows, rows),
            cells(2, rows, width),
            cells(items, rows, width),
            cells(items, rows, width),
            cells(2, rows, width),
            cells(2, rows, inner),
            cells(items, rows, inner),
            cells(items, rows, width),
            cells(2, rows, (5 + wide) * width),
            pltpu.VMEM((items, rows, 2), jnp.float32),
            pltpu.VMEM((rows, width), jnp.float32),
            cells(cap_rows, items, width),
            pltpu.SemaphoreType.DMA((8,)),
            pltpu.SemaphoreType.DMA((2,)),
            pltpu.SemaphoreType.DMA((2,)),
            pltpu.SemaphoreType.DMA((items,)),
            pltpu.SemaphoreType.DMA((items,)),
            pltpu.SemaphoreType.DMA((items,)),
            pltpu.SemaphoreType.DMA((items,)),
            pltpu.SemaphoreType.DMA((items, 8)),
        ],
        compiler_params=pltpu.CompilerParams(
            collective_id=0, has_side_effects=True, vmem_limit_bytes=VMEM_LIMIT
        ),
        cost_estimate=pl.CostEstimate(
            flops=4 * items * rows * (4 + 2 * wide) * width * width,
            bytes_accessed=60_000_000,
            transcendentals=0,
        ),
    )(image_ids, caption_lengths, captions.transpose(1, 0, 2), regions, cotangent, *stacked)


def body(
    captions,
    regions,
    image_ids,
    caption_lengths,
    cotangent,
    query_weight,
    query_bias,
    key_weight,
    value_weight,
    value_bias,
    out_weight,
    out_bias,
    norm1_gain,
    norm1_bias,
    up_weight,
    up_bias,
    down_weight,
    down_bias,
    norm2_gain,
    norm2_bias,
):
    stacked = (
        query_weight,
        query_bias,
        key_weight,
        value_weight,
        value_bias,
        out_weight,
        out_bias,
        norm1_gain,
        norm1_bias,
        up_weight,
        up_bias,
        down_weight,
        down_bias,
        norm2_gain,
        norm2_bias,
    )
    states, input_grads, a_side, b_side, small = layered(
        image_ids, caption_lengths, captions, regions, cotangent, stacked
    )
    sums, small_sums = reduced(a_side, b_side, small, lax.axis_size("batch"))
    return tuple(spread(sums, small_sums, states, input_grads, stacked))


def solution(mesh):
    placed = (
        P("batch", None, None),
        P("batch", None, None),
        P("batch"),
        P("batch"),
        P("batch", None, None),
        P("section", None, None),
        P("section", None),
        P("section", None, None),
        P("section", None, None),
        P("section", None),
        P("section", None, None),
        P("section", None),
        P("section", None),
        P("section", None),
        P("section", None, None),
        P("section", None),
        P("section", None, None),
        P("section", None),
        P("section", None),
        P("section", None),
    )
    return jax.shard_map(
        body,
        mesh=mesh,
        in_specs=placed,
        out_specs=(
            P("section", "batch", None, None),
            P("section", "batch", None, None),
            P("section", None, None),
            P("section", None),
            P("section", None, None),
            P("section", None, None),
            P("section", None),
            P("section", None, None),
            P("section", None),
            P("section", None),
            P("section", None),
            P("section", None, None),
            P("section", None),
            P("section", None, None),
            P("section", None),
            P("section", None),
            P("section", None),
        ),
        check_vma=False,
    )
```

```python
import functools
import math

import jax
import jax.numpy as jnp
from jax import lax
from jax.experimental import pallas as pl
from jax.experimental.pallas import tpu as pltpu
from jax.sharding import PartitionSpec as P

HEADS = 12
EPSILON = 1e-12
MESH = pl.DeviceIdType.MESH
VMEM_LIMIT = 63 * 1024 * 1024
VMEM_BESIDE = 47 * 1024 * 1024
GROUP = 16
CHUNK_GROUPS = 16
SLOTS = 18
SLOT_GROUPS = 24
LAG = 3
EARLY = 6
LINE = 4
SPLIT_BITS = 4


def reduce_kernel(
    bits,
    chunks,
    a_hbm,
    b_hbm,
    small_ref,
    whole,
    small_out,
    a_ref,
    b_ref,
    acc,
    recv,
    small_acc,
    small_recv,
    turned,
    unit,
    load_sem,
    send_sem,
    recv_sem,
    small_send_sem,
    small_recv_sem,
):
    width = acc.shape[2]
    extra = bits - SPLIT_BITS
    first_gather = SPLIT_BITS + 1 + extra
    stages = 2 * (SPLIT_BITS + 1) + extra
    me = lax.axis_index("batch")
    section = lax.axis_index("section")
    core, side, place = me % 2, (me // 2) % 2, (me // 4) % LINE
    blocks_a = a_hbm.shape[1] // width
    blocks_b = b_hbm.shape[1] // width
    per_block = width // (CHUNK_GROUPS * GROUP)

    def load(source, target, block, base):
        lanes = pl.ds(block * width, width)
        return pltpu.make_async_copy(source.at[:, lanes], target.at[:, lanes], load_sem.at[base + block])

    def load_a(block):
        return load(a_hbm, a_ref, block, 0)

    def load_b(block):
        return load(b_hbm, b_ref, block, blocks_a)

    wide = blocks_a - 3
    first_use = {0: [(load_a, 0), (load_b, 0)]}
    for j in range(1, wide):
        first_use[j] = [(load_a, j)]
    first_use[wide] = [(load_a, wide), (load_b, 1)]
    for j in range(1, wide):
        first_use[wide + j] = [(load_b, 1 + j)]
    first_use[2 * wide] = [(load_a, wide + 1), (load_b, wide + 1)]
    first_use[2 * wide + 1] = [(load_a, wide + 2), (load_b, wide + 2)]
    first_use[2 * wide + 2] = [(load_b, wide + 3)]
    first_use[2 * wide + 3] = [(load_b, wide + 4)]
    for j in range(2 * wide + 4):
        for kind, block in first_use[j]:
            kind(block).start()

    def bit_mate(k):
        bit = (me // 2**k) % 2
        return (section, me + 2**k * (1 - 2 * bit))

    core_mate, side_mate = bit_mate(0), bit_mate(1)
    mates = ((section, me - LINE), (section, me + LINE))
    ring = [(section, me + LINE * ((place + d) % LINE - place)) for d in (LINE - 1, 1)]

    barrier = pltpu.get_barrier_semaphore()
    for peer in [core_mate, side_mate] + ring + [bit_mate(k) for k in range(2, bits)]:
        pl.semaphore_signal(barrier, inc=1, device_id=peer, device_id_type=MESH)
    pl.semaphore_wait(barrier, bits + 2)

    def low_core(c):
        return c * CHUNK_GROUPS + core * 8

    def low_side(c):
        return low_core(c) + side * 4

    def block_start(c, kind, b):
        return low_side(c) + b if kind == 0 else low_core(c) + 2 * b

    def final(c, kind):
        return low_side(c) + place if kind == 0 else low_core(c) + 2 * place + side

    def remote(c, source, start, size, target, spot, index, peer):
        return pltpu.make_async_remote_copy(
            src_ref=source.at[pl.ds(start, size)],
            dst_ref=target.at[lax.rem(c, SLOTS), pl.ds(spot, size)] if target is recv else target.at[pl.ds(start, size)],
            send_sem=send_sem.at[lax.rem(c, SLOTS), index],
            recv_sem=recv_sem.at[lax.rem(c, SLOTS), index],
            device_id=peer,
            device_id_type=MESH,
        )

    def core_copy(c):
        return remote(c, acc, c * CHUNK_GROUPS + (1 - core) * 8, 8, recv, 0, 0, core_mate)

    def side_copy(c, kind):
        if kind == 0:
            return remote(c, acc, low_core(c) + (1 - side) * 4, 4, recv, 8, 1, side_mate)
        return remote(c, acc, low_core(c) + 2 * place + (1 - side), 1, recv, 8, 1, side_mate)

    def line_copy(c, kind, r, d):
        size = 1 + kind
        b = jnp.minimum(3 - r + place, 3) if d == 1 else jnp.maximum(r - 3 + place, 0)
        spot = 12 + 2 * (2 * r + d)
        return remote(c, acc, block_start(c, kind, b), size, recv, spot, 2 + 2 * r + d, mates[d])

    def spread_copy(c, kind, r, d):
        size = 1 + kind
        b = jnp.maximum(place - r, 0) if d == 1 else jnp.minimum(place + r, 3)
        return remote(c, whole, block_start(c, kind, b), size, whole, 0, 8 + 2 * r + d, mates[d])

    def side_back_copy(c, kind):
        if kind == 0:
            return remote(c, whole, low_side(c), 4, whole, 0, 14, side_mate)
        return remote(c, whole, final(c, kind), 1, whole, 0, 14, side_mate)

    def core_back_copy(c):
        return remote(c, whole, low_core(c), 8, whole, 0, 15, core_mate)

    def extra_copy(c, kind, e):
        return remote(c, acc, final(c, kind), 1, recv, 24 + e, 16 + e, bit_mate(SPLIT_BITS + e))

    def add_groups(start, count, c, spot):
        slot = lax.rem(c, SLOTS)
        for g in range(count):
            total = acc[start + g].astype(jnp.float32) + recv[slot, spot + g].astype(jnp.float32)
            acc[start + g] = total.astype(jnp.bfloat16)

    def name_of(kind, s):
        if s == 0:
            return ("core",)
        if s == stages - 1:
            return ("core_back",)
        if s < SPLIT_BITS + 1:
            order = [("side",), ("line", 0), ("line", 1), ("line", 2)]
            order = order if kind == 0 else order[1:] + order[:1]
            return order[s - 1]
        if s < first_gather:
            return ("extra", s - SPLIT_BITS - 1)
        order = [("spread", 0), ("spread", 1), ("spread", 2), ("side_back",)]
        order = order if kind == 0 else order[3:] + order[:3]
        return order[s - first_gather]

    def start_stage(c, kind, s):
        name = name_of(kind, s)
        if s == first_gather:
            whole[final(c, kind)] = acc[final(c, kind)]
        if name[0] == "core":
            core_copy(c).start()
        elif name[0] == "side":
            side_copy(c, kind).start()
        elif name[0] == "line":
            r = name[1]
            pl.when(place <= r)(lambda: line_copy(c, kind, r, 1).start())
            pl.when(place >= 3 - r)(lambda: line_copy(c, kind, r, 0).start())
        elif name[0] == "extra":
            extra_copy(c, kind, name[1]).start()
        elif name[0] == "spread":
            r = name[1]
            pl.when((place >= r) & (place <= 2))(lambda: spread_copy(c, kind, r, 1).start())
            pl.when((place >= 1) & (place <= 3 - r))(lambda: spread_copy(c, kind, r, 0).start())
        elif name[0] == "side_back":
            side_back_copy(c, kind).start()
        else:
            core_back_copy(c).start()

    def finish_stage(c, kind, s):
        name = name_of(kind, s)
        if name[0] == "core":
            core_copy(c).wait()
            add_groups(low_core(c), 8, c, 0)
        elif name[0] == "side":
            side_copy(c, kind).wait()
            if kind == 0:
                add_groups(low_side(c), 4, c, 8)
            else:
                add_groups(final(c, kind), 1, c, 8)
        elif name[0] == "line":
            r = name[1]

            @pl.when(place <= r)
            def _():
                line_copy(c, kind, r, 1).wait_send()

            @pl.when(place >= 3 - r)
            def _():
                line_copy(c, kind, r, 0).wait_send()

            @pl.when((place >= 1) & (place <= r + 1))
            def _():
                line_copy(c, kind, r, 1).wait_recv()
                add_groups(block_start(c, kind, 2 - r + place), 1 + kind, c, 12 + 2 * (2 * r + 1))

            @pl.when((place <= 2) & (place >= 2 - r))
            def _():
                line_copy(c, kind, r, 0).wait_recv()
                add_groups(block_start(c, kind, r - 2 + place), 1 + kind, c, 12 + 2 * (2 * r))

        elif name[0] == "extra":
            extra_copy(c, kind, name[1]).wait()
            add_groups(final(c, kind), 1, c, 24 + name[1])
        elif name[0] == "spread":
            r = name[1]
            pl.when((place >= r) & (place <= 2))(lambda: spread_copy(c, kind, r, 1).wait_send())
            pl.when((place >= 1) & (place <= 3 - r))(lambda: spread_copy(c, kind, r, 0).wait_send())
            pl.when(place >= r + 1)(lambda: spread_copy(c, kind, r, 1).wait_recv())
            pl.when(place <= 2 - r)(lambda: spread_copy(c, kind, r, 0).wait_recv())
        elif name[0] == "side_back":
            side_back_copy(c, kind).wait()
        else:
            core_back_copy(c).wait()

    def small_copy(k):
        return pltpu.make_async_remote_copy(
            src_ref=small_acc.at[k],
            dst_ref=small_recv.at[k],
            send_sem=small_send_sem.at[k],
            recv_sem=small_recv_sem.at[k],
            device_id=bit_mate(k),
            device_id_type=MESH,
        )

    small_acc[0] = small_ref[...]
    lines = CHUNK_GROUPS * GROUP
    same = lax.broadcasted_iota(jnp.int32, (lines, lines), 0) == lax.broadcasted_iota(jnp.int32, (lines, lines), 1)
    unit[...] = jnp.where(same, 1.0, 0.0).astype(jnp.bfloat16)

    def kind_of(c):
        early = 1 - jnp.minimum(c // EARLY, 1)
        return early * (c % 2) + (1 - early) * ((c - EARLY + 4) % 4 // 3)

    def step(t, carry):
        for s in range(stages, 0, -1):
            c = t - LAG * s
            for kind in range(2):

                @pl.when((c >= 0) & (c < chunks) & (kind_of(c) == kind))
                def _():
                    finish_stage(c, kind, s - 1)
                    if s < stages:
                        start_stage(c, kind, s)

        for j in range(2 * wide + 4):

            @pl.when(t == per_block * j)
            def _():
                for kind, block in first_use[j]:
                    kind(block).wait()

        @pl.when(t < chunks)
        def _():
            block, part = t // per_block, t % per_block
            a_col = jnp.minimum(block, wide) + jnp.minimum(block // (2 * wide), 1) + jnp.minimum(block // (2 * wide + 1), 1)
            b_col = jnp.maximum(block - wide + 1, 0)
            lines = CHUNK_GROUPS * GROUP
            left = a_ref[:, pl.ds(pl.multiple_of(a_col * width + part * lines, lines), lines)]
            right = b_ref[:, pl.ds(pl.multiple_of(b_col * width, width), width)]
            fresh = (block <= wide) | (block == 2 * wide) | (block == 2 * wide + 1)

            @pl.when(fresh)
            def _():
                turned[part] = product_t(unit[...], left).astype(jnp.bfloat16)

            grad = product(turned[part], right)
            acc[pl.ds(t * CHUNK_GROUPS, CHUNK_GROUPS)] = grad.astype(jnp.bfloat16).reshape(
                CHUNK_GROUPS, GROUP, width
            )
            core_copy(t).start()

        for k in range(bits + 1):

            @pl.when(t == LAG * k)
            def _():
                if k > 0:
                    small_copy(k - 1).wait()
                    small_acc[k] = small_acc[k - 1] + small_recv[k - 1]
                if k < bits:
                    small_copy(k).start()

        return carry

    lax.fori_loop(0, chunks + LAG * stages, step, 0)
    small_out[...] = small_acc[bits]


def reduced(a_side, b_side, small, count):
    rows = a_side.shape[0]
    width = small.shape[1]
    bits = count.bit_length() - 1
    extra = bits - SPLIT_BITS
    blocks = 2 * (a_side.shape[1] // width - 3) + 4
    chunks = blocks * width // (CHUNK_GROUPS * GROUP)
    groups = chunks * CHUNK_GROUPS
    loads = (a_side.shape[1] + b_side.shape[1]) // width
    return pl.pallas_call(
        functools.partial(reduce_kernel, bits, chunks),
        out_shape=(
            pltpu.VMEM((groups, GROUP, width), jnp.bfloat16),
            jax.ShapeDtypeStruct(small.shape, jnp.float32),
        ),
        in_specs=[
            pl.BlockSpec(memory_space=pl.ANY),
            pl.BlockSpec(memory_space=pl.ANY),
            pl.BlockSpec(memory_space=pltpu.VMEM),
        ],
        out_specs=(pl.BlockSpec(memory_space=pltpu.VMEM), pl.BlockSpec(memory_space=pltpu.VMEM)),
        scratch_shapes=[
            pltpu.VMEM(a_side.shape, jnp.bfloat16),
            pltpu.VMEM(b_side.shape, jnp.bfloat16),
            pltpu.VMEM((groups, GROUP, width), jnp.bfloat16),
            pltpu.VMEM((SLOTS, SLOT_GROUPS + extra, GROUP, width), jnp.bfloat16),
            pltpu.VMEM((bits + 1,) + small.shape, jnp.float32),
            pltpu.VMEM((bits,) + small.shape, jnp.float32),
            pltpu.VMEM((width // (CHUNK_GROUPS * GROUP), CHUNK_GROUPS * GROUP, rows), jnp.bfloat16),
            pltpu.VMEM((CHUNK_GROUPS * GROUP, CHUNK_GROUPS * GROUP), jnp.bfloat16),
            pltpu.SemaphoreType.DMA((loads,)),
            pltpu.SemaphoreType.DMA((SLOTS, 16 + extra)),
            pltpu.SemaphoreType.DMA((SLOTS, 16 + extra)),
            pltpu.SemaphoreType.DMA((bits,)),
            pltpu.SemaphoreType.DMA((bits,)),
        ],
        compiler_params=pltpu.CompilerParams(
            collective_id=1, has_side_effects=True, vmem_limit_bytes=VMEM_BESIDE
        ),
        cost_estimate=pl.CostEstimate(
            flops=2 * rows * blocks * width * width, bytes_accessed=80_000_000, transcendentals=0
        ),
    )(a_side, b_side, small)


PIECE = 768
DEPTH = 4


def spread_kernel(sum_ref, small_ref, states_hbm, grads_hbm, *refs):
    width = small_ref.shape[1]
    (o_wq, o_bq, o_wk, o_wv, o_bv, o_wo, o_bo, o_g1, o_s1, o_up, o_bu, o_dn, o_bd, o_g2, o_s2) = refs[2:17]
    states_out, grads_out = refs[:2]
    given, held, out_sem, held_sem = refs[17:]
    wide = o_bu.shape[1] // width
    targets = []
    for j in range(wide):
        targets += [o_dn.at[0, pl.ds(j * width + r, PIECE), :] for r in range(0, width, PIECE)]
    for j in range(wide):
        targets += [o_up.at[0, pl.ds(r, PIECE), pl.ds(j * width, width)] for r in range(0, width, PIECE)]
    for ref in (o_wo, o_wq, o_wk, o_wv):
        targets += [ref.at[0, pl.ds(r, PIECE), :] for r in range(0, width, PIECE)]

    items = states_hbm.shape[1]
    passes = [(states_hbm.at[0, i], states_out.at[0, i]) for i in range(items)]
    passes += [(grads_hbm.at[0, i], grads_out.at[0, i]) for i in range(items)]

    def pass_in(i):
        return pltpu.make_async_copy(passes[i][0], held.at[i], held_sem.at[i])

    def pass_out(i):
        return pltpu.make_async_copy(held.at[i], passes[i][1], held_sem.at[i])

    def store(i):
        return pltpu.make_async_copy(given.at[i % DEPTH], targets[i], out_sem.at[i % DEPTH])

    for i in range(len(passes)):
        pass_in(i).start()
    singles = [o_bq, o_bv, o_bo, o_g1, o_s1, o_bd, o_g2, o_s2]
    for i, ref in enumerate(singles):
        ref[...] = small_ref[pl.ds(i, 1), :]
    for j in range(wide):
        o_bu[:, pl.ds(j * width, width)] = small_ref[pl.ds(len(singles) + j, 1), :]
    for i in range(len(targets)):
        if i >= DEPTH:
            store(i - DEPTH).wait()

        def convert(r, carry):
            block = sum_ref[pl.ds(i * (PIECE // GROUP) + r * 4, 4)].astype(jnp.float32)
            rows = pl.ds(pl.multiple_of(r * 4 * GROUP, 4 * GROUP), 4 * GROUP)
            given[i % DEPTH, rows, :] = block.reshape(4 * GROUP, width)
            return carry

        lax.fori_loop(0, PIECE // (4 * GROUP), convert, 0)
        store(i).start()
        if i < len(passes):
            pass_in(i).wait()
            pass_out(i).start()
    for i in range(len(targets) - DEPTH, len(targets)):
        store(i).wait()
    for i in range(len(passes)):
        pass_out(i).wait()


def spread(sums, small, states, input_grads, params):
    width = small.shape[1]
    anywhere = pl.BlockSpec(memory_space=pl.ANY)
    local = pl.BlockSpec(memory_space=pltpu.VMEM)
    return pl.pallas_call(
        spread_kernel,
        out_shape=(
            jax.ShapeDtypeStruct(states.shape, states.dtype),
            jax.ShapeDtypeStruct(input_grads.shape, input_grads.dtype),
        )
        + tuple(jax.ShapeDtypeStruct(member.shape, jnp.float32) for member in params),
        in_specs=[local, local, anywhere, anywhere],
        out_specs=(anywhere, anywhere)
        + tuple(anywhere if len(member.shape) == 3 else local for member in params),
        scratch_shapes=[
            pltpu.VMEM((DEPTH, PIECE, width), jnp.float32),
            pltpu.VMEM((2 * states.shape[1],) + states.shape[2:], states.dtype),
            pltpu.SemaphoreType.DMA((DEPTH,)),
            pltpu.SemaphoreType.DMA((2 * states.shape[1],)),
        ],
        compiler_params=pltpu.CompilerParams(vmem_limit_bytes=VMEM_BESIDE),
        cost_estimate=pl.CostEstimate(
            flops=12 * width * width, bytes_accessed=80 * width * width, transcendentals=0
        ),
    )(pltpu.with_memory_space_constraint(sums, pltpu.VMEM), small, states, input_grads)


HALF_LOG = -0.5 / math.log(2.0)
BELL_SCALE = 1.0 / math.sqrt(2.0 * math.pi)
SINGLES = ("bq", "bv", "bo", "g1", "s1", "bd", "g2", "s2")


def product(left, right):
    return lax.dot_general(left, right, (((1,), (0,)), ((), ())), preferred_element_type=jnp.float32)


def product_t(left, right):
    return lax.dot_general(left, right, (((1,), (1,)), ((), ())), preferred_element_type=jnp.float32)


def gelu_pair(z):
    cdf = 0.5 * lax.erf(z * (1.0 / math.sqrt(2.0))) + 0.5
    bell = jnp.exp2(z * z * HALF_LOG)
    return z * cdf, z * BELL_SCALE * bell + cdf


def normed(values):
    average = jnp.mean(values, axis=-1, keepdims=True)
    centered = values - average
    inverse = lax.rsqrt(jnp.mean(centered * centered, axis=-1, keepdims=True) + EPSILON)
    return centered * inverse, inverse


def normed_back(grad, normal, inverse):
    first_mean = jnp.mean(grad, axis=-1, keepdims=True)
    second_mean = jnp.mean(grad * normal, axis=-1, keepdims=True)
    return inverse * (grad - first_mean - normal * second_mean)


def layer_kernel(
    ids_ref,
    lengths_ref,
    captions_hbm,
    regions_ref,
    cotangent_hbm,
    wq_hbm,
    bq_ref,
    wk_hbm,
    wv_hbm,
    bv_ref,
    wo_hbm,
    bo_ref,
    g1_ref,
    s1_ref,
    wu_hbm,
    bu_ref,
    wd_hbm,
    bd_ref,
    g2_ref,
    s2_ref,
    states_hbm,
    grads_hbm,
    a_hbm,
    b_hbm,
    small_ref,
    wqkv,
    wo,
    wu,
    wd,
    wqkv_t,
    wo_t,
    wu_t,
    wd_t,
    table,
    hidden,
    upstream,
    query,
    keys,
    values,
    probs,
    context,
    normal1,
    normal2,
    lowered,
    active,
    slope,
    result,
    staged,
    inverses,
    wide1,
    caption_cells,
    weight_sem,
    table_send,
    table_recv,
    fwd_send,
    fwd_recv,
    back_send,
    back_recv,
    out_sem,
):
    items, rows, width = hidden.shape
    held = regions_ref.shape[0]
    cap_rows = captions_hbm.shape[0]
    wide = wu.shape[1] // width
    pairs = HEADS // 2
    pair_width = width // pairs
    head = width // HEADS
    section = lax.axis_index("section")
    batch = lax.axis_index("batch")
    count = lax.axis_size("batch")
    right = (section, lax.rem(batch + 1, count))
    left = (section, lax.rem(batch + count - 1, count))
    other = (1 - section, batch)
    core = lax.rem(batch, 2)

    weight_copies = [
        pltpu.make_async_copy(source.at[0], target, weight_sem.at[n])
        for n, (source, target) in enumerate(
            (
                (wq_hbm, wqkv.at[:, pl.ds(0, width)]),
                (wk_hbm, wqkv.at[:, pl.ds(width, width)]),
                (wv_hbm, wqkv.at[:, pl.ds(2 * width, width)]),
                (wo_hbm, wo),
                (wu_hbm, wu),
                (wd_hbm, wd),
            )
        )
    ]
    for copy in weight_copies[:3]:
        copy.start()
    cotangent_copy = pltpu.make_async_copy(cotangent_hbm, upstream, weight_sem.at[6])

    barrier = pltpu.get_barrier_semaphore()
    for peer in (right, left, other):
        pl.semaphore_signal(barrier, inc=1, device_id=peer, device_id_type=MESH)
    pl.semaphore_wait(barrier, 3)

    def table_copy(n, peer):
        return pltpu.make_async_remote_copy(
            src_ref=regions_ref,
            dst_ref=table.at[pl.ds(2 * n * held, held)],
            send_sem=table_send.at[n],
            recv_sem=table_recv.at[n],
            device_id=peer,
            device_id_type=MESH,
        )

    @pl.when(section == 0)
    def _():
        caption_copy = pltpu.make_async_copy(captions_hbm, caption_cells, weight_sem.at[7])
        caption_copy.start()
        table_copy(0, right).start()
        table_copy(1, left).start()
        table[pl.ds(held, held)] = regions_ref[...]
        table_copy(0, right).wait()
        table_copy(1, left).wait()
        caption_copy.wait()

    for copy in weight_copies[3:]:
        copy.start()

    @pl.when(section == 1)
    def _():
        cotangent_copy.start()

    def forward_copy(i):
        return pltpu.make_async_remote_copy(
            src_ref=result.at[i],
            dst_ref=hidden.at[i],
            send_sem=fwd_send.at[i],
            recv_sem=fwd_recv.at[i],
            device_id=other,
            device_id_type=MESH,
        )

    def back_copy(i):
        return pltpu.make_async_remote_copy(
            src_ref=result.at[i],
            dst_ref=upstream.at[i],
            send_sem=back_send.at[i],
            recv_sem=back_recv.at[i],
            device_id=other,
            device_id_type=MESH,
        )

    def save(i, n):
        at = pl.ds(pl.multiple_of(i * rows, rows), rows)
        first = wide * width
        turn = lax.rem(i, 2)
        if n == 0:
            source, target = active.at[turn], a_hbm.at[at, pl.ds(0, first)]
        elif n == 1:
            source, target = lowered.at[turn], a_hbm.at[at, pl.ds(first, width)]
        elif n == 2:
            source, target = context.at[turn], a_hbm.at[at, pl.ds(first + width, width)]
        elif n == 3:
            source, target = hidden.at[i], a_hbm.at[at, pl.ds(first + 2 * width, width)]
        else:
            source, target = result.at[i], states_hbm.at[0, i]
        return pltpu.make_async_copy(source, target, out_sem.at[i, n])

    def staged_save(i):
        at = pl.ds(pl.multiple_of(i * rows, rows), rows)
        lanes = pl.ds((1 + wide) * width, 4 * width)
        return pltpu.make_async_copy(
            staged.at[lax.rem(i, 2), :, lanes], b_hbm.at[at, lanes], out_sem.at[i, 5]
        )

    def early_save(i):
        at = pl.ds(pl.multiple_of(i * rows, rows), rows)
        lanes = pl.ds(0, (1 + wide) * width)
        return pltpu.make_async_copy(
            staged.at[lax.rem(i, 2), :, lanes], b_hbm.at[at, lanes], out_sem.at[i, 7]
        )

    def grad_save(i):
        return pltpu.make_async_copy(result.at[i], grads_hbm.at[0, i], out_sem.at[i, 6])

    def vector(ref, j=0):
        return ref[:, j * width : (j + 1) * width].astype(jnp.float32)

    lane = lax.broadcasted_iota(jnp.int32, (rows, pair_width), 1)

    blocks = [slice(r, r + GROUP) for r in range(0, rows, GROUP)]
    spans = [slice(c, min(c + 128, rows)) for c in range(0, rows, 128)]

    def only(block, h):
        return jnp.where((lane // head) == h, block, jnp.zeros_like(block))

    def assemble(i):
        total = count * held
        spot = jnp.minimum(lax.rem(ids_ref[i] - (batch - 1) * held + total, total), 3 * held - 1)
        for n in range(items):

            @pl.when(i == n)
            def _():
                whole = jnp.concatenate(
                    [caption_cells[:, n, :].astype(jnp.float32), table[spot].astype(jnp.float32)], axis=0
                )
                hidden[n] = whole.astype(jnp.bfloat16)

    def forward(i):
        @pl.when((i == 0) & (section == 0))
        def _():
            for copy in weight_copies[:3]:
                copy.wait()

        turn = lax.rem(i, 2)
        source = hidden[i]
        mixed = product(source, wqkv[...])
        for at in blocks:
            scaled = (mixed[at, :width] + vector(bq_ref)) * (1.0 / math.sqrt(head))
            query[i, at, :] = scaled.astype(jnp.bfloat16)
            keys[i, at, :] = mixed[at, width : 2 * width].astype(jnp.bfloat16)
            values[i, at, :] = (mixed[at, 2 * width :] + vector(bv_ref)).astype(jnp.bfloat16)
        position = lax.broadcasted_iota(jnp.int32, (rows, 1), 0)
        live = (position >= cap_rows) | (position < lengths_ref[i])
        key_bias = jnp.where(live, 0.0, -1000000000.0)

        def wait_rest():
            @pl.when((i == 0) & (section == 0))
            def _():
                for copy in weight_copies[3:]:
                    copy.wait()

        def lanes_of(p):
            return slice(p * pair_width, (p + 1) * pair_width)

        def scored(p):
            k_pair = keys[i, :, lanes_of(p)]
            stacked = jnp.concatenate([only(k_pair, 0), only(k_pair, 1)], axis=0)
            v_turned = values[i, :, lanes_of(p)].astype(jnp.float32).T.astype(jnp.bfloat16)
            return product_t(stacked, query[i, :, lanes_of(p)]), v_turned

        def weighed(p, both):
            for h in range(2):
                for span in spans:
                    scores = both[h * rows : (h + 1) * rows, span] + key_bias
                    expo = jnp.exp(scores - jnp.max(scores, axis=0, keepdims=True))
                    share = pltpu.reciprocal(jnp.sum(expo, axis=0, keepdims=True), approx=True)
                    probs[i, 2 * p + h, :, span] = (expo * share).astype(jnp.bfloat16)

        def mixed_values(p, v_turned):
            return [product(v_turned[h * head : (h + 1) * head], probs[i, 2 * p + h]) for h in range(2)]

        def place_context(p, parts):
            context[turn, :, lanes_of(p)] = jnp.concatenate(parts, axis=0).T.astype(jnp.bfloat16)

        def projected(group):
            lanes = slice(group * 2 * pair_width, (group + 1) * 2 * pair_width)
            return product(context[turn, :, lanes], wo[lanes, :])

        ahead = scored(0)
        parts = None
        attended = None
        for p in range(pairs):
            both, v_turned = ahead
            if p + 1 < pairs:
                ahead = scored(p + 1)
            if parts is not None:
                place_context(p - 1, parts)
            if p in (2, 4):
                if p == 2:
                    wait_rest()
                piece = projected(p // 2 - 1)
                attended = piece if attended is None else attended + piece
            weighed(p, both)
            parts = mixed_values(p, v_turned)
        place_context(pairs - 1, parts)
        attended += projected(pairs // 2 - 1)

        @pl.when((section == 0) & (core == 1) & (i >= 1))
        def _():
            forward_copy(i - 1).start()

        for at in blocks:
            n1, inv1 = normed(hidden[i, at, :].astype(jnp.float32) + attended[at] + vector(bo_ref))
            normal1[i, at, :] = n1.astype(jnp.bfloat16)
            inverses[i, at, 0:1] = inv1
            first = n1 * vector(g1_ref) + vector(s1_ref)
            lowered[turn, at, :] = first.astype(jnp.bfloat16)
            wide1[at, :] = first + vector(bd_ref)
        half = wide * width // 2

        def raised(n):
            return product(lowered[turn], wu[:, n * half : (n + 1) * half])

        def bend(n, z_tile):
            for part in range(0, half, width):
                lanes = slice(n * half + part, n * half + part + width)
                bias = bu_ref[:, lanes].astype(jnp.float32)
                for at in blocks:
                    gelu, slant = gelu_pair(z_tile[at, part : part + width] + bias)
                    active[turn, at, lanes] = gelu.astype(jnp.bfloat16)
                    slope[i, at, lanes] = slant.astype(jnp.bfloat16)

        z_first = raised(0)
        z_second = raised(1)
        bend(0, z_first)
        wide1[...] += product(active[turn, :, :half], wd[:half, :])
        bend(1, z_second)
        lowest = product(active[turn, :, half:], wd[half:, :])
        for at in blocks:
            n2, inv2 = normed(wide1[at, :] + lowest[at])
            normal2[i, at, :] = n2.astype(jnp.bfloat16)
            inverses[i, at, 1:2] = inv2
            result[i, at, :] = (n2 * vector(g2_ref) + vector(s2_ref)).astype(jnp.bfloat16)

    def folded(value):
        return value[: GROUP // 2] + value[GROUP // 2 :]

    def keep_small(row, value):
        small_ref[row : row + 1, :] += jnp.sum(value, axis=0, keepdims=True)

    def single(name, value):
        keep_small(SINGLES.index(name), value)

    def backward(i):
        slot = lax.rem(i, 2)
        base = (2 + wide) * width

        def stage(at, column, value):
            staged[slot, at, column * width : (column + 1) * width] = value

        def norm_step(at, gradient, normal, layer_norm, gain, sums):
            n = normal[i, at, :].astype(jnp.float32)
            d_res = normed_back(gradient * vector(gain), n, inverses[i, at, layer_norm : layer_norm + 1])
            d_low = d_res.astype(jnp.bfloat16)
            terms = [folded(gradient * n), folded(gradient), folded(d_low.astype(jnp.float32))]
            return d_res, d_low, terms if sums is None else [a + b for a, b in zip(sums, terms)]

        sums = None
        for at in blocks:
            gradient = upstream[i, at, :].astype(jnp.float32)
            d_res, d_low, sums = norm_step(at, gradient, normal2, 1, g2_ref, sums)
            wide1[at, :] = d_res
            stage(at, 0, d_low)
        for name, value in zip(("g2", "s2", "bd"), sums):
            single(name, value)
        d_out = staged[slot, :, :width]
        half = wide * width // 2

        def opened_half(n):
            return product(d_out, wd_t[:, n * half : (n + 1) * half])

        def bent_half(n, d_active):
            for part in range(0, half, width):
                j = (n * half + part) // width
                lanes = slice(j * width, (j + 1) * width)
                total = None
                for at in blocks:
                    d_inner = d_active[at, part : part + width] * slope[i, at, lanes].astype(jnp.float32)
                    d_inner = d_inner.astype(jnp.bfloat16)
                    stage(at, 1 + j, d_inner)
                    term = folded(d_inner.astype(jnp.float32))
                    total = term if total is None else total + term
                keep_small(len(SINGLES) + j, total)

        def closed_half(n):
            at = width + n * half
            return product(staged[slot, :, at : at + half], wu_t[n * half : (n + 1) * half, :])

        d_first = opened_half(0)
        d_second = opened_half(1)
        bent_half(0, d_first)
        d_deep = closed_half(0)
        bent_half(1, d_second)
        d_deeper = closed_half(1)
        early_save(i).start()
        sums = None
        for at in blocks:
            d_res, d_low, sums = norm_step(at, wide1[at, :] + d_deep[at] + d_deeper[at], normal1, 0, g1_ref, sums)
            wide1[at, :] = d_res
            stage(at, 1 + wide, d_low)
        for name, value in zip(("g1", "s1", "bo"), sums):
            single(name, value)
        d_att = staged[slot, :, (1 + wide) * width : (2 + wide) * width]
        @pl.when(i == 0)
        def _():
            save(items - 2, 0).wait()
            save(items - 1, 0).wait()

        active[0, :, :width] = product(d_att, wo_t[...]).astype(jnp.bfloat16)

        def lanes_of(p):
            return slice(p * pair_width, (p + 1) * pair_width)

        def place_grad(n, p, block):
            at = base + n * width + p * pair_width
            staged[slot, :, at : at + pair_width] = block.astype(jnp.bfloat16)

        def opened(p):
            v_pair = values[i, :, lanes_of(p)]
            c_pair = active[0, :, lanes_of(p)]
            stacked = jnp.concatenate([only(v_pair, 0), only(v_pair, 1)], axis=0)
            k_turned = keys[i, :, lanes_of(p)].astype(jnp.float32).T.astype(jnp.bfloat16)
            d_value = product(probs[i, 2 * p], only(c_pair, 0))
            d_value += product(probs[i, 2 * p + 1], only(c_pair, 1))
            return product_t(stacked, c_pair), k_turned, d_value

        def score_base(p, h):
            return (2 * (p % 2) + h) * 2 * 128

        def score_grads(p, both):
            for h in range(2):
                for span in spans:
                    prob = probs[i, 2 * p + h, :, span].astype(jnp.float32)
                    d_prob = both[h * rows : (h + 1) * rows, span]
                    drift = jnp.sum(d_prob * prob, axis=0, keepdims=True)
                    at = score_base(p, h)
                    active[1, :, at + span.start : at + span.stop] = (prob * (d_prob - drift)).astype(jnp.bfloat16)
            return [active[1, :, score_base(p, h) : score_base(p, h) + rows] for h in range(2)]

        def closed(p, found, k_turned):
            q_pair = query[i, :, lanes_of(p)]
            d_key = product(found[0], only(q_pair, 0)) + product(found[1], only(q_pair, 1))
            return d_key, [product(k_turned[h * head : (h + 1) * head], found[h]) for h in range(2)]

        def place_grads(p, d_value, d_key, parts):
            place_grad(0, p, jnp.concatenate(parts, axis=0).T * (1.0 / math.sqrt(head)))
            place_grad(1, p, d_key)
            place_grad(2, p, d_value)

        ahead = opened(0)
        waiting = None
        d_source = None

        def source_grad(group):
            found = None
            for n in range(3):
                at = n * width + group * 2 * pair_width
                piece = product(
                    staged[slot, :, base + at : base + at + 2 * pair_width], wqkv_t[at : at + 2 * pair_width, :]
                )
                found = piece if found is None else found + piece
            return found

        for p in range(pairs):
            both, k_turned, d_value = ahead
            if p + 1 < pairs:
                ahead = opened(p + 1)
            if waiting is not None:
                place_grads(*waiting)
            if p in (2, 4):
                piece = source_grad(p // 2 - 1)
                d_source = piece if d_source is None else d_source + piece
            found = score_grads(p, both)
            d_key, parts = closed(p, found, k_turned)
            waiting = (p, d_value, d_key, parts)
        place_grads(*waiting)
        staged_save(i).start()
        d_source += source_grad(pairs // 2 - 1)
        sums = None
        for at in blocks:
            result[i, at, :] = (wide1[at, :] + d_source[at]).astype(jnp.bfloat16)
            terms = [
                folded(staged[slot, at, base : base + width].astype(jnp.float32)),
                folded(staged[slot, at, base + 2 * width : base + 3 * width].astype(jnp.float32)),
            ]
            sums = terms if sums is None else [a + b for a, b in zip(sums, terms)]
        single("bq", sums[0])
        single("bv", sums[1])

    small_ref[...] = jnp.zeros_like(small_ref)
    side = 256
    unit = lax.broadcasted_iota(jnp.int32, (side, side), 0) == lax.broadcasted_iota(jnp.int32, (side, side), 1)
    unit = jnp.where(unit, 1.0, 0.0).astype(jnp.bfloat16)

    def turn_weights():
        for natural, turned in ((wqkv, wqkv_t), (wo, wo_t), (wu, wu_t), (wd, wd_t)):
            for block in range(0, natural.shape[0], width):

                def one(n, carry):
                    at = pl.ds(pl.multiple_of(n * side, side), side)
                    tall = product_t(unit, natural[block : block + width, at])
                    turned[at, block : block + width] = tall.astype(jnp.bfloat16)
                    return carry

                lax.fori_loop(0, natural.shape[1] // side, one, 0)

    @pl.when(section == 1)
    def _():
        for copy in weight_copies:
            copy.wait()
        turn_weights()

    def forward_step(i, carry):
        @pl.when(section == 0)
        def _():
            assemble(i)

        @pl.when(section == 1)
        def _():
            forward_copy(i).wait_recv()

        @pl.when(i >= 2)
        def _():
            for n in range(3):
                save(i - 2, n).wait()

        forward(i)

        @pl.when((section == 0) & ((core == 0) | (i == items - 1)))
        def _():
            forward_copy(i).start()

        for n in range(5):
            save(i, n).start()
        return carry

    lax.fori_loop(0, items, forward_step, 0)

    @pl.when(section == 0)
    def _():
        turn_weights()

    @pl.when(section == 1)
    def _():
        cotangent_copy.wait()

    def backward_step(i, carry):
        @pl.when(section == 0)
        def _():
            back_copy(i).wait_recv()

        @pl.when(i >= 2)
        def _():
            staged_save(i - 2).wait()
            early_save(i - 2).wait()

        save(i, 4).wait()

        @pl.when(section == 0)
        def _():
            forward_copy(i).wait_send()

        backward(i)

        @pl.when(section == 1)
        def _():
            back_copy(i).start()

        grad_save(i).start()
        return carry

    lax.fori_loop(0, items, backward_step, 0)

    def finish(i, carry):
        save(i, 3).wait()
        grad_save(i).wait()

        @pl.when(i >= items - 2)
        def _():
            staged_save(i).wait()
            early_save(i).wait()
            for n in range(1, 3):
                save(i, n).wait()

        @pl.when(section == 1)
        def _():
            back_copy(i).wait_send()

        return carry

    lax.fori_loop(0, items, finish, 0)


def layered(image_ids, caption_lengths, captions, regions, cotangent, stacked):
    items, cap_rows, width = captions.shape
    held, region_rows, _ = regions.shape
    rows = cap_rows + region_rows
    inner = stacked[9].shape[2]
    low = jnp.bfloat16
    wide = inner // width

    def cells(*shape):
        return pltpu.VMEM(shape, low)

    anywhere = pl.BlockSpec(memory_space=pl.ANY)
    local = pl.BlockSpec(memory_space=pltpu.VMEM)
    scalars = pl.BlockSpec(memory_space=pltpu.SMEM)
    return pl.pallas_call(
        layer_kernel,
        out_shape=(
            jax.ShapeDtypeStruct((1, items, rows, width), low),
            jax.ShapeDtypeStruct((1, items, rows, width), low),
            jax.ShapeDtypeStruct((items * rows, (3 + wide) * width), low),
            jax.ShapeDtypeStruct((items * rows, (5 + wide) * width), low),
            jax.ShapeDtypeStruct((GROUP, width), jnp.float32),
        ),
        in_specs=[scalars, scalars, anywhere, local, anywhere]
        + [anywhere if len(member.shape) == 3 else local for member in stacked],
        out_specs=(anywhere, anywhere, anywhere, anywhere, local),
        scratch_shapes=[
            cells(width, 3 * width),
            cells(width, width),
            cells(width, inner),
            cells(inner, width),
            cells(3 * width, width),
            cells(width, width),
            cells(inner, width),
            cells(width, inner),
            cells(3 * held, region_rows, width),
            cells(items, rows, width),
            cells(items, rows, width),
            cells(items, rows, width),
            cells(items, rows, width),
            cells(items, rows, width),
            cells(items, HEADS, rows, rows),
            cells(2, rows, width),
            cells(items, rows, width),
            cells(items, rows, width),
            cells(2, rows, width),
            cells(2, rows, inner),
            cells(items, rows, inner),
            cells(items, rows, width),
            cells(2, rows, (5 + wide) * width),
            pltpu.VMEM((items, rows, 2), jnp.float32),
            pltpu.VMEM((rows, width), jnp.float32),
            cells(cap_rows, items, width),
            pltpu.SemaphoreType.DMA((8,)),
            pltpu.SemaphoreType.DMA((2,)),
            pltpu.SemaphoreType.DMA((2,)),
            pltpu.SemaphoreType.DMA((items,)),
            pltpu.SemaphoreType.DMA((items,)),
            pltpu.SemaphoreType.DMA((items,)),
            pltpu.SemaphoreType.DMA((items,)),
            pltpu.SemaphoreType.DMA((items, 8)),
        ],
        compiler_params=pltpu.CompilerParams(
            collective_id=0, has_side_effects=True, vmem_limit_bytes=VMEM_LIMIT
        ),
        cost_estimate=pl.CostEstimate(
            flops=4 * items * rows * (4 + 2 * wide) * width * width,
            bytes_accessed=60_000_000,
            transcendentals=0,
        ),
    )(image_ids, caption_lengths, captions.transpose(1, 0, 2), regions, cotangent, *stacked)


def body(
    captions,
    regions,
    image_ids,
    caption_lengths,
    cotangent,
    query_weight,
    query_bias,
    key_weight,
    value_weight,
    value_bias,
    out_weight,
    out_bias,
    norm1_gain,
    norm1_bias,
    up_weight,
    up_bias,
    down_weight,
    down_bias,
    norm2_gain,
    norm2_bias,
):
    stacked = (
        query_weight,
        query_bias,
        key_weight,
        value_weight,
        value_bias,
        out_weight,
        out_bias,
        norm1_gain,
        norm1_bias,
        up_weight,
        up_bias,
        down_weight,
        down_bias,
        norm2_gain,
        norm2_bias,
    )
    states, input_grads, a_side, b_side, small = layered(
        image_ids, caption_lengths, captions, regions, cotangent, stacked
    )
    sums, small_sums = reduced(a_side, b_side, small, lax.axis_size("batch"))
    return tuple(spread(sums, small_sums, states, input_grads, stacked))


def solution(mesh):
    placed = (
        P("batch", None, None),
        P("batch", None, None),
        P("batch"),
        P("batch"),
        P("batch", None, None),
        P("section", None, None),
        P("section", None),
        P("section", None, None),
        P("section", None, None),
        P("section", None),
        P("section", None, None),
        P("section", None),
        P("section", None),
        P("section", None),
        P("section", None, None),
        P("section", None),
        P("section", None, None),
        P("section", None),
        P("section", None),
        P("section", None),
    )
    return jax.shard_map(
        body,
        mesh=mesh,
        in_specs=placed,
        out_specs=(
            P("section", "batch", None, None),
            P("section", "batch", None, None),
            P("section", None, None),
            P("section", None),
            P("section", None, None),
            P("section", None, None),
            P("section", None),
            P("section", None, None),
            P("section", None),
            P("section", None),
            P("section", None),
            P("section", None, None),
            P("section", None),
            P("section", None, None),
            P("section", None),
            P("section", None),
            P("section", None),
        ),
        check_vma=False,
    )
```

```python
import functools
import math

import jax
import jax.numpy as jnp
from jax import lax
from jax.experimental import pallas as pl
from jax.experimental.pallas import tpu as pltpu
from jax.sharding import PartitionSpec as P

HEADS = 12
EPSILON = 1e-12
MESH = pl.DeviceIdType.MESH
VMEM_LIMIT = 63 * 1024 * 1024
VMEM_BESIDE = 47 * 1024 * 1024
GROUP = 16
CHUNK_GROUPS = 16
SLOTS = 18
SLOT_GROUPS = 24
LAG = 3
CYCLE = 3
LINE = 4
SPLIT_BITS = 4


def reduce_kernel(
    bits,
    chunks,
    a_hbm,
    b_hbm,
    small_ref,
    whole,
    small_out,
    a_ref,
    b_ref,
    acc,
    recv,
    small_acc,
    small_recv,
    load_sem,
    send_sem,
    recv_sem,
    small_send_sem,
    small_recv_sem,
):
    width = acc.shape[2]
    extra = bits - SPLIT_BITS
    first_gather = SPLIT_BITS + 1 + extra
    stages = 2 * (SPLIT_BITS + 1) + extra
    me = lax.axis_index("batch")
    section = lax.axis_index("section")
    core, side, place = me % 2, (me // 2) % 2, (me // 4) % LINE
    blocks_a = a_hbm.shape[1] // width
    blocks_b = b_hbm.shape[1] // width
    per_block = width // (CHUNK_GROUPS * GROUP)

    def load(source, target, block, base):
        lanes = pl.ds(block * width, width)
        return pltpu.make_async_copy(source.at[:, lanes], target.at[:, lanes], load_sem.at[base + block])

    def load_a(block):
        return load(a_hbm, a_ref, block, 0)

    def load_b(block):
        return load(b_hbm, b_ref, block, blocks_a)

    wide = blocks_a - 3
    first_use = {0: [(load_a, 0), (load_b, 0)]}
    for j in range(1, wide):
        first_use[j] = [(load_a, j)]
    first_use[wide] = [(load_a, wide), (load_b, 1)]
    for j in range(1, wide):
        first_use[wide + j] = [(load_b, 1 + j)]
    first_use[2 * wide] = [(load_a, wide + 1), (load_b, wide + 1)]
    first_use[2 * wide + 1] = [(load_a, wide + 2), (load_b, wide + 2)]
    first_use[2 * wide + 2] = [(load_b, wide + 3)]
    first_use[2 * wide + 3] = [(load_b, wide + 4)]
    for j in range(2 * wide + 4):
        for kind, block in first_use[j]:
            kind(block).start()

    def bit_mate(k):
        bit = (me // 2**k) % 2
        return (section, me + 2**k * (1 - 2 * bit))

    core_mate, side_mate = bit_mate(0), bit_mate(1)
    mates = ((section, me - LINE * jnp.minimum(place, 1)), (section, me + LINE * jnp.minimum(LINE - 1 - place, 1)))
    ring = [(section, me + LINE * ((place + d) % LINE - place)) for d in (LINE - 1, 1)]

    barrier = pltpu.get_barrier_semaphore()
    for peer in [core_mate, side_mate] + ring + [bit_mate(k) for k in range(2, bits)]:
        pl.semaphore_signal(barrier, inc=1, device_id=peer, device_id_type=MESH)
    pl.semaphore_wait(barrier, bits + 2)

    def low_core(c):
        return c * CHUNK_GROUPS + core * 8

    def low_side(c):
        return low_core(c) + side * 4

    def block_start(c, kind, b):
        return low_side(c) + b if kind == 0 else low_core(c) + 2 * b

    def final(c, kind):
        return low_side(c) + place if kind == 0 else low_core(c) + 2 * place + side

    def remote(c, source, start, size, target, spot, index, peer):
        return pltpu.make_async_remote_copy(
            src_ref=source.at[pl.ds(start, size)],
            dst_ref=target.at[lax.rem(c, SLOTS), pl.ds(spot, size)] if target is recv else target.at[pl.ds(start, size)],
            send_sem=send_sem.at[lax.rem(c, SLOTS), index],
            recv_sem=recv_sem.at[lax.rem(c, SLOTS), index],
            device_id=peer,
            device_id_type=MESH,
        )

    def core_copy(c):
        return remote(c, acc, c * CHUNK_GROUPS + (1 - core) * 8, 8, recv, 0, 0, core_mate)

    def side_copy(c, kind):
        if kind == 0:
            return remote(c, acc, low_core(c) + (1 - side) * 4, 4, recv, 8, 1, side_mate)
        return remote(c, acc, low_core(c) + 2 * place + (1 - side), 1, recv, 8, 1, side_mate)

    def line_copy(c, kind, r, d):
        size = 1 + kind
        b = jnp.minimum(3 - r + place, 3) if d == 1 else jnp.maximum(r - 3 + place, 0)
        spot = 12 + 2 * (2 * r + d)
        return remote(c, acc, block_start(c, kind, b), size, recv, spot, 2 + 2 * r + d, mates[d])

    def spread_copy(c, kind, r, d):
        size = 1 + kind
        b = jnp.maximum(place - r, 0) if d == 1 else jnp.minimum(place + r, 3)
        return remote(c, whole, block_start(c, kind, b), size, whole, 0, 8 + 2 * r + d, mates[d])

    def side_back_copy(c, kind):
        if kind == 0:
            return remote(c, whole, low_side(c), 4, whole, 0, 14, side_mate)
        return remote(c, whole, final(c, kind), 1, whole, 0, 14, side_mate)

    def core_back_copy(c):
        return remote(c, whole, low_core(c), 8, whole, 0, 15, core_mate)

    def extra_copy(c, kind, e):
        return remote(c, acc, final(c, kind), 1, recv, 24 + e, 16 + e, bit_mate(SPLIT_BITS + e))

    def add_groups(start, count, c, spot):
        slot = lax.rem(c, SLOTS)
        for g in range(count):
            total = acc[start + g].astype(jnp.float32) + recv[slot, spot + g].astype(jnp.float32)
            acc[start + g] = total.astype(jnp.bfloat16)

    def name_of(kind, s):
        if s == 0:
            return ("core",)
        if s == stages - 1:
            return ("core_back",)
        if s < SPLIT_BITS + 1:
            order = [("side",), ("line", 0), ("line", 1), ("line", 2)]
            order = order if kind == 0 else order[1:] + order[:1]
            return order[s - 1]
        if s < first_gather:
            return ("extra", s - SPLIT_BITS - 1)
        order = [("spread", 0), ("spread", 1), ("spread", 2), ("side_back",)]
        order = order if kind == 0 else order[3:] + order[:3]
        return order[s - first_gather]

    def start_stage(c, kind, s):
        name = name_of(kind, s)
        if s == first_gather:
            whole[final(c, kind)] = acc[final(c, kind)]
        if name[0] == "core":
            core_copy(c).start()
        elif name[0] == "side":
            side_copy(c, kind).start()
        elif name[0] == "line":
            r = name[1]
            pl.when(place <= r)(lambda: line_copy(c, kind, r, 1).start())
            pl.when(place >= 3 - r)(lambda: line_copy(c, kind, r, 0).start())
        elif name[0] == "extra":
            extra_copy(c, kind, name[1]).start()
        elif name[0] == "spread":
            r = name[1]
            pl.when((place >= r) & (place <= 2))(lambda: spread_copy(c, kind, r, 1).start())
            pl.when((place >= 1) & (place <= 3 - r))(lambda: spread_copy(c, kind, r, 0).start())
        elif name[0] == "side_back":
            side_back_copy(c, kind).start()
        else:
            core_back_copy(c).start()

    def finish_stage(c, kind, s):
        name = name_of(kind, s)
        if name[0] == "core":
            core_copy(c).wait()
            add_groups(low_core(c), 8, c, 0)
        elif name[0] == "side":
            side_copy(c, kind).wait()
            if kind == 0:
                add_groups(low_side(c), 4, c, 8)
            else:
                add_groups(final(c, kind), 1, c, 8)
        elif name[0] == "line":
            r = name[1]

            @pl.when(place <= r)
            def _():
                line_copy(c, kind, r, 1).wait_send()

            @pl.when(place >= 3 - r)
            def _():
                line_copy(c, kind, r, 0).wait_send()

            @pl.when((place >= 1) & (place <= r + 1))
            def _():
                line_copy(c, kind, r, 1).wait_recv()
                add_groups(block_start(c, kind, 2 - r + place), 1 + kind, c, 12 + 2 * (2 * r + 1))

            @pl.when((place <= 2) & (place >= 2 - r))
            def _():
                line_copy(c, kind, r, 0).wait_recv()
                add_groups(block_start(c, kind, r - 2 + place), 1 + kind, c, 12 + 2 * (2 * r))

        elif name[0] == "extra":
            extra_copy(c, kind, name[1]).wait()
            add_groups(final(c, kind), 1, c, 24 + name[1])
        elif name[0] == "spread":
            r = name[1]
            pl.when((place >= r) & (place <= 2))(lambda: spread_copy(c, kind, r, 1).wait_send())
            pl.when((place >= 1) & (place <= 3 - r))(lambda: spread_copy(c, kind, r, 0).wait_send())
            pl.when(place >= r + 1)(lambda: spread_copy(c, kind, r, 1).wait_recv())
            pl.when(place <= 2 - r)(lambda: spread_copy(c, kind, r, 0).wait_recv())
        elif name[0] == "side_back":
            side_back_copy(c, kind).wait()
        else:
            core_back_copy(c).wait()

    def small_copy(k):
        return pltpu.make_async_remote_copy(
            src_ref=small_acc.at[k],
            dst_ref=small_recv.at[k],
            send_sem=small_send_sem.at[k],
            recv_sem=small_recv_sem.at[k],
            device_id=bit_mate(k),
            device_id_type=MESH,
        )

    small_acc[0] = small_ref[...]

    def step(t, phase):
        for s in range(stages, 0, -1):
            c = t - LAG * s
            kind = (phase - LAG * s) % CYCLE // 2

            @pl.when((c >= 0) & (c < chunks))
            def _():
                finish_stage(c, kind, s - 1)
                if s < stages:
                    start_stage(c, kind, s)

        for j in range(2 * wide + 4):

            @pl.when(t == per_block * j)
            def _():
                for kind, block in first_use[j]:
                    kind(block).wait()

        @pl.when(t < chunks)
        def _():
            block, part = t // per_block, t % per_block
            a_col = jnp.minimum(block, wide) + jnp.minimum(block // (2 * wide), 1) + jnp.minimum(block // (2 * wide + 1), 1)
            b_col = jnp.maximum(block - wide + 1, 0)
            lines = CHUNK_GROUPS * GROUP
            left = a_ref[:, pl.ds(pl.multiple_of(a_col * width + part * lines, lines), lines)]
            right = b_ref[:, pl.ds(pl.multiple_of(b_col * width, width), width)]
            grad = lax.dot_general(left, right, (((0,), (0,)), ((), ())), preferred_element_type=jnp.float32)
            acc[pl.ds(t * CHUNK_GROUPS, CHUNK_GROUPS)] = grad.astype(jnp.bfloat16).reshape(
                CHUNK_GROUPS, GROUP, width
            )
            core_copy(t).start()

        for k in range(bits + 1):

            @pl.when(t == LAG * k)
            def _():
                if k > 0:
                    small_copy(k - 1).wait()
                    small_acc[k] = small_acc[k - 1] + small_recv[k - 1]
                if k < bits:
                    small_copy(k).start()

    def cycle(n, carry):
        for phase in range(CYCLE):
            step(n * CYCLE + phase, phase)
        return carry

    lax.fori_loop(0, pl.cdiv(chunks + LAG * stages, CYCLE), cycle, 0)
    small_out[...] = small_acc[bits]


def reduced(a_side, b_side, small, count):
    rows = a_side.shape[0]
    width = small.shape[1]
    bits = count.bit_length() - 1
    extra = bits - SPLIT_BITS
    blocks = 2 * (a_side.shape[1] // width - 3) + 4
    chunks = blocks * width // (CHUNK_GROUPS * GROUP)
    groups = chunks * CHUNK_GROUPS
    loads = (a_side.shape[1] + b_side.shape[1]) // width
    return pl.pallas_call(
        functools.partial(reduce_kernel, bits, chunks),
        out_shape=(
            pltpu.VMEM((groups, GROUP, width), jnp.bfloat16),
            jax.ShapeDtypeStruct(small.shape, jnp.float32),
        ),
        in_specs=[
            pl.BlockSpec(memory_space=pl.ANY),
            pl.BlockSpec(memory_space=pl.ANY),
            pl.BlockSpec(memory_space=pltpu.VMEM),
        ],
        out_specs=(pl.BlockSpec(memory_space=pltpu.VMEM), pl.BlockSpec(memory_space=pltpu.VMEM)),
        scratch_shapes=[
            pltpu.VMEM(a_side.shape, jnp.bfloat16),
            pltpu.VMEM(b_side.shape, jnp.bfloat16),
            pltpu.VMEM((groups, GROUP, width), jnp.bfloat16),
            pltpu.VMEM((SLOTS, SLOT_GROUPS + extra, GROUP, width), jnp.bfloat16),
            pltpu.VMEM((bits + 1,) + small.shape, jnp.float32),
            pltpu.VMEM((bits,) + small.shape, jnp.float32),
            pltpu.SemaphoreType.DMA((loads,)),
            pltpu.SemaphoreType.DMA((SLOTS, 16 + extra)),
            pltpu.SemaphoreType.DMA((SLOTS, 16 + extra)),
            pltpu.SemaphoreType.DMA((bits,)),
            pltpu.SemaphoreType.DMA((bits,)),
        ],
        compiler_params=pltpu.CompilerParams(
            collective_id=1, has_side_effects=True, vmem_limit_bytes=VMEM_BESIDE
        ),
        cost_estimate=pl.CostEstimate(
            flops=2 * rows * blocks * width * width, bytes_accessed=80_000_000, transcendentals=0
        ),
    )(a_side, b_side, small)


PIECE = 768
DEPTH = 4


def spread_kernel(sum_ref, small_ref, states_hbm, grads_hbm, *refs):
    width = small_ref.shape[1]
    (o_wq, o_bq, o_wk, o_wv, o_bv, o_wo, o_bo, o_g1, o_s1, o_up, o_bu, o_dn, o_bd, o_g2, o_s2) = refs[2:17]
    states_out, grads_out = refs[:2]
    given, held, out_sem, held_sem = refs[17:]
    wide = o_bu.shape[1] // width
    targets = []
    for j in range(wide):
        targets += [o_dn.at[0, pl.ds(j * width + r, PIECE), :] for r in range(0, width, PIECE)]
    for j in range(wide):
        targets += [o_up.at[0, pl.ds(r, PIECE), pl.ds(j * width, width)] for r in range(0, width, PIECE)]
    for ref in (o_wo, o_wq, o_wk, o_wv):
        targets += [ref.at[0, pl.ds(r, PIECE), :] for r in range(0, width, PIECE)]

    items = states_hbm.shape[1]
    passes = [(states_hbm.at[0, i], states_out.at[0, i]) for i in range(items)]
    passes += [(grads_hbm.at[0, i], grads_out.at[0, i]) for i in range(items)]

    def pass_in(i):
        return pltpu.make_async_copy(passes[i][0], held.at[i], held_sem.at[i])

    def pass_out(i):
        return pltpu.make_async_copy(held.at[i], passes[i][1], held_sem.at[i])

    def store(i):
        return pltpu.make_async_copy(given.at[i % DEPTH], targets[i], out_sem.at[i % DEPTH])

    for i in range(len(passes)):
        pass_in(i).start()
    singles = [o_bq, o_bv, o_bo, o_g1, o_s1, o_bd, o_g2, o_s2]
    for i, ref in enumerate(singles):
        ref[...] = small_ref[pl.ds(i, 1), :]
    for j in range(wide):
        o_bu[:, pl.ds(j * width, width)] = small_ref[pl.ds(len(singles) + j, 1), :]
    for i in range(len(targets)):
        if i >= DEPTH:
            store(i - DEPTH).wait()

        def convert(r, carry):
            block = sum_ref[pl.ds(i * (PIECE // GROUP) + r * 4, 4)].astype(jnp.float32)
            rows = pl.ds(pl.multiple_of(r * 4 * GROUP, 4 * GROUP), 4 * GROUP)
            given[i % DEPTH, rows, :] = block.reshape(4 * GROUP, width)
            return carry

        lax.fori_loop(0, PIECE // (4 * GROUP), convert, 0)
        store(i).start()
        if i < len(passes):
            pass_in(i).wait()
            pass_out(i).start()
    for i in range(len(targets) - DEPTH, len(targets)):
        store(i).wait()
    for i in range(len(passes)):
        pass_out(i).wait()


def spread(sums, small, states, input_grads, params):
    width = small.shape[1]
    anywhere = pl.BlockSpec(memory_space=pl.ANY)
    local = pl.BlockSpec(memory_space=pltpu.VMEM)
    return pl.pallas_call(
        spread_kernel,
        out_shape=(
            jax.ShapeDtypeStruct(states.shape, states.dtype),
            jax.ShapeDtypeStruct(input_grads.shape, input_grads.dtype),
        )
        + tuple(jax.ShapeDtypeStruct(member.shape, jnp.float32) for member in params),
        in_specs=[local, local, anywhere, anywhere],
        out_specs=(anywhere, anywhere)
        + tuple(anywhere if len(member.shape) == 3 else local for member in params),
        scratch_shapes=[
            pltpu.VMEM((DEPTH, PIECE, width), jnp.float32),
            pltpu.VMEM((2 * states.shape[1],) + states.shape[2:], states.dtype),
            pltpu.SemaphoreType.DMA((DEPTH,)),
            pltpu.SemaphoreType.DMA((2 * states.shape[1],)),
        ],
        compiler_params=pltpu.CompilerParams(vmem_limit_bytes=VMEM_BESIDE),
        cost_estimate=pl.CostEstimate(
            flops=12 * width * width, bytes_accessed=80 * width * width, transcendentals=0
        ),
    )(pltpu.with_memory_space_constraint(sums, pltpu.VMEM), small, states, input_grads)


HALF_LOG = -0.5 / math.log(2.0)
BELL_SCALE = 1.0 / math.sqrt(2.0 * math.pi)
SINGLES = ("bq", "bv", "bo", "g1", "s1", "bd", "g2", "s2")


def product(left, right):
    return lax.dot_general(left, right, (((1,), (0,)), ((), ())), preferred_element_type=jnp.float32)


def product_t(left, right):
    return lax.dot_general(left, right, (((1,), (1,)), ((), ())), preferred_element_type=jnp.float32)


def gelu_pair(z):
    cdf = 0.5 * lax.erf(z * (1.0 / math.sqrt(2.0))) + 0.5
    bell = jnp.exp2(z * z * HALF_LOG)
    return z * cdf, z * BELL_SCALE * bell + cdf


def normed(values):
    average = jnp.mean(values, axis=-1, keepdims=True)
    centered = values - average
    inverse = lax.rsqrt(jnp.mean(centered * centered, axis=-1, keepdims=True) + EPSILON)
    return centered * inverse, inverse


def normed_back(grad, normal, inverse):
    first_mean = jnp.mean(grad, axis=-1, keepdims=True)
    second_mean = jnp.mean(grad * normal, axis=-1, keepdims=True)
    return inverse * (grad - first_mean - normal * second_mean)


def layer_kernel(
    ids_ref,
    lengths_ref,
    captions_hbm,
    regions_ref,
    cotangent_hbm,
    wq_hbm,
    bq_ref,
    wk_hbm,
    wv_hbm,
    bv_ref,
    wo_hbm,
    bo_ref,
    g1_ref,
    s1_ref,
    wu_hbm,
    bu_ref,
    wd_hbm,
    bd_ref,
    g2_ref,
    s2_ref,
    states_hbm,
    grads_hbm,
    a_hbm,
    b_hbm,
    small_ref,
    wqkv,
    wo,
    wu,
    wd,
    wqkv_t,
    wo_t,
    wu_t,
    wd_t,
    table,
    hidden,
    upstream,
    query,
    keys,
    values,
    probs,
    context,
    normal1,
    normal2,
    lowered,
    active,
    slope,
    result,
    staged,
    inverses,
    wide1,
    caption_cells,
    weight_sem,
    table_send,
    table_recv,
    fwd_send,
    fwd_recv,
    back_send,
    back_recv,
    out_sem,
):
    items, rows, width = hidden.shape
    held = regions_ref.shape[0]
    cap_rows = captions_hbm.shape[0]
    wide = wu.shape[1] // width
    pairs = HEADS // 2
    pair_width = width // pairs
    head = width // HEADS
    section = lax.axis_index("section")
    batch = lax.axis_index("batch")
    count = lax.axis_size("batch")
    right = (section, lax.rem(batch + 1, count))
    left = (section, lax.rem(batch + count - 1, count))
    other = (1 - section, batch)
    core = lax.rem(batch, 2)

    weight_copies = [
        pltpu.make_async_copy(source.at[0], target, weight_sem.at[n])
        for n, (source, target) in enumerate(
            (
                (wq_hbm, wqkv.at[:, pl.ds(0, width)]),
                (wk_hbm, wqkv.at[:, pl.ds(width, width)]),
                (wv_hbm, wqkv.at[:, pl.ds(2 * width, width)]),
                (wo_hbm, wo),
                (wu_hbm, wu),
                (wd_hbm, wd),
            )
        )
    ]
    for copy in weight_copies[:3]:
        copy.start()
    cotangent_copy = pltpu.make_async_copy(cotangent_hbm, upstream, weight_sem.at[6])

    barrier = pltpu.get_barrier_semaphore()
    for peer in (right, left, other):
        pl.semaphore_signal(barrier, inc=1, device_id=peer, device_id_type=MESH)
    pl.semaphore_wait(barrier, 3)

    def table_copy(n, peer):
        return pltpu.make_async_remote_copy(
            src_ref=regions_ref,
            dst_ref=table.at[pl.ds(2 * n * held, held)],
            send_sem=table_send.at[n],
            recv_sem=table_recv.at[n],
            device_id=peer,
            device_id_type=MESH,
        )

    @pl.when(section == 0)
    def _():
        caption_copy = pltpu.make_async_copy(captions_hbm, caption_cells, weight_sem.at[7])
        caption_copy.start()
        table_copy(0, right).start()
        table_copy(1, left).start()
        table[pl.ds(held, held)] = regions_ref[...]
        table_copy(0, right).wait()
        table_copy(1, left).wait()
        caption_copy.wait()

    for copy in weight_copies[3:]:
        copy.start()

    @pl.when(section == 1)
    def _():
        cotangent_copy.start()

    def forward_copy(i):
        return pltpu.make_async_remote_copy(
            src_ref=result.at[i],
            dst_ref=hidden.at[i],
            send_sem=fwd_send.at[i],
            recv_sem=fwd_recv.at[i],
            device_id=other,
            device_id_type=MESH,
        )

    def back_copy(i):
        return pltpu.make_async_remote_copy(
            src_ref=result.at[i],
            dst_ref=upstream.at[i],
            send_sem=back_send.at[i],
            recv_sem=back_recv.at[i],
            device_id=other,
            device_id_type=MESH,
        )

    def save(i, n):
        at = pl.ds(pl.multiple_of(i * rows, rows), rows)
        first = wide * width
        turn = lax.rem(i, 2)
        if n == 0:
            source, target = active.at[turn], a_hbm.at[at, pl.ds(0, first)]
        elif n == 1:
            source, target = lowered.at[turn], a_hbm.at[at, pl.ds(first, width)]
        elif n == 2:
            source, target = context.at[turn], a_hbm.at[at, pl.ds(first + width, width)]
        elif n == 3:
            source, target = hidden.at[i], a_hbm.at[at, pl.ds(first + 2 * width, width)]
        else:
            source, target = result.at[i], states_hbm.at[0, i]
        return pltpu.make_async_copy(source, target, out_sem.at[i, n])

    def staged_save(i):
        at = pl.ds(pl.multiple_of(i * rows, rows), rows)
        return pltpu.make_async_copy(staged.at[lax.rem(i, 2)], b_hbm.at[at], out_sem.at[i, 5])

    def grad_save(i):
        return pltpu.make_async_copy(result.at[i], grads_hbm.at[0, i], out_sem.at[i, 6])

    def vector(ref, j=0):
        return ref[:, j * width : (j + 1) * width].astype(jnp.float32)

    lane = lax.broadcasted_iota(jnp.int32, (rows, pair_width), 1)

    blocks = [slice(r, r + GROUP) for r in range(0, rows, GROUP)]
    spans = [slice(c, min(c + 128, rows)) for c in range(0, rows, 128)]

    def only(block, h):
        return jnp.where((lane // head) == h, block, jnp.zeros_like(block))

    def assemble(i):
        total = count * held
        spot = jnp.minimum(lax.rem(ids_ref[i] - (batch - 1) * held + total, total), 3 * held - 1)
        for n in range(items):

            @pl.when(i == n)
            def _():
                whole = jnp.concatenate(
                    [caption_cells[:, n, :].astype(jnp.float32), table[spot].astype(jnp.float32)], axis=0
                )
                hidden[n] = whole.astype(jnp.bfloat16)

    def forward(i):
        @pl.when((i == 0) & (section == 0))
        def _():
            for copy in weight_copies[:3]:
                copy.wait()

        turn = lax.rem(i, 2)
        source = hidden[i]
        mixed = product(source, wqkv[...])
        for at in blocks:
            scaled = (mixed[at, :width] + vector(bq_ref)) * (1.0 / math.sqrt(head))
            query[i, at, :] = scaled.astype(jnp.bfloat16)
            keys[i, at, :] = mixed[at, width : 2 * width].astype(jnp.bfloat16)
            values[i, at, :] = (mixed[at, 2 * width :] + vector(bv_ref)).astype(jnp.bfloat16)
        position = lax.broadcasted_iota(jnp.int32, (rows, 1), 0)
        live = (position >= cap_rows) | (position < lengths_ref[i])
        key_bias = jnp.where(live, 0.0, -1000000000.0)

        def wait_rest():
            @pl.when((i == 0) & (section == 0))
            def _():
                for copy in weight_copies[3:]:
                    copy.wait()

        def lanes_of(p):
            return slice(p * pair_width, (p + 1) * pair_width)

        def scored(p):
            k_pair = keys[i, :, lanes_of(p)]
            stacked = jnp.concatenate([only(k_pair, 0), only(k_pair, 1)], axis=0)
            v_turned = values[i, :, lanes_of(p)].astype(jnp.float32).T.astype(jnp.bfloat16)
            return product_t(stacked, query[i, :, lanes_of(p)]), v_turned

        def weighed(p, both):
            for h in range(2):
                for span in spans:
                    scores = both[h * rows : (h + 1) * rows, span] + key_bias
                    expo = jnp.exp(scores - jnp.max(scores, axis=0, keepdims=True))
                    share = pltpu.reciprocal(jnp.sum(expo, axis=0, keepdims=True), approx=True)
                    probs[i, 2 * p + h, :, span] = (expo * share).astype(jnp.bfloat16)

        def mixed_values(p, v_turned):
            return [product(v_turned[h * head : (h + 1) * head], probs[i, 2 * p + h]) for h in range(2)]

        def place_context(p, parts):
            context[turn, :, lanes_of(p)] = jnp.concatenate(parts, axis=0).T.astype(jnp.bfloat16)

        def projected(group):
            lanes = slice(group * 2 * pair_width, (group + 1) * 2 * pair_width)
            return product(context[turn, :, lanes], wo[lanes, :])

        ahead = scored(0)
        parts = None
        attended = None
        for p in range(pairs):
            both, v_turned = ahead
            if p + 1 < pairs:
                ahead = scored(p + 1)
            if parts is not None:
                place_context(p - 1, parts)
            if p in (2, 4):
                if p == 2:
                    wait_rest()
                piece = projected(p // 2 - 1)
                attended = piece if attended is None else attended + piece
            weighed(p, both)
            parts = mixed_values(p, v_turned)
        place_context(pairs - 1, parts)
        attended += projected(pairs // 2 - 1)

        @pl.when((section == 0) & (core == 1) & (i >= 1))
        def _():
            forward_copy(i - 1).start()

        for at in blocks:
            n1, inv1 = normed(hidden[i, at, :].astype(jnp.float32) + attended[at] + vector(bo_ref))
            normal1[i, at, :] = n1.astype(jnp.bfloat16)
            inverses[i, at, 0:1] = inv1
            first = n1 * vector(g1_ref) + vector(s1_ref)
            lowered[turn, at, :] = first.astype(jnp.bfloat16)
            wide1[at, :] = first + vector(bd_ref)
        half = wide * width // 2

        def raised(n):
            return product(lowered[turn], wu[:, n * half : (n + 1) * half])

        def bend(n, z_tile):
            for part in range(0, half, width):
                lanes = slice(n * half + part, n * half + part + width)
                bias = bu_ref[:, lanes].astype(jnp.float32)
                for at in blocks:
                    gelu, slant = gelu_pair(z_tile[at, part : part + width] + bias)
                    active[turn, at, lanes] = gelu.astype(jnp.bfloat16)
                    slope[i, at, lanes] = slant.astype(jnp.bfloat16)

        z_first = raised(0)
        z_second = raised(1)
        bend(0, z_first)
        wide1[...] += product(active[turn, :, :half], wd[:half, :])
        bend(1, z_second)
        lowest = product(active[turn, :, half:], wd[half:, :])
        for at in blocks:
            n2, inv2 = normed(wide1[at, :] + lowest[at])
            normal2[i, at, :] = n2.astype(jnp.bfloat16)
            inverses[i, at, 1:2] = inv2
            result[i, at, :] = (n2 * vector(g2_ref) + vector(s2_ref)).astype(jnp.bfloat16)

    def folded(value):
        return value[: GROUP // 2] + value[GROUP // 2 :]

    def keep_small(row, value):
        small_ref[row : row + 1, :] += jnp.sum(value, axis=0, keepdims=True)

    def single(name, value):
        keep_small(SINGLES.index(name), value)

    def backward(i):
        slot = lax.rem(i, 2)
        base = (2 + wide) * width

        def stage(at, column, value):
            staged[slot, at, column * width : (column + 1) * width] = value

        def norm_step(at, gradient, normal, layer_norm, gain, sums):
            n = normal[i, at, :].astype(jnp.float32)
            d_res = normed_back(gradient * vector(gain), n, inverses[i, at, layer_norm : layer_norm + 1])
            d_low = d_res.astype(jnp.bfloat16)
            terms = [folded(gradient * n), folded(gradient), folded(d_low.astype(jnp.float32))]
            return d_res, d_low, terms if sums is None else [a + b for a, b in zip(sums, terms)]

        sums = None
        for at in blocks:
            gradient = upstream[i, at, :].astype(jnp.float32)
            d_res, d_low, sums = norm_step(at, gradient, normal2, 1, g2_ref, sums)
            wide1[at, :] = d_res
            stage(at, 0, d_low)
        for name, value in zip(("g2", "s2", "bd"), sums):
            single(name, value)
        d_out = staged[slot, :, :width]
        half = wide * width // 2

        def opened_half(n):
            return product(d_out, wd_t[:, n * half : (n + 1) * half])

        def bent_half(n, d_active):
            for part in range(0, half, width):
                j = (n * half + part) // width
                lanes = slice(j * width, (j + 1) * width)
                total = None
                for at in blocks:
                    d_inner = d_active[at, part : part + width] * slope[i, at, lanes].astype(jnp.float32)
                    d_inner = d_inner.astype(jnp.bfloat16)
                    stage(at, 1 + j, d_inner)
                    term = folded(d_inner.astype(jnp.float32))
                    total = term if total is None else total + term
                keep_small(len(SINGLES) + j, total)

        def closed_half(n):
            at = width + n * half
            return product(staged[slot, :, at : at + half], wu_t[n * half : (n + 1) * half, :])

        d_first = opened_half(0)
        d_second = opened_half(1)
        bent_half(0, d_first)
        d_deep = closed_half(0)
        bent_half(1, d_second)
        d_deeper = closed_half(1)
        sums = None
        for at in blocks:
            d_res, d_low, sums = norm_step(at, wide1[at, :] + d_deep[at] + d_deeper[at], normal1, 0, g1_ref, sums)
            wide1[at, :] = d_res
            stage(at, 1 + wide, d_low)
        for name, value in zip(("g1", "s1", "bo"), sums):
            single(name, value)
        d_att = staged[slot, :, (1 + wide) * width : (2 + wide) * width]
        @pl.when(i == 0)
        def _():
            save(items - 2, 0).wait()
            save(items - 1, 0).wait()

        active[0, :, :width] = product(d_att, wo_t[...]).astype(jnp.bfloat16)

        def lanes_of(p):
            return slice(p * pair_width, (p + 1) * pair_width)

        def place_grad(n, p, block):
            at = base + n * width + p * pair_width
            staged[slot, :, at : at + pair_width] = block.astype(jnp.bfloat16)

        def opened(p):
            v_pair = values[i, :, lanes_of(p)]
            c_pair = active[0, :, lanes_of(p)]
            stacked = jnp.concatenate([only(v_pair, 0), only(v_pair, 1)], axis=0)
            k_turned = keys[i, :, lanes_of(p)].astype(jnp.float32).T.astype(jnp.bfloat16)
            d_value = product(probs[i, 2 * p], only(c_pair, 0))
            d_value += product(probs[i, 2 * p + 1], only(c_pair, 1))
            return product_t(stacked, c_pair), k_turned, d_value

        def score_base(p, h):
            return (2 * (p % 2) + h) * 2 * 128

        def score_grads(p, both):
            for h in range(2):
                for span in spans:
                    prob = probs[i, 2 * p + h, :, span].astype(jnp.float32)
                    d_prob = both[h * rows : (h + 1) * rows, span]
                    drift = jnp.sum(d_prob * prob, axis=0, keepdims=True)
                    at = score_base(p, h)
                    active[1, :, at + span.start : at + span.stop] = (prob * (d_prob - drift)).astype(jnp.bfloat16)
            return [active[1, :, score_base(p, h) : score_base(p, h) + rows] for h in range(2)]

        def closed(p, found, k_turned):
            q_pair = query[i, :, lanes_of(p)]
            d_key = product(found[0], only(q_pair, 0)) + product(found[1], only(q_pair, 1))
            return d_key, [product(k_turned[h * head : (h + 1) * head], found[h]) for h in range(2)]

        def place_grads(p, d_value, d_key, parts):
            place_grad(0, p, jnp.concatenate(parts, axis=0).T * (1.0 / math.sqrt(head)))
            place_grad(1, p, d_key)
            place_grad(2, p, d_value)

        ahead = opened(0)
        waiting = None
        d_source = None

        def source_grad(group):
            found = None
            for n in range(3):
                at = n * width + group * 2 * pair_width
                piece = product(
                    staged[slot, :, base + at : base + at + 2 * pair_width], wqkv_t[at : at + 2 * pair_width, :]
                )
                found = piece if found is None else found + piece
            return found

        for p in range(pairs):
            both, k_turned, d_value = ahead
            if p + 1 < pairs:
                ahead = opened(p + 1)
            if waiting is not None:
                place_grads(*waiting)
            if p in (2, 4):
                piece = source_grad(p // 2 - 1)
                d_source = piece if d_source is None else d_source + piece
            found = score_grads(p, both)
            d_key, parts = closed(p, found, k_turned)
            waiting = (p, d_value, d_key, parts)
        place_grads(*waiting)
        d_source += source_grad(pairs // 2 - 1)
        sums = None
        for at in blocks:
            result[i, at, :] = (wide1[at, :] + d_source[at]).astype(jnp.bfloat16)
            terms = [
                folded(staged[slot, at, base : base + width].astype(jnp.float32)),
                folded(staged[slot, at, base + 2 * width : base + 3 * width].astype(jnp.float32)),
            ]
            sums = terms if sums is None else [a + b for a, b in zip(sums, terms)]
        single("bq", sums[0])
        single("bv", sums[1])

    small_ref[...] = jnp.zeros_like(small_ref)
    side = 256
    unit = lax.broadcasted_iota(jnp.int32, (side, side), 0) == lax.broadcasted_iota(jnp.int32, (side, side), 1)
    unit = jnp.where(unit, 1.0, 0.0).astype(jnp.bfloat16)

    def turn_weights():
        for natural, turned in ((wqkv, wqkv_t), (wo, wo_t), (wu, wu_t), (wd, wd_t)):
            for block in range(0, natural.shape[0], width):

                def one(n, carry):
                    at = pl.ds(pl.multiple_of(n * side, side), side)
                    tall = product_t(unit, natural[block : block + width, at])
                    turned[at, block : block + width] = tall.astype(jnp.bfloat16)
                    return carry

                lax.fori_loop(0, natural.shape[1] // side, one, 0)

    @pl.when(section == 1)
    def _():
        for copy in weight_copies:
            copy.wait()
        turn_weights()

    def forward_step(i, carry):
        @pl.when(section == 0)
        def _():
            assemble(i)

        @pl.when(section == 1)
        def _():
            forward_copy(i).wait_recv()

        @pl.when(i >= 2)
        def _():
            for n in range(3):
                save(i - 2, n).wait()

        forward(i)

        @pl.when((section == 0) & ((core == 0) | (i == items - 1)))
        def _():
            forward_copy(i).start()

        for n in range(5):
            save(i, n).start()
        return carry

    lax.fori_loop(0, items, forward_step, 0)

    @pl.when(section == 0)
    def _():
        turn_weights()

    @pl.when(section == 1)
    def _():
        cotangent_copy.wait()

    def backward_step(i, carry):
        @pl.when(section == 0)
        def _():
            back_copy(i).wait_recv()

        @pl.when(i >= 2)
        def _():
            staged_save(i - 2).wait()

        save(i, 4).wait()

        @pl.when(section == 0)
        def _():
            forward_copy(i).wait_send()

        backward(i)

        @pl.when(section == 1)
        def _():
            back_copy(i).start()

        staged_save(i).start()
        grad_save(i).start()
        return carry

    lax.fori_loop(0, items, backward_step, 0)

    def finish(i, carry):
        save(i, 3).wait()
        grad_save(i).wait()

        @pl.when(i >= items - 2)
        def _():
            staged_save(i).wait()
            for n in range(1, 3):
                save(i, n).wait()

        @pl.when(section == 1)
        def _():
            back_copy(i).wait_send()

        return carry

    lax.fori_loop(0, items, finish, 0)


def layered(image_ids, caption_lengths, captions, regions, cotangent, stacked):
    items, cap_rows, width = captions.shape
    held, region_rows, _ = regions.shape
    rows = cap_rows + region_rows
    inner = stacked[9].shape[2]
    low = jnp.bfloat16
    wide = inner // width

    def cells(*shape):
        return pltpu.VMEM(shape, low)

    anywhere = pl.BlockSpec(memory_space=pl.ANY)
    local = pl.BlockSpec(memory_space=pltpu.VMEM)
    scalars = pl.BlockSpec(memory_space=pltpu.SMEM)
    return pl.pallas_call(
        layer_kernel,
        out_shape=(
            jax.ShapeDtypeStruct((1, items, rows, width), low),
            jax.ShapeDtypeStruct((1, items, rows, width), low),
            jax.ShapeDtypeStruct((items * rows, (3 + wide) * width), low),
            jax.ShapeDtypeStruct((items * rows, (5 + wide) * width), low),
            jax.ShapeDtypeStruct((GROUP, width), jnp.float32),
        ),
        in_specs=[scalars, scalars, anywhere, local, anywhere]
        + [anywhere if len(member.shape) == 3 else local for member in stacked],
        out_specs=(anywhere, anywhere, anywhere, anywhere, local),
        scratch_shapes=[
            cells(width, 3 * width),
            cells(width, width),
            cells(width, inner),
            cells(inner, width),
            cells(3 * width, width),
            cells(width, width),
            cells(inner, width),
            cells(width, inner),
            cells(3 * held, region_rows, width),
            cells(items, rows, width),
            cells(items, rows, width),
            cells(items, rows, width),
            cells(items, rows, width),
            cells(items, rows, width),
            cells(items, HEADS, rows, rows),
            cells(2, rows, width),
            cells(items, rows, width),
            cells(items, rows, width),
            cells(2, rows, width),
            cells(2, rows, inner),
            cells(items, rows, inner),
            cells(items, rows, width),
            cells(2, rows, (5 + wide) * width),
            pltpu.VMEM((items, rows, 2), jnp.float32),
            pltpu.VMEM((rows, width), jnp.float32),
            cells(cap_rows, items, width),
            pltpu.SemaphoreType.DMA((8,)),
            pltpu.SemaphoreType.DMA((2,)),
            pltpu.SemaphoreType.DMA((2,)),
            pltpu.SemaphoreType.DMA((items,)),
            pltpu.SemaphoreType.DMA((items,)),
            pltpu.SemaphoreType.DMA((items,)),
            pltpu.SemaphoreType.DMA((items,)),
            pltpu.SemaphoreType.DMA((items, 7)),
        ],
        compiler_params=pltpu.CompilerParams(
            collective_id=0, has_side_effects=True, vmem_limit_bytes=VMEM_LIMIT
        ),
        cost_estimate=pl.CostEstimate(
            flops=4 * items * rows * (4 + 2 * wide) * width * width,
            bytes_accessed=60_000_000,
            transcendentals=0,
        ),
    )(image_ids, caption_lengths, captions.transpose(1, 0, 2), regions, cotangent, *stacked)


def body(
    captions,
    regions,
    image_ids,
    caption_lengths,
    cotangent,
    query_weight,
    query_bias,
    key_weight,
    value_weight,
    value_bias,
    out_weight,
    out_bias,
    norm1_gain,
    norm1_bias,
    up_weight,
    up_bias,
    down_weight,
    down_bias,
    norm2_gain,
    norm2_bias,
):
    stacked = (
        query_weight,
        query_bias,
        key_weight,
        value_weight,
        value_bias,
        out_weight,
        out_bias,
        norm1_gain,
        norm1_bias,
        up_weight,
        up_bias,
        down_weight,
        down_bias,
        norm2_gain,
        norm2_bias,
    )
    states, input_grads, a_side, b_side, small = layered(
        image_ids, caption_lengths, captions, regions, cotangent, stacked
    )
    sums, small_sums = reduced(a_side, b_side, small, lax.axis_size("batch"))
    return tuple(spread(sums, small_sums, states, input_grads, stacked))


def solution(mesh):
    placed = (
        P("batch", None, None),
        P("batch", None, None),
        P("batch"),
        P("batch"),
        P("batch", None, None),
        P("section", None, None),
        P("section", None),
        P("section", None, None),
        P("section", None, None),
        P("section", None),
        P("section", None, None),
        P("section", None),
        P("section", None),
        P("section", None),
        P("section", None, None),
        P("section", None),
        P("section", None, None),
        P("section", None),
        P("section", None),
        P("section", None),
    )
    return jax.shard_map(
        body,
        mesh=mesh,
        in_specs=placed,
        out_specs=(
            P("section", "batch", None, None),
            P("section", "batch", None, None),
            P("section", None, None),
            P("section", None),
            P("section", None, None),
            P("section", None, None),
            P("section", None),
            P("section", None, None),
            P("section", None),
            P("section", None),
            P("section", None),
            P("section", None, None),
            P("section", None),
            P("section", None, None),
            P("section", None),
            P("section", None),
            P("section", None),
        ),
        check_vma=False,
    )
```
